32 devices in a mesh: src: 4 (over z), gx: 2 (over x), gy: 4 (over y, core).
Axes of the slice: x: 2, y: 2, z: 4, core: 2. Of those that a mesh axis runs over, the one named last changes fastest.
Arguments:
- labels: int32 [16, 128, 128], P('gx', 'gy'), may hold values from 0 to 15
- kappa_table: float32 [16], replicated, may hold values from 0.5 to 2
- absorb_table: float32 [16], replicated, may hold values from 0.02 to 0.1
- background: float32 [16, 16, 128, 128], P('src', 'gx', 'gy'), may hold values from 0.1 to 10
- det_cells: int32 [1024], replicated, may hold values from 0 to 262143
- v_kappa: float32 [16, 128, 128], P('gx', 'gy', 'src'), may hold values from -6 to 6
- v_absorb: float32 [16, 128, 128], P('gx', 'gy', 'src'), may hold values from -6 to 6
- q_kappa: float32 [16, 128, 128], P('gx', 'gy', 'src'), may hold values from -6 to 6
- q_absorb: float32 [16, 128, 128], P('gx', 'gy', 'src'), may hold values from -6 to 6
- beta_prev: float32 [1], replicated, may hold values from 0.2 to 2
Outputs:
- next_kappa: float32 [16, 128, 128], P('gx', 'gy', 'src')
- next_absorb: float32 [16, 128, 128], P('gx', 'gy', 'src')
- coefs: float32 [2], replicated
The draws below stay inside these ranges and needn't reach their ends.
Inputs may be any that keep to these rules, and one draw needn't show every extreme that they name: `labels`: a region number for every cell. `det_cells`: flat index (x * 128 + y) * 128 + z of a grid cell; indices may repeat.
All inputs are finite; a program needn't handle non-finite values.
Results may differ from the reference program's by a relative error of at most 0.0001.
Values sent between devices are 32-bit elements; how exact they have to be, the bound alone decides.
No kernel may reach another device: no remote copies, remote signals or barrier semaphores. Data moves between devices by JAX's collectives and lax.ppermute only.
A program may use at most 128 MiB of HBM per device.

```python
import math
import jax
import jax.numpy as jnp
from jax import lax

DETS = 1024
REGIONS = 16
ITERS = 6
NX = 16
NY = 128
NZ = 128
SOURCES = 16
CELLS = 262144


def place_ends(values, stream_key, smallest, largest):
    dims = values.shape
    index_at = [jax.random.randint(jax.random.fold_in(stream_key, axis), (), 0, dims[axis]) for axis in range(len(dims))]
    values = values.at[tuple(index_at)].set(smallest)
    longest = dims.index(max(dims))
    index_at[longest] = (index_at[longest] + 1) % dims[longest]
    return values.at[tuple(index_at)].set(largest)


def steps_of(key, shape, pieces, least, top_value):
    level, own = 1.0, jax.random.fold_in(key, 6)
    for axis_at, parts in pieces:
        steps = jnp.exp(jax.random.uniform(jax.random.fold_in(own, axis_at), (parts,), jnp.float32, least / len(pieces), top_value / len(pieces)))
        level = level * jnp.repeat(steps, shape[axis_at] // parts).reshape([-1 if axis == axis_at else 1 for axis in range(len(shape))])
    return level


def normal_values(rng, dims, width, most, shards=(), dtype=jnp.bfloat16):
    drawn = jax.random.normal(rng, dims, jnp.float32) * width
    if len(shards) > 0:
        drawn = steps_of(rng, dims, shards, -0.22, 0.18) * drawn
    return jnp.clip(drawn, min=-most, max=most).astype(dtype)


def setup_inputs(seed: int = 0) -> dict:
    keys = jax.random.split(jax.random.key(seed), 11)
    labels = place_ends(jax.random.randint(keys[0], (NX, NY, NZ), 0, REGIONS), jax.random.fold_in(keys[0], 1), 0, REGIONS - 1).astype(jnp.int32)
    kappa_table = jnp.clip(jnp.exp(jax.random.uniform(keys[1], (REGIONS,), jnp.float32, math.log(0.5), math.log(2.0))), 0.5, 2.0)
    absorb_table = jnp.clip(jnp.exp(jax.random.uniform(keys[2], (REGIONS,), jnp.float32, math.log(0.02), math.log(0.1))), 0.02, 0.1)
    background = jnp.clip(jnp.exp(math.log(10.0) - 4.6051702 * jax.random.uniform(keys[3], (SOURCES, NX, NY, NZ), jnp.float32) ** steps_of(keys[3], (SOURCES, NX, NY, NZ), ((0, 4), (1, 2), (2, 4)), -0.2, 0.2)), 0.1, 10.0)
    det_cells = place_ends(jax.random.randint(keys[4], (DETS,), 0, NX * NY * NZ), jax.random.fold_in(keys[4], 1), 0, (NX * NY * NZ) - 1).astype(jnp.int32)
    v_kappa = normal_values(keys[5], (NX, NY, NZ), 1.0, 6.0, ((0, 2), (1, 4), (2, 4)), jnp.float32)
    v_absorb = normal_values(keys[6], (NX, NY, NZ), 1.0, 6.0, ((0, 2), (1, 4), (2, 4)), jnp.float32)
    q_kappa = normal_values(keys[7], (NX, NY, NZ), 1.0, 6.0, ((0, 2), (1, 4), (2, 4)), jnp.float32)
    q_absorb = normal_values(keys[8], (NX, NY, NZ), 1.0, 6.0, ((0, 2), (1, 4), (2, 4)), jnp.float32)
    beta_prev = jnp.clip(jnp.exp(jax.random.uniform(keys[9], (1,), jnp.float32, math.log(0.2), math.log(2.0))), 0.2, 2.0)
    return dict(labels=labels, kappa_table=kappa_table, absorb_table=absorb_table, background=background, det_cells=det_cells, v_kappa=v_kappa, v_absorb=v_absorb, q_kappa=q_kappa, q_absorb=q_absorb, beta_prev=beta_prev)


lam_low = 0.02
lam_high = 24.1
eps_norm = 1e-06

def regional(labels, table):
    field = jnp.zeros(labels.shape, jnp.float32)
    for region in range(REGIONS):
        field = field + jnp.where(labels == region, table[region], 0.0)
    return field

def beside(field):
    padded = jnp.pad(field, 1)
    return [padded[2:, 1:-1, 1:-1], padded[:-2, 1:-1, 1:-1], padded[1:-1, 2:, 1:-1], padded[1:-1, :-2, 1:-1], padded[1:-1, 1:-1, 2:], padded[1:-1, 1:-1, :-2]]

def chebyshev(rhs, apply_op):
    theta = 0.5 * (lam_high + lam_low)
    delta = 0.5 * (lam_high - lam_low)
    sigma = theta / delta
    rho = 1.0 / sigma
    solution = jnp.zeros_like(rhs)
    remain = rhs
    step_dir = rhs / theta
    for step in range(ITERS):
        solution = solution + step_dir
        if step + 1 < ITERS:
            remain = remain - apply_op(step_dir)
            rho_next = 1.0 / (2.0 * sigma - rho)
            step_dir = rho_next * rho * step_dir + 2.0 * rho_next / delta * remain
            rho = rho_next
    return solution

def reference(labels, kappa_table, absorb_table, background, det_cells, v_kappa, v_absorb, q_kappa, q_absorb, beta_prev):
    kappa = regional(labels, kappa_table)
    absorb = regional(labels, absorb_table)
    kappa_faces = [0.5 * (kappa + near) for near in beside(kappa)]
    vk_faces = [0.5 * (v_kappa + near) for near in beside(v_kappa)]

    def apply_op(field):
        result = absorb * field
        for face, near in zip(kappa_faces, beside(field)):
            result = result + face * (field - near)
        return result

    def one_source(carry, phi):
        rhs = v_absorb * phi
        for face, near in zip(vk_faces, beside(phi)):
            rhs = rhs + face * (phi - near)
        rhs = -rhs
        change = chebyshev(rhs, apply_op)
        seen = change.reshape(-1)[det_cells]
        base = phi.reshape(-1)[det_cells]
        total = jnp.sum(base)
        mean_base = total / DETS
        ratio = base / total
        jv_vals = (seen - ratio * jnp.sum(seen)) / mean_base
        weight = (jv_vals - jnp.sum(ratio * jv_vals)) / mean_base
        source = jnp.zeros((CELLS,), jnp.float32).at[det_cells].add(weight).reshape(phi.shape)
        dual = chebyshev(source, apply_op)
        grad_a = -phi * dual
        grad_k = jnp.zeros_like(phi)
        for near_phi, near_dual in zip(beside(phi), beside(dual)):
            grad_k = grad_k - 0.5 * (phi - near_phi) * (dual - near_dual)
        return ((carry[0] + grad_k, carry[1] + grad_a), None)
    zero_field = jnp.zeros_like(kappa)
    (hv_k, hv_a), _ = lax.scan(one_source, (zero_field, zero_field), background)
    w_k = hv_k - beta_prev[0] * q_kappa
    w_a = hv_a - beta_prev[0] * q_absorb
    wv_mean = (jnp.sum(w_k * v_kappa) + jnp.sum(w_a * v_absorb)) / CELLS
    vv_mean = (jnp.sum(v_kappa * v_kappa) + jnp.sum(v_absorb * v_absorb)) / CELLS
    alpha = wv_mean / (vv_mean + eps_norm)
    r_k = w_k - alpha * v_kappa
    r_a = w_a - alpha * v_absorb
    rr_mean = (jnp.sum(r_k * r_k) + jnp.sum(r_a * r_a)) / CELLS
    beta = jnp.sqrt(rr_mean + eps_norm)
    return (r_k / beta, r_a / beta, jnp.stack([alpha, beta]))
```

```python
import functools

import jax
import jax.numpy as jnp
from jax import lax
from jax.experimental import pallas as pl
from jax.experimental.pallas import tpu as pltpu
from jax.sharding import PartitionSpec as P

ITERS = 6


lam_low = 0.02
lam_high = 24.1
eps_norm = 1e-06


def padded_2(block, sides, width):
    for axis, dim in sides:
        count = lax.axis_size(axis)
        forward = [(i, i + 1) for i in range(count - 1)]
        backward = [(target, source) for source, target in forward]
        low = lax.ppermute(
            lax.slice_in_dim(block, block.shape[dim] - width, None, axis=dim), axis, forward
        )
        high = lax.ppermute(lax.slice_in_dim(block, 0, width, axis=dim), axis, backward)
        block = jnp.concatenate([low, block, high], axis=dim)
    return block


def regional(labels, table):
    field = jnp.zeros(labels.shape, jnp.float32)
    for region in range(table.shape[0]):
        field = field + jnp.where(labels == region, table[region], 0.0)
    return field


def beside(padded):
    widths = [(0, 0)] * (padded.ndim - 1) + [(1, 1)]
    full = jnp.pad(padded, widths)
    return [
        full[..., 2:, 1:-1, 1:-1],
        full[..., :-2, 1:-1, 1:-1],
        full[..., 1:-1, 2:, 1:-1],
        full[..., 1:-1, :-2, 1:-1],
        full[..., 1:-1, 1:-1, 2:],
        full[..., 1:-1, 1:-1, :-2],
    ]


def chebyshev(rhs, apply_op):
    theta = 0.5 * (lam_high + lam_low)
    delta = 0.5 * (lam_high - lam_low)
    sigma = theta / delta
    rho = 1.0 / sigma
    solution = jnp.zeros_like(rhs)
    remain = rhs
    step_dir = rhs / theta
    for step in range(ITERS):
        solution = solution + step_dir
        if step + 1 < ITERS:
            remain = remain - apply_op(step_dir)
            rho_next = 1.0 / (2.0 * sigma - rho)
            step_dir = rho_next * rho * step_dir + 2.0 * rho_next / delta * remain
            rho = rho_next
    return solution


def per_device(
    labels,
    kappa_table,
    absorb_table,
    background,
    det_cells,
    v_kappa,
    v_absorb,
    q_kappa,
    q_absorb,
    beta_prev,
):
    sources, cx, cy, cz = background.shape
    kappa = regional(labels, kappa_table)
    absorb = regional(labels, absorb_table)
    full_k, full_a = (
        lax.all_gather(v_kappa, "src", axis=2, tiled=True),
        lax.all_gather(v_absorb, "src", axis=2, tiled=True),
    )
    stacked = jnp.concatenate([background, kappa[None], full_k[None]], axis=0)
    rims = padded_2(stacked, (("gx", 1), ("gy", 2)), 1)
    near_all = beside(rims)
    kappa_faces = [0.5 * (kappa + near[sources]) for near in near_all]
    vk_faces = [0.5 * (full_k + near[sources + 1]) for near in near_all]
    phi_near = [near[:sources] for near in near_all]

    def apply_op(field):
        padded = padded_2(field, (("gx", 1), ("gy", 2)), 1)
        result = absorb * field
        for face, near in zip(kappa_faces, beside(padded)):
            result = result + face * (field - near)
        return result

    rhs = full_a * background
    for face, near in zip(vk_faces, phi_near):
        rhs = rhs + face * (background - near)
    rhs = -rhs
    change = chebyshev(rhs, apply_op)
    span_y = cy * lax.axis_size("gy")
    ix = det_cells // (span_y * cz)
    iy = det_cells // cz % span_y
    iz = det_cells % cz
    anchor_x = lax.axis_index("gx") * cx
    anchor_y = lax.axis_index("gy") * cy
    owned = (ix >= anchor_x) & (ix < anchor_x + cx) & (iy >= anchor_y) & (iy < anchor_y + cy)
    local = jnp.where(owned, ((ix - anchor_x) * cy + (iy - anchor_y)) * cz + iz, 0)
    seen_part = jnp.where(owned[None, :], change.reshape(sources, -1)[:, local], 0.0)
    base_part = jnp.where(owned[None, :], background.reshape(sources, -1)[:, local], 0.0)
    seen, base = lax.psum((seen_part, base_part), ("gx", "gy"))
    total = jnp.sum(base, axis=1, keepdims=True)
    mean_base = total / det_cells.shape[0]
    ratio = base / total
    jv_vals = (seen - ratio * jnp.sum(seen, axis=1, keepdims=True)) / mean_base
    weight = (jv_vals - jnp.sum(ratio * jv_vals, axis=1, keepdims=True)) / mean_base
    deposit = jnp.where(owned[None, :], weight, 0.0)
    source = (
        jnp.zeros((sources, cx * cy * cz), jnp.float32)
        .at[:, local]
        .add(deposit)
        .reshape(change.shape)
    )
    dual = chebyshev(source, apply_op)
    dual_rims = padded_2(dual, (("gx", 1), ("gy", 2)), 1)
    grad_a = -jnp.sum(background * dual, axis=0)
    grad_k = jnp.zeros_like(kappa)
    for near_phi, near_dual in zip(phi_near, beside(dual_rims)):
        grad_k = grad_k - 0.5 * jnp.sum((background - near_phi) * (dual - near_dual), axis=0)
    summed_k, summed_a = lax.psum((grad_k, grad_a), "src")
    slab = v_kappa.shape[2]
    offset = lax.axis_index("src") * slab
    hv_k = lax.dynamic_slice_in_dim(summed_k, offset, slab, 2)
    hv_a = lax.dynamic_slice_in_dim(summed_a, offset, slab, 2)
    cell_count = cx * lax.axis_size("gx") * cy * lax.axis_size("gy") * cz
    w_k = hv_k - beta_prev[0] * q_kappa
    w_a = hv_a - beta_prev[0] * q_absorb
    local_wv = jnp.sum(w_k * v_kappa) + jnp.sum(w_a * v_absorb)
    local_vv = jnp.sum(v_kappa * v_kappa) + jnp.sum(v_absorb * v_absorb)
    wv_sum, vv_sum = lax.psum((local_wv, local_vv), ("src", "gx", "gy"))
    alpha = wv_sum / cell_count / (vv_sum / cell_count + eps_norm)
    r_k = w_k - alpha * v_kappa
    r_a = w_a - alpha * v_absorb
    rr_sum = lax.psum(jnp.sum(r_k * r_k) + jnp.sum(r_a * r_a), ("src", "gx", "gy"))
    beta = jnp.sqrt(rr_sum / cell_count + eps_norm)
    return (r_k / beta, r_a / beta, jnp.stack([alpha, beta]))


def chebyshev_scalars():
    theta = 0.5 * (lam_high + lam_low)
    delta = 0.5 * (lam_high - lam_low)
    sigma = theta / delta
    rho = 1.0 / sigma
    pairs = []
    for _ in range(ITERS - 1):
        rho_next = 1.0 / (2.0 * sigma - rho)
        pairs.append((rho_next * rho, 2.0 * rho_next / delta))
        rho = rho_next
    return theta, pairs


def places(split):
    g = lax.axis_index("gy")
    return lax.axis_index("src"), lax.axis_index("gx"), g // split, g % split


def shifted(value, step, axis):
    return pltpu.roll(value, step % value.shape[axis], axis)


def index_along(shape, axis):
    return lax.broadcasted_iota(jnp.int32, shape, axis)


def beyond(value, step, axis):
    size = value.shape[axis]
    at = index_along(value.shape, axis)
    edge = size - 1 if step == 1 else 0
    return jnp.where(at == edge, 0.0, shifted(value, -step, axis))


def pack_kernel(bg, labels, vk, va, packed, message):
    _, x, _, _ = places(2)
    half = bg.shape[0] // 2
    for i in range(half):
        message[i] = bg[half * (1 - x) + i]
    message[half] = labels[...].astype(jnp.float32)
    per = 128 // vk.shape[2]
    for f, ref in enumerate((vk, va)):
        for q in range(ref.shape[0] // per):
            packed[f, q] = jnp.concatenate([ref[per * q + j] for j in range(per)], axis=1)


def count_kernel(dets, count, *, ny, nz, half, halo):
    _, _, y, _ = places(2)
    planes, rows, _ = count.shape
    flat = dets[...]
    iz = flat % nz
    line = flat // nz
    iy = line % ny
    ix = line // ny
    row = iy - (half - halo) * y
    spot = jnp.where((row >= 0) & (row < rows), ix * rows + row, -1)
    dets_n = flat.shape[1]
    at_z = (index_along((nz, dets_n), 0) == iz).astype(jnp.float32).astype(jnp.bfloat16)

    def body(i, carry):
        here = index_along((2 * rows, dets_n), 0) + i * (2 * rows)
        hot = (here == spot).astype(jnp.float32).astype(jnp.bfloat16)
        found = lax.dot_general(hot, at_z, (((1,), (1,)), ((), ())), preferred_element_type=jnp.float32)
        count[pl.ds(2 * i, 2)] = found.reshape(2, rows, nz)
        return carry

    lax.fori_loop(0, planes // 2, body, 0)


def gather_kernel(*refs, n):
    bg, labels, msg = refs[:3]
    own_v, other_v = refs[3 : 3 + n], refs[3 + n : 3 + 2 * n]
    mine, fields, edge_other, edge_mine = refs[3 + 2 * n :]
    s, x, y, c = places(2)
    half = bg.shape[0] // 2
    cx, cy, _ = labels.shape
    here, there = cx * x, cx * (1 - x)
    mine[pl.ds(here, cx)] = bg[half * x + c]
    mine[pl.ds(there, cx)] = msg[c]
    fields[0, pl.ds(here, cx)] = bg[half * x + 1 - c]
    fields[0, pl.ds(there, cx)] = msg[1 - c]
    fields[1, pl.ds(here, cx)] = labels[...].astype(jnp.float32)
    fields[1, pl.ds(there, cx)] = msg[half]
    slab = 128 // n
    lane = index_along((cy, 128), 1) // slab
    for start, parts in ((here, own_v), (there, other_v)):
        for f in range(2):
            for q in range(cx // n):
                blocks = [part[f, q] for part in parts]
                for j in range(n):
                    plane = jnp.zeros((cy, 128), jnp.float32)
                    for k in range(n):
                        home = (s - k + n) % n
                        moved = pltpu.roll(blocks[k], ((home - j + n) % n) * slab, 1)
                        plane = jnp.where(lane == home, moved, plane)
                    fields[2 + f, start + n * q + j] = plane
    halo = edge_mine.shape[2]
    first = (cy - halo) * (1 - y)
    edge_other[...] = fields[:, :, pl.ds(first, halo), :]
    edge_mine[0] = mine[:, pl.ds(first, halo), :]
    edge_mine[1:] = fields[1:, :, pl.ds(first, halo), :]


def solve(rem, sol, dirs, diag, fx, fy, fz):
    planes = rem.shape[0]
    _, pairs = chebyshev_scalars()
    for step, (keep, push) in enumerate(pairs):
        src, dst = dirs[step % 2], dirs[(step + 1) % 2]
        last = step + 1 == len(pairs)

        def body(i, carry):
            d = src[i + 1]
            coef_y, coef_z = fy[i], fz[i]
            left = rem[i] - diag[i] * d
            left = left + fx[i] * src[i] + fx[i + 1] * src[i + 2]
            left = left + coef_y * shifted(d, -1, 0) + shifted(coef_y * d, 1, 0)
            left = left + coef_z * shifted(d, -1, 1) + shifted(coef_z * d, 1, 1)
            d = keep * d + push * left
            sol[i] = sol[i] + d
            if not last:
                rem[i] = left
                dst[i + 1] = d
            return carry

        lax.fori_loop(0, planes, body, 0, unroll=2)


def folded(value):
    return jnp.sum(value.reshape(-1, 8, value.shape[1]), axis=0)


def first_kernel(
    kap_table, abs_table, mine, fields, got, edge_other, edge_mine, count,
    phi, sol, diag, fx, fy, fz, message,
    labels, vk, va, kap, rem, dir_a, dir_b,
):
    _, _, y, c = places(2)
    planes, cy, lanes = mine.shape
    halo = edge_mine.shape[2]
    rows = 2 * cy + halo
    base = halo * y
    for f, (ref, own, shift) in enumerate(
        ((phi, mine, 0), (labels, fields.at[1], 0), (vk, fields.at[2], 1), (va, fields.at[3], 0))
    ):
        there = pl.ds(shift, planes)
        ref[there, pl.ds(base + cy * c, cy), :] = own[...]
        ref[there, pl.ds(base + cy * (1 - c), cy), :] = got[f]
        ref[there, pl.ds(2 * cy * (1 - y), halo), :] = edge_other[f] + edge_mine[f]
    blank = jnp.zeros((rows, lanes), jnp.float32)
    for ref in (kap, vk, dir_a, dir_b):
        ref[0] = blank
        ref[planes + 1] = blank

    lane = index_along((rows, lanes), 1)
    kap_row, abs_row = blank, blank
    for region in range(kap_table.shape[0]):
        kap_row = jnp.where(lane == region, kap_table[region], kap_row)
        abs_row = jnp.where(lane == region, abs_table[region], abs_row)

    def look_up(i, carry):
        at = labels[i].astype(jnp.int32)
        kap[i + 1] = jnp.take_along_axis(kap_row, at, axis=1)
        diag[i] = jnp.take_along_axis(abs_row, at, axis=1)
        return carry

    lax.fori_loop(0, planes, look_up, 0)
    fx[0] = 0.5 * kap[1]
    theta, _ = chebyshev_scalars()

    def set_up(i, carry):
        k = kap[i + 1]
        along_x = 0.5 * (k + kap[i + 2])
        k_y, k_z = beyond(k, 1, 0), beyond(k, 1, 1)
        along_y, along_z = 0.5 * (k + k_y), 0.5 * (k + k_z)
        fx[i + 1] = along_x
        fy[i] = jnp.where(index_along(k.shape, 0) == rows - 1, 0.0, along_y)
        fz[i] = jnp.where(lane == lanes - 1, 0.0, along_z)
        back_y, back_z = 0.5 * (k + beyond(k, -1, 0)), 0.5 * (k + beyond(k, -1, 1))
        diag[i] = diag[i] + fx[i] + along_x + along_y + back_y + along_z + back_z
        v, p = vk[i + 1], phi[i]
        low_v, low_p = vk[i], phi[jnp.maximum(i - 1, 0)] * jnp.where(i > 0, 1.0, 0.0)
        high_v = vk[i + 2]
        high_p = phi[jnp.minimum(i + 1, planes - 1)] * jnp.where(i < planes - 1, 1.0, 0.0)
        total = va[i] * p + 0.5 * (v + low_v) * (p - low_p) + 0.5 * (v + high_v) * (p - high_p)
        for axis in range(2):
            for way in (1, -1):
                total = total + 0.5 * (v + beyond(v, way, axis)) * (p - beyond(p, way, axis))
        rem[i] = -total
        d = total * (-1.0 / theta)
        sol[i] = d
        dir_a[i + 1] = d
        return carry

    lax.fori_loop(0, planes, set_up, 0)
    solve(rem, sol, (dir_a, dir_b), diag, fx, fy, fz)

    at_row = index_along((rows, lanes), 0)
    owned = (at_row >= base) & (at_row < base + 2 * cy)

    def add_up(i, sums):
        n = jnp.where(owned, count[i], 0.0)
        p, u = phi[i], sol[i]
        np_ = n * p
        parts = (np_, n * u, np_ * u, np_ * p)
        return tuple(total + folded(part) for total, part in zip(sums, parts))

    zero = jnp.zeros((8, lanes), jnp.float32)
    sums = lax.fori_loop(0, planes, add_up, (zero,) * 4)
    message[pl.ds(0, planes)] = sol[:, pl.ds((2 * cy - halo) * (1 - y) + halo * y, halo), :]
    for i, part in enumerate(sums):
        message[planes + i] = part


def second_kernel(
    phi, change, diag, fx, fy, fz, count, sent, came,
    own, message,
    rem, sol, dir_a, dir_b, pad,
    *, dets,
):
    _, _, y, c = places(2)
    planes, rows, lanes = phi.shape
    halo = came.shape[1]
    cy = (rows - halo) // 2
    base = halo * y
    edge = 2 * cy * (1 - y)
    total, seen_sum, cross, square = (
        jnp.sum(sent[planes + i] + came[planes + i]) for i in range(4)
    )
    one = jnp.ones((1, 1), jnp.float32)
    total, seen_sum = total * one, seen_sum * one
    mean = total / dets
    part = seen_sum / total
    level = (cross - part * square) / (total * mean)
    inverse = 1.0 / mean
    blank = jnp.zeros((rows, lanes), jnp.float32)
    for ref in (dir_a, dir_b, pad):
        ref[0] = blank
        ref[planes + 1] = blank
    theta, _ = chebyshev_scalars()
    sol[...] = change[...]
    sol[:, pl.ds(edge, halo), :] = came[pl.ds(0, planes)]

    def set_up(i, carry):
        p = phi[i]
        jv = (sol[i] - p * part) * inverse
        b = count[i] * ((jv - level) * inverse)
        rem[i] = b
        d = b * (1.0 / theta)
        sol[i] = d
        dir_a[i + 1] = d
        pad[i + 1] = p
        return carry

    lax.fori_loop(0, planes, set_up, 0)
    solve(rem, sol, (dir_a, dir_b), diag, fx, fy, fz)
    dual = dir_a

    def keep(i, carry):
        dual[i + 1] = sol[i]
        return carry

    lax.fori_loop(0, planes, keep, 0)

    def product(i, carry):
        p, u = pad[i + 1], dual[i + 1]
        grad = (p - pad[i]) * (u - dual[i]) + (p - pad[i + 2]) * (u - dual[i + 2])
        for axis in range(2):
            for way in (1, -1):
                grad = grad + (p - beyond(p, way, axis)) * (u - beyond(u, way, axis))
        rem[i] = -0.5 * grad
        sol[i] = -(p * u)
        return carry

    lax.fori_loop(0, planes, product, 0)
    for f, ref in enumerate((rem, sol)):
        own[f] = ref[:, pl.ds(base + cy * c, cy), :]
        message[f] = ref[:, pl.ds(base + cy * (1 - c), cy), :]


def core_kernel(own, came, kept, message):
    _, x, _, _ = places(2)
    cx = kept.shape[1]
    kept[...] = own[:, pl.ds(cx * x, cx)] + came[:, pl.ds(cx * x, cx)]
    message[...] = own[:, pl.ds(cx * (1 - x), cx)] + came[:, pl.ds(cx * (1 - x), cx)]


def slab_kernel(kept, came, *outs):
    s, _, _, _ = places(2)
    n = len(outs)
    slab = 128 // n
    _, cx, cy, _ = kept.shape
    lane = index_along((cy, 128), 1) // slab
    for f in range(2):
        for q in range(cx // n):
            planes = [kept[f, n * q + j] + came[f, n * q + j] for j in range(n)]
            for k in range(n):
                to = (s + k) % n
                piece = jnp.zeros((cy, 128), jnp.float32)
                for j in range(n):
                    moved = pltpu.roll(planes[j], ((j - to + n) % n) * slab, 1)
                    piece = jnp.where(lane == j, moved, piece)
                outs[k][f, q] = piece


def project_kernel(*refs, n):
    beta_prev = refs[0]
    parts = refs[1 : 1 + n]
    vk, va, qk, qa, w_k, w_a, tile = refs[1 + n :]
    s, x, y, c = places(2)
    slab = 128 // n
    for f, (q_ref, w) in enumerate(((qk, w_k), (qa, w_a))):
        for q in range(vk.shape[0] // n):
            whole = sum(part[f, q] for part in parts[1:]) + parts[0][f, q]
            for j in range(n):
                i = n * q + j
                w[i] = whole[:, slab * j : slab * (j + 1)] - beta_prev[0] * q_ref[i]

    def dot(a, b):
        return jnp.sum(jnp.sum(a * b, axis=0))

    wk, wa, v_k, v_a = w_k[...], w_a[...], vk[...], va[...]
    one = jnp.ones((1, 1), jnp.float32)
    wv = (dot(wk, v_k) + dot(wa, v_a)) * one
    vv = (dot(v_k, v_k) + dot(v_a, v_a)) * one
    a = jnp.where(vv > 0.0, wv / jnp.where(vv > 0.0, vv, 1.0), 0.0)
    u_k, u_a = wk - a * v_k, wa - a * v_a
    uv = (dot(u_k, v_k) + dot(u_a, v_a)) * one
    uu = (dot(u_k, u_k) + dot(u_a, u_a)) * one
    me = ((s * 2 + x) * 2 + y) * 2 + c
    lane = index_along((8, 128), 1)
    row = index_along((8, 128), 0)
    values = jnp.zeros((8, 128), jnp.float32)
    for i, value in enumerate((wv, vv, a, uv, uu)):
        values = jnp.where(row == i, value, values)
    tile[...] = jnp.where(lane == me, values, 0.0)


def final_kernel(*refs, cells):
    tiles, (w_k, w_a, vk, va, next_k, next_a, coefs) = refs[:-7], refs[-7:]
    tile = tiles[0][...]
    for other in tiles[1:]:
        tile = tile + other[...]
    wv, vv, a, uv, uu = (tile[i : i + 1] for i in range(5))
    wv_sum = jnp.sum(wv, axis=1, keepdims=True)
    vv_sum = jnp.sum(vv, axis=1, keepdims=True)
    alpha = wv_sum / cells / (vv_sum / cells + eps_norm)
    off = alpha - a
    rr = jnp.sum(uu - 2.0 * off * uv + off * off * vv, axis=1, keepdims=True)
    beta = jnp.sqrt(rr / cells + eps_norm)
    next_k[...] = (w_k[...] - alpha * vk[...]) / beta
    next_a[...] = (w_a[...] - alpha * va[...]) / beta
    coefs[0] = jnp.sum(alpha)
    coefs[1] = jnp.sum(beta)


def f32(*shape):
    return jax.ShapeDtypeStruct(shape, jnp.float32)


def run(kernel, outs, *args, scratch=(), smem=(), mib=16, in_smem_out=(), cost=None):
    vmem = pl.BlockSpec(memory_space=pltpu.VMEM)
    scalar = pl.BlockSpec(memory_space=pltpu.SMEM)
    return pl.pallas_call(
        kernel,
        out_shape=tuple(outs),
        in_specs=[scalar if i in smem else vmem for i in range(len(args))],
        out_specs=tuple(scalar if i in in_smem_out else vmem for i in range(len(outs))),
        scratch_shapes=[pltpu.VMEM(shape, jnp.float32) for shape in scratch],
        compiler_params=pltpu.CompilerParams(vmem_limit_bytes=mib * 2**20),
        cost_estimate=cost,
    )(*args)


HALO = 8


def per_device_paired(
    labels, kappa_table, absorb_table, background, det_cells,
    v_kappa, v_absorb, q_kappa, q_absorb, beta_prev,
):
    sources, cx, cy, cz = background.shape
    n = lax.axis_size("src")
    planes, rows = 2 * cx, 2 * cy + HALO
    ny = cy * lax.axis_size("gy")
    dets = det_cells.shape[0]
    cells = planes * ny * cz
    groups = cx // n

    def swap_x(value):
        return lax.ppermute(value, "gx", [(0, 1), (1, 0)])

    def swap_core(value):
        return lax.ppermute(value, "gy", [(0, 1), (1, 0), (2, 3), (3, 2)])

    def along_z(value, k):
        return lax.ppermute(value, "src", [(i, (i + k) % n) for i in range(n)])

    packed, message = run(
        pack_kernel, (f32(2, groups, cy, cz), f32(sources // 2 + 1, cx, cy, cz)),
        background, labels, v_kappa, v_absorb,
    )
    other = swap_x(packed)
    came = swap_x(message)
    own_v = [packed] + [along_z(packed, k) for k in range(1, n)]
    other_v = [other] + [along_z(other, k) for k in range(1, n)]
    (count,) = run(
        functools.partial(count_kernel, ny=ny, nz=cz, half=2 * cy, halo=HALO),
        (f32(planes, rows, cz),), det_cells.reshape(1, dets),
        cost=pl.CostEstimate(flops=2 * planes * rows * cz * dets, bytes_accessed=planes * rows * cz * 4, transcendentals=0),
    )
    mine, fields, edge_other, edge_mine = run(
        functools.partial(gather_kernel, n=n),
        (f32(planes, cy, cz), f32(4, planes, cy, cz), f32(4, planes, HALO, cz), f32(4, planes, HALO, cz)),
        background, labels, came, *own_v, *other_v,
    )
    edge_other = lax.ppermute(edge_other, "gy", [(1, 2), (2, 1)])
    edge_mine = lax.ppermute(edge_mine, "gy", [(1, 3), (2, 0)])
    got = swap_core(fields)
    frame = (planes, rows, cz)
    wide = (planes + 2, rows, cz)
    phi, change, diag, fx, fy, fz, sent = run(
        first_kernel,
        (f32(*frame), f32(*frame), f32(*frame), f32(planes + 1, rows, cz), f32(*frame), f32(*frame),
         f32(planes + 4, HALO, cz)),
        kappa_table, absorb_table, mine, fields, got, edge_other, edge_mine, count,
        smem=(0, 1), scratch=(frame, wide, frame, wide, frame, wide, wide), mib=24,
    )
    heard = lax.ppermute(sent, "gy", [(i, (i + 2) % 4) for i in range(4)])
    own, message = run(
        functools.partial(second_kernel, dets=dets),
        (f32(2, planes, cy, cz), f32(2, planes, cy, cz)),
        phi, change, diag, fx, fy, fz, count, sent, heard,
        scratch=(frame, frame, wide, wide, wide), mib=24,
    )
    kept, message = run(
        core_kernel, (f32(2, cx, cy, cz), f32(2, cx, cy, cz)), own, swap_core(message)
    )
    pieces = run(
        slab_kernel, [f32(2, groups, cy, cz)] * n, kept, swap_x(message)
    )
    parts = [pieces[0]] + [along_z(pieces[k], k) for k in range(1, n)]
    w_k, w_a, tile = run(
        functools.partial(project_kernel, n=n),
        (f32(*v_kappa.shape), f32(*v_kappa.shape), f32(8, 128)),
        beta_prev, *parts, v_kappa, v_absorb, q_kappa, q_absorb, smem=(0,),
    )
    tile = tile + sum(along_z(tile, k) for k in range(1, n))
    over_x, over_core = swap_x(tile), swap_core(tile)
    over_both = lax.ppermute(
        tile, ("gx", "gy"), [(4 * a + b, 4 * (1 - a) + (b ^ 1)) for a in range(2) for b in range(4)]
    )
    tile = tile + over_x + over_core + over_both
    over_y = lax.ppermute(tile, "gy", [(i, (i + 2) % 4) for i in range(4)])
    return tuple(run(
        functools.partial(final_kernel, cells=cells),
        (f32(*v_kappa.shape), f32(*v_kappa.shape), f32(2)),
        tile, over_y, w_k, w_a, v_kappa, v_absorb, in_smem_out=(2,),
    ))


def paired_fits(mesh):
    return mesh.shape["gx"] == 2 and mesh.shape["gy"] == 4


def body_for(mesh):
    if not paired_fits(mesh):
        return per_device

    def chosen(*args):
        sources, cx, cy, cz = args[3].shape
        n = lax.axis_size("src")
        fits = sources == 4 and cz == 128 and cx % n == 0 and cz % n == 0 and cy % HALO == 0
        devices = 8 * n
        return (per_device_paired if fits and devices <= 128 else per_device)(*args)

    return chosen


def solution(mesh):
    return jax.shard_map(
        body_for(mesh),
        mesh=mesh,
        in_specs=(
            P("gx", "gy", None),
            P(),
            P(),
            P("src", "gx", "gy", None),
            P(),
            P("gx", "gy", "src"),
            P("gx", "gy", "src"),
            P("gx", "gy", "src"),
            P("gx", "gy", "src"),
            P(),
        ),
        out_specs=(P("gx", "gy", "src"), P("gx", "gy", "src"), P()),
        check_vma=False,
    )
```

```python
import functools

import jax
import jax.numpy as jnp
from jax import lax
from jax.experimental import pallas as pl
from jax.experimental.pallas import tpu as pltpu
from jax.sharding import PartitionSpec as P

ITERS = 6


lam_low = 0.02
lam_high = 24.1
eps_norm = 1e-06


def padded_2(block, sides, width):
    for axis, dim in sides:
        count = lax.axis_size(axis)
        forward = [(i, i + 1) for i in range(count - 1)]
        backward = [(target, source) for source, target in forward]
        low = lax.ppermute(
            lax.slice_in_dim(block, block.shape[dim] - width, None, axis=dim), axis, forward
        )
        high = lax.ppermute(lax.slice_in_dim(block, 0, width, axis=dim), axis, backward)
        block = jnp.concatenate([low, block, high], axis=dim)
    return block


def regional(labels, table):
    field = jnp.zeros(labels.shape, jnp.float32)
    for region in range(table.shape[0]):
        field = field + jnp.where(labels == region, table[region], 0.0)
    return field


def beside(padded):
    widths = [(0, 0)] * (padded.ndim - 1) + [(1, 1)]
    full = jnp.pad(padded, widths)
    return [
        full[..., 2:, 1:-1, 1:-1],
        full[..., :-2, 1:-1, 1:-1],
        full[..., 1:-1, 2:, 1:-1],
        full[..., 1:-1, :-2, 1:-1],
        full[..., 1:-1, 1:-1, 2:],
        full[..., 1:-1, 1:-1, :-2],
    ]


def chebyshev(rhs, apply_op):
    theta = 0.5 * (lam_high + lam_low)
    delta = 0.5 * (lam_high - lam_low)
    sigma = theta / delta
    rho = 1.0 / sigma
    solution = jnp.zeros_like(rhs)
    remain = rhs
    step_dir = rhs / theta
    for step in range(ITERS):
        solution = solution + step_dir
        if step + 1 < ITERS:
            remain = remain - apply_op(step_dir)
            rho_next = 1.0 / (2.0 * sigma - rho)
            step_dir = rho_next * rho * step_dir + 2.0 * rho_next / delta * remain
            rho = rho_next
    return solution


def per_device(
    labels,
    kappa_table,
    absorb_table,
    background,
    det_cells,
    v_kappa,
    v_absorb,
    q_kappa,
    q_absorb,
    beta_prev,
):
    sources, cx, cy, cz = background.shape
    kappa = regional(labels, kappa_table)
    absorb = regional(labels, absorb_table)
    full_k, full_a = (
        lax.all_gather(v_kappa, "src", axis=2, tiled=True),
        lax.all_gather(v_absorb, "src", axis=2, tiled=True),
    )
    stacked = jnp.concatenate([background, kappa[None], full_k[None]], axis=0)
    rims = padded_2(stacked, (("gx", 1), ("gy", 2)), 1)
    near_all = beside(rims)
    kappa_faces = [0.5 * (kappa + near[sources]) for near in near_all]
    vk_faces = [0.5 * (full_k + near[sources + 1]) for near in near_all]
    phi_near = [near[:sources] for near in near_all]

    def apply_op(field):
        padded = padded_2(field, (("gx", 1), ("gy", 2)), 1)
        result = absorb * field
        for face, near in zip(kappa_faces, beside(padded)):
            result = result + face * (field - near)
        return result

    rhs = full_a * background
    for face, near in zip(vk_faces, phi_near):
        rhs = rhs + face * (background - near)
    rhs = -rhs
    change = chebyshev(rhs, apply_op)
    span_y = cy * lax.axis_size("gy")
    ix = det_cells // (span_y * cz)
    iy = det_cells // cz % span_y
    iz = det_cells % cz
    anchor_x = lax.axis_index("gx") * cx
    anchor_y = lax.axis_index("gy") * cy
    owned = (ix >= anchor_x) & (ix < anchor_x + cx) & (iy >= anchor_y) & (iy < anchor_y + cy)
    local = jnp.where(owned, ((ix - anchor_x) * cy + (iy - anchor_y)) * cz + iz, 0)
    seen_part = jnp.where(owned[None, :], change.reshape(sources, -1)[:, local], 0.0)
    base_part = jnp.where(owned[None, :], background.reshape(sources, -1)[:, local], 0.0)
    seen, base = lax.psum((seen_part, base_part), ("gx", "gy"))
    total = jnp.sum(base, axis=1, keepdims=True)
    mean_base = total / det_cells.shape[0]
    ratio = base / total
    jv_vals = (seen - ratio * jnp.sum(seen, axis=1, keepdims=True)) / mean_base
    weight = (jv_vals - jnp.sum(ratio * jv_vals, axis=1, keepdims=True)) / mean_base
    deposit = jnp.where(owned[None, :], weight, 0.0)
    source = (
        jnp.zeros((sources, cx * cy * cz), jnp.float32)
        .at[:, local]
        .add(deposit)
        .reshape(change.shape)
    )
    dual = chebyshev(source, apply_op)
    dual_rims = padded_2(dual, (("gx", 1), ("gy", 2)), 1)
    grad_a = -jnp.sum(background * dual, axis=0)
    grad_k = jnp.zeros_like(kappa)
    for near_phi, near_dual in zip(phi_near, beside(dual_rims)):
        grad_k = grad_k - 0.5 * jnp.sum((background - near_phi) * (dual - near_dual), axis=0)
    summed_k, summed_a = lax.psum((grad_k, grad_a), "src")
    slab = v_kappa.shape[2]
    offset = lax.axis_index("src") * slab
    hv_k = lax.dynamic_slice_in_dim(summed_k, offset, slab, 2)
    hv_a = lax.dynamic_slice_in_dim(summed_a, offset, slab, 2)
    cell_count = cx * lax.axis_size("gx") * cy * lax.axis_size("gy") * cz
    w_k = hv_k - beta_prev[0] * q_kappa
    w_a = hv_a - beta_prev[0] * q_absorb
    local_wv = jnp.sum(w_k * v_kappa) + jnp.sum(w_a * v_absorb)
    local_vv = jnp.sum(v_kappa * v_kappa) + jnp.sum(v_absorb * v_absorb)
    wv_sum, vv_sum = lax.psum((local_wv, local_vv), ("src", "gx", "gy"))
    alpha = wv_sum / cell_count / (vv_sum / cell_count + eps_norm)
    r_k = w_k - alpha * v_kappa
    r_a = w_a - alpha * v_absorb
    rr_sum = lax.psum(jnp.sum(r_k * r_k) + jnp.sum(r_a * r_a), ("src", "gx", "gy"))
    beta = jnp.sqrt(rr_sum / cell_count + eps_norm)
    return (r_k / beta, r_a / beta, jnp.stack([alpha, beta]))


def chebyshev_scalars():
    theta = 0.5 * (lam_high + lam_low)
    delta = 0.5 * (lam_high - lam_low)
    sigma = theta / delta
    rho = 1.0 / sigma
    pairs = []
    for _ in range(ITERS - 1):
        rho_next = 1.0 / (2.0 * sigma - rho)
        pairs.append((rho_next * rho, 2.0 * rho_next / delta))
        rho = rho_next
    return theta, pairs


def places(split):
    g = lax.axis_index("gy")
    return lax.axis_index("src"), lax.axis_index("gx"), g // split, g % split


def shifted(value, step, axis):
    return pltpu.roll(value, step % value.shape[axis], axis)


def index_along(shape, axis):
    return lax.broadcasted_iota(jnp.int32, shape, axis)


def beyond(value, step, axis):
    size = value.shape[axis]
    at = index_along(value.shape, axis)
    edge = size - 1 if step == 1 else 0
    return jnp.where(at == edge, 0.0, shifted(value, -step, axis))


def pack_kernel(bg, labels, vk, va, packed, message, raw, v_in, sems):
    _, x, _, _ = places(2)
    half = bg.shape[0] // 2
    copies = [
        pltpu.make_async_copy(src, dst, sems.at[i])
        for i, (src, dst) in enumerate((
            (vk, v_in.at[0]),
            (va, v_in.at[1]),
            (bg.at[pl.ds(half * (1 - x), half)], message.at[pl.ds(0, half)]),
            (labels, raw),
        ))
    ]
    for copy in copies:
        copy.start()
    per = 128 // vk.shape[2]
    for f in range(2):
        copies[f].wait()
        for q in range(vk.shape[0] // per):
            packed[f, q] = jnp.concatenate([v_in[f, per * q + j] for j in range(per)], axis=1)
    copies[3].wait()
    message[half] = raw[...].astype(jnp.float32)
    copies[2].wait()


def count_kernel(dets, count, *, ny, nz, half, halo):
    _, _, y, _ = places(2)
    planes, rows, _ = count.shape
    flat = dets[...]
    iz = flat % nz
    line = flat // nz
    iy = line % ny
    ix = line // ny
    row = iy - (half - halo) * y
    spot = jnp.where((row >= 0) & (row < rows), ix * rows + row, -1)
    dets_n = flat.shape[1]
    at_z = (index_along((nz, dets_n), 0) == iz).astype(jnp.float32).astype(jnp.bfloat16)

    def body(i, carry):
        here = index_along((2 * rows, dets_n), 0) + i * (2 * rows)
        hot = (here == spot).astype(jnp.float32).astype(jnp.bfloat16)
        found = lax.dot_general(hot, at_z, (((1,), (1,)), ((), ())), preferred_element_type=jnp.float32)
        count[pl.ds(2 * i, 2)] = found.reshape(2, rows, nz)
        return carry

    lax.fori_loop(0, planes // 2, body, 0)


def photon_kernel(bg, labels, msg, mine, fields, edge_other, edge_mine, raw, sems):
    _, x, y, c = places(2)
    half = bg.shape[0] // 2
    cx, cy, _ = labels.shape
    here, there = cx * x, cx * (1 - x)
    copies = [
        pltpu.make_async_copy(src, dst, sems.at[i])
        for i, (src, dst) in enumerate((
            (bg.at[half * x + c], mine.at[pl.ds(here, cx)]),
            (bg.at[half * x + 1 - c], fields.at[0, pl.ds(here, cx)]),
            (labels, raw),
        ))
    ]
    for copy in copies:
        copy.start()
    mine[pl.ds(there, cx)] = msg[c]
    fields[0, pl.ds(there, cx)] = msg[1 - c]
    fields[1, pl.ds(there, cx)] = msg[half]
    for copy in copies:
        copy.wait()
    fields[1, pl.ds(here, cx)] = raw[...].astype(jnp.float32)
    halo = edge_mine.shape[2]
    first = (cy - halo) * (1 - y)
    edge_other[...] = fields[:, :, pl.ds(first, halo), :]
    edge_mine[0] = mine[:, pl.ds(first, halo), :]
    edge_mine[1] = fields[1, :, pl.ds(first, halo), :]


def unpack_kernel(*refs):
    parts, full = refs[:-1], refs[-1]
    n = len(parts)
    s, _, _, _ = places(2)
    slab = 128 // n
    _, cx, cy, _ = full.shape
    lane = index_along((cy, 128), 1) // slab
    for f in range(2):
        for q in range(cx // n):
            blocks = [part[f, q] for part in parts]
            for j in range(n):
                plane = jnp.zeros((cy, 128), jnp.float32)
                for k in range(n):
                    home = (s - k + n) % n
                    moved = pltpu.roll(blocks[k], ((home - j + n) % n) * slab, 1)
                    plane = jnp.where(lane == home, moved, plane)
                full[f, n * q + j] = plane


def vector_kernel(own, came, fields, edge):
    _, x, y, _ = places(2)
    cx, cy = own.shape[1:3]
    halo = edge.shape[2]
    first = (cy - halo) * (1 - y)
    for start, part in ((cx * x, own), (cx * (1 - x), came)):
        fields[:, pl.ds(start, cx)] = part[...]
        edge[:, pl.ds(start, cx)] = part[:, :, pl.ds(first, halo), :]


def solve(b, bufs, diag, fx, fy, fz, unroll):
    planes = b.shape[0]
    _, pairs = chebyshev_scalars()
    for step, (keep, push) in enumerate(pairs):
        src, dst = bufs[step % 2], bufs[(step + 1) % 2]

        def body(i, carry):
            u = src[i + 1]
            coef_y, coef_z = fy[i], fz[i]
            left = b[i] - diag[i] * u
            left = left + fx[i] * src[i] + fx[i + 1] * src[i + 2]
            left = left + coef_y * shifted(u, -1, 0) + shifted(coef_y * u, 1, 0)
            left = left + coef_z * shifted(u, -1, 1) + shifted(coef_z * u, 1, 1)
            change = u if step == 0 else u - dst[i + 1]
            dst[i + 1] = u + keep * change + push * left
            return carry

        lax.fori_loop(0, planes, body, 0, unroll=unroll)
    return bufs[len(pairs) % 2]


def folded(value):
    return jnp.sum(value.reshape(-1, 8, value.shape[1]), axis=0)


def framed(ref, shift, parts, planes, cy, halo, y, c):
    own, got, edge_a, edge_b = parts
    there = pl.ds(shift, planes)
    base = halo * y
    ref[there, pl.ds(base + cy * c, cy), :] = own
    ref[there, pl.ds(base + cy * (1 - c), cy), :] = got
    ref[there, pl.ds(2 * cy * (1 - y), halo), :] = edge_a + edge_b


def blank_ends(*refs):
    for ref in refs:
        blank = jnp.zeros(ref.shape[1:], jnp.float32)
        ref[0] = blank
        ref[ref.shape[0] - 1] = blank


def owned_rows(shape, base, count):
    at_row = index_along(shape, 0)
    return (at_row >= base) & (at_row < base + count)


def stencil_kernel(
    kap_table, abs_table, mine, fields, got, edge_other, edge_mine, count,
    phi, diag, fx, fy, fz, sums,
    labels, kap,
):
    _, _, y, c = places(2)
    planes, cy, lanes = mine.shape
    halo = edge_mine.shape[2]
    rows = 2 * cy + halo
    place = (planes, cy, halo, y, c)
    framed(phi, 1, (mine[...], got[0], edge_other[0], edge_mine[0]), *place)
    framed(labels, 0, (fields[1], got[1], edge_other[1], edge_mine[1]), *place)
    blank_ends(phi, kap)
    blank = jnp.zeros((rows, lanes), jnp.float32)
    lane = index_along((rows, lanes), 1)
    kap_row, abs_row = blank, blank
    for region in range(kap_table.shape[0]):
        kap_row = jnp.where(lane == region, kap_table[region], kap_row)
        abs_row = jnp.where(lane == region, abs_table[region], abs_row)

    def look_up(i, carry):
        at = labels[i].astype(jnp.int32)
        kap[i + 1] = jnp.take_along_axis(kap_row, at, axis=1)
        diag[i] = jnp.take_along_axis(abs_row, at, axis=1)
        return carry

    lax.fori_loop(0, planes, look_up, 0, unroll=2)
    fx[0] = 0.5 * kap[1]
    owned = owned_rows((rows, lanes), halo * y, 2 * cy)

    def set_up(i, carry):
        k = kap[i + 1]
        along_x = 0.5 * (k + kap[i + 2])
        along_y, along_z = 0.5 * (k + beyond(k, 1, 0)), 0.5 * (k + beyond(k, 1, 1))
        fx[i + 1] = along_x
        fy[i] = jnp.where(index_along(k.shape, 0) == rows - 1, 0.0, along_y)
        fz[i] = jnp.where(lane == lanes - 1, 0.0, along_z)
        back_y, back_z = 0.5 * (k + beyond(k, -1, 0)), 0.5 * (k + beyond(k, -1, 1))
        diag[i] = diag[i] + fx[i] + along_x + along_y + back_y + along_z + back_z
        p = phi[i + 1]
        part = jnp.where(owned, count[i], 0.0) * p
        return carry[0] + folded(part), carry[1] + folded(part * p)

    zero = jnp.zeros((8, lanes), jnp.float32)
    sums[0], sums[1] = lax.fori_loop(0, planes, set_up, (zero, zero), unroll=2)


def first_kernel(
    phi, diag, fx, fy, fz, count, sums, fields, got, edge_a, edge_b,
    change, message,
    vk, va, b, buf_a, buf_b,
):
    _, _, y, c = places(2)
    planes, rows, lanes = change.shape
    halo = edge_a.shape[2]
    cy = (rows - halo) // 2
    place = (planes, cy, halo, y, c)
    framed(vk, 1, (fields[0], got[0], edge_a[0], edge_b[0]), *place)
    framed(va, 0, (fields[1], got[1], edge_a[1], edge_b[1]), *place)
    blank_ends(vk, buf_a, buf_b)
    theta, _ = chebyshev_scalars()

    def set_up(i, carry):
        v, p = vk[i + 1], phi[i + 1]
        total = 0.5 * (v + vk[i]) * (p - phi[i]) + 0.5 * (v + vk[i + 2]) * (p - phi[i + 2])
        for axis in range(2):
            flow = 0.5 * (v + beyond(v, 1, axis)) * (p - beyond(p, 1, axis))
            first = index_along(v.shape, axis) == 0
            total = total + flow + jnp.where(first, 0.5 * v * p, -shifted(flow, 1, axis))
        total = -(va[i] * p + total)
        b[i] = total
        buf_a[i + 1] = total * (1.0 / theta)
        return carry

    lax.fori_loop(0, planes, set_up, 0, unroll=2)
    found = solve(b, (buf_a, buf_b), diag, fx, fy, fz, 8)
    owned = owned_rows((rows, lanes), halo * y, 2 * cy)

    def add_up(i, carry):
        u = found[i + 1]
        change[i] = u
        part = jnp.where(owned, count[i], 0.0) * u
        return carry[0] + folded(part), carry[1] + folded(part * phi[i + 1])

    zero = jnp.zeros((8, lanes), jnp.float32)
    seen, cross = lax.fori_loop(0, planes, add_up, (zero, zero), unroll=2)
    edge = (2 * cy - halo) * (1 - y) + halo * y
    message[pl.ds(0, planes)] = found[pl.ds(1, planes), pl.ds(edge, halo), :]
    for i, part in enumerate((sums[0], seen, cross, sums[1])):
        message[planes + i] = part


def second_kernel(
    phi, change, diag, fx, fy, fz, count, sent, came,
    own, message,
    b, buf_a, buf_b, grad_k, grad_a,
    *, dets,
):
    _, _, y, c = places(2)
    planes, rows, lanes = change.shape
    halo = came.shape[1]
    cy = (rows - halo) // 2
    base = halo * y
    edge = pl.ds(2 * cy * (1 - y), halo)
    one = jnp.ones((1, 1), jnp.float32)
    total, seen_sum, cross, square = (
        jnp.sum(sent[planes + i] + came[planes + i]) * one for i in range(4)
    )
    mean = total / dets
    part = seen_sum / total
    level = (cross - part * square) / (total * mean)
    inverse = 1.0 / mean
    blank_ends(buf_a, buf_b)
    theta, _ = chebyshev_scalars()

    def weighted(n, u, p):
        return n * (((u - p * part) * inverse - level) * inverse)

    def set_up(i, carry):
        value = weighted(count[i], change[i], phi[i + 1])
        b[i] = value
        buf_a[i + 1] = value * (1.0 / theta)
        value = weighted(count[i, edge, :], came[i], phi[i + 1, edge, :])
        b[i, edge, :] = value
        buf_a[i + 1, edge, :] = value * (1.0 / theta)
        return carry

    lax.fori_loop(0, planes, set_up, 0, unroll=2)
    dual = solve(b, (buf_a, buf_b), diag, fx, fy, fz, 8)

    def product(i, carry):
        p, u = phi[i + 1], dual[i + 1]
        grad = (p - phi[i]) * (u - dual[i]) + (p - phi[i + 2]) * (u - dual[i + 2])
        both = p * u
        for axis in range(2):
            flow = (p - beyond(p, 1, axis)) * (u - beyond(u, 1, axis))
            first = index_along(p.shape, axis) == 0
            grad = grad + flow + jnp.where(first, both, shifted(flow, 1, axis))
        grad_k[i] = -0.5 * grad
        grad_a[i] = -both
        for f, ref in enumerate((grad_k, grad_a)):
            own[f, i] = ref[i, pl.ds(base + cy * c, cy), :]
            message[f, i] = ref[i, pl.ds(base + cy * (1 - c), cy), :]
        return carry

    lax.fori_loop(0, planes, product, 0, unroll=2)


def core_kernel(own, came, kept, message):
    _, x, _, _ = places(2)
    cx = kept.shape[1]
    kept[...] = own[:, pl.ds(cx * x, cx)] + came[:, pl.ds(cx * x, cx)]
    message[...] = own[:, pl.ds(cx * (1 - x), cx)] + came[:, pl.ds(cx * (1 - x), cx)]


def slab_kernel(kept, came, *outs):
    s, _, _, _ = places(2)
    n = len(outs)
    slab = 128 // n
    _, cx, cy, _ = kept.shape
    lane = index_along((cy, 128), 1) // slab
    for f in range(2):
        for q in range(cx // n):
            planes = [kept[f, n * q + j] + came[f, n * q + j] for j in range(n)]
            for k in range(n):
                to = (s + k) % n
                piece = jnp.zeros((cy, 128), jnp.float32)
                for j in range(n):
                    moved = pltpu.roll(planes[j], ((j - to + n) % n) * slab, 1)
                    piece = jnp.where(lane == j, moved, piece)
                outs[k][f, q] = piece


def project_kernel(*refs, n):
    beta_prev = refs[0]
    parts = refs[1 : 1 + n]
    vk, va, qk, qa, w_k, w_a, tile = refs[1 + n :]
    s, x, y, c = places(2)
    slab = 128 // n
    for f, (q_ref, w) in enumerate(((qk, w_k), (qa, w_a))):
        for q in range(vk.shape[0] // n):
            whole = sum(part[f, q] for part in parts[1:]) + parts[0][f, q]
            for j in range(n):
                i = n * q + j
                w[i] = whole[:, slab * j : slab * (j + 1)] - beta_prev[...] * q_ref[i]

    def dot(a, b):
        return jnp.sum(jnp.sum(a * b, axis=0))

    wk, wa, v_k, v_a = w_k[...], w_a[...], vk[...], va[...]
    one = jnp.ones((1, 1), jnp.float32)
    wv = (dot(wk, v_k) + dot(wa, v_a)) * one
    vv = (dot(v_k, v_k) + dot(v_a, v_a)) * one
    a = jnp.where(vv > 0.0, wv / jnp.where(vv > 0.0, vv, 1.0), 0.0)
    u_k, u_a = wk - a * v_k, wa - a * v_a
    uv = (dot(u_k, v_k) + dot(u_a, v_a)) * one
    uu = (dot(u_k, u_k) + dot(u_a, u_a)) * one
    me = ((s * 2 + x) * 2 + y) * 2 + c
    lane = index_along((8, 128), 1)
    row = index_along((8, 128), 0)
    values = jnp.zeros((8, 128), jnp.float32)
    for i, value in enumerate((wv, vv, a, uv, uu)):
        values = jnp.where(row == i, value, values)
    tile[...] = jnp.where(lane == me, values, 0.0)


def final_kernel(*refs, cells):
    tiles, (w_k, w_a, vk, va, next_k, next_a, coefs) = refs[:-7], refs[-7:]
    tile = tiles[0][...]
    for other in tiles[1:]:
        tile = tile + other[...]
    wv, vv, a, uv, uu = (tile[i : i + 1] for i in range(5))
    wv_sum = jnp.sum(wv, axis=1, keepdims=True)
    vv_sum = jnp.sum(vv, axis=1, keepdims=True)
    alpha = wv_sum / cells / (vv_sum / cells + eps_norm)
    off = alpha - a
    rr = jnp.sum(uu - 2.0 * off * uv + off * off * vv, axis=1, keepdims=True)
    beta = jnp.sqrt(rr / cells + eps_norm)
    next_k[...] = (w_k[...] - alpha * vk[...]) / beta
    next_a[...] = (w_a[...] - alpha * va[...]) / beta
    coefs[0] = jnp.sum(alpha)
    coefs[1] = jnp.sum(beta)


def f32(*shape):
    return jax.ShapeDtypeStruct(shape, jnp.float32)


def run(kernel, outs, *args, scratch=(), copies=0, smem=(), hbm=(), mib=16, in_smem_out=(), cost=None):
    vmem = pl.BlockSpec(memory_space=pltpu.VMEM)
    scalar = pl.BlockSpec(memory_space=pltpu.SMEM)
    far = pl.BlockSpec(memory_space=pltpu.HBM)
    held = [pltpu.VMEM(shape, dtype) for shape, dtype in scratch]
    if copies:
        held.append(pltpu.SemaphoreType.DMA((copies,)))
    return pl.pallas_call(
        kernel,
        out_shape=tuple(outs),
        in_specs=[scalar if i in smem else far if i in hbm else vmem for i in range(len(args))],
        out_specs=tuple(scalar if i in in_smem_out else vmem for i in range(len(outs))),
        scratch_shapes=held,
        compiler_params=pltpu.CompilerParams(vmem_limit_bytes=mib * 2**20),
        cost_estimate=cost,
    )(*args)


HALO = 8


def per_device_paired(
    labels, kappa_table, absorb_table, background, det_cells,
    v_kappa, v_absorb, q_kappa, q_absorb, beta_prev,
):
    sources, cx, cy, cz = background.shape
    n = lax.axis_size("src")
    planes, rows = 2 * cx, 2 * cy + HALO
    ny = cy * lax.axis_size("gy")
    dets = det_cells.shape[0]
    cells = planes * ny * cz
    groups = cx // n

    def swap_x(value):
        return lax.ppermute(value, "gx", [(0, 1), (1, 0)])

    def swap_core(value):
        return lax.ppermute(value, "gy", [(0, 1), (1, 0), (2, 3), (3, 2)])

    def along_z(value, k):
        return lax.ppermute(value, "src", [(i, (i + k) % n) for i in range(n)])

    block = (cx, cy, cz)
    float_block = lambda *shape: (shape, jnp.float32)
    raw_labels = (block, jnp.int32)
    packed, message = run(
        pack_kernel, (f32(2, groups, cy, cz), f32(sources // 2 + 1, *block)),
        background, labels, v_kappa, v_absorb, hbm=(0, 1, 2, 3),
        scratch=(raw_labels, float_block(2, *v_kappa.shape)), copies=4,
    )
    came = swap_x(message)
    slabs = [packed] + [along_z(packed, k) for k in range(1, n)]
    (count,) = run(
        functools.partial(count_kernel, ny=ny, nz=cz, half=2 * cy, halo=HALO),
        (f32(planes, rows, cz),), det_cells.reshape(1, dets),
        cost=pl.CostEstimate(flops=2 * planes * rows * cz * dets, bytes_accessed=planes * rows * cz * 4, transcendentals=0),
    )
    (vector,) = run(unpack_kernel, (f32(2, *block),), *slabs)
    vector_came = swap_x(vector)

    def to_edges(edge_other, edge_mine):
        return lax.ppermute(edge_other, "gy", [(1, 2), (2, 1)]), lax.ppermute(edge_mine, "gy", [(1, 3), (2, 0)])

    mine, fields, edge_other, edge_mine = run(
        photon_kernel,
        (f32(planes, cy, cz), f32(2, planes, cy, cz), f32(2, planes, HALO, cz), f32(2, planes, HALO, cz)),
        background, labels, came, hbm=(0, 1), scratch=(raw_labels,), copies=3,
    )
    edges = to_edges(edge_other, edge_mine)
    got = swap_core(fields)
    frame, wide = (planes, rows, cz), (planes + 2, rows, cz)
    float_frame, float_wide = float_block(*frame), float_block(*wide)
    phi, diag, fx, fy, fz, sums = run(
        stencil_kernel,
        (f32(*wide), f32(*frame), f32(planes + 1, rows, cz), f32(*frame), f32(*frame), f32(2, 8, cz)),
        kappa_table, absorb_table, mine, fields, got, *edges, count,
        smem=(0, 1), scratch=(float_frame, float_wide),
    )
    fields, edge = run(
        vector_kernel, (f32(2, planes, cy, cz), f32(2, planes, HALO, cz)), vector, vector_came
    )
    edges = to_edges(edge, edge)
    got = swap_core(fields)
    change, sent = run(
        first_kernel, (f32(*frame), f32(planes + 4, HALO, cz)),
        phi, diag, fx, fy, fz, count, sums, fields, got, *edges,
        scratch=(float_wide, float_frame, float_frame, float_wide, float_wide),
    )
    heard = lax.ppermute(sent, "gy", [(i, (i + 2) % 4) for i in range(4)])
    own, message = run(
        functools.partial(second_kernel, dets=dets),
        (f32(2, planes, cy, cz), f32(2, planes, cy, cz)),
        phi, change, diag, fx, fy, fz, count, sent, heard,
        scratch=(float_frame, float_wide, float_wide, float_frame, float_frame),
    )
    kept, message = run(
        core_kernel, (f32(2, cx, cy, cz), f32(2, cx, cy, cz)), own, swap_core(message)
    )
    pieces = run(
        slab_kernel, [f32(2, groups, cy, cz)] * n, kept, swap_x(message)
    )
    parts = [pieces[0]] + [along_z(pieces[k], k) for k in range(1, n)]
    w_k, w_a, tile = run(
        functools.partial(project_kernel, n=n),
        (f32(*v_kappa.shape), f32(*v_kappa.shape), f32(8, 128)),
        beta_prev.reshape(1, 1), *parts, v_kappa, v_absorb, q_kappa, q_absorb,
    )
    tile = tile + sum(along_z(tile, k) for k in range(1, n))
    over_x, over_core = swap_x(tile), swap_core(tile)
    over_both = lax.ppermute(
        tile, ("gx", "gy"), [(4 * a + b, 4 * (1 - a) + (b ^ 1)) for a in range(2) for b in range(4)]
    )
    tile = tile + over_x + over_core + over_both
    over_y = lax.ppermute(tile, "gy", [(i, (i + 2) % 4) for i in range(4)])
    return tuple(run(
        functools.partial(final_kernel, cells=cells),
        (f32(*v_kappa.shape), f32(*v_kappa.shape), f32(2)),
        tile, over_y, w_k, w_a, v_kappa, v_absorb, in_smem_out=(2,),
    ))


def paired_fits(mesh):
    return mesh.shape["gx"] == 2 and mesh.shape["gy"] == 4


def body_for(mesh):
    if not paired_fits(mesh):
        return per_device

    def chosen(*args):
        sources, cx, cy, cz = args[3].shape
        n = lax.axis_size("src")
        fits = sources == 4 and cz == 128 and cx % n == 0 and cz % n == 0 and cy % HALO == 0
        devices = 8 * n
        return (per_device_paired if fits and devices <= 128 else per_device)(*args)

    return chosen


def solution(mesh):
    return jax.shard_map(
        body_for(mesh),
        mesh=mesh,
        in_specs=(
            P("gx", "gy", None),
            P(),
            P(),
            P("src", "gx", "gy", None),
            P(),
            P("gx", "gy", "src"),
            P("gx", "gy", "src"),
            P("gx", "gy", "src"),
            P("gx", "gy", "src"),
            P(),
        ),
        out_specs=(P("gx", "gy", "src"), P("gx", "gy", "src"), P()),
        check_vma=False,
    )
```

```python
import functools

import jax
import jax.numpy as jnp
from jax import lax
from jax.experimental import pallas as pl
from jax.experimental.pallas import tpu as pltpu
from jax.sharding import PartitionSpec as P

ITERS = 6


lam_low = 0.02
lam_high = 24.1
eps_norm = 1e-06


def padded_2(block, sides, width):
    for axis, dim in sides:
        count = lax.axis_size(axis)
        forward = [(i, i + 1) for i in range(count - 1)]
        backward = [(target, source) for source, target in forward]
        low = lax.ppermute(
            lax.slice_in_dim(block, block.shape[dim] - width, None, axis=dim), axis, forward
        )
        high = lax.ppermute(lax.slice_in_dim(block, 0, width, axis=dim), axis, backward)
        block = jnp.concatenate([low, block, high], axis=dim)
    return block


def regional(labels, table):
    field = jnp.zeros(labels.shape, jnp.float32)
    for region in range(table.shape[0]):
        field = field + jnp.where(labels == region, table[region], 0.0)
    return field


def beside(padded):
    widths = [(0, 0)] * (padded.ndim - 1) + [(1, 1)]
    full = jnp.pad(padded, widths)
    return [
        full[..., 2:, 1:-1, 1:-1],
        full[..., :-2, 1:-1, 1:-1],
        full[..., 1:-1, 2:, 1:-1],
        full[..., 1:-1, :-2, 1:-1],
        full[..., 1:-1, 1:-1, 2:],
        full[..., 1:-1, 1:-1, :-2],
    ]


def chebyshev(rhs, apply_op):
    theta = 0.5 * (lam_high + lam_low)
    delta = 0.5 * (lam_high - lam_low)
    sigma = theta / delta
    rho = 1.0 / sigma
    solution = jnp.zeros_like(rhs)
    remain = rhs
    step_dir = rhs / theta
    for step in range(ITERS):
        solution = solution + step_dir
        if step + 1 < ITERS:
            remain = remain - apply_op(step_dir)
            rho_next = 1.0 / (2.0 * sigma - rho)
            step_dir = rho_next * rho * step_dir + 2.0 * rho_next / delta * remain
            rho = rho_next
    return solution


def per_device(
    labels,
    kappa_table,
    absorb_table,
    background,
    det_cells,
    v_kappa,
    v_absorb,
    q_kappa,
    q_absorb,
    beta_prev,
):
    sources, cx, cy, cz = background.shape
    kappa = regional(labels, kappa_table)
    absorb = regional(labels, absorb_table)
    full_k, full_a = (
        lax.all_gather(v_kappa, "src", axis=2, tiled=True),
        lax.all_gather(v_absorb, "src", axis=2, tiled=True),
    )
    stacked = jnp.concatenate([background, kappa[None], full_k[None]], axis=0)
    rims = padded_2(stacked, (("gx", 1), ("gy", 2)), 1)
    near_all = beside(rims)
    kappa_faces = [0.5 * (kappa + near[sources]) for near in near_all]
    vk_faces = [0.5 * (full_k + near[sources + 1]) for near in near_all]
    phi_near = [near[:sources] for near in near_all]

    def apply_op(field):
        padded = padded_2(field, (("gx", 1), ("gy", 2)), 1)
        result = absorb * field
        for face, near in zip(kappa_faces, beside(padded)):
            result = result + face * (field - near)
        return result

    rhs = full_a * background
    for face, near in zip(vk_faces, phi_near):
        rhs = rhs + face * (background - near)
    rhs = -rhs
    change = chebyshev(rhs, apply_op)
    span_y = cy * lax.axis_size("gy")
    ix = det_cells // (span_y * cz)
    iy = det_cells // cz % span_y
    iz = det_cells % cz
    anchor_x = lax.axis_index("gx") * cx
    anchor_y = lax.axis_index("gy") * cy
    owned = (ix >= anchor_x) & (ix < anchor_x + cx) & (iy >= anchor_y) & (iy < anchor_y + cy)
    local = jnp.where(owned, ((ix - anchor_x) * cy + (iy - anchor_y)) * cz + iz, 0)
    seen_part = jnp.where(owned[None, :], change.reshape(sources, -1)[:, local], 0.0)
    base_part = jnp.where(owned[None, :], background.reshape(sources, -1)[:, local], 0.0)
    seen, base = lax.psum((seen_part, base_part), ("gx", "gy"))
    total = jnp.sum(base, axis=1, keepdims=True)
    mean_base = total / det_cells.shape[0]
    ratio = base / total
    jv_vals = (seen - ratio * jnp.sum(seen, axis=1, keepdims=True)) / mean_base
    weight = (jv_vals - jnp.sum(ratio * jv_vals, axis=1, keepdims=True)) / mean_base
    deposit = jnp.where(owned[None, :], weight, 0.0)
    source = (
        jnp.zeros((sources, cx * cy * cz), jnp.float32)
        .at[:, local]
        .add(deposit)
        .reshape(change.shape)
    )
    dual = chebyshev(source, apply_op)
    dual_rims = padded_2(dual, (("gx", 1), ("gy", 2)), 1)
    grad_a = -jnp.sum(background * dual, axis=0)
    grad_k = jnp.zeros_like(kappa)
    for near_phi, near_dual in zip(phi_near, beside(dual_rims)):
        grad_k = grad_k - 0.5 * jnp.sum((background - near_phi) * (dual - near_dual), axis=0)
    summed_k, summed_a = lax.psum((grad_k, grad_a), "src")
    slab = v_kappa.shape[2]
    offset = lax.axis_index("src") * slab
    hv_k = lax.dynamic_slice_in_dim(summed_k, offset, slab, 2)
    hv_a = lax.dynamic_slice_in_dim(summed_a, offset, slab, 2)
    cell_count = cx * lax.axis_size("gx") * cy * lax.axis_size("gy") * cz
    w_k = hv_k - beta_prev[0] * q_kappa
    w_a = hv_a - beta_prev[0] * q_absorb
    local_wv = jnp.sum(w_k * v_kappa) + jnp.sum(w_a * v_absorb)
    local_vv = jnp.sum(v_kappa * v_kappa) + jnp.sum(v_absorb * v_absorb)
    wv_sum, vv_sum = lax.psum((local_wv, local_vv), ("src", "gx", "gy"))
    alpha = wv_sum / cell_count / (vv_sum / cell_count + eps_norm)
    r_k = w_k - alpha * v_kappa
    r_a = w_a - alpha * v_absorb
    rr_sum = lax.psum(jnp.sum(r_k * r_k) + jnp.sum(r_a * r_a), ("src", "gx", "gy"))
    beta = jnp.sqrt(rr_sum / cell_count + eps_norm)
    return (r_k / beta, r_a / beta, jnp.stack([alpha, beta]))


def chebyshev_scalars():
    theta = 0.5 * (lam_high + lam_low)
    delta = 0.5 * (lam_high - lam_low)
    sigma = theta / delta
    rho = 1.0 / sigma
    pairs = []
    for _ in range(ITERS - 1):
        rho_next = 1.0 / (2.0 * sigma - rho)
        pairs.append((rho_next * rho, 2.0 * rho_next / delta))
        rho = rho_next
    return theta, pairs


def places(split):
    g = lax.axis_index("gy")
    return lax.axis_index("src"), lax.axis_index("gx"), g // split, g % split


def shifted(value, step, axis):
    return pltpu.roll(value, step % value.shape[axis], axis)


def index_along(shape, axis):
    return lax.broadcasted_iota(jnp.int32, shape, axis)


def beyond(value, step, axis):
    size = value.shape[axis]
    at = index_along(value.shape, axis)
    edge = size - 1 if step == 1 else 0
    return jnp.where(at == edge, 0.0, shifted(value, -step, axis))


def pack_kernel(bg, labels, vk, va, packed, message, raw, v_in, sems):
    _, x, _, _ = places(2)
    half = bg.shape[0] // 2
    copies = [
        pltpu.make_async_copy(src, dst, sems.at[i])
        for i, (src, dst) in enumerate((
            (vk, v_in.at[0]),
            (va, v_in.at[1]),
            (bg.at[pl.ds(half * (1 - x), half)], message.at[pl.ds(0, half)]),
            (labels, raw),
        ))
    ]
    for copy in copies:
        copy.start()
    per = 128 // vk.shape[2]
    for f in range(2):
        copies[f].wait()
        for q in range(vk.shape[0] // per):
            packed[f, q] = jnp.concatenate([v_in[f, per * q + j] for j in range(per)], axis=1)
    copies[3].wait()
    message[half] = raw[...].astype(jnp.float32)
    copies[2].wait()


def count_kernel(dets, count, *, ny, nz, half, halo):
    _, _, y, _ = places(2)
    planes, rows, _ = count.shape
    flat = dets[...]
    iz = flat % nz
    line = flat // nz
    iy = line % ny
    ix = line // ny
    row = iy - (half - halo) * y
    spot = jnp.where((row >= 0) & (row < rows), ix * rows + row, -1)
    dets_n = flat.shape[1]
    at_z = (index_along((nz, dets_n), 0) == iz).astype(jnp.float32).astype(jnp.bfloat16)

    def body(i, carry):
        here = index_along((2 * rows, dets_n), 0) + i * (2 * rows)
        hot = (here == spot).astype(jnp.float32).astype(jnp.bfloat16)
        found = lax.dot_general(hot, at_z, (((1,), (1,)), ((), ())), preferred_element_type=jnp.float32)
        count[pl.ds(2 * i, 2)] = found.reshape(2, rows, nz)
        return carry

    lax.fori_loop(0, planes // 2, body, 0)


def photon_kernel(bg, labels, msg, mine, fields, edge_other, edge_mine, raw, sems):
    _, x, y, c = places(2)
    half = bg.shape[0] // 2
    cx, cy, _ = labels.shape
    here, there = cx * x, cx * (1 - x)
    copies = [
        pltpu.make_async_copy(src, dst, sems.at[i])
        for i, (src, dst) in enumerate((
            (bg.at[half * x + c], mine.at[pl.ds(here, cx)]),
            (bg.at[half * x + 1 - c], fields.at[0, pl.ds(here, cx)]),
            (labels, raw),
        ))
    ]
    for copy in copies:
        copy.start()
    mine[pl.ds(there, cx)] = msg[c]
    fields[0, pl.ds(there, cx)] = msg[1 - c]
    fields[1, pl.ds(there, cx)] = msg[half]
    for copy in copies:
        copy.wait()
    fields[1, pl.ds(here, cx)] = raw[...].astype(jnp.float32)
    halo = edge_mine.shape[2]
    first = (cy - halo) * (1 - y)
    edge_other[...] = fields[:, :, pl.ds(first, halo), :]
    edge_mine[0] = mine[:, pl.ds(first, halo), :]
    edge_mine[1] = fields[1, :, pl.ds(first, halo), :]


def unpack_kernel(*refs, n):
    own, parts, full = refs[:2], refs[2 : n + 1], refs[-1]
    s, _, _, _ = places(2)
    slab = 128 // n
    _, cx, cy, _ = full.shape
    lane = index_along((cy, 128), 1) // slab
    for f in range(2):
        for q in range(cx // n):
            blocks = [part[f, q] for part in parts]
            for j in range(n):
                plane = jnp.concatenate([own[f][n * q + j]] * n, axis=1)
                for k in range(1, n):
                    home = (s - k + n) % n
                    moved = pltpu.roll(blocks[k - 1], ((home - j + n) % n) * slab, 1)
                    plane = jnp.where(lane == home, moved, plane)
                full[f, n * q + j] = plane


def vector_kernel(own, came, fields, edge):
    _, x, y, _ = places(2)
    cx, cy = own.shape[1:3]
    halo = edge.shape[2]
    first = (cy - halo) * (1 - y)
    for start, part in ((cx * x, own), (cx * (1 - x), came)):
        fields[:, pl.ds(start, cx)] = part[...]
        edge[:, pl.ds(start, cx)] = part[:, :, pl.ds(first, halo), :]


def solve(b, bufs, diag, fx, fy, fz, unroll):
    planes = b.shape[0]
    _, pairs = chebyshev_scalars()
    for step, (keep, push) in enumerate(pairs):
        src, dst = bufs[step % 2], bufs[(step + 1) % 2]

        def body(i, carry):
            u = src[i + 1]
            coef_y, coef_z = fy[i], fz[i]
            left = b[i] - diag[i] * u
            left = left + fx[i] * src[i] + fx[i + 1] * src[i + 2]
            left = left + coef_y * shifted(u, -1, 0) + shifted(coef_y * u, 1, 0)
            left = left + coef_z * shifted(u, -1, 1) + shifted(coef_z * u, 1, 1)
            change = u if step == 0 else u - dst[i + 1]
            dst[i + 1] = u + keep * change + push * left
            return carry

        lax.fori_loop(0, planes, body, 0, unroll=unroll)
    return bufs[len(pairs) % 2]


def folded(value):
    return jnp.sum(value.reshape(-1, 8, value.shape[1]), axis=0)


def framed(ref, shift, parts, planes, cy, halo, y, c):
    own, got, edge_a, edge_b = parts
    there = pl.ds(shift, planes)
    base = halo * y
    ref[there, pl.ds(base + cy * c, cy), :] = own
    ref[there, pl.ds(base + cy * (1 - c), cy), :] = got
    ref[there, pl.ds(2 * cy * (1 - y), halo), :] = edge_a + edge_b


def blank_ends(*refs):
    for ref in refs:
        blank = jnp.zeros(ref.shape[1:], jnp.float32)
        ref[0] = blank
        ref[ref.shape[0] - 1] = blank


def owned_rows(shape, base, count):
    at_row = index_along(shape, 0)
    return (at_row >= base) & (at_row < base + count)


def stencil_kernel(
    kap_table, abs_table, mine, fields, got, edge_other, edge_mine, count,
    phi, diag, fx, fy, fz, sums,
    labels, kap,
):
    _, _, y, c = places(2)
    planes, cy, lanes = mine.shape
    halo = edge_mine.shape[2]
    rows = 2 * cy + halo
    place = (planes, cy, halo, y, c)
    framed(phi, 1, (mine[...], got[0], edge_other[0], edge_mine[0]), *place)
    framed(labels, 0, (fields[1], got[1], edge_other[1], edge_mine[1]), *place)
    blank_ends(phi, kap)
    blank = jnp.zeros((rows, lanes), jnp.float32)
    lane = index_along((rows, lanes), 1)
    kap_row, abs_row = blank, blank
    for region in range(kap_table.shape[0]):
        kap_row = jnp.where(lane == region, kap_table[region], kap_row)
        abs_row = jnp.where(lane == region, abs_table[region], abs_row)

    def look_up(i, carry):
        at = labels[i].astype(jnp.int32)
        kap[i + 1] = jnp.take_along_axis(kap_row, at, axis=1)
        diag[i] = jnp.take_along_axis(abs_row, at, axis=1)
        return carry

    lax.fori_loop(0, planes, look_up, 0, unroll=2)
    fx[0] = 0.5 * kap[1]
    owned = owned_rows((rows, lanes), halo * y, 2 * cy)

    def set_up(i, carry):
        k = kap[i + 1]
        along_x = 0.5 * (k + kap[i + 2])
        along_y, along_z = 0.5 * (k + beyond(k, 1, 0)), 0.5 * (k + beyond(k, 1, 1))
        fx[i + 1] = along_x
        fy[i] = jnp.where(index_along(k.shape, 0) == rows - 1, 0.0, along_y)
        fz[i] = jnp.where(lane == lanes - 1, 0.0, along_z)
        back_y, back_z = 0.5 * (k + beyond(k, -1, 0)), 0.5 * (k + beyond(k, -1, 1))
        diag[i] = diag[i] + fx[i] + along_x + along_y + back_y + along_z + back_z
        p = phi[i + 1]
        part = jnp.where(owned, count[i], 0.0) * p
        return carry[0] + folded(part), carry[1] + folded(part * p)

    zero = jnp.zeros((8, lanes), jnp.float32)
    sums[0], sums[1] = lax.fori_loop(0, planes, set_up, (zero, zero), unroll=2)


def first_kernel(
    phi, diag, fx, fy, fz, count, sums, fields, got, edge_a, edge_b,
    change, message,
    vk, va, b, buf_a, buf_b,
):
    _, _, y, c = places(2)
    planes, rows, lanes = change.shape
    halo = edge_a.shape[2]
    cy = (rows - halo) // 2
    place = (planes, cy, halo, y, c)
    framed(vk, 1, (fields[0], got[0], edge_a[0], edge_b[0]), *place)
    framed(va, 0, (fields[1], got[1], edge_a[1], edge_b[1]), *place)
    blank_ends(vk, buf_a, buf_b)
    theta, _ = chebyshev_scalars()

    def set_up(i, carry):
        v, p = vk[i + 1], phi[i + 1]
        total = 0.5 * (v + vk[i]) * (p - phi[i]) + 0.5 * (v + vk[i + 2]) * (p - phi[i + 2])
        for axis in range(2):
            flow = 0.5 * (v + beyond(v, 1, axis)) * (p - beyond(p, 1, axis))
            first = index_along(v.shape, axis) == 0
            total = total + flow + jnp.where(first, 0.5 * v * p, -shifted(flow, 1, axis))
        total = -(va[i] * p + total)
        b[i] = total
        buf_a[i + 1] = total * (1.0 / theta)
        return carry

    lax.fori_loop(0, planes, set_up, 0, unroll=2)
    found = solve(b, (buf_a, buf_b), diag, fx, fy, fz, 8)
    owned = owned_rows((rows, lanes), halo * y, 2 * cy)

    def add_up(i, carry):
        u = found[i + 1]
        change[i] = u
        part = jnp.where(owned, count[i], 0.0) * u
        return carry[0] + folded(part), carry[1] + folded(part * phi[i + 1])

    zero = jnp.zeros((8, lanes), jnp.float32)
    seen, cross = lax.fori_loop(0, planes, add_up, (zero, zero), unroll=2)
    edge = (2 * cy - halo) * (1 - y) + halo * y
    message[pl.ds(0, planes)] = found[pl.ds(1, planes), pl.ds(edge, halo), :]
    for i, part in enumerate((sums[0], seen, cross, sums[1])):
        message[planes + i] = part


def second_kernel(
    phi, change, diag, fx, fy, fz, count, sent, came,
    own, message,
    b, buf_a, buf_b, grad_k, grad_a,
    *, dets,
):
    _, _, y, c = places(2)
    planes, rows, lanes = change.shape
    halo = came.shape[1]
    cy = (rows - halo) // 2
    base = halo * y
    edge = pl.ds(2 * cy * (1 - y), halo)
    one = jnp.ones((1, 1), jnp.float32)
    total, seen_sum, cross, square = (
        jnp.sum(sent[planes + i] + came[planes + i]) * one for i in range(4)
    )
    mean = total / dets
    part = seen_sum / total
    level = (cross - part * square) / (total * mean)
    inverse = 1.0 / mean
    blank_ends(buf_a, buf_b)
    theta, _ = chebyshev_scalars()

    def weighted(n, u, p):
        return n * (((u - p * part) * inverse - level) * inverse)

    def set_up(i, carry):
        value = weighted(count[i], change[i], phi[i + 1])
        b[i] = value
        buf_a[i + 1] = value * (1.0 / theta)
        value = weighted(count[i, edge, :], came[i], phi[i + 1, edge, :])
        b[i, edge, :] = value
        buf_a[i + 1, edge, :] = value * (1.0 / theta)
        return carry

    lax.fori_loop(0, planes, set_up, 0, unroll=2)
    dual = solve(b, (buf_a, buf_b), diag, fx, fy, fz, 8)

    def product(i, carry):
        p, u = phi[i + 1], dual[i + 1]
        grad = (p - phi[i]) * (u - dual[i]) + (p - phi[i + 2]) * (u - dual[i + 2])
        both = p * u
        for axis in range(2):
            flow = (p - beyond(p, 1, axis)) * (u - beyond(u, 1, axis))
            first = index_along(p.shape, axis) == 0
            grad = grad + flow + jnp.where(first, both, shifted(flow, 1, axis))
        grad_k[i] = -0.5 * grad
        grad_a[i] = -both
        for f, ref in enumerate((grad_k, grad_a)):
            own[f, i] = ref[i, pl.ds(base + cy * c, cy), :]
            message[f, i] = ref[i, pl.ds(base + cy * (1 - c), cy), :]
        return carry

    lax.fori_loop(0, planes, product, 0, unroll=2)


def core_kernel(own, came, kept, message):
    _, x, _, _ = places(2)
    cx = kept.shape[1]
    kept[...] = own[:, pl.ds(cx * x, cx)] + came[:, pl.ds(cx * x, cx)]
    message[...] = own[:, pl.ds(cx * (1 - x), cx)] + came[:, pl.ds(cx * (1 - x), cx)]


def slab_kernel(kept, came, *outs):
    s, _, _, _ = places(2)
    n = len(outs)
    slab = 128 // n
    _, cx, cy, _ = kept.shape
    lane = index_along((cy, 128), 1) // slab
    for f in range(2):
        for q in range(cx // n):
            planes = [kept[f, n * q + j] + came[f, n * q + j] for j in range(n)]
            for k in range(n):
                to = (s + k) % n
                piece = jnp.zeros((cy, 128), jnp.float32)
                for j in range(n):
                    moved = pltpu.roll(planes[j], ((j - to + n) % n) * slab, 1)
                    piece = jnp.where(lane == j, moved, piece)
                outs[k][f, q] = piece


def project_kernel(*refs, n):
    beta_prev = refs[0]
    parts = refs[1 : 1 + n]
    vk, va, qk, qa, w_k, w_a, tile = refs[1 + n :]
    s, x, y, c = places(2)
    slab = 128 // n
    for f, (q_ref, w) in enumerate(((qk, w_k), (qa, w_a))):
        for q in range(vk.shape[0] // n):
            whole = sum(part[f, q] for part in parts[1:]) + parts[0][f, q]
            for j in range(n):
                i = n * q + j
                w[i] = whole[:, slab * j : slab * (j + 1)] - beta_prev[...] * q_ref[i]

    def dot(a, b):
        return jnp.sum(jnp.sum(a * b, axis=0))

    wk, wa, v_k, v_a = w_k[...], w_a[...], vk[...], va[...]
    one = jnp.ones((1, 1), jnp.float32)
    wv = (dot(wk, v_k) + dot(wa, v_a)) * one
    vv = (dot(v_k, v_k) + dot(v_a, v_a)) * one
    a = jnp.where(vv > 0.0, wv / jnp.where(vv > 0.0, vv, 1.0), 0.0)
    u_k, u_a = wk - a * v_k, wa - a * v_a
    uv = (dot(u_k, v_k) + dot(u_a, v_a)) * one
    uu = (dot(u_k, u_k) + dot(u_a, u_a)) * one
    me = ((s * 2 + x) * 2 + y) * 2 + c
    lane = index_along((8, 128), 1)
    row = index_along((8, 128), 0)
    values = jnp.zeros((8, 128), jnp.float32)
    for i, value in enumerate((wv, vv, a, uv, uu)):
        values = jnp.where(row == i, value, values)
    tile[...] = jnp.where(lane == me, values, 0.0)


def final_kernel(*refs, cells):
    tiles, (w_k, w_a, vk, va, next_k, next_a, coefs) = refs[:-7], refs[-7:]
    tile = tiles[0][...]
    for other in tiles[1:]:
        tile = tile + other[...]
    wv, vv, a, uv, uu = (tile[i : i + 1] for i in range(5))
    wv_sum = jnp.sum(wv, axis=1, keepdims=True)
    vv_sum = jnp.sum(vv, axis=1, keepdims=True)
    alpha = wv_sum / cells / (vv_sum / cells + eps_norm)
    off = alpha - a
    rr = jnp.sum(uu - 2.0 * off * uv + off * off * vv, axis=1, keepdims=True)
    beta = jnp.sqrt(rr / cells + eps_norm)
    next_k[...] = (w_k[...] - alpha * vk[...]) / beta
    next_a[...] = (w_a[...] - alpha * va[...]) / beta
    coefs[0] = jnp.sum(alpha)
    coefs[1] = jnp.sum(beta)


def f32(*shape):
    return jax.ShapeDtypeStruct(shape, jnp.float32)


def run(kernel, outs, *args, after=(), scratch=(), copies=0, smem=(), hbm=(), mib=16, in_smem_out=(), cost=None):
    vmem = pl.BlockSpec(memory_space=pltpu.VMEM)
    scalar = pl.BlockSpec(memory_space=pltpu.SMEM)
    far = pl.BlockSpec(memory_space=pltpu.HBM)
    held = [pltpu.VMEM(shape, dtype) for shape, dtype in scratch]
    used, waits = len(args), len(after)

    def body(*refs):
        kernel(*refs[:used], *refs[used + waits :])

    args = (*args, *after)
    if copies:
        held.append(pltpu.SemaphoreType.DMA((copies,)))
    return pl.pallas_call(
        body if waits else kernel,
        out_shape=tuple(outs),
        in_specs=[scalar if i in smem else far if i in hbm else vmem for i in range(len(args))],
        out_specs=tuple(scalar if i in in_smem_out else vmem for i in range(len(outs))),
        scratch_shapes=held,
        compiler_params=pltpu.CompilerParams(vmem_limit_bytes=mib * 2**20),
        cost_estimate=cost,
    )(*args)


HALO = 8


def per_device_paired(
    labels, kappa_table, absorb_table, background, det_cells,
    v_kappa, v_absorb, q_kappa, q_absorb, beta_prev,
):
    sources, cx, cy, cz = background.shape
    n = lax.axis_size("src")
    planes, rows = 2 * cx, 2 * cy + HALO
    ny = cy * lax.axis_size("gy")
    dets = det_cells.shape[0]
    cells = planes * ny * cz
    groups = cx // n

    def swap_x(value):
        return lax.ppermute(value, "gx", [(0, 1), (1, 0)])

    def swap_core(value):
        return lax.ppermute(value, "gy", [(0, 1), (1, 0), (2, 3), (3, 2)])

    def along_z(value, k):
        return lax.ppermute(value, "src", [(i, (i + k) % n) for i in range(n)])

    block = (cx, cy, cz)
    float_block = lambda *shape: (shape, jnp.float32)
    raw_labels = (block, jnp.int32)
    packed, message = run(
        pack_kernel, (f32(2, groups, cy, cz), f32(sources // 2 + 1, *block)),
        background, labels, v_kappa, v_absorb, hbm=(0, 1, 2, 3),
        scratch=(raw_labels, float_block(2, *v_kappa.shape)), copies=4, mib=60,
    )
    came = swap_x(message)
    slabs = [along_z(packed, k) for k in range(1, n)]
    (count,) = run(
        functools.partial(count_kernel, ny=ny, nz=cz, half=2 * cy, halo=HALO),
        (f32(planes, rows, cz),), det_cells.reshape(1, dets),
        cost=pl.CostEstimate(flops=2 * planes * rows * cz * dets, bytes_accessed=planes * rows * cz * 4, transcendentals=0),
    )
    (vector,) = run(
        functools.partial(unpack_kernel, n=n), (f32(2, *block),), v_kappa, v_absorb, *slabs, after=(count,)
    )
    vector_came = swap_x(vector)

    def to_edges(edge_other, edge_mine):
        return lax.ppermute(edge_other, "gy", [(1, 2), (2, 1)]), lax.ppermute(edge_mine, "gy", [(1, 3), (2, 0)])

    mine, fields, edge_other, edge_mine = run(
        photon_kernel,
        (f32(planes, cy, cz), f32(2, planes, cy, cz), f32(2, planes, HALO, cz), f32(2, planes, HALO, cz)),
        background, labels, came, after=(vector,), hbm=(0, 1), scratch=(raw_labels,), copies=3,
    )
    edges = to_edges(edge_other, edge_mine)
    got = swap_core(fields)
    frame, wide = (planes, rows, cz), (planes + 2, rows, cz)
    float_frame, float_wide = float_block(*frame), float_block(*wide)
    phi, diag, fx, fy, fz, sums = run(
        stencil_kernel,
        (f32(*wide), f32(*frame), f32(planes + 1, rows, cz), f32(*frame), f32(*frame), f32(2, 8, cz)),
        kappa_table, absorb_table, mine, fields, got, *edges, count,
        smem=(0, 1), scratch=(float_frame, float_wide),
    )
    fields, edge = run(
        vector_kernel, (f32(2, planes, cy, cz), f32(2, planes, HALO, cz)), vector, vector_came,
        after=(got, *edges),
    )
    edges = to_edges(edge, edge)
    got = swap_core(fields)
    change, sent = run(
        first_kernel, (f32(*frame), f32(planes + 4, HALO, cz)),
        phi, diag, fx, fy, fz, count, sums, fields, got, *edges,
        scratch=(float_wide, float_frame, float_frame, float_wide, float_wide),
    )
    heard = lax.ppermute(sent, "gy", [(i, (i + 2) % 4) for i in range(4)])
    own, message = run(
        functools.partial(second_kernel, dets=dets),
        (f32(2, planes, cy, cz), f32(2, planes, cy, cz)),
        phi, change, diag, fx, fy, fz, count, sent, heard,
        scratch=(float_frame, float_wide, float_wide, float_frame, float_frame),
    )
    kept, message = run(
        core_kernel, (f32(2, cx, cy, cz), f32(2, cx, cy, cz)), own, swap_core(message)
    )
    pieces = run(
        slab_kernel, [f32(2, groups, cy, cz)] * n, kept, swap_x(message)
    )
    parts = [pieces[0]] + [along_z(pieces[k], k) for k in range(1, n)]
    w_k, w_a, tile = run(
        functools.partial(project_kernel, n=n),
        (f32(*v_kappa.shape), f32(*v_kappa.shape), f32(8, 128)),
        beta_prev.reshape(1, 1), *parts, v_kappa, v_absorb, q_kappa, q_absorb,
    )
    tile = tile + sum(along_z(tile, k) for k in range(1, n))
    over_x, over_core = swap_x(tile), swap_core(tile)
    over_both = lax.ppermute(
        tile, ("gx", "gy"), [(4 * a + b, 4 * (1 - a) + (b ^ 1)) for a in range(2) for b in range(4)]
    )
    tile = tile + over_x + over_core + over_both
    over_y = lax.ppermute(tile, "gy", [(i, (i + 2) % 4) for i in range(4)])
    return tuple(run(
        functools.partial(final_kernel, cells=cells),
        (f32(*v_kappa.shape), f32(*v_kappa.shape), f32(2)),
        tile, over_y, w_k, w_a, v_kappa, v_absorb, in_smem_out=(2,),
    ))


def paired_fits(mesh):
    return mesh.shape["gx"] == 2 and mesh.shape["gy"] == 4


def body_for(mesh):
    if not paired_fits(mesh):
        return per_device

    def chosen(*args):
        sources, cx, cy, cz = args[3].shape
        n = lax.axis_size("src")
        fits = sources == 4 and cz == 128 and cx % n == 0 and cz % n == 0 and cy % HALO == 0
        devices = 8 * n
        return (per_device_paired if fits and devices <= 128 else per_device)(*args)

    return chosen


def solution(mesh):
    return jax.shard_map(
        body_for(mesh),
        mesh=mesh,
        in_specs=(
            P("gx", "gy", None),
            P(),
            P(),
            P("src", "gx", "gy", None),
            P(),
            P("gx", "gy", "src"),
            P("gx", "gy", "src"),
            P("gx", "gy", "src"),
            P("gx", "gy", "src"),
            P(),
        ),
        out_specs=(P("gx", "gy", "src"), P("gx", "gy", "src"), P()),
        check_vma=False,
    )
```

```python
import functools

import jax
import jax.numpy as jnp
from jax import lax
from jax.experimental import pallas as pl
from jax.experimental.pallas import tpu as pltpu
from jax.sharding import PartitionSpec as P

ITERS = 6


lam_low = 0.02
lam_high = 24.1
eps_norm = 1e-06


def padded_2(block, sides, width):
    for axis, dim in sides:
        count = lax.axis_size(axis)
        forward = [(i, i + 1) for i in range(count - 1)]
        backward = [(target, source) for source, target in forward]
        low = lax.ppermute(
            lax.slice_in_dim(block, block.shape[dim] - width, None, axis=dim), axis, forward
        )
        high = lax.ppermute(lax.slice_in_dim(block, 0, width, axis=dim), axis, backward)
        block = jnp.concatenate([low, block, high], axis=dim)
    return block


def regional(labels, table):
    field = jnp.zeros(labels.shape, jnp.float32)
    for region in range(table.shape[0]):
        field = field + jnp.where(labels == region, table[region], 0.0)
    return field


def beside(padded):
    widths = [(0, 0)] * (padded.ndim - 1) + [(1, 1)]
    full = jnp.pad(padded, widths)
    return [
        full[..., 2:, 1:-1, 1:-1],
        full[..., :-2, 1:-1, 1:-1],
        full[..., 1:-1, 2:, 1:-1],
        full[..., 1:-1, :-2, 1:-1],
        full[..., 1:-1, 1:-1, 2:],
        full[..., 1:-1, 1:-1, :-2],
    ]


def chebyshev(rhs, apply_op):
    theta = 0.5 * (lam_high + lam_low)
    delta = 0.5 * (lam_high - lam_low)
    sigma = theta / delta
    rho = 1.0 / sigma
    solution = jnp.zeros_like(rhs)
    remain = rhs
    step_dir = rhs / theta
    for step in range(ITERS):
        solution = solution + step_dir
        if step + 1 < ITERS:
            remain = remain - apply_op(step_dir)
            rho_next = 1.0 / (2.0 * sigma - rho)
            step_dir = rho_next * rho * step_dir + 2.0 * rho_next / delta * remain
            rho = rho_next
    return solution


def per_device(
    labels,
    kappa_table,
    absorb_table,
    background,
    det_cells,
    v_kappa,
    v_absorb,
    q_kappa,
    q_absorb,
    beta_prev,
):
    sources, cx, cy, cz = background.shape
    kappa = regional(labels, kappa_table)
    absorb = regional(labels, absorb_table)
    full_k, full_a = (
        lax.all_gather(v_kappa, "src", axis=2, tiled=True),
        lax.all_gather(v_absorb, "src", axis=2, tiled=True),
    )
    stacked = jnp.concatenate([background, kappa[None], full_k[None]], axis=0)
    rims = padded_2(stacked, (("gx", 1), ("gy", 2)), 1)
    near_all = beside(rims)
    kappa_faces = [0.5 * (kappa + near[sources]) for near in near_all]
    vk_faces = [0.5 * (full_k + near[sources + 1]) for near in near_all]
    phi_near = [near[:sources] for near in near_all]

    def apply_op(field):
        padded = padded_2(field, (("gx", 1), ("gy", 2)), 1)
        result = absorb * field
        for face, near in zip(kappa_faces, beside(padded)):
            result = result + face * (field - near)
        return result

    rhs = full_a * background
    for face, near in zip(vk_faces, phi_near):
        rhs = rhs + face * (background - near)
    rhs = -rhs
    change = chebyshev(rhs, apply_op)
    span_y = cy * lax.axis_size("gy")
    ix = det_cells // (span_y * cz)
    iy = det_cells // cz % span_y
    iz = det_cells % cz
    anchor_x = lax.axis_index("gx") * cx
    anchor_y = lax.axis_index("gy") * cy
    owned = (ix >= anchor_x) & (ix < anchor_x + cx) & (iy >= anchor_y) & (iy < anchor_y + cy)
    local = jnp.where(owned, ((ix - anchor_x) * cy + (iy - anchor_y)) * cz + iz, 0)
    seen_part = jnp.where(owned[None, :], change.reshape(sources, -1)[:, local], 0.0)
    base_part = jnp.where(owned[None, :], background.reshape(sources, -1)[:, local], 0.0)
    seen, base = lax.psum((seen_part, base_part), ("gx", "gy"))
    total = jnp.sum(base, axis=1, keepdims=True)
    mean_base = total / det_cells.shape[0]
    ratio = base / total
    jv_vals = (seen - ratio * jnp.sum(seen, axis=1, keepdims=True)) / mean_base
    weight = (jv_vals - jnp.sum(ratio * jv_vals, axis=1, keepdims=True)) / mean_base
    deposit = jnp.where(owned[None, :], weight, 0.0)
    source = (
        jnp.zeros((sources, cx * cy * cz), jnp.float32)
        .at[:, local]
        .add(deposit)
        .reshape(change.shape)
    )
    dual = chebyshev(source, apply_op)
    dual_rims = padded_2(dual, (("gx", 1), ("gy", 2)), 1)
    grad_a = -jnp.sum(background * dual, axis=0)
    grad_k = jnp.zeros_like(kappa)
    for near_phi, near_dual in zip(phi_near, beside(dual_rims)):
        grad_k = grad_k - 0.5 * jnp.sum((background - near_phi) * (dual - near_dual), axis=0)
    summed_k, summed_a = lax.psum((grad_k, grad_a), "src")
    slab = v_kappa.shape[2]
    offset = lax.axis_index("src") * slab
    hv_k = lax.dynamic_slice_in_dim(summed_k, offset, slab, 2)
    hv_a = lax.dynamic_slice_in_dim(summed_a, offset, slab, 2)
    cell_count = cx * lax.axis_size("gx") * cy * lax.axis_size("gy") * cz
    w_k = hv_k - beta_prev[0] * q_kappa
    w_a = hv_a - beta_prev[0] * q_absorb
    local_wv = jnp.sum(w_k * v_kappa) + jnp.sum(w_a * v_absorb)
    local_vv = jnp.sum(v_kappa * v_kappa) + jnp.sum(v_absorb * v_absorb)
    wv_sum, vv_sum = lax.psum((local_wv, local_vv), ("src", "gx", "gy"))
    alpha = wv_sum / cell_count / (vv_sum / cell_count + eps_norm)
    r_k = w_k - alpha * v_kappa
    r_a = w_a - alpha * v_absorb
    rr_sum = lax.psum(jnp.sum(r_k * r_k) + jnp.sum(r_a * r_a), ("src", "gx", "gy"))
    beta = jnp.sqrt(rr_sum / cell_count + eps_norm)
    return (r_k / beta, r_a / beta, jnp.stack([alpha, beta]))


def chebyshev_scalars():
    theta = 0.5 * (lam_high + lam_low)
    delta = 0.5 * (lam_high - lam_low)
    sigma = theta / delta
    rho = 1.0 / sigma
    pairs = []
    for _ in range(ITERS - 1):
        rho_next = 1.0 / (2.0 * sigma - rho)
        pairs.append((rho_next * rho, 2.0 * rho_next / delta))
        rho = rho_next
    return theta, pairs


def places(split):
    g = lax.axis_index("gy")
    return lax.axis_index("src"), lax.axis_index("gx"), g // split, g % split


def shifted(value, step, axis):
    return pltpu.roll(value, step % value.shape[axis], axis)


def index_along(shape, axis):
    return lax.broadcasted_iota(jnp.int32, shape, axis)


def beyond(value, step, axis):
    size = value.shape[axis]
    at = index_along(value.shape, axis)
    edge = size - 1 if step == 1 else 0
    return jnp.where(at == edge, 0.0, shifted(value, -step, axis))


def pack_kernel(bg, labels, vk, va, packed, message, raw, v_in, sems):
    _, x, _, _ = places(2)
    half = bg.shape[0] // 2
    copies = [
        pltpu.make_async_copy(src, dst, sems.at[i])
        for i, (src, dst) in enumerate((
            (vk, v_in.at[0]),
            (va, v_in.at[1]),
            (bg.at[pl.ds(half * (1 - x), half)], message.at[pl.ds(0, half)]),
            (labels, raw),
        ))
    ]
    for copy in copies:
        copy.start()
    per = 128 // vk.shape[2]
    for f in range(2):
        copies[f].wait()
        for q in range(vk.shape[0] // per):
            packed[f, q] = jnp.concatenate([v_in[f, per * q + j] for j in range(per)], axis=1)
    copies[3].wait()
    message[half] = raw[...].astype(jnp.float32)
    copies[2].wait()


def count_kernel(dets, count, *, ny, nz, half, halo):
    _, _, y, _ = places(2)
    planes, rows, _ = count.shape
    flat = dets[...]
    iz = flat % nz
    line = flat // nz
    iy = line % ny
    ix = line // ny
    row = iy - (half - halo) * y
    spot = jnp.where((row >= 0) & (row < rows), ix * rows + row, -1)
    dets_n = flat.shape[1]
    at_z = (index_along((nz, dets_n), 0) == iz).astype(jnp.float32).astype(jnp.bfloat16)

    def body(i, carry):
        here = index_along((2 * rows, dets_n), 0) + i * (2 * rows)
        hot = (here == spot).astype(jnp.float32).astype(jnp.bfloat16)
        found = lax.dot_general(hot, at_z, (((1,), (1,)), ((), ())), preferred_element_type=jnp.float32)
        count[pl.ds(2 * i, 2)] = found.reshape(2, rows, nz)
        return carry

    lax.fori_loop(0, planes // 2, body, 0)


def photon_kernel(bg, labels, msg, mine, fields, edge_other, edge_mine, raw, sems):
    _, x, y, c = places(2)
    half = bg.shape[0] // 2
    cx, cy, _ = labels.shape
    here, there = cx * x, cx * (1 - x)
    copies = [
        pltpu.make_async_copy(src, dst, sems.at[i])
        for i, (src, dst) in enumerate((
            (bg.at[half * x + c], mine.at[pl.ds(here, cx)]),
            (bg.at[half * x + 1 - c], fields.at[0, pl.ds(here, cx)]),
            (labels, raw),
        ))
    ]
    for copy in copies:
        copy.start()
    mine[pl.ds(there, cx)] = msg[c]
    fields[0, pl.ds(there, cx)] = msg[1 - c]
    fields[1, pl.ds(there, cx)] = msg[half]
    for copy in copies:
        copy.wait()
    fields[1, pl.ds(here, cx)] = raw[...].astype(jnp.float32)
    halo = edge_mine.shape[2]
    first = (cy - halo) * (1 - y)
    edge_other[...] = fields[:, :, pl.ds(first, halo), :]
    edge_mine[0] = mine[:, pl.ds(first, halo), :]
    edge_mine[1] = fields[1, :, pl.ds(first, halo), :]


def unpack_kernel(*refs, n):
    own, parts, full = refs[:2], refs[2 : n + 1], refs[-1]
    s, _, _, _ = places(2)
    slab = 128 // n
    _, cx, cy, _ = full.shape
    lane = index_along((cy, 128), 1) // slab
    for f in range(2):
        for q in range(cx // n):
            blocks = [part[f, q] for part in parts]
            for j in range(n):
                plane = jnp.concatenate([own[f][n * q + j]] * n, axis=1)
                for k in range(1, n):
                    home = (s - k + n) % n
                    moved = pltpu.roll(blocks[k - 1], ((home - j + n) % n) * slab, 1)
                    plane = jnp.where(lane == home, moved, plane)
                full[f, n * q + j] = plane


def vector_kernel(own, came, fields, edge):
    _, x, y, _ = places(2)
    cx, cy = own.shape[1:3]
    halo = edge.shape[2]
    first = (cy - halo) * (1 - y)
    for start, part in ((cx * x, own), (cx * (1 - x), came)):
        fields[:, pl.ds(start, cx)] = part[...]
        edge[:, pl.ds(start, cx)] = part[:, :, pl.ds(first, halo), :]


def solve(b, bufs, diag, fx, fy, fz, unroll):
    planes = b.shape[0]
    _, pairs = chebyshev_scalars()
    for step, (keep, push) in enumerate(pairs):
        src, dst = bufs[step % 2], bufs[(step + 1) % 2]

        def body(i, carry):
            u = src[i + 1]
            coef_y, coef_z = fy[i], fz[i]
            left = b[i] - diag[i] * u
            left = left + fx[i] * src[i] + fx[i + 1] * src[i + 2]
            left = left + coef_y * shifted(u, -1, 0) + shifted(coef_y * u, 1, 0)
            left = left + coef_z * shifted(u, -1, 1) + shifted(coef_z * u, 1, 1)
            change = u if step == 0 else u - dst[i + 1]
            dst[i + 1] = u + keep * change + push * left
            return carry

        lax.fori_loop(0, planes, body, 0, unroll=unroll)
    return bufs[len(pairs) % 2]


def folded(value):
    return jnp.sum(value.reshape(-1, 8, value.shape[1]), axis=0)


def framed(ref, shift, parts, planes, cy, halo, y, c):
    own, got, edge_a, edge_b = parts
    there = pl.ds(shift, planes)
    base = halo * y
    ref[there, pl.ds(base + cy * c, cy), :] = own
    ref[there, pl.ds(base + cy * (1 - c), cy), :] = got
    ref[there, pl.ds(2 * cy * (1 - y), halo), :] = edge_a + edge_b


def blank_ends(*refs):
    for ref in refs:
        blank = jnp.zeros(ref.shape[1:], jnp.float32)
        ref[0] = blank
        ref[ref.shape[0] - 1] = blank


def owned_rows(shape, base, count):
    at_row = index_along(shape, 0)
    return (at_row >= base) & (at_row < base + count)


def stencil_kernel(
    kap_table, abs_table, mine, fields, got, edge_other, edge_mine, count,
    phi, diag, fx, fy, fz, sums,
    labels, kap,
):
    _, _, y, c = places(2)
    planes, cy, lanes = mine.shape
    halo = edge_mine.shape[2]
    rows = 2 * cy + halo
    place = (planes, cy, halo, y, c)
    framed(phi, 1, (mine[...], got[0], edge_other[0], edge_mine[0]), *place)
    framed(labels, 0, (fields[1], got[1], edge_other[1], edge_mine[1]), *place)
    blank_ends(phi, kap)
    blank = jnp.zeros((rows, lanes), jnp.float32)
    lane = index_along((rows, lanes), 1)
    kap_row, abs_row = blank, blank
    for region in range(kap_table.shape[0]):
        kap_row = jnp.where(lane == region, kap_table[region], kap_row)
        abs_row = jnp.where(lane == region, abs_table[region], abs_row)

    def look_up(i, carry):
        at = labels[i].astype(jnp.int32)
        kap[i + 1] = jnp.take_along_axis(kap_row, at, axis=1)
        diag[i] = jnp.take_along_axis(abs_row, at, axis=1)
        return carry

    lax.fori_loop(0, planes, look_up, 0, unroll=2)
    fx[0] = 0.5 * kap[1]
    owned = owned_rows((rows, lanes), halo * y, 2 * cy)

    def set_up(i, carry):
        k = kap[i + 1]
        along_x = 0.5 * (k + kap[i + 2])
        along_y, along_z = 0.5 * (k + beyond(k, 1, 0)), 0.5 * (k + beyond(k, 1, 1))
        fx[i + 1] = along_x
        fy[i] = jnp.where(index_along(k.shape, 0) == rows - 1, 0.0, along_y)
        fz[i] = jnp.where(lane == lanes - 1, 0.0, along_z)
        back_y, back_z = 0.5 * (k + beyond(k, -1, 0)), 0.5 * (k + beyond(k, -1, 1))
        diag[i] = diag[i] + fx[i] + along_x + along_y + back_y + along_z + back_z
        p = phi[i + 1]
        part = jnp.where(owned, count[i], 0.0) * p
        return carry[0] + folded(part), carry[1] + folded(part * p)

    zero = jnp.zeros((8, lanes), jnp.float32)
    sums[0], sums[1] = lax.fori_loop(0, planes, set_up, (zero, zero), unroll=2)


def first_kernel(
    phi, diag, fx, fy, fz, count, sums, fields, got, edge_a, edge_b,
    change, message,
    vk, va, b, buf_a, buf_b,
):
    _, _, y, c = places(2)
    planes, rows, lanes = change.shape
    halo = edge_a.shape[2]
    cy = (rows - halo) // 2
    place = (planes, cy, halo, y, c)
    framed(vk, 1, (fields[0], got[0], edge_a[0], edge_b[0]), *place)
    framed(va, 0, (fields[1], got[1], edge_a[1], edge_b[1]), *place)
    blank_ends(vk, buf_a, buf_b)
    theta, _ = chebyshev_scalars()

    def set_up(i, carry):
        v, p = vk[i + 1], phi[i + 1]
        total = 0.5 * (v + vk[i]) * (p - phi[i]) + 0.5 * (v + vk[i + 2]) * (p - phi[i + 2])
        for axis in range(2):
            flow = 0.5 * (v + beyond(v, 1, axis)) * (p - beyond(p, 1, axis))
            first = index_along(v.shape, axis) == 0
            total = total + flow + jnp.where(first, 0.5 * v * p, -shifted(flow, 1, axis))
        total = -(va[i] * p + total)
        b[i] = total
        buf_a[i + 1] = total * (1.0 / theta)
        return carry

    lax.fori_loop(0, planes, set_up, 0, unroll=2)
    found = solve(b, (buf_a, buf_b), diag, fx, fy, fz, 8)
    owned = owned_rows((rows, lanes), halo * y, 2 * cy)

    def add_up(i, carry):
        u = found[i + 1]
        change[i] = u
        part = jnp.where(owned, count[i], 0.0) * u
        return carry[0] + folded(part), carry[1] + folded(part * phi[i + 1])

    zero = jnp.zeros((8, lanes), jnp.float32)
    seen, cross = lax.fori_loop(0, planes, add_up, (zero, zero), unroll=2)
    edge = (2 * cy - halo) * (1 - y) + halo * y
    message[pl.ds(0, planes)] = found[pl.ds(1, planes), pl.ds(edge, halo), :]
    for i, part in enumerate((sums[0], seen, cross, sums[1])):
        message[planes + i] = part


def second_kernel(
    phi, change, diag, fx, fy, fz, count, sent, came,
    own, message,
    b, buf_a, buf_b, grad_k, grad_a,
    *, dets,
):
    _, _, y, c = places(2)
    planes, rows, lanes = change.shape
    halo = came.shape[1]
    cy = (rows - halo) // 2
    base = halo * y
    edge = pl.ds(2 * cy * (1 - y), halo)
    one = jnp.ones((1, 1), jnp.float32)
    total, seen_sum, cross, square = (
        jnp.sum(sent[planes + i] + came[planes + i]) * one for i in range(4)
    )
    mean = total / dets
    part = seen_sum / total
    level = (cross - part * square) / (total * mean)
    inverse = 1.0 / mean
    blank_ends(buf_a, buf_b)
    theta, _ = chebyshev_scalars()

    def weighted(n, u, p):
        return n * (((u - p * part) * inverse - level) * inverse)

    def set_up(i, carry):
        value = weighted(count[i], change[i], phi[i + 1])
        b[i] = value
        buf_a[i + 1] = value * (1.0 / theta)
        value = weighted(count[i, edge, :], came[i], phi[i + 1, edge, :])
        b[i, edge, :] = value
        buf_a[i + 1, edge, :] = value * (1.0 / theta)
        return carry

    lax.fori_loop(0, planes, set_up, 0, unroll=2)
    dual = solve(b, (buf_a, buf_b), diag, fx, fy, fz, 8)

    def product(i, carry):
        p, u = phi[i + 1], dual[i + 1]
        grad = (p - phi[i]) * (u - dual[i]) + (p - phi[i + 2]) * (u - dual[i + 2])
        both = p * u
        for axis in range(2):
            flow = (p - beyond(p, 1, axis)) * (u - beyond(u, 1, axis))
            first = index_along(p.shape, axis) == 0
            grad = grad + flow + jnp.where(first, both, shifted(flow, 1, axis))
        grad_k[i] = -0.5 * grad
        grad_a[i] = -both
        for f, ref in enumerate((grad_k, grad_a)):
            own[f, i] = ref[i, pl.ds(base + cy * c, cy), :]
            message[f, i] = ref[i, pl.ds(base + cy * (1 - c), cy), :]
        return carry

    lax.fori_loop(0, planes, product, 0, unroll=2)


def core_kernel(own, came, kept, message):
    _, x, _, _ = places(2)
    cx = kept.shape[1]
    kept[...] = own[:, pl.ds(cx * x, cx)] + came[:, pl.ds(cx * x, cx)]
    message[...] = own[:, pl.ds(cx * (1 - x), cx)] + came[:, pl.ds(cx * (1 - x), cx)]


def slab_kernel(kept, came, out):
    n = out.shape[0]
    slab = 128 // n
    _, cx, cy, _ = kept.shape
    lane = index_along((cy, 128), 1) // slab
    for f in range(2):
        for q in range(cx // n):
            planes = [kept[f, n * q + j] + came[f, n * q + j] for j in range(n)]
            for to in range(n):
                piece = jnp.zeros((cy, 128), jnp.float32)
                for j in range(n):
                    moved = pltpu.roll(planes[j], ((j - to) % n) * slab, 1)
                    piece = jnp.where(lane == j, moved, piece)
                out[to, f, q] = piece


def project_kernel(beta_prev, parts, vk, va, qk, qa, w_k, w_a, tile, *, n):
    s, x, y, c = places(2)
    slab = 128 // n
    for f, (q_ref, w) in enumerate(((qk, w_k), (qa, w_a))):
        for q in range(vk.shape[0] // n):
            whole = jnp.sum(parts[:, f, q], axis=0)
            for j in range(n):
                i = n * q + j
                w[i] = whole[:, slab * j : slab * (j + 1)] - beta_prev[...] * q_ref[i]

    def dot(a, b):
        return jnp.sum(jnp.sum(a * b, axis=0))

    wk, wa, v_k, v_a = w_k[...], w_a[...], vk[...], va[...]
    one = jnp.ones((1, 1), jnp.float32)
    wv = (dot(wk, v_k) + dot(wa, v_a)) * one
    vv = (dot(v_k, v_k) + dot(v_a, v_a)) * one
    a = jnp.where(vv > 0.0, wv / jnp.where(vv > 0.0, vv, 1.0), 0.0)
    u_k, u_a = wk - a * v_k, wa - a * v_a
    uv = (dot(u_k, v_k) + dot(u_a, v_a)) * one
    uu = (dot(u_k, u_k) + dot(u_a, u_a)) * one
    me = ((s * 2 + x) * 2 + y) * 2 + c
    lane = index_along((8, 128), 1)
    row = index_along((8, 128), 0)
    values = jnp.zeros((8, 128), jnp.float32)
    for i, value in enumerate((wv, vv, a, uv, uu)):
        values = jnp.where(row == i, value, values)
    tile[...] = jnp.where(lane == me, values, 0.0)


def final_kernel(tiles, w_k, w_a, vk, va, next_k, next_a, coefs, *, cells):
    tile = jnp.sum(tiles[...], axis=0)
    wv, vv, a, uv, uu = (tile[i : i + 1] for i in range(5))
    wv_sum = jnp.sum(wv, axis=1, keepdims=True)
    vv_sum = jnp.sum(vv, axis=1, keepdims=True)
    alpha = wv_sum / cells / (vv_sum / cells + eps_norm)
    off = alpha - a
    rr = jnp.sum(uu - 2.0 * off * uv + off * off * vv, axis=1, keepdims=True)
    beta = jnp.sqrt(rr / cells + eps_norm)
    next_k[...] = (w_k[...] - alpha * vk[...]) / beta
    next_a[...] = (w_a[...] - alpha * va[...]) / beta
    coefs[0] = jnp.sum(alpha)
    coefs[1] = jnp.sum(beta)


def f32(*shape):
    return jax.ShapeDtypeStruct(shape, jnp.float32)


def run(kernel, outs, *args, after=(), scratch=(), copies=0, smem=(), hbm=(), mib=16, in_smem_out=(), cost=None):
    vmem = pl.BlockSpec(memory_space=pltpu.VMEM)
    scalar = pl.BlockSpec(memory_space=pltpu.SMEM)
    far = pl.BlockSpec(memory_space=pltpu.HBM)
    held = [pltpu.VMEM(shape, dtype) for shape, dtype in scratch]
    used, waits = len(args), len(after)

    def body(*refs):
        kernel(*refs[:used], *refs[used + waits :])

    args = (*args, *after)
    if copies:
        held.append(pltpu.SemaphoreType.DMA((copies,)))
    return pl.pallas_call(
        body if waits else kernel,
        out_shape=tuple(outs),
        in_specs=[scalar if i in smem else far if i in hbm else vmem for i in range(len(args))],
        out_specs=tuple(scalar if i in in_smem_out else vmem for i in range(len(outs))),
        scratch_shapes=held,
        compiler_params=pltpu.CompilerParams(vmem_limit_bytes=mib * 2**20),
        cost_estimate=cost,
    )(*args)


HALO = 8


def per_device_paired(
    labels, kappa_table, absorb_table, background, det_cells,
    v_kappa, v_absorb, q_kappa, q_absorb, beta_prev,
):
    sources, cx, cy, cz = background.shape
    n = lax.axis_size("src")
    planes, rows = 2 * cx, 2 * cy + HALO
    ny = cy * lax.axis_size("gy")
    dets = det_cells.shape[0]
    cells = planes * ny * cz
    groups = cx // n

    def swap_x(value):
        return lax.ppermute(value, "gx", [(0, 1), (1, 0)])

    def swap_core(value):
        return lax.ppermute(value, "gy", [(0, 1), (1, 0), (2, 3), (3, 2)])

    def along_z(value, k):
        return lax.ppermute(value, "src", [(i, (i + k) % n) for i in range(n)])

    block = (cx, cy, cz)
    float_block = lambda *shape: (shape, jnp.float32)
    raw_labels = (block, jnp.int32)
    packed, message = run(
        pack_kernel, (f32(2, groups, cy, cz), f32(sources // 2 + 1, *block)),
        background, labels, v_kappa, v_absorb, hbm=(0, 1, 2, 3),
        scratch=(raw_labels, float_block(2, *v_kappa.shape)), copies=4, mib=60,
    )
    came = swap_x(message)
    slabs = [along_z(packed, k) for k in range(1, n)]
    (count,) = run(
        functools.partial(count_kernel, ny=ny, nz=cz, half=2 * cy, halo=HALO),
        (f32(planes, rows, cz),), det_cells.reshape(1, dets),
        cost=pl.CostEstimate(flops=2 * planes * rows * cz * dets, bytes_accessed=planes * rows * cz * 4, transcendentals=0),
    )
    (vector,) = run(
        functools.partial(unpack_kernel, n=n), (f32(2, *block),), v_kappa, v_absorb, *slabs, after=(count,)
    )
    vector_came = swap_x(vector)

    def to_edges(edge_other, edge_mine):
        return lax.ppermute(edge_other, "gy", [(1, 2), (2, 1)]), lax.ppermute(edge_mine, "gy", [(1, 3), (2, 0)])

    mine, fields, edge_other, edge_mine = run(
        photon_kernel,
        (f32(planes, cy, cz), f32(2, planes, cy, cz), f32(2, planes, HALO, cz), f32(2, planes, HALO, cz)),
        background, labels, came, after=(vector,), hbm=(0, 1), scratch=(raw_labels,), copies=3,
    )
    edges = to_edges(edge_other, edge_mine)
    got = swap_core(fields)
    frame, wide = (planes, rows, cz), (planes + 2, rows, cz)
    float_frame, float_wide = float_block(*frame), float_block(*wide)
    phi, diag, fx, fy, fz, sums = run(
        stencil_kernel,
        (f32(*wide), f32(*frame), f32(planes + 1, rows, cz), f32(*frame), f32(*frame), f32(2, 8, cz)),
        kappa_table, absorb_table, mine, fields, got, *edges, count,
        smem=(0, 1), scratch=(float_frame, float_wide),
    )
    fields, edge = run(
        vector_kernel, (f32(2, planes, cy, cz), f32(2, planes, HALO, cz)), vector, vector_came,
        after=(got, *edges),
    )
    edges = to_edges(edge, edge)
    got = swap_core(fields)
    change, sent = run(
        first_kernel, (f32(*frame), f32(planes + 4, HALO, cz)),
        phi, diag, fx, fy, fz, count, sums, fields, got, *edges,
        scratch=(float_wide, float_frame, float_frame, float_wide, float_wide),
    )
    heard = lax.ppermute(sent, "gy", [(i, (i + 2) % 4) for i in range(4)])
    own, message = run(
        functools.partial(second_kernel, dets=dets),
        (f32(2, planes, cy, cz), f32(2, planes, cy, cz)),
        phi, change, diag, fx, fy, fz, count, sent, heard,
        scratch=(float_frame, float_wide, float_wide, float_frame, float_frame),
    )
    kept, message = run(
        core_kernel, (f32(2, cx, cy, cz), f32(2, cx, cy, cz)), own, swap_core(message)
    )
    (pieces,) = run(slab_kernel, (f32(n, 2, groups, cy, cz),), kept, swap_x(message))
    parts = lax.all_to_all(pieces, "src", 0, 0)
    w_k, w_a, tile = run(
        functools.partial(project_kernel, n=n),
        (f32(*v_kappa.shape), f32(*v_kappa.shape), f32(8, 128)),
        beta_prev.reshape(1, 1), parts, v_kappa, v_absorb, q_kappa, q_absorb,
    )
    everyone = ("src", "gx", "gy")
    tiles = lax.all_to_all(jnp.broadcast_to(tile, (8 * n, 8, 128)), everyone, 0, 0)
    return tuple(run(
        functools.partial(final_kernel, cells=cells),
        (f32(*v_kappa.shape), f32(*v_kappa.shape), f32(2)),
        tiles, w_k, w_a, v_kappa, v_absorb, in_smem_out=(2,),
    ))


def paired_fits(mesh):
    return mesh.shape["gx"] == 2 and mesh.shape["gy"] == 4


def body_for(mesh):
    if not paired_fits(mesh):
        return per_device

    def chosen(*args):
        sources, cx, cy, cz = args[3].shape
        n = lax.axis_size("src")
        fits = sources == 4 and cz == 128 and cx % n == 0 and cz % n == 0 and cy % HALO == 0
        devices = 8 * n
        return (per_device_paired if fits and devices <= 128 else per_device)(*args)

    return chosen


def solution(mesh):
    return jax.shard_map(
        body_for(mesh),
        mesh=mesh,
        in_specs=(
            P("gx", "gy", None),
            P(),
            P(),
            P("src", "gx", "gy", None),
            P(),
            P("gx", "gy", "src"),
            P("gx", "gy", "src"),
            P("gx", "gy", "src"),
            P("gx", "gy", "src"),
            P(),
        ),
        out_specs=(P("gx", "gy", "src"), P("gx", "gy", "src"), P()),
        check_vma=False,
    )
```

```python
import functools

import jax
import jax.numpy as jnp
from jax import lax
from jax.experimental import pallas as pl
from jax.experimental.pallas import tpu as pltpu
from jax.sharding import PartitionSpec as P

ITERS = 6


lam_low = 0.02
lam_high = 24.1
eps_norm = 1e-06


def padded_2(block, sides, width):
    for axis, dim in sides:
        count = lax.axis_size(axis)
        forward = [(i, i + 1) for i in range(count - 1)]
        backward = [(target, source) for source, target in forward]
        low = lax.ppermute(
            lax.slice_in_dim(block, block.shape[dim] - width, None, axis=dim), axis, forward
        )
        high = lax.ppermute(lax.slice_in_dim(block, 0, width, axis=dim), axis, backward)
        block = jnp.concatenate([low, block, high], axis=dim)
    return block


def regional(labels, table):
    field = jnp.zeros(labels.shape, jnp.float32)
    for region in range(table.shape[0]):
        field = field + jnp.where(labels == region, table[region], 0.0)
    return field


def beside(padded):
    widths = [(0, 0)] * (padded.ndim - 1) + [(1, 1)]
    full = jnp.pad(padded, widths)
    return [
        full[..., 2:, 1:-1, 1:-1],
        full[..., :-2, 1:-1, 1:-1],
        full[..., 1:-1, 2:, 1:-1],
        full[..., 1:-1, :-2, 1:-1],
        full[..., 1:-1, 1:-1, 2:],
        full[..., 1:-1, 1:-1, :-2],
    ]


def chebyshev(rhs, apply_op):
    theta = 0.5 * (lam_high + lam_low)
    delta = 0.5 * (lam_high - lam_low)
    sigma = theta / delta
    rho = 1.0 / sigma
    solution = jnp.zeros_like(rhs)
    remain = rhs
    step_dir = rhs / theta
    for step in range(ITERS):
        solution = solution + step_dir
        if step + 1 < ITERS:
            remain = remain - apply_op(step_dir)
            rho_next = 1.0 / (2.0 * sigma - rho)
            step_dir = rho_next * rho * step_dir + 2.0 * rho_next / delta * remain
            rho = rho_next
    return solution


def per_device(
    labels,
    kappa_table,
    absorb_table,
    background,
    det_cells,
    v_kappa,
    v_absorb,
    q_kappa,
    q_absorb,
    beta_prev,
):
    sources, cx, cy, cz = background.shape
    kappa = regional(labels, kappa_table)
    absorb = regional(labels, absorb_table)
    full_k, full_a = (
        lax.all_gather(v_kappa, "src", axis=2, tiled=True),
        lax.all_gather(v_absorb, "src", axis=2, tiled=True),
    )
    stacked = jnp.concatenate([background, kappa[None], full_k[None]], axis=0)
    rims = padded_2(stacked, (("gx", 1), ("gy", 2)), 1)
    near_all = beside(rims)
    kappa_faces = [0.5 * (kappa + near[sources]) for near in near_all]
    vk_faces = [0.5 * (full_k + near[sources + 1]) for near in near_all]
    phi_near = [near[:sources] for near in near_all]

    def apply_op(field):
        padded = padded_2(field, (("gx", 1), ("gy", 2)), 1)
        result = absorb * field
        for face, near in zip(kappa_faces, beside(padded)):
            result = result + face * (field - near)
        return result

    rhs = full_a * background
    for face, near in zip(vk_faces, phi_near):
        rhs = rhs + face * (background - near)
    rhs = -rhs
    change = chebyshev(rhs, apply_op)
    span_y = cy * lax.axis_size("gy")
    ix = det_cells // (span_y * cz)
    iy = det_cells // cz % span_y
    iz = det_cells % cz
    anchor_x = lax.axis_index("gx") * cx
    anchor_y = lax.axis_index("gy") * cy
    owned = (ix >= anchor_x) & (ix < anchor_x + cx) & (iy >= anchor_y) & (iy < anchor_y + cy)
    local = jnp.where(owned, ((ix - anchor_x) * cy + (iy - anchor_y)) * cz + iz, 0)
    seen_part = jnp.where(owned[None, :], change.reshape(sources, -1)[:, local], 0.0)
    base_part = jnp.where(owned[None, :], background.reshape(sources, -1)[:, local], 0.0)
    seen, base = lax.psum((seen_part, base_part), ("gx", "gy"))
    total = jnp.sum(base, axis=1, keepdims=True)
    mean_base = total / det_cells.shape[0]
    ratio = base / total
    jv_vals = (seen - ratio * jnp.sum(seen, axis=1, keepdims=True)) / mean_base
    weight = (jv_vals - jnp.sum(ratio * jv_vals, axis=1, keepdims=True)) / mean_base
    deposit = jnp.where(owned[None, :], weight, 0.0)
    source = (
        jnp.zeros((sources, cx * cy * cz), jnp.float32)
        .at[:, local]
        .add(deposit)
        .reshape(change.shape)
    )
    dual = chebyshev(source, apply_op)
    dual_rims = padded_2(dual, (("gx", 1), ("gy", 2)), 1)
    grad_a = -jnp.sum(background * dual, axis=0)
    grad_k = jnp.zeros_like(kappa)
    for near_phi, near_dual in zip(phi_near, beside(dual_rims)):
        grad_k = grad_k - 0.5 * jnp.sum((background - near_phi) * (dual - near_dual), axis=0)
    summed_k, summed_a = lax.psum((grad_k, grad_a), "src")
    slab = v_kappa.shape[2]
    offset = lax.axis_index("src") * slab
    hv_k = lax.dynamic_slice_in_dim(summed_k, offset, slab, 2)
    hv_a = lax.dynamic_slice_in_dim(summed_a, offset, slab, 2)
    cell_count = cx * lax.axis_size("gx") * cy * lax.axis_size("gy") * cz
    w_k = hv_k - beta_prev[0] * q_kappa
    w_a = hv_a - beta_prev[0] * q_absorb
    local_wv = jnp.sum(w_k * v_kappa) + jnp.sum(w_a * v_absorb)
    local_vv = jnp.sum(v_kappa * v_kappa) + jnp.sum(v_absorb * v_absorb)
    wv_sum, vv_sum = lax.psum((local_wv, local_vv), ("src", "gx", "gy"))
    alpha = wv_sum / cell_count / (vv_sum / cell_count + eps_norm)
    r_k = w_k - alpha * v_kappa
    r_a = w_a - alpha * v_absorb
    rr_sum = lax.psum(jnp.sum(r_k * r_k) + jnp.sum(r_a * r_a), ("src", "gx", "gy"))
    beta = jnp.sqrt(rr_sum / cell_count + eps_norm)
    return (r_k / beta, r_a / beta, jnp.stack([alpha, beta]))


def chebyshev_scalars():
    theta = 0.5 * (lam_high + lam_low)
    delta = 0.5 * (lam_high - lam_low)
    sigma = theta / delta
    rho = 1.0 / sigma
    pairs = []
    for _ in range(ITERS - 1):
        rho_next = 1.0 / (2.0 * sigma - rho)
        pairs.append((rho_next * rho, 2.0 * rho_next / delta))
        rho = rho_next
    return theta, pairs


def places(split):
    g = lax.axis_index("gy")
    return lax.axis_index("src"), lax.axis_index("gx"), g // split, g % split


def shifted(value, step, axis):
    return pltpu.roll(value, step % value.shape[axis], axis)


def index_along(shape, axis):
    return lax.broadcasted_iota(jnp.int32, shape, axis)


def beyond(value, step, axis):
    size = value.shape[axis]
    at = index_along(value.shape, axis)
    edge = size - 1 if step == 1 else 0
    return jnp.where(at == edge, 0.0, shifted(value, -step, axis))


def packed_planes(ref, q):
    per = 128 // ref.shape[2]
    return jnp.concatenate([ref[per * q + j] for j in range(per)], axis=1)


def pack_kernel(bg, labels, vk, va, packed, message, raw, v_in, sems):
    _, x, _, _ = places(2)
    half = bg.shape[0] // 2
    copies = [
        pltpu.make_async_copy(src, dst, sems.at[i])
        for i, (src, dst) in enumerate((
            (vk, v_in.at[0]),
            (va, v_in.at[1]),
            (bg.at[pl.ds(half * (1 - x), half)], message.at[pl.ds(0, half)]),
            (labels, raw),
        ))
    ]
    for copy in copies:
        copy.start()
    for f in range(2):
        copies[f].wait()
        for q in range(packed.shape[1]):
            packed[f, q] = packed_planes(v_in.at[f], q)
    copies[3].wait()
    message[half] = raw[...].astype(jnp.float32)
    copies[2].wait()


def count_kernel(dets, count, *, ny, nz, half, halo):
    _, _, y, _ = places(2)
    planes, rows, _ = count.shape
    flat = dets[...]
    iz = flat % nz
    line = flat // nz
    iy = line % ny
    ix = line // ny
    row = iy - (half - halo) * y
    spot = jnp.where((row >= 0) & (row < rows), ix * rows + row, -1)
    dets_n = flat.shape[1]
    at_z = (index_along((nz, dets_n), 0) == iz).astype(jnp.float32).astype(jnp.bfloat16)

    def body(i, carry):
        here = index_along((2 * rows, dets_n), 0) + i * (2 * rows)
        hot = (here == spot).astype(jnp.float32).astype(jnp.bfloat16)
        found = lax.dot_general(hot, at_z, (((1,), (1,)), ((), ())), preferred_element_type=jnp.float32)
        count[pl.ds(2 * i, 2)] = found.reshape(2, rows, nz)
        return carry

    lax.fori_loop(0, planes // 2, body, 0)


def photon_kernel(bg, labels, msg, mine, fields, raw, sems):
    _, x, _, c = places(2)
    half = bg.shape[0] // 2
    cx = labels.shape[0]
    here, there = cx * x, cx * (1 - x)
    copies = [
        pltpu.make_async_copy(src, dst, sems.at[i])
        for i, (src, dst) in enumerate((
            (bg.at[half * x + c], mine.at[pl.ds(here, cx)]),
            (bg.at[half * x + 1 - c], fields.at[0, pl.ds(here, cx)]),
            (labels, raw),
        ))
    ]
    for copy in copies:
        copy.start()
    mine[pl.ds(there, cx)] = msg[c]
    fields[0, pl.ds(there, cx)] = msg[1 - c]
    fields[1, pl.ds(there, cx)] = msg[half]
    for copy in copies:
        copy.wait()
    fields[1, pl.ds(here, cx)] = raw[...].astype(jnp.float32)


def unpack_kernel(*refs):
    own, parts, full = refs[:2], refs[2:-1], refs[-1]
    n = len(parts) + 1
    s, _, _, _ = places(2)
    slab = 128 // n
    _, cx, cy, _ = full.shape
    lane = index_along((cy, 128), 1) // slab
    for f in range(2):
        for q in range(cx // n):
            blocks = [part[f, q] for part in parts]
            for j in range(n):
                plane = jnp.concatenate([own[f][n * q + j]] * n, axis=1)
                for k in range(1, n):
                    home = (s - k + n) % n
                    moved = pltpu.roll(blocks[k - 1], ((home - j + n) % n) * slab, 1)
                    plane = jnp.where(lane == home, moved, plane)
                full[f, n * q + j] = plane


def vector_kernel(own, came, fields):
    _, x, _, _ = places(2)
    cx = own.shape[1]
    fields[:, pl.ds(cx * x, cx)] = own[...]
    fields[:, pl.ds(cx * (1 - x), cx)] = came[...]


def edge_rows(ref, halo, y):
    return ref[pl.ds(0, ref.shape[0]), pl.ds((ref.shape[1] - halo) * (1 - y), halo), :]


def photon_edge_kernel(mine, fields, got, edge):
    _, _, y, c = places(2)
    halo = edge.shape[2]
    edge[0] = jnp.where(c != y, edge_rows(mine, halo, y), edge_rows(got.at[0], halo, y))
    edge[1] = jnp.where(c != y, edge_rows(fields.at[1], halo, y), edge_rows(got.at[1], halo, y))


def vector_edge_kernel(fields, got, edge):
    _, _, y, c = places(2)
    halo = edge.shape[2]
    for f in range(2):
        edge[f] = jnp.where(c != y, edge_rows(fields.at[f], halo, y), edge_rows(got.at[f], halo, y))


def solve(b, bufs, diag, fx, fy, fz, unroll):
    planes = b.shape[0]
    _, pairs = chebyshev_scalars()
    for step, (keep, push) in enumerate(pairs):
        src, dst = bufs[step % 2], bufs[(step + 1) % 2]

        def body(i, carry):
            u = src[i + 1]
            coef_y, coef_z = fy[i], fz[i]
            left = b[i] - diag[i] * u
            left = left + fx[i] * src[i] + fx[i + 1] * src[i + 2]
            left = left + coef_y * shifted(u, -1, 0) + shifted(coef_y * u, 1, 0)
            left = left + coef_z * shifted(u, -1, 1) + shifted(coef_z * u, 1, 1)
            change = u if step == 0 else u - dst[i + 1]
            dst[i + 1] = u + keep * change + push * left
            return carry

        lax.fori_loop(0, planes, body, 0, unroll=unroll)
    return bufs[len(pairs) % 2]


def folded(value):
    return jnp.sum(value.reshape(-1, 8, value.shape[1]), axis=0)


def framed(ref, shift, parts, planes, cy, halo, y, c):
    own, got, edge = parts
    there = pl.ds(shift, planes)
    base = halo * y
    ref[there, pl.ds(base + cy * c, cy), :] = own
    ref[there, pl.ds(base + cy * (1 - c), cy), :] = got
    ref[there, pl.ds(2 * cy * (1 - y), halo), :] = edge


def blank_ends(*refs):
    for ref in refs:
        blank = jnp.zeros(ref.shape[1:], jnp.float32)
        ref[0] = blank
        ref[ref.shape[0] - 1] = blank


def owned_rows(shape, base, count):
    at_row = index_along(shape, 0)
    return (at_row >= base) & (at_row < base + count)


def stencil_kernel(
    kap_table, abs_table, mine, fields, got, edge, count,
    phi, diag, fx, fy, fz, sums,
    labels, kap,
):
    _, _, y, c = places(2)
    planes, cy, lanes = mine.shape
    halo = edge.shape[2]
    rows = 2 * cy + halo
    place = (planes, cy, halo, y, c)
    framed(phi, 1, (mine[...], got[0], edge[0]), *place)
    framed(labels, 0, (fields[1], got[1], edge[1]), *place)
    blank_ends(phi, kap)
    blank = jnp.zeros((rows, lanes), jnp.float32)
    lane = index_along((rows, lanes), 1)
    kap_row, abs_row = blank, blank
    for region in range(kap_table.shape[0]):
        kap_row = jnp.where(lane == region, kap_table[region], kap_row)
        abs_row = jnp.where(lane == region, abs_table[region], abs_row)

    def look_up(i, carry):
        at = labels[i].astype(jnp.int32)
        kap[i + 1] = jnp.take_along_axis(kap_row, at, axis=1)
        diag[i] = jnp.take_along_axis(abs_row, at, axis=1)
        return carry

    lax.fori_loop(0, planes, look_up, 0, unroll=2)
    fx[0] = 0.5 * kap[1]
    owned = owned_rows((rows, lanes), halo * y, 2 * cy)

    def set_up(i, carry):
        k = kap[i + 1]
        along_x = 0.5 * (k + kap[i + 2])
        along_y, along_z = 0.5 * (k + beyond(k, 1, 0)), 0.5 * (k + beyond(k, 1, 1))
        fx[i + 1] = along_x
        fy[i] = jnp.where(index_along(k.shape, 0) == rows - 1, 0.0, along_y)
        fz[i] = jnp.where(lane == lanes - 1, 0.0, along_z)
        back_y, back_z = 0.5 * (k + beyond(k, -1, 0)), 0.5 * (k + beyond(k, -1, 1))
        diag[i] = diag[i] + fx[i] + along_x + along_y + back_y + along_z + back_z
        p = phi[i + 1]
        part = jnp.where(owned, count[i], 0.0) * p
        return carry[0] + folded(part), carry[1] + folded(part * p)

    zero = jnp.zeros((8, lanes), jnp.float32)
    sums[0], sums[1] = lax.fori_loop(0, planes, set_up, (zero, zero), unroll=2)


def first_kernel(
    phi, diag, fx, fy, fz, count, sums, fields, got, edge,
    change, message,
    vk, va, b, buf_a, buf_b,
):
    _, _, y, c = places(2)
    planes, rows, lanes = change.shape
    halo = edge.shape[2]
    cy = (rows - halo) // 2
    place = (planes, cy, halo, y, c)
    framed(vk, 1, (fields[0], got[0], edge[0]), *place)
    framed(va, 0, (fields[1], got[1], edge[1]), *place)
    blank_ends(vk, buf_a, buf_b)
    theta, _ = chebyshev_scalars()

    def set_up(i, carry):
        v, p = vk[i + 1], phi[i + 1]
        total = 0.5 * (v + vk[i]) * (p - phi[i]) + 0.5 * (v + vk[i + 2]) * (p - phi[i + 2])
        for axis in range(2):
            flow = 0.5 * (v + beyond(v, 1, axis)) * (p - beyond(p, 1, axis))
            first = index_along(v.shape, axis) == 0
            total = total + flow + jnp.where(first, 0.5 * v * p, -shifted(flow, 1, axis))
        total = -(va[i] * p + total)
        b[i] = total
        buf_a[i + 1] = total * (1.0 / theta)
        return carry

    lax.fori_loop(0, planes, set_up, 0, unroll=2)
    found = solve(b, (buf_a, buf_b), diag, fx, fy, fz, 8)
    owned = owned_rows((rows, lanes), halo * y, 2 * cy)

    def add_up(i, carry):
        u = found[i + 1]
        change[i] = u
        part = jnp.where(owned, count[i], 0.0) * u
        return carry[0] + folded(part), carry[1] + folded(part * phi[i + 1])

    zero = jnp.zeros((8, lanes), jnp.float32)
    seen, cross = lax.fori_loop(0, planes, add_up, (zero, zero), unroll=2)
    edge = (2 * cy - halo) * (1 - y) + halo * y
    message[pl.ds(0, planes)] = found[pl.ds(1, planes), pl.ds(edge, halo), :]
    for i, part in enumerate((sums[0], seen, cross, sums[1])):
        message[planes + i] = part


def second_kernel(
    phi, change, diag, fx, fy, fz, count, sent, came,
    own, message,
    b, buf_a, buf_b, grad_k, grad_a,
    *, dets,
):
    _, _, y, c = places(2)
    planes, rows, lanes = change.shape
    halo = came.shape[1]
    cy = (rows - halo) // 2
    base = halo * y
    edge = pl.ds(2 * cy * (1 - y), halo)
    one = jnp.ones((1, 1), jnp.float32)
    total, seen_sum, cross, square = (
        jnp.sum(sent[planes + i] + came[planes + i]) * one for i in range(4)
    )
    mean = total / dets
    part = seen_sum / total
    level = (cross - part * square) / (total * mean)
    inverse = 1.0 / mean
    blank_ends(buf_a, buf_b)
    theta, _ = chebyshev_scalars()

    def weighted(n, u, p):
        return n * (((u - p * part) * inverse - level) * inverse)

    def set_up(i, carry):
        value = weighted(count[i], change[i], phi[i + 1])
        b[i] = value
        buf_a[i + 1] = value * (1.0 / theta)
        value = weighted(count[i, edge, :], came[i], phi[i + 1, edge, :])
        b[i, edge, :] = value
        buf_a[i + 1, edge, :] = value * (1.0 / theta)
        return carry

    lax.fori_loop(0, planes, set_up, 0, unroll=2)
    dual = solve(b, (buf_a, buf_b), diag, fx, fy, fz, 8)

    def product(i, carry):
        p, u = phi[i + 1], dual[i + 1]
        grad = (p - phi[i]) * (u - dual[i]) + (p - phi[i + 2]) * (u - dual[i + 2])
        both = p * u
        for axis in range(2):
            flow = (p - beyond(p, 1, axis)) * (u - beyond(u, 1, axis))
            first = index_along(p.shape, axis) == 0
            grad = grad + flow + jnp.where(first, both, shifted(flow, 1, axis))
        grad_k[i] = -0.5 * grad
        grad_a[i] = -both
        for f, ref in enumerate((grad_k, grad_a)):
            own[f, i] = ref[i, pl.ds(base + cy * c, cy), :]
            message[f, i] = ref[i, pl.ds(base + cy * (1 - c), cy), :]
        return carry

    lax.fori_loop(0, planes, product, 0, unroll=2)


def core_kernel(own, came, kept, message):
    _, x, _, _ = places(2)
    cx = kept.shape[1]
    kept[...] = own[:, pl.ds(cx * x, cx)] + came[:, pl.ds(cx * x, cx)]
    message[...] = own[:, pl.ds(cx * (1 - x), cx)] + came[:, pl.ds(cx * (1 - x), cx)]


def slab_kernel(kept, came, *outs):
    s, _, _, _ = places(2)
    n = len(outs)
    slab = 128 // n
    _, cx, cy, _ = kept.shape
    lane = index_along((cy, 128), 1) // slab
    for f in range(2):
        for q in range(cx // n):
            planes = [kept[f, n * q + j] + came[f, n * q + j] for j in range(n)]
            for k in range(n):
                to = (s + k) % n
                piece = jnp.zeros((cy, 128), jnp.float32)
                for j in range(n):
                    moved = pltpu.roll(planes[j], ((j - to + n) % n) * slab, 1)
                    piece = jnp.where(lane == j, moved, piece)
                outs[k][f, q] = piece


def project_kernel(*refs, n):
    beta_prev = refs[0]
    parts = refs[1 : 1 + n]
    vk, va, qk, qa, w_k, w_a, tile = refs[1 + n :]
    s, x, y, c = places(2)
    slab = 128 // n
    for f, (q_ref, w) in enumerate(((qk, w_k), (qa, w_a))):
        for q in range(vk.shape[0] // n):
            whole = sum(part[f, q] for part in parts[1:]) + parts[0][f, q]
            for j in range(n):
                i = n * q + j
                w[i] = whole[:, slab * j : slab * (j + 1)] - beta_prev[...] * q_ref[i]

    def dot(a, b):
        return jnp.sum(jnp.sum(a * b, axis=0))

    wk, wa, v_k, v_a = w_k[...], w_a[...], vk[...], va[...]
    one = jnp.ones((1, 1), jnp.float32)
    wv = (dot(wk, v_k) + dot(wa, v_a)) * one
    vv = (dot(v_k, v_k) + dot(v_a, v_a)) * one
    a = jnp.where(vv > 0.0, wv / jnp.where(vv > 0.0, vv, 1.0), 0.0)
    u_k, u_a = wk - a * v_k, wa - a * v_a
    uv = (dot(u_k, v_k) + dot(u_a, v_a)) * one
    uu = (dot(u_k, u_k) + dot(u_a, u_a)) * one
    me = ((s * 2 + x) * 2 + y) * 2 + c
    lane = index_along((8, 128), 1)
    row = index_along((8, 128), 0)
    values = jnp.zeros((8, 128), jnp.float32)
    for i, value in enumerate((wv, vv, a, uv, uu)):
        values = jnp.where(row == i, value, values)
    tile[...] = jnp.where(lane == me, values, 0.0)


def final_kernel(tiles, w_k, w_a, vk, va, next_k, next_a, coefs, *, cells):
    tile = jnp.sum(tiles[...], axis=0)
    wv, vv, a, uv, uu = (tile[i : i + 1] for i in range(5))
    wv_sum = jnp.sum(wv, axis=1, keepdims=True)
    vv_sum = jnp.sum(vv, axis=1, keepdims=True)
    alpha = wv_sum / cells / (vv_sum / cells + eps_norm)
    off = alpha - a
    rr = jnp.sum(uu - 2.0 * off * uv + off * off * vv, axis=1, keepdims=True)
    beta = jnp.sqrt(rr / cells + eps_norm)
    next_k[...] = (w_k[...] - alpha * vk[...]) / beta
    next_a[...] = (w_a[...] - alpha * va[...]) / beta
    coefs[0] = jnp.sum(alpha)
    coefs[1] = jnp.sum(beta)


def f32(*shape):
    return jax.ShapeDtypeStruct(shape, jnp.float32)


def run(kernel, outs, *args, after=(), scratch=(), copies=0, smem=(), hbm=(), mib=16, in_smem_out=(), cost=None):
    vmem = pl.BlockSpec(memory_space=pltpu.VMEM)
    scalar = pl.BlockSpec(memory_space=pltpu.SMEM)
    far = pl.BlockSpec(memory_space=pltpu.HBM)
    held = [pltpu.VMEM(shape, dtype) for shape, dtype in scratch]
    used, waits = len(args), len(after)

    def body(*refs):
        kernel(*refs[:used], *refs[used + waits :])

    args = (*args, *after)
    if copies:
        held.append(pltpu.SemaphoreType.DMA((copies,)))
    return pl.pallas_call(
        body if waits else kernel,
        out_shape=tuple(outs),
        in_specs=[scalar if i in smem else far if i in hbm else vmem for i in range(len(args))],
        out_specs=tuple(scalar if i in in_smem_out else vmem for i in range(len(outs))),
        scratch_shapes=held,
        compiler_params=pltpu.CompilerParams(vmem_limit_bytes=mib * 2**20),
        cost_estimate=cost,
    )(*args)


HALO = 8


def per_device_paired(
    labels, kappa_table, absorb_table, background, det_cells,
    v_kappa, v_absorb, q_kappa, q_absorb, beta_prev,
):
    sources, cx, cy, cz = background.shape
    n = lax.axis_size("src")
    planes, rows = 2 * cx, 2 * cy + HALO
    ny = cy * lax.axis_size("gy")
    dets = det_cells.shape[0]
    cells = planes * ny * cz
    groups = cx // n

    def swap_x(value):
        return lax.ppermute(value, "gx", [(0, 1), (1, 0)])

    def swap_core(value):
        return lax.ppermute(value, "gy", [(0, 1), (1, 0), (2, 3), (3, 2)])

    def along_z(value, k):
        return lax.ppermute(value, "src", [(i, (i + k) % n) for i in range(n)])

    block = (cx, cy, cz)
    float_block = lambda *shape: (shape, jnp.float32)
    raw_labels = (block, jnp.int32)
    packed, message = run(
        pack_kernel, (f32(2, groups, cy, cz), f32(sources // 2 + 1, *block)),
        background, labels, v_kappa, v_absorb, hbm=(0, 1, 2, 3),
        scratch=(raw_labels, float_block(2, *v_kappa.shape)), copies=4, mib=60,
    )
    came = swap_x(message)
    slabs = [along_z(packed, k) for k in range(1, n)]
    (count,) = run(
        functools.partial(count_kernel, ny=ny, nz=cz, half=2 * cy, halo=HALO),
        (f32(planes, rows, cz),), det_cells.reshape(1, dets),
        cost=pl.CostEstimate(flops=2 * planes * rows * cz * dets, bytes_accessed=planes * rows * cz * 4, transcendentals=0),
    )

    def across_y(value):
        return lax.ppermute(value, "gy", [(i, (i + 2) % 4) for i in range(4)])

    edges = (f32(2, planes, HALO, cz),)
    (half_vector,) = run(unpack_kernel, (f32(2, *block),), v_kappa, v_absorb, *slabs, after=(count,))
    half_came = swap_x(half_vector)
    mine, fields = run(
        photon_kernel, (f32(planes, cy, cz), f32(2, planes, cy, cz)),
        background, labels, came, after=(half_vector,), hbm=(0, 1), scratch=(raw_labels,), copies=3,
    )
    got = swap_core(fields)
    (sent,) = run(photon_edge_kernel, edges, mine, fields, got)
    halo = across_y(sent)
    (vector,) = run(vector_kernel, (f32(2, planes, cy, cz),), half_vector, half_came, after=(halo,))
    vector_got = swap_core(vector)
    (vector_sent,) = run(vector_edge_kernel, edges, vector, vector_got)
    frame, wide = (planes, rows, cz), (planes + 2, rows, cz)
    float_frame, float_wide = float_block(*frame), float_block(*wide)
    phi, diag, fx, fy, fz, sums = run(
        stencil_kernel,
        (f32(*wide), f32(*frame), f32(planes + 1, rows, cz), f32(*frame), f32(*frame), f32(2, 8, cz)),
        kappa_table, absorb_table, mine, fields, got, halo, count, after=(vector_sent,),
        smem=(0, 1), scratch=(float_frame, float_wide),
    )
    change, sent = run(
        first_kernel, (f32(*frame), f32(planes + 4, HALO, cz)),
        phi, diag, fx, fy, fz, count, sums, vector, vector_got, across_y(vector_sent),
        scratch=(float_wide, float_frame, float_frame, float_wide, float_wide),
    )
    heard = across_y(sent)
    own, message = run(
        functools.partial(second_kernel, dets=dets),
        (f32(2, planes, cy, cz), f32(2, planes, cy, cz)),
        phi, change, diag, fx, fy, fz, count, sent, heard,
        scratch=(float_frame, float_wide, float_wide, float_frame, float_frame),
    )
    kept, message = run(
        core_kernel, (f32(2, cx, cy, cz), f32(2, cx, cy, cz)), own, swap_core(message)
    )
    pieces = run(
        slab_kernel, [f32(2, groups, cy, cz)] * n, kept, swap_x(message)
    )
    parts = [pieces[0]] + [along_z(pieces[k], k) for k in range(1, n)]
    w_k, w_a, tile = run(
        functools.partial(project_kernel, n=n),
        (f32(*v_kappa.shape), f32(*v_kappa.shape), f32(8, 128)),
        beta_prev.reshape(1, 1), *parts, v_kappa, v_absorb, q_kappa, q_absorb,
    )
    everyone = ("src", "gx", "gy")
    tiles = lax.all_to_all(jnp.broadcast_to(tile, (8 * n, 8, 128)), everyone, 0, 0)
    return tuple(run(
        functools.partial(final_kernel, cells=cells),
        (f32(*v_kappa.shape), f32(*v_kappa.shape), f32(2)),
        tiles, w_k, w_a, v_kappa, v_absorb, in_smem_out=(2,),
    ))


def paired_fits(mesh):
    return mesh.shape["gx"] == 2 and mesh.shape["gy"] == 4


def body_for(mesh):
    if not paired_fits(mesh):
        return per_device

    def chosen(*args):
        sources, cx, cy, cz = args[3].shape
        n = lax.axis_size("src")
        fits = sources == 4 and cz == 128 and cx % n == 0 and cz % n == 0 and cy % HALO == 0
        devices = 8 * n
        return (per_device_paired if fits and devices <= 128 else per_device)(*args)

    return chosen


def solution(mesh):
    return jax.shard_map(
        body_for(mesh),
        mesh=mesh,
        in_specs=(
            P("gx", "gy", None),
            P(),
            P(),
            P("src", "gx", "gy", None),
            P(),
            P("gx", "gy", "src"),
            P("gx", "gy", "src"),
            P("gx", "gy", "src"),
            P("gx", "gy", "src"),
            P(),
        ),
        out_specs=(P("gx", "gy", "src"), P("gx", "gy", "src"), P()),
        check_vma=False,
    )
```

```python
import functools

import jax
import jax.numpy as jnp
from jax import lax
from jax.experimental import pallas as pl
from jax.experimental.pallas import tpu as pltpu
from jax.sharding import PartitionSpec as P

ITERS = 6


lam_low = 0.02
lam_high = 24.1
eps_norm = 1e-06


def padded_2(block, sides, width):
    for axis, dim in sides:
        count = lax.axis_size(axis)
        forward = [(i, i + 1) for i in range(count - 1)]
        backward = [(target, source) for source, target in forward]
        low = lax.ppermute(
            lax.slice_in_dim(block, block.shape[dim] - width, None, axis=dim), axis, forward
        )
        high = lax.ppermute(lax.slice_in_dim(block, 0, width, axis=dim), axis, backward)
        block = jnp.concatenate([low, block, high], axis=dim)
    return block


def regional(labels, table):
    field = jnp.zeros(labels.shape, jnp.float32)
    for region in range(table.shape[0]):
        field = field + jnp.where(labels == region, table[region], 0.0)
    return field


def beside(padded):
    widths = [(0, 0)] * (padded.ndim - 1) + [(1, 1)]
    full = jnp.pad(padded, widths)
    return [
        full[..., 2:, 1:-1, 1:-1],
        full[..., :-2, 1:-1, 1:-1],
        full[..., 1:-1, 2:, 1:-1],
        full[..., 1:-1, :-2, 1:-1],
        full[..., 1:-1, 1:-1, 2:],
        full[..., 1:-1, 1:-1, :-2],
    ]


def chebyshev(rhs, apply_op):
    theta = 0.5 * (lam_high + lam_low)
    delta = 0.5 * (lam_high - lam_low)
    sigma = theta / delta
    rho = 1.0 / sigma
    solution = jnp.zeros_like(rhs)
    remain = rhs
    step_dir = rhs / theta
    for step in range(ITERS):
        solution = solution + step_dir
        if step + 1 < ITERS:
            remain = remain - apply_op(step_dir)
            rho_next = 1.0 / (2.0 * sigma - rho)
            step_dir = rho_next * rho * step_dir + 2.0 * rho_next / delta * remain
            rho = rho_next
    return solution


def per_device(
    labels,
    kappa_table,
    absorb_table,
    background,
    det_cells,
    v_kappa,
    v_absorb,
    q_kappa,
    q_absorb,
    beta_prev,
):
    sources, cx, cy, cz = background.shape
    kappa = regional(labels, kappa_table)
    absorb = regional(labels, absorb_table)
    full_k, full_a = (
        lax.all_gather(v_kappa, "src", axis=2, tiled=True),
        lax.all_gather(v_absorb, "src", axis=2, tiled=True),
    )
    stacked = jnp.concatenate([background, kappa[None], full_k[None]], axis=0)
    rims = padded_2(stacked, (("gx", 1), ("gy", 2)), 1)
    near_all = beside(rims)
    kappa_faces = [0.5 * (kappa + near[sources]) for near in near_all]
    vk_faces = [0.5 * (full_k + near[sources + 1]) for near in near_all]
    phi_near = [near[:sources] for near in near_all]

    def apply_op(field):
        padded = padded_2(field, (("gx", 1), ("gy", 2)), 1)
        result = absorb * field
        for face, near in zip(kappa_faces, beside(padded)):
            result = result + face * (field - near)
        return result

    rhs = full_a * background
    for face, near in zip(vk_faces, phi_near):
        rhs = rhs + face * (background - near)
    rhs = -rhs
    change = chebyshev(rhs, apply_op)
    span_y = cy * lax.axis_size("gy")
    ix = det_cells // (span_y * cz)
    iy = det_cells // cz % span_y
    iz = det_cells % cz
    anchor_x = lax.axis_index("gx") * cx
    anchor_y = lax.axis_index("gy") * cy
    owned = (ix >= anchor_x) & (ix < anchor_x + cx) & (iy >= anchor_y) & (iy < anchor_y + cy)
    local = jnp.where(owned, ((ix - anchor_x) * cy + (iy - anchor_y)) * cz + iz, 0)
    seen_part = jnp.where(owned[None, :], change.reshape(sources, -1)[:, local], 0.0)
    base_part = jnp.where(owned[None, :], background.reshape(sources, -1)[:, local], 0.0)
    seen, base = lax.psum((seen_part, base_part), ("gx", "gy"))
    total = jnp.sum(base, axis=1, keepdims=True)
    mean_base = total / det_cells.shape[0]
    ratio = base / total
    jv_vals = (seen - ratio * jnp.sum(seen, axis=1, keepdims=True)) / mean_base
    weight = (jv_vals - jnp.sum(ratio * jv_vals, axis=1, keepdims=True)) / mean_base
    deposit = jnp.where(owned[None, :], weight, 0.0)
    source = (
        jnp.zeros((sources, cx * cy * cz), jnp.float32)
        .at[:, local]
        .add(deposit)
        .reshape(change.shape)
    )
    dual = chebyshev(source, apply_op)
    dual_rims = padded_2(dual, (("gx", 1), ("gy", 2)), 1)
    grad_a = -jnp.sum(background * dual, axis=0)
    grad_k = jnp.zeros_like(kappa)
    for near_phi, near_dual in zip(phi_near, beside(dual_rims)):
        grad_k = grad_k - 0.5 * jnp.sum((background - near_phi) * (dual - near_dual), axis=0)
    summed_k, summed_a = lax.psum((grad_k, grad_a), "src")
    slab = v_kappa.shape[2]
    offset = lax.axis_index("src") * slab
    hv_k = lax.dynamic_slice_in_dim(summed_k, offset, slab, 2)
    hv_a = lax.dynamic_slice_in_dim(summed_a, offset, slab, 2)
    cell_count = cx * lax.axis_size("gx") * cy * lax.axis_size("gy") * cz
    w_k = hv_k - beta_prev[0] * q_kappa
    w_a = hv_a - beta_prev[0] * q_absorb
    local_wv = jnp.sum(w_k * v_kappa) + jnp.sum(w_a * v_absorb)
    local_vv = jnp.sum(v_kappa * v_kappa) + jnp.sum(v_absorb * v_absorb)
    wv_sum, vv_sum = lax.psum((local_wv, local_vv), ("src", "gx", "gy"))
    alpha = wv_sum / cell_count / (vv_sum / cell_count + eps_norm)
    r_k = w_k - alpha * v_kappa
    r_a = w_a - alpha * v_absorb
    rr_sum = lax.psum(jnp.sum(r_k * r_k) + jnp.sum(r_a * r_a), ("src", "gx", "gy"))
    beta = jnp.sqrt(rr_sum / cell_count + eps_norm)
    return (r_k / beta, r_a / beta, jnp.stack([alpha, beta]))


def chebyshev_scalars():
    theta = 0.5 * (lam_high + lam_low)
    delta = 0.5 * (lam_high - lam_low)
    sigma = theta / delta
    rho = 1.0 / sigma
    pairs = []
    for _ in range(ITERS - 1):
        rho_next = 1.0 / (2.0 * sigma - rho)
        pairs.append((rho_next * rho, 2.0 * rho_next / delta))
        rho = rho_next
    return theta, pairs


def places(split):
    g = lax.axis_index("gy")
    return lax.axis_index("src"), lax.axis_index("gx"), g // split, g % split


def shifted(value, step, axis):
    return pltpu.roll(value, step % value.shape[axis], axis)


def index_along(shape, axis):
    return lax.broadcasted_iota(jnp.int32, shape, axis)


def beyond(value, step, axis):
    size = value.shape[axis]
    at = index_along(value.shape, axis)
    edge = size - 1 if step == 1 else 0
    return jnp.where(at == edge, 0.0, shifted(value, -step, axis))


def packed_planes(ref, q):
    per = 128 // ref.shape[2]
    return jnp.concatenate([ref[per * q + j] for j in range(per)], axis=1)


def pack_kernel(bg, labels, vk, va, packed, message, raw, v_in, sems):
    _, x, _, _ = places(2)
    half = bg.shape[0] // 2
    copies = [
        pltpu.make_async_copy(src, dst, sems.at[i])
        for i, (src, dst) in enumerate((
            (vk, v_in.at[0]),
            (va, v_in.at[1]),
            (bg.at[pl.ds(half * (1 - x), half)], message.at[pl.ds(0, half)]),
            (labels, raw),
        ))
    ]
    for copy in copies:
        copy.start()
    for f in range(2):
        copies[f].wait()
        for q in range(packed.shape[1]):
            packed[f, q] = packed_planes(v_in.at[f], q)
    copies[3].wait()
    message[half] = raw[...].astype(jnp.float32)
    copies[2].wait()


def count_kernel(dets, count, *, ny, nz, half, halo):
    _, _, y, _ = places(2)
    planes, rows, _ = count.shape
    flat = dets[...]
    iz = flat % nz
    line = flat // nz
    iy = line % ny
    ix = line // ny
    row = iy - (half - halo) * y
    spot = jnp.where((row >= 0) & (row < rows), ix * rows + row, -1)
    dets_n = flat.shape[1]
    at_z = (index_along((nz, dets_n), 0) == iz).astype(jnp.float32).astype(jnp.bfloat16)

    def body(i, carry):
        here = index_along((2 * rows, dets_n), 0) + i * (2 * rows)
        hot = (here == spot).astype(jnp.float32).astype(jnp.bfloat16)
        found = lax.dot_general(hot, at_z, (((1,), (1,)), ((), ())), preferred_element_type=jnp.float32)
        count[pl.ds(2 * i, 2)] = found.reshape(2, rows, nz)
        return carry

    lax.fori_loop(0, planes // 2, body, 0)


def photon_kernel(bg, labels, msg, mine, fields, raw, sems):
    _, x, _, c = places(2)
    half = bg.shape[0] // 2
    cx = labels.shape[0]
    here, there = cx * x, cx * (1 - x)
    copies = [
        pltpu.make_async_copy(src, dst, sems.at[i])
        for i, (src, dst) in enumerate((
            (bg.at[half * x + c], mine.at[pl.ds(here, cx)]),
            (bg.at[half * x + 1 - c], fields.at[0, pl.ds(here, cx)]),
            (labels, raw),
        ))
    ]
    for copy in copies:
        copy.start()
    mine[pl.ds(there, cx)] = msg[c]
    fields[0, pl.ds(there, cx)] = msg[1 - c]
    fields[1, pl.ds(there, cx)] = msg[half]
    for copy in copies:
        copy.wait()
    fields[1, pl.ds(here, cx)] = raw[...].astype(jnp.float32)


def unpack_kernel(*refs):
    own, parts, full = refs[:2], refs[2:-1], refs[-1]
    n = len(parts) + 1
    s, _, _, _ = places(2)
    slab = 128 // n
    _, cx, cy, _ = full.shape
    lane = index_along((cy, 128), 1) // slab
    for f in range(2):
        for q in range(cx // n):
            blocks = [part[f, q] for part in parts]
            for j in range(n):
                plane = jnp.concatenate([own[f][n * q + j]] * n, axis=1)
                for k in range(1, n):
                    home = (s - k + n) % n
                    moved = pltpu.roll(blocks[k - 1], ((home - j + n) % n) * slab, 1)
                    plane = jnp.where(lane == home, moved, plane)
                full[f, n * q + j] = plane


def vector_kernel(own, came, fields):
    _, x, _, _ = places(2)
    cx = own.shape[1]
    fields[:, pl.ds(cx * x, cx)] = own[...]
    fields[:, pl.ds(cx * (1 - x), cx)] = came[...]


def edge_rows(ref, halo, y):
    return ref[pl.ds(0, ref.shape[0]), pl.ds((ref.shape[1] - halo) * (1 - y), halo), :]


def photon_edge_kernel(mine, fields, got, edge):
    _, _, y, c = places(2)
    halo = edge.shape[2]
    edge[0] = jnp.where(c != y, edge_rows(mine, halo, y), edge_rows(got.at[0], halo, y))
    edge[1] = jnp.where(c != y, edge_rows(fields.at[1], halo, y), edge_rows(got.at[1], halo, y))


def vector_edge_kernel(fields, got, edge):
    _, _, y, c = places(2)
    halo = edge.shape[2]
    for f in range(2):
        edge[f] = jnp.where(c != y, edge_rows(fields.at[f], halo, y), edge_rows(got.at[f], halo, y))


def solve(b, bufs, diag, fx, fy, fz, unroll):
    planes = b.shape[0]
    _, pairs = chebyshev_scalars()
    for step, (keep, push) in enumerate(pairs):
        src, dst = bufs[step % 2], bufs[(step + 1) % 2]

        def body(i, carry):
            u = src[i + 1]
            coef_y, coef_z = fy[i], fz[i]
            left = b[i] - diag[i] * u
            left = left + fx[i] * src[i] + fx[i + 1] * src[i + 2]
            left = left + coef_y * shifted(u, -1, 0) + shifted(coef_y * u, 1, 0)
            left = left + coef_z * shifted(u, -1, 1) + shifted(coef_z * u, 1, 1)
            change = u if step == 0 else u - dst[i + 1]
            dst[i + 1] = u + keep * change + push * left
            return carry

        lax.fori_loop(0, planes, body, 0, unroll=unroll)
    return bufs[len(pairs) % 2]


def folded(value):
    return jnp.sum(value.reshape(-1, 8, value.shape[1]), axis=0)


def framed(ref, shift, parts, planes, cy, halo, y, c):
    own, got, edge = parts
    there = pl.ds(shift, planes)
    base = halo * y
    ref[there, pl.ds(base + cy * c, cy), :] = own
    ref[there, pl.ds(base + cy * (1 - c), cy), :] = got
    ref[there, pl.ds(2 * cy * (1 - y), halo), :] = edge


def blank_ends(*refs):
    for ref in refs:
        blank = jnp.zeros(ref.shape[1:], jnp.float32)
        ref[0] = blank
        ref[ref.shape[0] - 1] = blank


def owned_rows(shape, base, count):
    at_row = index_along(shape, 0)
    return (at_row >= base) & (at_row < base + count)


def stencil_kernel(
    kap_table, abs_table, mine, fields, got, edge, count,
    phi, diag, fx, fy, fz, sums,
    labels, kap,
):
    _, _, y, c = places(2)
    planes, cy, lanes = mine.shape
    halo = edge.shape[2]
    rows = 2 * cy + halo
    place = (planes, cy, halo, y, c)
    framed(phi, 1, (mine[...], got[0], edge[0]), *place)
    framed(labels, 0, (fields[1], got[1], edge[1]), *place)
    blank_ends(phi, kap)
    blank = jnp.zeros((rows, lanes), jnp.float32)
    lane = index_along((rows, lanes), 1)
    kap_row, abs_row = blank, blank
    for region in range(kap_table.shape[0]):
        kap_row = jnp.where(lane == region, kap_table[region], kap_row)
        abs_row = jnp.where(lane == region, abs_table[region], abs_row)

    def look_up(i, carry):
        at = labels[i].astype(jnp.int32)
        kap[i + 1] = jnp.take_along_axis(kap_row, at, axis=1)
        diag[i] = jnp.take_along_axis(abs_row, at, axis=1)
        return carry

    lax.fori_loop(0, planes, look_up, 0, unroll=4)
    fx[0] = 0.5 * kap[1]
    owned = owned_rows((rows, lanes), halo * y, 2 * cy)

    def set_up(i, carry):
        k = kap[i + 1]
        along_x = 0.5 * (k + kap[i + 2])
        along_y, along_z = 0.5 * (k + beyond(k, 1, 0)), 0.5 * (k + beyond(k, 1, 1))
        fx[i + 1] = along_x
        fy[i] = jnp.where(index_along(k.shape, 0) == rows - 1, 0.0, along_y)
        fz[i] = jnp.where(lane == lanes - 1, 0.0, along_z)
        back_y, back_z = 0.5 * (k + beyond(k, -1, 0)), 0.5 * (k + beyond(k, -1, 1))
        diag[i] = diag[i] + fx[i] + along_x + along_y + back_y + along_z + back_z
        p = phi[i + 1]
        part = jnp.where(owned, count[i], 0.0) * p
        return carry[0] + folded(part), carry[1] + folded(part * p)

    zero = jnp.zeros((8, lanes), jnp.float32)
    sums[0], sums[1] = lax.fori_loop(0, planes, set_up, (zero, zero), unroll=4)


def first_kernel(
    phi, diag, fx, fy, fz, count, sums, fields, got, edge,
    change, message,
    vk, va, b, buf_a, buf_b,
):
    _, _, y, c = places(2)
    planes, rows, lanes = change.shape
    halo = edge.shape[2]
    cy = (rows - halo) // 2
    place = (planes, cy, halo, y, c)
    framed(vk, 1, (fields[0], got[0], edge[0]), *place)
    framed(va, 0, (fields[1], got[1], edge[1]), *place)
    blank_ends(vk, buf_a, buf_b)
    theta, _ = chebyshev_scalars()

    def set_up(i, carry):
        v, p = vk[i + 1], phi[i + 1]
        total = 0.5 * (v + vk[i]) * (p - phi[i]) + 0.5 * (v + vk[i + 2]) * (p - phi[i + 2])
        for axis in range(2):
            flow = 0.5 * (v + beyond(v, 1, axis)) * (p - beyond(p, 1, axis))
            first = index_along(v.shape, axis) == 0
            total = total + flow + jnp.where(first, 0.5 * v * p, -shifted(flow, 1, axis))
        total = -(va[i] * p + total)
        b[i] = total
        buf_a[i + 1] = total * (1.0 / theta)
        return carry

    lax.fori_loop(0, planes, set_up, 0, unroll=4)
    found = solve(b, (buf_a, buf_b), diag, fx, fy, fz, 16)
    owned = owned_rows((rows, lanes), halo * y, 2 * cy)

    def add_up(i, carry):
        u = found[i + 1]
        change[i] = u
        part = jnp.where(owned, count[i], 0.0) * u
        return carry[0] + folded(part), carry[1] + folded(part * phi[i + 1])

    zero = jnp.zeros((8, lanes), jnp.float32)
    seen, cross = lax.fori_loop(0, planes, add_up, (zero, zero), unroll=4)
    edge = (2 * cy - halo) * (1 - y) + halo * y
    message[pl.ds(0, planes)] = found[pl.ds(1, planes), pl.ds(edge, halo), :]
    for i, part in enumerate((sums[0], seen, cross, sums[1])):
        message[planes + i] = part


def second_kernel(
    phi, change, diag, fx, fy, fz, count, sent, came,
    own, message,
    b, buf_a, buf_b, grad_k, grad_a,
    *, dets,
):
    _, _, y, c = places(2)
    planes, rows, lanes = change.shape
    halo = came.shape[1]
    cy = (rows - halo) // 2
    base = halo * y
    edge = pl.ds(2 * cy * (1 - y), halo)
    one = jnp.ones((1, 1), jnp.float32)
    total, seen_sum, cross, square = (
        jnp.sum(sent[planes + i] + came[planes + i]) * one for i in range(4)
    )
    mean = total / dets
    part = seen_sum / total
    level = (cross - part * square) / (total * mean)
    inverse = 1.0 / mean
    blank_ends(buf_a, buf_b)
    theta, _ = chebyshev_scalars()

    def weighted(n, u, p):
        return n * (((u - p * part) * inverse - level) * inverse)

    def set_up(i, carry):
        value = weighted(count[i], change[i], phi[i + 1])
        b[i] = value
        buf_a[i + 1] = value * (1.0 / theta)
        value = weighted(count[i, edge, :], came[i], phi[i + 1, edge, :])
        b[i, edge, :] = value
        buf_a[i + 1, edge, :] = value * (1.0 / theta)
        return carry

    lax.fori_loop(0, planes, set_up, 0, unroll=4)
    dual = solve(b, (buf_a, buf_b), diag, fx, fy, fz, 16)

    def product(i, carry):
        p, u = phi[i + 1], dual[i + 1]
        grad = (p - phi[i]) * (u - dual[i]) + (p - phi[i + 2]) * (u - dual[i + 2])
        both = p * u
        for axis in range(2):
            flow = (p - beyond(p, 1, axis)) * (u - beyond(u, 1, axis))
            first = index_along(p.shape, axis) == 0
            grad = grad + flow + jnp.where(first, both, shifted(flow, 1, axis))
        grad_k[i] = -0.5 * grad
        grad_a[i] = -both
        for f, ref in enumerate((grad_k, grad_a)):
            own[f, i] = ref[i, pl.ds(base + cy * c, cy), :]
            message[f, i] = ref[i, pl.ds(base + cy * (1 - c), cy), :]
        return carry

    lax.fori_loop(0, planes, product, 0, unroll=4)


def core_kernel(own, came, kept, message):
    _, x, _, _ = places(2)
    cx = kept.shape[1]
    kept[...] = own[:, pl.ds(cx * x, cx)] + came[:, pl.ds(cx * x, cx)]
    message[...] = own[:, pl.ds(cx * (1 - x), cx)] + came[:, pl.ds(cx * (1 - x), cx)]


def slab_kernel(kept, came, *outs):
    s, _, _, _ = places(2)
    n = len(outs)
    slab = 128 // n
    _, cx, cy, _ = kept.shape
    lane = index_along((cy, 128), 1) // slab
    for f in range(2):
        for q in range(cx // n):
            planes = [kept[f, n * q + j] + came[f, n * q + j] for j in range(n)]
            for k in range(n):
                to = (s + k) % n
                piece = jnp.zeros((cy, 128), jnp.float32)
                for j in range(n):
                    moved = pltpu.roll(planes[j], ((j - to + n) % n) * slab, 1)
                    piece = jnp.where(lane == j, moved, piece)
                outs[k][f, q] = piece


def project_kernel(*refs, n):
    beta_prev = refs[0]
    parts = refs[1 : 1 + n]
    vk, va, qk, qa, w_k, w_a, tile = refs[1 + n :]
    s, x, y, c = places(2)
    slab = 128 // n
    for f, (q_ref, w) in enumerate(((qk, w_k), (qa, w_a))):
        for q in range(vk.shape[0] // n):
            whole = sum(part[f, q] for part in parts[1:]) + parts[0][f, q]
            for j in range(n):
                i = n * q + j
                w[i] = whole[:, slab * j : slab * (j + 1)] - beta_prev[...] * q_ref[i]

    def dot(a, b):
        return jnp.sum(jnp.sum(a * b, axis=0))

    wk, wa, v_k, v_a = w_k[...], w_a[...], vk[...], va[...]
    one = jnp.ones((1, 1), jnp.float32)
    wv = (dot(wk, v_k) + dot(wa, v_a)) * one
    vv = (dot(v_k, v_k) + dot(v_a, v_a)) * one
    a = jnp.where(vv > 0.0, wv / jnp.where(vv > 0.0, vv, 1.0), 0.0)
    u_k, u_a = wk - a * v_k, wa - a * v_a
    uv = (dot(u_k, v_k) + dot(u_a, v_a)) * one
    uu = (dot(u_k, u_k) + dot(u_a, u_a)) * one
    me = ((s * 2 + x) * 2 + y) * 2 + c
    lane = index_along((8, 128), 1)
    row = index_along((8, 128), 0)
    values = jnp.zeros((8, 128), jnp.float32)
    for i, value in enumerate((wv, vv, a, uv, uu)):
        values = jnp.where(row == i, value, values)
    tile[...] = jnp.where(lane == me, values, 0.0)


def final_kernel(tiles, w_k, w_a, vk, va, next_k, next_a, coefs, *, cells):
    tile = jnp.sum(tiles[...], axis=0)
    wv, vv, a, uv, uu = (tile[i : i + 1] for i in range(5))
    wv_sum = jnp.sum(wv, axis=1, keepdims=True)
    vv_sum = jnp.sum(vv, axis=1, keepdims=True)
    alpha = wv_sum / cells / (vv_sum / cells + eps_norm)
    off = alpha - a
    rr = jnp.sum(uu - 2.0 * off * uv + off * off * vv, axis=1, keepdims=True)
    beta = jnp.sqrt(rr / cells + eps_norm)
    next_k[...] = (w_k[...] - alpha * vk[...]) / beta
    next_a[...] = (w_a[...] - alpha * va[...]) / beta
    coefs[0] = jnp.sum(alpha)
    coefs[1] = jnp.sum(beta)


def f32(*shape):
    return jax.ShapeDtypeStruct(shape, jnp.float32)


def run(kernel, outs, *args, after=(), scratch=(), copies=0, smem=(), hbm=(), mib=16, in_smem_out=(), cost=None):
    vmem = pl.BlockSpec(memory_space=pltpu.VMEM)
    scalar = pl.BlockSpec(memory_space=pltpu.SMEM)
    far = pl.BlockSpec(memory_space=pltpu.HBM)
    held = [pltpu.VMEM(shape, dtype) for shape, dtype in scratch]
    used, waits = len(args), len(after)

    def body(*refs):
        kernel(*refs[:used], *refs[used + waits :])

    args = (*args, *after)
    if copies:
        held.append(pltpu.SemaphoreType.DMA((copies,)))
    return pl.pallas_call(
        body if waits else kernel,
        out_shape=tuple(outs),
        in_specs=[scalar if i in smem else far if i in hbm else vmem for i in range(len(args))],
        out_specs=tuple(scalar if i in in_smem_out else vmem for i in range(len(outs))),
        scratch_shapes=held,
        compiler_params=pltpu.CompilerParams(vmem_limit_bytes=mib * 2**20),
        cost_estimate=cost,
    )(*args)


HALO = 8


def per_device_paired(
    labels, kappa_table, absorb_table, background, det_cells,
    v_kappa, v_absorb, q_kappa, q_absorb, beta_prev,
):
    sources, cx, cy, cz = background.shape
    n = lax.axis_size("src")
    planes, rows = 2 * cx, 2 * cy + HALO
    ny = cy * lax.axis_size("gy")
    dets = det_cells.shape[0]
    cells = planes * ny * cz
    groups = cx // n

    def swap_x(value):
        return lax.ppermute(value, "gx", [(0, 1), (1, 0)])

    def swap_core(value):
        return lax.ppermute(value, "gy", [(0, 1), (1, 0), (2, 3), (3, 2)])

    def along_z(value, k):
        return lax.ppermute(value, "src", [(i, (i + k) % n) for i in range(n)])

    block = (cx, cy, cz)
    float_block = lambda *shape: (shape, jnp.float32)
    raw_labels = (block, jnp.int32)
    packed, message = run(
        pack_kernel, (f32(2, groups, cy, cz), f32(sources // 2 + 1, *block)),
        background, labels, v_kappa, v_absorb, hbm=(0, 1, 2, 3),
        scratch=(raw_labels, float_block(2, *v_kappa.shape)), copies=4, mib=60,
    )
    came = swap_x(message)
    slabs = [along_z(packed, k) for k in range(1, n)]
    (count,) = run(
        functools.partial(count_kernel, ny=ny, nz=cz, half=2 * cy, halo=HALO),
        (f32(planes, rows, cz),), det_cells.reshape(1, dets),
        cost=pl.CostEstimate(flops=2 * planes * rows * cz * dets, bytes_accessed=planes * rows * cz * 4, transcendentals=0),
    )

    def across_y(value):
        return lax.ppermute(value, "gy", [(i, (i + 2) % 4) for i in range(4)])

    edges = (f32(2, planes, HALO, cz),)
    (half_vector,) = run(unpack_kernel, (f32(2, *block),), v_kappa, v_absorb, *slabs, after=(count,))
    half_came = swap_x(half_vector)
    mine, fields = run(
        photon_kernel, (f32(planes, cy, cz), f32(2, planes, cy, cz)),
        background, labels, came, after=(half_vector,), hbm=(0, 1), scratch=(raw_labels,), copies=3,
    )
    got = swap_core(fields)
    (vector,) = run(vector_kernel, (f32(2, planes, cy, cz),), half_vector, half_came)
    (sent,) = run(photon_edge_kernel, edges, mine, fields, got, after=(vector,))
    halo = across_y(sent)
    vector_got = swap_core(vector)
    (vector_sent,) = run(vector_edge_kernel, edges, vector, vector_got)
    frame, wide = (planes, rows, cz), (planes + 2, rows, cz)
    float_frame, float_wide = float_block(*frame), float_block(*wide)
    phi, diag, fx, fy, fz, sums = run(
        stencil_kernel,
        (f32(*wide), f32(*frame), f32(planes + 1, rows, cz), f32(*frame), f32(*frame), f32(2, 8, cz)),
        kappa_table, absorb_table, mine, fields, got, halo, count, after=(vector_sent,),
        smem=(0, 1), scratch=(float_frame, float_wide),
    )
    change, sent = run(
        first_kernel, (f32(*frame), f32(planes + 4, HALO, cz)),
        phi, diag, fx, fy, fz, count, sums, vector, vector_got, across_y(vector_sent),
        scratch=(float_wide, float_frame, float_frame, float_wide, float_wide),
    )
    heard = across_y(sent)
    own, message = run(
        functools.partial(second_kernel, dets=dets),
        (f32(2, planes, cy, cz), f32(2, planes, cy, cz)),
        phi, change, diag, fx, fy, fz, count, sent, heard,
        scratch=(float_frame, float_wide, float_wide, float_frame, float_frame),
    )
    kept, message = run(
        core_kernel, (f32(2, cx, cy, cz), f32(2, cx, cy, cz)), own, swap_core(message)
    )
    pieces = run(
        slab_kernel, [f32(2, groups, cy, cz)] * n, kept, swap_x(message)
    )
    parts = [pieces[0]] + [along_z(pieces[k], k) for k in range(1, n)]
    w_k, w_a, tile = run(
        functools.partial(project_kernel, n=n),
        (f32(*v_kappa.shape), f32(*v_kappa.shape), f32(8, 128)),
        beta_prev.reshape(1, 1), *parts, v_kappa, v_absorb, q_kappa, q_absorb,
    )
    everyone = ("src", "gx", "gy")
    tiles = lax.all_to_all(jnp.broadcast_to(tile, (8 * n, 8, 128)), everyone, 0, 0)
    return tuple(run(
        functools.partial(final_kernel, cells=cells),
        (f32(*v_kappa.shape), f32(*v_kappa.shape), f32(2)),
        tiles, w_k, w_a, v_kappa, v_absorb, in_smem_out=(2,),
    ))


def paired_fits(mesh):
    return mesh.shape["gx"] == 2 and mesh.shape["gy"] == 4


def body_for(mesh):
    if not paired_fits(mesh):
        return per_device

    def chosen(*args):
        sources, cx, cy, cz = args[3].shape
        n = lax.axis_size("src")
        fits = sources == 4 and cz == 128 and cx % n == 0 and cz % n == 0 and cy % HALO == 0
        devices = 8 * n
        return (per_device_paired if fits and devices <= 128 else per_device)(*args)

    return chosen


def solution(mesh):
    return jax.shard_map(
        body_for(mesh),
        mesh=mesh,
        in_specs=(
            P("gx", "gy", None),
            P(),
            P(),
            P("src", "gx", "gy", None),
            P(),
            P("gx", "gy", "src"),
            P("gx", "gy", "src"),
            P("gx", "gy", "src"),
            P("gx", "gy", "src"),
            P(),
        ),
        out_specs=(P("gx", "gy", "src"), P("gx", "gy", "src"), P()),
        check_vma=False,
    )
```

```python
import functools

import jax
import jax.numpy as jnp
from jax import lax
from jax.experimental import pallas as pl
from jax.experimental.pallas import tpu as pltpu
from jax.sharding import PartitionSpec as P

ITERS = 6


lam_low = 0.02
lam_high = 24.1
eps_norm = 1e-06


def padded_2(block, sides, width):
    for axis, dim in sides:
        count = lax.axis_size(axis)
        forward = [(i, i + 1) for i in range(count - 1)]
        backward = [(target, source) for source, target in forward]
        low = lax.ppermute(
            lax.slice_in_dim(block, block.shape[dim] - width, None, axis=dim), axis, forward
        )
        high = lax.ppermute(lax.slice_in_dim(block, 0, width, axis=dim), axis, backward)
        block = jnp.concatenate([low, block, high], axis=dim)
    return block


def regional(labels, table):
    field = jnp.zeros(labels.shape, jnp.float32)
    for region in range(table.shape[0]):
        field = field + jnp.where(labels == region, table[region], 0.0)
    return field


def beside(padded):
    widths = [(0, 0)] * (padded.ndim - 1) + [(1, 1)]
    full = jnp.pad(padded, widths)
    return [
        full[..., 2:, 1:-1, 1:-1],
        full[..., :-2, 1:-1, 1:-1],
        full[..., 1:-1, 2:, 1:-1],
        full[..., 1:-1, :-2, 1:-1],
        full[..., 1:-1, 1:-1, 2:],
        full[..., 1:-1, 1:-1, :-2],
    ]


def chebyshev(rhs, apply_op):
    theta = 0.5 * (lam_high + lam_low)
    delta = 0.5 * (lam_high - lam_low)
    sigma = theta / delta
    rho = 1.0 / sigma
    solution = jnp.zeros_like(rhs)
    remain = rhs
    step_dir = rhs / theta
    for step in range(ITERS):
        solution = solution + step_dir
        if step + 1 < ITERS:
            remain = remain - apply_op(step_dir)
            rho_next = 1.0 / (2.0 * sigma - rho)
            step_dir = rho_next * rho * step_dir + 2.0 * rho_next / delta * remain
            rho = rho_next
    return solution


def per_device(
    labels,
    kappa_table,
    absorb_table,
    background,
    det_cells,
    v_kappa,
    v_absorb,
    q_kappa,
    q_absorb,
    beta_prev,
):
    sources, cx, cy, cz = background.shape
    kappa = regional(labels, kappa_table)
    absorb = regional(labels, absorb_table)
    full_k, full_a = (
        lax.all_gather(v_kappa, "src", axis=2, tiled=True),
        lax.all_gather(v_absorb, "src", axis=2, tiled=True),
    )
    stacked = jnp.concatenate([background, kappa[None], full_k[None]], axis=0)
    rims = padded_2(stacked, (("gx", 1), ("gy", 2)), 1)
    near_all = beside(rims)
    kappa_faces = [0.5 * (kappa + near[sources]) for near in near_all]
    vk_faces = [0.5 * (full_k + near[sources + 1]) for near in near_all]
    phi_near = [near[:sources] for near in near_all]

    def apply_op(field):
        padded = padded_2(field, (("gx", 1), ("gy", 2)), 1)
        result = absorb * field
        for face, near in zip(kappa_faces, beside(padded)):
            result = result + face * (field - near)
        return result

    rhs = full_a * background
    for face, near in zip(vk_faces, phi_near):
        rhs = rhs + face * (background - near)
    rhs = -rhs
    change = chebyshev(rhs, apply_op)
    span_y = cy * lax.axis_size("gy")
    ix = det_cells // (span_y * cz)
    iy = det_cells // cz % span_y
    iz = det_cells % cz
    anchor_x = lax.axis_index("gx") * cx
    anchor_y = lax.axis_index("gy") * cy
    owned = (ix >= anchor_x) & (ix < anchor_x + cx) & (iy >= anchor_y) & (iy < anchor_y + cy)
    local = jnp.where(owned, ((ix - anchor_x) * cy + (iy - anchor_y)) * cz + iz, 0)
    seen_part = jnp.where(owned[None, :], change.reshape(sources, -1)[:, local], 0.0)
    base_part = jnp.where(owned[None, :], background.reshape(sources, -1)[:, local], 0.0)
    seen, base = lax.psum((seen_part, base_part), ("gx", "gy"))
    total = jnp.sum(base, axis=1, keepdims=True)
    mean_base = total / det_cells.shape[0]
    ratio = base / total
    jv_vals = (seen - ratio * jnp.sum(seen, axis=1, keepdims=True)) / mean_base
    weight = (jv_vals - jnp.sum(ratio * jv_vals, axis=1, keepdims=True)) / mean_base
    deposit = jnp.where(owned[None, :], weight, 0.0)
    source = (
        jnp.zeros((sources, cx * cy * cz), jnp.float32)
        .at[:, local]
        .add(deposit)
        .reshape(change.shape)
    )
    dual = chebyshev(source, apply_op)
    dual_rims = padded_2(dual, (("gx", 1), ("gy", 2)), 1)
    grad_a = -jnp.sum(background * dual, axis=0)
    grad_k = jnp.zeros_like(kappa)
    for near_phi, near_dual in zip(phi_near, beside(dual_rims)):
        grad_k = grad_k - 0.5 * jnp.sum((background - near_phi) * (dual - near_dual), axis=0)
    summed_k, summed_a = lax.psum((grad_k, grad_a), "src")
    slab = v_kappa.shape[2]
    offset = lax.axis_index("src") * slab
    hv_k = lax.dynamic_slice_in_dim(summed_k, offset, slab, 2)
    hv_a = lax.dynamic_slice_in_dim(summed_a, offset, slab, 2)
    cell_count = cx * lax.axis_size("gx") * cy * lax.axis_size("gy") * cz
    w_k = hv_k - beta_prev[0] * q_kappa
    w_a = hv_a - beta_prev[0] * q_absorb
    local_wv = jnp.sum(w_k * v_kappa) + jnp.sum(w_a * v_absorb)
    local_vv = jnp.sum(v_kappa * v_kappa) + jnp.sum(v_absorb * v_absorb)
    wv_sum, vv_sum = lax.psum((local_wv, local_vv), ("src", "gx", "gy"))
    alpha = wv_sum / cell_count / (vv_sum / cell_count + eps_norm)
    r_k = w_k - alpha * v_kappa
    r_a = w_a - alpha * v_absorb
    rr_sum = lax.psum(jnp.sum(r_k * r_k) + jnp.sum(r_a * r_a), ("src", "gx", "gy"))
    beta = jnp.sqrt(rr_sum / cell_count + eps_norm)
    return (r_k / beta, r_a / beta, jnp.stack([alpha, beta]))


def chebyshev_scalars():
    theta = 0.5 * (lam_high + lam_low)
    delta = 0.5 * (lam_high - lam_low)
    sigma = theta / delta
    rho = 1.0 / sigma
    pairs = []
    for _ in range(ITERS - 1):
        rho_next = 1.0 / (2.0 * sigma - rho)
        pairs.append((rho_next * rho, 2.0 * rho_next / delta))
        rho = rho_next
    return theta, pairs


def places(split):
    g = lax.axis_index("gy")
    return lax.axis_index("src"), lax.axis_index("gx"), g // split, g % split


def shifted(value, step, axis):
    return pltpu.roll(value, step % value.shape[axis], axis)


def index_along(shape, axis):
    return lax.broadcasted_iota(jnp.int32, shape, axis)


def beyond(value, step, axis):
    size = value.shape[axis]
    at = index_along(value.shape, axis)
    edge = size - 1 if step == 1 else 0
    return jnp.where(at == edge, 0.0, shifted(value, -step, axis))


def packed_planes(ref, q):
    per = 128 // ref.shape[2]
    return jnp.concatenate([ref[per * q + j] for j in range(per)], axis=1)


def pack_kernel(bg, labels, vk, va, packed, message, raw, v_in, sems):
    _, x, _, _ = places(2)
    half = bg.shape[0] // 2
    copies = [
        pltpu.make_async_copy(src, dst, sems.at[i])
        for i, (src, dst) in enumerate((
            (vk, v_in.at[0]),
            (va, v_in.at[1]),
            (bg.at[pl.ds(half * (1 - x), half)], message.at[pl.ds(0, half)]),
            (labels, raw),
        ))
    ]
    for copy in copies:
        copy.start()
    for f in range(2):
        copies[f].wait()
        for q in range(packed.shape[1]):
            packed[f, q] = packed_planes(v_in.at[f], q)
    copies[3].wait()
    message[half] = raw[...].astype(jnp.float32)
    copies[2].wait()


def count_kernel(dets, count, *, ny, nz, half, halo):
    _, _, y, _ = places(2)
    planes, rows, _ = count.shape
    flat = dets[...]
    iz = flat % nz
    line = flat // nz
    iy = line % ny
    ix = line // ny
    row = iy - (half - halo) * y
    spot = jnp.where((row >= 0) & (row < rows), ix * rows + row, -1)
    dets_n = flat.shape[1]
    at_z = (index_along((nz, dets_n), 0) == iz).astype(jnp.float32).astype(jnp.bfloat16)

    def body(i, carry):
        here = index_along((2 * rows, dets_n), 0) + i * (2 * rows)
        hot = (here == spot).astype(jnp.float32).astype(jnp.bfloat16)
        found = lax.dot_general(hot, at_z, (((1,), (1,)), ((), ())), preferred_element_type=jnp.float32)
        count[pl.ds(2 * i, 2)] = found.reshape(2, rows, nz)
        return carry

    lax.fori_loop(0, planes // 2, body, 0)


def photon_kernel(bg, labels, msg, mine, fields, raw, sems):
    _, x, _, c = places(2)
    half = bg.shape[0] // 2
    cx = labels.shape[0]
    here, there = cx * x, cx * (1 - x)
    copies = [
        pltpu.make_async_copy(src, dst, sems.at[i])
        for i, (src, dst) in enumerate((
            (bg.at[half * x + c], mine.at[pl.ds(here, cx)]),
            (bg.at[half * x + 1 - c], fields.at[0, pl.ds(here, cx)]),
            (labels, raw),
        ))
    ]
    for copy in copies:
        copy.start()
    mine[pl.ds(there, cx)] = msg[c]
    fields[0, pl.ds(there, cx)] = msg[1 - c]
    fields[1, pl.ds(there, cx)] = msg[half]
    for copy in copies:
        copy.wait()
    fields[1, pl.ds(here, cx)] = raw[...].astype(jnp.float32)


def unpack_kernel(*refs):
    own, parts, full = refs[:2], refs[2:-1], refs[-1]
    n = len(parts) + 1
    s, _, _, _ = places(2)
    slab = 128 // n
    _, cx, cy, _ = full.shape
    lane = index_along((cy, 128), 1) // slab
    for f in range(2):
        for q in range(cx // n):
            blocks = [part[f, q] for part in parts]
            for j in range(n):
                plane = jnp.concatenate([own[f][n * q + j]] * n, axis=1)
                for k in range(1, n):
                    home = (s - k + n) % n
                    moved = pltpu.roll(blocks[k - 1], ((home - j + n) % n) * slab, 1)
                    plane = jnp.where(lane == home, moved, plane)
                full[f, n * q + j] = plane


def vector_kernel(own, came, fields):
    _, x, _, _ = places(2)
    cx = own.shape[1]
    fields[:, pl.ds(cx * x, cx)] = own[...]
    fields[:, pl.ds(cx * (1 - x), cx)] = came[...]


def edge_rows(ref, halo, y):
    return ref[pl.ds(0, ref.shape[0]), pl.ds((ref.shape[1] - halo) * (1 - y), halo), :]


def photon_edge_kernel(mine, fields, got, edge):
    _, _, y, c = places(2)
    halo = edge.shape[2]
    edge[0] = jnp.where(c != y, edge_rows(mine, halo, y), edge_rows(got.at[0], halo, y))
    edge[1] = jnp.where(c != y, edge_rows(fields.at[1], halo, y), edge_rows(got.at[1], halo, y))


def vector_edge_kernel(fields, got, edge):
    _, _, y, c = places(2)
    halo = edge.shape[2]
    for f in range(2):
        edge[f] = jnp.where(c != y, edge_rows(fields.at[f], halo, y), edge_rows(got.at[f], halo, y))


def solve(b, bufs, diag, fx, fy, fz, unroll):
    planes = b.shape[0]
    _, pairs = chebyshev_scalars()
    for step, (keep, push) in enumerate(pairs):
        src, dst = bufs[step % 2], bufs[(step + 1) % 2]

        def body(i, carry):
            u = src[i + 1]
            coef_y, coef_z = fy[i], fz[i]
            left = b[i] - diag[i] * u
            left = left + fx[i] * src[i] + fx[i + 1] * src[i + 2]
            left = left + coef_y * shifted(u, -1, 0) + shifted(coef_y * u, 1, 0)
            left = left + coef_z * shifted(u, -1, 1) + shifted(coef_z * u, 1, 1)
            change = u if step == 0 else u - dst[i + 1]
            dst[i + 1] = u + keep * change + push * left
            return carry

        lax.fori_loop(0, planes, body, 0, unroll=unroll)
    return bufs[len(pairs) % 2]


def folded(value):
    return jnp.sum(value.reshape(-1, 8, value.shape[1]), axis=0)


def framed(ref, shift, parts, planes, cy, halo, y, c):
    own, got, edge = parts
    there = pl.ds(shift, planes)
    base = halo * y
    ref[there, pl.ds(base + cy * c, cy), :] = own
    ref[there, pl.ds(base + cy * (1 - c), cy), :] = got
    ref[there, pl.ds(2 * cy * (1 - y), halo), :] = edge


def blank_ends(*refs):
    for ref in refs:
        blank = jnp.zeros(ref.shape[1:], jnp.float32)
        ref[0] = blank
        ref[ref.shape[0] - 1] = blank


def owned_rows(shape, base, count):
    at_row = index_along(shape, 0)
    return (at_row >= base) & (at_row < base + count)


def stencil_kernel(
    kap_table, abs_table, mine, fields, got, edge, count,
    phi, diag, fx, fy, fz, sums,
    labels, kap,
):
    _, _, y, c = places(2)
    planes, cy, lanes = mine.shape
    halo = edge.shape[2]
    rows = 2 * cy + halo
    place = (planes, cy, halo, y, c)
    framed(phi, 1, (mine[...], got[0], edge[0]), *place)
    framed(labels, 0, (fields[1], got[1], edge[1]), *place)
    blank_ends(phi, kap)
    blank = jnp.zeros((rows, lanes), jnp.float32)
    lane = index_along((rows, lanes), 1)
    kap_row, abs_row = blank, blank
    for region in range(kap_table.shape[0]):
        kap_row = jnp.where(lane == region, kap_table[region], kap_row)
        abs_row = jnp.where(lane == region, abs_table[region], abs_row)

    def look_up(i, carry):
        at = labels[i].astype(jnp.int32)
        kap[i + 1] = jnp.take_along_axis(kap_row, at, axis=1)
        diag[i] = jnp.take_along_axis(abs_row, at, axis=1)
        return carry

    lax.fori_loop(0, planes, look_up, 0, unroll=4)
    fx[0] = 0.5 * kap[1]
    owned = owned_rows((rows, lanes), halo * y, 2 * cy)

    def set_up(i, carry):
        k = kap[i + 1]
        along_x = 0.5 * (k + kap[i + 2])
        along_y, along_z = 0.5 * (k + beyond(k, 1, 0)), 0.5 * (k + beyond(k, 1, 1))
        fx[i + 1] = along_x
        fy[i] = jnp.where(index_along(k.shape, 0) == rows - 1, 0.0, along_y)
        fz[i] = jnp.where(lane == lanes - 1, 0.0, along_z)
        back_y, back_z = 0.5 * (k + beyond(k, -1, 0)), 0.5 * (k + beyond(k, -1, 1))
        diag[i] = diag[i] + fx[i] + along_x + along_y + back_y + along_z + back_z
        p = phi[i + 1]
        part = jnp.where(owned, count[i], 0.0) * p
        return carry[0] + folded(part), carry[1] + folded(part * p)

    zero = jnp.zeros((8, lanes), jnp.float32)
    sums[0], sums[1] = lax.fori_loop(0, planes, set_up, (zero, zero), unroll=4)


def first_kernel(
    phi, diag, fx, fy, fz, count, sums, fields, got, edge,
    change, message,
    vk, va, b, buf_a, buf_b,
):
    _, _, y, c = places(2)
    planes, rows, lanes = change.shape
    halo = edge.shape[2]
    cy = (rows - halo) // 2
    place = (planes, cy, halo, y, c)
    framed(vk, 1, (fields[0], got[0], edge[0]), *place)
    framed(va, 0, (fields[1], got[1], edge[1]), *place)
    blank_ends(vk, buf_a, buf_b)
    theta, _ = chebyshev_scalars()

    def set_up(i, carry):
        v, p = vk[i + 1], phi[i + 1]
        total = 0.5 * (v + vk[i]) * (p - phi[i]) + 0.5 * (v + vk[i + 2]) * (p - phi[i + 2])
        for axis in range(2):
            flow = 0.5 * (v + beyond(v, 1, axis)) * (p - beyond(p, 1, axis))
            first = index_along(v.shape, axis) == 0
            total = total + flow + jnp.where(first, 0.5 * v * p, -shifted(flow, 1, axis))
        total = -(va[i] * p + total)
        b[i] = total
        buf_a[i + 1] = total * (1.0 / theta)
        return carry

    lax.fori_loop(0, planes, set_up, 0, unroll=4)
    found = solve(b, (buf_a, buf_b), diag, fx, fy, fz, 16)
    owned = owned_rows((rows, lanes), halo * y, 2 * cy)

    def add_up(i, carry):
        u = found[i + 1]
        change[i] = u
        part = jnp.where(owned, count[i], 0.0) * u
        return carry[0] + folded(part), carry[1] + folded(part * phi[i + 1])

    zero = jnp.zeros((8, lanes), jnp.float32)
    seen, cross = lax.fori_loop(0, planes, add_up, (zero, zero), unroll=4)
    edge = (2 * cy - halo) * (1 - y) + halo * y
    message[pl.ds(0, planes)] = found[pl.ds(1, planes), pl.ds(edge, halo), :]
    for i, part in enumerate((sums[0], seen, cross, sums[1])):
        message[planes + i] = part


def second_kernel(
    phi, change, diag, fx, fy, fz, count, sent, came,
    own, message,
    b, buf_a, buf_b, grad_k, grad_a,
    *, dets,
):
    _, _, y, c = places(2)
    planes, rows, lanes = change.shape
    halo = came.shape[1]
    cy = (rows - halo) // 2
    base = halo * y
    edge = pl.ds(2 * cy * (1 - y), halo)
    one = jnp.ones((1, 1), jnp.float32)
    total, seen_sum, cross, square = (
        jnp.sum(sent[planes + i] + came[planes + i]) * one for i in range(4)
    )
    mean = total / dets
    part = seen_sum / total
    level = (cross - part * square) / (total * mean)
    inverse = 1.0 / mean
    blank_ends(buf_a, buf_b)
    theta, _ = chebyshev_scalars()

    def weighted(n, u, p):
        return n * (((u - p * part) * inverse - level) * inverse)

    def set_up(i, carry):
        value = weighted(count[i], change[i], phi[i + 1])
        b[i] = value
        buf_a[i + 1] = value * (1.0 / theta)
        value = weighted(count[i, edge, :], came[i], phi[i + 1, edge, :])
        b[i, edge, :] = value
        buf_a[i + 1, edge, :] = value * (1.0 / theta)
        return carry

    lax.fori_loop(0, planes, set_up, 0, unroll=4)
    dual = solve(b, (buf_a, buf_b), diag, fx, fy, fz, 16)

    def product(i, carry):
        p, u = phi[i + 1], dual[i + 1]
        grad = (p - phi[i]) * (u - dual[i]) + (p - phi[i + 2]) * (u - dual[i + 2])
        both = p * u
        for axis in range(2):
            flow = (p - beyond(p, 1, axis)) * (u - beyond(u, 1, axis))
            first = index_along(p.shape, axis) == 0
            grad = grad + flow + jnp.where(first, both, shifted(flow, 1, axis))
        grad_k[i] = -0.5 * grad
        grad_a[i] = -both
        for f, ref in enumerate((grad_k, grad_a)):
            own[f, i] = ref[i, pl.ds(base + cy * c, cy), :]
            message[f, i] = ref[i, pl.ds(base + cy * (1 - c), cy), :]
        return carry

    lax.fori_loop(0, planes, product, 0, unroll=4)


def core_kernel(own, came, kept, far, near):
    s, x, _, _ = places(2)
    n, _, groups, cy, lanes = kept.shape
    slab = lanes // n
    lane = index_along((cy, lanes), 1) // slab
    for h in range(2):
        for f in range(2):
            for q in range(groups):
                at = n * (groups * (x if h == 0 else 1 - x) + q)
                planes = [own[f, at + j] + came[f, at + j] for j in range(n)]
                for k in range(n):
                    to = (s + k) % n
                    piece = jnp.zeros((cy, lanes), jnp.float32)
                    for j in range(n):
                        moved = pltpu.roll(planes[j], ((j - to + n) % n) * slab, 1)
                        piece = jnp.where(lane == j, moved, piece)
                    if h == 0:
                        kept[k, f, q] = piece
                    elif k >= n // 2:
                        far[k - n // 2, f, q] = piece
                    else:
                        near[k, f, q] = piece


def add_kernel(kept, came, *outs, first):
    for i, out in enumerate(outs):
        out[...] = kept[first + i] + came[i]


def project_kernel(*refs, n):
    beta_prev = refs[0]
    parts = refs[1 : 1 + n]
    vk, va, qk, qa, w_k, w_a, tile = refs[1 + n :]
    s, x, y, c = places(2)
    slab = 128 // n
    for f, (q_ref, w) in enumerate(((qk, w_k), (qa, w_a))):
        for q in range(vk.shape[0] // n):
            whole = sum(part[f, q] for part in parts[1:]) + parts[0][f, q]
            for j in range(n):
                i = n * q + j
                w[i] = whole[:, slab * j : slab * (j + 1)] - beta_prev[...] * q_ref[i]

    def dot(a, b):
        return jnp.sum(jnp.sum(a * b, axis=0))

    wk, wa, v_k, v_a = w_k[...], w_a[...], vk[...], va[...]
    one = jnp.ones((1, 1), jnp.float32)
    wv = (dot(wk, v_k) + dot(wa, v_a)) * one
    vv = (dot(v_k, v_k) + dot(v_a, v_a)) * one
    a = jnp.where(vv > 0.0, wv / jnp.where(vv > 0.0, vv, 1.0), 0.0)
    u_k, u_a = wk - a * v_k, wa - a * v_a
    uv = (dot(u_k, v_k) + dot(u_a, v_a)) * one
    uu = (dot(u_k, u_k) + dot(u_a, u_a)) * one
    me = ((s * 2 + x) * 2 + y) * 2 + c
    lane = index_along((8, 128), 1)
    row = index_along((8, 128), 0)
    values = jnp.zeros((8, 128), jnp.float32)
    for i, value in enumerate((wv, vv, a, uv, uu)):
        values = jnp.where(row == i, value, values)
    tile[...] = jnp.where(lane == me, values, 0.0)


def final_kernel(tiles, w_k, w_a, vk, va, next_k, next_a, coefs, *, cells):
    tile = jnp.sum(tiles[...], axis=0)
    wv, vv, a, uv, uu = (tile[i : i + 1] for i in range(5))
    wv_sum = jnp.sum(wv, axis=1, keepdims=True)
    vv_sum = jnp.sum(vv, axis=1, keepdims=True)
    alpha = wv_sum / cells / (vv_sum / cells + eps_norm)
    off = alpha - a
    rr = jnp.sum(uu - 2.0 * off * uv + off * off * vv, axis=1, keepdims=True)
    beta = jnp.sqrt(rr / cells + eps_norm)
    next_k[...] = (w_k[...] - alpha * vk[...]) / beta
    next_a[...] = (w_a[...] - alpha * va[...]) / beta
    coefs[0] = jnp.sum(alpha)
    coefs[1] = jnp.sum(beta)


def f32(*shape):
    return jax.ShapeDtypeStruct(shape, jnp.float32)


def run(kernel, outs, *args, after=(), scratch=(), copies=0, smem=(), hbm=(), mib=16, in_smem_out=(), cost=None):
    vmem = pl.BlockSpec(memory_space=pltpu.VMEM)
    scalar = pl.BlockSpec(memory_space=pltpu.SMEM)
    far = pl.BlockSpec(memory_space=pltpu.HBM)
    held = [pltpu.VMEM(shape, dtype) for shape, dtype in scratch]
    used, waits = len(args), len(after)

    def body(*refs):
        kernel(*refs[:used], *refs[used + waits :])

    args = (*args, *after)
    if copies:
        held.append(pltpu.SemaphoreType.DMA((copies,)))
    return pl.pallas_call(
        body if waits else kernel,
        out_shape=tuple(outs),
        in_specs=[scalar if i in smem else far if i in hbm else vmem for i in range(len(args))],
        out_specs=tuple(scalar if i in in_smem_out else vmem for i in range(len(outs))),
        scratch_shapes=held,
        compiler_params=pltpu.CompilerParams(vmem_limit_bytes=mib * 2**20),
        cost_estimate=cost,
    )(*args)


HALO = 8


def per_device_paired(
    labels, kappa_table, absorb_table, background, det_cells,
    v_kappa, v_absorb, q_kappa, q_absorb, beta_prev,
):
    sources, cx, cy, cz = background.shape
    n = lax.axis_size("src")
    planes, rows = 2 * cx, 2 * cy + HALO
    ny = cy * lax.axis_size("gy")
    dets = det_cells.shape[0]
    cells = planes * ny * cz
    groups = cx // n

    def swap_x(value):
        return lax.ppermute(value, "gx", [(0, 1), (1, 0)])

    def swap_core(value):
        return lax.ppermute(value, "gy", [(0, 1), (1, 0), (2, 3), (3, 2)])

    def along_z(value, k):
        return lax.ppermute(value, "src", [(i, (i + k) % n) for i in range(n)])

    block = (cx, cy, cz)
    float_block = lambda *shape: (shape, jnp.float32)
    raw_labels = (block, jnp.int32)
    packed, message = run(
        pack_kernel, (f32(2, groups, cy, cz), f32(sources // 2 + 1, *block)),
        background, labels, v_kappa, v_absorb, hbm=(0, 1, 2, 3),
        scratch=(raw_labels, float_block(2, *v_kappa.shape)), copies=4, mib=60,
    )
    came = swap_x(message)
    slabs = [along_z(packed, k) for k in range(1, n)]
    (count,) = run(
        functools.partial(count_kernel, ny=ny, nz=cz, half=2 * cy, halo=HALO),
        (f32(planes, rows, cz),), det_cells.reshape(1, dets),
        cost=pl.CostEstimate(flops=2 * planes * rows * cz * dets, bytes_accessed=planes * rows * cz * 4, transcendentals=0),
    )

    def across_y(value):
        return lax.ppermute(value, "gy", [(i, (i + 2) % 4) for i in range(4)])

    edges = (f32(2, planes, HALO, cz),)
    (half_vector,) = run(unpack_kernel, (f32(2, *block),), v_kappa, v_absorb, *slabs, after=(count,))
    half_came = swap_x(half_vector)
    mine, fields = run(
        photon_kernel, (f32(planes, cy, cz), f32(2, planes, cy, cz)),
        background, labels, came, after=(half_vector,), hbm=(0, 1), scratch=(raw_labels,), copies=3,
    )
    got = swap_core(fields)
    (vector,) = run(vector_kernel, (f32(2, planes, cy, cz),), half_vector, half_came)
    (sent,) = run(photon_edge_kernel, edges, mine, fields, got, after=(vector,))
    halo = across_y(sent)
    vector_got = swap_core(vector)
    (vector_sent,) = run(vector_edge_kernel, edges, vector, vector_got)
    frame, wide = (planes, rows, cz), (planes + 2, rows, cz)
    float_frame, float_wide = float_block(*frame), float_block(*wide)
    phi, diag, fx, fy, fz, sums = run(
        stencil_kernel,
        (f32(*wide), f32(*frame), f32(planes + 1, rows, cz), f32(*frame), f32(*frame), f32(2, 8, cz)),
        kappa_table, absorb_table, mine, fields, got, halo, count, after=(vector_sent,),
        smem=(0, 1), scratch=(float_frame, float_wide),
    )
    change, sent = run(
        first_kernel, (f32(*frame), f32(planes + 4, HALO, cz)),
        phi, diag, fx, fy, fz, count, sums, vector, vector_got, across_y(vector_sent),
        scratch=(float_wide, float_frame, float_frame, float_wide, float_wide),
    )
    heard = across_y(sent)
    own, message = run(
        functools.partial(second_kernel, dets=dets),
        (f32(2, planes, cy, cz), f32(2, planes, cy, cz)),
        phi, change, diag, fx, fy, fz, count, sent, heard,
        scratch=(float_frame, float_wide, float_wide, float_frame, float_frame),
    )
    piece = f32(2, groups, cy, cz)
    half = n // 2
    kept, far, near = run(
        core_kernel,
        (f32(n, *piece.shape), f32(n - half, *piece.shape), f32(half, *piece.shape)),
        own, swap_core(message),
    )
    far, near = swap_x(far), swap_x(near)
    pieces = run(functools.partial(add_kernel, first=half), [piece] * (n - half), kept, far)
    parts = [along_z(value, half + i) for i, value in enumerate(pieces)]
    pieces = run(functools.partial(add_kernel, first=0), [piece] * half, kept, near)
    parts = [pieces[0]] + parts + [along_z(pieces[k], k) for k in range(1, half)]
    w_k, w_a, tile = run(
        functools.partial(project_kernel, n=n),
        (f32(*v_kappa.shape), f32(*v_kappa.shape), f32(8, 128)),
        beta_prev.reshape(1, 1), *parts, v_kappa, v_absorb, q_kappa, q_absorb,
    )
    everyone = ("src", "gx", "gy")
    tiles = lax.all_to_all(jnp.broadcast_to(tile, (8 * n, 8, 128)), everyone, 0, 0)
    return tuple(run(
        functools.partial(final_kernel, cells=cells),
        (f32(*v_kappa.shape), f32(*v_kappa.shape), f32(2)),
        tiles, w_k, w_a, v_kappa, v_absorb, in_smem_out=(2,),
    ))


def paired_fits(mesh):
    return mesh.shape["gx"] == 2 and mesh.shape["gy"] == 4


def body_for(mesh):
    if not paired_fits(mesh):
        return per_device

    def chosen(*args):
        sources, cx, cy, cz = args[3].shape
        n = lax.axis_size("src")
        fits = sources == 4 and cz == 128 and cx % n == 0 and cz % n == 0 and cy % HALO == 0
        devices = 8 * n
        return (per_device_paired if fits and devices <= 128 else per_device)(*args)

    return chosen


def solution(mesh):
    return jax.shard_map(
        body_for(mesh),
        mesh=mesh,
        in_specs=(
            P("gx", "gy", None),
            P(),
            P(),
            P("src", "gx", "gy", None),
            P(),
            P("gx", "gy", "src"),
            P("gx", "gy", "src"),
            P("gx", "gy", "src"),
            P("gx", "gy", "src"),
            P(),
        ),
        out_specs=(P("gx", "gy", "src"), P("gx", "gy", "src"), P()),
        check_vma=False,
    )
```

```python
import functools

import jax
import jax.numpy as jnp
from jax import lax
from jax.experimental import pallas as pl
from jax.experimental.pallas import tpu as pltpu
from jax.sharding import PartitionSpec as P

ITERS = 6


lam_low = 0.02
lam_high = 24.1
eps_norm = 1e-06


def padded_2(block, sides, width):
    for axis, dim in sides:
        count = lax.axis_size(axis)
        forward = [(i, i + 1) for i in range(count - 1)]
        backward = [(target, source) for source, target in forward]
        low = lax.ppermute(
            lax.slice_in_dim(block, block.shape[dim] - width, None, axis=dim), axis, forward
        )
        high = lax.ppermute(lax.slice_in_dim(block, 0, width, axis=dim), axis, backward)
        block = jnp.concatenate([low, block, high], axis=dim)
    return block


def regional(labels, table):
    field = jnp.zeros(labels.shape, jnp.float32)
    for region in range(table.shape[0]):
        field = field + jnp.where(labels == region, table[region], 0.0)
    return field


def beside(padded):
    widths = [(0, 0)] * (padded.ndim - 1) + [(1, 1)]
    full = jnp.pad(padded, widths)
    return [
        full[..., 2:, 1:-1, 1:-1],
        full[..., :-2, 1:-1, 1:-1],
        full[..., 1:-1, 2:, 1:-1],
        full[..., 1:-1, :-2, 1:-1],
        full[..., 1:-1, 1:-1, 2:],
        full[..., 1:-1, 1:-1, :-2],
    ]


def chebyshev(rhs, apply_op):
    theta = 0.5 * (lam_high + lam_low)
    delta = 0.5 * (lam_high - lam_low)
    sigma = theta / delta
    rho = 1.0 / sigma
    solution = jnp.zeros_like(rhs)
    remain = rhs
    step_dir = rhs / theta
    for step in range(ITERS):
        solution = solution + step_dir
        if step + 1 < ITERS:
            remain = remain - apply_op(step_dir)
            rho_next = 1.0 / (2.0 * sigma - rho)
            step_dir = rho_next * rho * step_dir + 2.0 * rho_next / delta * remain
            rho = rho_next
    return solution


def per_device(
    labels,
    kappa_table,
    absorb_table,
    background,
    det_cells,
    v_kappa,
    v_absorb,
    q_kappa,
    q_absorb,
    beta_prev,
):
    sources, cx, cy, cz = background.shape
    kappa = regional(labels, kappa_table)
    absorb = regional(labels, absorb_table)
    full_k, full_a = (
        lax.all_gather(v_kappa, "src", axis=2, tiled=True),
        lax.all_gather(v_absorb, "src", axis=2, tiled=True),
    )
    stacked = jnp.concatenate([background, kappa[None], full_k[None]], axis=0)
    rims = padded_2(stacked, (("gx", 1), ("gy", 2)), 1)
    near_all = beside(rims)
    kappa_faces = [0.5 * (kappa + near[sources]) for near in near_all]
    vk_faces = [0.5 * (full_k + near[sources + 1]) for near in near_all]
    phi_near = [near[:sources] for near in near_all]

    def apply_op(field):
        padded = padded_2(field, (("gx", 1), ("gy", 2)), 1)
        result = absorb * field
        for face, near in zip(kappa_faces, beside(padded)):
            result = result + face * (field - near)
        return result

    rhs = full_a * background
    for face, near in zip(vk_faces, phi_near):
        rhs = rhs + face * (background - near)
    rhs = -rhs
    change = chebyshev(rhs, apply_op)
    span_y = cy * lax.axis_size("gy")
    ix = det_cells // (span_y * cz)
    iy = det_cells // cz % span_y
    iz = det_cells % cz
    anchor_x = lax.axis_index("gx") * cx
    anchor_y = lax.axis_index("gy") * cy
    owned = (ix >= anchor_x) & (ix < anchor_x + cx) & (iy >= anchor_y) & (iy < anchor_y + cy)
    local = jnp.where(owned, ((ix - anchor_x) * cy + (iy - anchor_y)) * cz + iz, 0)
    seen_part = jnp.where(owned[None, :], change.reshape(sources, -1)[:, local], 0.0)
    base_part = jnp.where(owned[None, :], background.reshape(sources, -1)[:, local], 0.0)
    seen, base = lax.psum((seen_part, base_part), ("gx", "gy"))
    total = jnp.sum(base, axis=1, keepdims=True)
    mean_base = total / det_cells.shape[0]
    ratio = base / total
    jv_vals = (seen - ratio * jnp.sum(seen, axis=1, keepdims=True)) / mean_base
    weight = (jv_vals - jnp.sum(ratio * jv_vals, axis=1, keepdims=True)) / mean_base
    deposit = jnp.where(owned[None, :], weight, 0.0)
    source = (
        jnp.zeros((sources, cx * cy * cz), jnp.float32)
        .at[:, local]
        .add(deposit)
        .reshape(change.shape)
    )
    dual = chebyshev(source, apply_op)
    dual_rims = padded_2(dual, (("gx", 1), ("gy", 2)), 1)
    grad_a = -jnp.sum(background * dual, axis=0)
    grad_k = jnp.zeros_like(kappa)
    for near_phi, near_dual in zip(phi_near, beside(dual_rims)):
        grad_k = grad_k - 0.5 * jnp.sum((background - near_phi) * (dual - near_dual), axis=0)
    summed_k, summed_a = lax.psum((grad_k, grad_a), "src")
    slab = v_kappa.shape[2]
    offset = lax.axis_index("src") * slab
    hv_k = lax.dynamic_slice_in_dim(summed_k, offset, slab, 2)
    hv_a = lax.dynamic_slice_in_dim(summed_a, offset, slab, 2)
    cell_count = cx * lax.axis_size("gx") * cy * lax.axis_size("gy") * cz
    w_k = hv_k - beta_prev[0] * q_kappa
    w_a = hv_a - beta_prev[0] * q_absorb
    local_wv = jnp.sum(w_k * v_kappa) + jnp.sum(w_a * v_absorb)
    local_vv = jnp.sum(v_kappa * v_kappa) + jnp.sum(v_absorb * v_absorb)
    wv_sum, vv_sum = lax.psum((local_wv, local_vv), ("src", "gx", "gy"))
    alpha = wv_sum / cell_count / (vv_sum / cell_count + eps_norm)
    r_k = w_k - alpha * v_kappa
    r_a = w_a - alpha * v_absorb
    rr_sum = lax.psum(jnp.sum(r_k * r_k) + jnp.sum(r_a * r_a), ("src", "gx", "gy"))
    beta = jnp.sqrt(rr_sum / cell_count + eps_norm)
    return (r_k / beta, r_a / beta, jnp.stack([alpha, beta]))


def chebyshev_scalars():
    theta = 0.5 * (lam_high + lam_low)
    delta = 0.5 * (lam_high - lam_low)
    sigma = theta / delta
    rho = 1.0 / sigma
    pairs = []
    for _ in range(ITERS - 1):
        rho_next = 1.0 / (2.0 * sigma - rho)
        pairs.append((rho_next * rho, 2.0 * rho_next / delta))
        rho = rho_next
    return theta, pairs


def places(split):
    g = lax.axis_index("gy")
    return lax.axis_index("src"), lax.axis_index("gx"), g // split, g % split


def shifted(value, step, axis):
    return pltpu.roll(value, step % value.shape[axis], axis)


def index_along(shape, axis):
    return lax.broadcasted_iota(jnp.int32, shape, axis)


def beyond(value, step, axis):
    size = value.shape[axis]
    at = index_along(value.shape, axis)
    edge = size - 1 if step == 1 else 0
    return jnp.where(at == edge, 0.0, shifted(value, -step, axis))


def packed_planes(ref, q):
    per = 128 // ref.shape[2]
    return jnp.concatenate([ref[per * q + j] for j in range(per)], axis=1)


def pack_kernel(bg, labels, vk, va, packed, message, raw, v_in, sems):
    _, x, _, _ = places(2)
    half = bg.shape[0] // 2
    copies = [
        pltpu.make_async_copy(src, dst, sems.at[i])
        for i, (src, dst) in enumerate((
            (vk, v_in.at[0]),
            (va, v_in.at[1]),
            (bg.at[pl.ds(half * (1 - x), half)], message.at[pl.ds(0, half)]),
            (labels, raw),
        ))
    ]
    for copy in copies:
        copy.start()
    for f in range(2):
        copies[f].wait()
        for q in range(packed.shape[1]):
            packed[f, q] = packed_planes(v_in.at[f], q)
    copies[3].wait()
    message[half] = raw[...].astype(jnp.float32)
    copies[2].wait()


def count_kernel(dets, beta_prev, count, beta_row, *, ny, nz, half, halo):
    beta_row[...] = jnp.full(beta_row.shape, beta_prev[0])
    _, _, y, _ = places(2)
    planes, rows, _ = count.shape
    flat = dets[...]
    iz = flat % nz
    line = flat // nz
    iy = line % ny
    ix = line // ny
    row = iy - (half - halo) * y
    spot = jnp.where((row >= 0) & (row < rows), ix * rows + row, -1)
    dets_n = flat.shape[1]
    at_z = (index_along((nz, dets_n), 0) == iz).astype(jnp.float32).astype(jnp.bfloat16)

    def body(i, carry):
        here = index_along((2 * rows, dets_n), 0) + i * (2 * rows)
        hot = (here == spot).astype(jnp.float32).astype(jnp.bfloat16)
        found = lax.dot_general(hot, at_z, (((1,), (1,)), ((), ())), preferred_element_type=jnp.float32)
        count[pl.ds(2 * i, 2)] = found.reshape(2, rows, nz)
        return carry

    lax.fori_loop(0, planes // 2, body, 0)


def photon_kernel(bg, labels, msg, mine, fields, raw, sems):
    _, x, _, c = places(2)
    half = bg.shape[0] // 2
    cx = labels.shape[0]
    here, there = cx * x, cx * (1 - x)
    copies = [
        pltpu.make_async_copy(src, dst, sems.at[i])
        for i, (src, dst) in enumerate((
            (bg.at[half * x + c], mine.at[pl.ds(here, cx)]),
            (bg.at[half * x + 1 - c], fields.at[0, pl.ds(here, cx)]),
            (labels, raw),
        ))
    ]
    for copy in copies:
        copy.start()
    mine[pl.ds(there, cx)] = msg[c]
    fields[0, pl.ds(there, cx)] = msg[1 - c]
    fields[1, pl.ds(there, cx)] = msg[half]
    for copy in copies:
        copy.wait()
    fields[1, pl.ds(here, cx)] = raw[...].astype(jnp.float32)


def unpack_kernel(*refs):
    own, parts, full = refs[:2], refs[2:-1], refs[-1]
    n = len(parts) + 1
    s, _, _, _ = places(2)
    slab = 128 // n
    _, cx, cy, _ = full.shape
    lane = index_along((cy, 128), 1) // slab
    for f in range(2):
        for q in range(cx // n):
            blocks = [part[f, q] for part in parts]
            for j in range(n):
                plane = jnp.concatenate([own[f][n * q + j]] * n, axis=1)
                for k in range(1, n):
                    home = s ^ k
                    moved = pltpu.roll(blocks[k - 1], ((home - j + n) % n) * slab, 1)
                    plane = jnp.where(lane == home, moved, plane)
                full[f, n * q + j] = plane


def vector_kernel(own, came, fields):
    _, x, _, _ = places(2)
    cx = own.shape[1]
    fields[:, pl.ds(cx * x, cx)] = own[...]
    fields[:, pl.ds(cx * (1 - x), cx)] = came[...]


def edge_shape(planes, lanes):
    return planes // GROUP, GROUP * REACH, lanes


def packed_edges(tiles):
    return jnp.concatenate([tile[:REACH] for tile in tiles], axis=0)


def edge_tile(packed, j, y):
    rows = packed[REACH * j : REACH * (j + 1)]
    tile = jnp.concatenate([rows, jnp.zeros((HALO - REACH, rows.shape[1]), jnp.float32)], axis=0)
    return jnp.where(y == 0, tile, shifted(tile, HALO - REACH, 0))


def near_rows(ref, i, first, y):
    tile = ref[i, pl.ds(first, HALO), :]
    return jnp.where(y == 0, shifted(tile, REACH - HALO, 0), tile)


def edges_of(own, got, edge, y, c):
    first = (own.shape[1] - HALO) * (1 - y)
    for g in range(edge.shape[0]):
        edge[g] = packed_edges([
            jnp.where(c != y, near_rows(own, GROUP * g + j, first, y), near_rows(got, GROUP * g + j, first, y))
            for j in range(GROUP)
        ])


def photon_edge_kernel(mine, fields, got, edge):
    _, _, y, c = places(2)
    edges_of(mine, got.at[0], edge.at[0], y, c)
    edges_of(fields.at[1], got.at[1], edge.at[1], y, c)


def vector_edge_kernel(fields, got, edge):
    _, _, y, c = places(2)
    for f in range(2):
        edges_of(fields.at[f], got.at[f], edge.at[f], y, c)


def solve(b, bufs, diag, fx, fy, fz, unroll):
    planes = b.shape[0]
    _, pairs = chebyshev_scalars()
    for step, (keep, push) in enumerate(pairs):
        src, dst = bufs[step % 2], bufs[(step + 1) % 2]

        def body(i, carry):
            u = src[i + 1]
            coef_y, coef_z = fy[i], fz[i]
            left = b[i] - diag[i] * u
            left = left + fx[i] * src[i] + fx[i + 1] * src[i + 2]
            left = left + coef_y * shifted(u, -1, 0) + shifted(coef_y * u, 1, 0)
            left = left + coef_z * shifted(u, -1, 1) + shifted(coef_z * u, 1, 1)
            change = u if step == 0 else u - dst[i + 1]
            dst[i + 1] = u + keep * change + push * left
            return carry

        lax.fori_loop(0, planes, body, 0, unroll=unroll)
    return bufs[len(pairs) % 2]


def folded(value):
    return jnp.sum(value.reshape(-1, 8, value.shape[1]), axis=0)


def framed(ref, shift, own, got, edge, y, c):
    planes, cy, _ = own.shape
    there = pl.ds(shift, planes)
    base = HALO * y
    ref[there, pl.ds(base + cy * c, cy), :] = own[...]
    ref[there, pl.ds(base + cy * (1 - c), cy), :] = got[...]
    for g in range(edge.shape[0]):
        packed = edge[g]
        for j in range(GROUP):
            ref[shift + GROUP * g + j, pl.ds(2 * cy * (1 - y), HALO), :] = edge_tile(packed, j, y)


def blank_ends(*refs):
    for ref in refs:
        blank = jnp.zeros(ref.shape[1:], jnp.float32)
        ref[0] = blank
        ref[ref.shape[0] - 1] = blank


def owned_rows(shape, base, count):
    at_row = index_along(shape, 0)
    return (at_row >= base) & (at_row < base + count)


def stencil_kernel(
    kap_table, abs_table, mine, fields, got, edge, count,
    diag, fx, fy, fz, sums,
    labels, kap,
):
    _, _, y, c = places(2)
    planes, cy, lanes = mine.shape
    rows = 2 * cy + HALO
    framed(labels, 0, fields.at[1], got.at[1], edge.at[1], y, c)
    blank_ends(kap)
    blank = jnp.zeros((rows, lanes), jnp.float32)
    lane = index_along((rows, lanes), 1)
    kap_row, abs_row = blank, blank
    for region in range(kap_table.shape[0]):
        kap_row = jnp.where(lane == region, kap_table[region], kap_row)
        abs_row = jnp.where(lane == region, abs_table[region], abs_row)

    def look_up(i, carry):
        at = labels[i].astype(jnp.int32)
        kap[i + 1] = jnp.take_along_axis(kap_row, at, axis=1)
        diag[i] = jnp.take_along_axis(abs_row, at, axis=1)
        return carry

    lax.fori_loop(0, planes, look_up, 0, unroll=4)
    fx[0] = 0.5 * kap[1]
    base = HALO * y

    def set_up(i, carry):
        k = kap[i + 1]
        along_x = 0.5 * (k + kap[i + 2])
        along_y, along_z = 0.5 * (k + beyond(k, 1, 0)), 0.5 * (k + beyond(k, 1, 1))
        fx[i + 1] = along_x
        fy[i] = jnp.where(index_along(k.shape, 0) == rows - 1, 0.0, along_y)
        fz[i] = jnp.where(lane == lanes - 1, 0.0, along_z)
        back_y, back_z = 0.5 * (k + beyond(k, -1, 0)), 0.5 * (k + beyond(k, -1, 1))
        diag[i] = diag[i] + fx[i] + along_x + along_y + back_y + along_z + back_z
        total, square = carry
        for p, at in ((mine[i], c), (got[0, i], 1 - c)):
            part = count[i, pl.ds(base + cy * at, cy), :] * p
            total, square = total + folded(part), square + folded(part * p)
        return total, square

    zero = jnp.zeros((8, lanes), jnp.float32)
    sums[0], sums[1] = lax.fori_loop(0, planes, set_up, (zero, zero), unroll=4)


def first_kernel(
    diag, fx, fy, fz, count, sums, mine, got_photon, vector, got_vector, photon_edge, edge,
    phi, change, message,
    vk, va, b, buf_a, buf_b,
):
    _, _, y, c = places(2)
    planes, rows, lanes = change.shape
    cy = mine.shape[1]
    framed(phi, 1, mine, got_photon.at[0], photon_edge.at[0], y, c)
    framed(vk, 1, vector.at[0], got_vector.at[0], edge.at[0], y, c)
    framed(va, 0, vector.at[1], got_vector.at[1], edge.at[1], y, c)
    blank_ends(phi, vk, buf_a, buf_b)
    theta, _ = chebyshev_scalars()

    def set_up(i, carry):
        v, p = vk[i + 1], phi[i + 1]
        total = 0.5 * (v + vk[i]) * (p - phi[i]) + 0.5 * (v + vk[i + 2]) * (p - phi[i + 2])
        for axis in range(2):
            flow = 0.5 * (v + beyond(v, 1, axis)) * (p - beyond(p, 1, axis))
            first = index_along(v.shape, axis) == 0
            total = total + flow + jnp.where(first, 0.5 * v * p, -shifted(flow, 1, axis))
        total = -(va[i] * p + total)
        b[i] = total
        buf_a[i + 1] = total * (1.0 / theta)
        return carry

    lax.fori_loop(0, planes, set_up, 0, unroll=4)
    found = solve(b, (buf_a, buf_b), diag, fx, fy, fz, 16)
    owned = owned_rows((rows, lanes), HALO * y, 2 * cy)

    def add_up(i, carry):
        u = found[i + 1]
        change[i] = u
        part = jnp.where(owned, count[i], 0.0) * u
        return carry[0] + folded(part), carry[1] + folded(part * phi[i + 1])

    zero = jnp.zeros((8, lanes), jnp.float32)
    seen, cross = lax.fori_loop(0, planes, add_up, (zero, zero), unroll=4)
    first = (2 * cy - HALO) * (1 - y) + HALO * y
    for g, part in enumerate((sums[0], seen, cross, sums[1])):
        message[g, pl.ds(0, GROUP * REACH), :] = packed_edges(
            [near_rows(found, 1 + GROUP * g + j, first, y) for j in range(GROUP)]
        )
        message[g, pl.ds(GROUP * REACH, 8), :] = part


def second_kernel(
    phi, change, diag, fx, fy, fz, count, sent, came,
    own, message,
    b, buf_a, buf_b, grad_k, grad_a,
    *, dets,
):
    _, _, y, c = places(2)
    planes, rows, lanes = change.shape
    cy = (rows - HALO) // 2
    base = HALO * y
    edge = pl.ds(2 * cy * (1 - y), HALO)
    tail = pl.ds(GROUP * REACH, 8)
    total, seen_sum, cross, square = (
        jnp.sum(jnp.sum(sent[g, tail, :] + came[g, tail, :], axis=0, keepdims=True), axis=1, keepdims=True)
        for g in range(4)
    )
    mean = total / dets
    part = seen_sum / total
    level = (cross - part * square) / (total * mean)
    inverse = 1.0 / mean
    blank_ends(buf_a, buf_b)
    theta, _ = chebyshev_scalars()

    def weighted(n, u, p):
        return n * (((u - p * part) * inverse - level) * inverse)

    def set_up(i, carry):
        value = weighted(count[i], change[i], phi[i + 1])
        b[i] = value
        buf_a[i + 1] = value * (1.0 / theta)
        return carry

    lax.fori_loop(0, planes, set_up, 0, unroll=4)
    for i in range(planes):
        u = edge_tile(came[i // GROUP], i % GROUP, y)
        value = weighted(count[i, edge, :], u, phi[i + 1, edge, :])
        b[i, edge, :] = value
        buf_a[i + 1, edge, :] = value * (1.0 / theta)
    dual = solve(b, (buf_a, buf_b), diag, fx, fy, fz, 16)

    def product(i, carry):
        p, u = phi[i + 1], dual[i + 1]
        grad = (p - phi[i]) * (u - dual[i]) + (p - phi[i + 2]) * (u - dual[i + 2])
        both = p * u
        for axis in range(2):
            flow = (p - beyond(p, 1, axis)) * (u - beyond(u, 1, axis))
            first = index_along(p.shape, axis) == 0
            grad = grad + flow + jnp.where(first, both, shifted(flow, 1, axis))
        grad_k[i] = -0.5 * grad
        grad_a[i] = -both
        for f, ref in enumerate((grad_k, grad_a)):
            own[f, i] = ref[i, pl.ds(base + cy * c, cy), :]
            message[f, i] = ref[i, pl.ds(base + cy * (1 - c), cy), :]
        return carry

    lax.fori_loop(0, planes, product, 0, unroll=4)


def core_kernel(own, came, kept, far, near):
    s, x, _, _ = places(2)
    n, _, groups, cy, lanes = kept.shape
    slab = lanes // n
    lane = index_along((cy, lanes), 1) // slab
    for h in range(2):
        for f in range(2):
            for q in range(groups):
                at = n * (groups * (x if h == 0 else 1 - x) + q)
                planes = [own[f, at + j] + came[f, at + j] for j in range(n)]
                for k in range(n):
                    to = s ^ k
                    piece = jnp.zeros((cy, lanes), jnp.float32)
                    for j in range(n):
                        moved = pltpu.roll(planes[j], ((j - to + n) % n) * slab, 1)
                        piece = jnp.where(lane == j, moved, piece)
                    if h == 0:
                        kept[k, f, q] = piece
                    elif k >= n // 2:
                        far[k - n // 2, f, q] = piece
                    else:
                        near[k, f, q] = piece


def add_kernel(kept, came, *outs, first):
    for i, out in enumerate(outs):
        out[...] = kept[first + i] + came[i]


def sum_kernel(*refs):
    total = refs[0][...]
    for ref in refs[1:-1]:
        total = total + ref[...]
    refs[-1][...] = total


def project_kernel(*refs, parts_n, n):
    beta_prev = refs[0]
    parts = refs[1 : 1 + parts_n]
    vk, va, qk, qa, w_k, w_a, tile = refs[1 + parts_n :]
    s, x, y, c = places(2)
    slab = 128 // n
    for f, (q_ref, w) in enumerate(((qk, w_k), (qa, w_a))):
        for q in range(vk.shape[0] // n):
            whole = sum(part[f, q] for part in parts[1:]) + parts[0][f, q]
            for j in range(n):
                i = n * q + j
                w[i] = whole[:, slab * j : slab * (j + 1)] - beta_prev[:, : vk.shape[2]] * q_ref[i]

    def dot(a, b):
        return jnp.sum(jnp.sum(a * b, axis=0))

    wk, wa, v_k, v_a = w_k[...], w_a[...], vk[...], va[...]
    one = jnp.ones((1, 1), jnp.float32)
    wv = (dot(wk, v_k) + dot(wa, v_a)) * one
    vv = (dot(v_k, v_k) + dot(v_a, v_a)) * one
    a = jnp.where(vv > 0.0, wv / jnp.where(vv > 0.0, vv, 1.0), 0.0)
    u_k, u_a = wk - a * v_k, wa - a * v_a
    uv = (dot(u_k, v_k) + dot(u_a, v_a)) * one
    uu = (dot(u_k, u_k) + dot(u_a, u_a)) * one
    me = ((s * 2 + x) * 2 + y) * 2 + c
    lane = index_along((8, 128), 1)
    row = index_along((8, 128), 0)
    values = jnp.zeros((8, 128), jnp.float32)
    for i, value in enumerate((wv, vv, a, uv, uu)):
        values = jnp.where(row == i, value, values)
    tile[...] = jnp.where(lane == me, values, 0.0)


def final_kernel(tiles, w_k, w_a, vk, va, next_k, next_a, coefs, *, cells):
    tile = jnp.sum(tiles[...], axis=0)
    wv, vv, a, uv, uu = (tile[i : i + 1] for i in range(5))
    wv_sum = jnp.sum(wv, axis=1, keepdims=True)
    vv_sum = jnp.sum(vv, axis=1, keepdims=True)
    alpha = wv_sum / cells / (vv_sum / cells + eps_norm)
    off = alpha - a
    rr = jnp.sum(uu - 2.0 * off * uv + off * off * vv, axis=1, keepdims=True)
    beta = jnp.sqrt(rr / cells + eps_norm)
    next_k[...] = (w_k[...] - alpha * vk[...]) / beta
    next_a[...] = (w_a[...] - alpha * va[...]) / beta
    coefs[0] = jnp.sum(alpha)
    coefs[1] = jnp.sum(beta)


def f32(*shape):
    return jax.ShapeDtypeStruct(shape, jnp.float32)


def run(kernel, outs, *args, after=(), scratch=(), copies=0, smem=(), hbm=(), mib=16, in_smem_out=(), cost=None):
    vmem = pl.BlockSpec(memory_space=pltpu.VMEM)
    scalar = pl.BlockSpec(memory_space=pltpu.SMEM)
    far = pl.BlockSpec(memory_space=pltpu.HBM)
    held = [pltpu.VMEM(shape, dtype) for shape, dtype in scratch]
    used, waits = len(args), len(after)

    def body(*refs):
        kernel(*refs[:used], *refs[used + waits :])

    args = (*args, *after)
    if copies:
        held.append(pltpu.SemaphoreType.DMA((copies,)))
    return pl.pallas_call(
        body if waits else kernel,
        out_shape=tuple(outs),
        in_specs=[scalar if i in smem else far if i in hbm else vmem for i in range(len(args))],
        out_specs=tuple(scalar if i in in_smem_out else vmem for i in range(len(outs))),
        scratch_shapes=held,
        compiler_params=pltpu.CompilerParams(vmem_limit_bytes=mib * 2**20),
        cost_estimate=cost,
    )(*args)


HALO = 8
REACH = 6
GROUP = 4


def per_device_paired(
    labels, kappa_table, absorb_table, background, det_cells,
    v_kappa, v_absorb, q_kappa, q_absorb, beta_prev,
):
    sources, cx, cy, cz = background.shape
    n = lax.axis_size("src")
    planes, rows = 2 * cx, 2 * cy + HALO
    ny = cy * lax.axis_size("gy")
    dets = det_cells.shape[0]
    cells = planes * ny * cz
    groups = cx // n

    def swap_x(value):
        return lax.ppermute(value, "gx", [(0, 1), (1, 0)])

    def swap_core(value):
        return lax.ppermute(value, "gy", [(0, 1), (1, 0), (2, 3), (3, 2)])

    def along_z(value, k):
        return lax.ppermute(value, "src", [(i, i ^ k) for i in range(n)])

    block = (cx, cy, cz)
    float_block = lambda *shape: (shape, jnp.float32)
    raw_labels = (block, jnp.int32)
    packed, message = run(
        pack_kernel, (f32(2, groups, cy, cz), f32(sources // 2 + 1, *block)),
        background, labels, v_kappa, v_absorb, hbm=(0, 1, 2, 3),
        scratch=(raw_labels, float_block(2, *v_kappa.shape)), copies=4, mib=60,
    )
    long = pl.CostEstimate(flops=10**9, bytes_accessed=2**26, transcendentals=0)
    came = swap_x(message)
    slabs = [along_z(packed, k) for k in range(1, n)]
    count, beta_row = run(
        functools.partial(count_kernel, ny=ny, nz=cz, half=2 * cy, halo=HALO),
        (f32(planes, rows, cz), f32(1, cz)), det_cells.reshape(1, dets), beta_prev, smem=(1,),
        cost=pl.CostEstimate(flops=2 * planes * rows * cz * dets, bytes_accessed=planes * rows * cz * 4, transcendentals=0),
    )

    def across_y(value):
        return lax.ppermute(value, "gy", [(i, (i + 2) % 4) for i in range(4)])

    (half_vector,) = run(unpack_kernel, (f32(2, *block),), v_kappa, v_absorb, *slabs, after=(count,))
    half_came = swap_x(half_vector)
    mine, fields = run(
        photon_kernel, (f32(planes, cy, cz), f32(2, planes, cy, cz)),
        background, labels, came, after=(half_vector,), hbm=(0, 1), scratch=(raw_labels,), copies=3,
    )
    got = swap_core(fields)
    (vector,) = run(vector_kernel, (f32(2, planes, cy, cz),), half_vector, half_came, after=(mine,))
    edge = (f32(2, *edge_shape(planes, cz)),)
    (sent,) = run(photon_edge_kernel, edge, mine, fields, got, after=(vector,))
    photon_edge = across_y(sent)
    vector_got = swap_core(vector)
    (vector_sent,) = run(vector_edge_kernel, edge, vector, vector_got, after=(sent,))
    frame, wide = (planes, rows, cz), (planes + 2, rows, cz)
    float_frame, float_wide = float_block(*frame), float_block(*wide)
    diag, fx, fy, fz, sums = run(
        stencil_kernel,
        (f32(*frame), f32(planes + 1, rows, cz), f32(*frame), f32(*frame), f32(2, 8, cz)),
        kappa_table, absorb_table, mine, fields, got, photon_edge, count, after=(vector_sent,), cost=long,
        smem=(0, 1), scratch=(float_frame, float_wide),
    )
    phi, change, sent = run(
        first_kernel, (f32(*wide), f32(*frame), f32(4, GROUP * REACH + 8, cz)),
        diag, fx, fy, fz, count, sums, mine, got, vector, vector_got,
        photon_edge, across_y(vector_sent),
        scratch=(float_wide, float_frame, float_frame, float_wide, float_wide),
    )
    heard = across_y(sent)
    own, message = run(
        functools.partial(second_kernel, dets=dets),
        (f32(2, planes, cy, cz), f32(2, planes, cy, cz)),
        phi, change, diag, fx, fy, fz, count, sent, heard,
        scratch=(float_frame, float_wide, float_wide, float_frame, float_frame),
    )
    piece = f32(2, groups, cy, cz)
    half = n // 2
    kept, far, near = run(
        core_kernel,
        (f32(n, *piece.shape), f32(n - half, *piece.shape), f32(half, *piece.shape)),
        own, swap_core(message),
    )
    far, near = swap_x(far), swap_x(near)
    pieces = run(functools.partial(add_kernel, first=half), [piece] * (n - half), kept, far)
    (distant,) = run(sum_kernel, (piece,), *(along_z(value, half + i) for i, value in enumerate(pieces)), cost=long)
    pieces = run(functools.partial(add_kernel, first=0), [piece] * half, kept, near)
    parts = [pieces[0], distant] + [along_z(pieces[k], k) for k in range(1, half)]
    w_k, w_a, tile = run(
        functools.partial(project_kernel, parts_n=len(parts), n=n),
        (f32(*v_kappa.shape), f32(*v_kappa.shape), f32(8, 128)),
        beta_row, *parts, v_kappa, v_absorb, q_kappa, q_absorb,
    )
    everyone = ("src", "gx", "gy")
    tiles = lax.all_to_all(jnp.broadcast_to(tile, (8 * n, 8, 128)), everyone, 0, 0)
    return tuple(run(
        functools.partial(final_kernel, cells=cells),
        (f32(*v_kappa.shape), f32(*v_kappa.shape), f32(2)),
        tiles, w_k, w_a, v_kappa, v_absorb, in_smem_out=(2,),
    ))


def paired_fits(mesh):
    return mesh.shape["gx"] == 2 and mesh.shape["gy"] == 4


def body_for(mesh):
    if not paired_fits(mesh):
        return per_device

    def chosen(*args):
        sources, cx, cy, cz = args[3].shape
        n = lax.axis_size("src")
        fits = sources == 4 and cz == 128 and cx % n == 0 and cx % GROUP == 0 and cy % HALO == 0 and n & (n - 1) == 0
        devices = 8 * n
        return (per_device_paired if fits and devices <= 128 else per_device)(*args)

    return chosen


def solution(mesh):
    return jax.shard_map(
        body_for(mesh),
        mesh=mesh,
        in_specs=(
            P("gx", "gy", None),
            P(),
            P(),
            P("src", "gx", "gy", None),
            P(),
            P("gx", "gy", "src"),
            P("gx", "gy", "src"),
            P("gx", "gy", "src"),
            P("gx", "gy", "src"),
            P(),
        ),
        out_specs=(P("gx", "gy", "src"), P("gx", "gy", "src"), P()),
        check_vma=False,
    )
```

```python
import functools

import jax
import jax.numpy as jnp
from jax import lax
from jax.experimental import pallas as pl
from jax.experimental.pallas import tpu as pltpu
from jax.sharding import PartitionSpec as P

ITERS = 6


lam_low = 0.02
lam_high = 24.1
eps_norm = 1e-06


def padded_2(block, sides, width):
    for axis, dim in sides:
        count = lax.axis_size(axis)
        forward = [(i, i + 1) for i in range(count - 1)]
        backward = [(target, source) for source, target in forward]
        low = lax.ppermute(
            lax.slice_in_dim(block, block.shape[dim] - width, None, axis=dim), axis, forward
        )
        high = lax.ppermute(lax.slice_in_dim(block, 0, width, axis=dim), axis, backward)
        block = jnp.concatenate([low, block, high], axis=dim)
    return block


def regional(labels, table):
    field = jnp.zeros(labels.shape, jnp.float32)
    for region in range(table.shape[0]):
        field = field + jnp.where(labels == region, table[region], 0.0)
    return field


def beside(padded):
    widths = [(0, 0)] * (padded.ndim - 1) + [(1, 1)]
    full = jnp.pad(padded, widths)
    return [
        full[..., 2:, 1:-1, 1:-1],
        full[..., :-2, 1:-1, 1:-1],
        full[..., 1:-1, 2:, 1:-1],
        full[..., 1:-1, :-2, 1:-1],
        full[..., 1:-1, 1:-1, 2:],
        full[..., 1:-1, 1:-1, :-2],
    ]


def chebyshev(rhs, apply_op):
    theta = 0.5 * (lam_high + lam_low)
    delta = 0.5 * (lam_high - lam_low)
    sigma = theta / delta
    rho = 1.0 / sigma
    solution = jnp.zeros_like(rhs)
    remain = rhs
    step_dir = rhs / theta
    for step in range(ITERS):
        solution = solution + step_dir
        if step + 1 < ITERS:
            remain = remain - apply_op(step_dir)
            rho_next = 1.0 / (2.0 * sigma - rho)
            step_dir = rho_next * rho * step_dir + 2.0 * rho_next / delta * remain
            rho = rho_next
    return solution


def per_device(
    labels,
    kappa_table,
    absorb_table,
    background,
    det_cells,
    v_kappa,
    v_absorb,
    q_kappa,
    q_absorb,
    beta_prev,
):
    sources, cx, cy, cz = background.shape
    kappa = regional(labels, kappa_table)
    absorb = regional(labels, absorb_table)
    full_k, full_a = (
        lax.all_gather(v_kappa, "src", axis=2, tiled=True),
        lax.all_gather(v_absorb, "src", axis=2, tiled=True),
    )
    stacked = jnp.concatenate([background, kappa[None], full_k[None]], axis=0)
    rims = padded_2(stacked, (("gx", 1), ("gy", 2)), 1)
    near_all = beside(rims)
    kappa_faces = [0.5 * (kappa + near[sources]) for near in near_all]
    vk_faces = [0.5 * (full_k + near[sources + 1]) for near in near_all]
    phi_near = [near[:sources] for near in near_all]

    def apply_op(field):
        padded = padded_2(field, (("gx", 1), ("gy", 2)), 1)
        result = absorb * field
        for face, near in zip(kappa_faces, beside(padded)):
            result = result + face * (field - near)
        return result

    rhs = full_a * background
    for face, near in zip(vk_faces, phi_near):
        rhs = rhs + face * (background - near)
    rhs = -rhs
    change = chebyshev(rhs, apply_op)
    span_y = cy * lax.axis_size("gy")
    ix = det_cells // (span_y * cz)
    iy = det_cells // cz % span_y
    iz = det_cells % cz
    anchor_x = lax.axis_index("gx") * cx
    anchor_y = lax.axis_index("gy") * cy
    owned = (ix >= anchor_x) & (ix < anchor_x + cx) & (iy >= anchor_y) & (iy < anchor_y + cy)
    local = jnp.where(owned, ((ix - anchor_x) * cy + (iy - anchor_y)) * cz + iz, 0)
    seen_part = jnp.where(owned[None, :], change.reshape(sources, -1)[:, local], 0.0)
    base_part = jnp.where(owned[None, :], background.reshape(sources, -1)[:, local], 0.0)
    seen, base = lax.psum((seen_part, base_part), ("gx", "gy"))
    total = jnp.sum(base, axis=1, keepdims=True)
    mean_base = total / det_cells.shape[0]
    ratio = base / total
    jv_vals = (seen - ratio * jnp.sum(seen, axis=1, keepdims=True)) / mean_base
    weight = (jv_vals - jnp.sum(ratio * jv_vals, axis=1, keepdims=True)) / mean_base
    deposit = jnp.where(owned[None, :], weight, 0.0)
    source = (
        jnp.zeros((sources, cx * cy * cz), jnp.float32)
        .at[:, local]
        .add(deposit)
        .reshape(change.shape)
    )
    dual = chebyshev(source, apply_op)
    dual_rims = padded_2(dual, (("gx", 1), ("gy", 2)), 1)
    grad_a = -jnp.sum(background * dual, axis=0)
    grad_k = jnp.zeros_like(kappa)
    for near_phi, near_dual in zip(phi_near, beside(dual_rims)):
        grad_k = grad_k - 0.5 * jnp.sum((background - near_phi) * (dual - near_dual), axis=0)
    summed_k, summed_a = lax.psum((grad_k, grad_a), "src")
    slab = v_kappa.shape[2]
    offset = lax.axis_index("src") * slab
    hv_k = lax.dynamic_slice_in_dim(summed_k, offset, slab, 2)
    hv_a = lax.dynamic_slice_in_dim(summed_a, offset, slab, 2)
    cell_count = cx * lax.axis_size("gx") * cy * lax.axis_size("gy") * cz
    w_k = hv_k - beta_prev[0] * q_kappa
    w_a = hv_a - beta_prev[0] * q_absorb
    local_wv = jnp.sum(w_k * v_kappa) + jnp.sum(w_a * v_absorb)
    local_vv = jnp.sum(v_kappa * v_kappa) + jnp.sum(v_absorb * v_absorb)
    wv_sum, vv_sum = lax.psum((local_wv, local_vv), ("src", "gx", "gy"))
    alpha = wv_sum / cell_count / (vv_sum / cell_count + eps_norm)
    r_k = w_k - alpha * v_kappa
    r_a = w_a - alpha * v_absorb
    rr_sum = lax.psum(jnp.sum(r_k * r_k) + jnp.sum(r_a * r_a), ("src", "gx", "gy"))
    beta = jnp.sqrt(rr_sum / cell_count + eps_norm)
    return (r_k / beta, r_a / beta, jnp.stack([alpha, beta]))


def chebyshev_scalars():
    theta = 0.5 * (lam_high + lam_low)
    delta = 0.5 * (lam_high - lam_low)
    sigma = theta / delta
    rho = 1.0 / sigma
    pairs = []
    for _ in range(ITERS - 1):
        rho_next = 1.0 / (2.0 * sigma - rho)
        pairs.append((rho_next * rho, 2.0 * rho_next / delta))
        rho = rho_next
    return theta, pairs


def places(split):
    g = lax.axis_index("gy")
    return lax.axis_index("src"), lax.axis_index("gx"), g // split, g % split


def shifted(value, step, axis):
    return pltpu.roll(value, step % value.shape[axis], axis)


def index_along(shape, axis):
    return lax.broadcasted_iota(jnp.int32, shape, axis)


def beyond(value, step, axis):
    size = value.shape[axis]
    at = index_along(value.shape, axis)
    edge = size - 1 if step == 1 else 0
    return jnp.where(at == edge, 0.0, shifted(value, -step, axis))


def packed_planes(ref, q):
    per = 128 // ref.shape[2]
    return jnp.concatenate([ref[per * q + j] for j in range(per)], axis=1)


def pack_kernel(bg, labels, vk, va, packed, message, raw, v_in, sems):
    _, x, _, _ = places(2)
    half = bg.shape[0] // 2
    copies = [
        pltpu.make_async_copy(src, dst, sems.at[i])
        for i, (src, dst) in enumerate((
            (vk, v_in.at[0]),
            (va, v_in.at[1]),
            (bg.at[pl.ds(half * (1 - x), half)], message.at[pl.ds(0, half)]),
            (labels, raw),
        ))
    ]
    for copy in copies:
        copy.start()
    for f in range(2):
        copies[f].wait()
        for q in range(packed.shape[1]):
            packed[f, q] = packed_planes(v_in.at[f], q)
    copies[3].wait()
    message[half] = raw[...].astype(jnp.float32)
    copies[2].wait()


def count_kernel(dets, beta_prev, count, beta_row, *, ny, nz, half, halo):
    beta_row[...] = jnp.full(beta_row.shape, beta_prev[0])
    _, _, y, _ = places(2)
    planes, rows, _ = count.shape
    flat = dets[...]
    iz = flat % nz
    line = flat // nz
    iy = line % ny
    ix = line // ny
    row = iy - (half - halo) * y
    spot = jnp.where((row >= 0) & (row < rows), ix * rows + row, -1)
    dets_n = flat.shape[1]
    at_z = (index_along((nz, dets_n), 0) == iz).astype(jnp.float32).astype(jnp.bfloat16)

    def body(i, carry):
        here = index_along((2 * rows, dets_n), 0) + i * (2 * rows)
        hot = (here == spot).astype(jnp.float32).astype(jnp.bfloat16)
        found = lax.dot_general(hot, at_z, (((1,), (1,)), ((), ())), preferred_element_type=jnp.float32)
        count[pl.ds(2 * i, 2)] = found.reshape(2, rows, nz)
        return carry

    lax.fori_loop(0, planes // 2, body, 0)


def photon_kernel(bg, labels, msg, mine, fields, raw, sems):
    _, x, _, c = places(2)
    half = bg.shape[0] // 2
    cx = labels.shape[0]
    here, there = cx * x, cx * (1 - x)
    copies = [
        pltpu.make_async_copy(src, dst, sems.at[i])
        for i, (src, dst) in enumerate((
            (bg.at[half * x + c], mine.at[pl.ds(here, cx)]),
            (bg.at[half * x + 1 - c], fields.at[0, pl.ds(here, cx)]),
            (labels, raw),
        ))
    ]
    for copy in copies:
        copy.start()
    mine[pl.ds(there, cx)] = msg[c]
    fields[0, pl.ds(there, cx)] = msg[1 - c]
    fields[1, pl.ds(there, cx)] = msg[half]
    for copy in copies:
        copy.wait()
    fields[1, pl.ds(here, cx)] = raw[...].astype(jnp.float32)


def unpack_kernel(*refs):
    own, parts, full = refs[:2], refs[2:-1], refs[-1]
    n = len(parts) + 1
    s, _, _, _ = places(2)
    slab = 128 // n
    _, cx, cy, _ = full.shape
    lane = index_along((cy, 128), 1) // slab
    for f in range(2):
        for q in range(cx // n):
            blocks = [part[f, q] for part in parts]
            for j in range(n):
                plane = jnp.concatenate([own[f][n * q + j]] * n, axis=1)
                for k in range(1, n):
                    home = s ^ k
                    moved = pltpu.roll(blocks[k - 1], ((home - j + n) % n) * slab, 1)
                    plane = jnp.where(lane == home, moved, plane)
                full[f, n * q + j] = plane


def vector_kernel(own, came, fields):
    _, x, _, _ = places(2)
    cx = own.shape[1]
    fields[:, pl.ds(cx * x, cx)] = own[...]
    fields[:, pl.ds(cx * (1 - x), cx)] = came[...]


def edge_shape(planes, lanes):
    return planes // GROUP, GROUP * REACH, lanes


def packed_edges(tiles):
    return jnp.concatenate([tile[:REACH] for tile in tiles], axis=0)


def edge_tile(packed, j, y):
    rows = packed[REACH * j : REACH * (j + 1)]
    tile = jnp.concatenate([rows, jnp.zeros((HALO - REACH, rows.shape[1]), jnp.float32)], axis=0)
    return jnp.where(y == 0, tile, shifted(tile, HALO - REACH, 0))


def near_rows(ref, i, first, y):
    tile = ref[i, pl.ds(first, HALO), :]
    return jnp.where(y == 0, shifted(tile, REACH - HALO, 0), tile)


def edges_of(own, got, edge, y, c):
    first = (own.shape[1] - HALO) * (1 - y)
    for g in range(edge.shape[0]):
        edge[g] = packed_edges([
            jnp.where(c != y, near_rows(own, GROUP * g + j, first, y), near_rows(got, GROUP * g + j, first, y))
            for j in range(GROUP)
        ])


def photon_edge_kernel(mine, fields, got, edge):
    _, _, y, c = places(2)
    edges_of(mine, got.at[0], edge.at[0], y, c)
    edges_of(fields.at[1], got.at[1], edge.at[1], y, c)


def vector_edge_kernel(fields, got, edge):
    _, _, y, c = places(2)
    for f in range(2):
        edges_of(fields.at[f], got.at[f], edge.at[f], y, c)


def solve(b, bufs, diag, fx, fy, fz, unroll):
    planes = b.shape[0]
    _, pairs = chebyshev_scalars()
    for step, (keep, push) in enumerate(pairs):
        src, dst = bufs[step % 2], bufs[(step + 1) % 2]

        def body(i, carry):
            u, flow = carry
            beyond_x = src[i + 2]
            coef_y, coef_z = fy[i], fz[i]
            next_flow = fx[i + 1] * (beyond_x - u)
            left = b[i] - diag[i] * u + (next_flow - flow)
            left = left + coef_y * shifted(u, -1, 0) + shifted(coef_y * u, 1, 0)
            left = left + coef_z * shifted(u, -1, 1) + shifted(coef_z * u, 1, 1)
            change = u if step == 0 else u - dst[i + 1]
            dst[i + 1] = u + keep * change + push * left
            return beyond_x, next_flow

        first = src[1]
        lax.fori_loop(0, planes, body, (first, fx[0] * first), unroll=unroll)
    return bufs[len(pairs) % 2]


def folded(value):
    return jnp.sum(value.reshape(-1, 8, value.shape[1]), axis=0)


def framed(ref, shift, own, got, edge, y, c):
    planes, cy, _ = own.shape
    there = pl.ds(shift, planes)
    base = HALO * y
    ref[there, pl.ds(base + cy * c, cy), :] = own[...]
    ref[there, pl.ds(base + cy * (1 - c), cy), :] = got[...]
    for g in range(edge.shape[0]):
        packed = edge[g]
        for j in range(GROUP):
            ref[shift + GROUP * g + j, pl.ds(2 * cy * (1 - y), HALO), :] = edge_tile(packed, j, y)


def blank_ends(*refs):
    for ref in refs:
        blank = jnp.zeros(ref.shape[1:], jnp.float32)
        ref[0] = blank
        ref[ref.shape[0] - 1] = blank


def owned_rows(shape, base, count):
    at_row = index_along(shape, 0)
    return (at_row >= base) & (at_row < base + count)


def stencil_kernel(
    kap_table, abs_table, mine, fields, got, edge, count,
    diag, fx, fy, fz, sums,
    labels, kap,
):
    _, _, y, c = places(2)
    planes, cy, lanes = mine.shape
    rows = 2 * cy + HALO
    framed(labels, 0, fields.at[1], got.at[1], edge.at[1], y, c)
    blank_ends(kap)
    blank = jnp.zeros((rows, lanes), jnp.float32)
    lane = index_along((rows, lanes), 1)
    kap_row, abs_row = blank, blank
    for region in range(kap_table.shape[0]):
        kap_row = jnp.where(lane == region, kap_table[region], kap_row)
        abs_row = jnp.where(lane == region, abs_table[region], abs_row)

    def look_up(i, carry):
        at = labels[i].astype(jnp.int32)
        kap[i + 1] = jnp.take_along_axis(kap_row, at, axis=1)
        diag[i] = jnp.take_along_axis(abs_row, at, axis=1)
        return carry

    lax.fori_loop(0, planes, look_up, 0, unroll=4)
    fx[0] = 0.5 * kap[1]
    base = HALO * y

    def set_up(i, carry):
        k = kap[i + 1]
        along_y, along_z = 0.5 * (k + beyond(k, 1, 0)), 0.5 * (k + beyond(k, 1, 1))
        fx[i + 1] = 0.5 * (k + kap[i + 2])
        fy[i] = jnp.where(index_along(k.shape, 0) == rows - 1, 0.0, along_y)
        fz[i] = jnp.where(lane == lanes - 1, 0.0, along_z)
        back_y, back_z = 0.5 * (k + beyond(k, -1, 0)), 0.5 * (k + beyond(k, -1, 1))
        diag[i] = diag[i] + along_y + back_y + along_z + back_z
        total, square = carry
        for p, at in ((mine[i], c), (got[0, i], 1 - c)):
            part = count[i, pl.ds(base + cy * at, cy), :] * p
            total, square = total + folded(part), square + folded(part * p)
        return total, square

    zero = jnp.zeros((8, lanes), jnp.float32)
    sums[0], sums[1] = lax.fori_loop(0, planes, set_up, (zero, zero), unroll=4)


def first_kernel(
    diag, fx, fy, fz, count, sums, mine, got_photon, vector, got_vector, photon_edge, edge,
    phi, change, message,
    vk, va, b, buf_a, buf_b,
):
    _, _, y, c = places(2)
    planes, rows, lanes = change.shape
    cy = mine.shape[1]
    framed(phi, 1, mine, got_photon.at[0], photon_edge.at[0], y, c)
    framed(vk, 1, vector.at[0], got_vector.at[0], edge.at[0], y, c)
    framed(va, 0, vector.at[1], got_vector.at[1], edge.at[1], y, c)
    blank_ends(phi, vk, buf_a, buf_b)
    theta, _ = chebyshev_scalars()

    def set_up(i, carry):
        v, p = vk[i + 1], phi[i + 1]
        total = 0.5 * (v + vk[i]) * (p - phi[i]) + 0.5 * (v + vk[i + 2]) * (p - phi[i + 2])
        for axis in range(2):
            flow = 0.5 * (v + beyond(v, 1, axis)) * (p - beyond(p, 1, axis))
            first = index_along(v.shape, axis) == 0
            total = total + flow + jnp.where(first, 0.5 * v * p, -shifted(flow, 1, axis))
        total = -(va[i] * p + total)
        b[i] = total
        buf_a[i + 1] = total * (1.0 / theta)
        return carry

    lax.fori_loop(0, planes, set_up, 0, unroll=4)
    found = solve(b, (buf_a, buf_b), diag, fx, fy, fz, 16)
    owned = owned_rows((rows, lanes), HALO * y, 2 * cy)

    def add_up(i, carry):
        u = found[i + 1]
        change[i] = u
        part = jnp.where(owned, count[i], 0.0) * u
        return carry[0] + folded(part), carry[1] + folded(part * phi[i + 1])

    zero = jnp.zeros((8, lanes), jnp.float32)
    seen, cross = lax.fori_loop(0, planes, add_up, (zero, zero), unroll=4)
    first = (2 * cy - HALO) * (1 - y) + HALO * y
    for g, part in enumerate((sums[0], seen, cross, sums[1])):
        message[g, pl.ds(0, GROUP * REACH), :] = packed_edges(
            [near_rows(found, 1 + GROUP * g + j, first, y) for j in range(GROUP)]
        )
        message[g, pl.ds(GROUP * REACH, 8), :] = part


def second_kernel(
    phi, change, diag, fx, fy, fz, count, sent, came,
    own, message,
    b, buf_a, buf_b, grad_k, grad_a,
    *, dets,
):
    _, _, y, c = places(2)
    planes, rows, lanes = change.shape
    cy = (rows - HALO) // 2
    base = HALO * y
    edge = pl.ds(2 * cy * (1 - y), HALO)
    tail = pl.ds(GROUP * REACH, 8)
    total, seen_sum, cross, square = (
        jnp.sum(jnp.sum(sent[g, tail, :] + came[g, tail, :], axis=0, keepdims=True), axis=1, keepdims=True)
        for g in range(4)
    )
    mean = total / dets
    part = seen_sum / total
    level = (cross - part * square) / (total * mean)
    inverse = 1.0 / mean
    blank_ends(buf_a, buf_b)
    theta, _ = chebyshev_scalars()

    def weighted(n, u, p):
        return n * (((u - p * part) * inverse - level) * inverse)

    def set_up(i, carry):
        value = weighted(count[i], change[i], phi[i + 1])
        b[i] = value
        buf_a[i + 1] = value * (1.0 / theta)
        return carry

    lax.fori_loop(0, planes, set_up, 0, unroll=4)
    for i in range(planes):
        u = edge_tile(came[i // GROUP], i % GROUP, y)
        value = weighted(count[i, edge, :], u, phi[i + 1, edge, :])
        b[i, edge, :] = value
        buf_a[i + 1, edge, :] = value * (1.0 / theta)
    dual = solve(b, (buf_a, buf_b), diag, fx, fy, fz, 16)

    def product(i, carry):
        p, u = phi[i + 1], dual[i + 1]
        grad = (p - phi[i]) * (u - dual[i]) + (p - phi[i + 2]) * (u - dual[i + 2])
        both = p * u
        for axis in range(2):
            flow = (p - beyond(p, 1, axis)) * (u - beyond(u, 1, axis))
            first = index_along(p.shape, axis) == 0
            grad = grad + flow + jnp.where(first, both, shifted(flow, 1, axis))
        grad_k[i] = -0.5 * grad
        grad_a[i] = -both
        for f, ref in enumerate((grad_k, grad_a)):
            own[f, i] = ref[i, pl.ds(base + cy * c, cy), :]
            message[f, i] = ref[i, pl.ds(base + cy * (1 - c), cy), :]
        return carry

    lax.fori_loop(0, planes, product, 0, unroll=4)


def packed_slabs(own, came, half, choices, outs):
    s, _, _, _ = places(2)
    _, planes, cy, lanes = own.shape
    n = planes // 2 // outs.shape[2]
    slab = lanes // n
    lane = index_along((cy, lanes), 1) // slab
    for f in range(2):
        for q in range(outs.shape[2]):
            at = planes // 2 * half + n * q
            parts = [own[f, at + j] + came[f, at + j] for j in range(n)]
            for i, k in enumerate(choices):
                to = s ^ k
                piece = jnp.zeros((cy, lanes), jnp.float32)
                for j in range(n):
                    moved = pltpu.roll(parts[j], ((j - to + n) % n) * slab, 1)
                    piece = jnp.where(lane == j, moved, piece)
                outs[i, f, q] = piece


def far_kernel(own, came, far):
    _, x, _, _ = places(2)
    packed_slabs(own, came, 1 - x, range(far.shape[0], 2 * far.shape[0]), far)


def near_kernel(own, came, kept, near):
    _, x, _, _ = places(2)
    packed_slabs(own, came, 1 - x, range(near.shape[0]), near)
    packed_slabs(own, came, x, range(kept.shape[0]), kept)


def add_kernel(kept, came, *outs, first):
    for i, out in enumerate(outs):
        out[...] = kept[first + i] + came[i]


def sum_kernel(*refs):
    total = refs[0][...]
    for ref in refs[1:-1]:
        total = total + ref[...]
    refs[-1][...] = total


def project_kernel(*refs, parts_n, n):
    beta_prev = refs[0]
    parts = refs[1 : 1 + parts_n]
    vk, va, qk, qa, w_k, w_a, tile = refs[1 + parts_n :]
    s, x, y, c = places(2)
    slab = 128 // n
    for f, (q_ref, w) in enumerate(((qk, w_k), (qa, w_a))):
        for q in range(vk.shape[0] // n):
            whole = sum(part[f, q] for part in parts[1:]) + parts[0][f, q]
            for j in range(n):
                i = n * q + j
                w[i] = whole[:, slab * j : slab * (j + 1)] - beta_prev[:, : vk.shape[2]] * q_ref[i]

    def dot(a, b):
        return jnp.sum(jnp.sum(a * b, axis=0))

    wk, wa, v_k, v_a = w_k[...], w_a[...], vk[...], va[...]
    one = jnp.ones((1, 1), jnp.float32)
    wv = (dot(wk, v_k) + dot(wa, v_a)) * one
    vv = (dot(v_k, v_k) + dot(v_a, v_a)) * one
    a = jnp.where(vv > 0.0, wv / jnp.where(vv > 0.0, vv, 1.0), 0.0)
    u_k, u_a = wk - a * v_k, wa - a * v_a
    uv = (dot(u_k, v_k) + dot(u_a, v_a)) * one
    uu = (dot(u_k, u_k) + dot(u_a, u_a)) * one
    me = ((s * 2 + x) * 2 + y) * 2 + c
    lane = index_along((8, 128), 1)
    row = index_along((8, 128), 0)
    values = jnp.zeros((8, 128), jnp.float32)
    for i, value in enumerate((wv, vv, a, uv, uu)):
        values = jnp.where(row == i, value, values)
    tile[...] = jnp.where(lane == me, values, 0.0)


def final_kernel(tiles, w_k, w_a, vk, va, next_k, next_a, coefs, *, cells):
    tile = jnp.sum(tiles[...], axis=0)
    wv, vv, a, uv, uu = (tile[i : i + 1] for i in range(5))
    wv_sum = jnp.sum(wv, axis=1, keepdims=True)
    vv_sum = jnp.sum(vv, axis=1, keepdims=True)
    alpha = wv_sum / cells / (vv_sum / cells + eps_norm)
    off = alpha - a
    rr = jnp.sum(uu - 2.0 * off * uv + off * off * vv, axis=1, keepdims=True)
    beta = jnp.sqrt(rr / cells + eps_norm)
    next_k[...] = (w_k[...] - alpha * vk[...]) / beta
    next_a[...] = (w_a[...] - alpha * va[...]) / beta
    coefs[0] = jnp.sum(alpha)
    coefs[1] = jnp.sum(beta)


def f32(*shape):
    return jax.ShapeDtypeStruct(shape, jnp.float32)


def run(kernel, outs, *args, after=(), scratch=(), copies=0, smem=(), hbm=(), mib=16, in_smem_out=(), cost=None):
    vmem = pl.BlockSpec(memory_space=pltpu.VMEM)
    scalar = pl.BlockSpec(memory_space=pltpu.SMEM)
    far = pl.BlockSpec(memory_space=pltpu.HBM)
    held = [pltpu.VMEM(shape, dtype) for shape, dtype in scratch]
    used, waits = len(args), len(after)

    def body(*refs):
        kernel(*refs[:used], *refs[used + waits :])

    args = (*args, *after)
    if copies:
        held.append(pltpu.SemaphoreType.DMA((copies,)))
    return pl.pallas_call(
        body if waits else kernel,
        out_shape=tuple(outs),
        in_specs=[scalar if i in smem else far if i in hbm else vmem for i in range(len(args))],
        out_specs=tuple(scalar if i in in_smem_out else vmem for i in range(len(outs))),
        scratch_shapes=held,
        compiler_params=pltpu.CompilerParams(vmem_limit_bytes=mib * 2**20),
        cost_estimate=cost,
    )(*args)


HALO = 8
REACH = 6
GROUP = 4


def per_device_paired(
    labels, kappa_table, absorb_table, background, det_cells,
    v_kappa, v_absorb, q_kappa, q_absorb, beta_prev,
):
    sources, cx, cy, cz = background.shape
    n = lax.axis_size("src")
    planes, rows = 2 * cx, 2 * cy + HALO
    ny = cy * lax.axis_size("gy")
    dets = det_cells.shape[0]
    cells = planes * ny * cz
    groups = cx // n

    def swap_x(value):
        return lax.ppermute(value, "gx", [(0, 1), (1, 0)])

    def swap_core(value):
        return lax.ppermute(value, "gy", [(0, 1), (1, 0), (2, 3), (3, 2)])

    def along_z(value, k):
        return lax.ppermute(value, "src", [(i, i ^ k) for i in range(n)])

    block = (cx, cy, cz)
    float_block = lambda *shape: (shape, jnp.float32)
    raw_labels = (block, jnp.int32)
    packed, message = run(
        pack_kernel, (f32(2, groups, cy, cz), f32(sources // 2 + 1, *block)),
        background, labels, v_kappa, v_absorb, hbm=(0, 1, 2, 3),
        scratch=(raw_labels, float_block(2, *v_kappa.shape)), copies=4, mib=60,
    )
    long = pl.CostEstimate(flops=10**9, bytes_accessed=2**26, transcendentals=0)
    came = swap_x(message)
    slabs = [along_z(packed, k) for k in range(1, n)]
    count, beta_row = run(
        functools.partial(count_kernel, ny=ny, nz=cz, half=2 * cy, halo=HALO),
        (f32(planes, rows, cz), f32(1, cz)), det_cells.reshape(1, dets), beta_prev, smem=(1,),
        cost=pl.CostEstimate(flops=2 * planes * rows * cz * dets, bytes_accessed=planes * rows * cz * 4, transcendentals=0),
    )

    def across_y(value):
        return lax.ppermute(value, "gy", [(i, (i + 2) % 4) for i in range(4)])

    (half_vector,) = run(unpack_kernel, (f32(2, *block),), v_kappa, v_absorb, *slabs, after=(count,))
    half_came = swap_x(half_vector)
    mine, fields = run(
        photon_kernel, (f32(planes, cy, cz), f32(2, planes, cy, cz)),
        background, labels, came, after=(half_vector,), hbm=(0, 1), scratch=(raw_labels,), copies=3,
    )
    got = swap_core(fields)
    (vector,) = run(vector_kernel, (f32(2, planes, cy, cz),), half_vector, half_came, after=(mine,))
    edge = (f32(2, *edge_shape(planes, cz)),)
    (sent,) = run(photon_edge_kernel, edge, mine, fields, got, after=(vector,))
    photon_edge = across_y(sent)
    vector_got = swap_core(vector)
    (vector_sent,) = run(vector_edge_kernel, edge, vector, vector_got, after=(sent,))
    frame, wide = (planes, rows, cz), (planes + 2, rows, cz)
    float_frame, float_wide = float_block(*frame), float_block(*wide)
    diag, fx, fy, fz, sums = run(
        stencil_kernel,
        (f32(*frame), f32(planes + 1, rows, cz), f32(*frame), f32(*frame), f32(2, 8, cz)),
        kappa_table, absorb_table, mine, fields, got, photon_edge, count, after=(vector_sent,), cost=long,
        smem=(0, 1), scratch=(float_frame, float_wide),
    )
    phi, change, sent = run(
        first_kernel, (f32(*wide), f32(*frame), f32(4, GROUP * REACH + 8, cz)),
        diag, fx, fy, fz, count, sums, mine, got, vector, vector_got,
        photon_edge, across_y(vector_sent),
        scratch=(float_wide, float_frame, float_frame, float_wide, float_wide),
    )
    heard = across_y(sent)
    own, message = run(
        functools.partial(second_kernel, dets=dets),
        (f32(2, planes, cy, cz), f32(2, planes, cy, cz)),
        phi, change, diag, fx, fy, fz, count, sent, heard,
        scratch=(float_frame, float_wide, float_wide, float_frame, float_frame),
    )
    piece = f32(2, groups, cy, cz)
    half = n // 2
    got = swap_core(message)
    (far,) = run(far_kernel, (f32(half, *piece.shape),), own, got)
    kept, near = run(
        near_kernel, (f32(n, *piece.shape), f32(half, *piece.shape)), own, got, after=(far,)
    )
    far, near = swap_x(far), swap_x(near)
    pieces = run(functools.partial(add_kernel, first=half), [piece] * (n - half), kept, far)
    (distant,) = run(sum_kernel, (piece,), *(along_z(value, half + i) for i, value in enumerate(pieces)), cost=long)
    pieces = run(functools.partial(add_kernel, first=0), [piece] * half, kept, near)
    parts = [pieces[0], distant] + [along_z(pieces[k], k) for k in range(1, half)]
    w_k, w_a, tile = run(
        functools.partial(project_kernel, parts_n=len(parts), n=n),
        (f32(*v_kappa.shape), f32(*v_kappa.shape), f32(8, 128)),
        beta_row, *parts, v_kappa, v_absorb, q_kappa, q_absorb,
    )
    everyone = ("src", "gx", "gy")
    tiles = lax.all_to_all(jnp.broadcast_to(tile, (8 * n, 8, 128)), everyone, 0, 0)
    return tuple(run(
        functools.partial(final_kernel, cells=cells),
        (f32(*v_kappa.shape), f32(*v_kappa.shape), f32(2)),
        tiles, w_k, w_a, v_kappa, v_absorb, in_smem_out=(2,),
    ))


def paired_fits(mesh):
    return mesh.shape["gx"] == 2 and mesh.shape["gy"] == 4


def body_for(mesh):
    if not paired_fits(mesh):
        return per_device

    def chosen(*args):
        sources, cx, cy, cz = args[3].shape
        n = lax.axis_size("src")
        fits = sources == 4 and cz == 128 and cx % n == 0 and cx % GROUP == 0 and cy % HALO == 0 and n > 1 and n & (n - 1) == 0
        devices = 8 * n
        return (per_device_paired if fits and devices <= 128 else per_device)(*args)

    return chosen


def solution(mesh):
    return jax.shard_map(
        body_for(mesh),
        mesh=mesh,
        in_specs=(
            P("gx", "gy", None),
            P(),
            P(),
            P("src", "gx", "gy", None),
            P(),
            P("gx", "gy", "src"),
            P("gx", "gy", "src"),
            P("gx", "gy", "src"),
            P("gx", "gy", "src"),
            P(),
        ),
        out_specs=(P("gx", "gy", "src"), P("gx", "gy", "src"), P()),
        check_vma=False,
    )
```

```python
import functools

import jax
import jax.numpy as jnp
from jax import lax
from jax.experimental import pallas as pl
from jax.experimental.pallas import tpu as pltpu
from jax.sharding import PartitionSpec as P

ITERS = 6


lam_low = 0.02
lam_high = 24.1
eps_norm = 1e-06


def padded_2(block, sides, width):
    for axis, dim in sides:
        count = lax.axis_size(axis)
        forward = [(i, i + 1) for i in range(count - 1)]
        backward = [(target, source) for source, target in forward]
        low = lax.ppermute(
            lax.slice_in_dim(block, block.shape[dim] - width, None, axis=dim), axis, forward
        )
        high = lax.ppermute(lax.slice_in_dim(block, 0, width, axis=dim), axis, backward)
        block = jnp.concatenate([low, block, high], axis=dim)
    return block


def regional(labels, table):
    field = jnp.zeros(labels.shape, jnp.float32)
    for region in range(table.shape[0]):
        field = field + jnp.where(labels == region, table[region], 0.0)
    return field


def beside(padded):
    widths = [(0, 0)] * (padded.ndim - 1) + [(1, 1)]
    full = jnp.pad(padded, widths)
    return [
        full[..., 2:, 1:-1, 1:-1],
        full[..., :-2, 1:-1, 1:-1],
        full[..., 1:-1, 2:, 1:-1],
        full[..., 1:-1, :-2, 1:-1],
        full[..., 1:-1, 1:-1, 2:],
        full[..., 1:-1, 1:-1, :-2],
    ]


def chebyshev(rhs, apply_op):
    theta = 0.5 * (lam_high + lam_low)
    delta = 0.5 * (lam_high - lam_low)
    sigma = theta / delta
    rho = 1.0 / sigma
    solution = jnp.zeros_like(rhs)
    remain = rhs
    step_dir = rhs / theta
    for step in range(ITERS):
        solution = solution + step_dir
        if step + 1 < ITERS:
            remain = remain - apply_op(step_dir)
            rho_next = 1.0 / (2.0 * sigma - rho)
            step_dir = rho_next * rho * step_dir + 2.0 * rho_next / delta * remain
            rho = rho_next
    return solution


def per_device(
    labels,
    kappa_table,
    absorb_table,
    background,
    det_cells,
    v_kappa,
    v_absorb,
    q_kappa,
    q_absorb,
    beta_prev,
):
    sources, cx, cy, cz = background.shape
    kappa = regional(labels, kappa_table)
    absorb = regional(labels, absorb_table)
    full_k, full_a = (
        lax.all_gather(v_kappa, "src", axis=2, tiled=True),
        lax.all_gather(v_absorb, "src", axis=2, tiled=True),
    )
    stacked = jnp.concatenate([background, kappa[None], full_k[None]], axis=0)
    rims = padded_2(stacked, (("gx", 1), ("gy", 2)), 1)
    near_all = beside(rims)
    kappa_faces = [0.5 * (kappa + near[sources]) for near in near_all]
    vk_faces = [0.5 * (full_k + near[sources + 1]) for near in near_all]
    phi_near = [near[:sources] for near in near_all]

    def apply_op(field):
        padded = padded_2(field, (("gx", 1), ("gy", 2)), 1)
        result = absorb * field
        for face, near in zip(kappa_faces, beside(padded)):
            result = result + face * (field - near)
        return result

    rhs = full_a * background
    for face, near in zip(vk_faces, phi_near):
        rhs = rhs + face * (background - near)
    rhs = -rhs
    change = chebyshev(rhs, apply_op)
    span_y = cy * lax.axis_size("gy")
    ix = det_cells // (span_y * cz)
    iy = det_cells // cz % span_y
    iz = det_cells % cz
    anchor_x = lax.axis_index("gx") * cx
    anchor_y = lax.axis_index("gy") * cy
    owned = (ix >= anchor_x) & (ix < anchor_x + cx) & (iy >= anchor_y) & (iy < anchor_y + cy)
    local = jnp.where(owned, ((ix - anchor_x) * cy + (iy - anchor_y)) * cz + iz, 0)
    seen_part = jnp.where(owned[None, :], change.reshape(sources, -1)[:, local], 0.0)
    base_part = jnp.where(owned[None, :], background.reshape(sources, -1)[:, local], 0.0)
    seen, base = lax.psum((seen_part, base_part), ("gx", "gy"))
    total = jnp.sum(base, axis=1, keepdims=True)
    mean_base = total / det_cells.shape[0]
    ratio = base / total
    jv_vals = (seen - ratio * jnp.sum(seen, axis=1, keepdims=True)) / mean_base
    weight = (jv_vals - jnp.sum(ratio * jv_vals, axis=1, keepdims=True)) / mean_base
    deposit = jnp.where(owned[None, :], weight, 0.0)
    source = (
        jnp.zeros((sources, cx * cy * cz), jnp.float32)
        .at[:, local]
        .add(deposit)
        .reshape(change.shape)
    )
    dual = chebyshev(source, apply_op)
    dual_rims = padded_2(dual, (("gx", 1), ("gy", 2)), 1)
    grad_a = -jnp.sum(background * dual, axis=0)
    grad_k = jnp.zeros_like(kappa)
    for near_phi, near_dual in zip(phi_near, beside(dual_rims)):
        grad_k = grad_k - 0.5 * jnp.sum((background - near_phi) * (dual - near_dual), axis=0)
    summed_k, summed_a = lax.psum((grad_k, grad_a), "src")
    slab = v_kappa.shape[2]
    offset = lax.axis_index("src") * slab
    hv_k = lax.dynamic_slice_in_dim(summed_k, offset, slab, 2)
    hv_a = lax.dynamic_slice_in_dim(summed_a, offset, slab, 2)
    cell_count = cx * lax.axis_size("gx") * cy * lax.axis_size("gy") * cz
    w_k = hv_k - beta_prev[0] * q_kappa
    w_a = hv_a - beta_prev[0] * q_absorb
    local_wv = jnp.sum(w_k * v_kappa) + jnp.sum(w_a * v_absorb)
    local_vv = jnp.sum(v_kappa * v_kappa) + jnp.sum(v_absorb * v_absorb)
    wv_sum, vv_sum = lax.psum((local_wv, local_vv), ("src", "gx", "gy"))
    alpha = wv_sum / cell_count / (vv_sum / cell_count + eps_norm)
    r_k = w_k - alpha * v_kappa
    r_a = w_a - alpha * v_absorb
    rr_sum = lax.psum(jnp.sum(r_k * r_k) + jnp.sum(r_a * r_a), ("src", "gx", "gy"))
    beta = jnp.sqrt(rr_sum / cell_count + eps_norm)
    return (r_k / beta, r_a / beta, jnp.stack([alpha, beta]))


def chebyshev_scalars():
    theta = 0.5 * (lam_high + lam_low)
    delta = 0.5 * (lam_high - lam_low)
    sigma = theta / delta
    rho = 1.0 / sigma
    pairs = []
    for _ in range(ITERS - 1):
        rho_next = 1.0 / (2.0 * sigma - rho)
        pairs.append((rho_next * rho, 2.0 * rho_next / delta))
        rho = rho_next
    return theta, pairs


def places(split):
    g = lax.axis_index("gy")
    return lax.axis_index("src"), lax.axis_index("gx"), g // split, g % split


def shifted(value, step, axis):
    return pltpu.roll(value, step % value.shape[axis], axis)


def index_along(shape, axis):
    return lax.broadcasted_iota(jnp.int32, shape, axis)


def beyond(value, step, axis):
    size = value.shape[axis]
    at = index_along(value.shape, axis)
    edge = size - 1 if step == 1 else 0
    return jnp.where(at == edge, 0.0, shifted(value, -step, axis))


def packed_planes(ref, q):
    per = 128 // ref.shape[2]
    return jnp.concatenate([ref[per * q + j] for j in range(per)], axis=1)


def pack_kernel(bg, labels, vk, va, packed, message, raw, v_in, sems):
    _, x, _, _ = places(2)
    half = bg.shape[0] // 2
    cx = labels.shape[0]
    copies = [
        pltpu.make_async_copy(src, dst, sems.at[i])
        for i, (src, dst) in enumerate((
            (vk, v_in.at[0]),
            (va, v_in.at[1]),
            (labels, raw),
            *((bg.at[half * (1 - x) + i], message.at[pl.ds(cx * i, cx)]) for i in range(half)),
        ))
    ]
    for copy in copies:
        copy.start()
    groups = packed.shape[0] // 2
    for f in range(2):
        copies[f].wait()
        for q in range(groups):
            planes = packed_planes(v_in.at[f], q)
            packed[groups * f + q] = planes
            message[cx * (half + 1) + groups * f + q] = planes
    copies[2].wait()
    message[pl.ds(cx * half, cx)] = raw[...].astype(jnp.float32)
    for copy in copies[3:]:
        copy.wait()


def count_kernel(dets, beta_prev, count, beta_row, *, ny, nz, half, halo):
    beta_row[...] = jnp.full(beta_row.shape, beta_prev[0])
    _, _, y, _ = places(2)
    planes, rows, _ = count.shape
    flat = dets[...]
    iz = flat % nz
    line = flat // nz
    iy = line % ny
    ix = line // ny
    row = iy - (half - halo) * y
    spot = jnp.where((row >= 0) & (row < rows), ix * rows + row, -1)
    dets_n = flat.shape[1]
    at_z = (index_along((nz, dets_n), 0) == iz).astype(jnp.float32).astype(jnp.bfloat16)

    def body(i, carry):
        here = index_along((2 * rows, dets_n), 0) + i * (2 * rows)
        hot = (here == spot).astype(jnp.float32).astype(jnp.bfloat16)
        found = lax.dot_general(hot, at_z, (((1,), (1,)), ((), ())), preferred_element_type=jnp.float32)
        count[pl.ds(2 * i, 2)] = found.reshape(2, rows, nz)
        return carry

    lax.fori_loop(0, planes // 2, body, 0)


def photon_kernel(bg, labels, msg, mine, fields, raw, sems):
    _, x, _, c = places(2)
    half = bg.shape[0] // 2
    cx = labels.shape[0]
    here, there = cx * x, cx * (1 - x)
    copies = [
        pltpu.make_async_copy(src, dst, sems.at[i])
        for i, (src, dst) in enumerate((
            (bg.at[half * x + c], mine.at[pl.ds(here, cx)]),
            (bg.at[half * x + 1 - c], fields.at[0, pl.ds(here, cx)]),
            (labels, raw),
        ))
    ]
    for copy in copies:
        copy.start()
    mine[pl.ds(there, cx)] = msg[pl.ds(cx * c, cx)]
    fields[0, pl.ds(there, cx)] = msg[pl.ds(cx * (1 - c), cx)]
    fields[1, pl.ds(there, cx)] = msg[pl.ds(cx * half, cx)]
    for copy in copies:
        copy.wait()
    fields[1, pl.ds(here, cx)] = raw[...].astype(jnp.float32)


def unpacked(blocks, groups, s, store):
    n = len(blocks)
    cy, lanes = blocks[0][0].shape
    slab = lanes // n
    lane = index_along((cy, lanes), 1) // slab
    for f in range(2):
        for q in range(groups):
            values = [block[groups * f + q] for block in blocks]
            for j in range(n):
                plane = jnp.zeros((cy, lanes), jnp.float32)
                for k in range(n):
                    home = s ^ k
                    moved = pltpu.roll(values[k], ((home - j + n) % n) * slab, 1)
                    plane = jnp.where(lane == home, moved, plane)
                store(f, n * q + j, plane)


def join_kernel(*refs):
    joined, size = refs[-1], refs[0].shape[0]
    for i, ref in enumerate(refs[:-1]):
        joined[pl.ds(size * i, size)] = ref[...]


def own_half_kernel(vk, va, joined, half):
    s, _, _, _ = places(2)
    size = half.shape[1]
    groups = joined.shape[0] // 2 // (128 // vk.shape[2] - 1)
    n = size // groups
    own = [packed_planes(ref, q) for ref in (vk, va) for q in range(groups)]
    blocks = [own] + [[joined[2 * groups * k + i] for i in range(2 * groups)] for k in range(n - 1)]

    def store(f, i, plane):
        half[f, i] = plane

    unpacked(blocks, groups, s, store)


def vector_kernel(half, msg, joined, fields):
    s, x, _, _ = places(2)
    cx = half.shape[1]
    fields[:, pl.ds(cx * x, cx)] = half[...]
    n = lax.axis_size("src")
    groups = cx // n
    own = msg.shape[0] - 2 * groups
    blocks = [[msg[own + i] for i in range(2 * groups)]]
    blocks += [[joined[2 * groups * k + i] for i in range(2 * groups)] for k in range(n - 1)]
    there = cx * (1 - x)

    def store(f, i, plane):
        fields[f, there + i] = plane

    unpacked(blocks, groups, s, store)


def edge_shape(planes, lanes):
    return planes // GROUP, GROUP * REACH, lanes


def packed_edges(tiles):
    return jnp.concatenate([tile[:REACH] for tile in tiles], axis=0)


def edge_tile(packed, j, y):
    rows = packed[REACH * j : REACH * (j + 1)]
    tile = jnp.concatenate([rows, jnp.zeros((HALO - REACH, rows.shape[1]), jnp.float32)], axis=0)
    return jnp.where(y == 0, tile, shifted(tile, HALO - REACH, 0))


def near_rows(ref, i, first, y):
    tile = ref[i, pl.ds(first, HALO), :]
    return jnp.where(y == 0, shifted(tile, REACH - HALO, 0), tile)


def edges_of(own, got, edge, y, c):
    first = (own.shape[1] - HALO) * (1 - y)
    for g in range(edge.shape[0]):
        edge[g] = packed_edges([
            jnp.where(c != y, near_rows(own, GROUP * g + j, first, y), near_rows(got, GROUP * g + j, first, y))
            for j in range(GROUP)
        ])


def photon_edge_kernel(mine, fields, got, edge):
    _, _, y, c = places(2)
    edges_of(mine, got.at[0], edge.at[0], y, c)
    edges_of(fields.at[1], got.at[1], edge.at[1], y, c)


def vector_edge_kernel(fields, got, edge):
    _, _, y, c = places(2)
    for f in range(2):
        edges_of(fields.at[f], got.at[f], edge.at[f], y, c)


def solve(b, bufs, diag, fx, fy, fz, unroll):
    planes = b.shape[0]
    _, pairs = chebyshev_scalars()
    for step, (keep, push) in enumerate(pairs):
        src, dst = bufs[step % 2], bufs[(step + 1) % 2]

        def body(i, carry):
            u = src[i + 1]
            coef_y, coef_z = fy[i], fz[i]
            left = b[i] - diag[i] * u
            left = left + fx[i] * src[i] + fx[i + 1] * src[i + 2]
            left = left + coef_y * shifted(u, -1, 0) + shifted(coef_y * u, 1, 0)
            left = left + coef_z * shifted(u, -1, 1) + shifted(coef_z * u, 1, 1)
            change = u if step == 0 else u - dst[i + 1]
            dst[i + 1] = u + keep * change + push * left
            return carry

        lax.fori_loop(0, planes, body, 0, unroll=unroll)
    return bufs[len(pairs) % 2]


def folded(value):
    return jnp.sum(value.reshape(-1, 8, value.shape[1]), axis=0)


def framed(ref, shift, own, got, edge, y, c):
    planes, cy, _ = own.shape
    there = pl.ds(shift, planes)
    base = HALO * y
    ref[there, pl.ds(base + cy * c, cy), :] = own[...]
    ref[there, pl.ds(base + cy * (1 - c), cy), :] = got[...]
    for g in range(edge.shape[0]):
        packed = edge[g]
        for j in range(GROUP):
            ref[shift + GROUP * g + j, pl.ds(2 * cy * (1 - y), HALO), :] = edge_tile(packed, j, y)


def blank_ends(*refs):
    for ref in refs:
        blank = jnp.zeros(ref.shape[1:], jnp.float32)
        ref[0] = blank
        ref[ref.shape[0] - 1] = blank


def owned_rows(shape, base, count):
    at_row = index_along(shape, 0)
    return (at_row >= base) & (at_row < base + count)


def stencil_kernel(
    kap_table, abs_table, mine, fields, got, edge, count,
    diag, fx, fy, fz, sums,
    labels, kap,
):
    _, _, y, c = places(2)
    planes, cy, lanes = mine.shape
    rows = 2 * cy + HALO
    framed(labels, 0, fields.at[1], got.at[1], edge.at[1], y, c)
    blank_ends(kap)
    blank = jnp.zeros((rows, lanes), jnp.float32)
    lane = index_along((rows, lanes), 1)
    kap_row, abs_row = blank, blank
    for region in range(kap_table.shape[0]):
        kap_row = jnp.where(lane == region, kap_table[region], kap_row)
        abs_row = jnp.where(lane == region, abs_table[region], abs_row)

    def look_up(i, carry):
        at = labels[i].astype(jnp.int32)
        kap[i + 1] = jnp.take_along_axis(kap_row, at, axis=1)
        diag[i] = jnp.take_along_axis(abs_row, at, axis=1)
        return carry

    lax.fori_loop(0, planes, look_up, 0, unroll=4)
    fx[0] = 0.5 * kap[1]
    base = HALO * y

    def set_up(i, carry):
        k = kap[i + 1]
        along_x = 0.5 * (k + kap[i + 2])
        along_y, along_z = 0.5 * (k + beyond(k, 1, 0)), 0.5 * (k + beyond(k, 1, 1))
        fx[i + 1] = along_x
        fy[i] = jnp.where(index_along(k.shape, 0) == rows - 1, 0.0, along_y)
        fz[i] = jnp.where(lane == lanes - 1, 0.0, along_z)
        back_y, back_z = 0.5 * (k + beyond(k, -1, 0)), 0.5 * (k + beyond(k, -1, 1))
        diag[i] = diag[i] + fx[i] + along_x + along_y + back_y + along_z + back_z
        total, square = carry
        for p, at in ((mine[i], c), (got[0, i], 1 - c)):
            part = count[i, pl.ds(base + cy * at, cy), :] * p
            total, square = total + folded(part), square + folded(part * p)
        return total, square

    zero = jnp.zeros((8, lanes), jnp.float32)
    sums[0], sums[1] = lax.fori_loop(0, planes, set_up, (zero, zero), unroll=4)


def first_kernel(
    diag, fx, fy, fz, count, sums, mine, got_photon, vector, got_vector, photon_edge, edge,
    phi, change, message,
    vk, va, b, buf_a, buf_b,
):
    _, _, y, c = places(2)
    planes, rows, lanes = change.shape
    cy = mine.shape[1]
    framed(phi, 1, mine, got_photon.at[0], photon_edge.at[0], y, c)
    framed(vk, 1, vector.at[0], got_vector.at[0], edge.at[0], y, c)
    framed(va, 0, vector.at[1], got_vector.at[1], edge.at[1], y, c)
    blank_ends(phi, vk, buf_a, buf_b)
    theta, _ = chebyshev_scalars()

    def set_up(i, carry):
        v, p = vk[i + 1], phi[i + 1]
        total = 0.5 * (v + vk[i]) * (p - phi[i]) + 0.5 * (v + vk[i + 2]) * (p - phi[i + 2])
        for axis in range(2):
            flow = 0.5 * (v + beyond(v, 1, axis)) * (p - beyond(p, 1, axis))
            first = index_along(v.shape, axis) == 0
            total = total + flow + jnp.where(first, 0.5 * v * p, -shifted(flow, 1, axis))
        total = -(va[i] * p + total)
        b[i] = total
        buf_a[i + 1] = total * (1.0 / theta)
        return carry

    lax.fori_loop(0, planes, set_up, 0, unroll=4)
    found = solve(b, (buf_a, buf_b), diag, fx, fy, fz, 16)
    owned = owned_rows((rows, lanes), HALO * y, 2 * cy)

    def add_up(i, carry):
        u = found[i + 1]
        change[i] = u
        part = jnp.where(owned, count[i], 0.0) * u
        return carry[0] + folded(part), carry[1] + folded(part * phi[i + 1])

    zero = jnp.zeros((8, lanes), jnp.float32)
    seen, cross = lax.fori_loop(0, planes, add_up, (zero, zero), unroll=4)
    first = (2 * cy - HALO) * (1 - y) + HALO * y
    for g, part in enumerate((sums[0], seen, cross, sums[1])):
        message[g, pl.ds(0, GROUP * REACH), :] = packed_edges(
            [near_rows(found, 1 + GROUP * g + j, first, y) for j in range(GROUP)]
        )
        message[g, pl.ds(GROUP * REACH, 8), :] = part


def second_kernel(
    phi, change, diag, fx, fy, fz, count, sent, came,
    own, message,
    b, buf_a, buf_b, grad_k, grad_a,
    *, dets,
):
    _, _, y, c = places(2)
    planes, rows, lanes = change.shape
    cy = (rows - HALO) // 2
    base = HALO * y
    edge = pl.ds(2 * cy * (1 - y), HALO)
    tail = pl.ds(GROUP * REACH, 8)
    total, seen_sum, cross, square = (
        jnp.sum(jnp.sum(sent[g, tail, :] + came[g, tail, :], axis=0, keepdims=True), axis=1, keepdims=True)
        for g in range(4)
    )
    mean = total / dets
    part = seen_sum / total
    level = (cross - part * square) / (total * mean)
    inverse = 1.0 / mean
    blank_ends(buf_a, buf_b)
    theta, _ = chebyshev_scalars()

    def weighted(n, u, p):
        return n * (((u - p * part) * inverse - level) * inverse)

    def set_up(i, carry):
        value = weighted(count[i], change[i], phi[i + 1])
        b[i] = value
        buf_a[i + 1] = value * (1.0 / theta)
        return carry

    lax.fori_loop(0, planes, set_up, 0, unroll=4)
    for i in range(planes):
        u = edge_tile(came[i // GROUP], i % GROUP, y)
        value = weighted(count[i, edge, :], u, phi[i + 1, edge, :])
        b[i, edge, :] = value
        buf_a[i + 1, edge, :] = value * (1.0 / theta)
    dual = solve(b, (buf_a, buf_b), diag, fx, fy, fz, 16)

    def product(i, carry):
        p, u = phi[i + 1], dual[i + 1]
        grad = (p - phi[i]) * (u - dual[i]) + (p - phi[i + 2]) * (u - dual[i + 2])
        both = p * u
        for axis in range(2):
            flow = (p - beyond(p, 1, axis)) * (u - beyond(u, 1, axis))
            first = index_along(p.shape, axis) == 0
            grad = grad + flow + jnp.where(first, both, shifted(flow, 1, axis))
        grad_k[i] = -0.5 * grad
        grad_a[i] = -both
        for f, ref in enumerate((grad_k, grad_a)):
            own[f, i] = ref[i, pl.ds(base + cy * c, cy), :]
            message[f, i] = ref[i, pl.ds(base + cy * (1 - c), cy), :]
        return carry

    lax.fori_loop(0, planes, product, 0, unroll=4)


def packed_slabs(own, came, half, choices, outs):
    s, _, _, _ = places(2)
    _, planes, cy, lanes = own.shape
    n = planes // 2 // outs.shape[2]
    slab = lanes // n
    lane = index_along((cy, lanes), 1) // slab
    for f in range(2):
        for q in range(outs.shape[2]):
            at = planes // 2 * half + n * q
            parts = [own[f, at + j] + came[f, at + j] for j in range(n)]
            for i, k in enumerate(choices):
                to = s ^ k
                piece = jnp.zeros((cy, lanes), jnp.float32)
                for j in range(n):
                    moved = pltpu.roll(parts[j], ((j - to + n) % n) * slab, 1)
                    piece = jnp.where(lane == j, moved, piece)
                outs[i, f, q] = piece


def send_kernel(own, came, out, *, k):
    _, x, _, _ = places(2)
    packed_slabs(own, came, 1 - x, (k,), out)


def keep_kernel(own, came, kept):
    _, x, _, _ = places(2)
    packed_slabs(own, came, x, range(kept.shape[0]), kept)


def add_kernel(kept, came, out, *, k):
    out[...] = kept[k] + came[0]


def sum_kernel(*refs):
    total = refs[0][...]
    for ref in refs[1:-1]:
        total = total + ref[...]
    refs[-1][...] = total


def project_kernel(*refs, parts_n, n):
    beta_prev = refs[0]
    parts = refs[1 : 1 + parts_n]
    vk, va, qk, qa, w_k, w_a, tile = refs[1 + parts_n :]
    s, x, y, c = places(2)
    slab = 128 // n
    for f, (q_ref, w) in enumerate(((qk, w_k), (qa, w_a))):
        for q in range(vk.shape[0] // n):
            whole = sum(part[f, q] for part in parts[1:]) + parts[0][f, q]
            for j in range(n):
                i = n * q + j
                w[i] = whole[:, slab * j : slab * (j + 1)] - beta_prev[:, : vk.shape[2]] * q_ref[i]

    def dot(a, b):
        return jnp.sum(jnp.sum(a * b, axis=0))

    wk, wa, v_k, v_a = w_k[...], w_a[...], vk[...], va[...]
    one = jnp.ones((1, 1), jnp.float32)
    wv = (dot(wk, v_k) + dot(wa, v_a)) * one
    vv = (dot(v_k, v_k) + dot(v_a, v_a)) * one
    a = jnp.where(vv > 0.0, wv / jnp.where(vv > 0.0, vv, 1.0), 0.0)
    u_k, u_a = wk - a * v_k, wa - a * v_a
    uv = (dot(u_k, v_k) + dot(u_a, v_a)) * one
    uu = (dot(u_k, u_k) + dot(u_a, u_a)) * one
    me = ((s * 2 + x) * 2 + y) * 2 + c
    lane = index_along((8, 128), 1)
    row = index_along((8, 128), 0)
    values = jnp.zeros((8, 128), jnp.float32)
    for i, value in enumerate((wv, vv, a, uv, uu)):
        values = jnp.where(row == i, value, values)
    tile[...] = jnp.where(lane == me, values, 0.0)


def final_kernel(tiles, w_k, w_a, vk, va, next_k, next_a, coefs, *, cells):
    tile = jnp.sum(tiles[...], axis=0)
    wv, vv, a, uv, uu = (tile[i : i + 1] for i in range(5))
    wv_sum = jnp.sum(wv, axis=1, keepdims=True)
    vv_sum = jnp.sum(vv, axis=1, keepdims=True)
    alpha = wv_sum / cells / (vv_sum / cells + eps_norm)
    off = alpha - a
    rr = jnp.sum(uu - 2.0 * off * uv + off * off * vv, axis=1, keepdims=True)
    beta = jnp.sqrt(rr / cells + eps_norm)
    next_k[...] = (w_k[...] - alpha * vk[...]) / beta
    next_a[...] = (w_a[...] - alpha * va[...]) / beta
    coefs[0] = jnp.sum(alpha)
    coefs[1] = jnp.sum(beta)


def f32(*shape):
    return jax.ShapeDtypeStruct(shape, jnp.float32)


def run(kernel, outs, *args, after=(), scratch=(), copies=0, smem=(), hbm=(), mib=16, in_smem_out=(), cost=None):
    vmem = pl.BlockSpec(memory_space=pltpu.VMEM)
    scalar = pl.BlockSpec(memory_space=pltpu.SMEM)
    far = pl.BlockSpec(memory_space=pltpu.HBM)
    held = [pltpu.VMEM(shape, dtype) for shape, dtype in scratch]
    used, waits = len(args), len(after)

    def body(*refs):
        kernel(*refs[:used], *refs[used + waits :])

    args = (*args, *after)
    if copies:
        held.append(pltpu.SemaphoreType.DMA((copies,)))
    return pl.pallas_call(
        body if waits else kernel,
        out_shape=tuple(outs),
        in_specs=[scalar if i in smem else far if i in hbm else vmem for i in range(len(args))],
        out_specs=tuple(scalar if i in in_smem_out else vmem for i in range(len(outs))),
        scratch_shapes=held,
        compiler_params=pltpu.CompilerParams(vmem_limit_bytes=mib * 2**20),
        cost_estimate=cost,
    )(*args)


HALO = 8
REACH = 6
GROUP = 4


def per_device_paired(
    labels, kappa_table, absorb_table, background, det_cells,
    v_kappa, v_absorb, q_kappa, q_absorb, beta_prev,
):
    sources, cx, cy, cz = background.shape
    n = lax.axis_size("src")
    planes, rows = 2 * cx, 2 * cy + HALO
    ny = cy * lax.axis_size("gy")
    dets = det_cells.shape[0]
    cells = planes * ny * cz
    groups = cx // n

    def swap_x(value):
        return lax.ppermute(value, "gx", [(0, 1), (1, 0)])

    def swap_core(value):
        return lax.ppermute(value, "gy", [(0, 1), (1, 0), (2, 3), (3, 2)])

    def along_z(value, k):
        return lax.ppermute(value, "src", [(i, i ^ k) for i in range(n)])

    block = (cx, cy, cz)
    float_block = lambda *shape: (shape, jnp.float32)
    raw_labels = (block, jnp.int32)
    packed, message = run(
        pack_kernel, (f32(2 * groups, cy, cz), f32((sources // 2 + 1) * cx + 2 * groups, cy, cz)),
        background, labels, v_kappa, v_absorb, hbm=(0, 1, 2, 3),
        scratch=(raw_labels, float_block(2, *v_kappa.shape)), copies=3 + sources // 2, mib=60,
    )
    long = pl.CostEstimate(flops=10**9, bytes_accessed=2**26, transcendentals=0)
    came = swap_x(message)
    slabs = [along_z(packed, k) for k in range(1, n)]
    count, beta_row = run(
        functools.partial(count_kernel, ny=ny, nz=cz, half=2 * cy, halo=HALO),
        (f32(planes, rows, cz), f32(1, cz)), det_cells.reshape(1, dets), beta_prev, smem=(1,),
        cost=pl.CostEstimate(flops=2 * planes * rows * cz * dets, bytes_accessed=planes * rows * cz * 4, transcendentals=0),
    )

    def across_y(value):
        return lax.ppermute(value, "gy", [(i, (i + 2) % 4) for i in range(4)])

    (joined,) = run(join_kernel, (f32(2 * groups * (n - 1), cy, cz),), *slabs, after=(count,))
    joined_came = swap_x(joined)
    (half_vector,) = run(own_half_kernel, (f32(2, *block),), v_kappa, v_absorb, joined)
    mine, fields = run(
        photon_kernel, (f32(planes, cy, cz), f32(2, planes, cy, cz)),
        background, labels, came, after=(joined,), hbm=(0, 1), scratch=(raw_labels,), copies=3,
    )
    got = swap_core(fields)
    (vector,) = run(
        vector_kernel, (f32(2, planes, cy, cz),), half_vector, came, joined_came, after=(mine,)
    )
    edge = (f32(2, *edge_shape(planes, cz)),)
    (sent,) = run(photon_edge_kernel, edge, mine, fields, got, after=(vector,))
    photon_edge = across_y(sent)
    vector_got = swap_core(vector)
    (vector_sent,) = run(vector_edge_kernel, edge, vector, vector_got, after=(sent,))
    frame, wide = (planes, rows, cz), (planes + 2, rows, cz)
    float_frame, float_wide = float_block(*frame), float_block(*wide)
    diag, fx, fy, fz, sums = run(
        stencil_kernel,
        (f32(*frame), f32(planes + 1, rows, cz), f32(*frame), f32(*frame), f32(2, 8, cz)),
        kappa_table, absorb_table, mine, fields, got, photon_edge, count, after=(vector_sent,), cost=long,
        smem=(0, 1), scratch=(float_frame, float_wide),
    )
    phi, change, sent = run(
        first_kernel, (f32(*wide), f32(*frame), f32(4, GROUP * REACH + 8, cz)),
        diag, fx, fy, fz, count, sums, mine, got, vector, vector_got,
        photon_edge, across_y(vector_sent),
        scratch=(float_wide, float_frame, float_frame, float_wide, float_wide),
    )
    heard = across_y(sent)
    own, message = run(
        functools.partial(second_kernel, dets=dets),
        (f32(2, planes, cy, cz), f32(2, planes, cy, cz)),
        phi, change, diag, fx, fy, fz, count, sent, heard,
        scratch=(float_frame, float_wide, float_wide, float_frame, float_frame),
    )
    piece = f32(2, groups, cy, cz)
    got = swap_core(message)
    crossed, last = {}, ()
    for k in reversed(range(n)):
        last = run(functools.partial(send_kernel, k=k), (f32(1, *piece.shape),), own, got, after=last)
        crossed[k] = swap_x(last[0])
    (kept,) = run(keep_kernel, (f32(n, *piece.shape),), own, got, after=last)
    totals = {
        k: run(functools.partial(add_kernel, k=k), (piece,), kept, value)[0] for k, value in crossed.items()
    }
    received = {k: along_z(totals[k], k) for k in reversed(range(1, n))}
    (distant,) = run(sum_kernel, (piece,), *(received[k] for k in range(n // 2, n)), cost=long)
    parts = [distant, totals[0]] + [received[k] for k in range(1, n // 2)]
    w_k, w_a, tile = run(
        functools.partial(project_kernel, parts_n=len(parts), n=n),
        (f32(*v_kappa.shape), f32(*v_kappa.shape), f32(8, 128)),
        beta_row, *parts, v_kappa, v_absorb, q_kappa, q_absorb,
    )
    everyone = ("src", "gx", "gy")
    tiles = lax.all_to_all(jnp.broadcast_to(tile, (8 * n, 8, 128)), everyone, 0, 0)
    return tuple(run(
        functools.partial(final_kernel, cells=cells),
        (f32(*v_kappa.shape), f32(*v_kappa.shape), f32(2)),
        tiles, w_k, w_a, v_kappa, v_absorb, in_smem_out=(2,),
    ))


def paired_fits(mesh):
    return mesh.shape["gx"] == 2 and mesh.shape["gy"] == 4


def body_for(mesh):
    if not paired_fits(mesh):
        return per_device

    def chosen(*args):
        sources, cx, cy, cz = args[3].shape
        n = lax.axis_size("src")
        fits = sources == 4 and cz == 128 and cx % n == 0 and cx % GROUP == 0 and cy % HALO == 0 and n > 1 and n & (n - 1) == 0
        devices = 8 * n
        return (per_device_paired if fits and devices <= 128 else per_device)(*args)

    return chosen


def solution(mesh):
    return jax.shard_map(
        body_for(mesh),
        mesh=mesh,
        in_specs=(
            P("gx", "gy", None),
            P(),
            P(),
            P("src", "gx", "gy", None),
            P(),
            P("gx", "gy", "src"),
            P("gx", "gy", "src"),
            P("gx", "gy", "src"),
            P("gx", "gy", "src"),
            P(),
        ),
        out_specs=(P("gx", "gy", "src"), P("gx", "gy", "src"), P()),
        check_vma=False,
    )
```

```python
import functools

import jax
import jax.numpy as jnp
from jax import lax
from jax.experimental import pallas as pl
from jax.experimental.pallas import tpu as pltpu
from jax.sharding import PartitionSpec as P

ITERS = 6


lam_low = 0.02
lam_high = 24.1
eps_norm = 1e-06


def padded_2(block, sides, width):
    for axis, dim in sides:
        count = lax.axis_size(axis)
        forward = [(i, i + 1) for i in range(count - 1)]
        backward = [(target, source) for source, target in forward]
        low = lax.ppermute(
            lax.slice_in_dim(block, block.shape[dim] - width, None, axis=dim), axis, forward
        )
        high = lax.ppermute(lax.slice_in_dim(block, 0, width, axis=dim), axis, backward)
        block = jnp.concatenate([low, block, high], axis=dim)
    return block


def regional(labels, table):
    field = jnp.zeros(labels.shape, jnp.float32)
    for region in range(table.shape[0]):
        field = field + jnp.where(labels == region, table[region], 0.0)
    return field


def beside(padded):
    widths = [(0, 0)] * (padded.ndim - 1) + [(1, 1)]
    full = jnp.pad(padded, widths)
    return [
        full[..., 2:, 1:-1, 1:-1],
        full[..., :-2, 1:-1, 1:-1],
        full[..., 1:-1, 2:, 1:-1],
        full[..., 1:-1, :-2, 1:-1],
        full[..., 1:-1, 1:-1, 2:],
        full[..., 1:-1, 1:-1, :-2],
    ]


def chebyshev(rhs, apply_op):
    theta = 0.5 * (lam_high + lam_low)
    delta = 0.5 * (lam_high - lam_low)
    sigma = theta / delta
    rho = 1.0 / sigma
    solution = jnp.zeros_like(rhs)
    remain = rhs
    step_dir = rhs / theta
    for step in range(ITERS):
        solution = solution + step_dir
        if step + 1 < ITERS:
            remain = remain - apply_op(step_dir)
            rho_next = 1.0 / (2.0 * sigma - rho)
            step_dir = rho_next * rho * step_dir + 2.0 * rho_next / delta * remain
            rho = rho_next
    return solution


def per_device(
    labels,
    kappa_table,
    absorb_table,
    background,
    det_cells,
    v_kappa,
    v_absorb,
    q_kappa,
    q_absorb,
    beta_prev,
):
    sources, cx, cy, cz = background.shape
    kappa = regional(labels, kappa_table)
    absorb = regional(labels, absorb_table)
    full_k, full_a = (
        lax.all_gather(v_kappa, "src", axis=2, tiled=True),
        lax.all_gather(v_absorb, "src", axis=2, tiled=True),
    )
    stacked = jnp.concatenate([background, kappa[None], full_k[None]], axis=0)
    rims = padded_2(stacked, (("gx", 1), ("gy", 2)), 1)
    near_all = beside(rims)
    kappa_faces = [0.5 * (kappa + near[sources]) for near in near_all]
    vk_faces = [0.5 * (full_k + near[sources + 1]) for near in near_all]
    phi_near = [near[:sources] for near in near_all]

    def apply_op(field):
        padded = padded_2(field, (("gx", 1), ("gy", 2)), 1)
        result = absorb * field
        for face, near in zip(kappa_faces, beside(padded)):
            result = result + face * (field - near)
        return result

    rhs = full_a * background
    for face, near in zip(vk_faces, phi_near):
        rhs = rhs + face * (background - near)
    rhs = -rhs
    change = chebyshev(rhs, apply_op)
    span_y = cy * lax.axis_size("gy")
    ix = det_cells // (span_y * cz)
    iy = det_cells // cz % span_y
    iz = det_cells % cz
    anchor_x = lax.axis_index("gx") * cx
    anchor_y = lax.axis_index("gy") * cy
    owned = (ix >= anchor_x) & (ix < anchor_x + cx) & (iy >= anchor_y) & (iy < anchor_y + cy)
    local = jnp.where(owned, ((ix - anchor_x) * cy + (iy - anchor_y)) * cz + iz, 0)
    seen_part = jnp.where(owned[None, :], change.reshape(sources, -1)[:, local], 0.0)
    base_part = jnp.where(owned[None, :], background.reshape(sources, -1)[:, local], 0.0)
    seen, base = lax.psum((seen_part, base_part), ("gx", "gy"))
    total = jnp.sum(base, axis=1, keepdims=True)
    mean_base = total / det_cells.shape[0]
    ratio = base / total
    jv_vals = (seen - ratio * jnp.sum(seen, axis=1, keepdims=True)) / mean_base
    weight = (jv_vals - jnp.sum(ratio * jv_vals, axis=1, keepdims=True)) / mean_base
    deposit = jnp.where(owned[None, :], weight, 0.0)
    source = (
        jnp.zeros((sources, cx * cy * cz), jnp.float32)
        .at[:, local]
        .add(deposit)
        .reshape(change.shape)
    )
    dual = chebyshev(source, apply_op)
    dual_rims = padded_2(dual, (("gx", 1), ("gy", 2)), 1)
    grad_a = -jnp.sum(background * dual, axis=0)
    grad_k = jnp.zeros_like(kappa)
    for near_phi, near_dual in zip(phi_near, beside(dual_rims)):
        grad_k = grad_k - 0.5 * jnp.sum((background - near_phi) * (dual - near_dual), axis=0)
    summed_k, summed_a = lax.psum((grad_k, grad_a), "src")
    slab = v_kappa.shape[2]
    offset = lax.axis_index("src") * slab
    hv_k = lax.dynamic_slice_in_dim(summed_k, offset, slab, 2)
    hv_a = lax.dynamic_slice_in_dim(summed_a, offset, slab, 2)
    cell_count = cx * lax.axis_size("gx") * cy * lax.axis_size("gy") * cz
    w_k = hv_k - beta_prev[0] * q_kappa
    w_a = hv_a - beta_prev[0] * q_absorb
    local_wv = jnp.sum(w_k * v_kappa) + jnp.sum(w_a * v_absorb)
    local_vv = jnp.sum(v_kappa * v_kappa) + jnp.sum(v_absorb * v_absorb)
    wv_sum, vv_sum = lax.psum((local_wv, local_vv), ("src", "gx", "gy"))
    alpha = wv_sum / cell_count / (vv_sum / cell_count + eps_norm)
    r_k = w_k - alpha * v_kappa
    r_a = w_a - alpha * v_absorb
    rr_sum = lax.psum(jnp.sum(r_k * r_k) + jnp.sum(r_a * r_a), ("src", "gx", "gy"))
    beta = jnp.sqrt(rr_sum / cell_count + eps_norm)
    return (r_k / beta, r_a / beta, jnp.stack([alpha, beta]))


def chebyshev_scalars():
    theta = 0.5 * (lam_high + lam_low)
    delta = 0.5 * (lam_high - lam_low)
    sigma = theta / delta
    rho = 1.0 / sigma
    pairs = []
    for _ in range(ITERS - 1):
        rho_next = 1.0 / (2.0 * sigma - rho)
        pairs.append((rho_next * rho, 2.0 * rho_next / delta))
        rho = rho_next
    return theta, pairs


def places(split):
    g = lax.axis_index("gy")
    return lax.axis_index("src"), lax.axis_index("gx"), g // split, g % split


def shifted(value, step, axis):
    return pltpu.roll(value, step % value.shape[axis], axis)


def index_along(shape, axis):
    return lax.broadcasted_iota(jnp.int32, shape, axis)


def beyond(value, step, axis):
    size = value.shape[axis]
    at = index_along(value.shape, axis)
    edge = size - 1 if step == 1 else 0
    return jnp.where(at == edge, 0.0, shifted(value, -step, axis))


def packed_planes(ref, q):
    per = 128 // ref.shape[2]
    return jnp.concatenate([ref[per * q + j] for j in range(per)], axis=1)


def pack_kernel(bg, labels, vk, va, packed, message, raw, v_in, slabs, floats, sems):
    _, x, _, _ = places(2)
    half = bg.shape[0] // 2
    cx = labels.shape[0]
    size = slabs.shape[0]

    def copy(i, src, dst):
        started = pltpu.make_async_copy(src, dst, sems.at[i])
        started.start()
        return started

    arrive = [copy(i, src, dst) for i, (src, dst) in enumerate(((vk, v_in.at[0]), (va, v_in.at[1]), (labels, raw)))]
    leave = [
        copy(3 + i, bg.at[half * (1 - x) + i], message.at[pl.ds(cx * i, cx)]) for i in range(half)
    ]
    for f in range(2):
        arrive[f].wait()
        for q in range(size // 2):
            slabs[size // 2 * f + q] = packed_planes(v_in.at[f], q)
    leave.append(copy(3 + half, slabs, packed))
    leave.append(copy(4 + half, slabs, message.at[pl.ds(cx * (half + 1), size)]))
    arrive[2].wait()
    floats[...] = raw[...].astype(jnp.float32)
    leave.append(copy(5 + half, floats, message.at[pl.ds(cx * half, cx)]))
    for left in leave:
        left.wait()


def count_kernel(dets, beta_prev, count, beta_row, *, ny, nz, half, halo):
    beta_row[...] = jnp.full(beta_row.shape, beta_prev[0])
    _, _, y, _ = places(2)
    planes, rows, _ = count.shape
    flat = dets[...]
    iz = flat % nz
    line = flat // nz
    iy = line % ny
    ix = line // ny
    row = iy - (half - halo) * y
    spot = jnp.where((row >= 0) & (row < rows), ix * rows + row, -1)
    dets_n = flat.shape[1]
    at_z = (index_along((nz, dets_n), 0) == iz).astype(jnp.float32).astype(jnp.bfloat16)

    def body(i, carry):
        here = index_along((2 * rows, dets_n), 0) + i * (2 * rows)
        hot = (here == spot).astype(jnp.float32).astype(jnp.bfloat16)
        found = lax.dot_general(hot, at_z, (((1,), (1,)), ((), ())), preferred_element_type=jnp.float32)
        count[pl.ds(2 * i, 2)] = found.reshape(2, rows, nz)
        return carry

    lax.fori_loop(0, planes // 2, body, 0)


def photon_kernel(bg, labels, msg, mine, fields, raw, sems):
    _, x, _, c = places(2)
    half = bg.shape[0] // 2
    cx = labels.shape[0]
    here, there = cx * x, cx * (1 - x)
    copies = [
        pltpu.make_async_copy(src, dst, sems.at[i])
        for i, (src, dst) in enumerate((
            (bg.at[half * x + c], mine.at[pl.ds(here, cx)]),
            (bg.at[half * x + 1 - c], fields.at[0, pl.ds(here, cx)]),
            (labels, raw),
        ))
    ]
    for copy in copies:
        copy.start()
    mine[pl.ds(there, cx)] = msg[pl.ds(cx * c, cx)]
    fields[0, pl.ds(there, cx)] = msg[pl.ds(cx * (1 - c), cx)]
    fields[1, pl.ds(there, cx)] = msg[pl.ds(cx * half, cx)]
    for copy in copies:
        copy.wait()
    fields[1, pl.ds(here, cx)] = raw[...].astype(jnp.float32)


def unpacked(blocks, groups, s, store):
    n = len(blocks)
    cy, lanes = blocks[0][0].shape
    slab = lanes // n
    lane = index_along((cy, lanes), 1) // slab
    for f in range(2):
        for q in range(groups):
            values = [block[groups * f + q] for block in blocks]
            for j in range(n):
                plane = jnp.zeros((cy, lanes), jnp.float32)
                for k in range(n):
                    home = s ^ k
                    moved = pltpu.roll(values[k], ((home - j + n) % n) * slab, 1)
                    plane = jnp.where(lane == home, moved, plane)
                store(f, n * q + j, plane)


def join_kernel(*refs):
    joined, size = refs[-1], refs[0].shape[0]
    for i, ref in enumerate(refs[:-1]):
        joined[pl.ds(size * i, size)] = ref[...]


def own_half_kernel(vk, va, joined, half):
    s, _, _, _ = places(2)
    size = half.shape[1]
    groups = joined.shape[0] // 2 // (128 // vk.shape[2] - 1)
    n = size // groups
    own = [packed_planes(ref, q) for ref in (vk, va) for q in range(groups)]
    blocks = [own] + [[joined[2 * groups * k + i] for i in range(2 * groups)] for k in range(n - 1)]

    def store(f, i, plane):
        half[f, i] = plane

    unpacked(blocks, groups, s, store)


def vector_kernel(half, msg, joined, fields):
    s, x, _, _ = places(2)
    cx = half.shape[1]
    fields[:, pl.ds(cx * x, cx)] = half[...]
    n = lax.axis_size("src")
    groups = cx // n
    own = msg.shape[0] - 2 * groups
    blocks = [[msg[own + i] for i in range(2 * groups)]]
    blocks += [[joined[2 * groups * k + i] for i in range(2 * groups)] for k in range(n - 1)]
    there = cx * (1 - x)

    def store(f, i, plane):
        fields[f, there + i] = plane

    unpacked(blocks, groups, s, store)


def edge_shape(planes, lanes):
    return planes // GROUP, GROUP * REACH, lanes


def packed_edges(tiles):
    return jnp.concatenate([tile[:REACH] for tile in tiles], axis=0)


def edge_tile(packed, j, y):
    rows = packed[REACH * j : REACH * (j + 1)]
    tile = jnp.concatenate([rows, jnp.zeros((HALO - REACH, rows.shape[1]), jnp.float32)], axis=0)
    return jnp.where(y == 0, tile, shifted(tile, HALO - REACH, 0))


def near_rows(ref, i, first, y):
    tile = ref[i, pl.ds(first, HALO), :]
    return jnp.where(y == 0, shifted(tile, REACH - HALO, 0), tile)


def edges_of(own, got, edge, y, c):
    first = (own.shape[1] - HALO) * (1 - y)
    for g in range(edge.shape[0]):
        edge[g] = packed_edges([
            jnp.where(c != y, near_rows(own, GROUP * g + j, first, y), near_rows(got, GROUP * g + j, first, y))
            for j in range(GROUP)
        ])


def photon_edge_kernel(mine, fields, got, edge):
    _, _, y, c = places(2)
    edges_of(mine, got.at[0], edge.at[0], y, c)
    edges_of(fields.at[1], got.at[1], edge.at[1], y, c)


def vector_edge_kernel(fields, got, edge):
    _, _, y, c = places(2)
    for f in range(2):
        edges_of(fields.at[f], got.at[f], edge.at[f], y, c)


def solve(b, bufs, diag, fx, fy, fz, unroll):
    planes = b.shape[0]
    _, pairs = chebyshev_scalars()
    for step, (keep, push) in enumerate(pairs):
        src, dst = bufs[step % 2], bufs[(step + 1) % 2]

        def body(i, carry):
            u = src[i + 1]
            coef_y, coef_z = fy[i], fz[i]
            left = b[i] - diag[i] * u
            left = left + fx[i] * src[i] + fx[i + 1] * src[i + 2]
            left = left + coef_y * shifted(u, -1, 0) + shifted(coef_y * u, 1, 0)
            left = left + coef_z * shifted(u, -1, 1) + shifted(coef_z * u, 1, 1)
            change = u if step == 0 else u - dst[i + 1]
            dst[i + 1] = u + keep * change + push * left
            return carry

        lax.fori_loop(0, planes, body, 0, unroll=unroll)
    return bufs[len(pairs) % 2]


def folded(value):
    return jnp.sum(value.reshape(-1, 8, value.shape[1]), axis=0)


def framed_own(ref, shift, own, got, y, c):
    planes, cy, _ = own.shape
    there = pl.ds(shift, planes)
    base = HALO * y
    ref[there, pl.ds(base + cy * c, cy), :] = own[...]
    ref[there, pl.ds(base + cy * (1 - c), cy), :] = got[...]


def framed(ref, shift, own, got, edge, y, c):
    framed_own(ref, shift, own, got, y, c)
    cy = own.shape[1]
    for g in range(edge.shape[0]):
        packed = edge[g]
        for j in range(GROUP):
            ref[shift + GROUP * g + j, pl.ds(2 * cy * (1 - y), HALO), :] = edge_tile(packed, j, y)


def blank_ends(*refs):
    for ref in refs:
        blank = jnp.zeros(ref.shape[1:], jnp.float32)
        ref[0] = blank
        ref[ref.shape[0] - 1] = blank


def owned_rows(shape, base, count):
    at_row = index_along(shape, 0)
    return (at_row >= base) & (at_row < base + count)


def table_rows(kap_table, abs_table, shape):
    lane = index_along(shape, 1)
    kap_row = abs_row = jnp.zeros(shape, jnp.float32)
    for region in range(kap_table.shape[0]):
        kap_row = jnp.where(lane == region, kap_table[region], kap_row)
        abs_row = jnp.where(lane == region, abs_table[region], abs_row)
    return kap_row, abs_row


def stencil_kernel(
    kap_table, abs_table, mine, fields, got, count,
    kap, diag, fx, fy, fz, sums,
    labels,
):
    _, _, y, c = places(2)
    planes, cy, lanes = mine.shape
    rows = 2 * cy + HALO
    base = HALO * y
    framed_own(labels, 0, fields.at[1], got.at[1], y, c)
    labels[:, pl.ds(2 * cy * (1 - y), HALO), :] = jnp.zeros((planes, HALO, lanes), jnp.float32)
    blank_ends(kap)
    shape = (rows, lanes)
    lane = index_along(shape, 1)
    kap_row, abs_row = table_rows(kap_table, abs_table, shape)
    owned = owned_rows(shape, base, 2 * cy)

    def look_up(i, carry):
        at = labels[i].astype(jnp.int32)
        kap[i + 1] = jnp.where(owned, jnp.take_along_axis(kap_row, at, axis=1), 0.0)
        diag[i] = jnp.take_along_axis(abs_row, at, axis=1)
        return carry

    lax.fori_loop(0, planes, look_up, 0, unroll=UNROLL)
    fx[0] = 0.5 * kap[1]

    def set_up(i, carry):
        k = kap[i + 1]
        along_x = 0.5 * (k + kap[i + 2])
        along_y, along_z = 0.5 * (k + beyond(k, 1, 0)), 0.5 * (k + beyond(k, 1, 1))
        fx[i + 1] = along_x
        fy[i] = jnp.where(index_along(shape, 0) == rows - 1, 0.0, along_y)
        fz[i] = jnp.where(lane == lanes - 1, 0.0, along_z)
        back_y, back_z = 0.5 * (k + beyond(k, -1, 0)), 0.5 * (k + beyond(k, -1, 1))
        diag[i] = diag[i] + fx[i] + along_x + along_y + back_y + along_z + back_z
        total, square = carry
        for p, at in ((mine[i], c), (got[0, i], 1 - c)):
            part = count[i, pl.ds(base + cy * at, cy), :] * p
            total, square = total + folded(part), square + folded(part * p)
        return total, square

    zero = jnp.zeros((8, lanes), jnp.float32)
    sums[0], sums[1] = lax.fori_loop(0, planes, set_up, (zero, zero), unroll=UNROLL)


def halo_kernel(kap_table, abs_table, edge, kap, diag_in, fx_in, fy_in, fz_in, diag, fx, fy, fz):
    _, _, y, _ = places(2)
    planes, rows, lanes = diag.shape
    for ref, old in ((diag, diag_in), (fx, fx_in), (fy, fy_in), (fz, fz_in)):
        ref[...] = old[...]
    shape = (HALO, lanes)
    lane, row = index_along(shape, 1), index_along(shape, 0)
    kap_row, abs_row = table_rows(kap_table, abs_table, shape)
    low = y == 0
    here = pl.ds((rows - HALO) * (1 - y), HALO)
    beside_it = pl.ds((rows - 2 * HALO) * (1 - y) + HALO * y, HALO)
    labels = [edge_tile(edge[1, i // GROUP], i % GROUP, y).astype(jnp.int32) for i in range(planes)]
    tiles = [jnp.take_along_axis(kap_row, at, axis=1) for at in labels]
    none = jnp.zeros(shape, jnp.float32)
    before = 0.5 * tiles[0]
    fx[0, here, :] = before
    for i, k in enumerate(tiles):
        after = 0.5 * (k + (tiles[i + 1] if i + 1 < planes else none))
        own = kap[i + 1, beside_it, :]
        up, down = shifted(k, -1, 0), shifted(k, 1, 0)
        k_up = jnp.where(row == HALO - 1, jnp.where(low, 0.0, shifted(own, -1, 0)), up)
        k_down = jnp.where(row == 0, jnp.where(low, shifted(own, 1, 0), 0.0), down)
        along_y, back_y = 0.5 * (k + k_up), 0.5 * (k + k_down)
        along_z, back_z = 0.5 * (k + beyond(k, 1, 1)), 0.5 * (k + beyond(k, -1, 1))
        fx[i + 1, here, :] = after
        fy[i, here, :] = jnp.where(low & (row == HALO - 1), 0.0, along_y)
        fz[i, here, :] = jnp.where(lane == lanes - 1, 0.0, along_z)
        absorb = jnp.take_along_axis(abs_row, labels[i], axis=1)
        diag[i, here, :] = absorb + before + after + along_y + back_y + along_z + back_z
        before = after
        face_up = jnp.where(low & (row == HALO - 1), 0.5 * up, 0.0)
        face_down = jnp.where(low | (row > 0), 0.0, 0.5 * down)
        fy[i, beside_it, :] = fy_in[i, beside_it, :] + face_up
        diag[i, beside_it, :] = diag_in[i, beside_it, :] + face_up + face_down


def first_kernel(
    diag, fx, fy, fz, count, sums, mine, got_photon, vector, got_vector, photon_edge, edge,
    phi, change, message,
    vk, va, b, buf_a, buf_b,
):
    _, _, y, c = places(2)
    planes, rows, lanes = change.shape
    cy = mine.shape[1]
    framed(phi, 1, mine, got_photon.at[0], photon_edge.at[0], y, c)
    framed(vk, 1, vector.at[0], got_vector.at[0], edge.at[0], y, c)
    framed(va, 0, vector.at[1], got_vector.at[1], edge.at[1], y, c)
    blank_ends(phi, vk, buf_a, buf_b)
    theta, _ = chebyshev_scalars()

    def set_up(i, carry):
        v, p = vk[i + 1], phi[i + 1]
        total = 0.5 * (v + vk[i]) * (p - phi[i]) + 0.5 * (v + vk[i + 2]) * (p - phi[i + 2])
        for axis in range(2):
            flow = 0.5 * (v + beyond(v, 1, axis)) * (p - beyond(p, 1, axis))
            first = index_along(v.shape, axis) == 0
            total = total + flow + jnp.where(first, 0.5 * v * p, -shifted(flow, 1, axis))
        total = -(va[i] * p + total)
        b[i] = total
        buf_a[i + 1] = total * (1.0 / theta)
        return carry

    lax.fori_loop(0, planes, set_up, 0, unroll=UNROLL)
    found = solve(b, (buf_a, buf_b), diag, fx, fy, fz, UNROLL)
    owned = owned_rows((rows, lanes), HALO * y, 2 * cy)

    def add_up(i, carry):
        u = found[i + 1]
        change[i] = u
        part = jnp.where(owned, count[i], 0.0) * u
        return carry[0] + folded(part), carry[1] + folded(part * phi[i + 1])

    zero = jnp.zeros((8, lanes), jnp.float32)
    seen, cross = lax.fori_loop(0, planes, add_up, (zero, zero), unroll=UNROLL)
    first = (2 * cy - HALO) * (1 - y) + HALO * y
    for g, part in enumerate((sums[0], seen, cross, sums[1])):
        message[g, pl.ds(0, GROUP * REACH), :] = packed_edges(
            [near_rows(found, 1 + GROUP * g + j, first, y) for j in range(GROUP)]
        )
        message[g, pl.ds(GROUP * REACH, 8), :] = part


def second_kernel(
    phi, change, diag, fx, fy, fz, count, sent, came,
    own, message,
    b, buf_a, buf_b, grad_k, grad_a,
    *, dets,
):
    _, _, y, c = places(2)
    planes, rows, lanes = change.shape
    cy = (rows - HALO) // 2
    base = HALO * y
    edge = pl.ds(2 * cy * (1 - y), HALO)
    tail = pl.ds(GROUP * REACH, 8)
    total, seen_sum, cross, square = (
        jnp.sum(jnp.sum(sent[g, tail, :] + came[g, tail, :], axis=0, keepdims=True), axis=1, keepdims=True)
        for g in range(4)
    )
    mean = total / dets
    part = seen_sum / total
    level = (cross - part * square) / (total * mean)
    inverse = 1.0 / mean
    blank_ends(buf_a, buf_b)
    theta, _ = chebyshev_scalars()

    def weighted(n, u, p):
        return n * (((u - p * part) * inverse - level) * inverse)

    def set_up(i, carry):
        value = weighted(count[i], change[i], phi[i + 1])
        b[i] = value
        buf_a[i + 1] = value * (1.0 / theta)
        return carry

    lax.fori_loop(0, planes, set_up, 0, unroll=UNROLL)
    for i in range(planes):
        u = edge_tile(came[i // GROUP], i % GROUP, y)
        value = weighted(count[i, edge, :], u, phi[i + 1, edge, :])
        b[i, edge, :] = value
        buf_a[i + 1, edge, :] = value * (1.0 / theta)
    dual = solve(b, (buf_a, buf_b), diag, fx, fy, fz, UNROLL)

    def product(i, carry):
        p, u = phi[i + 1], dual[i + 1]
        grad = (p - phi[i]) * (u - dual[i]) + (p - phi[i + 2]) * (u - dual[i + 2])
        both = p * u
        for axis in range(2):
            flow = (p - beyond(p, 1, axis)) * (u - beyond(u, 1, axis))
            first = index_along(p.shape, axis) == 0
            grad = grad + flow + jnp.where(first, both, shifted(flow, 1, axis))
        grad_k[i] = -0.5 * grad
        grad_a[i] = -both
        for f, ref in enumerate((grad_k, grad_a)):
            own[f, i] = ref[i, pl.ds(base + cy * c, cy), :]
            message[f, i] = ref[i, pl.ds(base + cy * (1 - c), cy), :]
        return carry

    lax.fori_loop(0, planes, product, 0, unroll=UNROLL)


def packed_slabs(own, came, half, choices, outs):
    s, _, _, _ = places(2)
    _, planes, cy, lanes = own.shape
    n = planes // 2 // outs.shape[2]
    slab = lanes // n
    lane = index_along((cy, lanes), 1) // slab
    for f in range(2):
        for q in range(outs.shape[2]):
            at = planes // 2 * half + n * q
            parts = [own[f, at + j] + came[f, at + j] for j in range(n)]
            for i, k in enumerate(choices):
                to = s ^ k
                piece = jnp.zeros((cy, lanes), jnp.float32)
                for j in range(n):
                    moved = pltpu.roll(parts[j], ((j - to + n) % n) * slab, 1)
                    piece = jnp.where(lane == j, moved, piece)
                outs[i, f, q] = piece


def send_kernel(own, came, out, *, k):
    _, x, _, _ = places(2)
    packed_slabs(own, came, 1 - x, (k,), out)


def keep_kernel(own, came, kept):
    _, x, _, _ = places(2)
    packed_slabs(own, came, x, range(kept.shape[0]), kept)


def add_kernel(kept, came, out, *, k):
    out[...] = kept[k] + came[0]


def sum_kernel(*refs):
    total = refs[0][...]
    for ref in refs[1:-1]:
        total = total + ref[...]
    refs[-1][...] = total


def project_kernel(*refs, parts_n, n):
    beta_prev = refs[0]
    parts = refs[1 : 1 + parts_n]
    vk, va, qk, qa, w_k, w_a, tile = refs[1 + parts_n :]
    s, x, y, c = places(2)
    slab = 128 // n
    for f, (q_ref, w) in enumerate(((qk, w_k), (qa, w_a))):
        for q in range(vk.shape[0] // n):
            whole = sum(part[f, q] for part in parts[1:]) + parts[0][f, q]
            for j in range(n):
                i = n * q + j
                w[i] = whole[:, slab * j : slab * (j + 1)] - beta_prev[:, : vk.shape[2]] * q_ref[i]

    def dot(a, b):
        return jnp.sum(jnp.sum(a * b, axis=0))

    wk, wa, v_k, v_a = w_k[...], w_a[...], vk[...], va[...]
    one = jnp.ones((1, 1), jnp.float32)
    wv = (dot(wk, v_k) + dot(wa, v_a)) * one
    vv = (dot(v_k, v_k) + dot(v_a, v_a)) * one
    a = jnp.where(vv > 0.0, wv / jnp.where(vv > 0.0, vv, 1.0), 0.0)
    u_k, u_a = wk - a * v_k, wa - a * v_a
    uv = (dot(u_k, v_k) + dot(u_a, v_a)) * one
    uu = (dot(u_k, u_k) + dot(u_a, u_a)) * one
    me = ((s * 2 + x) * 2 + y) * 2 + c
    lane = index_along((8, 128), 1)
    row = index_along((8, 128), 0)
    values = jnp.zeros((8, 128), jnp.float32)
    for i, value in enumerate((wv, vv, a, uv, uu)):
        values = jnp.where(row == i, value, values)
    tile[...] = jnp.where(lane == me, values, 0.0)


def final_kernel(tiles, w_k, w_a, vk, va, next_k, next_a, coefs, *, cells):
    tile = jnp.sum(tiles[...], axis=0)
    wv, vv, a, uv, uu = (tile[i : i + 1] for i in range(5))
    wv_sum = jnp.sum(wv, axis=1, keepdims=True)
    vv_sum = jnp.sum(vv, axis=1, keepdims=True)
    alpha = wv_sum / cells / (vv_sum / cells + eps_norm)
    off = alpha - a
    rr = jnp.sum(uu - 2.0 * off * uv + off * off * vv, axis=1, keepdims=True)
    beta = jnp.sqrt(rr / cells + eps_norm)
    next_k[...] = (w_k[...] - alpha * vk[...]) / beta
    next_a[...] = (w_a[...] - alpha * va[...]) / beta
    coefs[0] = jnp.sum(alpha)
    coefs[1] = jnp.sum(beta)


def f32(*shape):
    return jax.ShapeDtypeStruct(shape, jnp.float32)


def run(kernel, outs, *args, after=(), scratch=(), copies=0, smem=(), hbm=(), mib=16, in_smem_out=(), hbm_out=False, cost=None):
    vmem = pl.BlockSpec(memory_space=pltpu.VMEM)
    scalar = pl.BlockSpec(memory_space=pltpu.SMEM)
    far = pl.BlockSpec(memory_space=pltpu.HBM)
    held = [pltpu.VMEM(shape, dtype) for shape, dtype in scratch]
    used, waits = len(args), len(after)

    def body(*refs):
        kernel(*refs[:used], *refs[used + waits :])

    args = (*args, *after)
    if copies:
        held.append(pltpu.SemaphoreType.DMA((copies,)))
    return pl.pallas_call(
        body if waits else kernel,
        out_shape=tuple(outs),
        in_specs=[scalar if i in smem else far if i in hbm else vmem for i in range(len(args))],
        out_specs=tuple(scalar if i in in_smem_out else far if hbm_out else vmem for i in range(len(outs))),
        scratch_shapes=held,
        compiler_params=pltpu.CompilerParams(vmem_limit_bytes=mib * 2**20),
        cost_estimate=cost,
    )(*args)


HALO = 8
UNROLL = 16
REACH = 6
GROUP = 4


def per_device_paired(
    labels, kappa_table, absorb_table, background, det_cells,
    v_kappa, v_absorb, q_kappa, q_absorb, beta_prev,
):
    sources, cx, cy, cz = background.shape
    n = lax.axis_size("src")
    planes, rows = 2 * cx, 2 * cy + HALO
    ny = cy * lax.axis_size("gy")
    dets = det_cells.shape[0]
    cells = planes * ny * cz
    groups = cx // n

    def swap_x(value):
        return lax.ppermute(value, "gx", [(0, 1), (1, 0)])

    def swap_core(value):
        return lax.ppermute(value, "gy", [(0, 1), (1, 0), (2, 3), (3, 2)])

    def along_z(value, k):
        return lax.ppermute(value, "src", [(i, i ^ k) for i in range(n)])

    block = (cx, cy, cz)
    float_block = lambda *shape: (shape, jnp.float32)
    raw_labels = (block, jnp.int32)
    packed, message = run(
        pack_kernel, (f32(2 * groups, cy, cz), f32((sources // 2 + 1) * cx + 2 * groups, cy, cz)),
        background, labels, v_kappa, v_absorb, hbm=(0, 1, 2, 3),
        scratch=(raw_labels, float_block(2, *v_kappa.shape), float_block(2 * groups, cy, cz), float_block(*block)),
        copies=6 + sources // 2, hbm_out=True, mib=60,
    )
    long = pl.CostEstimate(flops=10**9, bytes_accessed=2**26, transcendentals=0)
    came = swap_x(message)
    slabs = [along_z(packed, k) for k in range(1, n)]
    count, beta_row = run(
        functools.partial(count_kernel, ny=ny, nz=cz, half=2 * cy, halo=HALO),
        (f32(planes, rows, cz), f32(1, cz)), det_cells.reshape(1, dets), beta_prev, smem=(1,),
        cost=pl.CostEstimate(flops=2 * planes * rows * cz * dets, bytes_accessed=planes * rows * cz * 4, transcendentals=0),
    )

    def across_y(value):
        return lax.ppermute(value, "gy", [(i, (i + 2) % 4) for i in range(4)])

    (joined,) = run(join_kernel, (f32(2 * groups * (n - 1), cy, cz),), *slabs, after=(count,))
    joined_came = swap_x(joined)
    (half_vector,) = run(own_half_kernel, (f32(2, *block),), v_kappa, v_absorb, joined)
    mine, fields = run(
        photon_kernel, (f32(planes, cy, cz), f32(2, planes, cy, cz)),
        background, labels, came, after=(joined,), hbm=(0, 1), scratch=(raw_labels,), copies=3,
    )
    got = swap_core(fields)
    (vector,) = run(
        vector_kernel, (f32(2, planes, cy, cz),), half_vector, came, joined_came, after=(mine,)
    )
    edge = (f32(2, *edge_shape(planes, cz)),)
    (sent,) = run(photon_edge_kernel, edge, mine, fields, got, after=(vector,))
    photon_edge = across_y(sent)
    vector_got = swap_core(vector)
    (vector_sent,) = run(vector_edge_kernel, edge, vector, vector_got, after=(sent,))
    frame, wide = (planes, rows, cz), (planes + 2, rows, cz)
    float_frame, float_wide = float_block(*frame), float_block(*wide)
    coefs = (f32(*frame), f32(planes + 1, rows, cz), f32(*frame), f32(*frame))
    kap, *partial, sums = run(
        stencil_kernel, (f32(*wide), *coefs, f32(2, 8, cz)),
        kappa_table, absorb_table, mine, fields, got, count, after=(vector_sent,), cost=long,
        smem=(0, 1), scratch=(float_frame,),
    )
    diag, fx, fy, fz = run(
        halo_kernel, coefs, kappa_table, absorb_table, photon_edge, kap, *partial, smem=(0, 1)
    )
    phi, change, sent = run(
        first_kernel, (f32(*wide), f32(*frame), f32(4, GROUP * REACH + 8, cz)),
        diag, fx, fy, fz, count, sums, mine, got, vector, vector_got,
        photon_edge, across_y(vector_sent),
        scratch=(float_wide, float_frame, float_frame, float_wide, float_wide),
    )
    heard = across_y(sent)
    own, message = run(
        functools.partial(second_kernel, dets=dets),
        (f32(2, planes, cy, cz), f32(2, planes, cy, cz)),
        phi, change, diag, fx, fy, fz, count, sent, heard,
        scratch=(float_frame, float_wide, float_wide, float_frame, float_frame),
    )
    piece = f32(2, groups, cy, cz)
    got = swap_core(message)
    crossed, last = {}, ()
    for k in reversed(range(n)):
        last = run(functools.partial(send_kernel, k=k), (f32(1, *piece.shape),), own, got, after=last)
        crossed[k] = swap_x(last[0])
    (kept,) = run(keep_kernel, (f32(n, *piece.shape),), own, got, after=last)
    totals = {
        k: run(functools.partial(add_kernel, k=k), (piece,), kept, value)[0] for k, value in crossed.items()
    }
    received = {k: along_z(totals[k], k) for k in reversed(range(1, n))}
    (distant,) = run(sum_kernel, (piece,), *(received[k] for k in range(n // 2, n)), cost=long)
    parts = [distant, totals[0]] + [received[k] for k in range(1, n // 2)]
    w_k, w_a, tile = run(
        functools.partial(project_kernel, parts_n=len(parts), n=n),
        (f32(*v_kappa.shape), f32(*v_kappa.shape), f32(8, 128)),
        beta_row, *parts, v_kappa, v_absorb, q_kappa, q_absorb,
    )
    everyone = ("src", "gx", "gy")
    tiles = lax.all_to_all(jnp.broadcast_to(tile, (8 * n, 8, 128)), everyone, 0, 0)
    return tuple(run(
        functools.partial(final_kernel, cells=cells),
        (f32(*v_kappa.shape), f32(*v_kappa.shape), f32(2)),
        tiles, w_k, w_a, v_kappa, v_absorb, in_smem_out=(2,),
    ))


def paired_fits(mesh):
    return mesh.shape["gx"] == 2 and mesh.shape["gy"] == 4


def body_for(mesh):
    if not paired_fits(mesh):
        return per_device

    def chosen(*args):
        sources, cx, cy, cz = args[3].shape
        n = lax.axis_size("src")
        fits = sources == 4 and cz == 128 and cx % n == 0 and cx % GROUP == 0 and cy % HALO == 0 and n > 1 and n & (n - 1) == 0
        devices = 8 * n
        return (per_device_paired if fits and devices <= 128 else per_device)(*args)

    return chosen


def solution(mesh):
    return jax.shard_map(
        body_for(mesh),
        mesh=mesh,
        in_specs=(
            P("gx", "gy", None),
            P(),
            P(),
            P("src", "gx", "gy", None),
            P(),
            P("gx", "gy", "src"),
            P("gx", "gy", "src"),
            P("gx", "gy", "src"),
            P("gx", "gy", "src"),
            P(),
        ),
        out_specs=(P("gx", "gy", "src"), P("gx", "gy", "src"), P()),
        check_vma=False,
    )
```

```python
import functools

import jax
import jax.numpy as jnp
from jax import lax
from jax.experimental import pallas as pl
from jax.experimental.pallas import tpu as pltpu
from jax.sharding import PartitionSpec as P

ITERS = 6


lam_low = 0.02
lam_high = 24.1
eps_norm = 1e-06


def padded_2(block, sides, width):
    for axis, dim in sides:
        count = lax.axis_size(axis)
        forward = [(i, i + 1) for i in range(count - 1)]
        backward = [(target, source) for source, target in forward]
        low = lax.ppermute(
            lax.slice_in_dim(block, block.shape[dim] - width, None, axis=dim), axis, forward
        )
        high = lax.ppermute(lax.slice_in_dim(block, 0, width, axis=dim), axis, backward)
        block = jnp.concatenate([low, block, high], axis=dim)
    return block


def regional(labels, table):
    field = jnp.zeros(labels.shape, jnp.float32)
    for region in range(table.shape[0]):
        field = field + jnp.where(labels == region, table[region], 0.0)
    return field


def beside(padded):
    widths = [(0, 0)] * (padded.ndim - 1) + [(1, 1)]
    full = jnp.pad(padded, widths)
    return [
        full[..., 2:, 1:-1, 1:-1],
        full[..., :-2, 1:-1, 1:-1],
        full[..., 1:-1, 2:, 1:-1],
        full[..., 1:-1, :-2, 1:-1],
        full[..., 1:-1, 1:-1, 2:],
        full[..., 1:-1, 1:-1, :-2],
    ]


def chebyshev(rhs, apply_op):
    theta = 0.5 * (lam_high + lam_low)
    delta = 0.5 * (lam_high - lam_low)
    sigma = theta / delta
    rho = 1.0 / sigma
    solution = jnp.zeros_like(rhs)
    remain = rhs
    step_dir = rhs / theta
    for step in range(ITERS):
        solution = solution + step_dir
        if step + 1 < ITERS:
            remain = remain - apply_op(step_dir)
            rho_next = 1.0 / (2.0 * sigma - rho)
            step_dir = rho_next * rho * step_dir + 2.0 * rho_next / delta * remain
            rho = rho_next
    return solution


def per_device(
    labels,
    kappa_table,
    absorb_table,
    background,
    det_cells,
    v_kappa,
    v_absorb,
    q_kappa,
    q_absorb,
    beta_prev,
):
    sources, cx, cy, cz = background.shape
    kappa = regional(labels, kappa_table)
    absorb = regional(labels, absorb_table)
    full_k, full_a = (
        lax.all_gather(v_kappa, "src", axis=2, tiled=True),
        lax.all_gather(v_absorb, "src", axis=2, tiled=True),
    )
    stacked = jnp.concatenate([background, kappa[None], full_k[None]], axis=0)
    rims = padded_2(stacked, (("gx", 1), ("gy", 2)), 1)
    near_all = beside(rims)
    kappa_faces = [0.5 * (kappa + near[sources]) for near in near_all]
    vk_faces = [0.5 * (full_k + near[sources + 1]) for near in near_all]
    phi_near = [near[:sources] for near in near_all]

    def apply_op(field):
        padded = padded_2(field, (("gx", 1), ("gy", 2)), 1)
        result = absorb * field
        for face, near in zip(kappa_faces, beside(padded)):
            result = result + face * (field - near)
        return result

    rhs = full_a * background
    for face, near in zip(vk_faces, phi_near):
        rhs = rhs + face * (background - near)
    rhs = -rhs
    change = chebyshev(rhs, apply_op)
    span_y = cy * lax.axis_size("gy")
    ix = det_cells // (span_y * cz)
    iy = det_cells // cz % span_y
    iz = det_cells % cz
    anchor_x = lax.axis_index("gx") * cx
    anchor_y = lax.axis_index("gy") * cy
    owned = (ix >= anchor_x) & (ix < anchor_x + cx) & (iy >= anchor_y) & (iy < anchor_y + cy)
    local = jnp.where(owned, ((ix - anchor_x) * cy + (iy - anchor_y)) * cz + iz, 0)
    seen_part = jnp.where(owned[None, :], change.reshape(sources, -1)[:, local], 0.0)
    base_part = jnp.where(owned[None, :], background.reshape(sources, -1)[:, local], 0.0)
    seen, base = lax.psum((seen_part, base_part), ("gx", "gy"))
    total = jnp.sum(base, axis=1, keepdims=True)
    mean_base = total / det_cells.shape[0]
    ratio = base / total
    jv_vals = (seen - ratio * jnp.sum(seen, axis=1, keepdims=True)) / mean_base
    weight = (jv_vals - jnp.sum(ratio * jv_vals, axis=1, keepdims=True)) / mean_base
    deposit = jnp.where(owned[None, :], weight, 0.0)
    source = (
        jnp.zeros((sources, cx * cy * cz), jnp.float32)
        .at[:, local]
        .add(deposit)
        .reshape(change.shape)
    )
    dual = chebyshev(source, apply_op)
    dual_rims = padded_2(dual, (("gx", 1), ("gy", 2)), 1)
    grad_a = -jnp.sum(background * dual, axis=0)
    grad_k = jnp.zeros_like(kappa)
    for near_phi, near_dual in zip(phi_near, beside(dual_rims)):
        grad_k = grad_k - 0.5 * jnp.sum((background - near_phi) * (dual - near_dual), axis=0)
    summed_k, summed_a = lax.psum((grad_k, grad_a), "src")
    slab = v_kappa.shape[2]
    offset = lax.axis_index("src") * slab
    hv_k = lax.dynamic_slice_in_dim(summed_k, offset, slab, 2)
    hv_a = lax.dynamic_slice_in_dim(summed_a, offset, slab, 2)
    cell_count = cx * lax.axis_size("gx") * cy * lax.axis_size("gy") * cz
    w_k = hv_k - beta_prev[0] * q_kappa
    w_a = hv_a - beta_prev[0] * q_absorb
    local_wv = jnp.sum(w_k * v_kappa) + jnp.sum(w_a * v_absorb)
    local_vv = jnp.sum(v_kappa * v_kappa) + jnp.sum(v_absorb * v_absorb)
    wv_sum, vv_sum = lax.psum((local_wv, local_vv), ("src", "gx", "gy"))
    alpha = wv_sum / cell_count / (vv_sum / cell_count + eps_norm)
    r_k = w_k - alpha * v_kappa
    r_a = w_a - alpha * v_absorb
    rr_sum = lax.psum(jnp.sum(r_k * r_k) + jnp.sum(r_a * r_a), ("src", "gx", "gy"))
    beta = jnp.sqrt(rr_sum / cell_count + eps_norm)
    return (r_k / beta, r_a / beta, jnp.stack([alpha, beta]))


def chebyshev_scalars():
    theta = 0.5 * (lam_high + lam_low)
    delta = 0.5 * (lam_high - lam_low)
    sigma = theta / delta
    rho = 1.0 / sigma
    pairs = []
    for _ in range(ITERS - 1):
        rho_next = 1.0 / (2.0 * sigma - rho)
        pairs.append((rho_next * rho, 2.0 * rho_next / delta))
        rho = rho_next
    return theta, pairs


def places(split):
    g = lax.axis_index("gy")
    return lax.axis_index("src"), lax.axis_index("gx"), g // split, g % split


def shifted(value, step, axis):
    return pltpu.roll(value, step % value.shape[axis], axis)


def index_along(shape, axis):
    return lax.broadcasted_iota(jnp.int32, shape, axis)


def beyond(value, step, axis):
    size = value.shape[axis]
    at = index_along(value.shape, axis)
    edge = size - 1 if step == 1 else 0
    return jnp.where(at == edge, 0.0, shifted(value, -step, axis))


def packed_planes(ref, q):
    per = 128 // ref.shape[2]
    return jnp.concatenate([ref[per * q + j] for j in range(per)], axis=1)


def pack_kernel(bg, labels, vk, va, packed, message, raw, v_in, sems):
    _, x, _, _ = places(2)
    half = bg.shape[0] // 2
    cx = labels.shape[0]
    copies = [
        pltpu.make_async_copy(src, dst, sems.at[i])
        for i, (src, dst) in enumerate((
            (vk, v_in.at[0]),
            (va, v_in.at[1]),
            (labels, raw),
            *((bg.at[half * (1 - x) + i], message.at[pl.ds(cx * i, cx)]) for i in range(half)),
        ))
    ]
    for copy in copies:
        copy.start()
    groups = packed.shape[0] // 2
    for f in range(2):
        copies[f].wait()
        for q in range(groups):
            planes = packed_planes(v_in.at[f], q)
            packed[groups * f + q] = planes
            message[cx * (half + 1) + groups * f + q] = planes
    copies[2].wait()
    message[pl.ds(cx * half, cx)] = raw[...].astype(jnp.float32)
    for copy in copies[3:]:
        copy.wait()


def count_kernel(dets, beta_prev, count, beta_row, *, ny, nz, half, halo):
    beta_row[...] = jnp.full(beta_row.shape, beta_prev[0])
    _, _, y, _ = places(2)
    planes, rows, _ = count.shape
    flat = dets[...]
    iz = flat % nz
    line = flat // nz
    iy = line % ny
    ix = line // ny
    row = iy - (half - halo) * y
    spot = jnp.where((row >= 0) & (row < rows), ix * rows + row, -1)
    dets_n = flat.shape[1]
    at_z = (index_along((nz, dets_n), 0) == iz).astype(jnp.float32).astype(jnp.bfloat16)

    def body(i, carry):
        here = index_along((2 * rows, dets_n), 0) + i * (2 * rows)
        hot = (here == spot).astype(jnp.float32).astype(jnp.bfloat16)
        found = lax.dot_general(hot, at_z, (((1,), (1,)), ((), ())), preferred_element_type=jnp.float32)
        count[pl.ds(2 * i, 2)] = found.reshape(2, rows, nz)
        return carry

    lax.fori_loop(0, planes // 2, body, 0)


def photon_kernel(bg, labels, msg, mine, fields, raw, sems):
    _, x, _, c = places(2)
    half = bg.shape[0] // 2
    cx = labels.shape[0]
    here, there = cx * x, cx * (1 - x)
    copies = [
        pltpu.make_async_copy(src, dst, sems.at[i])
        for i, (src, dst) in enumerate((
            (bg.at[half * x + c], mine.at[pl.ds(here, cx)]),
            (bg.at[half * x + 1 - c], fields.at[0, pl.ds(here, cx)]),
            (labels, raw),
        ))
    ]
    for copy in copies:
        copy.start()
    mine[pl.ds(there, cx)] = msg[pl.ds(cx * c, cx)]
    fields[0, pl.ds(there, cx)] = msg[pl.ds(cx * (1 - c), cx)]
    fields[1, pl.ds(there, cx)] = msg[pl.ds(cx * half, cx)]
    for copy in copies:
        copy.wait()
    fields[1, pl.ds(here, cx)] = raw[...].astype(jnp.float32)


def unpacked(blocks, groups, s, store):
    n = len(blocks)
    cy, lanes = blocks[0][0].shape
    slab = lanes // n
    lane = index_along((cy, lanes), 1) // slab
    for f in range(2):
        for q in range(groups):
            values = [block[groups * f + q] for block in blocks]
            for j in range(n):
                plane = jnp.zeros((cy, lanes), jnp.float32)
                for k in range(n):
                    home = s ^ k
                    moved = pltpu.roll(values[k], ((home - j + n) % n) * slab, 1)
                    plane = jnp.where(lane == home, moved, plane)
                store(f, n * q + j, plane)


def join_kernel(*refs):
    joined, size = refs[-1], refs[0].shape[0]
    for i, ref in enumerate(refs[:-1]):
        joined[pl.ds(size * i, size)] = ref[...]


def own_half_kernel(vk, va, joined, bg, labels, half, straight, across):
    s, _, y, _ = places(2)
    size = half.shape[1]
    groups = joined.shape[0] // 2 // (128 // vk.shape[2] - 1)
    n = size // groups
    own = [packed_planes(ref, q) for ref in (vk, va) for q in range(groups)]
    blocks = [own] + [[joined[2 * groups * k + i] for i in range(2 * groups)] for k in range(n - 1)]

    def store(f, i, plane):
        half[f, i] = plane

    unpacked(blocks, groups, s, store)
    first = straight.shape[0] - 2
    photon_edges(bg, labels, straight, across)
    for f in range(2):
        for g in range(straight.shape[1]):
            edge = packed_edges([near_rows(half.at[f], GROUP * g + j, y) for j in range(GROUP)])
            straight[first + f, g] = across[first + f, g] = edge


def vector_kernel(half, msg, joined, straight, across, fields, mine_edge):
    s, x, _, c = places(2)
    _, cx, cy, _ = half.shape
    n = lax.axis_size("src")
    groups = cx // n
    own = msg.shape[0] - 2 * groups
    blocks = [[msg[own + i] for i in range(2 * groups)]]
    blocks += [[joined[2 * groups * k + i] for i in range(2 * groups)] for k in range(n - 1)]
    here, there = cx * x, cx * (1 - x)
    edge_groups = straight.shape[1]
    labels = straight.shape[0] - 3

    def store(f, i, plane):
        fields[f, plane_rows(there + i, cy), :] = plane

    for f in range(2):
        for i in range(cx):
            fields[f, plane_rows(here + i, cy), :] = half[f, i]
    for g in range(edge_groups):
        for part, at in ((straight, edge_groups * x + g), (across, edge_groups * (1 - x) + g)):
            mine_edge[at] = part[c, g]
            for f, second in ((0, 1 - c), (1, labels)):
                fields[f, edge_rows(2 * cx, cy, 0, at), :] = part[labels + 1 + f, g]
                fields[f, edge_rows(2 * cx, cy, 1, at), :] = part[second, g]
    unpacked(blocks, groups, s, store)


def edge_rows(planes, cy, which, g):
    return pl.ds(pl.multiple_of(planes * (cy + REACH * which) + GROUP * REACH * g, 8), GROUP * REACH)


def plane_rows(i, cy):
    return pl.ds(pl.multiple_of(cy * i, 8), cy)


def message_rows(planes, cy):
    return planes * (cy + 2 * REACH)


def packed_edges(tiles):
    return jnp.concatenate([tile[:REACH] for tile in tiles], axis=0)


def edge_tile(packed, j, y):
    rows = packed[REACH * j : REACH * (j + 1)]
    tile = jnp.concatenate([rows, jnp.zeros((HALO - REACH, rows.shape[1]), jnp.float32)], axis=0)
    return jnp.where(y == 0, tile, shifted(tile, HALO - REACH, 0))


def near_tile(tile, y):
    return jnp.where(y == 0, shifted(tile, REACH - HALO, 0), tile)


def near_rows(ref, i, y):
    first = (ref.shape[1] - HALO) * (1 - y)
    return near_tile(ref[i, pl.ds(pl.multiple_of(first, 8), HALO), :], y)


def photon_edges(bg, labels, straight, across):
    _, x, y, _ = places(2)
    half = bg.shape[0] // 2
    first = pl.ds(pl.multiple_of((labels.shape[1] - HALO) * (1 - y), 8), HALO)
    for g in range(straight.shape[1]):
        tiles = [near_tile(labels[GROUP * g + j, first, :].astype(jnp.float32), y) for j in range(GROUP)]
        straight[half, g] = across[half, g] = packed_edges(tiles)
        for out, at in ((straight, half * x), (across, half * (1 - x))):
            for i in range(half):
                out[i, g] = packed_edges([near_rows(bg.at[at + i], GROUP * g + j, y) for j in range(GROUP)])


def framed_own(ref, shift, planes, cy, own, got, y, c):
    base = HALO * y
    for i in range(planes):
        ref[shift + i, pl.ds(base + cy * c, cy), :] = own(i)
        ref[shift + i, pl.ds(base + cy * (1 - c), cy), :] = got(i)


def framed_edges(ref, shift, planes, own, got, y, c):
    row = (ref.shape[1] - HALO) * (1 - y)
    for g in range(planes // GROUP):
        packed = jnp.where(c != y, own(g), got(g))
        for j in range(GROUP):
            ref[shift + GROUP * g + j, pl.ds(row, HALO), :] = edge_tile(packed, j, y)


def solve(b, bufs, diag, fx, fy, fz, unroll):
    planes = b.shape[0]
    _, pairs = chebyshev_scalars()
    for step, (keep, push) in enumerate(pairs):
        src, dst = bufs[step % 2], bufs[(step + 1) % 2]

        def body(i, carry):
            u = src[i + 1]
            coef_y, coef_z = fy[i], fz[i]
            left = b[i] - diag[i] * u
            left = left + fx[i] * src[i] + fx[i + 1] * src[i + 2]
            left = left + coef_y * shifted(u, -1, 0) + shifted(coef_y * u, 1, 0)
            left = left + coef_z * shifted(u, -1, 1) + shifted(coef_z * u, 1, 1)
            change = u if step == 0 else u - dst[i + 1]
            dst[i + 1] = u + keep * change + push * left
            return carry

        lax.fori_loop(0, planes, body, 0, unroll=unroll)
    return bufs[len(pairs) % 2]


def folded(value):
    return jnp.sum(value.reshape(-1, 8, value.shape[1]), axis=0)


def blank_ends(*refs):
    for ref in refs:
        blank = jnp.zeros(ref.shape[1:], jnp.float32)
        ref[0] = blank
        ref[ref.shape[0] - 1] = blank


def owned_rows(shape, base, count):
    at_row = index_along(shape, 0)
    return (at_row >= base) & (at_row < base + count)


def table_rows(kap_table, abs_table, shape):
    lane = index_along(shape, 1)
    kap_row = abs_row = jnp.zeros(shape, jnp.float32)
    for region in range(kap_table.shape[0]):
        kap_row = jnp.where(lane == region, kap_table[region], kap_row)
        abs_row = jnp.where(lane == region, abs_table[region], abs_row)
    return kap_row, abs_row


def stencil_kernel(
    kap_table, abs_table, mine, fields, got, count,
    kap, diag, fx, fy, fz, sums,
    labels,
):
    _, _, y, c = places(2)
    planes, cy, lanes = mine.shape
    rows = 2 * cy + HALO
    base = HALO * y
    framed_own(labels, 0, planes, cy, lambda i: fields[1, i], lambda i: got[1, i], y, c)
    labels[:, pl.ds(2 * cy * (1 - y), HALO), :] = jnp.zeros((planes, HALO, lanes), jnp.float32)
    blank_ends(kap)
    shape = (rows, lanes)
    lane = index_along(shape, 1)
    kap_row, abs_row = table_rows(kap_table, abs_table, shape)
    owned = owned_rows(shape, base, 2 * cy)

    def look_up(i, carry):
        at = labels[i].astype(jnp.int32)
        kap[i + 1] = jnp.where(owned, jnp.take_along_axis(kap_row, at, axis=1), 0.0)
        diag[i] = jnp.take_along_axis(abs_row, at, axis=1)
        return carry

    lax.fori_loop(0, planes, look_up, 0, unroll=4)
    fx[0] = 0.5 * kap[1]

    def set_up(i, carry):
        k = kap[i + 1]
        along_x = 0.5 * (k + kap[i + 2])
        along_y, along_z = 0.5 * (k + beyond(k, 1, 0)), 0.5 * (k + beyond(k, 1, 1))
        fx[i + 1] = along_x
        fy[i] = jnp.where(index_along(shape, 0) == rows - 1, 0.0, along_y)
        fz[i] = jnp.where(lane == lanes - 1, 0.0, along_z)
        back_y, back_z = 0.5 * (k + beyond(k, -1, 0)), 0.5 * (k + beyond(k, -1, 1))
        diag[i] = diag[i] + fx[i] + along_x + along_y + back_y + along_z + back_z
        total, square = carry
        for p, at in ((mine[i], c), (got[0, i], 1 - c)):
            part = count[i, pl.ds(base + cy * at, cy), :] * p
            total, square = total + folded(part), square + folded(part * p)
        return total, square

    zero = jnp.zeros((8, lanes), jnp.float32)
    sums[0], sums[1] = lax.fori_loop(0, planes, set_up, (zero, zero), unroll=4)


def halo_kernel(kap_table, abs_table, vector, got_vector, kap, diag_in, fx_in, fy_in, fz_in, diag, fx, fy, fz):
    _, _, y, c = places(2)
    planes, rows, lanes = diag.shape
    cy = (rows - HALO) // 2
    edges = [
        jnp.where(c != y, *(ref[1, edge_rows(planes, cy, 1, g), :] for ref in (vector, got_vector)))
        for g in range(planes // GROUP)
    ]
    for ref, old in ((diag, diag_in), (fx, fx_in), (fy, fy_in), (fz, fz_in)):
        ref[...] = old[...]
    shape = (HALO, lanes)
    lane, row = index_along(shape, 1), index_along(shape, 0)
    kap_row, abs_row = table_rows(kap_table, abs_table, shape)
    low = y == 0
    here = pl.ds((rows - HALO) * (1 - y), HALO)
    beside_it = pl.ds((rows - 2 * HALO) * (1 - y) + HALO * y, HALO)
    labels = [edge_tile(edges[i // GROUP], i % GROUP, y).astype(jnp.int32) for i in range(planes)]
    tiles = [jnp.take_along_axis(kap_row, at, axis=1) for at in labels]
    none = jnp.zeros(shape, jnp.float32)
    before = 0.5 * tiles[0]
    fx[0, here, :] = before
    for i, k in enumerate(tiles):
        after = 0.5 * (k + (tiles[i + 1] if i + 1 < planes else none))
        own = kap[i + 1, beside_it, :]
        up, down = shifted(k, -1, 0), shifted(k, 1, 0)
        k_up = jnp.where(row == HALO - 1, jnp.where(low, 0.0, shifted(own, -1, 0)), up)
        k_down = jnp.where(row == 0, jnp.where(low, shifted(own, 1, 0), 0.0), down)
        along_y, back_y = 0.5 * (k + k_up), 0.5 * (k + k_down)
        along_z, back_z = 0.5 * (k + beyond(k, 1, 1)), 0.5 * (k + beyond(k, -1, 1))
        fx[i + 1, here, :] = after
        fy[i, here, :] = jnp.where(low & (row == HALO - 1), 0.0, along_y)
        fz[i, here, :] = jnp.where(lane == lanes - 1, 0.0, along_z)
        absorb = jnp.take_along_axis(abs_row, labels[i], axis=1)
        diag[i, here, :] = absorb + before + after + along_y + back_y + along_z + back_z
        before = after
        face_up = jnp.where(low & (row == HALO - 1), 0.5 * up, 0.0)
        face_down = jnp.where(low | (row > 0), 0.0, 0.5 * down)
        fy[i, beside_it, :] = fy_in[i, beside_it, :] + face_up
        diag[i, beside_it, :] = diag_in[i, beside_it, :] + face_up + face_down


def first_kernel(
    diag, fx, fy, fz, count, sums, mine, mine_edge, got_photon, vector, got_vector,
    phi, change, message,
    vk, va, b, buf_a, buf_b,
):
    _, _, y, c = places(2)
    planes, rows, lanes = change.shape
    cy = mine.shape[1]
    framed_own(phi, 1, planes, cy, lambda i: mine[i], lambda i: got_photon[0, i], y, c)
    second = lambda g: got_vector[0, edge_rows(planes, cy, 1, g), :]
    framed_edges(phi, 1, planes, lambda g: mine_edge[g], second, y, c)
    for ref, shift, f in ((vk, 1, 0), (va, 0, 1)):
        rows_of = lambda message: lambda i: message[f, plane_rows(i, cy), :]
        edges_of = lambda message: lambda g: message[f, edge_rows(planes, cy, 0, g), :]
        framed_own(ref, shift, planes, cy, rows_of(vector), rows_of(got_vector), y, c)
        framed_edges(ref, shift, planes, edges_of(vector), edges_of(got_vector), y, c)
    blank_ends(phi, vk, buf_a, buf_b)
    theta, _ = chebyshev_scalars()

    def set_up(i, carry):
        v, p = vk[i + 1], phi[i + 1]
        total = 0.5 * (v + vk[i]) * (p - phi[i]) + 0.5 * (v + vk[i + 2]) * (p - phi[i + 2])
        for axis in range(2):
            flow = 0.5 * (v + beyond(v, 1, axis)) * (p - beyond(p, 1, axis))
            first = index_along(v.shape, axis) == 0
            total = total + flow + jnp.where(first, 0.5 * v * p, -shifted(flow, 1, axis))
        total = -(va[i] * p + total)
        b[i] = total
        buf_a[i + 1] = total * (1.0 / theta)
        return carry

    lax.fori_loop(0, planes, set_up, 0, unroll=4)
    found = solve(b, (buf_a, buf_b), diag, fx, fy, fz, 16)
    owned = owned_rows((rows, lanes), HALO * y, 2 * cy)

    def add_up(i, carry):
        u = found[i + 1]
        change[i] = u
        part = jnp.where(owned, count[i], 0.0) * u
        return carry[0] + folded(part), carry[1] + folded(part * phi[i + 1])

    zero = jnp.zeros((8, lanes), jnp.float32)
    seen, cross = lax.fori_loop(0, planes, add_up, (zero, zero), unroll=4)
    first = (2 * cy - HALO) * (1 - y) + HALO * y
    for g, part in enumerate((sums[0], seen, cross, sums[1])):
        message[g, pl.ds(0, GROUP * REACH), :] = packed_edges(
            [near_tile(found[1 + GROUP * g + j, pl.ds(first, HALO), :], y) for j in range(GROUP)]
        )
        message[g, pl.ds(GROUP * REACH, 8), :] = part


def second_kernel(
    phi, change, diag, fx, fy, fz, count, sent, came,
    own, message,
    b, buf_a, buf_b, grad_k, grad_a,
    *, dets,
):
    _, _, y, c = places(2)
    planes, rows, lanes = change.shape
    cy = (rows - HALO) // 2
    base = HALO * y
    edge = pl.ds(2 * cy * (1 - y), HALO)
    tail = pl.ds(GROUP * REACH, 8)
    total, seen_sum, cross, square = (
        jnp.sum(jnp.sum(sent[g, tail, :] + came[g, tail, :], axis=0, keepdims=True), axis=1, keepdims=True)
        for g in range(4)
    )
    mean = total / dets
    part = seen_sum / total
    level = (cross - part * square) / (total * mean)
    inverse = 1.0 / mean
    blank_ends(buf_a, buf_b)
    theta, _ = chebyshev_scalars()

    def weighted(n, u, p):
        return n * (((u - p * part) * inverse - level) * inverse)

    def set_up(i, carry):
        value = weighted(count[i], change[i], phi[i + 1])
        b[i] = value
        buf_a[i + 1] = value * (1.0 / theta)
        return carry

    lax.fori_loop(0, planes, set_up, 0, unroll=4)
    for i in range(planes):
        u = edge_tile(came[i // GROUP], i % GROUP, y)
        value = weighted(count[i, edge, :], u, phi[i + 1, edge, :])
        b[i, edge, :] = value
        buf_a[i + 1, edge, :] = value * (1.0 / theta)
    dual = solve(b, (buf_a, buf_b), diag, fx, fy, fz, 16)

    def product(i, carry):
        p, u = phi[i + 1], dual[i + 1]
        grad = (p - phi[i]) * (u - dual[i]) + (p - phi[i + 2]) * (u - dual[i + 2])
        both = p * u
        for axis in range(2):
            flow = (p - beyond(p, 1, axis)) * (u - beyond(u, 1, axis))
            first = index_along(p.shape, axis) == 0
            grad = grad + flow + jnp.where(first, both, shifted(flow, 1, axis))
        grad_k[i] = -0.5 * grad
        grad_a[i] = -both
        for f, ref in enumerate((grad_k, grad_a)):
            own[f, i] = ref[i, pl.ds(base + cy * c, cy), :]
            message[f, i] = ref[i, pl.ds(base + cy * (1 - c), cy), :]
        return carry

    lax.fori_loop(0, planes, product, 0, unroll=4)


def packed_slabs(own, came, half, choices, outs):
    s, _, _, _ = places(2)
    _, planes, cy, lanes = own.shape
    n = planes // 2 // outs.shape[2]
    slab = lanes // n
    lane = index_along((cy, lanes), 1) // slab
    for f in range(2):
        for q in range(outs.shape[2]):
            at = planes // 2 * half + n * q
            parts = [own[f, at + j] + came[f, at + j] for j in range(n)]
            for i, k in enumerate(choices):
                to = s ^ k
                piece = jnp.zeros((cy, lanes), jnp.float32)
                for j in range(n):
                    moved = pltpu.roll(parts[j], ((j - to + n) % n) * slab, 1)
                    piece = jnp.where(lane == j, moved, piece)
                outs[i, f, q] = piece


def send_kernel(own, came, out, *, k):
    _, x, _, _ = places(2)
    packed_slabs(own, came, 1 - x, (k,), out)


def keep_kernel(own, came, kept):
    _, x, _, _ = places(2)
    packed_slabs(own, came, x, range(kept.shape[0]), kept)


def add_kernel(kept, came, out, *, k):
    out[...] = kept[k] + came[0]


def sum_kernel(*refs):
    total = refs[0][...]
    for ref in refs[1:-1]:
        total = total + ref[...]
    refs[-1][...] = total


def project_kernel(*refs, parts_n, n):
    beta_prev = refs[0]
    parts = refs[1 : 1 + parts_n]
    vk, va, qk, qa, w_k, w_a, tile = refs[1 + parts_n :]
    s, x, y, c = places(2)
    slab = 128 // n
    for f, (q_ref, w) in enumerate(((qk, w_k), (qa, w_a))):
        for q in range(vk.shape[0] // n):
            whole = sum(part[f, q] for part in parts[1:]) + parts[0][f, q]
            for j in range(n):
                i = n * q + j
                w[i] = whole[:, slab * j : slab * (j + 1)] - beta_prev[:, : vk.shape[2]] * q_ref[i]

    def dot(a, b):
        return jnp.sum(jnp.sum(a * b, axis=0))

    wk, wa, v_k, v_a = w_k[...], w_a[...], vk[...], va[...]
    one = jnp.ones((1, 1), jnp.float32)
    wv = (dot(wk, v_k) + dot(wa, v_a)) * one
    vv = (dot(v_k, v_k) + dot(v_a, v_a)) * one
    a = jnp.where(vv > 0.0, wv / jnp.where(vv > 0.0, vv, 1.0), 0.0)
    u_k, u_a = wk - a * v_k, wa - a * v_a
    uv = (dot(u_k, v_k) + dot(u_a, v_a)) * one
    uu = (dot(u_k, u_k) + dot(u_a, u_a)) * one
    me = ((s * 2 + x) * 2 + y) * 2 + c
    lane = index_along((8, 128), 1)
    row = index_along((8, 128), 0)
    values = jnp.zeros((8, 128), jnp.float32)
    for i, value in enumerate((wv, vv, a, uv, uu)):
        values = jnp.where(row == i, value, values)
    tile[...] = jnp.where(lane == me, values, 0.0)


def final_kernel(tiles, w_k, w_a, vk, va, next_k, next_a, coefs, *, cells):
    tile = jnp.sum(tiles[...], axis=0)
    wv, vv, a, uv, uu = (tile[i : i + 1] for i in range(5))
    wv_sum = jnp.sum(wv, axis=1, keepdims=True)
    vv_sum = jnp.sum(vv, axis=1, keepdims=True)
    alpha = wv_sum / cells / (vv_sum / cells + eps_norm)
    off = alpha - a
    rr = jnp.sum(uu - 2.0 * off * uv + off * off * vv, axis=1, keepdims=True)
    beta = jnp.sqrt(rr / cells + eps_norm)
    next_k[...] = (w_k[...] - alpha * vk[...]) / beta
    next_a[...] = (w_a[...] - alpha * va[...]) / beta
    coefs[0] = jnp.sum(alpha)
    coefs[1] = jnp.sum(beta)


def f32(*shape):
    return jax.ShapeDtypeStruct(shape, jnp.float32)


def run(kernel, outs, *args, after=(), scratch=(), copies=0, smem=(), hbm=(), mib=16, in_smem_out=(), cost=None):
    vmem = pl.BlockSpec(memory_space=pltpu.VMEM)
    scalar = pl.BlockSpec(memory_space=pltpu.SMEM)
    far = pl.BlockSpec(memory_space=pltpu.HBM)
    held = [pltpu.VMEM(shape, dtype) for shape, dtype in scratch]
    used, waits = len(args), len(after)

    def body(*refs):
        kernel(*refs[:used], *refs[used + waits :])

    args = (*args, *after)
    if copies:
        held.append(pltpu.SemaphoreType.DMA((copies,)))
    return pl.pallas_call(
        body if waits else kernel,
        out_shape=tuple(outs),
        in_specs=[
            scalar if i in smem else far if i in hbm or i >= used else vmem for i in range(len(args))
        ],
        out_specs=tuple(scalar if i in in_smem_out else vmem for i in range(len(outs))),
        scratch_shapes=held,
        compiler_params=pltpu.CompilerParams(vmem_limit_bytes=mib * 2**20),
        cost_estimate=cost,
    )(*args)


HALO = 8
REACH = 6
GROUP = 4


def per_device_paired(
    labels, kappa_table, absorb_table, background, det_cells,
    v_kappa, v_absorb, q_kappa, q_absorb, beta_prev,
):
    sources, cx, cy, cz = background.shape
    n = lax.axis_size("src")
    planes, rows = 2 * cx, 2 * cy + HALO
    ny = cy * lax.axis_size("gy")
    dets = det_cells.shape[0]
    cells = planes * ny * cz
    groups = cx // n

    def swap_x(value):
        return lax.ppermute(value, "gx", [(0, 1), (1, 0)])

    def swap_core(value):
        return lax.ppermute(value, "gy", [(0, 1), (1, 0), (2, 3), (3, 2)])

    def along_z(value, k):
        return lax.ppermute(value, "src", [(i, i ^ k) for i in range(n)])

    block = (cx, cy, cz)
    float_block = lambda *shape: (shape, jnp.float32)
    raw_labels = (block, jnp.int32)
    packed, message = run(
        pack_kernel, (f32(2 * groups, cy, cz), f32((sources // 2 + 1) * cx + 2 * groups, cy, cz)),
        background, labels, v_kappa, v_absorb, hbm=(0, 1, 2, 3),
        scratch=(raw_labels, float_block(2, *v_kappa.shape)), copies=3 + sources // 2, mib=60,
    )
    long = pl.CostEstimate(flops=10**9, bytes_accessed=2**26, transcendentals=0)
    came = swap_x(message)
    slabs = [along_z(packed, k) for k in range(1, n)]
    def to_inner(straight, across):
        over = [(1, 6), (6, 1), (2, 5), (5, 2)]
        return lax.ppermute(straight, "gy", [(1, 2), (2, 1)]), lax.ppermute(across, ("gx", "gy"), over)

    def across_y(value):
        return lax.ppermute(value, "gy", [(i, (i + 2) % 4) for i in range(4)])

    edge = (cx // GROUP, GROUP * REACH, cz)
    count, beta_row = run(
        functools.partial(count_kernel, ny=ny, nz=cz, half=2 * cy, halo=HALO),
        (f32(planes, rows, cz), f32(1, cz)), det_cells.reshape(1, dets), beta_prev, smem=(1,),
        cost=pl.CostEstimate(flops=2 * planes * rows * cz * dets, bytes_accessed=planes * rows * cz * 4, transcendentals=0),
    )
    (joined,) = run(join_kernel, (f32(2 * groups * (n - 1), cy, cz),), *slabs, after=(count,))
    joined_came = swap_x(joined)
    half_vector, *edges = run(
        own_half_kernel, (f32(2, *block), *[f32(sources // 2 + 3, *edge)] * 2),
        v_kappa, v_absorb, joined, background, labels,
    )
    edges = to_inner(*edges)
    message = f32(2, message_rows(planes, cy), cz)
    mine, fields = run(
        photon_kernel, (f32(planes, cy, cz), f32(2, planes, cy, cz)),
        background, labels, came, after=(joined,), hbm=(0, 1), scratch=(raw_labels,), copies=3,
    )
    got = swap_core(fields)
    vector, mine_edge = run(
        vector_kernel, (message, f32(planes // GROUP, *edge[1:])), half_vector, came, joined_came, *edges, after=(mine,)
    )
    vector_got = swap_core(vector)
    frame, wide = (planes, rows, cz), (planes + 2, rows, cz)
    float_frame, float_wide = float_block(*frame), float_block(*wide)
    coefs = (f32(*frame), f32(planes + 1, rows, cz), f32(*frame), f32(*frame))
    kap, *partial, sums = run(
        stencil_kernel, (f32(*wide), *coefs, f32(2, 8, cz)),
        kappa_table, absorb_table, mine, fields, got, count, after=(vector,),
        smem=(0, 1), scratch=(float_frame,),
    )
    diag, fx, fy, fz = run(
        halo_kernel, coefs, kappa_table, absorb_table, vector, vector_got, kap, *partial, smem=(0, 1)
    )
    phi, change, sent = run(
        first_kernel, (f32(*wide), f32(*frame), f32(4, GROUP * REACH + 8, cz)),
        diag, fx, fy, fz, count, sums, mine, mine_edge, got, vector, vector_got,
        scratch=(float_wide, float_frame, float_frame, float_wide, float_wide),
    )
    heard = across_y(sent)
    own, message = run(
        functools.partial(second_kernel, dets=dets),
        (f32(2, planes, cy, cz), f32(2, planes, cy, cz)),
        phi, change, diag, fx, fy, fz, count, sent, heard,
        scratch=(float_frame, float_wide, float_wide, float_frame, float_frame),
    )
    piece = f32(2, groups, cy, cz)
    got = swap_core(message)
    crossed, last = {}, ()
    for k in reversed(range(n)):
        last = run(functools.partial(send_kernel, k=k), (f32(1, *piece.shape),), own, got, after=last)
        crossed[k] = swap_x(last[0])
    (kept,) = run(keep_kernel, (f32(n, *piece.shape),), own, got, after=last)
    totals = {
        k: run(functools.partial(add_kernel, k=k), (piece,), kept, value)[0] for k, value in crossed.items()
    }
    received = {k: along_z(totals[k], k) for k in reversed(range(1, n))}
    (distant,) = run(sum_kernel, (piece,), *(received[k] for k in range(n // 2, n)), cost=long)
    parts = [distant, totals[0]] + [received[k] for k in range(1, n // 2)]
    w_k, w_a, tile = run(
        functools.partial(project_kernel, parts_n=len(parts), n=n),
        (f32(*v_kappa.shape), f32(*v_kappa.shape), f32(8, 128)),
        beta_row, *parts, v_kappa, v_absorb, q_kappa, q_absorb,
    )
    everyone = ("src", "gx", "gy")
    tiles = lax.all_to_all(jnp.broadcast_to(tile, (8 * n, 8, 128)), everyone, 0, 0)
    return tuple(run(
        functools.partial(final_kernel, cells=cells),
        (f32(*v_kappa.shape), f32(*v_kappa.shape), f32(2)),
        tiles, w_k, w_a, v_kappa, v_absorb, in_smem_out=(2,),
    ))


def paired_fits(mesh):
    return mesh.shape["gx"] == 2 and mesh.shape["gy"] == 4


def body_for(mesh):
    if not paired_fits(mesh):
        return per_device

    def chosen(*args):
        sources, cx, cy, cz = args[3].shape
        n = lax.axis_size("src")
        fits = sources == 4 and cz == 128 and cx % n == 0 and cx % GROUP == 0 and cy % HALO == 0 and n > 1 and n & (n - 1) == 0
        devices = 8 * n
        return (per_device_paired if fits and devices <= 128 else per_device)(*args)

    return chosen


def solution(mesh):
    return jax.shard_map(
        body_for(mesh),
        mesh=mesh,
        in_specs=(
            P("gx", "gy", None),
            P(),
            P(),
            P("src", "gx", "gy", None),
            P(),
            P("gx", "gy", "src"),
            P("gx", "gy", "src"),
            P("gx", "gy", "src"),
            P("gx", "gy", "src"),
            P(),
        ),
        out_specs=(P("gx", "gy", "src"), P("gx", "gy", "src"), P()),
        check_vma=False,
    )
```

```python
import functools

import jax
import jax.numpy as jnp
from jax import lax
from jax.experimental import pallas as pl
from jax.experimental.pallas import tpu as pltpu
from jax.sharding import PartitionSpec as P

ITERS = 6


lam_low = 0.02
lam_high = 24.1
eps_norm = 1e-06


def padded_2(block, sides, width):
    for axis, dim in sides:
        count = lax.axis_size(axis)
        forward = [(i, i + 1) for i in range(count - 1)]
        backward = [(target, source) for source, target in forward]
        low = lax.ppermute(
            lax.slice_in_dim(block, block.shape[dim] - width, None, axis=dim), axis, forward
        )
        high = lax.ppermute(lax.slice_in_dim(block, 0, width, axis=dim), axis, backward)
        block = jnp.concatenate([low, block, high], axis=dim)
    return block


def regional(labels, table):
    field = jnp.zeros(labels.shape, jnp.float32)
    for region in range(table.shape[0]):
        field = field + jnp.where(labels == region, table[region], 0.0)
    return field


def beside(padded):
    widths = [(0, 0)] * (padded.ndim - 1) + [(1, 1)]
    full = jnp.pad(padded, widths)
    return [
        full[..., 2:, 1:-1, 1:-1],
        full[..., :-2, 1:-1, 1:-1],
        full[..., 1:-1, 2:, 1:-1],
        full[..., 1:-1, :-2, 1:-1],
        full[..., 1:-1, 1:-1, 2:],
        full[..., 1:-1, 1:-1, :-2],
    ]


def chebyshev(rhs, apply_op):
    theta = 0.5 * (lam_high + lam_low)
    delta = 0.5 * (lam_high - lam_low)
    sigma = theta / delta
    rho = 1.0 / sigma
    solution = jnp.zeros_like(rhs)
    remain = rhs
    step_dir = rhs / theta
    for step in range(ITERS):
        solution = solution + step_dir
        if step + 1 < ITERS:
            remain = remain - apply_op(step_dir)
            rho_next = 1.0 / (2.0 * sigma - rho)
            step_dir = rho_next * rho * step_dir + 2.0 * rho_next / delta * remain
            rho = rho_next
    return solution


def per_device(
    labels,
    kappa_table,
    absorb_table,
    background,
    det_cells,
    v_kappa,
    v_absorb,
    q_kappa,
    q_absorb,
    beta_prev,
):
    sources, cx, cy, cz = background.shape
    kappa = regional(labels, kappa_table)
    absorb = regional(labels, absorb_table)
    full_k, full_a = (
        lax.all_gather(v_kappa, "src", axis=2, tiled=True),
        lax.all_gather(v_absorb, "src", axis=2, tiled=True),
    )
    stacked = jnp.concatenate([background, kappa[None], full_k[None]], axis=0)
    rims = padded_2(stacked, (("gx", 1), ("gy", 2)), 1)
    near_all = beside(rims)
    kappa_faces = [0.5 * (kappa + near[sources]) for near in near_all]
    vk_faces = [0.5 * (full_k + near[sources + 1]) for near in near_all]
    phi_near = [near[:sources] for near in near_all]

    def apply_op(field):
        padded = padded_2(field, (("gx", 1), ("gy", 2)), 1)
        result = absorb * field
        for face, near in zip(kappa_faces, beside(padded)):
            result = result + face * (field - near)
        return result

    rhs = full_a * background
    for face, near in zip(vk_faces, phi_near):
        rhs = rhs + face * (background - near)
    rhs = -rhs
    change = chebyshev(rhs, apply_op)
    span_y = cy * lax.axis_size("gy")
    ix = det_cells // (span_y * cz)
    iy = det_cells // cz % span_y
    iz = det_cells % cz
    anchor_x = lax.axis_index("gx") * cx
    anchor_y = lax.axis_index("gy") * cy
    owned = (ix >= anchor_x) & (ix < anchor_x + cx) & (iy >= anchor_y) & (iy < anchor_y + cy)
    local = jnp.where(owned, ((ix - anchor_x) * cy + (iy - anchor_y)) * cz + iz, 0)
    seen_part = jnp.where(owned[None, :], change.reshape(sources, -1)[:, local], 0.0)
    base_part = jnp.where(owned[None, :], background.reshape(sources, -1)[:, local], 0.0)
    seen, base = lax.psum((seen_part, base_part), ("gx", "gy"))
    total = jnp.sum(base, axis=1, keepdims=True)
    mean_base = total / det_cells.shape[0]
    ratio = base / total
    jv_vals = (seen - ratio * jnp.sum(seen, axis=1, keepdims=True)) / mean_base
    weight = (jv_vals - jnp.sum(ratio * jv_vals, axis=1, keepdims=True)) / mean_base
    deposit = jnp.where(owned[None, :], weight, 0.0)
    source = (
        jnp.zeros((sources, cx * cy * cz), jnp.float32)
        .at[:, local]
        .add(deposit)
        .reshape(change.shape)
    )
    dual = chebyshev(source, apply_op)
    dual_rims = padded_2(dual, (("gx", 1), ("gy", 2)), 1)
    grad_a = -jnp.sum(background * dual, axis=0)
    grad_k = jnp.zeros_like(kappa)
    for near_phi, near_dual in zip(phi_near, beside(dual_rims)):
        grad_k = grad_k - 0.5 * jnp.sum((background - near_phi) * (dual - near_dual), axis=0)
    summed_k, summed_a = lax.psum((grad_k, grad_a), "src")
    slab = v_kappa.shape[2]
    offset = lax.axis_index("src") * slab
    hv_k = lax.dynamic_slice_in_dim(summed_k, offset, slab, 2)
    hv_a = lax.dynamic_slice_in_dim(summed_a, offset, slab, 2)
    cell_count = cx * lax.axis_size("gx") * cy * lax.axis_size("gy") * cz
    w_k = hv_k - beta_prev[0] * q_kappa
    w_a = hv_a - beta_prev[0] * q_absorb
    local_wv = jnp.sum(w_k * v_kappa) + jnp.sum(w_a * v_absorb)
    local_vv = jnp.sum(v_kappa * v_kappa) + jnp.sum(v_absorb * v_absorb)
    wv_sum, vv_sum = lax.psum((local_wv, local_vv), ("src", "gx", "gy"))
    alpha = wv_sum / cell_count / (vv_sum / cell_count + eps_norm)
    r_k = w_k - alpha * v_kappa
    r_a = w_a - alpha * v_absorb
    rr_sum = lax.psum(jnp.sum(r_k * r_k) + jnp.sum(r_a * r_a), ("src", "gx", "gy"))
    beta = jnp.sqrt(rr_sum / cell_count + eps_norm)
    return (r_k / beta, r_a / beta, jnp.stack([alpha, beta]))


def chebyshev_scalars():
    theta = 0.5 * (lam_high + lam_low)
    delta = 0.5 * (lam_high - lam_low)
    sigma = theta / delta
    rho = 1.0 / sigma
    pairs = []
    for _ in range(ITERS - 1):
        rho_next = 1.0 / (2.0 * sigma - rho)
        pairs.append((rho_next * rho, 2.0 * rho_next / delta))
        rho = rho_next
    return theta, pairs


def places(split):
    g = lax.axis_index("gy")
    return lax.axis_index("src"), lax.axis_index("gx"), g // split, g % split


def shifted(value, step, axis):
    return pltpu.roll(value, step % value.shape[axis], axis)


def index_along(shape, axis):
    return lax.broadcasted_iota(jnp.int32, shape, axis)


def beyond(value, step, axis):
    size = value.shape[axis]
    at = index_along(value.shape, axis)
    edge = size - 1 if step == 1 else 0
    return jnp.where(at == edge, 0.0, shifted(value, -step, axis))


def packed_planes(ref, q):
    per = 128 // ref.shape[2]
    return jnp.concatenate([ref[per * q + j] for j in range(per)], axis=1)


def pack_kernel(bg, labels, vk, va, packed, message, raw, v_in, sems):
    _, x, _, _ = places(2)
    half = bg.shape[0] // 2
    cx = labels.shape[0]
    copies = [
        pltpu.make_async_copy(src, dst, sems.at[i])
        for i, (src, dst) in enumerate((
            (vk, v_in.at[0]),
            (va, v_in.at[1]),
            (labels, raw),
            *((bg.at[half * (1 - x) + i], message.at[pl.ds(cx * i, cx)]) for i in range(half)),
        ))
    ]
    for copy in copies:
        copy.start()
    groups = packed.shape[0] // 2
    for f in range(2):
        copies[f].wait()
        for q in range(groups):
            planes = packed_planes(v_in.at[f], q)
            packed[groups * f + q] = planes
            message[cx * (half + 1) + groups * f + q] = planes
    copies[2].wait()
    message[pl.ds(cx * half, cx)] = raw[...].astype(jnp.float32)
    for copy in copies[3:]:
        copy.wait()


def count_kernel(dets, beta_prev, count, beta_row, *, ny, nz, half, halo):
    beta_row[...] = jnp.full(beta_row.shape, beta_prev[0])
    _, _, y, _ = places(2)
    planes, rows, _ = count.shape
    flat = dets[...]
    iz = flat % nz
    line = flat // nz
    iy = line % ny
    ix = line // ny
    row = iy - (half - halo) * y
    spot = jnp.where((row >= 0) & (row < rows), ix * rows + row, -1)
    dets_n = flat.shape[1]
    at_z = (index_along((nz, dets_n), 0) == iz).astype(jnp.float32).astype(jnp.bfloat16)

    def body(i, carry):
        here = index_along((2 * rows, dets_n), 0) + i * (2 * rows)
        hot = (here == spot).astype(jnp.float32).astype(jnp.bfloat16)
        found = lax.dot_general(hot, at_z, (((1,), (1,)), ((), ())), preferred_element_type=jnp.float32)
        count[pl.ds(2 * i, 2)] = found.reshape(2, rows, nz)
        return carry

    lax.fori_loop(0, planes // 2, body, 0)


def photon_kernel(bg, labels, msg, mine, fields, raw, sems):
    _, x, _, c = places(2)
    half = bg.shape[0] // 2
    cx = labels.shape[0]
    here, there = cx * x, cx * (1 - x)
    copies = [
        pltpu.make_async_copy(src, dst, sems.at[i])
        for i, (src, dst) in enumerate((
            (bg.at[half * x + c], mine.at[pl.ds(here, cx)]),
            (bg.at[half * x + 1 - c], fields.at[0, pl.ds(here, cx)]),
            (labels, raw),
        ))
    ]
    for copy in copies:
        copy.start()
    mine[pl.ds(there, cx)] = msg[pl.ds(cx * c, cx)]
    fields[0, pl.ds(there, cx)] = msg[pl.ds(cx * (1 - c), cx)]
    fields[1, pl.ds(there, cx)] = msg[pl.ds(cx * half, cx)]
    for copy in copies:
        copy.wait()
    fields[1, pl.ds(here, cx)] = raw[...].astype(jnp.float32)


def unpacked(blocks, groups, s, store):
    n = len(blocks)
    cy, lanes = blocks[0][0].shape
    slab = lanes // n
    lane = index_along((cy, lanes), 1) // slab
    for f in range(2):
        for q in range(groups):
            values = [block[groups * f + q] for block in blocks]
            for j in range(n):
                plane = jnp.zeros((cy, lanes), jnp.float32)
                for k in range(n):
                    home = s ^ k
                    moved = pltpu.roll(values[k], ((home - j + n) % n) * slab, 1)
                    plane = jnp.where(lane == home, moved, plane)
                store(f, n * q + j, plane)


def join_kernel(*refs):
    joined, size = refs[-1], refs[0].shape[0]
    for i, ref in enumerate(refs[:-1]):
        joined[pl.ds(size * i, size)] = ref[...]


def own_half_kernel(vk, va, joined, half):
    s, _, _, _ = places(2)
    size = half.shape[1]
    groups = joined.shape[0] // 2 // (128 // vk.shape[2] - 1)
    n = size // groups
    own = [packed_planes(ref, q) for ref in (vk, va) for q in range(groups)]
    blocks = [own] + [[joined[2 * groups * k + i] for i in range(2 * groups)] for k in range(n - 1)]

    def store(f, i, plane):
        half[f, i] = plane

    unpacked(blocks, groups, s, store)


def vector_kernel(half, msg, joined, fields):
    s, x, _, _ = places(2)
    cx = half.shape[1]
    fields[:, pl.ds(cx * x, cx)] = half[...]
    n = lax.axis_size("src")
    groups = cx // n
    own = msg.shape[0] - 2 * groups
    blocks = [[msg[own + i] for i in range(2 * groups)]]
    blocks += [[joined[2 * groups * k + i] for i in range(2 * groups)] for k in range(n - 1)]
    there = cx * (1 - x)

    def store(f, i, plane):
        fields[f, there + i] = plane

    unpacked(blocks, groups, s, store)


def edge_shape(planes, lanes):
    return planes // GROUP, GROUP * REACH, lanes


def packed_edges(tiles):
    return jnp.concatenate([tile[:REACH] for tile in tiles], axis=0)


def edge_tile(packed, j, y):
    rows = packed[REACH * j : REACH * (j + 1)]
    tile = jnp.concatenate([rows, jnp.zeros((HALO - REACH, rows.shape[1]), jnp.float32)], axis=0)
    return jnp.where(y == 0, tile, shifted(tile, HALO - REACH, 0))


def near_rows(ref, i, first, y):
    tile = ref[i, pl.ds(first, HALO), :]
    return jnp.where(y == 0, shifted(tile, REACH - HALO, 0), tile)


def edges_of(own, got, edge, y, c):
    first = (own.shape[1] - HALO) * (1 - y)
    for g in range(edge.shape[0]):
        edge[g] = packed_edges([
            jnp.where(c != y, near_rows(own, GROUP * g + j, first, y), near_rows(got, GROUP * g + j, first, y))
            for j in range(GROUP)
        ])


def photon_edge_kernel(mine, fields, got, edge):
    _, _, y, c = places(2)
    edges_of(mine, got.at[0], edge.at[0], y, c)
    edges_of(fields.at[1], got.at[1], edge.at[1], y, c)


def vector_edge_kernel(fields, got, edge):
    _, _, y, c = places(2)
    for f in range(2):
        edges_of(fields.at[f], got.at[f], edge.at[f], y, c)


def solve(b, bufs, diag, fx, fy, fz, unroll):
    planes = b.shape[0]
    _, pairs = chebyshev_scalars()
    for step, (keep, push) in enumerate(pairs):
        src, dst = bufs[step % 2], bufs[(step + 1) % 2]

        def body(i, carry):
            u = src[i + 1]
            coef_y, coef_z = fy[i], fz[i]
            left = b[i] - diag[i] * u
            left = left + fx[i] * src[i] + fx[i + 1] * src[i + 2]
            left = left + coef_y * shifted(u, -1, 0) + shifted(coef_y * u, 1, 0)
            left = left + coef_z * shifted(u, -1, 1) + shifted(coef_z * u, 1, 1)
            change = u if step == 0 else u - dst[i + 1]
            dst[i + 1] = u + keep * change + push * left
            return carry

        lax.fori_loop(0, planes, body, 0, unroll=unroll)
    return bufs[len(pairs) % 2]


def folded(value):
    return jnp.sum(value.reshape(-1, 8, value.shape[1]), axis=0)


def framed_own(ref, shift, own, got, y, c):
    planes, cy, _ = own.shape
    there = pl.ds(shift, planes)
    base = HALO * y
    ref[there, pl.ds(base + cy * c, cy), :] = own[...]
    ref[there, pl.ds(base + cy * (1 - c), cy), :] = got[...]


def framed(ref, shift, own, got, edge, y, c):
    framed_own(ref, shift, own, got, y, c)
    cy = own.shape[1]
    for g in range(edge.shape[0]):
        packed = edge[g]
        for j in range(GROUP):
            ref[shift + GROUP * g + j, pl.ds(2 * cy * (1 - y), HALO), :] = edge_tile(packed, j, y)


def blank_ends(*refs):
    for ref in refs:
        blank = jnp.zeros(ref.shape[1:], jnp.float32)
        ref[0] = blank
        ref[ref.shape[0] - 1] = blank


def owned_rows(shape, base, count):
    at_row = index_along(shape, 0)
    return (at_row >= base) & (at_row < base + count)


def table_rows(kap_table, abs_table, shape):
    lane = index_along(shape, 1)
    kap_row = abs_row = jnp.zeros(shape, jnp.float32)
    for region in range(kap_table.shape[0]):
        kap_row = jnp.where(lane == region, kap_table[region], kap_row)
        abs_row = jnp.where(lane == region, abs_table[region], abs_row)
    return kap_row, abs_row


def stencil_kernel(
    kap_table, abs_table, mine, fields, got, count,
    kap, diag, fx, fy, fz, sums,
    labels,
):
    _, _, y, c = places(2)
    planes, cy, lanes = mine.shape
    rows = 2 * cy + HALO
    base = HALO * y
    framed_own(labels, 0, fields.at[1], got.at[1], y, c)
    labels[:, pl.ds(2 * cy * (1 - y), HALO), :] = jnp.zeros((planes, HALO, lanes), jnp.float32)
    blank_ends(kap)
    shape = (rows, lanes)
    lane = index_along(shape, 1)
    kap_row, abs_row = table_rows(kap_table, abs_table, shape)
    owned = owned_rows(shape, base, 2 * cy)

    def look_up(i, carry):
        at = labels[i].astype(jnp.int32)
        kap[i + 1] = jnp.where(owned, jnp.take_along_axis(kap_row, at, axis=1), 0.0)
        diag[i] = jnp.take_along_axis(abs_row, at, axis=1)
        return carry

    lax.fori_loop(0, planes, look_up, 0, unroll=4)
    fx[0] = 0.5 * kap[1]

    def set_up(i, carry):
        k = kap[i + 1]
        along_x = 0.5 * (k + kap[i + 2])
        along_y, along_z = 0.5 * (k + beyond(k, 1, 0)), 0.5 * (k + beyond(k, 1, 1))
        fx[i + 1] = along_x
        fy[i] = jnp.where(index_along(shape, 0) == rows - 1, 0.0, along_y)
        fz[i] = jnp.where(lane == lanes - 1, 0.0, along_z)
        back_y, back_z = 0.5 * (k + beyond(k, -1, 0)), 0.5 * (k + beyond(k, -1, 1))
        diag[i] = diag[i] + fx[i] + along_x + along_y + back_y + along_z + back_z
        total, square = carry
        for p, at in ((mine[i], c), (got[0, i], 1 - c)):
            part = count[i, pl.ds(base + cy * at, cy), :] * p
            total, square = total + folded(part), square + folded(part * p)
        return total, square

    zero = jnp.zeros((8, lanes), jnp.float32)
    sums[0], sums[1] = lax.fori_loop(0, planes, set_up, (zero, zero), unroll=4)


def halo_kernel(kap_table, abs_table, edge, kap, diag_in, fx_in, fy_in, fz_in, diag, fx, fy, fz):
    _, _, y, _ = places(2)
    planes, rows, lanes = diag.shape
    for ref, old in ((diag, diag_in), (fx, fx_in), (fy, fy_in), (fz, fz_in)):
        ref[...] = old[...]
    shape = (HALO, lanes)
    lane, row = index_along(shape, 1), index_along(shape, 0)
    kap_row, abs_row = table_rows(kap_table, abs_table, shape)
    low = y == 0
    here = pl.ds((rows - HALO) * (1 - y), HALO)
    beside_it = pl.ds((rows - 2 * HALO) * (1 - y) + HALO * y, HALO)
    labels = [edge_tile(edge[1, i // GROUP], i % GROUP, y).astype(jnp.int32) for i in range(planes)]
    tiles = [jnp.take_along_axis(kap_row, at, axis=1) for at in labels]
    none = jnp.zeros(shape, jnp.float32)
    before = 0.5 * tiles[0]
    fx[0, here, :] = before
    for i, k in enumerate(tiles):
        after = 0.5 * (k + (tiles[i + 1] if i + 1 < planes else none))
        own = kap[i + 1, beside_it, :]
        up, down = shifted(k, -1, 0), shifted(k, 1, 0)
        k_up = jnp.where(row == HALO - 1, jnp.where(low, 0.0, shifted(own, -1, 0)), up)
        k_down = jnp.where(row == 0, jnp.where(low, shifted(own, 1, 0), 0.0), down)
        along_y, back_y = 0.5 * (k + k_up), 0.5 * (k + k_down)
        along_z, back_z = 0.5 * (k + beyond(k, 1, 1)), 0.5 * (k + beyond(k, -1, 1))
        fx[i + 1, here, :] = after
        fy[i, here, :] = jnp.where(low & (row == HALO - 1), 0.0, along_y)
        fz[i, here, :] = jnp.where(lane == lanes - 1, 0.0, along_z)
        absorb = jnp.take_along_axis(abs_row, labels[i], axis=1)
        diag[i, here, :] = absorb + before + after + along_y + back_y + along_z + back_z
        before = after
        face_up = jnp.where(low & (row == HALO - 1), 0.5 * up, 0.0)
        face_down = jnp.where(low | (row > 0), 0.0, 0.5 * down)
        fy[i, beside_it, :] = fy_in[i, beside_it, :] + face_up
        diag[i, beside_it, :] = diag_in[i, beside_it, :] + face_up + face_down


def first_kernel(
    diag, fx, fy, fz, count, sums, mine, got_photon, vector, got_vector, photon_edge, edge,
    phi, change, message,
    vk, va, b, buf_a, buf_b,
):
    _, _, y, c = places(2)
    planes, rows, lanes = change.shape
    cy = mine.shape[1]
    framed(phi, 1, mine, got_photon.at[0], photon_edge.at[0], y, c)
    framed(vk, 1, vector.at[0], got_vector.at[0], edge.at[0], y, c)
    framed(va, 0, vector.at[1], got_vector.at[1], edge.at[1], y, c)
    blank_ends(phi, vk, buf_a, buf_b)
    theta, _ = chebyshev_scalars()

    def set_up(i, carry):
        v, p = vk[i + 1], phi[i + 1]
        total = 0.5 * (v + vk[i]) * (p - phi[i]) + 0.5 * (v + vk[i + 2]) * (p - phi[i + 2])
        for axis in range(2):
            flow = 0.5 * (v + beyond(v, 1, axis)) * (p - beyond(p, 1, axis))
            first = index_along(v.shape, axis) == 0
            total = total + flow + jnp.where(first, 0.5 * v * p, -shifted(flow, 1, axis))
        total = -(va[i] * p + total)
        b[i] = total
        buf_a[i + 1] = total * (1.0 / theta)
        return carry

    lax.fori_loop(0, planes, set_up, 0, unroll=4)
    found = solve(b, (buf_a, buf_b), diag, fx, fy, fz, UNROLL)
    owned = owned_rows((rows, lanes), HALO * y, 2 * cy)

    def add_up(i, carry):
        u = found[i + 1]
        change[i] = u
        part = jnp.where(owned, count[i], 0.0) * u
        return carry[0] + folded(part), carry[1] + folded(part * phi[i + 1])

    zero = jnp.zeros((8, lanes), jnp.float32)
    seen, cross = lax.fori_loop(0, planes, add_up, (zero, zero), unroll=4)
    first = (2 * cy - HALO) * (1 - y) + HALO * y
    for g, part in enumerate((sums[0], seen, cross, sums[1])):
        message[g, pl.ds(0, GROUP * REACH), :] = packed_edges(
            [near_rows(found, 1 + GROUP * g + j, first, y) for j in range(GROUP)]
        )
        message[g, pl.ds(GROUP * REACH, 8), :] = part


def second_kernel(
    phi, change, diag, fx, fy, fz, count, sent, came,
    own, message,
    b, buf_a, buf_b, grad_k, grad_a,
    *, dets,
):
    _, _, y, c = places(2)
    planes, rows, lanes = change.shape
    cy = (rows - HALO) // 2
    base = HALO * y
    edge = pl.ds(2 * cy * (1 - y), HALO)
    tail = pl.ds(GROUP * REACH, 8)
    total, seen_sum, cross, square = (
        jnp.sum(jnp.sum(sent[g, tail, :] + came[g, tail, :], axis=0, keepdims=True), axis=1, keepdims=True)
        for g in range(4)
    )
    mean = total / dets
    part = seen_sum / total
    level = (cross - part * square) / (total * mean)
    inverse = 1.0 / mean
    blank_ends(buf_a, buf_b)
    theta, _ = chebyshev_scalars()

    def weighted(n, u, p):
        return n * (((u - p * part) * inverse - level) * inverse)

    def set_up(i, carry):
        value = weighted(count[i], change[i], phi[i + 1])
        b[i] = value
        buf_a[i + 1] = value * (1.0 / theta)
        return carry

    lax.fori_loop(0, planes, set_up, 0, unroll=4)
    for i in range(planes):
        u = edge_tile(came[i // GROUP], i % GROUP, y)
        value = weighted(count[i, edge, :], u, phi[i + 1, edge, :])
        b[i, edge, :] = value
        buf_a[i + 1, edge, :] = value * (1.0 / theta)
    dual = solve(b, (buf_a, buf_b), diag, fx, fy, fz, UNROLL)

    def product(i, carry):
        p, u = phi[i + 1], dual[i + 1]
        grad = (p - phi[i]) * (u - dual[i]) + (p - phi[i + 2]) * (u - dual[i + 2])
        both = p * u
        for axis in range(2):
            flow = (p - beyond(p, 1, axis)) * (u - beyond(u, 1, axis))
            first = index_along(p.shape, axis) == 0
            grad = grad + flow + jnp.where(first, both, shifted(flow, 1, axis))
        grad_k[i] = -0.5 * grad
        grad_a[i] = -both
        for f, ref in enumerate((grad_k, grad_a)):
            own[f, i] = ref[i, pl.ds(base + cy * c, cy), :]
            message[f, i] = ref[i, pl.ds(base + cy * (1 - c), cy), :]
        return carry

    lax.fori_loop(0, planes, product, 0, unroll=4)


def packed_slabs(own, came, half, choices, outs):
    s, _, _, _ = places(2)
    _, planes, cy, lanes = own.shape
    n = planes // 2 // outs.shape[2]
    slab = lanes // n
    lane = index_along((cy, lanes), 1) // slab
    for f in range(2):
        for q in range(outs.shape[2]):
            at = planes // 2 * half + n * q
            parts = [own[f, at + j] + came[f, at + j] for j in range(n)]
            for i, k in enumerate(choices):
                to = s ^ k
                piece = jnp.zeros((cy, lanes), jnp.float32)
                for j in range(n):
                    moved = pltpu.roll(parts[j], ((j - to + n) % n) * slab, 1)
                    piece = jnp.where(lane == j, moved, piece)
                outs[i, f, q] = piece


def send_kernel(own, came, out, *, k):
    _, x, _, _ = places(2)
    packed_slabs(own, came, 1 - x, (k,), out)


def keep_kernel(own, came, kept):
    _, x, _, _ = places(2)
    packed_slabs(own, came, x, range(kept.shape[0]), kept)


def add_kernel(kept, came, out, *, k):
    out[...] = kept[k] + came[0]


def sum_kernel(*refs):
    total = refs[0][...]
    for ref in refs[1:-1]:
        total = total + ref[...]
    refs[-1][...] = total


def project_kernel(*refs, parts_n, n):
    beta_prev = refs[0]
    parts = refs[1 : 1 + parts_n]
    vk, va, qk, qa, w_k, w_a, tile = refs[1 + parts_n :]
    s, x, y, c = places(2)
    slab = 128 // n
    for f, (q_ref, w) in enumerate(((qk, w_k), (qa, w_a))):
        for q in range(vk.shape[0] // n):
            whole = sum(part[f, q] for part in parts[1:]) + parts[0][f, q]
            for j in range(n):
                i = n * q + j
                w[i] = whole[:, slab * j : slab * (j + 1)] - beta_prev[:, : vk.shape[2]] * q_ref[i]

    def dot(a, b):
        return jnp.sum(jnp.sum(a * b, axis=0))

    wk, wa, v_k, v_a = w_k[...], w_a[...], vk[...], va[...]
    one = jnp.ones((1, 1), jnp.float32)
    wv = (dot(wk, v_k) + dot(wa, v_a)) * one
    vv = (dot(v_k, v_k) + dot(v_a, v_a)) * one
    a = jnp.where(vv > 0.0, wv / jnp.where(vv > 0.0, vv, 1.0), 0.0)
    u_k, u_a = wk - a * v_k, wa - a * v_a
    uv = (dot(u_k, v_k) + dot(u_a, v_a)) * one
    uu = (dot(u_k, u_k) + dot(u_a, u_a)) * one
    me = ((s * 2 + x) * 2 + y) * 2 + c
    lane = index_along((8, 128), 1)
    row = index_along((8, 128), 0)
    values = jnp.zeros((8, 128), jnp.float32)
    for i, value in enumerate((wv, vv, a, uv, uu)):
        values = jnp.where(row == i, value, values)
    tile[...] = jnp.where(lane == me, values, 0.0)


def final_kernel(tiles, w_k, w_a, vk, va, next_k, next_a, coefs, *, cells):
    tile = jnp.sum(tiles[...], axis=0)
    wv, vv, a, uv, uu = (tile[i : i + 1] for i in range(5))
    wv_sum = jnp.sum(wv, axis=1, keepdims=True)
    vv_sum = jnp.sum(vv, axis=1, keepdims=True)
    alpha = wv_sum / cells / (vv_sum / cells + eps_norm)
    off = alpha - a
    rr = jnp.sum(uu - 2.0 * off * uv + off * off * vv, axis=1, keepdims=True)
    beta = jnp.sqrt(rr / cells + eps_norm)
    next_k[...] = (w_k[...] - alpha * vk[...]) / beta
    next_a[...] = (w_a[...] - alpha * va[...]) / beta
    coefs[0] = jnp.sum(alpha)
    coefs[1] = jnp.sum(beta)


def f32(*shape):
    return jax.ShapeDtypeStruct(shape, jnp.float32)


def run(kernel, outs, *args, after=(), scratch=(), copies=0, smem=(), hbm=(), mib=16, in_smem_out=(), cost=None):
    vmem = pl.BlockSpec(memory_space=pltpu.VMEM)
    scalar = pl.BlockSpec(memory_space=pltpu.SMEM)
    far = pl.BlockSpec(memory_space=pltpu.HBM)
    held = [pltpu.VMEM(shape, dtype) for shape, dtype in scratch]
    used, waits = len(args), len(after)

    def body(*refs):
        kernel(*refs[:used], *refs[used + waits :])

    args = (*args, *after)
    if copies:
        held.append(pltpu.SemaphoreType.DMA((copies,)))
    return pl.pallas_call(
        body if waits else kernel,
        out_shape=tuple(outs),
        in_specs=[scalar if i in smem else far if i in hbm else vmem for i in range(len(args))],
        out_specs=tuple(scalar if i in in_smem_out else vmem for i in range(len(outs))),
        scratch_shapes=held,
        compiler_params=pltpu.CompilerParams(vmem_limit_bytes=mib * 2**20),
        cost_estimate=cost,
    )(*args)


HALO = 8
UNROLL = 16
REACH = 6
GROUP = 4


def per_device_paired(
    labels, kappa_table, absorb_table, background, det_cells,
    v_kappa, v_absorb, q_kappa, q_absorb, beta_prev,
):
    sources, cx, cy, cz = background.shape
    n = lax.axis_size("src")
    planes, rows = 2 * cx, 2 * cy + HALO
    ny = cy * lax.axis_size("gy")
    dets = det_cells.shape[0]
    cells = planes * ny * cz
    groups = cx // n

    def swap_x(value):
        return lax.ppermute(value, "gx", [(0, 1), (1, 0)])

    def swap_core(value):
        return lax.ppermute(value, "gy", [(0, 1), (1, 0), (2, 3), (3, 2)])

    def along_z(value, k):
        return lax.ppermute(value, "src", [(i, i ^ k) for i in range(n)])

    block = (cx, cy, cz)
    float_block = lambda *shape: (shape, jnp.float32)
    raw_labels = (block, jnp.int32)
    packed, message = run(
        pack_kernel, (f32(2 * groups, cy, cz), f32((sources // 2 + 1) * cx + 2 * groups, cy, cz)),
        background, labels, v_kappa, v_absorb, hbm=(0, 1, 2, 3),
        scratch=(raw_labels, float_block(2, *v_kappa.shape)), copies=3 + sources // 2, mib=60,
    )
    long = pl.CostEstimate(flops=10**9, bytes_accessed=2**26, transcendentals=0)
    came = swap_x(message)
    slabs = [along_z(packed, k) for k in range(1, n)]
    count, beta_row = run(
        functools.partial(count_kernel, ny=ny, nz=cz, half=2 * cy, halo=HALO),
        (f32(planes, rows, cz), f32(1, cz)), det_cells.reshape(1, dets), beta_prev, smem=(1,),
        cost=pl.CostEstimate(flops=2 * planes * rows * cz * dets, bytes_accessed=planes * rows * cz * 4, transcendentals=0),
    )

    def across_y(value):
        return lax.ppermute(value, "gy", [(i, (i + 2) % 4) for i in range(4)])

    (joined,) = run(join_kernel, (f32(2 * groups * (n - 1), cy, cz),), *slabs, after=(count,))
    joined_came = swap_x(joined)
    (half_vector,) = run(own_half_kernel, (f32(2, *block),), v_kappa, v_absorb, joined)
    mine, fields = run(
        photon_kernel, (f32(planes, cy, cz), f32(2, planes, cy, cz)),
        background, labels, came, after=(joined,), hbm=(0, 1), scratch=(raw_labels,), copies=3,
    )
    got = swap_core(fields)
    (vector,) = run(
        vector_kernel, (f32(2, planes, cy, cz),), half_vector, came, joined_came, after=(mine,)
    )
    edge = (f32(2, *edge_shape(planes, cz)),)
    (sent,) = run(photon_edge_kernel, edge, mine, fields, got, after=(vector,))
    photon_edge = across_y(sent)
    vector_got = swap_core(vector)
    (vector_sent,) = run(vector_edge_kernel, edge, vector, vector_got, after=(sent,))
    frame, wide = (planes, rows, cz), (planes + 2, rows, cz)
    float_frame, float_wide = float_block(*frame), float_block(*wide)
    coefs = (f32(*frame), f32(planes + 1, rows, cz), f32(*frame), f32(*frame))
    kap, *partial, sums = run(
        stencil_kernel, (f32(*wide), *coefs, f32(2, 8, cz)),
        kappa_table, absorb_table, mine, fields, got, count, after=(vector_sent,), cost=long,
        smem=(0, 1), scratch=(float_frame,),
    )
    diag, fx, fy, fz = run(
        halo_kernel, coefs, kappa_table, absorb_table, photon_edge, kap, *partial, smem=(0, 1)
    )
    phi, change, sent = run(
        first_kernel, (f32(*wide), f32(*frame), f32(4, GROUP * REACH + 8, cz)),
        diag, fx, fy, fz, count, sums, mine, got, vector, vector_got,
        photon_edge, across_y(vector_sent),
        scratch=(float_wide, float_frame, float_frame, float_wide, float_wide),
    )
    heard = across_y(sent)
    own, message = run(
        functools.partial(second_kernel, dets=dets),
        (f32(2, planes, cy, cz), f32(2, planes, cy, cz)),
        phi, change, diag, fx, fy, fz, count, sent, heard,
        scratch=(float_frame, float_wide, float_wide, float_frame, float_frame),
    )
    piece = f32(2, groups, cy, cz)
    got = swap_core(message)
    crossed, last = {}, ()
    for k in reversed(range(n)):
        last = run(functools.partial(send_kernel, k=k), (f32(1, *piece.shape),), own, got, after=last)
        crossed[k] = swap_x(last[0])
    (kept,) = run(keep_kernel, (f32(n, *piece.shape),), own, got, after=last)
    totals = {
        k: run(functools.partial(add_kernel, k=k), (piece,), kept, value)[0] for k, value in crossed.items()
    }
    received = {k: along_z(totals[k], k) for k in reversed(range(1, n))}
    (distant,) = run(sum_kernel, (piece,), *(received[k] for k in range(n // 2, n)), cost=long)
    parts = [distant, totals[0]] + [received[k] for k in range(1, n // 2)]
    w_k, w_a, tile = run(
        functools.partial(project_kernel, parts_n=len(parts), n=n),
        (f32(*v_kappa.shape), f32(*v_kappa.shape), f32(8, 128)),
        beta_row, *parts, v_kappa, v_absorb, q_kappa, q_absorb,
    )
    everyone = ("src", "gx", "gy")
    tiles = lax.all_to_all(jnp.broadcast_to(tile, (8 * n, 8, 128)), everyone, 0, 0)
    return tuple(run(
        functools.partial(final_kernel, cells=cells),
        (f32(*v_kappa.shape), f32(*v_kappa.shape), f32(2)),
        tiles, w_k, w_a, v_kappa, v_absorb, in_smem_out=(2,),
    ))


def paired_fits(mesh):
    return mesh.shape["gx"] == 2 and mesh.shape["gy"] == 4


def body_for(mesh):
    if not paired_fits(mesh):
        return per_device

    def chosen(*args):
        sources, cx, cy, cz = args[3].shape
        n = lax.axis_size("src")
        fits = sources == 4 and cz == 128 and cx % n == 0 and cx % GROUP == 0 and cy % HALO == 0 and n > 1 and n & (n - 1) == 0
        devices = 8 * n
        return (per_device_paired if fits and devices <= 128 else per_device)(*args)

    return chosen


def solution(mesh):
    return jax.shard_map(
        body_for(mesh),
        mesh=mesh,
        in_specs=(
            P("gx", "gy", None),
            P(),
            P(),
            P("src", "gx", "gy", None),
            P(),
            P("gx", "gy", "src"),
            P("gx", "gy", "src"),
            P("gx", "gy", "src"),
            P("gx", "gy", "src"),
            P(),
        ),
        out_specs=(P("gx", "gy", "src"), P("gx", "gy", "src"), P()),
        check_vma=False,
    )
```

```python
import functools

import jax
import jax.numpy as jnp
from jax import lax
from jax.experimental import pallas as pl
from jax.experimental.pallas import tpu as pltpu
from jax.sharding import PartitionSpec as P

ITERS = 6


lam_low = 0.02
lam_high = 24.1
eps_norm = 1e-06


def padded_2(block, sides, width):
    for axis, dim in sides:
        count = lax.axis_size(axis)
        forward = [(i, i + 1) for i in range(count - 1)]
        backward = [(target, source) for source, target in forward]
        low = lax.ppermute(
            lax.slice_in_dim(block, block.shape[dim] - width, None, axis=dim), axis, forward
        )
        high = lax.ppermute(lax.slice_in_dim(block, 0, width, axis=dim), axis, backward)
        block = jnp.concatenate([low, block, high], axis=dim)
    return block


def regional(labels, table):
    field = jnp.zeros(labels.shape, jnp.float32)
    for region in range(table.shape[0]):
        field = field + jnp.where(labels == region, table[region], 0.0)
    return field


def beside(padded):
    widths = [(0, 0)] * (padded.ndim - 1) + [(1, 1)]
    full = jnp.pad(padded, widths)
    return [
        full[..., 2:, 1:-1, 1:-1],
        full[..., :-2, 1:-1, 1:-1],
        full[..., 1:-1, 2:, 1:-1],
        full[..., 1:-1, :-2, 1:-1],
        full[..., 1:-1, 1:-1, 2:],
        full[..., 1:-1, 1:-1, :-2],
    ]


def chebyshev(rhs, apply_op):
    theta = 0.5 * (lam_high + lam_low)
    delta = 0.5 * (lam_high - lam_low)
    sigma = theta / delta
    rho = 1.0 / sigma
    solution = jnp.zeros_like(rhs)
    remain = rhs
    step_dir = rhs / theta
    for step in range(ITERS):
        solution = solution + step_dir
        if step + 1 < ITERS:
            remain = remain - apply_op(step_dir)
            rho_next = 1.0 / (2.0 * sigma - rho)
            step_dir = rho_next * rho * step_dir + 2.0 * rho_next / delta * remain
            rho = rho_next
    return solution


def per_device(
    labels,
    kappa_table,
    absorb_table,
    background,
    det_cells,
    v_kappa,
    v_absorb,
    q_kappa,
    q_absorb,
    beta_prev,
):
    sources, cx, cy, cz = background.shape
    kappa = regional(labels, kappa_table)
    absorb = regional(labels, absorb_table)
    full_k, full_a = (
        lax.all_gather(v_kappa, "src", axis=2, tiled=True),
        lax.all_gather(v_absorb, "src", axis=2, tiled=True),
    )
    stacked = jnp.concatenate([background, kappa[None], full_k[None]], axis=0)
    rims = padded_2(stacked, (("gx", 1), ("gy", 2)), 1)
    near_all = beside(rims)
    kappa_faces = [0.5 * (kappa + near[sources]) for near in near_all]
    vk_faces = [0.5 * (full_k + near[sources + 1]) for near in near_all]
    phi_near = [near[:sources] for near in near_all]

    def apply_op(field):
        padded = padded_2(field, (("gx", 1), ("gy", 2)), 1)
        result = absorb * field
        for face, near in zip(kappa_faces, beside(padded)):
            result = result + face * (field - near)
        return result

    rhs = full_a * background
    for face, near in zip(vk_faces, phi_near):
        rhs = rhs + face * (background - near)
    rhs = -rhs
    change = chebyshev(rhs, apply_op)
    span_y = cy * lax.axis_size("gy")
    ix = det_cells // (span_y * cz)
    iy = det_cells // cz % span_y
    iz = det_cells % cz
    anchor_x = lax.axis_index("gx") * cx
    anchor_y = lax.axis_index("gy") * cy
    owned = (ix >= anchor_x) & (ix < anchor_x + cx) & (iy >= anchor_y) & (iy < anchor_y + cy)
    local = jnp.where(owned, ((ix - anchor_x) * cy + (iy - anchor_y)) * cz + iz, 0)
    seen_part = jnp.where(owned[None, :], change.reshape(sources, -1)[:, local], 0.0)
    base_part = jnp.where(owned[None, :], background.reshape(sources, -1)[:, local], 0.0)
    seen, base = lax.psum((seen_part, base_part), ("gx", "gy"))
    total = jnp.sum(base, axis=1, keepdims=True)
    mean_base = total / det_cells.shape[0]
    ratio = base / total
    jv_vals = (seen - ratio * jnp.sum(seen, axis=1, keepdims=True)) / mean_base
    weight = (jv_vals - jnp.sum(ratio * jv_vals, axis=1, keepdims=True)) / mean_base
    deposit = jnp.where(owned[None, :], weight, 0.0)
    source = (
        jnp.zeros((sources, cx * cy * cz), jnp.float32)
        .at[:, local]
        .add(deposit)
        .reshape(change.shape)
    )
    dual = chebyshev(source, apply_op)
    dual_rims = padded_2(dual, (("gx", 1), ("gy", 2)), 1)
    grad_a = -jnp.sum(background * dual, axis=0)
    grad_k = jnp.zeros_like(kappa)
    for near_phi, near_dual in zip(phi_near, beside(dual_rims)):
        grad_k = grad_k - 0.5 * jnp.sum((background - near_phi) * (dual - near_dual), axis=0)
    summed_k, summed_a = lax.psum((grad_k, grad_a), "src")
    slab = v_kappa.shape[2]
    offset = lax.axis_index("src") * slab
    hv_k = lax.dynamic_slice_in_dim(summed_k, offset, slab, 2)
    hv_a = lax.dynamic_slice_in_dim(summed_a, offset, slab, 2)
    cell_count = cx * lax.axis_size("gx") * cy * lax.axis_size("gy") * cz
    w_k = hv_k - beta_prev[0] * q_kappa
    w_a = hv_a - beta_prev[0] * q_absorb
    local_wv = jnp.sum(w_k * v_kappa) + jnp.sum(w_a * v_absorb)
    local_vv = jnp.sum(v_kappa * v_kappa) + jnp.sum(v_absorb * v_absorb)
    wv_sum, vv_sum = lax.psum((local_wv, local_vv), ("src", "gx", "gy"))
    alpha = wv_sum / cell_count / (vv_sum / cell_count + eps_norm)
    r_k = w_k - alpha * v_kappa
    r_a = w_a - alpha * v_absorb
    rr_sum = lax.psum(jnp.sum(r_k * r_k) + jnp.sum(r_a * r_a), ("src", "gx", "gy"))
    beta = jnp.sqrt(rr_sum / cell_count + eps_norm)
    return (r_k / beta, r_a / beta, jnp.stack([alpha, beta]))


def chebyshev_scalars():
    theta = 0.5 * (lam_high + lam_low)
    delta = 0.5 * (lam_high - lam_low)
    sigma = theta / delta
    rho = 1.0 / sigma
    pairs = []
    for _ in range(ITERS - 1):
        rho_next = 1.0 / (2.0 * sigma - rho)
        pairs.append((rho_next * rho, 2.0 * rho_next / delta))
        rho = rho_next
    return theta, pairs


def places(split):
    g = lax.axis_index("gy")
    return lax.axis_index("src"), lax.axis_index("gx"), g // split, g % split


def shifted(value, step, axis):
    return pltpu.roll(value, step % value.shape[axis], axis)


def index_along(shape, axis):
    return lax.broadcasted_iota(jnp.int32, shape, axis)


def beyond(value, step, axis):
    size = value.shape[axis]
    at = index_along(value.shape, axis)
    edge = size - 1 if step == 1 else 0
    return jnp.where(at == edge, 0.0, shifted(value, -step, axis))


def packed_planes(ref, q):
    per = 128 // ref.shape[2]
    return jnp.concatenate([ref[per * q + j] for j in range(per)], axis=1)


def pack_kernel(bg, labels, vk, va, packed, message, raw, v_in, sems):
    _, x, _, _ = places(2)
    half = bg.shape[0] // 2
    cx = labels.shape[0]
    copies = [
        pltpu.make_async_copy(src, dst, sems.at[i])
        for i, (src, dst) in enumerate((
            (vk, v_in.at[0]),
            (va, v_in.at[1]),
            (labels, raw),
            *((bg.at[half * (1 - x) + i], message.at[pl.ds(cx * i, cx)]) for i in range(half)),
        ))
    ]
    for copy in copies:
        copy.start()
    groups = packed.shape[0] // 2
    for f in range(2):
        copies[f].wait()
        for q in range(groups):
            planes = packed_planes(v_in.at[f], q)
            packed[groups * f + q] = planes
            message[cx * (half + 1) + groups * f + q] = planes
    copies[2].wait()
    message[pl.ds(cx * half, cx)] = raw[...].astype(jnp.float32)
    for copy in copies[3:]:
        copy.wait()


def count_kernel(dets, beta_prev, count, beta_row, *, ny, nz, half, halo):
    beta_row[...] = jnp.full(beta_row.shape, beta_prev[0])
    _, _, y, _ = places(2)
    planes, rows, _ = count.shape
    flat = dets[...]
    iz = flat % nz
    line = flat // nz
    iy = line % ny
    ix = line // ny
    row = iy - (half - halo) * y
    spot = jnp.where((row >= 0) & (row < rows), ix * rows + row, -1)
    dets_n = flat.shape[1]
    at_z = (index_along((nz, dets_n), 0) == iz).astype(jnp.float32).astype(jnp.bfloat16)

    def body(i, carry):
        here = index_along((2 * rows, dets_n), 0) + i * (2 * rows)
        hot = (here == spot).astype(jnp.float32).astype(jnp.bfloat16)
        found = lax.dot_general(hot, at_z, (((1,), (1,)), ((), ())), preferred_element_type=jnp.float32)
        count[pl.ds(2 * i, 2)] = found.reshape(2, rows, nz)
        return carry

    lax.fori_loop(0, planes // 2, body, 0)


def photon_kernel(bg, labels, msg, mine, fields, raw, sems):
    _, x, _, c = places(2)
    half = bg.shape[0] // 2
    cx = labels.shape[0]
    here, there = cx * x, cx * (1 - x)
    copies = [
        pltpu.make_async_copy(src, dst, sems.at[i])
        for i, (src, dst) in enumerate((
            (bg.at[half * x + c], mine.at[pl.ds(here, cx)]),
            (bg.at[half * x + 1 - c], fields.at[0, pl.ds(here, cx)]),
            (labels, raw),
        ))
    ]
    for copy in copies:
        copy.start()
    mine[pl.ds(there, cx)] = msg[pl.ds(cx * c, cx)]
    fields[0, pl.ds(there, cx)] = msg[pl.ds(cx * (1 - c), cx)]
    fields[1, pl.ds(there, cx)] = msg[pl.ds(cx * half, cx)]
    for copy in copies:
        copy.wait()
    fields[1, pl.ds(here, cx)] = raw[...].astype(jnp.float32)


def unpacked(blocks, groups, s, store):
    n = len(blocks)
    cy, lanes = blocks[0][0].shape
    slab = lanes // n
    lane = index_along((cy, lanes), 1) // slab
    for f in range(2):
        for q in range(groups):
            values = [block[groups * f + q] for block in blocks]
            for j in range(n):
                plane = jnp.zeros((cy, lanes), jnp.float32)
                for k in range(n):
                    home = s ^ k
                    moved = pltpu.roll(values[k], ((home - j + n) % n) * slab, 1)
                    plane = jnp.where(lane == home, moved, plane)
                store(f, n * q + j, plane)


def join_kernel(*refs):
    joined, size = refs[-1], refs[0].shape[0]
    for i, ref in enumerate(refs[:-1]):
        joined[pl.ds(size * i, size)] = ref[...]


def own_half_kernel(vk, va, joined, half):
    s, _, _, _ = places(2)
    size = half.shape[1]
    groups = joined.shape[0] // 2 // (128 // vk.shape[2] - 1)
    n = size // groups
    own = [packed_planes(ref, q) for ref in (vk, va) for q in range(groups)]
    blocks = [own] + [[joined[2 * groups * k + i] for i in range(2 * groups)] for k in range(n - 1)]

    def store(f, i, plane):
        half[f, i] = plane

    unpacked(blocks, groups, s, store)


def vector_kernel(half, msg, joined, fields):
    s, x, _, _ = places(2)
    cx = half.shape[1]
    fields[:, pl.ds(cx * x, cx)] = half[...]
    n = lax.axis_size("src")
    groups = cx // n
    own = msg.shape[0] - 2 * groups
    blocks = [[msg[own + i] for i in range(2 * groups)]]
    blocks += [[joined[2 * groups * k + i] for i in range(2 * groups)] for k in range(n - 1)]
    there = cx * (1 - x)

    def store(f, i, plane):
        fields[f, there + i] = plane

    unpacked(blocks, groups, s, store)


def edge_shape(planes, lanes):
    return planes // GROUP, GROUP * REACH, lanes


def packed_edges(tiles):
    return jnp.concatenate([tile[:REACH] for tile in tiles], axis=0)


def edge_tile(packed, j, y):
    rows = packed[REACH * j : REACH * (j + 1)]
    tile = jnp.concatenate([rows, jnp.zeros((HALO - REACH, rows.shape[1]), jnp.float32)], axis=0)
    return jnp.where(y == 0, tile, shifted(tile, HALO - REACH, 0))


def near_rows(ref, i, first, y):
    tile = ref[i, pl.ds(first, HALO), :]
    return jnp.where(y == 0, shifted(tile, REACH - HALO, 0), tile)


def edges_of(own, got, edge, y, c):
    first = (own.shape[1] - HALO) * (1 - y)
    for g in range(edge.shape[0]):
        edge[g] = packed_edges([
            jnp.where(c != y, near_rows(own, GROUP * g + j, first, y), near_rows(got, GROUP * g + j, first, y))
            for j in range(GROUP)
        ])


def photon_edge_kernel(mine, fields, got, edge):
    _, _, y, c = places(2)
    edges_of(mine, got.at[0], edge.at[0], y, c)
    edges_of(fields.at[1], got.at[1], edge.at[1], y, c)


def vector_edge_kernel(fields, got, edge):
    _, _, y, c = places(2)
    for f in range(2):
        edges_of(fields.at[f], got.at[f], edge.at[f], y, c)


def solve(b, bufs, diag, fx, fy, fy_back, fz, y, unroll):
    planes, rows, _ = b.shape
    _, pairs = chebyshev_scalars()
    one = jnp.where(y >= 0, 1, 0)
    at = pl.ds(HALO, rows)
    for step, (keep, push) in enumerate(pairs):
        src, dst = bufs[step % 2], bufs[(step + 1) % 2]

        def body(i, carry):
            u = src[i + 1, at, :]
            coef_z = fz[i]
            left = b[i] - diag[i] * u
            left = left + fx[i] * src[i, at, :] + fx[i + 1] * src[i + 2, at, :]
            left = left + fy[i] * src[i + 1, pl.ds(HALO + one, rows), :]
            left = left + fy_back[i] * src[i + 1, pl.ds(HALO - one, rows), :]
            left = left + coef_z * shifted(u, -1, 1) + shifted(coef_z * u, 1, 1)
            change = u if step == 0 else u - dst[i + 1, at, :]
            dst[i + 1, at, :] = u + keep * change + push * left
            return carry

        lax.fori_loop(0, planes, body, 0, unroll=unroll)
    return bufs[len(pairs) % 2]


def folded(value):
    return jnp.sum(value.reshape(-1, 8, value.shape[1]), axis=0)


def framed_own(ref, shift, own, got, y, c):
    planes, cy, _ = own.shape
    there = pl.ds(shift, planes)
    base = HALO * y
    ref[there, pl.ds(base + cy * c, cy), :] = own[...]
    ref[there, pl.ds(base + cy * (1 - c), cy), :] = got[...]


def framed(ref, shift, own, got, edge, y, c):
    framed_own(ref, shift, own, got, y, c)
    cy = own.shape[1]
    for g in range(edge.shape[0]):
        packed = edge[g]
        for j in range(GROUP):
            ref[shift + GROUP * g + j, pl.ds(2 * cy * (1 - y), HALO), :] = edge_tile(packed, j, y)


def blank_ends(*refs):
    for ref in refs:
        blank = jnp.zeros(ref.shape[1:], jnp.float32)
        ref[0] = blank
        ref[ref.shape[0] - 1] = blank


def blank_rim(*refs):
    blank_ends(*refs)
    for ref in refs:
        planes, rows, lanes = ref.shape
        none = jnp.zeros((planes, HALO, lanes), jnp.float32)
        ref[:, pl.ds(0, HALO), :] = none
        ref[:, pl.ds(rows - HALO, HALO), :] = none


def owned_rows(shape, base, count):
    at_row = index_along(shape, 0)
    return (at_row >= base) & (at_row < base + count)


def table_rows(kap_table, abs_table, shape):
    lane = index_along(shape, 1)
    kap_row = abs_row = jnp.zeros(shape, jnp.float32)
    for region in range(kap_table.shape[0]):
        kap_row = jnp.where(lane == region, kap_table[region], kap_row)
        abs_row = jnp.where(lane == region, abs_table[region], abs_row)
    return kap_row, abs_row


def stencil_kernel(
    kap_table, abs_table, mine, fields, got, count,
    kap, diag, fx, fy, fz, sums,
    labels,
):
    _, _, y, c = places(2)
    planes, cy, lanes = mine.shape
    rows = 2 * cy + HALO
    base = HALO * y
    framed_own(labels, 0, fields.at[1], got.at[1], y, c)
    labels[:, pl.ds(2 * cy * (1 - y), HALO), :] = jnp.zeros((planes, HALO, lanes), jnp.float32)
    blank_ends(kap)
    shape = (rows, lanes)
    lane = index_along(shape, 1)
    kap_row, abs_row = table_rows(kap_table, abs_table, shape)
    owned = owned_rows(shape, base, 2 * cy)

    def look_up(i, carry):
        at = labels[i].astype(jnp.int32)
        kap[i + 1] = jnp.where(owned, jnp.take_along_axis(kap_row, at, axis=1), 0.0)
        diag[i] = jnp.take_along_axis(abs_row, at, axis=1)
        return carry

    lax.fori_loop(0, planes, look_up, 0, unroll=4)
    fx[0] = 0.5 * kap[1]

    def set_up(i, carry):
        k = kap[i + 1]
        along_x = 0.5 * (k + kap[i + 2])
        along_y, along_z = 0.5 * (k + beyond(k, 1, 0)), 0.5 * (k + beyond(k, 1, 1))
        fx[i + 1] = along_x
        fy[i] = jnp.where(index_along(shape, 0) == rows - 1, 0.0, along_y)
        fz[i] = jnp.where(lane == lanes - 1, 0.0, along_z)
        back_y, back_z = 0.5 * (k + beyond(k, -1, 0)), 0.5 * (k + beyond(k, -1, 1))
        diag[i] = diag[i] + fx[i] + along_x + along_y + back_y + along_z + back_z
        total, square = carry
        for p, at in ((mine[i], c), (got[0, i], 1 - c)):
            part = count[i, pl.ds(base + cy * at, cy), :] * p
            total, square = total + folded(part), square + folded(part * p)
        return total, square

    zero = jnp.zeros((8, lanes), jnp.float32)
    sums[0], sums[1] = lax.fori_loop(0, planes, set_up, (zero, zero), unroll=4)


def halo_kernel(kap_table, abs_table, edge, kap, diag_in, fx_in, fy_in, fz_in, diag, fx, fy, fy_back, fz):
    _, _, y, _ = places(2)
    planes, rows, lanes = diag.shape
    for ref, old in ((diag, diag_in), (fx, fx_in), (fy, fy_in), (fz, fz_in)):
        ref[...] = old[...]
    shape = (HALO, lanes)
    lane, row = index_along(shape, 1), index_along(shape, 0)
    kap_row, abs_row = table_rows(kap_table, abs_table, shape)
    low = y == 0
    here = pl.ds((rows - HALO) * (1 - y), HALO)
    beside_it = pl.ds((rows - 2 * HALO) * (1 - y) + HALO * y, HALO)
    labels = [edge_tile(edge[1, i // GROUP], i % GROUP, y).astype(jnp.int32) for i in range(planes)]
    tiles = [jnp.take_along_axis(kap_row, at, axis=1) for at in labels]
    none = jnp.zeros(shape, jnp.float32)
    before = 0.5 * tiles[0]
    fx[0, here, :] = before
    for i, k in enumerate(tiles):
        after = 0.5 * (k + (tiles[i + 1] if i + 1 < planes else none))
        own = kap[i + 1, beside_it, :]
        up, down = shifted(k, -1, 0), shifted(k, 1, 0)
        k_up = jnp.where(row == HALO - 1, jnp.where(low, 0.0, shifted(own, -1, 0)), up)
        k_down = jnp.where(row == 0, jnp.where(low, shifted(own, 1, 0), 0.0), down)
        along_y, back_y = 0.5 * (k + k_up), 0.5 * (k + k_down)
        along_z, back_z = 0.5 * (k + beyond(k, 1, 1)), 0.5 * (k + beyond(k, -1, 1))
        fx[i + 1, here, :] = after
        fy[i, here, :] = jnp.where(low & (row == HALO - 1), 0.0, along_y)
        fz[i, here, :] = jnp.where(lane == lanes - 1, 0.0, along_z)
        absorb = jnp.take_along_axis(abs_row, labels[i], axis=1)
        diag[i, here, :] = absorb + before + after + along_y + back_y + along_z + back_z
        before = after
        face_up = jnp.where(low & (row == HALO - 1), 0.5 * up, 0.0)
        face_down = jnp.where(low | (row > 0), 0.0, 0.5 * down)
        fy[i, beside_it, :] = fy_in[i, beside_it, :] + face_up
        diag[i, beside_it, :] = diag_in[i, beside_it, :] + face_up + face_down

    def turn(i, carry):
        fy_back[i] = shifted(fy[i], 1, 0)
        return carry

    lax.fori_loop(0, planes, turn, 0, unroll=4)


def first_kernel(
    diag, fx, fy, fy_back, fz, count, sums, mine, got_photon, vector, got_vector, photon_edge, edge,
    phi, change, message,
    vk, va, b, buf_a, buf_b,
):
    _, _, y, c = places(2)
    planes, rows, lanes = change.shape
    cy = mine.shape[1]
    framed(phi, 1, mine, got_photon.at[0], photon_edge.at[0], y, c)
    framed(vk, 1, vector.at[0], got_vector.at[0], edge.at[0], y, c)
    framed(va, 0, vector.at[1], got_vector.at[1], edge.at[1], y, c)
    blank_ends(phi, vk)
    blank_rim(buf_a, buf_b)
    at = pl.ds(HALO, rows)
    theta, _ = chebyshev_scalars()

    def set_up(i, carry):
        v, p = vk[i + 1], phi[i + 1]
        total = 0.5 * (v + vk[i]) * (p - phi[i]) + 0.5 * (v + vk[i + 2]) * (p - phi[i + 2])
        for axis in range(2):
            flow = 0.5 * (v + beyond(v, 1, axis)) * (p - beyond(p, 1, axis))
            first = index_along(v.shape, axis) == 0
            total = total + flow + jnp.where(first, 0.5 * v * p, -shifted(flow, 1, axis))
        total = -(va[i] * p + total)
        b[i] = total
        buf_a[i + 1, at, :] = total * (1.0 / theta)
        return carry

    lax.fori_loop(0, planes, set_up, 0, unroll=4)
    found = solve(b, (buf_a, buf_b), diag, fx, fy, fy_back, fz, y, UNROLL)
    owned = owned_rows((rows, lanes), HALO * y, 2 * cy)

    def add_up(i, carry):
        u = found[i + 1, at, :]
        change[i] = u
        part = jnp.where(owned, count[i], 0.0) * u
        return carry[0] + folded(part), carry[1] + folded(part * phi[i + 1])

    zero = jnp.zeros((8, lanes), jnp.float32)
    seen, cross = lax.fori_loop(0, planes, add_up, (zero, zero), unroll=4)
    first = (2 * cy - HALO) * (1 - y) + HALO * y
    for g, part in enumerate((sums[0], seen, cross, sums[1])):
        message[g, pl.ds(0, GROUP * REACH), :] = packed_edges(
            [near_rows(found, 1 + GROUP * g + j, HALO + first, y) for j in range(GROUP)]
        )
        message[g, pl.ds(GROUP * REACH, 8), :] = part


def second_kernel(
    phi, change, diag, fx, fy, fy_back, fz, count, sent, came,
    own, message,
    b, buf_a, buf_b, grad_k, grad_a,
    *, dets,
):
    _, _, y, c = places(2)
    planes, rows, lanes = change.shape
    cy = (rows - HALO) // 2
    base = HALO * y
    edge = pl.ds(2 * cy * (1 - y), HALO)
    tail = pl.ds(GROUP * REACH, 8)
    total, seen_sum, cross, square = (
        jnp.sum(jnp.sum(sent[g, tail, :] + came[g, tail, :], axis=0, keepdims=True), axis=1, keepdims=True)
        for g in range(4)
    )
    mean = total / dets
    part = seen_sum / total
    level = (cross - part * square) / (total * mean)
    inverse = 1.0 / mean
    blank_rim(buf_a, buf_b)
    at = pl.ds(HALO, rows)
    theta, _ = chebyshev_scalars()

    def weighted(n, u, p):
        return n * (((u - p * part) * inverse - level) * inverse)

    def set_up(i, carry):
        value = weighted(count[i], change[i], phi[i + 1])
        b[i] = value
        buf_a[i + 1, at, :] = value * (1.0 / theta)
        return carry

    lax.fori_loop(0, planes, set_up, 0, unroll=4)
    for i in range(planes):
        u = edge_tile(came[i // GROUP], i % GROUP, y)
        value = weighted(count[i, edge, :], u, phi[i + 1, edge, :])
        b[i, edge, :] = value
        buf_a[i + 1, pl.ds(HALO + 2 * cy * (1 - y), HALO), :] = value * (1.0 / theta)
    dual = solve(b, (buf_a, buf_b), diag, fx, fy, fy_back, fz, y, UNROLL)

    def product(i, carry):
        p, u = phi[i + 1], dual[i + 1, at, :]
        grad = (p - phi[i]) * (u - dual[i, at, :]) + (p - phi[i + 2]) * (u - dual[i + 2, at, :])
        both = p * u
        for axis in range(2):
            flow = (p - beyond(p, 1, axis)) * (u - beyond(u, 1, axis))
            first = index_along(p.shape, axis) == 0
            grad = grad + flow + jnp.where(first, both, shifted(flow, 1, axis))
        grad_k[i] = -0.5 * grad
        grad_a[i] = -both
        for f, ref in enumerate((grad_k, grad_a)):
            own[f, i] = ref[i, pl.ds(base + cy * c, cy), :]
            message[f, i] = ref[i, pl.ds(base + cy * (1 - c), cy), :]
        return carry

    lax.fori_loop(0, planes, product, 0, unroll=4)


def packed_slabs(own, came, half, choices, outs):
    s, _, _, _ = places(2)
    _, planes, cy, lanes = own.shape
    n = planes // 2 // outs.shape[2]
    slab = lanes // n
    lane = index_along((cy, lanes), 1) // slab
    for f in range(2):
        for q in range(outs.shape[2]):
            at = planes // 2 * half + n * q
            parts = [own[f, at + j] + came[f, at + j] for j in range(n)]
            for i, k in enumerate(choices):
                to = s ^ k
                piece = jnp.zeros((cy, lanes), jnp.float32)
                for j in range(n):
                    moved = pltpu.roll(parts[j], ((j - to + n) % n) * slab, 1)
                    piece = jnp.where(lane == j, moved, piece)
                outs[i, f, q] = piece


def send_kernel(own, came, out, *, k):
    _, x, _, _ = places(2)
    packed_slabs(own, came, 1 - x, (k,), out)


def keep_kernel(own, came, kept):
    _, x, _, _ = places(2)
    packed_slabs(own, came, x, range(kept.shape[0]), kept)


def add_kernel(kept, came, out, *, k):
    out[...] = kept[k] + came[0]


def sum_kernel(*refs):
    total = refs[0][...]
    for ref in refs[1:-1]:
        total = total + ref[...]
    refs[-1][...] = total


def project_kernel(*refs, parts_n, n):
    beta_prev = refs[0]
    parts = refs[1 : 1 + parts_n]
    vk, va, qk, qa, w_k, w_a, tile = refs[1 + parts_n :]
    s, x, y, c = places(2)
    slab = 128 // n
    for f, (q_ref, w) in enumerate(((qk, w_k), (qa, w_a))):
        for q in range(vk.shape[0] // n):
            whole = sum(part[f, q] for part in parts[1:]) + parts[0][f, q]
            for j in range(n):
                i = n * q + j
                w[i] = whole[:, slab * j : slab * (j + 1)] - beta_prev[:, : vk.shape[2]] * q_ref[i]

    def dot(a, b):
        return jnp.sum(jnp.sum(a * b, axis=0))

    wk, wa, v_k, v_a = w_k[...], w_a[...], vk[...], va[...]
    one = jnp.ones((1, 1), jnp.float32)
    wv = (dot(wk, v_k) + dot(wa, v_a)) * one
    vv = (dot(v_k, v_k) + dot(v_a, v_a)) * one
    a = jnp.where(vv > 0.0, wv / jnp.where(vv > 0.0, vv, 1.0), 0.0)
    u_k, u_a = wk - a * v_k, wa - a * v_a
    uv = (dot(u_k, v_k) + dot(u_a, v_a)) * one
    uu = (dot(u_k, u_k) + dot(u_a, u_a)) * one
    me = ((s * 2 + x) * 2 + y) * 2 + c
    lane = index_along((8, 128), 1)
    row = index_along((8, 128), 0)
    values = jnp.zeros((8, 128), jnp.float32)
    for i, value in enumerate((wv, vv, a, uv, uu)):
        values = jnp.where(row == i, value, values)
    tile[...] = jnp.where(lane == me, values, 0.0)


def final_kernel(tiles, w_k, w_a, vk, va, next_k, next_a, coefs, *, cells):
    tile = jnp.sum(tiles[...], axis=0)
    wv, vv, a, uv, uu = (tile[i : i + 1] for i in range(5))
    wv_sum = jnp.sum(wv, axis=1, keepdims=True)
    vv_sum = jnp.sum(vv, axis=1, keepdims=True)
    alpha = wv_sum / cells / (vv_sum / cells + eps_norm)
    off = alpha - a
    rr = jnp.sum(uu - 2.0 * off * uv + off * off * vv, axis=1, keepdims=True)
    beta = jnp.sqrt(rr / cells + eps_norm)
    next_k[...] = (w_k[...] - alpha * vk[...]) / beta
    next_a[...] = (w_a[...] - alpha * va[...]) / beta
    coefs[0] = jnp.sum(alpha)
    coefs[1] = jnp.sum(beta)


def f32(*shape):
    return jax.ShapeDtypeStruct(shape, jnp.float32)


def run(kernel, outs, *args, after=(), scratch=(), copies=0, smem=(), hbm=(), mib=16, in_smem_out=(), cost=None):
    vmem = pl.BlockSpec(memory_space=pltpu.VMEM)
    scalar = pl.BlockSpec(memory_space=pltpu.SMEM)
    far = pl.BlockSpec(memory_space=pltpu.HBM)
    held = [pltpu.VMEM(shape, dtype) for shape, dtype in scratch]
    used, waits = len(args), len(after)

    def body(*refs):
        kernel(*refs[:used], *refs[used + waits :])

    args = (*args, *after)
    if copies:
        held.append(pltpu.SemaphoreType.DMA((copies,)))
    return pl.pallas_call(
        body if waits else kernel,
        out_shape=tuple(outs),
        in_specs=[scalar if i in smem else far if i in hbm else vmem for i in range(len(args))],
        out_specs=tuple(scalar if i in in_smem_out else vmem for i in range(len(outs))),
        scratch_shapes=held,
        compiler_params=pltpu.CompilerParams(vmem_limit_bytes=mib * 2**20),
        cost_estimate=cost,
    )(*args)


HALO = 8
UNROLL = 16
REACH = 6
GROUP = 4


def per_device_paired(
    labels, kappa_table, absorb_table, background, det_cells,
    v_kappa, v_absorb, q_kappa, q_absorb, beta_prev,
):
    sources, cx, cy, cz = background.shape
    n = lax.axis_size("src")
    planes, rows = 2 * cx, 2 * cy + HALO
    ny = cy * lax.axis_size("gy")
    dets = det_cells.shape[0]
    cells = planes * ny * cz
    groups = cx // n

    def swap_x(value):
        return lax.ppermute(value, "gx", [(0, 1), (1, 0)])

    def swap_core(value):
        return lax.ppermute(value, "gy", [(0, 1), (1, 0), (2, 3), (3, 2)])

    def along_z(value, k):
        return lax.ppermute(value, "src", [(i, i ^ k) for i in range(n)])

    block = (cx, cy, cz)
    float_block = lambda *shape: (shape, jnp.float32)
    raw_labels = (block, jnp.int32)
    packed, message = run(
        pack_kernel, (f32(2 * groups, cy, cz), f32((sources // 2 + 1) * cx + 2 * groups, cy, cz)),
        background, labels, v_kappa, v_absorb, hbm=(0, 1, 2, 3),
        scratch=(raw_labels, float_block(2, *v_kappa.shape)), copies=3 + sources // 2, mib=60,
    )
    long = pl.CostEstimate(flops=10**9, bytes_accessed=2**26, transcendentals=0)
    came = swap_x(message)
    slabs = [along_z(packed, k) for k in range(1, n)]
    count, beta_row = run(
        functools.partial(count_kernel, ny=ny, nz=cz, half=2 * cy, halo=HALO),
        (f32(planes, rows, cz), f32(1, cz)), det_cells.reshape(1, dets), beta_prev, smem=(1,),
        cost=pl.CostEstimate(flops=2 * planes * rows * cz * dets, bytes_accessed=planes * rows * cz * 4, transcendentals=0),
    )

    def across_y(value):
        return lax.ppermute(value, "gy", [(i, (i + 2) % 4) for i in range(4)])

    (joined,) = run(join_kernel, (f32(2 * groups * (n - 1), cy, cz),), *slabs, after=(count,))
    joined_came = swap_x(joined)
    (half_vector,) = run(own_half_kernel, (f32(2, *block),), v_kappa, v_absorb, joined)
    mine, fields = run(
        photon_kernel, (f32(planes, cy, cz), f32(2, planes, cy, cz)),
        background, labels, came, after=(joined,), hbm=(0, 1), scratch=(raw_labels,), copies=3,
    )
    got = swap_core(fields)
    (vector,) = run(
        vector_kernel, (f32(2, planes, cy, cz),), half_vector, came, joined_came, after=(mine,)
    )
    edge = (f32(2, *edge_shape(planes, cz)),)
    (sent,) = run(photon_edge_kernel, edge, mine, fields, got, after=(vector,))
    photon_edge = across_y(sent)
    vector_got = swap_core(vector)
    (vector_sent,) = run(vector_edge_kernel, edge, vector, vector_got, after=(sent,))
    frame, wide = (planes, rows, cz), (planes + 2, rows, cz)
    float_frame, float_wide = float_block(*frame), float_block(*wide)
    rimmed = float_block(planes + 2, rows + 2 * HALO, cz)
    coefs = (f32(*frame), f32(planes + 1, rows, cz), f32(*frame), f32(*frame))
    kap, *partial, sums = run(
        stencil_kernel, (f32(*wide), *coefs, f32(2, 8, cz)),
        kappa_table, absorb_table, mine, fields, got, count, after=(vector_sent,), cost=long,
        smem=(0, 1), scratch=(float_frame,),
    )
    diag, fx, fy, fy_back, fz = run(
        halo_kernel, (*coefs[:3], f32(*frame), coefs[3]), kappa_table, absorb_table, photon_edge, kap, *partial, smem=(0, 1)
    )
    phi, change, sent = run(
        first_kernel, (f32(*wide), f32(*frame), f32(4, GROUP * REACH + 8, cz)),
        diag, fx, fy, fy_back, fz, count, sums, mine, got, vector, vector_got,
        photon_edge, across_y(vector_sent),
        scratch=(float_wide, float_frame, float_frame, rimmed, rimmed),
    )
    heard = across_y(sent)
    own, message = run(
        functools.partial(second_kernel, dets=dets),
        (f32(2, planes, cy, cz), f32(2, planes, cy, cz)),
        phi, change, diag, fx, fy, fy_back, fz, count, sent, heard,
        scratch=(float_frame, rimmed, rimmed, float_frame, float_frame),
    )
    piece = f32(2, groups, cy, cz)
    got = swap_core(message)
    crossed, last = {}, ()
    for k in reversed(range(n)):
        last = run(functools.partial(send_kernel, k=k), (f32(1, *piece.shape),), own, got, after=last)
        crossed[k] = swap_x(last[0])
    (kept,) = run(keep_kernel, (f32(n, *piece.shape),), own, got, after=last)
    totals = {
        k: run(functools.partial(add_kernel, k=k), (piece,), kept, value)[0] for k, value in crossed.items()
    }
    received = {k: along_z(totals[k], k) for k in reversed(range(1, n))}
    (distant,) = run(sum_kernel, (piece,), *(received[k] for k in range(n // 2, n)), cost=long)
    parts = [distant, totals[0]] + [received[k] for k in range(1, n // 2)]
    w_k, w_a, tile = run(
        functools.partial(project_kernel, parts_n=len(parts), n=n),
        (f32(*v_kappa.shape), f32(*v_kappa.shape), f32(8, 128)),
        beta_row, *parts, v_kappa, v_absorb, q_kappa, q_absorb,
    )
    everyone = ("src", "gx", "gy")
    tiles = lax.all_to_all(jnp.broadcast_to(tile, (8 * n, 8, 128)), everyone, 0, 0)
    return tuple(run(
        functools.partial(final_kernel, cells=cells),
        (f32(*v_kappa.shape), f32(*v_kappa.shape), f32(2)),
        tiles, w_k, w_a, v_kappa, v_absorb, in_smem_out=(2,),
    ))


def paired_fits(mesh):
    return mesh.shape["gx"] == 2 and mesh.shape["gy"] == 4


def body_for(mesh):
    if not paired_fits(mesh):
        return per_device

    def chosen(*args):
        sources, cx, cy, cz = args[3].shape
        n = lax.axis_size("src")
        fits = sources == 4 and cz == 128 and cx % n == 0 and cx % GROUP == 0 and cy % HALO == 0 and n > 1 and n & (n - 1) == 0
        devices = 8 * n
        return (per_device_paired if fits and devices <= 128 else per_device)(*args)

    return chosen


def solution(mesh):
    return jax.shard_map(
        body_for(mesh),
        mesh=mesh,
        in_specs=(
            P("gx", "gy", None),
            P(),
            P(),
            P("src", "gx", "gy", None),
            P(),
            P("gx", "gy", "src"),
            P("gx", "gy", "src"),
            P("gx", "gy", "src"),
            P("gx", "gy", "src"),
            P(),
        ),
        out_specs=(P("gx", "gy", "src"), P("gx", "gy", "src"), P()),
        check_vma=False,
    )
```

```python
import functools

import jax
import jax.numpy as jnp
from jax import lax
from jax.experimental import pallas as pl
from jax.experimental.pallas import tpu as pltpu
from jax.sharding import PartitionSpec as P

ITERS = 6


lam_low = 0.02
lam_high = 24.1
eps_norm = 1e-06


def padded_2(block, sides, width):
    for axis, dim in sides:
        count = lax.axis_size(axis)
        forward = [(i, i + 1) for i in range(count - 1)]
        backward = [(target, source) for source, target in forward]
        low = lax.ppermute(
            lax.slice_in_dim(block, block.shape[dim] - width, None, axis=dim), axis, forward
        )
        high = lax.ppermute(lax.slice_in_dim(block, 0, width, axis=dim), axis, backward)
        block = jnp.concatenate([low, block, high], axis=dim)
    return block


def regional(labels, table):
    field = jnp.zeros(labels.shape, jnp.float32)
    for region in range(table.shape[0]):
        field = field + jnp.where(labels == region, table[region], 0.0)
    return field


def beside(padded):
    widths = [(0, 0)] * (padded.ndim - 1) + [(1, 1)]
    full = jnp.pad(padded, widths)
    return [
        full[..., 2:, 1:-1, 1:-1],
        full[..., :-2, 1:-1, 1:-1],
        full[..., 1:-1, 2:, 1:-1],
        full[..., 1:-1, :-2, 1:-1],
        full[..., 1:-1, 1:-1, 2:],
        full[..., 1:-1, 1:-1, :-2],
    ]


def chebyshev(rhs, apply_op):
    theta = 0.5 * (lam_high + lam_low)
    delta = 0.5 * (lam_high - lam_low)
    sigma = theta / delta
    rho = 1.0 / sigma
    solution = jnp.zeros_like(rhs)
    remain = rhs
    step_dir = rhs / theta
    for step in range(ITERS):
        solution = solution + step_dir
        if step + 1 < ITERS:
            remain = remain - apply_op(step_dir)
            rho_next = 1.0 / (2.0 * sigma - rho)
            step_dir = rho_next * rho * step_dir + 2.0 * rho_next / delta * remain
            rho = rho_next
    return solution


def per_device(
    labels,
    kappa_table,
    absorb_table,
    background,
    det_cells,
    v_kappa,
    v_absorb,
    q_kappa,
    q_absorb,
    beta_prev,
):
    sources, cx, cy, cz = background.shape
    kappa = regional(labels, kappa_table)
    absorb = regional(labels, absorb_table)
    full_k, full_a = (
        lax.all_gather(v_kappa, "src", axis=2, tiled=True),
        lax.all_gather(v_absorb, "src", axis=2, tiled=True),
    )
    stacked = jnp.concatenate([background, kappa[None], full_k[None]], axis=0)
    rims = padded_2(stacked, (("gx", 1), ("gy", 2)), 1)
    near_all = beside(rims)
    kappa_faces = [0.5 * (kappa + near[sources]) for near in near_all]
    vk_faces = [0.5 * (full_k + near[sources + 1]) for near in near_all]
    phi_near = [near[:sources] for near in near_all]

    def apply_op(field):
        padded = padded_2(field, (("gx", 1), ("gy", 2)), 1)
        result = absorb * field
        for face, near in zip(kappa_faces, beside(padded)):
            result = result + face * (field - near)
        return result

    rhs = full_a * background
    for face, near in zip(vk_faces, phi_near):
        rhs = rhs + face * (background - near)
    rhs = -rhs
    change = chebyshev(rhs, apply_op)
    span_y = cy * lax.axis_size("gy")
    ix = det_cells // (span_y * cz)
    iy = det_cells // cz % span_y
    iz = det_cells % cz
    anchor_x = lax.axis_index("gx") * cx
    anchor_y = lax.axis_index("gy") * cy
    owned = (ix >= anchor_x) & (ix < anchor_x + cx) & (iy >= anchor_y) & (iy < anchor_y + cy)
    local = jnp.where(owned, ((ix - anchor_x) * cy + (iy - anchor_y)) * cz + iz, 0)
    seen_part = jnp.where(owned[None, :], change.reshape(sources, -1)[:, local], 0.0)
    base_part = jnp.where(owned[None, :], background.reshape(sources, -1)[:, local], 0.0)
    seen, base = lax.psum((seen_part, base_part), ("gx", "gy"))
    total = jnp.sum(base, axis=1, keepdims=True)
    mean_base = total / det_cells.shape[0]
    ratio = base / total
    jv_vals = (seen - ratio * jnp.sum(seen, axis=1, keepdims=True)) / mean_base
    weight = (jv_vals - jnp.sum(ratio * jv_vals, axis=1, keepdims=True)) / mean_base
    deposit = jnp.where(owned[None, :], weight, 0.0)
    source = (
        jnp.zeros((sources, cx * cy * cz), jnp.float32)
        .at[:, local]
        .add(deposit)
        .reshape(change.shape)
    )
    dual = chebyshev(source, apply_op)
    dual_rims = padded_2(dual, (("gx", 1), ("gy", 2)), 1)
    grad_a = -jnp.sum(background * dual, axis=0)
    grad_k = jnp.zeros_like(kappa)
    for near_phi, near_dual in zip(phi_near, beside(dual_rims)):
        grad_k = grad_k - 0.5 * jnp.sum((background - near_phi) * (dual - near_dual), axis=0)
    summed_k, summed_a = lax.psum((grad_k, grad_a), "src")
    slab = v_kappa.shape[2]
    offset = lax.axis_index("src") * slab
    hv_k = lax.dynamic_slice_in_dim(summed_k, offset, slab, 2)
    hv_a = lax.dynamic_slice_in_dim(summed_a, offset, slab, 2)
    cell_count = cx * lax.axis_size("gx") * cy * lax.axis_size("gy") * cz
    w_k = hv_k - beta_prev[0] * q_kappa
    w_a = hv_a - beta_prev[0] * q_absorb
    local_wv = jnp.sum(w_k * v_kappa) + jnp.sum(w_a * v_absorb)
    local_vv = jnp.sum(v_kappa * v_kappa) + jnp.sum(v_absorb * v_absorb)
    wv_sum, vv_sum = lax.psum((local_wv, local_vv), ("src", "gx", "gy"))
    alpha = wv_sum / cell_count / (vv_sum / cell_count + eps_norm)
    r_k = w_k - alpha * v_kappa
    r_a = w_a - alpha * v_absorb
    rr_sum = lax.psum(jnp.sum(r_k * r_k) + jnp.sum(r_a * r_a), ("src", "gx", "gy"))
    beta = jnp.sqrt(rr_sum / cell_count + eps_norm)
    return (r_k / beta, r_a / beta, jnp.stack([alpha, beta]))


def chebyshev_scalars():
    theta = 0.5 * (lam_high + lam_low)
    delta = 0.5 * (lam_high - lam_low)
    sigma = theta / delta
    rho = 1.0 / sigma
    pairs = []
    for _ in range(ITERS - 1):
        rho_next = 1.0 / (2.0 * sigma - rho)
        pairs.append((rho_next * rho, 2.0 * rho_next / delta))
        rho = rho_next
    return theta, pairs


def places(split):
    g = lax.axis_index("gy")
    return lax.axis_index("src"), lax.axis_index("gx"), g // split, g % split


def shifted(value, step, axis):
    return pltpu.roll(value, step % value.shape[axis], axis)


def index_along(shape, axis):
    return lax.broadcasted_iota(jnp.int32, shape, axis)


def beyond(value, step, axis):
    size = value.shape[axis]
    at = index_along(value.shape, axis)
    edge = size - 1 if step == 1 else 0
    return jnp.where(at == edge, 0.0, shifted(value, -step, axis))


def packed_planes(ref, q):
    per = 128 // ref.shape[2]
    return jnp.concatenate([ref[per * q + j] for j in range(per)], axis=1)


def pack_kernel(bg, labels, vk, va, packed, message, raw, v_in, sems):
    _, x, _, _ = places(2)
    half = bg.shape[0] // 2
    cx = labels.shape[0]
    copies = [
        pltpu.make_async_copy(src, dst, sems.at[i])
        for i, (src, dst) in enumerate((
            (vk, v_in.at[0]),
            (va, v_in.at[1]),
            (labels, raw),
            *((bg.at[half * (1 - x) + i], message.at[pl.ds(cx * i, cx)]) for i in range(half)),
        ))
    ]
    for copy in copies:
        copy.start()
    groups = packed.shape[0] // 2
    for f in range(2):
        copies[f].wait()
        for q in range(groups):
            planes = packed_planes(v_in.at[f], q)
            packed[groups * f + q] = planes
            message[cx * (half + 1) + groups * f + q] = planes
    copies[2].wait()
    message[pl.ds(cx * half, cx)] = raw[...].astype(jnp.float32)
    for copy in copies[3:]:
        copy.wait()


def count_kernel(dets, beta_prev, count, beta_row, *, ny, nz, half, halo):
    beta_row[...] = jnp.full(beta_row.shape, beta_prev[0])
    _, _, y, _ = places(2)
    planes, rows, _ = count.shape
    flat = dets[...]
    iz = flat % nz
    line = flat // nz
    iy = line % ny
    ix = line // ny
    row = iy - (half - halo) * y
    spot = jnp.where((row >= 0) & (row < rows), ix * rows + row, -1)
    dets_n = flat.shape[1]
    at_z = (index_along((nz, dets_n), 0) == iz).astype(jnp.float32).astype(jnp.bfloat16)

    def body(i, carry):
        here = index_along((2 * rows, dets_n), 0) + i * (2 * rows)
        hot = (here == spot).astype(jnp.float32).astype(jnp.bfloat16)
        found = lax.dot_general(hot, at_z, (((1,), (1,)), ((), ())), preferred_element_type=jnp.float32)
        count[pl.ds(2 * i, 2)] = found.reshape(2, rows, nz)
        return carry

    lax.fori_loop(0, planes // 2, body, 0)


def photon_kernel(bg, labels, msg, mine, fields, raw, sems):
    _, x, _, c = places(2)
    half = bg.shape[0] // 2
    cx = labels.shape[0]
    here, there = cx * x, cx * (1 - x)
    copies = [
        pltpu.make_async_copy(src, dst, sems.at[i])
        for i, (src, dst) in enumerate((
            (bg.at[half * x + c], mine.at[pl.ds(here, cx)]),
            (bg.at[half * x + 1 - c], fields.at[0, pl.ds(here, cx)]),
            (labels, raw),
        ))
    ]
    for copy in copies:
        copy.start()
    mine[pl.ds(there, cx)] = msg[pl.ds(cx * c, cx)]
    fields[0, pl.ds(there, cx)] = msg[pl.ds(cx * (1 - c), cx)]
    fields[1, pl.ds(there, cx)] = msg[pl.ds(cx * half, cx)]
    for copy in copies:
        copy.wait()
    fields[1, pl.ds(here, cx)] = raw[...].astype(jnp.float32)


def unpacked(blocks, groups, s, store):
    n = len(blocks)
    cy, lanes = blocks[0][0].shape
    slab = lanes // n
    lane = index_along((cy, lanes), 1) // slab
    for f in range(2):
        for q in range(groups):
            values = [block[groups * f + q] for block in blocks]
            for j in range(n):
                plane = jnp.zeros((cy, lanes), jnp.float32)
                for k in range(n):
                    home = s ^ k
                    moved = pltpu.roll(values[k], ((home - j + n) % n) * slab, 1)
                    plane = jnp.where(lane == home, moved, plane)
                store(f, n * q + j, plane)


def join_kernel(*refs):
    joined, size = refs[-1], refs[0].shape[0]
    for i, ref in enumerate(refs[:-1]):
        joined[pl.ds(size * i, size)] = ref[...]


def own_half_kernel(vk, va, joined, half):
    s, _, _, _ = places(2)
    size = half.shape[1]
    groups = joined.shape[0] // 2 // (128 // vk.shape[2] - 1)
    n = size // groups
    own = [packed_planes(ref, q) for ref in (vk, va) for q in range(groups)]
    blocks = [own] + [[joined[2 * groups * k + i] for i in range(2 * groups)] for k in range(n - 1)]

    def store(f, i, plane):
        half[f, i] = plane

    unpacked(blocks, groups, s, store)


def vector_kernel(half, msg, joined, fields):
    s, x, _, _ = places(2)
    cx = half.shape[1]
    fields[:, pl.ds(cx * x, cx)] = half[...]
    n = lax.axis_size("src")
    groups = cx // n
    own = msg.shape[0] - 2 * groups
    blocks = [[msg[own + i] for i in range(2 * groups)]]
    blocks += [[joined[2 * groups * k + i] for i in range(2 * groups)] for k in range(n - 1)]
    there = cx * (1 - x)

    def store(f, i, plane):
        fields[f, there + i] = plane

    unpacked(blocks, groups, s, store)


def edge_shape(planes, lanes):
    return planes // GROUP, GROUP * REACH, lanes


def packed_edges(tiles):
    return jnp.concatenate([tile[:REACH] for tile in tiles], axis=0)


def edge_tile(packed, j, y):
    rows = packed[REACH * j : REACH * (j + 1)]
    tile = jnp.concatenate([rows, jnp.zeros((HALO - REACH, rows.shape[1]), jnp.float32)], axis=0)
    return jnp.where(y == 0, tile, shifted(tile, HALO - REACH, 0))


def near_rows(ref, i, first, y):
    tile = ref[i, pl.ds(first, HALO), :]
    return jnp.where(y == 0, shifted(tile, REACH - HALO, 0), tile)


def edges_of(own, got, edge, y, c):
    first = (own.shape[1] - HALO) * (1 - y)
    for g in range(edge.shape[0]):
        edge[g] = packed_edges([
            jnp.where(c != y, near_rows(own, GROUP * g + j, first, y), near_rows(got, GROUP * g + j, first, y))
            for j in range(GROUP)
        ])


def photon_edge_kernel(mine, fields, got, edge):
    _, _, y, c = places(2)
    edges_of(mine, got.at[0], edge.at[0], y, c)
    edges_of(fields.at[1], got.at[1], edge.at[1], y, c)


def vector_edge_kernel(fields, got, edge):
    _, _, y, c = places(2)
    for f in range(2):
        edges_of(fields.at[f], got.at[f], edge.at[f], y, c)


def solve(b, bufs, diag, fx, fy, fz, unroll):
    planes = b.shape[0]
    _, pairs = chebyshev_scalars()
    for step, (keep, push) in enumerate(pairs):
        src, dst = bufs[step % 2], bufs[(step + 1) % 2]

        def body(i, carry):
            u = src[i + 1]
            coef_y, coef_z = fy[i], fz[i]
            left = b[i] - diag[i] * u
            left = left + fx[i] * src[i] + fx[i + 1] * src[i + 2]
            left = left + coef_y * shifted(u, -1, 0) + shifted(coef_y * u, 1, 0)
            left = left + coef_z * shifted(u, -1, 1) + shifted(coef_z * u, 1, 1)
            change = u if step == 0 else u - dst[i + 1]
            dst[i + 1] = u + keep * change + push * left
            return carry

        lax.fori_loop(0, planes, body, 0, unroll=unroll)
    return bufs[len(pairs) % 2]


def folded(value):
    return jnp.sum(value.reshape(-1, 8, value.shape[1]), axis=0)


def framed_own(ref, shift, own, got, y, c):
    planes, cy, _ = own.shape
    there = pl.ds(shift, planes)
    base = HALO * y
    ref[there, pl.ds(base + cy * c, cy), :] = own[...]
    ref[there, pl.ds(base + cy * (1 - c), cy), :] = got[...]


def framed(ref, shift, own, got, edge, y, c):
    framed_own(ref, shift, own, got, y, c)
    cy = own.shape[1]
    for g in range(edge.shape[0]):
        packed = edge[g]
        for j in range(GROUP):
            ref[shift + GROUP * g + j, pl.ds(2 * cy * (1 - y), HALO), :] = edge_tile(packed, j, y)


def blank_ends(*refs):
    for ref in refs:
        blank = jnp.zeros(ref.shape[1:], jnp.float32)
        ref[0] = blank
        ref[ref.shape[0] - 1] = blank


def owned_rows(shape, base, count):
    at_row = index_along(shape, 0)
    return (at_row >= base) & (at_row < base + count)


def table_rows(kap_table, abs_table, shape):
    lane = index_along(shape, 1)
    kap_row = abs_row = jnp.zeros(shape, jnp.float32)
    for region in range(kap_table.shape[0]):
        kap_row = jnp.where(lane == region, kap_table[region], kap_row)
        abs_row = jnp.where(lane == region, abs_table[region], abs_row)
    return kap_row, abs_row


def stencil_kernel(
    kap_table, abs_table, mine, fields, got, count,
    kap, diag, fx, fy, fz, sums,
    labels,
):
    _, _, y, c = places(2)
    planes, cy, lanes = mine.shape
    rows = 2 * cy + HALO
    base = HALO * y
    framed_own(labels, 0, fields.at[1], got.at[1], y, c)
    labels[:, pl.ds(2 * cy * (1 - y), HALO), :] = jnp.zeros((planes, HALO, lanes), jnp.float32)
    blank_ends(kap)
    shape = (rows, lanes)
    lane = index_along(shape, 1)
    kap_row, abs_row = table_rows(kap_table, abs_table, shape)
    owned = owned_rows(shape, base, 2 * cy)

    def look_up(i, carry):
        at = labels[i].astype(jnp.int32)
        kap[i + 1] = jnp.where(owned, jnp.take_along_axis(kap_row, at, axis=1), 0.0)
        diag[i] = jnp.take_along_axis(abs_row, at, axis=1)
        return carry

    lax.fori_loop(0, planes, look_up, 0, unroll=4)
    fx[0] = 0.5 * kap[1]

    def set_up(i, carry):
        k = kap[i + 1]
        along_x = 0.5 * (k + kap[i + 2])
        along_y, along_z = 0.5 * (k + beyond(k, 1, 0)), 0.5 * (k + beyond(k, 1, 1))
        fx[i + 1] = along_x
        fy[i] = jnp.where(index_along(shape, 0) == rows - 1, 0.0, along_y)
        fz[i] = jnp.where(lane == lanes - 1, 0.0, along_z)
        back_y, back_z = 0.5 * (k + beyond(k, -1, 0)), 0.5 * (k + beyond(k, -1, 1))
        diag[i] = diag[i] + fx[i] + along_x + along_y + back_y + along_z + back_z
        total, square = carry
        for p, at in ((mine[i], c), (got[0, i], 1 - c)):
            part = count[i, pl.ds(base + cy * at, cy), :] * p
            total, square = total + folded(part), square + folded(part * p)
        return total, square

    zero = jnp.zeros((8, lanes), jnp.float32)
    sums[0], sums[1] = lax.fori_loop(0, planes, set_up, (zero, zero), unroll=4)


def halo_kernel(kap_table, abs_table, edge, kap, diag_in, fx_in, fy_in, fz_in, diag, fx, fy, fz):
    _, _, y, _ = places(2)
    planes, rows, lanes = diag.shape
    for ref, old in ((diag, diag_in), (fx, fx_in), (fy, fy_in), (fz, fz_in)):
        ref[...] = old[...]
    shape = (HALO, lanes)
    lane, row = index_along(shape, 1), index_along(shape, 0)
    kap_row, abs_row = table_rows(kap_table, abs_table, shape)
    low = y == 0
    here = pl.ds((rows - HALO) * (1 - y), HALO)
    beside_it = pl.ds((rows - 2 * HALO) * (1 - y) + HALO * y, HALO)
    labels = [edge_tile(edge[1, i // GROUP], i % GROUP, y).astype(jnp.int32) for i in range(planes)]
    tiles = [jnp.take_along_axis(kap_row, at, axis=1) for at in labels]
    none = jnp.zeros(shape, jnp.float32)
    before = 0.5 * tiles[0]
    fx[0, here, :] = before
    for i, k in enumerate(tiles):
        after = 0.5 * (k + (tiles[i + 1] if i + 1 < planes else none))
        own = kap[i + 1, beside_it, :]
        up, down = shifted(k, -1, 0), shifted(k, 1, 0)
        k_up = jnp.where(row == HALO - 1, jnp.where(low, 0.0, shifted(own, -1, 0)), up)
        k_down = jnp.where(row == 0, jnp.where(low, shifted(own, 1, 0), 0.0), down)
        along_y, back_y = 0.5 * (k + k_up), 0.5 * (k + k_down)
        along_z, back_z = 0.5 * (k + beyond(k, 1, 1)), 0.5 * (k + beyond(k, -1, 1))
        fx[i + 1, here, :] = after
        fy[i, here, :] = jnp.where(low & (row == HALO - 1), 0.0, along_y)
        fz[i, here, :] = jnp.where(lane == lanes - 1, 0.0, along_z)
        absorb = jnp.take_along_axis(abs_row, labels[i], axis=1)
        diag[i, here, :] = absorb + before + after + along_y + back_y + along_z + back_z
        before = after
        face_up = jnp.where(low & (row == HALO - 1), 0.5 * up, 0.0)
        face_down = jnp.where(low | (row > 0), 0.0, 0.5 * down)
        fy[i, beside_it, :] = fy_in[i, beside_it, :] + face_up
        diag[i, beside_it, :] = diag_in[i, beside_it, :] + face_up + face_down


def first_kernel(
    diag, fx, fy, fz, count, sums, mine, got_photon, vector, got_vector, photon_edge, edge,
    phi, change, message,
    vk, va, b, buf_a, buf_b,
):
    _, _, y, c = places(2)
    planes, rows, lanes = change.shape
    cy = mine.shape[1]
    framed(phi, 1, mine, got_photon.at[0], photon_edge.at[0], y, c)
    framed(vk, 1, vector.at[0], got_vector.at[0], edge.at[0], y, c)
    framed(va, 0, vector.at[1], got_vector.at[1], edge.at[1], y, c)
    blank_ends(phi, vk, buf_a, buf_b)
    theta, _ = chebyshev_scalars()

    def set_up(i, carry):
        v, p = vk[i + 1], phi[i + 1]
        total = 0.5 * (v + vk[i]) * (p - phi[i]) + 0.5 * (v + vk[i + 2]) * (p - phi[i + 2])
        for axis in range(2):
            flow = 0.5 * (v + beyond(v, 1, axis)) * (p - beyond(p, 1, axis))
            first = index_along(v.shape, axis) == 0
            total = total + flow + jnp.where(first, 0.5 * v * p, -shifted(flow, 1, axis))
        total = -(va[i] * p + total)
        b[i] = total
        buf_a[i + 1] = total * (1.0 / theta)
        return carry

    lax.fori_loop(0, planes, set_up, 0, unroll=4)
    found = solve(b, (buf_a, buf_b), diag, fx, fy, fz, UNROLL)
    owned = owned_rows((rows, lanes), HALO * y, 2 * cy)

    def add_up(i, carry):
        u = found[i + 1]
        change[i] = u
        part = jnp.where(owned, count[i], 0.0) * u
        return carry[0] + folded(part), carry[1] + folded(part * phi[i + 1])

    zero = jnp.zeros((8, lanes), jnp.float32)
    seen, cross = lax.fori_loop(0, planes, add_up, (zero, zero), unroll=4)
    first = (2 * cy - HALO) * (1 - y) + HALO * y
    for g, part in enumerate((sums[0], seen, cross, sums[1])):
        message[g, pl.ds(0, GROUP * REACH), :] = packed_edges(
            [near_rows(found, 1 + GROUP * g + j, first, y) for j in range(GROUP)]
        )
        message[g, pl.ds(GROUP * REACH, 8), :] = part


def second_kernel(
    phi, change, diag, fx, fy, fz, count, sent, came,
    own, message,
    b, buf_a, buf_b, grad_k, grad_a,
    *, dets,
):
    _, _, y, c = places(2)
    planes, rows, lanes = change.shape
    cy = (rows - HALO) // 2
    base = HALO * y
    edge = pl.ds(2 * cy * (1 - y), HALO)
    tail = pl.ds(GROUP * REACH, 8)
    total, seen_sum, cross, square = (
        jnp.sum(jnp.sum(sent[g, tail, :] + came[g, tail, :], axis=0, keepdims=True), axis=1, keepdims=True)
        for g in range(4)
    )
    mean = total / dets
    part = seen_sum / total
    level = (cross - part * square) / (total * mean)
    inverse = 1.0 / mean
    blank_ends(buf_a, buf_b)
    theta, _ = chebyshev_scalars()

    def weighted(n, u, p):
        return n * (((u - p * part) * inverse - level) * inverse)

    def set_up(i, carry):
        value = weighted(count[i], change[i], phi[i + 1])
        b[i] = value
        buf_a[i + 1] = value * (1.0 / theta)
        return carry

    lax.fori_loop(0, planes, set_up, 0, unroll=4)
    for i in range(planes):
        u = edge_tile(came[i // GROUP], i % GROUP, y)
        value = weighted(count[i, edge, :], u, phi[i + 1, edge, :])
        b[i, edge, :] = value
        buf_a[i + 1, edge, :] = value * (1.0 / theta)
    dual = solve(b, (buf_a, buf_b), diag, fx, fy, fz, UNROLL)

    def product(i, carry):
        p, u = phi[i + 1], dual[i + 1]
        grad = (p - phi[i]) * (u - dual[i]) + (p - phi[i + 2]) * (u - dual[i + 2])
        both = p * u
        for axis in range(2):
            flow = (p - beyond(p, 1, axis)) * (u - beyond(u, 1, axis))
            first = index_along(p.shape, axis) == 0
            grad = grad + flow + jnp.where(first, both, shifted(flow, 1, axis))
        grad_k[i] = -0.5 * grad
        grad_a[i] = -both
        for f, ref in enumerate((grad_k, grad_a)):
            own[f, i] = ref[i, pl.ds(base + cy * c, cy), :]
            message[f, i] = ref[i, pl.ds(base + cy * (1 - c), cy), :]
        return carry

    lax.fori_loop(0, planes, product, 0, unroll=4)


def packed_slabs(own, came, half, choices, outs):
    s, _, _, _ = places(2)
    _, planes, cy, lanes = own.shape
    n = planes // 2 // outs.shape[2]
    slab = lanes // n
    lane = index_along((cy, lanes), 1) // slab
    for f in range(2):
        for q in range(outs.shape[2]):
            at = planes // 2 * half + n * q
            parts = [own[f, at + j] + came[f, at + j] for j in range(n)]
            for i, k in enumerate(choices):
                to = s ^ k
                piece = jnp.zeros((cy, lanes), jnp.float32)
                for j in range(n):
                    moved = pltpu.roll(parts[j], ((j - to + n) % n) * slab, 1)
                    piece = jnp.where(lane == j, moved, piece)
                outs[i, f, q] = piece


def send_kernel(own, came, out, *, k):
    _, x, _, _ = places(2)
    packed_slabs(own, came, 1 - x, (k,), out)


def keep_kernel(own, came, kept):
    _, x, _, _ = places(2)
    packed_slabs(own, came, x, range(kept.shape[0]), kept)


def add_kernel(kept, came, out, *, k):
    out[...] = kept[k] + came[0]


def sum_kernel(*refs):
    total = refs[0][...]
    for ref in refs[1:-1]:
        total = total + ref[...]
    refs[-1][...] = total


def project_kernel(*refs, parts_n, n):
    beta_prev = refs[0]
    parts = refs[1 : 1 + parts_n]
    vk, va, qk, qa, w_k, w_a, tile = refs[1 + parts_n :]
    slab = 128 // n
    for f, (q_ref, w) in enumerate(((qk, w_k), (qa, w_a))):
        for q in range(vk.shape[0] // n):
            whole = sum(part[f, q] for part in parts[1:]) + parts[0][f, q]
            for j in range(n):
                i = n * q + j
                w[i] = whole[:, slab * j : slab * (j + 1)] - beta_prev[:, : vk.shape[2]] * q_ref[i]

    def total(value):
        return jnp.sum(jnp.sum(jnp.sum(value, axis=0), axis=0, keepdims=True), axis=1, keepdims=True)

    wk, wa, v_k, v_a = w_k[...], w_a[...], vk[...], va[...]
    wv = total(wk * v_k + wa * v_a)
    vv = total(v_k * v_k + v_a * v_a)
    a = jnp.where(vv > 0.0, wv / jnp.where(vv > 0.0, vv, 1.0), 0.0)
    u_k, u_a = wk - a * v_k, wa - a * v_a
    uv = total(u_k * v_k + u_a * v_a)
    uu = total(u_k * u_k + u_a * u_a)
    lane = index_along((1, 128), 1)
    values = jnp.zeros((1, 128), jnp.float32)
    for i, value in enumerate((wv, vv, a, uv, uu)):
        values = jnp.where(lane == i, value, values)
    tile[...] = values


def final_kernel(tiles, w_k, w_a, vk, va, next_k, next_a, coefs, *, cells):
    tile = jnp.concatenate([tiles[i] for i in range(tiles.shape[0])], axis=0)
    wv, vv, a, uv, uu = (tile[:, i : i + 1] for i in range(5))
    wv_sum = jnp.sum(wv, axis=0, keepdims=True)
    vv_sum = jnp.sum(vv, axis=0, keepdims=True)
    alpha = wv_sum / cells / (vv_sum / cells + eps_norm)
    off = alpha - a
    rr = jnp.sum(uu - 2.0 * off * uv + off * off * vv, axis=0, keepdims=True)
    beta = jnp.sqrt(rr / cells + eps_norm)
    next_k[...] = (w_k[...] - alpha * vk[...]) / beta
    next_a[...] = (w_a[...] - alpha * va[...]) / beta
    coefs[0] = jnp.sum(alpha)
    coefs[1] = jnp.sum(beta)


def f32(*shape):
    return jax.ShapeDtypeStruct(shape, jnp.float32)


def run(kernel, outs, *args, after=(), scratch=(), copies=0, smem=(), hbm=(), mib=16, in_smem_out=(), cost=None):
    vmem = pl.BlockSpec(memory_space=pltpu.VMEM)
    scalar = pl.BlockSpec(memory_space=pltpu.SMEM)
    far = pl.BlockSpec(memory_space=pltpu.HBM)
    held = [pltpu.VMEM(shape, dtype) for shape, dtype in scratch]
    used, waits = len(args), len(after)

    def body(*refs):
        kernel(*refs[:used], *refs[used + waits :])

    args = (*args, *after)
    if copies:
        held.append(pltpu.SemaphoreType.DMA((copies,)))
    return pl.pallas_call(
        body if waits else kernel,
        out_shape=tuple(outs),
        in_specs=[scalar if i in smem else far if i in hbm else vmem for i in range(len(args))],
        out_specs=tuple(scalar if i in in_smem_out else vmem for i in range(len(outs))),
        scratch_shapes=held,
        compiler_params=pltpu.CompilerParams(vmem_limit_bytes=mib * 2**20),
        cost_estimate=cost,
    )(*args)


HALO = 8
UNROLL = 16
REACH = 6
GROUP = 4


def per_device_paired(
    labels, kappa_table, absorb_table, background, det_cells,
    v_kappa, v_absorb, q_kappa, q_absorb, beta_prev,
):
    sources, cx, cy, cz = background.shape
    n = lax.axis_size("src")
    planes, rows = 2 * cx, 2 * cy + HALO
    ny = cy * lax.axis_size("gy")
    dets = det_cells.shape[0]
    cells = planes * ny * cz
    groups = cx // n

    def swap_x(value):
        return lax.ppermute(value, "gx", [(0, 1), (1, 0)])

    def swap_core(value):
        return lax.ppermute(value, "gy", [(0, 1), (1, 0), (2, 3), (3, 2)])

    def along_z(value, k):
        return lax.ppermute(value, "src", [(i, i ^ k) for i in range(n)])

    block = (cx, cy, cz)
    float_block = lambda *shape: (shape, jnp.float32)
    raw_labels = (block, jnp.int32)
    packed, message = run(
        pack_kernel, (f32(2 * groups, cy, cz), f32((sources // 2 + 1) * cx + 2 * groups, cy, cz)),
        background, labels, v_kappa, v_absorb, hbm=(0, 1, 2, 3),
        scratch=(raw_labels, float_block(2, *v_kappa.shape)), copies=3 + sources // 2, mib=60,
    )
    long = pl.CostEstimate(flops=10**9, bytes_accessed=2**26, transcendentals=0)
    came = swap_x(message)
    slabs = [along_z(packed, k) for k in range(1, n)]
    count, beta_row = run(
        functools.partial(count_kernel, ny=ny, nz=cz, half=2 * cy, halo=HALO),
        (f32(planes, rows, cz), f32(1, cz)), det_cells.reshape(1, dets), beta_prev, smem=(1,),
        cost=pl.CostEstimate(flops=2 * planes * rows * cz * dets, bytes_accessed=planes * rows * cz * 4, transcendentals=0),
    )

    def across_y(value):
        return lax.ppermute(value, "gy", [(i, (i + 2) % 4) for i in range(4)])

    (joined,) = run(join_kernel, (f32(2 * groups * (n - 1), cy, cz),), *slabs, after=(count,))
    joined_came = swap_x(joined)
    (half_vector,) = run(own_half_kernel, (f32(2, *block),), v_kappa, v_absorb, joined)
    mine, fields = run(
        photon_kernel, (f32(planes, cy, cz), f32(2, planes, cy, cz)),
        background, labels, came, after=(joined,), hbm=(0, 1), scratch=(raw_labels,), copies=3,
    )
    got = swap_core(fields)
    (vector,) = run(
        vector_kernel, (f32(2, planes, cy, cz),), half_vector, came, joined_came, after=(mine,)
    )
    edge = (f32(2, *edge_shape(planes, cz)),)
    (sent,) = run(photon_edge_kernel, edge, mine, fields, got, after=(vector,))
    photon_edge = across_y(sent)
    vector_got = swap_core(vector)
    (vector_sent,) = run(vector_edge_kernel, edge, vector, vector_got, after=(sent,))
    frame, wide = (planes, rows, cz), (planes + 2, rows, cz)
    float_frame, float_wide = float_block(*frame), float_block(*wide)
    coefs = (f32(*frame), f32(planes + 1, rows, cz), f32(*frame), f32(*frame))
    kap, *partial, sums = run(
        stencil_kernel, (f32(*wide), *coefs, f32(2, 8, cz)),
        kappa_table, absorb_table, mine, fields, got, count, after=(vector_sent,), cost=long,
        smem=(0, 1), scratch=(float_frame,),
    )
    diag, fx, fy, fz = run(
        halo_kernel, coefs, kappa_table, absorb_table, photon_edge, kap, *partial, smem=(0, 1)
    )
    phi, change, sent = run(
        first_kernel, (f32(*wide), f32(*frame), f32(4, GROUP * REACH + 8, cz)),
        diag, fx, fy, fz, count, sums, mine, got, vector, vector_got,
        photon_edge, across_y(vector_sent),
        scratch=(float_wide, float_frame, float_frame, float_wide, float_wide),
    )
    heard = across_y(sent)
    own, message = run(
        functools.partial(second_kernel, dets=dets),
        (f32(2, planes, cy, cz), f32(2, planes, cy, cz)),
        phi, change, diag, fx, fy, fz, count, sent, heard,
        scratch=(float_frame, float_wide, float_wide, float_frame, float_frame),
    )
    piece = f32(2, groups, cy, cz)
    got = swap_core(message)
    crossed, last = {}, ()
    for k in reversed(range(n)):
        last = run(functools.partial(send_kernel, k=k), (f32(1, *piece.shape),), own, got, after=last)
        crossed[k] = swap_x(last[0])
    (kept,) = run(keep_kernel, (f32(n, *piece.shape),), own, got, after=last)
    totals = {
        k: run(functools.partial(add_kernel, k=k), (piece,), kept, value)[0] for k, value in crossed.items()
    }
    received = {k: along_z(totals[k], k) for k in reversed(range(1, n))}
    (distant,) = run(sum_kernel, (piece,), *(received[k] for k in range(n // 2, n)), cost=long)
    parts = [distant, totals[0]] + [received[k] for k in range(1, n // 2)]
    w_k, w_a, tile = run(
        functools.partial(project_kernel, parts_n=len(parts), n=n),
        (f32(*v_kappa.shape), f32(*v_kappa.shape), f32(1, 128)),
        beta_row, *parts, v_kappa, v_absorb, q_kappa, q_absorb,
    )
    everyone = ("src", "gx", "gy")
    tiles = lax.all_to_all(jnp.broadcast_to(tile, (8 * n, 1, 128)), everyone, 0, 0)
    return tuple(run(
        functools.partial(final_kernel, cells=cells),
        (f32(*v_kappa.shape), f32(*v_kappa.shape), f32(2)),
        tiles, w_k, w_a, v_kappa, v_absorb, in_smem_out=(2,),
    ))


def paired_fits(mesh):
    return mesh.shape["gx"] == 2 and mesh.shape["gy"] == 4


def body_for(mesh):
    if not paired_fits(mesh):
        return per_device

    def chosen(*args):
        sources, cx, cy, cz = args[3].shape
        n = lax.axis_size("src")
        fits = sources == 4 and cz == 128 and cx % n == 0 and cx % GROUP == 0 and cy % HALO == 0 and n > 1 and n & (n - 1) == 0
        devices = 8 * n
        return (per_device_paired if fits and devices <= 128 else per_device)(*args)

    return chosen


def solution(mesh):
    return jax.shard_map(
        body_for(mesh),
        mesh=mesh,
        in_specs=(
            P("gx", "gy", None),
            P(),
            P(),
            P("src", "gx", "gy", None),
            P(),
            P("gx", "gy", "src"),
            P("gx", "gy", "src"),
            P("gx", "gy", "src"),
            P("gx", "gy", "src"),
            P(),
        ),
        out_specs=(P("gx", "gy", "src"), P("gx", "gy", "src"), P()),
        check_vma=False,
    )
```

```python
import functools

import jax
import jax.numpy as jnp
from jax import lax
from jax.experimental import pallas as pl
from jax.experimental.pallas import tpu as pltpu
from jax.sharding import PartitionSpec as P

ITERS = 6


lam_low = 0.02
lam_high = 24.1
eps_norm = 1e-06


def padded_2(block, sides, width):
    for axis, dim in sides:
        count = lax.axis_size(axis)
        forward = [(i, i + 1) for i in range(count - 1)]
        backward = [(target, source) for source, target in forward]
        low = lax.ppermute(
            lax.slice_in_dim(block, block.shape[dim] - width, None, axis=dim), axis, forward
        )
        high = lax.ppermute(lax.slice_in_dim(block, 0, width, axis=dim), axis, backward)
        block = jnp.concatenate([low, block, high], axis=dim)
    return block


def regional(labels, table):
    field = jnp.zeros(labels.shape, jnp.float32)
    for region in range(table.shape[0]):
        field = field + jnp.where(labels == region, table[region], 0.0)
    return field


def beside(padded):
    widths = [(0, 0)] * (padded.ndim - 1) + [(1, 1)]
    full = jnp.pad(padded, widths)
    return [
        full[..., 2:, 1:-1, 1:-1],
        full[..., :-2, 1:-1, 1:-1],
        full[..., 1:-1, 2:, 1:-1],
        full[..., 1:-1, :-2, 1:-1],
        full[..., 1:-1, 1:-1, 2:],
        full[..., 1:-1, 1:-1, :-2],
    ]


def chebyshev(rhs, apply_op):
    theta = 0.5 * (lam_high + lam_low)
    delta = 0.5 * (lam_high - lam_low)
    sigma = theta / delta
    rho = 1.0 / sigma
    solution = jnp.zeros_like(rhs)
    remain = rhs
    step_dir = rhs / theta
    for step in range(ITERS):
        solution = solution + step_dir
        if step + 1 < ITERS:
            remain = remain - apply_op(step_dir)
            rho_next = 1.0 / (2.0 * sigma - rho)
            step_dir = rho_next * rho * step_dir + 2.0 * rho_next / delta * remain
            rho = rho_next
    return solution


def per_device(
    labels,
    kappa_table,
    absorb_table,
    background,
    det_cells,
    v_kappa,
    v_absorb,
    q_kappa,
    q_absorb,
    beta_prev,
):
    sources, cx, cy, cz = background.shape
    kappa = regional(labels, kappa_table)
    absorb = regional(labels, absorb_table)
    full_k, full_a = (
        lax.all_gather(v_kappa, "src", axis=2, tiled=True),
        lax.all_gather(v_absorb, "src", axis=2, tiled=True),
    )
    stacked = jnp.concatenate([background, kappa[None], full_k[None]], axis=0)
    rims = padded_2(stacked, (("gx", 1), ("gy", 2)), 1)
    near_all = beside(rims)
    kappa_faces = [0.5 * (kappa + near[sources]) for near in near_all]
    vk_faces = [0.5 * (full_k + near[sources + 1]) for near in near_all]
    phi_near = [near[:sources] for near in near_all]

    def apply_op(field):
        padded = padded_2(field, (("gx", 1), ("gy", 2)), 1)
        result = absorb * field
        for face, near in zip(kappa_faces, beside(padded)):
            result = result + face * (field - near)
        return result

    rhs = full_a * background
    for face, near in zip(vk_faces, phi_near):
        rhs = rhs + face * (background - near)
    rhs = -rhs
    change = chebyshev(rhs, apply_op)
    span_y = cy * lax.axis_size("gy")
    ix = det_cells // (span_y * cz)
    iy = det_cells // cz % span_y
    iz = det_cells % cz
    anchor_x = lax.axis_index("gx") * cx
    anchor_y = lax.axis_index("gy") * cy
    owned = (ix >= anchor_x) & (ix < anchor_x + cx) & (iy >= anchor_y) & (iy < anchor_y + cy)
    local = jnp.where(owned, ((ix - anchor_x) * cy + (iy - anchor_y)) * cz + iz, 0)
    seen_part = jnp.where(owned[None, :], change.reshape(sources, -1)[:, local], 0.0)
    base_part = jnp.where(owned[None, :], background.reshape(sources, -1)[:, local], 0.0)
    seen, base = lax.psum((seen_part, base_part), ("gx", "gy"))
    total = jnp.sum(base, axis=1, keepdims=True)
    mean_base = total / det_cells.shape[0]
    ratio = base / total
    jv_vals = (seen - ratio * jnp.sum(seen, axis=1, keepdims=True)) / mean_base
    weight = (jv_vals - jnp.sum(ratio * jv_vals, axis=1, keepdims=True)) / mean_base
    deposit = jnp.where(owned[None, :], weight, 0.0)
    source = (
        jnp.zeros((sources, cx * cy * cz), jnp.float32)
        .at[:, local]
        .add(deposit)
        .reshape(change.shape)
    )
    dual = chebyshev(source, apply_op)
    dual_rims = padded_2(dual, (("gx", 1), ("gy", 2)), 1)
    grad_a = -jnp.sum(background * dual, axis=0)
    grad_k = jnp.zeros_like(kappa)
    for near_phi, near_dual in zip(phi_near, beside(dual_rims)):
        grad_k = grad_k - 0.5 * jnp.sum((background - near_phi) * (dual - near_dual), axis=0)
    summed_k, summed_a = lax.psum((grad_k, grad_a), "src")
    slab = v_kappa.shape[2]
    offset = lax.axis_index("src") * slab
    hv_k = lax.dynamic_slice_in_dim(summed_k, offset, slab, 2)
    hv_a = lax.dynamic_slice_in_dim(summed_a, offset, slab, 2)
    cell_count = cx * lax.axis_size("gx") * cy * lax.axis_size("gy") * cz
    w_k = hv_k - beta_prev[0] * q_kappa
    w_a = hv_a - beta_prev[0] * q_absorb
    local_wv = jnp.sum(w_k * v_kappa) + jnp.sum(w_a * v_absorb)
    local_vv = jnp.sum(v_kappa * v_kappa) + jnp.sum(v_absorb * v_absorb)
    wv_sum, vv_sum = lax.psum((local_wv, local_vv), ("src", "gx", "gy"))
    alpha = wv_sum / cell_count / (vv_sum / cell_count + eps_norm)
    r_k = w_k - alpha * v_kappa
    r_a = w_a - alpha * v_absorb
    rr_sum = lax.psum(jnp.sum(r_k * r_k) + jnp.sum(r_a * r_a), ("src", "gx", "gy"))
    beta = jnp.sqrt(rr_sum / cell_count + eps_norm)
    return (r_k / beta, r_a / beta, jnp.stack([alpha, beta]))


def chebyshev_scalars():
    theta = 0.5 * (lam_high + lam_low)
    delta = 0.5 * (lam_high - lam_low)
    sigma = theta / delta
    rho = 1.0 / sigma
    pairs = []
    for _ in range(ITERS - 1):
        rho_next = 1.0 / (2.0 * sigma - rho)
        pairs.append((rho_next * rho, 2.0 * rho_next / delta))
        rho = rho_next
    return theta, pairs


def places(split):
    g = lax.axis_index("gy")
    return lax.axis_index("src"), lax.axis_index("gx"), g // split, g % split


def shifted(value, step, axis):
    return pltpu.roll(value, step % value.shape[axis], axis)


def index_along(shape, axis):
    return lax.broadcasted_iota(jnp.int32, shape, axis)


def beyond(value, step, axis):
    size = value.shape[axis]
    at = index_along(value.shape, axis)
    edge = size - 1 if step == 1 else 0
    return jnp.where(at == edge, 0.0, shifted(value, -step, axis))


def packed_planes(ref, q):
    per = 128 // ref.shape[2]
    return jnp.concatenate([ref[per * q + j] for j in range(per)], axis=1)


def pack_kernel(bg, vk, va, packed, message, v_in, sems):
    _, x, _, _ = places(2)
    half = bg.shape[0] // 2
    cx = bg.shape[1]
    copies = [
        pltpu.make_async_copy(src, dst, sems.at[i])
        for i, (src, dst) in enumerate((
            (vk, v_in.at[0]),
            (va, v_in.at[1]),
            *((bg.at[half * (1 - x) + i], message.at[pl.ds(cx * i, cx)]) for i in range(half)),
        ))
    ]
    for copy in copies:
        copy.start()
    groups = packed.shape[0] // 2
    for f in range(2):
        copies[f].wait()
        for q in range(groups):
            planes = packed_planes(v_in.at[f], q)
            packed[groups * f + q] = planes
            message[cx * half + groups * f + q] = planes
    for copy in copies[2:]:
        copy.wait()


def count_kernel(dets, beta_prev, count, beta_row, *, ny, nz, half, halo):
    beta_row[...] = jnp.full(beta_row.shape, beta_prev[0])
    _, _, y, _ = places(2)
    planes, rows, _ = count.shape
    flat = dets[...]
    iz = flat % nz
    line = flat // nz
    iy = line % ny
    ix = line // ny
    row = iy - (half - halo) * y
    spot = jnp.where((row >= 0) & (row < rows), ix * rows + row, -1)
    dets_n = flat.shape[1]
    at_z = (index_along((nz, dets_n), 0) == iz).astype(jnp.float32).astype(jnp.bfloat16)

    def body(i, carry):
        here = index_along((2 * rows, dets_n), 0) + i * (2 * rows)
        hot = (here == spot).astype(jnp.float32).astype(jnp.bfloat16)
        found = lax.dot_general(hot, at_z, (((1,), (1,)), ((), ())), preferred_element_type=jnp.float32)
        count[pl.ds(2 * i, 2)] = found.reshape(2, rows, nz)
        return carry

    lax.fori_loop(0, planes // 2, body, 0)


def photon_kernel(bg, labels, msg, labels_came, mine, fields, raw, sems):
    _, x, _, c = places(2)
    half = bg.shape[0] // 2
    cx = labels.shape[0]
    here, there = cx * x, cx * (1 - x)
    copies = [
        pltpu.make_async_copy(src, dst, sems.at[i])
        for i, (src, dst) in enumerate((
            (bg.at[half * x + c], mine.at[pl.ds(here, cx)]),
            (bg.at[half * x + 1 - c], fields.at[0, pl.ds(here, cx)]),
            (labels, raw),
        ))
    ]
    for copy in copies:
        copy.start()
    mine[pl.ds(there, cx)] = msg[pl.ds(cx * c, cx)]
    fields[0, pl.ds(there, cx)] = msg[pl.ds(cx * (1 - c), cx)]
    fields[1, pl.ds(there, cx)] = labels_came[...].astype(jnp.float32)
    for copy in copies:
        copy.wait()
    fields[1, pl.ds(here, cx)] = raw[...].astype(jnp.float32)


def unpacked(blocks, groups, s, store):
    n = len(blocks)
    cy, lanes = blocks[0][0].shape
    slab = lanes // n
    lane = index_along((cy, lanes), 1) // slab
    for f in range(2):
        for q in range(groups):
            values = [block[groups * f + q] for block in blocks]
            for j in range(n):
                plane = jnp.zeros((cy, lanes), jnp.float32)
                for k in range(n):
                    home = s ^ k
                    moved = pltpu.roll(values[k], ((home - j + n) % n) * slab, 1)
                    plane = jnp.where(lane == home, moved, plane)
                store(f, n * q + j, plane)


def join_kernel(*refs):
    joined, size = refs[-1], refs[0].shape[0]
    for i, ref in enumerate(refs[:-1]):
        joined[pl.ds(size * i, size)] = ref[...]


def own_half_kernel(vk, va, joined, half):
    s, _, _, _ = places(2)
    size = half.shape[1]
    groups = joined.shape[0] // 2 // (128 // vk.shape[2] - 1)
    n = size // groups
    own = [packed_planes(ref, q) for ref in (vk, va) for q in range(groups)]
    blocks = [own] + [[joined[2 * groups * k + i] for i in range(2 * groups)] for k in range(n - 1)]

    def store(f, i, plane):
        half[f, i] = plane

    unpacked(blocks, groups, s, store)


def vector_kernel(half, msg, joined, fields):
    s, x, _, _ = places(2)
    cx = half.shape[1]
    fields[:, pl.ds(cx * x, cx)] = half[...]
    n = lax.axis_size("src")
    groups = cx // n
    own = msg.shape[0] - 2 * groups
    blocks = [[msg[own + i] for i in range(2 * groups)]]
    blocks += [[joined[2 * groups * k + i] for i in range(2 * groups)] for k in range(n - 1)]
    there = cx * (1 - x)

    def store(f, i, plane):
        fields[f, there + i] = plane

    unpacked(blocks, groups, s, store)


def edge_shape(planes, lanes):
    return planes // GROUP, GROUP * REACH, lanes


def packed_edges(tiles):
    return jnp.concatenate([tile[:REACH] for tile in tiles], axis=0)


def edge_tile(packed, j, y):
    rows = packed[REACH * j : REACH * (j + 1)]
    tile = jnp.concatenate([rows, jnp.zeros((HALO - REACH, rows.shape[1]), jnp.float32)], axis=0)
    return jnp.where(y == 0, tile, shifted(tile, HALO - REACH, 0))


def near_rows(ref, i, first, y):
    tile = ref[i, pl.ds(first, HALO), :]
    return jnp.where(y == 0, shifted(tile, REACH - HALO, 0), tile)


def edges_of(own, got, edge, y, c):
    first = (own.shape[1] - HALO) * (1 - y)
    for g in range(edge.shape[0]):
        edge[g] = packed_edges([
            jnp.where(c != y, near_rows(own, GROUP * g + j, first, y), near_rows(got, GROUP * g + j, first, y))
            for j in range(GROUP)
        ])


def photon_edge_kernel(mine, fields, got, edge):
    _, _, y, c = places(2)
    edges_of(mine, got.at[0], edge.at[0], y, c)
    edges_of(fields.at[1], got.at[1], edge.at[1], y, c)


def vector_edge_kernel(fields, got, edge):
    _, _, y, c = places(2)
    for f in range(2):
        edges_of(fields.at[f], got.at[f], edge.at[f], y, c)


def solve(b, bufs, diag, fx, fy, fz, unroll):
    planes = b.shape[0]
    _, pairs = chebyshev_scalars()
    for step, (keep, push) in enumerate(pairs):
        src, dst = bufs[step % 2], bufs[(step + 1) % 2]

        def body(i, carry):
            u = src[i + 1]
            coef_y, coef_z = fy[i], fz[i]
            left = b[i] - diag[i] * u
            left = left + fx[i] * src[i] + fx[i + 1] * src[i + 2]
            left = left + coef_y * shifted(u, -1, 0) + shifted(coef_y * u, 1, 0)
            left = left + coef_z * shifted(u, -1, 1) + shifted(coef_z * u, 1, 1)
            change = u if step == 0 else u - dst[i + 1]
            dst[i + 1] = u + keep * change + push * left
            return carry

        lax.fori_loop(0, planes, body, 0, unroll=unroll)
    return bufs[len(pairs) % 2]


def folded(value):
    return jnp.sum(value.reshape(-1, 8, value.shape[1]), axis=0)


def framed_own(ref, shift, own, got, y, c):
    planes, cy, _ = own.shape
    there = pl.ds(shift, planes)
    base = HALO * y
    ref[there, pl.ds(base + cy * c, cy), :] = own[...]
    ref[there, pl.ds(base + cy * (1 - c), cy), :] = got[...]


def framed(ref, shift, own, got, edge, y, c):
    framed_own(ref, shift, own, got, y, c)
    cy = own.shape[1]
    for g in range(edge.shape[0]):
        packed = edge[g]
        for j in range(GROUP):
            ref[shift + GROUP * g + j, pl.ds(2 * cy * (1 - y), HALO), :] = edge_tile(packed, j, y)


def blank_ends(*refs):
    for ref in refs:
        blank = jnp.zeros(ref.shape[1:], jnp.float32)
        ref[0] = blank
        ref[ref.shape[0] - 1] = blank


def owned_rows(shape, base, count):
    at_row = index_along(shape, 0)
    return (at_row >= base) & (at_row < base + count)


def table_rows(kap_table, abs_table, shape):
    lane = index_along(shape, 1)
    kap_row = abs_row = jnp.zeros(shape, jnp.float32)
    for region in range(kap_table.shape[0]):
        kap_row = jnp.where(lane == region, kap_table[region], kap_row)
        abs_row = jnp.where(lane == region, abs_table[region], abs_row)
    return kap_row, abs_row


def stencil_kernel(
    kap_table, abs_table, mine, fields, got, count,
    kap, diag, fx, fy, fz, sums,
    labels,
):
    _, _, y, c = places(2)
    planes, cy, lanes = mine.shape
    rows = 2 * cy + HALO
    base = HALO * y
    framed_own(labels, 0, fields.at[1], got.at[1], y, c)
    labels[:, pl.ds(2 * cy * (1 - y), HALO), :] = jnp.zeros((planes, HALO, lanes), jnp.float32)
    blank_ends(kap)
    shape = (rows, lanes)
    lane = index_along(shape, 1)
    kap_row, abs_row = table_rows(kap_table, abs_table, shape)
    owned = owned_rows(shape, base, 2 * cy)

    def look_up(i, carry):
        at = labels[i].astype(jnp.int32)
        kap[i + 1] = jnp.where(owned, jnp.take_along_axis(kap_row, at, axis=1), 0.0)
        diag[i] = jnp.take_along_axis(abs_row, at, axis=1)
        return carry

    lax.fori_loop(0, planes, look_up, 0, unroll=4)
    fx[0] = 0.5 * kap[1]

    def set_up(i, carry):
        k = kap[i + 1]
        along_x = 0.5 * (k + kap[i + 2])
        along_y, along_z = 0.5 * (k + beyond(k, 1, 0)), 0.5 * (k + beyond(k, 1, 1))
        fx[i + 1] = along_x
        fy[i] = jnp.where(index_along(shape, 0) == rows - 1, 0.0, along_y)
        fz[i] = jnp.where(lane == lanes - 1, 0.0, along_z)
        back_y, back_z = 0.5 * (k + beyond(k, -1, 0)), 0.5 * (k + beyond(k, -1, 1))
        diag[i] = diag[i] + fx[i] + along_x + along_y + back_y + along_z + back_z
        total, square = carry
        for p, at in ((mine[i], c), (got[0, i], 1 - c)):
            part = count[i, pl.ds(base + cy * at, cy), :] * p
            total, square = total + folded(part), square + folded(part * p)
        return total, square

    zero = jnp.zeros((8, lanes), jnp.float32)
    sums[0], sums[1] = lax.fori_loop(0, planes, set_up, (zero, zero), unroll=4)


def halo_kernel(kap_table, abs_table, edge, kap, diag_in, fx_in, fy_in, fz_in, diag, fx, fy, fz):
    _, _, y, _ = places(2)
    planes, rows, lanes = diag.shape
    for ref, old in ((diag, diag_in), (fx, fx_in), (fy, fy_in), (fz, fz_in)):
        ref[...] = old[...]
    shape = (HALO, lanes)
    lane, row = index_along(shape, 1), index_along(shape, 0)
    kap_row, abs_row = table_rows(kap_table, abs_table, shape)
    low = y == 0
    here = pl.ds((rows - HALO) * (1 - y), HALO)
    beside_it = pl.ds((rows - 2 * HALO) * (1 - y) + HALO * y, HALO)
    labels = [edge_tile(edge[1, i // GROUP], i % GROUP, y).astype(jnp.int32) for i in range(planes)]
    tiles = [jnp.take_along_axis(kap_row, at, axis=1) for at in labels]
    none = jnp.zeros(shape, jnp.float32)
    before = 0.5 * tiles[0]
    fx[0, here, :] = before
    for i, k in enumerate(tiles):
        after = 0.5 * (k + (tiles[i + 1] if i + 1 < planes else none))
        own = kap[i + 1, beside_it, :]
        up, down = shifted(k, -1, 0), shifted(k, 1, 0)
        k_up = jnp.where(row == HALO - 1, jnp.where(low, 0.0, shifted(own, -1, 0)), up)
        k_down = jnp.where(row == 0, jnp.where(low, shifted(own, 1, 0), 0.0), down)
        along_y, back_y = 0.5 * (k + k_up), 0.5 * (k + k_down)
        along_z, back_z = 0.5 * (k + beyond(k, 1, 1)), 0.5 * (k + beyond(k, -1, 1))
        fx[i + 1, here, :] = after
        fy[i, here, :] = jnp.where(low & (row == HALO - 1), 0.0, along_y)
        fz[i, here, :] = jnp.where(lane == lanes - 1, 0.0, along_z)
        absorb = jnp.take_along_axis(abs_row, labels[i], axis=1)
        diag[i, here, :] = absorb + before + after + along_y + back_y + along_z + back_z
        before = after
        face_up = jnp.where(low & (row == HALO - 1), 0.5 * up, 0.0)
        face_down = jnp.where(low | (row > 0), 0.0, 0.5 * down)
        fy[i, beside_it, :] = fy_in[i, beside_it, :] + face_up
        diag[i, beside_it, :] = diag_in[i, beside_it, :] + face_up + face_down


def first_kernel(
    diag, fx, fy, fz, count, sums, mine, got_photon, vector, got_vector, photon_edge, edge,
    phi, change, message,
    vk, va, b, buf_a, buf_b,
):
    _, _, y, c = places(2)
    planes, rows, lanes = change.shape
    cy = mine.shape[1]
    framed(phi, 1, mine, got_photon.at[0], photon_edge.at[0], y, c)
    framed(vk, 1, vector.at[0], got_vector.at[0], edge.at[0], y, c)
    framed(va, 0, vector.at[1], got_vector.at[1], edge.at[1], y, c)
    blank_ends(phi, vk, buf_a, buf_b)
    theta, _ = chebyshev_scalars()

    def set_up(i, carry):
        v, p = vk[i + 1], phi[i + 1]
        total = 0.5 * (v + vk[i]) * (p - phi[i]) + 0.5 * (v + vk[i + 2]) * (p - phi[i + 2])
        for axis in range(2):
            flow = 0.5 * (v + beyond(v, 1, axis)) * (p - beyond(p, 1, axis))
            first = index_along(v.shape, axis) == 0
            total = total + flow + jnp.where(first, 0.5 * v * p, -shifted(flow, 1, axis))
        total = -(va[i] * p + total)
        b[i] = total
        buf_a[i + 1] = total * (1.0 / theta)
        return carry

    lax.fori_loop(0, planes, set_up, 0, unroll=4)
    found = solve(b, (buf_a, buf_b), diag, fx, fy, fz, UNROLL)
    owned = owned_rows((rows, lanes), HALO * y, 2 * cy)

    def add_up(i, carry):
        u = found[i + 1]
        change[i] = u
        part = jnp.where(owned, count[i], 0.0) * u
        return carry[0] + folded(part), carry[1] + folded(part * phi[i + 1])

    zero = jnp.zeros((8, lanes), jnp.float32)
    seen, cross = lax.fori_loop(0, planes, add_up, (zero, zero), unroll=4)
    first = (2 * cy - HALO) * (1 - y) + HALO * y
    for g, part in enumerate((sums[0], seen, cross, sums[1])):
        message[g, pl.ds(0, GROUP * REACH), :] = packed_edges(
            [near_rows(found, 1 + GROUP * g + j, first, y) for j in range(GROUP)]
        )
        message[g, pl.ds(GROUP * REACH, 8), :] = part


def second_kernel(
    phi, change, diag, fx, fy, fz, count, sent, came,
    own, message,
    b, buf_a, buf_b, grad_k, grad_a,
    *, dets,
):
    _, _, y, c = places(2)
    planes, rows, lanes = change.shape
    cy = (rows - HALO) // 2
    base = HALO * y
    edge = pl.ds(2 * cy * (1 - y), HALO)
    tail = pl.ds(GROUP * REACH, 8)
    total, seen_sum, cross, square = (
        jnp.sum(jnp.sum(sent[g, tail, :] + came[g, tail, :], axis=0, keepdims=True), axis=1, keepdims=True)
        for g in range(4)
    )
    mean = total / dets
    part = seen_sum / total
    level = (cross - part * square) / (total * mean)
    inverse = 1.0 / mean
    blank_ends(buf_a, buf_b)
    theta, _ = chebyshev_scalars()

    def weighted(n, u, p):
        return n * (((u - p * part) * inverse - level) * inverse)

    def set_up(i, carry):
        value = weighted(count[i], change[i], phi[i + 1])
        b[i] = value
        buf_a[i + 1] = value * (1.0 / theta)
        return carry

    lax.fori_loop(0, planes, set_up, 0, unroll=4)
    for i in range(planes):
        u = edge_tile(came[i // GROUP], i % GROUP, y)
        value = weighted(count[i, edge, :], u, phi[i + 1, edge, :])
        b[i, edge, :] = value
        buf_a[i + 1, edge, :] = value * (1.0 / theta)
    dual = solve(b, (buf_a, buf_b), diag, fx, fy, fz, UNROLL)

    def product(i, carry):
        p, u = phi[i + 1], dual[i + 1]
        grad = (p - phi[i]) * (u - dual[i]) + (p - phi[i + 2]) * (u - dual[i + 2])
        both = p * u
        for axis in range(2):
            flow = (p - beyond(p, 1, axis)) * (u - beyond(u, 1, axis))
            first = index_along(p.shape, axis) == 0
            grad = grad + flow + jnp.where(first, both, shifted(flow, 1, axis))
        grad_k[i] = -0.5 * grad
        grad_a[i] = -both
        for f, ref in enumerate((grad_k, grad_a)):
            own[f, i] = ref[i, pl.ds(base + cy * c, cy), :]
            message[f, i] = ref[i, pl.ds(base + cy * (1 - c), cy), :]
        return carry

    lax.fori_loop(0, planes, product, 0, unroll=4)


def packed_slabs(own, came, half, choices, outs):
    s, _, _, _ = places(2)
    _, planes, cy, lanes = own.shape
    n = planes // 2 // outs.shape[2]
    slab = lanes // n
    lane = index_along((cy, lanes), 1) // slab
    for f in range(2):
        for q in range(outs.shape[2]):
            at = planes // 2 * half + n * q
            parts = [own[f, at + j] + came[f, at + j] for j in range(n)]
            for i, k in enumerate(choices):
                to = s ^ k
                piece = jnp.zeros((cy, lanes), jnp.float32)
                for j in range(n):
                    moved = pltpu.roll(parts[j], ((j - to + n) % n) * slab, 1)
                    piece = jnp.where(lane == j, moved, piece)
                outs[i, f, q] = piece


def send_kernel(own, came, out, *, k):
    _, x, _, _ = places(2)
    packed_slabs(own, came, 1 - x, (k,), out)


def keep_kernel(own, came, kept):
    _, x, _, _ = places(2)
    packed_slabs(own, came, x, range(kept.shape[0]), kept)


def add_kernel(kept, came, out, *, k):
    out[...] = kept[k] + came[0]


def sum_kernel(*refs):
    total = refs[0][...]
    for ref in refs[1:-1]:
        total = total + ref[...]
    refs[-1][...] = total


def project_kernel(*refs, parts_n, n):
    beta_prev = refs[0]
    parts = refs[1 : 1 + parts_n]
    vk, va, qk, qa, w_k, w_a, tile = refs[1 + parts_n :]
    slab = 128 // n
    for f, (q_ref, w) in enumerate(((qk, w_k), (qa, w_a))):
        for q in range(vk.shape[0] // n):
            whole = sum(part[f, q] for part in parts[1:]) + parts[0][f, q]
            for j in range(n):
                i = n * q + j
                w[i] = whole[:, slab * j : slab * (j + 1)] - beta_prev[:, : vk.shape[2]] * q_ref[i]

    def total(value):
        return jnp.sum(jnp.sum(jnp.sum(value, axis=0), axis=0, keepdims=True), axis=1, keepdims=True)

    wk, wa, v_k, v_a = w_k[...], w_a[...], vk[...], va[...]
    wv = total(wk * v_k + wa * v_a)
    vv = total(v_k * v_k + v_a * v_a)
    a = jnp.where(vv > 0.0, wv / jnp.where(vv > 0.0, vv, 1.0), 0.0)
    u_k, u_a = wk - a * v_k, wa - a * v_a
    uv = total(u_k * v_k + u_a * v_a)
    uu = total(u_k * u_k + u_a * u_a)
    lane = index_along((1, 128), 1)
    values = jnp.zeros((1, 128), jnp.float32)
    for i, value in enumerate((wv, vv, a, uv, uu)):
        values = jnp.where(lane == i, value, values)
    tile[...] = values


def final_kernel(tiles, w_k, w_a, vk, va, next_k, next_a, coefs, *, cells):
    tile = jnp.concatenate([tiles[i] for i in range(tiles.shape[0])], axis=0)
    wv, vv, a, uv, uu = (tile[:, i : i + 1] for i in range(5))
    wv_sum = jnp.sum(wv, axis=0, keepdims=True)
    vv_sum = jnp.sum(vv, axis=0, keepdims=True)
    alpha = wv_sum / cells / (vv_sum / cells + eps_norm)
    off = alpha - a
    rr = jnp.sum(uu - 2.0 * off * uv + off * off * vv, axis=0, keepdims=True)
    beta = jnp.sqrt(rr / cells + eps_norm)
    next_k[...] = (w_k[...] - alpha * vk[...]) / beta
    next_a[...] = (w_a[...] - alpha * va[...]) / beta
    coefs[0] = jnp.sum(alpha)
    coefs[1] = jnp.sum(beta)


def f32(*shape):
    return jax.ShapeDtypeStruct(shape, jnp.float32)


def run(kernel, outs, *args, after=(), scratch=(), copies=0, smem=(), hbm=(), mib=16, in_smem_out=(), cost=None):
    vmem = pl.BlockSpec(memory_space=pltpu.VMEM)
    scalar = pl.BlockSpec(memory_space=pltpu.SMEM)
    far = pl.BlockSpec(memory_space=pltpu.HBM)
    held = [pltpu.VMEM(shape, dtype) for shape, dtype in scratch]
    used, waits = len(args), len(after)

    def body(*refs):
        kernel(*refs[:used], *refs[used + waits :])

    args = (*args, *after)
    if copies:
        held.append(pltpu.SemaphoreType.DMA((copies,)))
    return pl.pallas_call(
        body if waits else kernel,
        out_shape=tuple(outs),
        in_specs=[scalar if i in smem else far if i in hbm else vmem for i in range(len(args))],
        out_specs=tuple(scalar if i in in_smem_out else vmem for i in range(len(outs))),
        scratch_shapes=held,
        compiler_params=pltpu.CompilerParams(vmem_limit_bytes=mib * 2**20),
        cost_estimate=cost,
    )(*args)


HALO = 8
UNROLL = 16
REACH = 6
GROUP = 4


def per_device_paired(
    labels, kappa_table, absorb_table, background, det_cells,
    v_kappa, v_absorb, q_kappa, q_absorb, beta_prev,
):
    sources, cx, cy, cz = background.shape
    n = lax.axis_size("src")
    planes, rows = 2 * cx, 2 * cy + HALO
    ny = cy * lax.axis_size("gy")
    dets = det_cells.shape[0]
    cells = planes * ny * cz
    groups = cx // n

    def swap_x(value):
        return lax.ppermute(value, "gx", [(0, 1), (1, 0)])

    def swap_core(value):
        return lax.ppermute(value, "gy", [(0, 1), (1, 0), (2, 3), (3, 2)])

    def along_z(value, k):
        return lax.ppermute(value, "src", [(i, i ^ k) for i in range(n)])

    block = (cx, cy, cz)
    float_block = lambda *shape: (shape, jnp.float32)
    raw_labels = (block, jnp.int32)
    packed, message = run(
        pack_kernel, (f32(2 * groups, cy, cz), f32(sources // 2 * cx + 2 * groups, cy, cz)),
        background, v_kappa, v_absorb, hbm=(0, 1, 2),
        scratch=(float_block(2, *v_kappa.shape),), copies=2 + sources // 2, mib=60,
    )
    long = pl.CostEstimate(flops=10**9, bytes_accessed=2**26, transcendentals=0)
    labels_came = swap_x(labels)
    came = swap_x(message)
    slabs = [along_z(packed, k) for k in range(1, n)]
    count, beta_row = run(
        functools.partial(count_kernel, ny=ny, nz=cz, half=2 * cy, halo=HALO),
        (f32(planes, rows, cz), f32(1, cz)), det_cells.reshape(1, dets), beta_prev, smem=(1,), after=(labels_came,),
        cost=pl.CostEstimate(flops=2 * planes * rows * cz * dets, bytes_accessed=planes * rows * cz * 4, transcendentals=0),
    )

    def across_y(value):
        return lax.ppermute(value, "gy", [(i, (i + 2) % 4) for i in range(4)])

    (joined,) = run(join_kernel, (f32(2 * groups * (n - 1), cy, cz),), *slabs, after=(count,))
    joined_came = swap_x(joined)
    (half_vector,) = run(own_half_kernel, (f32(2, *block),), v_kappa, v_absorb, joined)
    mine, fields = run(
        photon_kernel, (f32(planes, cy, cz), f32(2, planes, cy, cz)),
        background, labels, came, labels_came, after=(joined,), hbm=(0, 1), scratch=(raw_labels,), copies=3,
    )
    got = swap_core(fields)
    (vector,) = run(
        vector_kernel, (f32(2, planes, cy, cz),), half_vector, came, joined_came, after=(mine,)
    )
    edge = (f32(2, *edge_shape(planes, cz)),)
    (sent,) = run(photon_edge_kernel, edge, mine, fields, got, after=(vector,))
    photon_edge = across_y(sent)
    vector_got = swap_core(vector)
    (vector_sent,) = run(vector_edge_kernel, edge, vector, vector_got, after=(sent,))
    frame, wide = (planes, rows, cz), (planes + 2, rows, cz)
    float_frame, float_wide = float_block(*frame), float_block(*wide)
    coefs = (f32(*frame), f32(planes + 1, rows, cz), f32(*frame), f32(*frame))
    kap, *partial, sums = run(
        stencil_kernel, (f32(*wide), *coefs, f32(2, 8, cz)),
        kappa_table, absorb_table, mine, fields, got, count, after=(vector_sent,), cost=long,
        smem=(0, 1), scratch=(float_frame,),
    )
    diag, fx, fy, fz = run(
        halo_kernel, coefs, kappa_table, absorb_table, photon_edge, kap, *partial, smem=(0, 1)
    )
    phi, change, sent = run(
        first_kernel, (f32(*wide), f32(*frame), f32(4, GROUP * REACH + 8, cz)),
        diag, fx, fy, fz, count, sums, mine, got, vector, vector_got,
        photon_edge, across_y(vector_sent),
        scratch=(float_wide, float_frame, float_frame, float_wide, float_wide),
    )
    heard = across_y(sent)
    own, message = run(
        functools.partial(second_kernel, dets=dets),
        (f32(2, planes, cy, cz), f32(2, planes, cy, cz)),
        phi, change, diag, fx, fy, fz, count, sent, heard,
        scratch=(float_frame, float_wide, float_wide, float_frame, float_frame),
    )
    piece = f32(2, groups, cy, cz)
    got = swap_core(message)
    crossed, last = {}, ()
    for k in reversed(range(n)):
        last = run(functools.partial(send_kernel, k=k), (f32(1, *piece.shape),), own, got, after=last)
        crossed[k] = swap_x(last[0])
    (kept,) = run(keep_kernel, (f32(n, *piece.shape),), own, got, after=last)
    totals = {
        k: run(functools.partial(add_kernel, k=k), (piece,), kept, value)[0] for k, value in crossed.items()
    }
    received = {k: along_z(totals[k], k) for k in reversed(range(1, n))}
    (distant,) = run(sum_kernel, (piece,), *(received[k] for k in range(n // 2, n)), cost=long)
    parts = [distant, totals[0]] + [received[k] for k in range(1, n // 2)]
    w_k, w_a, tile = run(
        functools.partial(project_kernel, parts_n=len(parts), n=n),
        (f32(*v_kappa.shape), f32(*v_kappa.shape), f32(1, 128)),
        beta_row, *parts, v_kappa, v_absorb, q_kappa, q_absorb,
    )
    everyone = ("src", "gx", "gy")
    tiles = lax.all_to_all(jnp.broadcast_to(tile, (8 * n, 1, 128)), everyone, 0, 0)
    return tuple(run(
        functools.partial(final_kernel, cells=cells),
        (f32(*v_kappa.shape), f32(*v_kappa.shape), f32(2)),
        tiles, w_k, w_a, v_kappa, v_absorb, in_smem_out=(2,),
    ))


def paired_fits(mesh):
    return mesh.shape["gx"] == 2 and mesh.shape["gy"] == 4


def body_for(mesh):
    if not paired_fits(mesh):
        return per_device

    def chosen(*args):
        sources, cx, cy, cz = args[3].shape
        n = lax.axis_size("src")
        fits = sources == 4 and cz == 128 and cx % n == 0 and cx % GROUP == 0 and cy % HALO == 0 and n > 1 and n & (n - 1) == 0
        devices = 8 * n
        return (per_device_paired if fits and devices <= 128 else per_device)(*args)

    return chosen


def solution(mesh):
    return jax.shard_map(
        body_for(mesh),
        mesh=mesh,
        in_specs=(
            P("gx", "gy", None),
            P(),
            P(),
            P("src", "gx", "gy", None),
            P(),
            P("gx", "gy", "src"),
            P("gx", "gy", "src"),
            P("gx", "gy", "src"),
            P("gx", "gy", "src"),
            P(),
        ),
        out_specs=(P("gx", "gy", "src"), P("gx", "gy", "src"), P()),
        check_vma=False,
    )
```

```python
import functools

import jax
import jax.numpy as jnp
from jax import lax
from jax.experimental import pallas as pl
from jax.experimental.pallas import tpu as pltpu
from jax.sharding import PartitionSpec as P

ITERS = 6


lam_low = 0.02
lam_high = 24.1
eps_norm = 1e-06


def padded_2(block, sides, width):
    for axis, dim in sides:
        count = lax.axis_size(axis)
        forward = [(i, i + 1) for i in range(count - 1)]
        backward = [(target, source) for source, target in forward]
        low = lax.ppermute(
            lax.slice_in_dim(block, block.shape[dim] - width, None, axis=dim), axis, forward
        )
        high = lax.ppermute(lax.slice_in_dim(block, 0, width, axis=dim), axis, backward)
        block = jnp.concatenate([low, block, high], axis=dim)
    return block


def regional(labels, table):
    field = jnp.zeros(labels.shape, jnp.float32)
    for region in range(table.shape[0]):
        field = field + jnp.where(labels == region, table[region], 0.0)
    return field


def beside(padded):
    widths = [(0, 0)] * (padded.ndim - 1) + [(1, 1)]
    full = jnp.pad(padded, widths)
    return [
        full[..., 2:, 1:-1, 1:-1],
        full[..., :-2, 1:-1, 1:-1],
        full[..., 1:-1, 2:, 1:-1],
        full[..., 1:-1, :-2, 1:-1],
        full[..., 1:-1, 1:-1, 2:],
        full[..., 1:-1, 1:-1, :-2],
    ]


def chebyshev(rhs, apply_op):
    theta = 0.5 * (lam_high + lam_low)
    delta = 0.5 * (lam_high - lam_low)
    sigma = theta / delta
    rho = 1.0 / sigma
    solution = jnp.zeros_like(rhs)
    remain = rhs
    step_dir = rhs / theta
    for step in range(ITERS):
        solution = solution + step_dir
        if step + 1 < ITERS:
            remain = remain - apply_op(step_dir)
            rho_next = 1.0 / (2.0 * sigma - rho)
            step_dir = rho_next * rho * step_dir + 2.0 * rho_next / delta * remain
            rho = rho_next
    return solution


def per_device(
    labels,
    kappa_table,
    absorb_table,
    background,
    det_cells,
    v_kappa,
    v_absorb,
    q_kappa,
    q_absorb,
    beta_prev,
):
    sources, cx, cy, cz = background.shape
    kappa = regional(labels, kappa_table)
    absorb = regional(labels, absorb_table)
    full_k, full_a = (
        lax.all_gather(v_kappa, "src", axis=2, tiled=True),
        lax.all_gather(v_absorb, "src", axis=2, tiled=True),
    )
    stacked = jnp.concatenate([background, kappa[None], full_k[None]], axis=0)
    rims = padded_2(stacked, (("gx", 1), ("gy", 2)), 1)
    near_all = beside(rims)
    kappa_faces = [0.5 * (kappa + near[sources]) for near in near_all]
    vk_faces = [0.5 * (full_k + near[sources + 1]) for near in near_all]
    phi_near = [near[:sources] for near in near_all]

    def apply_op(field):
        padded = padded_2(field, (("gx", 1), ("gy", 2)), 1)
        result = absorb * field
        for face, near in zip(kappa_faces, beside(padded)):
            result = result + face * (field - near)
        return result

    rhs = full_a * background
    for face, near in zip(vk_faces, phi_near):
        rhs = rhs + face * (background - near)
    rhs = -rhs
    change = chebyshev(rhs, apply_op)
    span_y = cy * lax.axis_size("gy")
    ix = det_cells // (span_y * cz)
    iy = det_cells // cz % span_y
    iz = det_cells % cz
    anchor_x = lax.axis_index("gx") * cx
    anchor_y = lax.axis_index("gy") * cy
    owned = (ix >= anchor_x) & (ix < anchor_x + cx) & (iy >= anchor_y) & (iy < anchor_y + cy)
    local = jnp.where(owned, ((ix - anchor_x) * cy + (iy - anchor_y)) * cz + iz, 0)
    seen_part = jnp.where(owned[None, :], change.reshape(sources, -1)[:, local], 0.0)
    base_part = jnp.where(owned[None, :], background.reshape(sources, -1)[:, local], 0.0)
    seen, base = lax.psum((seen_part, base_part), ("gx", "gy"))
    total = jnp.sum(base, axis=1, keepdims=True)
    mean_base = total / det_cells.shape[0]
    ratio = base / total
    jv_vals = (seen - ratio * jnp.sum(seen, axis=1, keepdims=True)) / mean_base
    weight = (jv_vals - jnp.sum(ratio * jv_vals, axis=1, keepdims=True)) / mean_base
    deposit = jnp.where(owned[None, :], weight, 0.0)
    source = (
        jnp.zeros((sources, cx * cy * cz), jnp.float32)
        .at[:, local]
        .add(deposit)
        .reshape(change.shape)
    )
    dual = chebyshev(source, apply_op)
    dual_rims = padded_2(dual, (("gx", 1), ("gy", 2)), 1)
    grad_a = -jnp.sum(background * dual, axis=0)
    grad_k = jnp.zeros_like(kappa)
    for near_phi, near_dual in zip(phi_near, beside(dual_rims)):
        grad_k = grad_k - 0.5 * jnp.sum((background - near_phi) * (dual - near_dual), axis=0)
    summed_k, summed_a = lax.psum((grad_k, grad_a), "src")
    slab = v_kappa.shape[2]
    offset = lax.axis_index("src") * slab
    hv_k = lax.dynamic_slice_in_dim(summed_k, offset, slab, 2)
    hv_a = lax.dynamic_slice_in_dim(summed_a, offset, slab, 2)
    cell_count = cx * lax.axis_size("gx") * cy * lax.axis_size("gy") * cz
    w_k = hv_k - beta_prev[0] * q_kappa
    w_a = hv_a - beta_prev[0] * q_absorb
    local_wv = jnp.sum(w_k * v_kappa) + jnp.sum(w_a * v_absorb)
    local_vv = jnp.sum(v_kappa * v_kappa) + jnp.sum(v_absorb * v_absorb)
    wv_sum, vv_sum = lax.psum((local_wv, local_vv), ("src", "gx", "gy"))
    alpha = wv_sum / cell_count / (vv_sum / cell_count + eps_norm)
    r_k = w_k - alpha * v_kappa
    r_a = w_a - alpha * v_absorb
    rr_sum = lax.psum(jnp.sum(r_k * r_k) + jnp.sum(r_a * r_a), ("src", "gx", "gy"))
    beta = jnp.sqrt(rr_sum / cell_count + eps_norm)
    return (r_k / beta, r_a / beta, jnp.stack([alpha, beta]))


def chebyshev_scalars():
    theta = 0.5 * (lam_high + lam_low)
    delta = 0.5 * (lam_high - lam_low)
    sigma = theta / delta
    rho = 1.0 / sigma
    pairs = []
    for _ in range(ITERS - 1):
        rho_next = 1.0 / (2.0 * sigma - rho)
        pairs.append((rho_next * rho, 2.0 * rho_next / delta))
        rho = rho_next
    return theta, pairs


def places(split):
    g = lax.axis_index("gy")
    return lax.axis_index("src"), lax.axis_index("gx"), g // split, g % split


def shifted(value, step, axis):
    return pltpu.roll(value, step % value.shape[axis], axis)


def index_along(shape, axis):
    return lax.broadcasted_iota(jnp.int32, shape, axis)


def beyond(value, step, axis):
    size = value.shape[axis]
    at = index_along(value.shape, axis)
    edge = size - 1 if step == 1 else 0
    return jnp.where(at == edge, 0.0, shifted(value, -step, axis))


def packed_planes(ref, q):
    per = 128 // ref.shape[2]
    return jnp.concatenate([ref[per * q + j] for j in range(per)], axis=1)


def pack_kernel(bg, vk, va, packed, message, v_in, sems):
    _, x, _, _ = places(2)
    half = bg.shape[0] // 2
    cx = bg.shape[1]
    copies = [
        pltpu.make_async_copy(src, dst, sems.at[i])
        for i, (src, dst) in enumerate((
            (vk, v_in.at[0]),
            (va, v_in.at[1]),
            *((bg.at[half * (1 - x) + i], message.at[pl.ds(cx * i, cx)]) for i in range(half)),
        ))
    ]
    for copy in copies:
        copy.start()
    groups = packed.shape[0] // 2
    for f in range(2):
        copies[f].wait()
        for q in range(groups):
            planes = packed_planes(v_in.at[f], q)
            packed[groups * f + q] = planes
            message[cx * half + groups * f + q] = planes
    for copy in copies[2:]:
        copy.wait()


def count_kernel(dets, beta_prev, count, beta_row, *, ny, nz, half, halo):
    beta_row[...] = jnp.full(beta_row.shape, beta_prev[0])
    _, _, y, _ = places(2)
    planes, rows, _ = count.shape
    flat = dets[...]
    iz = flat % nz
    line = flat // nz
    iy = line % ny
    ix = line // ny
    row = iy - (half - halo) * y
    spot = jnp.where((row >= 0) & (row < rows), ix * rows + row, -1)
    dets_n = flat.shape[1]
    at_z = (index_along((nz, dets_n), 0) == iz).astype(jnp.float32).astype(jnp.bfloat16)

    def body(i, carry):
        here = index_along((2 * rows, dets_n), 0) + i * (2 * rows)
        hot = (here == spot).astype(jnp.float32).astype(jnp.bfloat16)
        found = lax.dot_general(hot, at_z, (((1,), (1,)), ((), ())), preferred_element_type=jnp.float32)
        count[pl.ds(2 * i, 2)] = found.reshape(2, rows, nz)
        return carry

    lax.fori_loop(0, planes // 2, body, 0)


def photon_kernel(bg, labels, msg, labels_came, mine, fields, raw, sems):
    _, x, _, c = places(2)
    half = bg.shape[0] // 2
    cx = labels.shape[0]
    here, there = cx * x, cx * (1 - x)
    copies = [
        pltpu.make_async_copy(src, dst, sems.at[i])
        for i, (src, dst) in enumerate((
            (bg.at[half * x + c], mine.at[pl.ds(here, cx)]),
            (bg.at[half * x + 1 - c], fields.at[0, pl.ds(here, cx)]),
            (labels, raw),
        ))
    ]
    for copy in copies:
        copy.start()
    mine[pl.ds(there, cx)] = msg[pl.ds(cx * c, cx)]
    fields[0, pl.ds(there, cx)] = msg[pl.ds(cx * (1 - c), cx)]
    fields[1, pl.ds(there, cx)] = labels_came[...].astype(jnp.float32)
    for copy in copies:
        copy.wait()
    fields[1, pl.ds(here, cx)] = raw[...].astype(jnp.float32)


def unpacked(blocks, groups, s, store):
    n = len(blocks)
    cy, lanes = blocks[0][0].shape
    slab = lanes // n
    lane = index_along((cy, lanes), 1) // slab
    for f in range(2):
        for q in range(groups):
            values = [block[groups * f + q] for block in blocks]
            for j in range(n):
                plane = jnp.zeros((cy, lanes), jnp.float32)
                for k in range(n):
                    home = s ^ k
                    moved = pltpu.roll(values[k], ((home - j + n) % n) * slab, 1)
                    plane = jnp.where(lane == home, moved, plane)
                store(f, n * q + j, plane)


def join_kernel(*refs):
    joined, size = refs[-1], refs[0].shape[0]
    for i, ref in enumerate(refs[:-1]):
        joined[pl.ds(size * i, size)] = ref[...]


def own_half_kernel(vk, va, joined, half):
    s, _, _, _ = places(2)
    size = half.shape[1]
    groups = joined.shape[0] // 2 // (128 // vk.shape[2] - 1)
    n = size // groups
    own = [packed_planes(ref, q) for ref in (vk, va) for q in range(groups)]
    blocks = [own] + [[joined[2 * groups * k + i] for i in range(2 * groups)] for k in range(n - 1)]

    def store(f, i, plane):
        half[f, i] = plane

    unpacked(blocks, groups, s, store)


def vector_kernel(half, msg, joined, fields):
    s, x, _, _ = places(2)
    cx = half.shape[1]
    fields[:, pl.ds(cx * x, cx)] = half[...]
    n = lax.axis_size("src")
    groups = cx // n
    own = msg.shape[0] - 2 * groups
    blocks = [[msg[own + i] for i in range(2 * groups)]]
    blocks += [[joined[2 * groups * k + i] for i in range(2 * groups)] for k in range(n - 1)]
    there = cx * (1 - x)

    def store(f, i, plane):
        fields[f, there + i] = plane

    unpacked(blocks, groups, s, store)


def edge_shape(planes, lanes):
    return planes // GROUP, GROUP * REACH, lanes


def packed_edges(tiles):
    return jnp.concatenate([tile[:REACH] for tile in tiles], axis=0)


def edge_tile(packed, j, y):
    rows = packed[REACH * j : REACH * (j + 1)]
    tile = jnp.concatenate([rows, jnp.zeros((HALO - REACH, rows.shape[1]), jnp.float32)], axis=0)
    return jnp.where(y == 0, tile, shifted(tile, HALO - REACH, 0))


def near_rows(ref, i, first, y):
    tile = ref[i, pl.ds(first, HALO), :]
    return jnp.where(y == 0, shifted(tile, REACH - HALO, 0), tile)


def edges_of(own, got, edge, y, c):
    first = (own.shape[1] - HALO) * (1 - y)
    for g in range(edge.shape[0]):
        edge[g] = packed_edges([
            jnp.where(c != y, near_rows(own, GROUP * g + j, first, y), near_rows(got, GROUP * g + j, first, y))
            for j in range(GROUP)
        ])


def photon_edge_kernel(mine, fields, got, edge):
    _, _, y, c = places(2)
    edges_of(mine, got.at[0], edge.at[0], y, c)
    edges_of(fields.at[1], got.at[1], edge.at[1], y, c)


def vector_edge_kernel(fields, got, edge):
    _, _, y, c = places(2)
    for f in range(2):
        edges_of(fields.at[f], got.at[f], edge.at[f], y, c)


def solve(b, bufs, diag, fx, fy, fz, unroll):
    planes = b.shape[0]
    _, pairs = chebyshev_scalars()
    for step, (keep, push) in enumerate(pairs):
        src, dst = bufs[step % 2], bufs[(step + 1) % 2]

        def body(i, carry):
            u = src[i + 1]
            coef_y, coef_z = fy[i], fz[i]
            left = b[i] - diag[i] * u
            left = left + fx[i] * src[i] + fx[i + 1] * src[i + 2]
            left = left + coef_y * shifted(u, -1, 0) + shifted(coef_y * u, 1, 0)
            left = left + coef_z * shifted(u, -1, 1) + shifted(coef_z * u, 1, 1)
            change = u if step == 0 else u - dst[i + 1]
            dst[i + 1] = u + keep * change + push * left
            return carry

        lax.fori_loop(0, planes, body, 0, unroll=unroll)
    return bufs[len(pairs) % 2]


def folded(value):
    return jnp.sum(value.reshape(-1, 8, value.shape[1]), axis=0)


def framed_own(ref, shift, own, got, y, c):
    planes, cy, _ = own.shape
    there = pl.ds(shift, planes)
    base = HALO * y
    ref[there, pl.ds(base + cy * c, cy), :] = own[...]
    ref[there, pl.ds(base + cy * (1 - c), cy), :] = got[...]


def framed(ref, shift, own, got, edge, y, c):
    framed_own(ref, shift, own, got, y, c)
    cy = own.shape[1]
    for g in range(edge.shape[0]):
        packed = edge[g]
        for j in range(GROUP):
            ref[shift + GROUP * g + j, pl.ds(2 * cy * (1 - y), HALO), :] = edge_tile(packed, j, y)


def blank_ends(*refs):
    for ref in refs:
        blank = jnp.zeros(ref.shape[1:], jnp.float32)
        ref[0] = blank
        ref[ref.shape[0] - 1] = blank


def owned_rows(shape, base, count):
    at_row = index_along(shape, 0)
    return (at_row >= base) & (at_row < base + count)


def table_rows(kap_table, abs_table, shape):
    lane = index_along(shape, 1)
    kap_row = abs_row = jnp.zeros(shape, jnp.float32)
    for region in range(kap_table.shape[0]):
        kap_row = jnp.where(lane == region, kap_table[region], kap_row)
        abs_row = jnp.where(lane == region, abs_table[region], abs_row)
    return kap_row, abs_row


def stencil_kernel(
    kap_table, abs_table, mine, fields, got, count,
    kap, diag, fx, fy, fz, sums,
    labels,
):
    _, _, y, c = places(2)
    planes, cy, lanes = mine.shape
    rows = 2 * cy + HALO
    base = HALO * y
    framed_own(labels, 0, fields.at[1], got.at[1], y, c)
    labels[:, pl.ds(2 * cy * (1 - y), HALO), :] = jnp.zeros((planes, HALO, lanes), jnp.float32)
    blank_ends(kap)
    shape = (rows, lanes)
    lane = index_along(shape, 1)
    kap_row, abs_row = table_rows(kap_table, abs_table, shape)
    owned = owned_rows(shape, base, 2 * cy)

    def look_up(i, carry):
        at = labels[i].astype(jnp.int32)
        kap[i + 1] = jnp.where(owned, jnp.take_along_axis(kap_row, at, axis=1), 0.0)
        diag[i] = jnp.take_along_axis(abs_row, at, axis=1)
        return carry

    lax.fori_loop(0, planes, look_up, 0, unroll=4)
    fx[0] = 0.5 * kap[1]

    def set_up(i, carry):
        k = kap[i + 1]
        along_x = 0.5 * (k + kap[i + 2])
        along_y, along_z = 0.5 * (k + beyond(k, 1, 0)), 0.5 * (k + beyond(k, 1, 1))
        fx[i + 1] = along_x
        fy[i] = jnp.where(index_along(shape, 0) == rows - 1, 0.0, along_y)
        fz[i] = jnp.where(lane == lanes - 1, 0.0, along_z)
        back_y, back_z = 0.5 * (k + beyond(k, -1, 0)), 0.5 * (k + beyond(k, -1, 1))
        diag[i] = diag[i] + fx[i] + along_x + along_y + back_y + along_z + back_z
        total, square = carry
        for p, at in ((mine[i], c), (got[0, i], 1 - c)):
            part = count[i, pl.ds(base + cy * at, cy), :] * p
            total, square = total + folded(part), square + folded(part * p)
        return total, square

    zero = jnp.zeros((8, lanes), jnp.float32)
    sums[0], sums[1] = lax.fori_loop(0, planes, set_up, (zero, zero), unroll=4)


def halo_kernel(kap_table, abs_table, edge, kap, diag_in, fx_in, fy_in, fz_in, diag, fx, fy, fz):
    _, _, y, _ = places(2)
    planes, rows, lanes = diag.shape
    for ref, old in ((diag, diag_in), (fx, fx_in), (fy, fy_in), (fz, fz_in)):
        ref[...] = old[...]
    shape = (HALO, lanes)
    lane, row = index_along(shape, 1), index_along(shape, 0)
    kap_row, abs_row = table_rows(kap_table, abs_table, shape)
    low = y == 0
    here = pl.ds((rows - HALO) * (1 - y), HALO)
    beside_it = pl.ds((rows - 2 * HALO) * (1 - y) + HALO * y, HALO)
    labels = [edge_tile(edge[1, i // GROUP], i % GROUP, y).astype(jnp.int32) for i in range(planes)]
    tiles = [jnp.take_along_axis(kap_row, at, axis=1) for at in labels]
    none = jnp.zeros(shape, jnp.float32)
    before = 0.5 * tiles[0]
    fx[0, here, :] = before
    for i, k in enumerate(tiles):
        after = 0.5 * (k + (tiles[i + 1] if i + 1 < planes else none))
        own = kap[i + 1, beside_it, :]
        up, down = shifted(k, -1, 0), shifted(k, 1, 0)
        k_up = jnp.where(row == HALO - 1, jnp.where(low, 0.0, shifted(own, -1, 0)), up)
        k_down = jnp.where(row == 0, jnp.where(low, shifted(own, 1, 0), 0.0), down)
        along_y, back_y = 0.5 * (k + k_up), 0.5 * (k + k_down)
        along_z, back_z = 0.5 * (k + beyond(k, 1, 1)), 0.5 * (k + beyond(k, -1, 1))
        fx[i + 1, here, :] = after
        fy[i, here, :] = jnp.where(low & (row == HALO - 1), 0.0, along_y)
        fz[i, here, :] = jnp.where(lane == lanes - 1, 0.0, along_z)
        absorb = jnp.take_along_axis(abs_row, labels[i], axis=1)
        diag[i, here, :] = absorb + before + after + along_y + back_y + along_z + back_z
        before = after
        face_up = jnp.where(low & (row == HALO - 1), 0.5 * up, 0.0)
        face_down = jnp.where(low | (row > 0), 0.0, 0.5 * down)
        fy[i, beside_it, :] = fy_in[i, beside_it, :] + face_up
        diag[i, beside_it, :] = diag_in[i, beside_it, :] + face_up + face_down


def density_kernel(mine, got, edge, phi, phi_y, phi_z):
    _, _, y, c = places(2)
    framed(phi, 1, mine, got.at[0], edge.at[0], y, c)
    blank_ends(phi)

    def differ(i, carry):
        p = phi[i + 1]
        phi_y[i], phi_z[i] = p - beyond(p, 1, 0), p - beyond(p, 1, 1)
        return carry

    lax.fori_loop(0, phi_y.shape[0], differ, 0, unroll=4)


def first_kernel(
    phi, phi_y, phi_z, diag, fx, fy, fz, count, sums, vector, got_vector, edge,
    change, message,
    vk, va, b, buf_a, buf_b,
):
    _, _, y, c = places(2)
    planes, rows, lanes = change.shape
    cy = vector.shape[2]
    framed(vk, 1, vector.at[0], got_vector.at[0], edge.at[0], y, c)
    framed(va, 0, vector.at[1], got_vector.at[1], edge.at[1], y, c)
    blank_ends(vk, buf_a, buf_b)
    theta, _ = chebyshev_scalars()

    def set_up(i, carry):
        v, p = vk[i + 1], phi[i + 1]
        total = 0.5 * (v + vk[i]) * (p - phi[i]) + 0.5 * (v + vk[i + 2]) * (p - phi[i + 2])
        for axis, step in enumerate((phi_y, phi_z)):
            flow = 0.5 * (v + beyond(v, 1, axis)) * step[i]
            first = index_along(v.shape, axis) == 0
            total = total + flow + jnp.where(first, 0.5 * v * p, -shifted(flow, 1, axis))
        total = -(va[i] * p + total)
        b[i] = total
        buf_a[i + 1] = total * (1.0 / theta)
        return carry

    lax.fori_loop(0, planes, set_up, 0, unroll=4)
    found = solve(b, (buf_a, buf_b), diag, fx, fy, fz, UNROLL)
    owned = owned_rows((rows, lanes), HALO * y, 2 * cy)

    def add_up(i, carry):
        u = found[i + 1]
        change[i] = u
        part = jnp.where(owned, count[i], 0.0) * u
        return carry[0] + folded(part), carry[1] + folded(part * phi[i + 1])

    zero = jnp.zeros((8, lanes), jnp.float32)
    seen, cross = lax.fori_loop(0, planes, add_up, (zero, zero), unroll=4)
    first = (2 * cy - HALO) * (1 - y) + HALO * y
    size = GROUP * REACH
    for g in range(planes // GROUP):
        message[pl.ds(size * g, size), :] = packed_edges(
            [near_rows(found, 1 + GROUP * g + j, first, y) for j in range(GROUP)]
        )
    rows_of_sums = [jnp.sum(part, axis=0, keepdims=True) for part in (sums[0], seen, cross, sums[1])]
    message[pl.ds(REACH * planes, 8), :] = jnp.concatenate([*rows_of_sums, zero[:4]], axis=0)


def second_kernel(
    phi, phi_y, phi_z, change, diag, fx, fy, fz, count, sent, came,
    own, message,
    b, buf_a, buf_b, grad_k, grad_a,
    *, dets,
):
    _, _, y, c = places(2)
    planes, rows, lanes = change.shape
    cy = (rows - HALO) // 2
    base = HALO * y
    edge = pl.ds(2 * cy * (1 - y), HALO)
    tail = pl.ds(REACH * planes, 8)
    sums = jnp.sum(sent[tail, :] + came[tail, :], axis=1, keepdims=True)
    total, seen_sum, cross, square = (sums[g : g + 1] for g in range(4))
    mean = total / dets
    part = seen_sum / total
    level = (cross - part * square) / (total * mean)
    inverse = 1.0 / mean
    blank_ends(buf_a, buf_b)
    theta, _ = chebyshev_scalars()

    def weighted(n, u, p):
        return n * (((u - p * part) * inverse - level) * inverse)

    def set_up(i, carry):
        value = weighted(count[i], change[i], phi[i + 1])
        b[i] = value
        buf_a[i + 1] = value * (1.0 / theta)
        return carry

    lax.fori_loop(0, planes, set_up, 0, unroll=4)
    size = GROUP * REACH
    for i in range(planes):
        u = edge_tile(came[pl.ds(size * (i // GROUP), size), :], i % GROUP, y)
        value = weighted(count[i, edge, :], u, phi[i + 1, edge, :])
        b[i, edge, :] = value
        buf_a[i + 1, edge, :] = value * (1.0 / theta)
    dual = solve(b, (buf_a, buf_b), diag, fx, fy, fz, UNROLL)

    def product(i, carry):
        p, u = phi[i + 1], dual[i + 1]
        grad = (p - phi[i]) * (u - dual[i]) + (p - phi[i + 2]) * (u - dual[i + 2])
        both = p * u
        for axis, step in enumerate((phi_y, phi_z)):
            flow = step[i] * (u - beyond(u, 1, axis))
            first = index_along(p.shape, axis) == 0
            grad = grad + flow + jnp.where(first, both, shifted(flow, 1, axis))
        grad_k[i] = -0.5 * grad
        grad_a[i] = -both
        for f, ref in enumerate((grad_k, grad_a)):
            own[f, i] = ref[i, pl.ds(base + cy * c, cy), :]
            message[f, i] = ref[i, pl.ds(base + cy * (1 - c), cy), :]
        return carry

    lax.fori_loop(0, planes, product, 0, unroll=4)


def packed_slabs(own, came, half, choices, outs):
    s, _, _, _ = places(2)
    _, planes, cy, lanes = own.shape
    n = planes // 2 // outs.shape[2]
    slab = lanes // n
    lane = index_along((cy, lanes), 1) // slab
    for f in range(2):
        for q in range(outs.shape[2]):
            at = planes // 2 * half + n * q
            parts = [own[f, at + j] + came[f, at + j] for j in range(n)]
            for i, k in enumerate(choices):
                to = s ^ k
                piece = jnp.zeros((cy, lanes), jnp.float32)
                for j in range(n):
                    moved = pltpu.roll(parts[j], ((j - to + n) % n) * slab, 1)
                    piece = jnp.where(lane == j, moved, piece)
                outs[i, f, q] = piece


def send_kernel(own, came, out, *, k):
    _, x, _, _ = places(2)
    packed_slabs(own, came, 1 - x, (k,), out)


def keep_kernel(own, came, kept):
    _, x, _, _ = places(2)
    packed_slabs(own, came, x, range(kept.shape[0]), kept)


def add_kernel(kept, came, out, *, k):
    out[...] = kept[k] + came[0]


def sum_kernel(*refs):
    total = refs[0][...]
    for ref in refs[1:-1]:
        total = total + ref[...]
    refs[-1][...] = total


def project_kernel(*refs, parts_n, n):
    beta_prev = refs[0]
    parts = refs[1 : 1 + parts_n]
    vk, va, qk, qa, w_k, w_a, tile = refs[1 + parts_n :]
    slab = 128 // n
    for f, (q_ref, w) in enumerate(((qk, w_k), (qa, w_a))):
        for q in range(vk.shape[0] // n):
            whole = sum(part[f, q] for part in parts[1:]) + parts[0][f, q]
            for j in range(n):
                i = n * q + j
                w[i] = whole[:, slab * j : slab * (j + 1)] - beta_prev[:, : vk.shape[2]] * q_ref[i]

    def total(value):
        return jnp.sum(jnp.sum(jnp.sum(value, axis=0), axis=0, keepdims=True), axis=1, keepdims=True)

    wk, wa, v_k, v_a = w_k[...], w_a[...], vk[...], va[...]
    wv = total(wk * v_k + wa * v_a)
    vv = total(v_k * v_k + v_a * v_a)
    a = jnp.where(vv > 0.0, wv / jnp.where(vv > 0.0, vv, 1.0), 0.0)
    u_k, u_a = wk - a * v_k, wa - a * v_a
    uv = total(u_k * v_k + u_a * v_a)
    uu = total(u_k * u_k + u_a * u_a)
    lane = index_along((1, 128), 1)
    values = jnp.zeros((1, 128), jnp.float32)
    for i, value in enumerate((wv, vv, a, uv, uu)):
        values = jnp.where(lane == i, value, values)
    tile[...] = values


def final_kernel(tiles, w_k, w_a, vk, va, next_k, next_a, coefs, *, cells):
    tile = jnp.concatenate([tiles[i] for i in range(tiles.shape[0])], axis=0)
    wv, vv, a, uv, uu = (tile[:, i : i + 1] for i in range(5))
    wv_sum = jnp.sum(wv, axis=0, keepdims=True)
    vv_sum = jnp.sum(vv, axis=0, keepdims=True)
    alpha = wv_sum / cells / (vv_sum / cells + eps_norm)
    off = alpha - a
    rr = jnp.sum(uu - 2.0 * off * uv + off * off * vv, axis=0, keepdims=True)
    beta = jnp.sqrt(rr / cells + eps_norm)
    next_k[...] = (w_k[...] - alpha * vk[...]) / beta
    next_a[...] = (w_a[...] - alpha * va[...]) / beta
    coefs[0] = jnp.sum(alpha)
    coefs[1] = jnp.sum(beta)


def f32(*shape):
    return jax.ShapeDtypeStruct(shape, jnp.float32)


def run(kernel, outs, *args, after=(), scratch=(), copies=0, smem=(), hbm=(), mib=16, in_smem_out=(), cost=None):
    vmem = pl.BlockSpec(memory_space=pltpu.VMEM)
    scalar = pl.BlockSpec(memory_space=pltpu.SMEM)
    far = pl.BlockSpec(memory_space=pltpu.HBM)
    held = [pltpu.VMEM(shape, dtype) for shape, dtype in scratch]
    used, waits = len(args), len(after)

    def body(*refs):
        kernel(*refs[:used], *refs[used + waits :])

    args = (*args, *after)
    if copies:
        held.append(pltpu.SemaphoreType.DMA((copies,)))
    return pl.pallas_call(
        body if waits else kernel,
        out_shape=tuple(outs),
        in_specs=[scalar if i in smem else far if i in hbm else vmem for i in range(len(args))],
        out_specs=tuple(scalar if i in in_smem_out else vmem for i in range(len(outs))),
        scratch_shapes=held,
        compiler_params=pltpu.CompilerParams(vmem_limit_bytes=mib * 2**20),
        cost_estimate=cost,
    )(*args)


HALO = 8
UNROLL = 16
REACH = 6
GROUP = 4


def per_device_paired(
    labels, kappa_table, absorb_table, background, det_cells,
    v_kappa, v_absorb, q_kappa, q_absorb, beta_prev,
):
    sources, cx, cy, cz = background.shape
    n = lax.axis_size("src")
    planes, rows = 2 * cx, 2 * cy + HALO
    ny = cy * lax.axis_size("gy")
    dets = det_cells.shape[0]
    cells = planes * ny * cz
    groups = cx // n

    def swap_x(value):
        return lax.ppermute(value, "gx", [(0, 1), (1, 0)])

    def swap_core(value):
        return lax.ppermute(value, "gy", [(0, 1), (1, 0), (2, 3), (3, 2)])

    def along_z(value, k):
        return lax.ppermute(value, "src", [(i, i ^ k) for i in range(n)])

    block = (cx, cy, cz)
    float_block = lambda *shape: (shape, jnp.float32)
    raw_labels = (block, jnp.int32)
    packed, message = run(
        pack_kernel, (f32(2 * groups, cy, cz), f32(sources // 2 * cx + 2 * groups, cy, cz)),
        background, v_kappa, v_absorb, hbm=(0, 1, 2),
        scratch=(float_block(2, *v_kappa.shape),), copies=2 + sources // 2, mib=60,
    )
    long = pl.CostEstimate(flops=10**9, bytes_accessed=2**26, transcendentals=0)
    labels_came = swap_x(labels)
    came = swap_x(message)
    slabs = [along_z(packed, k) for k in range(1, n)]
    count, beta_row = run(
        functools.partial(count_kernel, ny=ny, nz=cz, half=2 * cy, halo=HALO),
        (f32(planes, rows, cz), f32(1, cz)), det_cells.reshape(1, dets), beta_prev, smem=(1,), after=(labels_came,),
        cost=pl.CostEstimate(flops=2 * planes * rows * cz * dets, bytes_accessed=planes * rows * cz * 4, transcendentals=0),
    )

    def across_y(value):
        return lax.ppermute(value, "gy", [(i, (i + 2) % 4) for i in range(4)])

    (joined,) = run(join_kernel, (f32(2 * groups * (n - 1), cy, cz),), *slabs, after=(count,))
    joined_came = swap_x(joined)
    (half_vector,) = run(own_half_kernel, (f32(2, *block),), v_kappa, v_absorb, joined)
    mine, fields = run(
        photon_kernel, (f32(planes, cy, cz), f32(2, planes, cy, cz)),
        background, labels, came, labels_came, after=(joined,), hbm=(0, 1), scratch=(raw_labels,), copies=3,
    )
    got = swap_core(fields)
    (vector,) = run(
        vector_kernel, (f32(2, planes, cy, cz),), half_vector, came, joined_came, after=(mine,)
    )
    edge = (f32(2, *edge_shape(planes, cz)),)
    (sent,) = run(photon_edge_kernel, edge, mine, fields, got, after=(vector,))
    photon_edge = across_y(sent)
    vector_got = swap_core(vector)
    (vector_sent,) = run(vector_edge_kernel, edge, vector, vector_got, after=(sent,))
    frame, wide = (planes, rows, cz), (planes + 2, rows, cz)
    float_frame, float_wide = float_block(*frame), float_block(*wide)
    coefs = (f32(*frame), f32(planes + 1, rows, cz), f32(*frame), f32(*frame))
    kap, *partial, sums = run(
        stencil_kernel, (f32(*wide), *coefs, f32(2, 8, cz)),
        kappa_table, absorb_table, mine, fields, got, count, after=(vector_sent,), cost=long,
        smem=(0, 1), scratch=(float_frame,),
    )
    diag, fx, fy, fz = run(
        halo_kernel, coefs, kappa_table, absorb_table, photon_edge, kap, *partial, smem=(0, 1)
    )
    densities = run(
        density_kernel, (f32(*wide), f32(*frame), f32(*frame)), mine, got, photon_edge, after=(fz,)
    )
    change, sent = run(
        first_kernel, (f32(*frame), f32(REACH * planes + 8, cz)),
        *densities, diag, fx, fy, fz, count, sums, vector, vector_got, across_y(vector_sent),
        scratch=(float_wide, float_frame, float_frame, float_wide, float_wide),
    )
    heard = across_y(sent)
    own, message = run(
        functools.partial(second_kernel, dets=dets),
        (f32(2, planes, cy, cz), f32(2, planes, cy, cz)),
        *densities, change, diag, fx, fy, fz, count, sent, heard,
        scratch=(float_frame, float_wide, float_wide, float_frame, float_frame),
    )
    piece = f32(2, groups, cy, cz)
    got = swap_core(message)
    crossed, last = {}, ()
    for k in reversed(range(n)):
        last = run(functools.partial(send_kernel, k=k), (f32(1, *piece.shape),), own, got, after=last)
        crossed[k] = swap_x(last[0])
    (kept,) = run(keep_kernel, (f32(n, *piece.shape),), own, got, after=last)
    totals = {
        k: run(functools.partial(add_kernel, k=k), (piece,), kept, value)[0] for k, value in crossed.items()
    }
    received = {k: along_z(totals[k], k) for k in reversed(range(1, n))}
    (distant,) = run(sum_kernel, (piece,), *(received[k] for k in range(n // 2, n)), cost=long)
    parts = [distant, totals[0]] + [received[k] for k in range(1, n // 2)]
    w_k, w_a, tile = run(
        functools.partial(project_kernel, parts_n=len(parts), n=n),
        (f32(*v_kappa.shape), f32(*v_kappa.shape), f32(1, 128)),
        beta_row, *parts, v_kappa, v_absorb, q_kappa, q_absorb,
    )
    everyone = ("src", "gx", "gy")
    tiles = lax.all_to_all(jnp.broadcast_to(tile, (8 * n, 1, 128)), everyone, 0, 0)
    return tuple(run(
        functools.partial(final_kernel, cells=cells),
        (f32(*v_kappa.shape), f32(*v_kappa.shape), f32(2)),
        tiles, w_k, w_a, v_kappa, v_absorb, in_smem_out=(2,),
    ))


def paired_fits(mesh):
    return mesh.shape["gx"] == 2 and mesh.shape["gy"] == 4


def body_for(mesh):
    if not paired_fits(mesh):
        return per_device

    def chosen(*args):
        sources, cx, cy, cz = args[3].shape
        n = lax.axis_size("src")
        fits = sources == 4 and cz == 128 and cx % n == 0 and cx % GROUP == 0 and cy % HALO == 0 and n > 1 and n & (n - 1) == 0
        devices = 8 * n
        return (per_device_paired if fits and devices <= 128 else per_device)(*args)

    return chosen


def solution(mesh):
    return jax.shard_map(
        body_for(mesh),
        mesh=mesh,
        in_specs=(
            P("gx", "gy", None),
            P(),
            P(),
            P("src", "gx", "gy", None),
            P(),
            P("gx", "gy", "src"),
            P("gx", "gy", "src"),
            P("gx", "gy", "src"),
            P("gx", "gy", "src"),
            P(),
        ),
        out_specs=(P("gx", "gy", "src"), P("gx", "gy", "src"), P()),
        check_vma=False,
    )
```

```python
import functools

import jax
import jax.numpy as jnp
from jax import lax
from jax.experimental import pallas as pl
from jax.experimental.pallas import tpu as pltpu
from jax.sharding import PartitionSpec as P

ITERS = 6


lam_low = 0.02
lam_high = 24.1
eps_norm = 1e-06


def padded_2(block, sides, width):
    for axis, dim in sides:
        count = lax.axis_size(axis)
        forward = [(i, i + 1) for i in range(count - 1)]
        backward = [(target, source) for source, target in forward]
        low = lax.ppermute(
            lax.slice_in_dim(block, block.shape[dim] - width, None, axis=dim), axis, forward
        )
        high = lax.ppermute(lax.slice_in_dim(block, 0, width, axis=dim), axis, backward)
        block = jnp.concatenate([low, block, high], axis=dim)
    return block


def regional(labels, table):
    field = jnp.zeros(labels.shape, jnp.float32)
    for region in range(table.shape[0]):
        field = field + jnp.where(labels == region, table[region], 0.0)
    return field


def beside(padded):
    widths = [(0, 0)] * (padded.ndim - 1) + [(1, 1)]
    full = jnp.pad(padded, widths)
    return [
        full[..., 2:, 1:-1, 1:-1],
        full[..., :-2, 1:-1, 1:-1],
        full[..., 1:-1, 2:, 1:-1],
        full[..., 1:-1, :-2, 1:-1],
        full[..., 1:-1, 1:-1, 2:],
        full[..., 1:-1, 1:-1, :-2],
    ]


def chebyshev(rhs, apply_op):
    theta = 0.5 * (lam_high + lam_low)
    delta = 0.5 * (lam_high - lam_low)
    sigma = theta / delta
    rho = 1.0 / sigma
    solution = jnp.zeros_like(rhs)
    remain = rhs
    step_dir = rhs / theta
    for step in range(ITERS):
        solution = solution + step_dir
        if step + 1 < ITERS:
            remain = remain - apply_op(step_dir)
            rho_next = 1.0 / (2.0 * sigma - rho)
            step_dir = rho_next * rho * step_dir + 2.0 * rho_next / delta * remain
            rho = rho_next
    return solution


def per_device(
    labels,
    kappa_table,
    absorb_table,
    background,
    det_cells,
    v_kappa,
    v_absorb,
    q_kappa,
    q_absorb,
    beta_prev,
):
    sources, cx, cy, cz = background.shape
    kappa = regional(labels, kappa_table)
    absorb = regional(labels, absorb_table)
    full_k, full_a = (
        lax.all_gather(v_kappa, "src", axis=2, tiled=True),
        lax.all_gather(v_absorb, "src", axis=2, tiled=True),
    )
    stacked = jnp.concatenate([background, kappa[None], full_k[None]], axis=0)
    rims = padded_2(stacked, (("gx", 1), ("gy", 2)), 1)
    near_all = beside(rims)
    kappa_faces = [0.5 * (kappa + near[sources]) for near in near_all]
    vk_faces = [0.5 * (full_k + near[sources + 1]) for near in near_all]
    phi_near = [near[:sources] for near in near_all]

    def apply_op(field):
        padded = padded_2(field, (("gx", 1), ("gy", 2)), 1)
        result = absorb * field
        for face, near in zip(kappa_faces, beside(padded)):
            result = result + face * (field - near)
        return result

    rhs = full_a * background
    for face, near in zip(vk_faces, phi_near):
        rhs = rhs + face * (background - near)
    rhs = -rhs
    change = chebyshev(rhs, apply_op)
    span_y = cy * lax.axis_size("gy")
    ix = det_cells // (span_y * cz)
    iy = det_cells // cz % span_y
    iz = det_cells % cz
    anchor_x = lax.axis_index("gx") * cx
    anchor_y = lax.axis_index("gy") * cy
    owned = (ix >= anchor_x) & (ix < anchor_x + cx) & (iy >= anchor_y) & (iy < anchor_y + cy)
    local = jnp.where(owned, ((ix - anchor_x) * cy + (iy - anchor_y)) * cz + iz, 0)
    seen_part = jnp.where(owned[None, :], change.reshape(sources, -1)[:, local], 0.0)
    base_part = jnp.where(owned[None, :], background.reshape(sources, -1)[:, local], 0.0)
    seen, base = lax.psum((seen_part, base_part), ("gx", "gy"))
    total = jnp.sum(base, axis=1, keepdims=True)
    mean_base = total / det_cells.shape[0]
    ratio = base / total
    jv_vals = (seen - ratio * jnp.sum(seen, axis=1, keepdims=True)) / mean_base
    weight = (jv_vals - jnp.sum(ratio * jv_vals, axis=1, keepdims=True)) / mean_base
    deposit = jnp.where(owned[None, :], weight, 0.0)
    source = (
        jnp.zeros((sources, cx * cy * cz), jnp.float32)
        .at[:, local]
        .add(deposit)
        .reshape(change.shape)
    )
    dual = chebyshev(source, apply_op)
    dual_rims = padded_2(dual, (("gx", 1), ("gy", 2)), 1)
    grad_a = -jnp.sum(background * dual, axis=0)
    grad_k = jnp.zeros_like(kappa)
    for near_phi, near_dual in zip(phi_near, beside(dual_rims)):
        grad_k = grad_k - 0.5 * jnp.sum((background - near_phi) * (dual - near_dual), axis=0)
    summed_k, summed_a = lax.psum((grad_k, grad_a), "src")
    slab = v_kappa.shape[2]
    offset = lax.axis_index("src") * slab
    hv_k = lax.dynamic_slice_in_dim(summed_k, offset, slab, 2)
    hv_a = lax.dynamic_slice_in_dim(summed_a, offset, slab, 2)
    cell_count = cx * lax.axis_size("gx") * cy * lax.axis_size("gy") * cz
    w_k = hv_k - beta_prev[0] * q_kappa
    w_a = hv_a - beta_prev[0] * q_absorb
    local_wv = jnp.sum(w_k * v_kappa) + jnp.sum(w_a * v_absorb)
    local_vv = jnp.sum(v_kappa * v_kappa) + jnp.sum(v_absorb * v_absorb)
    wv_sum, vv_sum = lax.psum((local_wv, local_vv), ("src", "gx", "gy"))
    alpha = wv_sum / cell_count / (vv_sum / cell_count + eps_norm)
    r_k = w_k - alpha * v_kappa
    r_a = w_a - alpha * v_absorb
    rr_sum = lax.psum(jnp.sum(r_k * r_k) + jnp.sum(r_a * r_a), ("src", "gx", "gy"))
    beta = jnp.sqrt(rr_sum / cell_count + eps_norm)
    return (r_k / beta, r_a / beta, jnp.stack([alpha, beta]))


def chebyshev_scalars():
    theta = 0.5 * (lam_high + lam_low)
    delta = 0.5 * (lam_high - lam_low)
    sigma = theta / delta
    rho = 1.0 / sigma
    pairs = []
    for _ in range(ITERS - 1):
        rho_next = 1.0 / (2.0 * sigma - rho)
        pairs.append((rho_next * rho, 2.0 * rho_next / delta))
        rho = rho_next
    return theta, pairs


def places(split):
    g = lax.axis_index("gy")
    return lax.axis_index("src"), lax.axis_index("gx"), g // split, g % split


def shifted(value, step, axis):
    return pltpu.roll(value, step % value.shape[axis], axis)


def index_along(shape, axis):
    return lax.broadcasted_iota(jnp.int32, shape, axis)


def beyond(value, step, axis):
    size = value.shape[axis]
    at = index_along(value.shape, axis)
    edge = size - 1 if step == 1 else 0
    return jnp.where(at == edge, 0.0, shifted(value, -step, axis))


def packed_planes(ref, q):
    per = 128 // ref.shape[2]
    return jnp.concatenate([ref[per * q + j] for j in range(per)], axis=1)


def pack_kernel(bg, vk, va, packed, message, v_in, sems):
    _, x, _, _ = places(2)
    half = bg.shape[0] // 2
    cx = bg.shape[1]
    copies = [
        pltpu.make_async_copy(src, dst, sems.at[i])
        for i, (src, dst) in enumerate((
            (vk, v_in.at[0]),
            (va, v_in.at[1]),
            *((bg.at[half * (1 - x) + i], message.at[pl.ds(cx * i, cx)]) for i in range(half)),
        ))
    ]
    for copy in copies:
        copy.start()
    groups = packed.shape[0] // 2
    for f in range(2):
        copies[f].wait()
        for q in range(groups):
            planes = packed_planes(v_in.at[f], q)
            packed[groups * f + q] = planes
            message[cx * half + groups * f + q] = planes
    for copy in copies[2:]:
        copy.wait()


def count_kernel(dets, beta_prev, count, beta_row, *, ny, nz, half, halo):
    beta_row[...] = jnp.full(beta_row.shape, beta_prev[0])
    _, _, y, _ = places(2)
    planes, rows, _ = count.shape
    flat = dets[...]
    iz = flat % nz
    line = flat // nz
    iy = line % ny
    ix = line // ny
    row = iy - (half - halo) * y
    spot = jnp.where((row >= 0) & (row < rows), ix * rows + row, -1)
    dets_n = flat.shape[1]
    at_z = (index_along((nz, dets_n), 0) == iz).astype(jnp.float32).astype(jnp.bfloat16)

    def body(i, carry):
        here = index_along((2 * rows, dets_n), 0) + i * (2 * rows)
        hot = (here == spot).astype(jnp.float32).astype(jnp.bfloat16)
        found = lax.dot_general(hot, at_z, (((1,), (1,)), ((), ())), preferred_element_type=jnp.float32)
        count[pl.ds(2 * i, 2)] = found.reshape(2, rows, nz)
        return carry

    lax.fori_loop(0, planes // 2, body, 0)


def photon_kernel(bg, labels, msg, labels_came, mine, fields, raw, sems):
    _, x, _, c = places(2)
    half = bg.shape[0] // 2
    cx = labels.shape[0]
    here, there = cx * x, cx * (1 - x)
    copies = [
        pltpu.make_async_copy(src, dst, sems.at[i])
        for i, (src, dst) in enumerate((
            (bg.at[half * x + c], mine.at[pl.ds(here, cx)]),
            (bg.at[half * x + 1 - c], fields.at[0, pl.ds(here, cx)]),
            (labels, raw),
        ))
    ]
    for copy in copies:
        copy.start()
    mine[pl.ds(there, cx)] = msg[pl.ds(cx * c, cx)]
    fields[0, pl.ds(there, cx)] = msg[pl.ds(cx * (1 - c), cx)]
    fields[1, pl.ds(there, cx)] = labels_came[...].astype(jnp.float32)
    for copy in copies:
        copy.wait()
    fields[1, pl.ds(here, cx)] = raw[...].astype(jnp.float32)


def unpacked(blocks, groups, s, store):
    n = len(blocks)
    cy, lanes = blocks[0][0].shape
    slab = lanes // n
    lane = index_along((cy, lanes), 1) // slab
    for f in range(2):
        for q in range(groups):
            values = [block[groups * f + q] for block in blocks]
            for j in range(n):
                plane = jnp.zeros((cy, lanes), jnp.float32)
                for k in range(n):
                    home = s ^ k
                    moved = pltpu.roll(values[k], ((home - j + n) % n) * slab, 1)
                    plane = jnp.where(lane == home, moved, plane)
                store(f, n * q + j, plane)


def join_kernel(*refs):
    joined, size = refs[-1], refs[0].shape[0]
    for i, ref in enumerate(refs[:-1]):
        joined[pl.ds(size * i, size)] = ref[...]


def own_half_kernel(vk, va, joined, half):
    s, _, _, _ = places(2)
    size = half.shape[1]
    groups = joined.shape[0] // 2 // (128 // vk.shape[2] - 1)
    n = size // groups
    own = [packed_planes(ref, q) for ref in (vk, va) for q in range(groups)]
    blocks = [own] + [[joined[2 * groups * k + i] for i in range(2 * groups)] for k in range(n - 1)]

    def store(f, i, plane):
        half[f, i] = plane

    unpacked(blocks, groups, s, store)


def vector_kernel(half, msg, joined, fields):
    s, x, _, _ = places(2)
    cx = half.shape[1]
    fields[:, pl.ds(cx * x, cx)] = half[...]
    n = lax.axis_size("src")
    groups = cx // n
    own = msg.shape[0] - 2 * groups
    blocks = [[msg[own + i] for i in range(2 * groups)]]
    blocks += [[joined[2 * groups * k + i] for i in range(2 * groups)] for k in range(n - 1)]
    there = cx * (1 - x)

    def store(f, i, plane):
        fields[f, there + i] = plane

    unpacked(blocks, groups, s, store)


def edge_shape(planes, lanes):
    return planes // GROUP, GROUP * REACH, lanes


def packed_edges(tiles):
    return jnp.concatenate([tile[:REACH] for tile in tiles], axis=0)


def edge_tile(packed, j, y):
    rows = packed[REACH * j : REACH * (j + 1)]
    tile = jnp.concatenate([rows, jnp.zeros((HALO - REACH, rows.shape[1]), jnp.float32)], axis=0)
    return jnp.where(y == 0, tile, shifted(tile, HALO - REACH, 0))


def near_rows(ref, i, first, y):
    tile = ref[i, pl.ds(first, HALO), :]
    return jnp.where(y == 0, shifted(tile, REACH - HALO, 0), tile)


def edges_of(own, got, edge, y, c):
    first = (own.shape[1] - HALO) * (1 - y)
    for g in range(edge.shape[0]):
        edge[g] = packed_edges([
            jnp.where(c != y, near_rows(own, GROUP * g + j, first, y), near_rows(got, GROUP * g + j, first, y))
            for j in range(GROUP)
        ])


def photon_edge_kernel(mine, fields, got, edge):
    _, _, y, c = places(2)
    edges_of(mine, got.at[0], edge.at[0], y, c)
    edges_of(fields.at[1], got.at[1], edge.at[1], y, c)


def vector_edge_kernel(fields, got, edge):
    _, _, y, c = places(2)
    for f in range(2):
        edges_of(fields.at[f], got.at[f], edge.at[f], y, c)


def solve(b, bufs, diag, fx, fy, fz, unroll, finish=None, begin=0):
    planes = b.shape[0]
    _, pairs = chebyshev_scalars()
    for step, (keep, push) in enumerate(pairs):
        src, dst = bufs[step % 2], bufs[(step + 1) % 2]
        ends = finish is not None and step + 1 == len(pairs)

        def body(i, carry):
            u = src[i + 1]
            coef_y, coef_z = fy[i], fz[i]
            left = b[i] - diag[i] * u
            left = left + fx[i] * src[i] + fx[i + 1] * src[i + 2]
            left = left + coef_y * shifted(u, -1, 0) + shifted(coef_y * u, 1, 0)
            left = left + coef_z * shifted(u, -1, 1) + shifted(coef_z * u, 1, 1)
            change = u if step == 0 else u - dst[i + 1]
            value = u + keep * change + push * left
            if ends:
                return finish(i, value, carry)
            dst[i + 1] = value
            return carry

        added = lax.fori_loop(0, planes, body, begin if ends else 0, unroll=unroll)
    return bufs[len(pairs) % 2] if finish is None else added


def folded(value):
    return jnp.sum(value.reshape(-1, 8, value.shape[1]), axis=0)


def framed_own(ref, shift, own, got, y, c):
    planes, cy, _ = own.shape
    there = pl.ds(shift, planes)
    base = HALO * y
    ref[there, pl.ds(base + cy * c, cy), :] = own[...]
    ref[there, pl.ds(base + cy * (1 - c), cy), :] = got[...]


def framed(ref, shift, own, got, edge, y, c):
    framed_own(ref, shift, own, got, y, c)
    cy = own.shape[1]
    for g in range(edge.shape[0]):
        packed = edge[g]
        for j in range(GROUP):
            ref[shift + GROUP * g + j, pl.ds(2 * cy * (1 - y), HALO), :] = edge_tile(packed, j, y)


def blank_ends(*refs):
    for ref in refs:
        blank = jnp.zeros(ref.shape[1:], jnp.float32)
        ref[0] = blank
        ref[ref.shape[0] - 1] = blank


def owned_rows(shape, base, count):
    at_row = index_along(shape, 0)
    return (at_row >= base) & (at_row < base + count)


def table_rows(kap_table, abs_table, shape):
    lane = index_along(shape, 1)
    kap_row = abs_row = jnp.zeros(shape, jnp.float32)
    for region in range(kap_table.shape[0]):
        kap_row = jnp.where(lane == region, kap_table[region], kap_row)
        abs_row = jnp.where(lane == region, abs_table[region], abs_row)
    return kap_row, abs_row


def stencil_kernel(
    kap_table, abs_table, mine, fields, got, count,
    kap, diag, fx, fy, fz, sums,
    labels,
):
    _, _, y, c = places(2)
    planes, cy, lanes = mine.shape
    rows = 2 * cy + HALO
    base = HALO * y
    framed_own(labels, 0, fields.at[1], got.at[1], y, c)
    labels[:, pl.ds(2 * cy * (1 - y), HALO), :] = jnp.zeros((planes, HALO, lanes), jnp.float32)
    blank_ends(kap)
    shape = (rows, lanes)
    lane = index_along(shape, 1)
    kap_row, abs_row = table_rows(kap_table, abs_table, shape)
    owned = owned_rows(shape, base, 2 * cy)

    def look_up(i, carry):
        at = labels[i].astype(jnp.int32)
        kap[i + 1] = jnp.where(owned, jnp.take_along_axis(kap_row, at, axis=1), 0.0)
        diag[i] = jnp.take_along_axis(abs_row, at, axis=1)
        return carry

    lax.fori_loop(0, planes, look_up, 0, unroll=4)
    fx[0] = 0.5 * kap[1]

    def set_up(i, carry):
        k = kap[i + 1]
        along_x = 0.5 * (k + kap[i + 2])
        along_y, along_z = 0.5 * (k + beyond(k, 1, 0)), 0.5 * (k + beyond(k, 1, 1))
        fx[i + 1] = along_x
        fy[i] = jnp.where(index_along(shape, 0) == rows - 1, 0.0, along_y)
        fz[i] = jnp.where(lane == lanes - 1, 0.0, along_z)
        back_y, back_z = 0.5 * (k + beyond(k, -1, 0)), 0.5 * (k + beyond(k, -1, 1))
        diag[i] = diag[i] + fx[i] + along_x + along_y + back_y + along_z + back_z
        total, square = carry
        for p, at in ((mine[i], c), (got[0, i], 1 - c)):
            part = count[i, pl.ds(base + cy * at, cy), :] * p
            total, square = total + folded(part), square + folded(part * p)
        return total, square

    zero = jnp.zeros((8, lanes), jnp.float32)
    sums[0], sums[1] = lax.fori_loop(0, planes, set_up, (zero, zero), unroll=4)


def halo_kernel(kap_table, abs_table, edge, kap, diag_in, fx_in, fy_in, fz_in, diag, fx, fy, fz):
    _, _, y, _ = places(2)
    planes, rows, lanes = diag.shape
    for ref, old in ((diag, diag_in), (fx, fx_in), (fy, fy_in), (fz, fz_in)):
        ref[...] = old[...]
    shape = (HALO, lanes)
    lane, row = index_along(shape, 1), index_along(shape, 0)
    kap_row, abs_row = table_rows(kap_table, abs_table, shape)
    low = y == 0
    here = pl.ds((rows - HALO) * (1 - y), HALO)
    beside_it = pl.ds((rows - 2 * HALO) * (1 - y) + HALO * y, HALO)
    labels = [edge_tile(edge[1, i // GROUP], i % GROUP, y).astype(jnp.int32) for i in range(planes)]
    tiles = [jnp.take_along_axis(kap_row, at, axis=1) for at in labels]
    none = jnp.zeros(shape, jnp.float32)
    before = 0.5 * tiles[0]
    fx[0, here, :] = before
    for i, k in enumerate(tiles):
        after = 0.5 * (k + (tiles[i + 1] if i + 1 < planes else none))
        own = kap[i + 1, beside_it, :]
        up, down = shifted(k, -1, 0), shifted(k, 1, 0)
        k_up = jnp.where(row == HALO - 1, jnp.where(low, 0.0, shifted(own, -1, 0)), up)
        k_down = jnp.where(row == 0, jnp.where(low, shifted(own, 1, 0), 0.0), down)
        along_y, back_y = 0.5 * (k + k_up), 0.5 * (k + k_down)
        along_z, back_z = 0.5 * (k + beyond(k, 1, 1)), 0.5 * (k + beyond(k, -1, 1))
        fx[i + 1, here, :] = after
        fy[i, here, :] = jnp.where(low & (row == HALO - 1), 0.0, along_y)
        fz[i, here, :] = jnp.where(lane == lanes - 1, 0.0, along_z)
        absorb = jnp.take_along_axis(abs_row, labels[i], axis=1)
        diag[i, here, :] = absorb + before + after + along_y + back_y + along_z + back_z
        before = after
        face_up = jnp.where(low & (row == HALO - 1), 0.5 * up, 0.0)
        face_down = jnp.where(low | (row > 0), 0.0, 0.5 * down)
        fy[i, beside_it, :] = fy_in[i, beside_it, :] + face_up
        diag[i, beside_it, :] = diag_in[i, beside_it, :] + face_up + face_down


def density_kernel(mine, got, edge, phi, phi_y, phi_z):
    _, _, y, c = places(2)
    framed(phi, 1, mine, got.at[0], edge.at[0], y, c)
    blank_ends(phi)

    def differ(i, carry):
        p = phi[i + 1]
        phi_y[i], phi_z[i] = p - beyond(p, 1, 0), p - beyond(p, 1, 1)
        return carry

    lax.fori_loop(0, phi_y.shape[0], differ, 0, unroll=4)


def first_kernel(
    phi, phi_y, phi_z, diag, fx, fy, fz, count, sums, vector, got_vector, edge,
    change, message,
    vk, va, b, buf_a, buf_b,
):
    _, _, y, c = places(2)
    planes, rows, lanes = change.shape
    cy = vector.shape[2]
    framed(vk, 1, vector.at[0], got_vector.at[0], edge.at[0], y, c)
    framed(va, 0, vector.at[1], got_vector.at[1], edge.at[1], y, c)
    blank_ends(vk, buf_a, buf_b)
    theta, _ = chebyshev_scalars()

    def set_up(i, carry):
        v, p = vk[i + 1], phi[i + 1]
        total = 0.5 * (v + vk[i]) * (p - phi[i]) + 0.5 * (v + vk[i + 2]) * (p - phi[i + 2])
        for axis, step in enumerate((phi_y, phi_z)):
            flow = 0.5 * (v + beyond(v, 1, axis)) * step[i]
            first = index_along(v.shape, axis) == 0
            total = total + flow + jnp.where(first, 0.5 * v * p, -shifted(flow, 1, axis))
        total = -(va[i] * p + total)
        b[i] = total
        buf_a[i + 1] = total * (1.0 / theta)
        return carry

    lax.fori_loop(0, planes, set_up, 0, unroll=4)
    owned = owned_rows((rows, lanes), HALO * y, 2 * cy)

    def add_up(i, u, carry):
        change[i] = u
        part = jnp.where(owned, count[i], 0.0) * u
        return carry[0] + folded(part), carry[1] + folded(part * phi[i + 1])

    zero = jnp.zeros((8, lanes), jnp.float32)
    seen, cross = solve(b, (buf_a, buf_b), diag, fx, fy, fz, UNROLL, add_up, (zero, zero))
    first = (2 * cy - HALO) * (1 - y) + HALO * y
    size = GROUP * REACH
    for g in range(planes // GROUP):
        message[pl.ds(size * g, size), :] = packed_edges(
            [near_rows(change, GROUP * g + j, first, y) for j in range(GROUP)]
        )
    rows_of_sums = [jnp.sum(part, axis=0, keepdims=True) for part in (sums[0], seen, cross, sums[1])]
    message[pl.ds(REACH * planes, 8), :] = jnp.concatenate([*rows_of_sums, zero[:4]], axis=0)


def second_kernel(
    phi, phi_y, phi_z, change, diag, fx, fy, fz, count, sent, came,
    own, message,
    b, buf_a, buf_b, grad_k, grad_a,
    *, dets,
):
    _, _, y, c = places(2)
    planes, rows, lanes = change.shape
    cy = (rows - HALO) // 2
    base = HALO * y
    edge = pl.ds(2 * cy * (1 - y), HALO)
    tail = pl.ds(REACH * planes, 8)
    sums = jnp.sum(sent[tail, :] + came[tail, :], axis=1, keepdims=True)
    total, seen_sum, cross, square = (sums[g : g + 1] for g in range(4))
    mean = total / dets
    part = seen_sum / total
    level = (cross - part * square) / (total * mean)
    inverse = 1.0 / mean
    blank_ends(buf_a, buf_b)
    theta, _ = chebyshev_scalars()

    def weighted(n, u, p):
        return n * (((u - p * part) * inverse - level) * inverse)

    def set_up(i, carry):
        value = weighted(count[i], change[i], phi[i + 1])
        b[i] = value
        buf_a[i + 1] = value * (1.0 / theta)
        return carry

    lax.fori_loop(0, planes, set_up, 0, unroll=4)
    size = GROUP * REACH
    for i in range(planes):
        u = edge_tile(came[pl.ds(size * (i // GROUP), size), :], i % GROUP, y)
        value = weighted(count[i, edge, :], u, phi[i + 1, edge, :])
        b[i, edge, :] = value
        buf_a[i + 1, edge, :] = value * (1.0 / theta)
    dual = solve(b, (buf_a, buf_b), diag, fx, fy, fz, UNROLL)

    def product(i, carry):
        p, u = phi[i + 1], dual[i + 1]
        grad = (p - phi[i]) * (u - dual[i]) + (p - phi[i + 2]) * (u - dual[i + 2])
        both = p * u
        for axis, step in enumerate((phi_y, phi_z)):
            flow = step[i] * (u - beyond(u, 1, axis))
            first = index_along(p.shape, axis) == 0
            grad = grad + flow + jnp.where(first, both, shifted(flow, 1, axis))
        grad_k[i] = -0.5 * grad
        grad_a[i] = -both
        for f, ref in enumerate((grad_k, grad_a)):
            own[f, i] = ref[i, pl.ds(base + cy * c, cy), :]
            message[f, i] = ref[i, pl.ds(base + cy * (1 - c), cy), :]
        return carry

    lax.fori_loop(0, planes, product, 0, unroll=4)


def packed_slabs(own, came, half, choices, outs):
    s, _, _, _ = places(2)
    _, planes, cy, lanes = own.shape
    n = planes // 2 // outs.shape[2]
    slab = lanes // n
    lane = index_along((cy, lanes), 1) // slab
    for f in range(2):
        for q in range(outs.shape[2]):
            at = planes // 2 * half + n * q
            parts = [own[f, at + j] + came[f, at + j] for j in range(n)]
            for i, k in enumerate(choices):
                to = s ^ k
                piece = jnp.zeros((cy, lanes), jnp.float32)
                for j in range(n):
                    moved = pltpu.roll(parts[j], ((j - to + n) % n) * slab, 1)
                    piece = jnp.where(lane == j, moved, piece)
                outs[i, f, q] = piece


def send_kernel(own, came, out, *, k):
    _, x, _, _ = places(2)
    packed_slabs(own, came, 1 - x, (k,), out)


def keep_kernel(own, came, kept):
    _, x, _, _ = places(2)
    packed_slabs(own, came, x, range(kept.shape[0]), kept)


def add_kernel(kept, came, out, *, k):
    out[...] = kept[k] + came[0]


def sum_kernel(*refs):
    total = refs[0][...]
    for ref in refs[1:-1]:
        total = total + ref[...]
    refs[-1][...] = total


def project_kernel(*refs, parts_n, n):
    beta_prev = refs[0]
    parts = refs[1 : 1 + parts_n]
    vk, va, qk, qa, w_k, w_a, tile = refs[1 + parts_n :]
    slab = 128 // n
    for f, (q_ref, w) in enumerate(((qk, w_k), (qa, w_a))):
        for q in range(vk.shape[0] // n):
            whole = sum(part[f, q] for part in parts[1:]) + parts[0][f, q]
            for j in range(n):
                i = n * q + j
                w[i] = whole[:, slab * j : slab * (j + 1)] - beta_prev[:, : vk.shape[2]] * q_ref[i]

    def total(value):
        return jnp.sum(jnp.sum(jnp.sum(value, axis=0), axis=0, keepdims=True), axis=1, keepdims=True)

    wk, wa, v_k, v_a = w_k[...], w_a[...], vk[...], va[...]
    wv = total(wk * v_k + wa * v_a)
    vv = total(v_k * v_k + v_a * v_a)
    a = jnp.where(vv > 0.0, wv / jnp.where(vv > 0.0, vv, 1.0), 0.0)
    u_k, u_a = wk - a * v_k, wa - a * v_a
    uv = total(u_k * v_k + u_a * v_a)
    uu = total(u_k * u_k + u_a * u_a)
    lane = index_along((1, 128), 1)
    values = jnp.zeros((1, 128), jnp.float32)
    for i, value in enumerate((wv, vv, a, uv, uu)):
        values = jnp.where(lane == i, value, values)
    tile[...] = values


def final_kernel(tiles, w_k, w_a, vk, va, next_k, next_a, coefs, *, cells):
    tile = jnp.concatenate([tiles[i] for i in range(tiles.shape[0])], axis=0)
    wv, vv, a, uv, uu = (tile[:, i : i + 1] for i in range(5))
    wv_sum = jnp.sum(wv, axis=0, keepdims=True)
    vv_sum = jnp.sum(vv, axis=0, keepdims=True)
    alpha = wv_sum / cells / (vv_sum / cells + eps_norm)
    off = alpha - a
    rr = jnp.sum(uu - 2.0 * off * uv + off * off * vv, axis=0, keepdims=True)
    beta = jnp.sqrt(rr / cells + eps_norm)
    next_k[...] = (w_k[...] - alpha * vk[...]) / beta
    next_a[...] = (w_a[...] - alpha * va[...]) / beta
    coefs[0] = jnp.sum(alpha)
    coefs[1] = jnp.sum(beta)


def f32(*shape):
    return jax.ShapeDtypeStruct(shape, jnp.float32)


def run(kernel, outs, *args, after=(), scratch=(), copies=0, smem=(), hbm=(), mib=16, in_smem_out=(), cost=None):
    vmem = pl.BlockSpec(memory_space=pltpu.VMEM)
    scalar = pl.BlockSpec(memory_space=pltpu.SMEM)
    far = pl.BlockSpec(memory_space=pltpu.HBM)
    held = [pltpu.VMEM(shape, dtype) for shape, dtype in scratch]
    used, waits = len(args), len(after)

    def body(*refs):
        kernel(*refs[:used], *refs[used + waits :])

    args = (*args, *after)
    if copies:
        held.append(pltpu.SemaphoreType.DMA((copies,)))
    return pl.pallas_call(
        body if waits else kernel,
        out_shape=tuple(outs),
        in_specs=[scalar if i in smem else far if i in hbm else vmem for i in range(len(args))],
        out_specs=tuple(scalar if i in in_smem_out else vmem for i in range(len(outs))),
        scratch_shapes=held,
        compiler_params=pltpu.CompilerParams(vmem_limit_bytes=mib * 2**20),
        cost_estimate=cost,
    )(*args)


HALO = 8
UNROLL = 8
REACH = 6
GROUP = 4


def per_device_paired(
    labels, kappa_table, absorb_table, background, det_cells,
    v_kappa, v_absorb, q_kappa, q_absorb, beta_prev,
):
    sources, cx, cy, cz = background.shape
    n = lax.axis_size("src")
    planes, rows = 2 * cx, 2 * cy + HALO
    ny = cy * lax.axis_size("gy")
    dets = det_cells.shape[0]
    cells = planes * ny * cz
    groups = cx // n

    def swap_x(value):
        return lax.ppermute(value, "gx", [(0, 1), (1, 0)])

    def swap_core(value):
        return lax.ppermute(value, "gy", [(0, 1), (1, 0), (2, 3), (3, 2)])

    def along_z(value, k):
        return lax.ppermute(value, "src", [(i, i ^ k) for i in range(n)])

    block = (cx, cy, cz)
    float_block = lambda *shape: (shape, jnp.float32)
    raw_labels = (block, jnp.int32)
    packed, message = run(
        pack_kernel, (f32(2 * groups, cy, cz), f32(sources // 2 * cx + 2 * groups, cy, cz)),
        background, v_kappa, v_absorb, hbm=(0, 1, 2),
        scratch=(float_block(2, *v_kappa.shape),), copies=2 + sources // 2, mib=60,
    )
    long = pl.CostEstimate(flops=10**9, bytes_accessed=2**26, transcendentals=0)
    labels_came = swap_x(labels)
    came = swap_x(message)
    slabs = [along_z(packed, k) for k in range(1, n)]
    count, beta_row = run(
        functools.partial(count_kernel, ny=ny, nz=cz, half=2 * cy, halo=HALO),
        (f32(planes, rows, cz), f32(1, cz)), det_cells.reshape(1, dets), beta_prev, smem=(1,), after=(labels_came,),
        cost=pl.CostEstimate(flops=2 * planes * rows * cz * dets, bytes_accessed=planes * rows * cz * 4, transcendentals=0),
    )

    def across_y(value):
        return lax.ppermute(value, "gy", [(i, (i + 2) % 4) for i in range(4)])

    (joined,) = run(join_kernel, (f32(2 * groups * (n - 1), cy, cz),), *slabs, after=(count,))
    joined_came = swap_x(joined)
    (half_vector,) = run(own_half_kernel, (f32(2, *block),), v_kappa, v_absorb, joined)
    mine, fields = run(
        photon_kernel, (f32(planes, cy, cz), f32(2, planes, cy, cz)),
        background, labels, came, labels_came, after=(joined,), hbm=(0, 1), scratch=(raw_labels,), copies=3,
    )
    got = swap_core(fields)
    (vector,) = run(
        vector_kernel, (f32(2, planes, cy, cz),), half_vector, came, joined_came, after=(mine,)
    )
    edge = (f32(2, *edge_shape(planes, cz)),)
    (sent,) = run(photon_edge_kernel, edge, mine, fields, got, after=(vector,))
    photon_edge = across_y(sent)
    vector_got = swap_core(vector)
    (vector_sent,) = run(vector_edge_kernel, edge, vector, vector_got, after=(sent,))
    frame, wide = (planes, rows, cz), (planes + 2, rows, cz)
    float_frame, float_wide = float_block(*frame), float_block(*wide)
    coefs = (f32(*frame), f32(planes + 1, rows, cz), f32(*frame), f32(*frame))
    kap, *partial, sums = run(
        stencil_kernel, (f32(*wide), *coefs, f32(2, 8, cz)),
        kappa_table, absorb_table, mine, fields, got, count, after=(vector_sent,), cost=long,
        smem=(0, 1), scratch=(float_frame,),
    )
    diag, fx, fy, fz = run(
        halo_kernel, coefs, kappa_table, absorb_table, photon_edge, kap, *partial, smem=(0, 1)
    )
    densities = run(
        density_kernel, (f32(*wide), f32(*frame), f32(*frame)), mine, got, photon_edge, after=(fz,)
    )
    change, sent = run(
        first_kernel, (f32(*frame), f32(REACH * planes + 8, cz)),
        *densities, diag, fx, fy, fz, count, sums, vector, vector_got, across_y(vector_sent),
        scratch=(float_wide, float_frame, float_frame, float_wide, float_wide),
    )
    heard = across_y(sent)
    own, message = run(
        functools.partial(second_kernel, dets=dets),
        (f32(2, planes, cy, cz), f32(2, planes, cy, cz)),
        *densities, change, diag, fx, fy, fz, count, sent, heard,
        scratch=(float_frame, float_wide, float_wide, float_frame, float_frame),
    )
    piece = f32(2, groups, cy, cz)
    got = swap_core(message)
    crossed, last = {}, ()
    for k in reversed(range(n)):
        last = run(functools.partial(send_kernel, k=k), (f32(1, *piece.shape),), own, got, after=last)
        crossed[k] = swap_x(last[0])
    (kept,) = run(keep_kernel, (f32(n, *piece.shape),), own, got, after=last)
    totals = {
        k: run(functools.partial(add_kernel, k=k), (piece,), kept, value)[0] for k, value in crossed.items()
    }
    received = {k: along_z(totals[k], k) for k in reversed(range(1, n))}
    (distant,) = run(sum_kernel, (piece,), *(received[k] for k in range(n // 2, n)), cost=long)
    parts = [distant, totals[0]] + [received[k] for k in range(1, n // 2)]
    w_k, w_a, tile = run(
        functools.partial(project_kernel, parts_n=len(parts), n=n),
        (f32(*v_kappa.shape), f32(*v_kappa.shape), f32(1, 128)),
        beta_row, *parts, v_kappa, v_absorb, q_kappa, q_absorb,
    )
    everyone = ("src", "gx", "gy")
    tiles = lax.all_to_all(jnp.broadcast_to(tile, (8 * n, 1, 128)), everyone, 0, 0)
    return tuple(run(
        functools.partial(final_kernel, cells=cells),
        (f32(*v_kappa.shape), f32(*v_kappa.shape), f32(2)),
        tiles, w_k, w_a, v_kappa, v_absorb, in_smem_out=(2,),
    ))


def paired_fits(mesh):
    return mesh.shape["gx"] == 2 and mesh.shape["gy"] == 4


def body_for(mesh):
    if not paired_fits(mesh):
        return per_device

    def chosen(*args):
        sources, cx, cy, cz = args[3].shape
        n = lax.axis_size("src")
        fits = sources == 4 and cz == 128 and cx % n == 0 and cx % GROUP == 0 and cy % HALO == 0 and n > 1 and n & (n - 1) == 0
        devices = 8 * n
        return (per_device_paired if fits and devices <= 128 else per_device)(*args)

    return chosen


def solution(mesh):
    return jax.shard_map(
        body_for(mesh),
        mesh=mesh,
        in_specs=(
            P("gx", "gy", None),
            P(),
            P(),
            P("src", "gx", "gy", None),
            P(),
            P("gx", "gy", "src"),
            P("gx", "gy", "src"),
            P("gx", "gy", "src"),
            P("gx", "gy", "src"),
            P(),
        ),
        out_specs=(P("gx", "gy", "src"), P("gx", "gy", "src"), P()),
        check_vma=False,
    )
```

```python
import functools

import jax
import jax.numpy as jnp
from jax import lax
from jax.experimental import pallas as pl
from jax.experimental.pallas import tpu as pltpu
from jax.sharding import PartitionSpec as P

ITERS = 6


lam_low = 0.02
lam_high = 24.1
eps_norm = 1e-06


def padded_2(block, sides, width):
    for axis, dim in sides:
        count = lax.axis_size(axis)
        forward = [(i, i + 1) for i in range(count - 1)]
        backward = [(target, source) for source, target in forward]
        low = lax.ppermute(
            lax.slice_in_dim(block, block.shape[dim] - width, None, axis=dim), axis, forward
        )
        high = lax.ppermute(lax.slice_in_dim(block, 0, width, axis=dim), axis, backward)
        block = jnp.concatenate([low, block, high], axis=dim)
    return block


def regional(labels, table):
    field = jnp.zeros(labels.shape, jnp.float32)
    for region in range(table.shape[0]):
        field = field + jnp.where(labels == region, table[region], 0.0)
    return field


def beside(padded):
    widths = [(0, 0)] * (padded.ndim - 1) + [(1, 1)]
    full = jnp.pad(padded, widths)
    return [
        full[..., 2:, 1:-1, 1:-1],
        full[..., :-2, 1:-1, 1:-1],
        full[..., 1:-1, 2:, 1:-1],
        full[..., 1:-1, :-2, 1:-1],
        full[..., 1:-1, 1:-1, 2:],
        full[..., 1:-1, 1:-1, :-2],
    ]


def chebyshev(rhs, apply_op):
    theta = 0.5 * (lam_high + lam_low)
    delta = 0.5 * (lam_high - lam_low)
    sigma = theta / delta
    rho = 1.0 / sigma
    solution = jnp.zeros_like(rhs)
    remain = rhs
    step_dir = rhs / theta
    for step in range(ITERS):
        solution = solution + step_dir
        if step + 1 < ITERS:
            remain = remain - apply_op(step_dir)
            rho_next = 1.0 / (2.0 * sigma - rho)
            step_dir = rho_next * rho * step_dir + 2.0 * rho_next / delta * remain
            rho = rho_next
    return solution


def per_device(
    labels,
    kappa_table,
    absorb_table,
    background,
    det_cells,
    v_kappa,
    v_absorb,
    q_kappa,
    q_absorb,
    beta_prev,
):
    sources, cx, cy, cz = background.shape
    kappa = regional(labels, kappa_table)
    absorb = regional(labels, absorb_table)
    full_k, full_a = (
        lax.all_gather(v_kappa, "src", axis=2, tiled=True),
        lax.all_gather(v_absorb, "src", axis=2, tiled=True),
    )
    stacked = jnp.concatenate([background, kappa[None], full_k[None]], axis=0)
    rims = padded_2(stacked, (("gx", 1), ("gy", 2)), 1)
    near_all = beside(rims)
    kappa_faces = [0.5 * (kappa + near[sources]) for near in near_all]
    vk_faces = [0.5 * (full_k + near[sources + 1]) for near in near_all]
    phi_near = [near[:sources] for near in near_all]

    def apply_op(field):
        padded = padded_2(field, (("gx", 1), ("gy", 2)), 1)
        result = absorb * field
        for face, near in zip(kappa_faces, beside(padded)):
            result = result + face * (field - near)
        return result

    rhs = full_a * background
    for face, near in zip(vk_faces, phi_near):
        rhs = rhs + face * (background - near)
    rhs = -rhs
    change = chebyshev(rhs, apply_op)
    span_y = cy * lax.axis_size("gy")
    ix = det_cells // (span_y * cz)
    iy = det_cells // cz % span_y
    iz = det_cells % cz
    anchor_x = lax.axis_index("gx") * cx
    anchor_y = lax.axis_index("gy") * cy
    owned = (ix >= anchor_x) & (ix < anchor_x + cx) & (iy >= anchor_y) & (iy < anchor_y + cy)
    local = jnp.where(owned, ((ix - anchor_x) * cy + (iy - anchor_y)) * cz + iz, 0)
    seen_part = jnp.where(owned[None, :], change.reshape(sources, -1)[:, local], 0.0)
    base_part = jnp.where(owned[None, :], background.reshape(sources, -1)[:, local], 0.0)
    seen, base = lax.psum((seen_part, base_part), ("gx", "gy"))
    total = jnp.sum(base, axis=1, keepdims=True)
    mean_base = total / det_cells.shape[0]
    ratio = base / total
    jv_vals = (seen - ratio * jnp.sum(seen, axis=1, keepdims=True)) / mean_base
    weight = (jv_vals - jnp.sum(ratio * jv_vals, axis=1, keepdims=True)) / mean_base
    deposit = jnp.where(owned[None, :], weight, 0.0)
    source = (
        jnp.zeros((sources, cx * cy * cz), jnp.float32)
        .at[:, local]
        .add(deposit)
        .reshape(change.shape)
    )
    dual = chebyshev(source, apply_op)
    dual_rims = padded_2(dual, (("gx", 1), ("gy", 2)), 1)
    grad_a = -jnp.sum(background * dual, axis=0)
    grad_k = jnp.zeros_like(kappa)
    for near_phi, near_dual in zip(phi_near, beside(dual_rims)):
        grad_k = grad_k - 0.5 * jnp.sum((background - near_phi) * (dual - near_dual), axis=0)
    summed_k, summed_a = lax.psum((grad_k, grad_a), "src")
    slab = v_kappa.shape[2]
    offset = lax.axis_index("src") * slab
    hv_k = lax.dynamic_slice_in_dim(summed_k, offset, slab, 2)
    hv_a = lax.dynamic_slice_in_dim(summed_a, offset, slab, 2)
    cell_count = cx * lax.axis_size("gx") * cy * lax.axis_size("gy") * cz
    w_k = hv_k - beta_prev[0] * q_kappa
    w_a = hv_a - beta_prev[0] * q_absorb
    local_wv = jnp.sum(w_k * v_kappa) + jnp.sum(w_a * v_absorb)
    local_vv = jnp.sum(v_kappa * v_kappa) + jnp.sum(v_absorb * v_absorb)
    wv_sum, vv_sum = lax.psum((local_wv, local_vv), ("src", "gx", "gy"))
    alpha = wv_sum / cell_count / (vv_sum / cell_count + eps_norm)
    r_k = w_k - alpha * v_kappa
    r_a = w_a - alpha * v_absorb
    rr_sum = lax.psum(jnp.sum(r_k * r_k) + jnp.sum(r_a * r_a), ("src", "gx", "gy"))
    beta = jnp.sqrt(rr_sum / cell_count + eps_norm)
    return (r_k / beta, r_a / beta, jnp.stack([alpha, beta]))


def chebyshev_scalars():
    theta = 0.5 * (lam_high + lam_low)
    delta = 0.5 * (lam_high - lam_low)
    sigma = theta / delta
    rho = 1.0 / sigma
    pairs = []
    for _ in range(ITERS - 1):
        rho_next = 1.0 / (2.0 * sigma - rho)
        pairs.append((rho_next * rho, 2.0 * rho_next / delta))
        rho = rho_next
    return theta, pairs


def places(split):
    g = lax.axis_index("gy")
    return lax.axis_index("src"), lax.axis_index("gx"), g // split, g % split


def shifted(value, step, axis):
    return pltpu.roll(value, step % value.shape[axis], axis)


def index_along(shape, axis):
    return lax.broadcasted_iota(jnp.int32, shape, axis)


def beyond(value, step, axis):
    size = value.shape[axis]
    at = index_along(value.shape, axis)
    edge = size - 1 if step == 1 else 0
    return jnp.where(at == edge, 0.0, shifted(value, -step, axis))


def packed_planes(ref, q):
    per = 128 // ref.shape[2]
    return jnp.concatenate([ref[per * q + j] for j in range(per)], axis=1)


def pack_kernel(bg, vk, va, packed, message, v_in, sems):
    _, x, _, _ = places(2)
    half = bg.shape[0] // 2
    cx = bg.shape[1]
    copies = [
        pltpu.make_async_copy(src, dst, sems.at[i])
        for i, (src, dst) in enumerate((
            (vk, v_in.at[0]),
            (va, v_in.at[1]),
            *((bg.at[half * (1 - x) + i], message.at[pl.ds(cx * i, cx)]) for i in range(half)),
        ))
    ]
    for copy in copies:
        copy.start()
    groups = packed.shape[0] // 2
    for f in range(2):
        copies[f].wait()
        for q in range(groups):
            planes = packed_planes(v_in.at[f], q)
            packed[groups * f + q] = planes
            message[cx * half + groups * f + q] = planes
    for copy in copies[2:]:
        copy.wait()


def count_kernel(dets, beta_prev, count, beta_row, *, ny, nz, half, halo):
    beta_row[...] = jnp.full(beta_row.shape, beta_prev[0])
    _, _, y, _ = places(2)
    planes, rows, _ = count.shape
    flat = dets[...]
    iz = flat % nz
    line = flat // nz
    iy = line % ny
    ix = line // ny
    row = iy - (half - halo) * y
    spot = jnp.where((row >= 0) & (row < rows), ix * rows + row, -1)
    dets_n = flat.shape[1]
    at_z = (index_along((nz, dets_n), 0) == iz).astype(jnp.float32).astype(jnp.bfloat16)

    def body(i, carry):
        here = index_along((2 * rows, dets_n), 0) + i * (2 * rows)
        hot = (here == spot).astype(jnp.float32).astype(jnp.bfloat16)
        found = lax.dot_general(hot, at_z, (((1,), (1,)), ((), ())), preferred_element_type=jnp.float32)
        count[pl.ds(2 * i, 2)] = found.reshape(2, rows, nz)
        return carry

    lax.fori_loop(0, planes // 2, body, 0)


def photon_kernel(bg, labels, msg, labels_came, mine, fields, raw, sems):
    _, x, _, c = places(2)
    half = bg.shape[0] // 2
    cx = labels.shape[0]
    here, there = cx * x, cx * (1 - x)
    copies = [
        pltpu.make_async_copy(src, dst, sems.at[i])
        for i, (src, dst) in enumerate((
            (bg.at[half * x + c], mine.at[pl.ds(here, cx)]),
            (bg.at[half * x + 1 - c], fields.at[0, pl.ds(here, cx)]),
            (labels, raw),
        ))
    ]
    for copy in copies:
        copy.start()
    mine[pl.ds(there, cx)] = msg[pl.ds(cx * c, cx)]
    fields[0, pl.ds(there, cx)] = msg[pl.ds(cx * (1 - c), cx)]
    fields[1, pl.ds(there, cx)] = labels_came[...].astype(jnp.float32)
    for copy in copies:
        copy.wait()
    fields[1, pl.ds(here, cx)] = raw[...].astype(jnp.float32)


def unpacked(blocks, groups, s, store):
    n = len(blocks)
    cy, lanes = blocks[0][0].shape
    slab = lanes // n
    lane = index_along((cy, lanes), 1) // slab
    for f in range(2):
        for q in range(groups):
            values = [block[groups * f + q] for block in blocks]
            for j in range(n):
                plane = jnp.zeros((cy, lanes), jnp.float32)
                for k in range(n):
                    home = s ^ k
                    moved = pltpu.roll(values[k], ((home - j + n) % n) * slab, 1)
                    plane = jnp.where(lane == home, moved, plane)
                store(f, n * q + j, plane)


def join_kernel(*refs):
    joined, size = refs[-1], refs[0].shape[0]
    for i, ref in enumerate(refs[:-1]):
        joined[pl.ds(size * i, size)] = ref[...]


def own_half_kernel(vk, va, joined, half):
    s, _, _, _ = places(2)
    size = half.shape[1]
    groups = joined.shape[0] // 2 // (128 // vk.shape[2] - 1)
    n = size // groups
    own = [packed_planes(ref, q) for ref in (vk, va) for q in range(groups)]
    blocks = [own] + [[joined[2 * groups * k + i] for i in range(2 * groups)] for k in range(n - 1)]

    def store(f, i, plane):
        half[f, i] = plane

    unpacked(blocks, groups, s, store)


def vector_kernel(half, msg, joined, fields):
    s, x, _, _ = places(2)
    cx = half.shape[1]
    fields[:, pl.ds(cx * x, cx)] = half[...]
    n = lax.axis_size("src")
    groups = cx // n
    own = msg.shape[0] - 2 * groups
    blocks = [[msg[own + i] for i in range(2 * groups)]]
    blocks += [[joined[2 * groups * k + i] for i in range(2 * groups)] for k in range(n - 1)]
    there = cx * (1 - x)

    def store(f, i, plane):
        fields[f, there + i] = plane

    unpacked(blocks, groups, s, store)


def edge_shape(planes, lanes):
    return planes // GROUP, GROUP * REACH, lanes


def packed_edges(tiles):
    return jnp.concatenate([tile[:REACH] for tile in tiles], axis=0)


def edge_tile(packed, j, y):
    rows = packed[REACH * j : REACH * (j + 1)]
    tile = jnp.concatenate([rows, jnp.zeros((HALO - REACH, rows.shape[1]), jnp.float32)], axis=0)
    return jnp.where(y == 0, tile, shifted(tile, HALO - REACH, 0))


def near_rows(ref, i, first, y):
    tile = ref[i, pl.ds(first, HALO), :]
    return jnp.where(y == 0, shifted(tile, REACH - HALO, 0), tile)


def edges_of(own, got, edge, y, c):
    first = (own.shape[1] - HALO) * (1 - y)
    for g in range(edge.shape[0]):
        edge[g] = packed_edges([
            jnp.where(c != y, near_rows(own, GROUP * g + j, first, y), near_rows(got, GROUP * g + j, first, y))
            for j in range(GROUP)
        ])


def photon_edge_kernel(mine, fields, got, edge):
    _, _, y, c = places(2)
    edges_of(mine, got.at[0], edge.at[0], y, c)
    edges_of(fields.at[1], got.at[1], edge.at[1], y, c)


def vector_edge_kernel(fields, got, edge):
    _, _, y, c = places(2)
    for f in range(2):
        edges_of(fields.at[f], got.at[f], edge.at[f], y, c)


def solve(b, bufs, diag, fx, fy, fz, unroll):
    planes = b.shape[0]
    _, pairs = chebyshev_scalars()
    for step, (keep, push) in enumerate(pairs):
        src, dst = bufs[step % 2], bufs[(step + 1) % 2]

        def body(i, carry):
            u = src[i + 1]
            coef_y, coef_z = fy[i], fz[i]
            left = b[i] - diag[i] * u
            left = left + fx[i] * src[i] + fx[i + 1] * src[i + 2]
            left = left + coef_y * shifted(u, -1, 0) + shifted(coef_y * u, 1, 0)
            left = left + coef_z * shifted(u, -1, 1) + shifted(coef_z * u, 1, 1)
            change = u if step == 0 else u - dst[i + 1]
            dst[i + 1] = u + keep * change + push * left
            return carry

        lax.fori_loop(0, planes, body, 0, unroll=unroll)
    return bufs[len(pairs) % 2]


def folded(value):
    return jnp.sum(value.reshape(-1, 8, value.shape[1]), axis=0)


def framed_own(ref, shift, own, got, y, c):
    planes, cy, _ = own.shape
    there = pl.ds(shift, planes)
    base = HALO * y
    ref[there, pl.ds(base + cy * c, cy), :] = own[...]
    ref[there, pl.ds(base + cy * (1 - c), cy), :] = got[...]


def framed(ref, shift, own, got, edge, y, c):
    framed_own(ref, shift, own, got, y, c)
    cy = own.shape[1]
    for g in range(edge.shape[0]):
        packed = edge[g]
        for j in range(GROUP):
            ref[shift + GROUP * g + j, pl.ds(2 * cy * (1 - y), HALO), :] = edge_tile(packed, j, y)


def blank_ends(*refs):
    for ref in refs:
        blank = jnp.zeros(ref.shape[1:], jnp.float32)
        ref[0] = blank
        ref[ref.shape[0] - 1] = blank


def owned_rows(shape, base, count):
    at_row = index_along(shape, 0)
    return (at_row >= base) & (at_row < base + count)


def table_rows(kap_table, abs_table, shape):
    lane = index_along(shape, 1)
    kap_row = abs_row = jnp.zeros(shape, jnp.float32)
    for region in range(kap_table.shape[0]):
        kap_row = jnp.where(lane == region, kap_table[region], kap_row)
        abs_row = jnp.where(lane == region, abs_table[region], abs_row)
    return kap_row, abs_row


def stencil_kernel(
    kap_table, abs_table, mine, fields, got, count,
    kap, diag, fx, fy, fz, sums,
    labels,
):
    _, _, y, c = places(2)
    planes, cy, lanes = mine.shape
    rows = 2 * cy + HALO
    base = HALO * y
    framed_own(labels, 0, fields.at[1], got.at[1], y, c)
    labels[:, pl.ds(2 * cy * (1 - y), HALO), :] = jnp.zeros((planes, HALO, lanes), jnp.float32)
    blank_ends(kap)
    shape = (rows, lanes)
    lane = index_along(shape, 1)
    kap_row, abs_row = table_rows(kap_table, abs_table, shape)
    owned = owned_rows(shape, base, 2 * cy)

    def look_up(i, carry):
        at = labels[i].astype(jnp.int32)
        kap[i + 1] = jnp.where(owned, jnp.take_along_axis(kap_row, at, axis=1), 0.0)
        diag[i] = jnp.take_along_axis(abs_row, at, axis=1)
        return carry

    lax.fori_loop(0, planes, look_up, 0, unroll=4)
    fx[0] = 0.5 * kap[1]

    def set_up(i, carry):
        k = kap[i + 1]
        along_x = 0.5 * (k + kap[i + 2])
        along_y, along_z = 0.5 * (k + beyond(k, 1, 0)), 0.5 * (k + beyond(k, 1, 1))
        fx[i + 1] = along_x
        fy[i] = jnp.where(index_along(shape, 0) == rows - 1, 0.0, along_y)
        fz[i] = jnp.where(lane == lanes - 1, 0.0, along_z)
        back_y, back_z = 0.5 * (k + beyond(k, -1, 0)), 0.5 * (k + beyond(k, -1, 1))
        diag[i] = diag[i] + fx[i] + along_x + along_y + back_y + along_z + back_z
        total, square = carry
        for p, at in ((mine[i], c), (got[0, i], 1 - c)):
            part = count[i, pl.ds(base + cy * at, cy), :] * p
            total, square = total + folded(part), square + folded(part * p)
        return total, square

    zero = jnp.zeros((8, lanes), jnp.float32)
    sums[0], sums[1] = lax.fori_loop(0, planes, set_up, (zero, zero), unroll=4)


def halo_kernel(kap_table, abs_table, edge, kap, diag_in, fx_in, fy_in, fz_in, diag, fx, fy, fz):
    _, _, y, _ = places(2)
    planes, rows, lanes = diag.shape
    for ref, old in ((diag, diag_in), (fx, fx_in), (fy, fy_in), (fz, fz_in)):
        ref[...] = old[...]
    shape = (HALO, lanes)
    lane, row = index_along(shape, 1), index_along(shape, 0)
    kap_row, abs_row = table_rows(kap_table, abs_table, shape)
    low = y == 0
    here = pl.ds((rows - HALO) * (1 - y), HALO)
    beside_it = pl.ds((rows - 2 * HALO) * (1 - y) + HALO * y, HALO)
    labels = [edge_tile(edge[1, i // GROUP], i % GROUP, y).astype(jnp.int32) for i in range(planes)]
    tiles = [jnp.take_along_axis(kap_row, at, axis=1) for at in labels]
    none = jnp.zeros(shape, jnp.float32)
    before = 0.5 * tiles[0]
    fx[0, here, :] = before
    for i, k in enumerate(tiles):
        after = 0.5 * (k + (tiles[i + 1] if i + 1 < planes else none))
        own = kap[i + 1, beside_it, :]
        up, down = shifted(k, -1, 0), shifted(k, 1, 0)
        k_up = jnp.where(row == HALO - 1, jnp.where(low, 0.0, shifted(own, -1, 0)), up)
        k_down = jnp.where(row == 0, jnp.where(low, shifted(own, 1, 0), 0.0), down)
        along_y, back_y = 0.5 * (k + k_up), 0.5 * (k + k_down)
        along_z, back_z = 0.5 * (k + beyond(k, 1, 1)), 0.5 * (k + beyond(k, -1, 1))
        fx[i + 1, here, :] = after
        fy[i, here, :] = jnp.where(low & (row == HALO - 1), 0.0, along_y)
        fz[i, here, :] = jnp.where(lane == lanes - 1, 0.0, along_z)
        absorb = jnp.take_along_axis(abs_row, labels[i], axis=1)
        diag[i, here, :] = absorb + before + after + along_y + back_y + along_z + back_z
        before = after
        face_up = jnp.where(low & (row == HALO - 1), 0.5 * up, 0.0)
        face_down = jnp.where(low | (row > 0), 0.0, 0.5 * down)
        fy[i, beside_it, :] = fy_in[i, beside_it, :] + face_up
        diag[i, beside_it, :] = diag_in[i, beside_it, :] + face_up + face_down


def density_kernel(mine, got, edge, phi, phi_y, phi_z):
    _, _, y, c = places(2)
    framed(phi, 1, mine, got.at[0], edge.at[0], y, c)
    blank_ends(phi)

    def differ(i, carry):
        p = phi[i + 1]
        phi_y[i], phi_z[i] = p - beyond(p, 1, 0), p - beyond(p, 1, 1)
        return carry

    lax.fori_loop(0, phi_y.shape[0], differ, 0, unroll=4)


def first_kernel(
    phi, phi_y, phi_z, diag, fx, fy, fz, count, sums, vector, got_vector, edge,
    change, message,
    vk, va, b, buf_a, buf_b,
):
    _, _, y, c = places(2)
    planes, rows, lanes = change.shape
    cy = vector.shape[2]
    framed(vk, 1, vector.at[0], got_vector.at[0], edge.at[0], y, c)
    framed(va, 0, vector.at[1], got_vector.at[1], edge.at[1], y, c)
    blank_ends(vk, buf_a, buf_b)
    theta, _ = chebyshev_scalars()

    def set_up(i, carry):
        v, p = vk[i + 1], phi[i + 1]
        total = 0.5 * (v + vk[i]) * (p - phi[i]) + 0.5 * (v + vk[i + 2]) * (p - phi[i + 2])
        for axis, step in enumerate((phi_y, phi_z)):
            flow = 0.5 * (v + beyond(v, 1, axis)) * step[i]
            first = index_along(v.shape, axis) == 0
            total = total + flow + jnp.where(first, 0.5 * v * p, -shifted(flow, 1, axis))
        total = -(va[i] * p + total)
        b[i] = total
        buf_a[i + 1] = total * (1.0 / theta)
        return carry

    lax.fori_loop(0, planes, set_up, 0, unroll=4)
    found = solve(b, (buf_a, buf_b), diag, fx, fy, fz, UNROLL)
    owned = owned_rows((rows, lanes), HALO * y, 2 * cy)

    def add_up(i, carry):
        u = found[i + 1]
        change[i] = u
        part = jnp.where(owned, count[i], 0.0) * u
        return carry[0] + folded(part), carry[1] + folded(part * phi[i + 1])

    zero = jnp.zeros((8, lanes), jnp.float32)
    seen, cross = lax.fori_loop(0, planes, add_up, (zero, zero), unroll=4)
    first = (2 * cy - HALO) * (1 - y) + HALO * y
    size = GROUP * REACH
    for g in range(planes // GROUP):
        message[pl.ds(size * g, size), :] = packed_edges(
            [near_rows(found, 1 + GROUP * g + j, first, y) for j in range(GROUP)]
        )
    rows_of_sums = [jnp.sum(part, axis=0, keepdims=True) for part in (sums[0], seen, cross, sums[1])]
    message[pl.ds(REACH * planes, 8), :] = jnp.concatenate([*rows_of_sums, zero[:4]], axis=0)


def second_kernel(
    phi, phi_y, phi_z, change, diag, fx, fy, fz, count, sent, came,
    own, message,
    b, buf_a, buf_b, grad_k, grad_a,
    *, dets,
):
    _, _, y, c = places(2)
    planes, rows, lanes = change.shape
    cy = (rows - HALO) // 2
    base = HALO * y
    edge = pl.ds(2 * cy * (1 - y), HALO)
    tail = pl.ds(REACH * planes, 8)
    sums = jnp.sum(sent[tail, :] + came[tail, :], axis=1, keepdims=True)
    total, seen_sum, cross, square = (sums[g : g + 1] for g in range(4))
    mean = total / dets
    part = seen_sum / total
    level = (cross - part * square) / (total * mean)
    inverse = 1.0 / mean
    blank_ends(buf_a, buf_b)
    theta, _ = chebyshev_scalars()

    def weighted(n, u, p):
        return n * (((u - p * part) * inverse - level) * inverse)

    def set_up(i, carry):
        value = weighted(count[i], change[i], phi[i + 1])
        b[i] = value
        buf_a[i + 1] = value * (1.0 / theta)
        return carry

    lax.fori_loop(0, planes, set_up, 0, unroll=4)
    size = GROUP * REACH
    for i in range(planes):
        u = edge_tile(came[pl.ds(size * (i // GROUP), size), :], i % GROUP, y)
        value = weighted(count[i, edge, :], u, phi[i + 1, edge, :])
        b[i, edge, :] = value
        buf_a[i + 1, edge, :] = value * (1.0 / theta)
    dual = solve(b, (buf_a, buf_b), diag, fx, fy, fz, UNROLL)

    def product(i, carry):
        p, u = phi[i + 1], dual[i + 1]
        grad = (p - phi[i]) * (u - dual[i]) + (p - phi[i + 2]) * (u - dual[i + 2])
        both = p * u
        for axis, step in enumerate((phi_y, phi_z)):
            flow = step[i] * (u - beyond(u, 1, axis))
            first = index_along(p.shape, axis) == 0
            grad = grad + flow + jnp.where(first, both, shifted(flow, 1, axis))
        grad_k[i] = -0.5 * grad
        grad_a[i] = -both
        for f, ref in enumerate((grad_k, grad_a)):
            own[f, i] = ref[i, pl.ds(base + cy * c, cy), :]
            message[f, i] = ref[i, pl.ds(base + cy * (1 - c), cy), :]
        return carry

    lax.fori_loop(0, planes, product, 0, unroll=4)


def packed_slabs(own, came, half, choices, outs):
    s, _, _, _ = places(2)
    _, planes, cy, lanes = own.shape
    n = planes // 2 // outs.shape[2]
    slab = lanes // n
    lane = index_along((cy, lanes), 1) // slab
    for f in range(2):
        for q in range(outs.shape[2]):
            at = planes // 2 * half + n * q
            parts = [own[f, at + j] + came[f, at + j] for j in range(n)]
            for i, k in enumerate(choices):
                to = s ^ k
                piece = jnp.zeros((cy, lanes), jnp.float32)
                for j in range(n):
                    moved = pltpu.roll(parts[j], ((j - to + n) % n) * slab, 1)
                    piece = jnp.where(lane == j, moved, piece)
                outs[i, f, q] = piece


def send_kernel(own, came, out, *, k):
    _, x, _, _ = places(2)
    packed_slabs(own, came, 1 - x, (k,), out)


def keep_kernel(own, came, kept):
    _, x, _, _ = places(2)
    packed_slabs(own, came, x, range(kept.shape[0]), kept)


def add_kernel(kept, came, out, *, k):
    out[...] = kept[k] + came[0]


def sum_kernel(*refs):
    total = refs[0][...]
    for ref in refs[1:-1]:
        total = total + ref[...]
    refs[-1][...] = total


def project_kernel(*refs, parts_n, n):
    beta_prev = refs[0]
    parts = refs[1 : 1 + parts_n]
    vk, va, qk, qa, w_k, w_a, tile = refs[1 + parts_n :]
    slab = 128 // n
    for f, (q_ref, w) in enumerate(((qk, w_k), (qa, w_a))):
        for q in range(vk.shape[0] // n):
            whole = sum(part[f, q] for part in parts[1:]) + parts[0][f, q]
            for j in range(n):
                i = n * q + j
                w[i] = whole[:, slab * j : slab * (j + 1)] - beta_prev[:, : vk.shape[2]] * q_ref[i]

    def total(value):
        return jnp.sum(jnp.sum(jnp.sum(value, axis=0), axis=0, keepdims=True), axis=1, keepdims=True)

    wk, wa, v_k, v_a = w_k[...], w_a[...], vk[...], va[...]
    wv = total(wk * v_k + wa * v_a)
    vv = total(v_k * v_k + v_a * v_a)
    a = jnp.where(vv > 0.0, wv / jnp.where(vv > 0.0, vv, 1.0), 0.0)
    u_k, u_a = wk - a * v_k, wa - a * v_a
    uv = total(u_k * v_k + u_a * v_a)
    uu = total(u_k * u_k + u_a * u_a)
    lane = index_along((1, 128), 1)
    values = jnp.zeros((1, 128), jnp.float32)
    for i, value in enumerate((wv, vv, a, uv, uu)):
        values = jnp.where(lane == i, value, values)
    tile[...] = values


def final_kernel(tiles, w_k, w_a, vk, va, next_k, next_a, coefs, *, cells):
    tile = jnp.concatenate([tiles[i] for i in range(tiles.shape[0])], axis=0)
    wv, vv, a, uv, uu = (tile[:, i : i + 1] for i in range(5))
    wv_sum = jnp.sum(wv, axis=0, keepdims=True)
    vv_sum = jnp.sum(vv, axis=0, keepdims=True)
    alpha = wv_sum / cells / (vv_sum / cells + eps_norm)
    off = alpha - a
    rr = jnp.sum(uu - 2.0 * off * uv + off * off * vv, axis=0, keepdims=True)
    beta = jnp.sqrt(rr / cells + eps_norm)
    next_k[...] = (w_k[...] - alpha * vk[...]) / beta
    next_a[...] = (w_a[...] - alpha * va[...]) / beta
    coefs[0] = jnp.sum(alpha)
    coefs[1] = jnp.sum(beta)


def f32(*shape):
    return jax.ShapeDtypeStruct(shape, jnp.float32)


def run(kernel, outs, *args, after=(), scratch=(), copies=0, smem=(), hbm=(), mib=16, in_smem_out=(), cost=None):
    vmem = pl.BlockSpec(memory_space=pltpu.VMEM)
    scalar = pl.BlockSpec(memory_space=pltpu.SMEM)
    far = pl.BlockSpec(memory_space=pltpu.HBM)
    held = [pltpu.VMEM(shape, dtype) for shape, dtype in scratch]
    used, waits = len(args), len(after)

    def body(*refs):
        kernel(*refs[:used], *refs[used + waits :])

    args = (*args, *after)
    if copies:
        held.append(pltpu.SemaphoreType.DMA((copies,)))
    return pl.pallas_call(
        body if waits else kernel,
        out_shape=tuple(outs),
        in_specs=[scalar if i in smem else far if i in hbm else vmem for i in range(len(args))],
        out_specs=tuple(scalar if i in in_smem_out else vmem for i in range(len(outs))),
        scratch_shapes=held,
        compiler_params=pltpu.CompilerParams(vmem_limit_bytes=mib * 2**20),
        cost_estimate=cost,
    )(*args)


HALO = 8
UNROLL = 16
REACH = 6
GROUP = 4


def per_device_paired(
    labels, kappa_table, absorb_table, background, det_cells,
    v_kappa, v_absorb, q_kappa, q_absorb, beta_prev,
):
    sources, cx, cy, cz = background.shape
    n = lax.axis_size("src")
    planes, rows = 2 * cx, 2 * cy + HALO
    ny = cy * lax.axis_size("gy")
    dets = det_cells.shape[0]
    cells = planes * ny * cz
    groups = cx // n

    def swap_x(value):
        return lax.ppermute(value, "gx", [(0, 1), (1, 0)])

    def swap_core(value):
        return lax.ppermute(value, "gy", [(0, 1), (1, 0), (2, 3), (3, 2)])

    def along_z(value, k):
        return lax.ppermute(value, "src", [(i, i ^ k) for i in range(n)])

    block = (cx, cy, cz)
    float_block = lambda *shape: (shape, jnp.float32)
    raw_labels = (block, jnp.int32)
    packed, message = run(
        pack_kernel, (f32(2 * groups, cy, cz), f32(sources // 2 * cx + 2 * groups, cy, cz)),
        background, v_kappa, v_absorb, hbm=(0, 1, 2),
        scratch=(float_block(2, *v_kappa.shape),), copies=2 + sources // 2, mib=60,
    )
    long = pl.CostEstimate(flops=10**9, bytes_accessed=2**26, transcendentals=0)
    labels_came = swap_x(labels)
    came = swap_x(message)
    slabs = [along_z(packed, k) for k in range(1, n)]
    count, beta_row = run(
        functools.partial(count_kernel, ny=ny, nz=cz, half=2 * cy, halo=HALO),
        (f32(planes, rows, cz), f32(1, cz)), det_cells.reshape(1, dets), beta_prev, smem=(1,), after=(labels_came,),
        cost=pl.CostEstimate(flops=2 * planes * rows * cz * dets, bytes_accessed=planes * rows * cz * 4, transcendentals=0),
    )

    def across_y(value):
        return lax.ppermute(value, "gy", [(i, (i + 2) % 4) for i in range(4)])

    (joined,) = run(join_kernel, (f32(2 * groups * (n - 1), cy, cz),), *slabs, after=(count,))
    joined_came = swap_x(joined)
    (half_vector,) = run(own_half_kernel, (f32(2, *block),), v_kappa, v_absorb, joined)
    mine, fields = run(
        photon_kernel, (f32(planes, cy, cz), f32(2, planes, cy, cz)),
        background, labels, came, labels_came, after=(joined,), hbm=(0, 1), scratch=(raw_labels,), copies=3,
    )
    got = swap_core(fields)
    (vector,) = run(
        vector_kernel, (f32(2, planes, cy, cz),), half_vector, came, joined_came, after=(mine,)
    )
    edge = (f32(2, *edge_shape(planes, cz)),)
    (sent,) = run(photon_edge_kernel, edge, mine, fields, got, after=(vector,))
    photon_edge = across_y(sent)
    vector_got = swap_core(vector)
    (vector_sent,) = run(vector_edge_kernel, edge, vector, vector_got, after=(sent,))
    frame, wide = (planes, rows, cz), (planes + 2, rows, cz)
    float_frame, float_wide = float_block(*frame), float_block(*wide)
    coefs = (f32(*frame), f32(planes + 1, rows, cz), f32(*frame), f32(*frame))
    kap, *partial, sums = run(
        stencil_kernel, (f32(*wide), *coefs, f32(2, 8, cz)),
        kappa_table, absorb_table, mine, fields, got, count, after=(vector_sent,), cost=long,
        smem=(0, 1), scratch=(float_frame,),
    )
    diag, fx, fy, fz = run(
        halo_kernel, coefs, kappa_table, absorb_table, photon_edge, kap, *partial, smem=(0, 1)
    )
    densities = run(
        density_kernel, (f32(*wide), f32(*frame), f32(*frame)), mine, got, photon_edge, after=(fz,)
    )
    change, sent = run(
        first_kernel, (f32(*frame), f32(REACH * planes + 8, cz)),
        *densities, diag, fx, fy, fz, count, sums, vector, vector_got, across_y(vector_sent),
        scratch=(float_wide, float_frame, float_frame, float_wide, float_wide),
    )
    heard = across_y(sent)
    own, message = run(
        functools.partial(second_kernel, dets=dets),
        (f32(2, planes, cy, cz), f32(2, planes, cy, cz)),
        *densities, change, diag, fx, fy, fz, count, sent, heard,
        scratch=(float_frame, float_wide, float_wide, float_frame, float_frame),
    )
    piece = f32(2, groups, cy, cz)
    got = swap_core(message)
    crossed, last = {}, ()
    for k in reversed(range(n)):
        last = run(functools.partial(send_kernel, k=k), (f32(1, *piece.shape),), own, got, after=last)
        crossed[k] = swap_x(last[0])
    (kept,) = run(keep_kernel, (f32(n, *piece.shape),), own, got, after=last)
    totals = {
        k: run(functools.partial(add_kernel, k=k), (piece,), kept, value)[0] for k, value in crossed.items()
    }
    received = {k: along_z(totals[k], k) for k in reversed(range(1, n))}
    (distant,) = run(sum_kernel, (piece,), *(received[k] for k in range(n // 2, n)), cost=long)
    parts = [distant, totals[0]] + [received[k] for k in range(1, n // 2)]
    w_k, w_a, tile = run(
        functools.partial(project_kernel, parts_n=len(parts), n=n),
        (f32(*v_kappa.shape), f32(*v_kappa.shape), f32(1, 128)),
        beta_row, *parts, v_kappa, v_absorb, q_kappa, q_absorb,
    )
    everyone = ("src", "gx", "gy")
    tiles = lax.all_gather(tile, everyone)
    return tuple(run(
        functools.partial(final_kernel, cells=cells),
        (f32(*v_kappa.shape), f32(*v_kappa.shape), f32(2)),
        tiles, w_k, w_a, v_kappa, v_absorb, in_smem_out=(2,),
    ))


def paired_fits(mesh):
    return mesh.shape["gx"] == 2 and mesh.shape["gy"] == 4


def body_for(mesh):
    if not paired_fits(mesh):
        return per_device

    def chosen(*args):
        sources, cx, cy, cz = args[3].shape
        n = lax.axis_size("src")
        fits = sources == 4 and cz == 128 and cx % n == 0 and cx % GROUP == 0 and cy % HALO == 0 and n > 1 and n & (n - 1) == 0
        devices = 8 * n
        return (per_device_paired if fits and devices <= 128 else per_device)(*args)

    return chosen


def solution(mesh):
    return jax.shard_map(
        body_for(mesh),
        mesh=mesh,
        in_specs=(
            P("gx", "gy", None),
            P(),
            P(),
            P("src", "gx", "gy", None),
            P(),
            P("gx", "gy", "src"),
            P("gx", "gy", "src"),
            P("gx", "gy", "src"),
            P("gx", "gy", "src"),
            P(),
        ),
        out_specs=(P("gx", "gy", "src"), P("gx", "gy", "src"), P()),
        check_vma=False,
    )
```

```python
import functools

import jax
import jax.numpy as jnp
from jax import lax
from jax.experimental import pallas as pl
from jax.experimental.pallas import tpu as pltpu
from jax.sharding import PartitionSpec as P

ITERS = 6


lam_low = 0.02
lam_high = 24.1
eps_norm = 1e-06


def padded_2(block, sides, width):
    for axis, dim in sides:
        count = lax.axis_size(axis)
        forward = [(i, i + 1) for i in range(count - 1)]
        backward = [(target, source) for source, target in forward]
        low = lax.ppermute(
            lax.slice_in_dim(block, block.shape[dim] - width, None, axis=dim), axis, forward
        )
        high = lax.ppermute(lax.slice_in_dim(block, 0, width, axis=dim), axis, backward)
        block = jnp.concatenate([low, block, high], axis=dim)
    return block


def regional(labels, table):
    field = jnp.zeros(labels.shape, jnp.float32)
    for region in range(table.shape[0]):
        field = field + jnp.where(labels == region, table[region], 0.0)
    return field


def beside(padded):
    widths = [(0, 0)] * (padded.ndim - 1) + [(1, 1)]
    full = jnp.pad(padded, widths)
    return [
        full[..., 2:, 1:-1, 1:-1],
        full[..., :-2, 1:-1, 1:-1],
        full[..., 1:-1, 2:, 1:-1],
        full[..., 1:-1, :-2, 1:-1],
        full[..., 1:-1, 1:-1, 2:],
        full[..., 1:-1, 1:-1, :-2],
    ]


def chebyshev(rhs, apply_op):
    theta = 0.5 * (lam_high + lam_low)
    delta = 0.5 * (lam_high - lam_low)
    sigma = theta / delta
    rho = 1.0 / sigma
    solution = jnp.zeros_like(rhs)
    remain = rhs
    step_dir = rhs / theta
    for step in range(ITERS):
        solution = solution + step_dir
        if step + 1 < ITERS:
            remain = remain - apply_op(step_dir)
            rho_next = 1.0 / (2.0 * sigma - rho)
            step_dir = rho_next * rho * step_dir + 2.0 * rho_next / delta * remain
            rho = rho_next
    return solution


def per_device(
    labels,
    kappa_table,
    absorb_table,
    background,
    det_cells,
    v_kappa,
    v_absorb,
    q_kappa,
    q_absorb,
    beta_prev,
):
    sources, cx, cy, cz = background.shape
    kappa = regional(labels, kappa_table)
    absorb = regional(labels, absorb_table)
    full_k, full_a = (
        lax.all_gather(v_kappa, "src", axis=2, tiled=True),
        lax.all_gather(v_absorb, "src", axis=2, tiled=True),
    )
    stacked = jnp.concatenate([background, kappa[None], full_k[None]], axis=0)
    rims = padded_2(stacked, (("gx", 1), ("gy", 2)), 1)
    near_all = beside(rims)
    kappa_faces = [0.5 * (kappa + near[sources]) for near in near_all]
    vk_faces = [0.5 * (full_k + near[sources + 1]) for near in near_all]
    phi_near = [near[:sources] for near in near_all]

    def apply_op(field):
        padded = padded_2(field, (("gx", 1), ("gy", 2)), 1)
        result = absorb * field
        for face, near in zip(kappa_faces, beside(padded)):
            result = result + face * (field - near)
        return result

    rhs = full_a * background
    for face, near in zip(vk_faces, phi_near):
        rhs = rhs + face * (background - near)
    rhs = -rhs
    change = chebyshev(rhs, apply_op)
    span_y = cy * lax.axis_size("gy")
    ix = det_cells // (span_y * cz)
    iy = det_cells // cz % span_y
    iz = det_cells % cz
    anchor_x = lax.axis_index("gx") * cx
    anchor_y = lax.axis_index("gy") * cy
    owned = (ix >= anchor_x) & (ix < anchor_x + cx) & (iy >= anchor_y) & (iy < anchor_y + cy)
    local = jnp.where(owned, ((ix - anchor_x) * cy + (iy - anchor_y)) * cz + iz, 0)
    seen_part = jnp.where(owned[None, :], change.reshape(sources, -1)[:, local], 0.0)
    base_part = jnp.where(owned[None, :], background.reshape(sources, -1)[:, local], 0.0)
    seen, base = lax.psum((seen_part, base_part), ("gx", "gy"))
    total = jnp.sum(base, axis=1, keepdims=True)
    mean_base = total / det_cells.shape[0]
    ratio = base / total
    jv_vals = (seen - ratio * jnp.sum(seen, axis=1, keepdims=True)) / mean_base
    weight = (jv_vals - jnp.sum(ratio * jv_vals, axis=1, keepdims=True)) / mean_base
    deposit = jnp.where(owned[None, :], weight, 0.0)
    source = (
        jnp.zeros((sources, cx * cy * cz), jnp.float32)
        .at[:, local]
        .add(deposit)
        .reshape(change.shape)
    )
    dual = chebyshev(source, apply_op)
    dual_rims = padded_2(dual, (("gx", 1), ("gy", 2)), 1)
    grad_a = -jnp.sum(background * dual, axis=0)
    grad_k = jnp.zeros_like(kappa)
    for near_phi, near_dual in zip(phi_near, beside(dual_rims)):
        grad_k = grad_k - 0.5 * jnp.sum((background - near_phi) * (dual - near_dual), axis=0)
    summed_k, summed_a = lax.psum((grad_k, grad_a), "src")
    slab = v_kappa.shape[2]
    offset = lax.axis_index("src") * slab
    hv_k = lax.dynamic_slice_in_dim(summed_k, offset, slab, 2)
    hv_a = lax.dynamic_slice_in_dim(summed_a, offset, slab, 2)
    cell_count = cx * lax.axis_size("gx") * cy * lax.axis_size("gy") * cz
    w_k = hv_k - beta_prev[0] * q_kappa
    w_a = hv_a - beta_prev[0] * q_absorb
    local_wv = jnp.sum(w_k * v_kappa) + jnp.sum(w_a * v_absorb)
    local_vv = jnp.sum(v_kappa * v_kappa) + jnp.sum(v_absorb * v_absorb)
    wv_sum, vv_sum = lax.psum((local_wv, local_vv), ("src", "gx", "gy"))
    alpha = wv_sum / cell_count / (vv_sum / cell_count + eps_norm)
    r_k = w_k - alpha * v_kappa
    r_a = w_a - alpha * v_absorb
    rr_sum = lax.psum(jnp.sum(r_k * r_k) + jnp.sum(r_a * r_a), ("src", "gx", "gy"))
    beta = jnp.sqrt(rr_sum / cell_count + eps_norm)
    return (r_k / beta, r_a / beta, jnp.stack([alpha, beta]))


def chebyshev_scalars():
    theta = 0.5 * (lam_high + lam_low)
    delta = 0.5 * (lam_high - lam_low)
    sigma = theta / delta
    rho = 1.0 / sigma
    pairs = []
    for _ in range(ITERS - 1):
        rho_next = 1.0 / (2.0 * sigma - rho)
        pairs.append((rho_next * rho, 2.0 * rho_next / delta))
        rho = rho_next
    return theta, pairs


def places(split):
    g = lax.axis_index("gy")
    return lax.axis_index("src"), lax.axis_index("gx"), g // split, g % split


def shifted(value, step, axis):
    return pltpu.roll(value, step % value.shape[axis], axis)


def index_along(shape, axis):
    return lax.broadcasted_iota(jnp.int32, shape, axis)


def beyond(value, step, axis):
    size = value.shape[axis]
    at = index_along(value.shape, axis)
    edge = size - 1 if step == 1 else 0
    return jnp.where(at == edge, 0.0, shifted(value, -step, axis))


def packed_planes(ref, q):
    per = 128 // ref.shape[2]
    return jnp.concatenate([ref[per * q + j] for j in range(per)], axis=1)


def pack_kernel(bg, vk, va, packed, message, v_in, sems):
    _, x, _, _ = places(2)
    half = bg.shape[0] // 2
    cx = bg.shape[1]
    copies = [
        pltpu.make_async_copy(src, dst, sems.at[i])
        for i, (src, dst) in enumerate((
            (vk, v_in.at[0]),
            (va, v_in.at[1]),
            *((bg.at[half * (1 - x) + i], message.at[pl.ds(cx * i, cx)]) for i in range(half)),
        ))
    ]
    for copy in copies:
        copy.start()
    groups = packed.shape[0] // 2
    for f in range(2):
        copies[f].wait()
        for q in range(groups):
            planes = packed_planes(v_in.at[f], q)
            packed[groups * f + q] = planes
            message[cx * half + groups * f + q] = planes
    for copy in copies[2:]:
        copy.wait()


def count_kernel(dets, beta_prev, count, beta_row, *, ny, nz, half, halo):
    beta_row[...] = jnp.full(beta_row.shape, beta_prev[0])
    _, _, y, _ = places(2)
    planes, rows, _ = count.shape
    flat = dets[...]
    iz = flat % nz
    line = flat // nz
    iy = line % ny
    ix = line // ny
    row = iy - (half - halo) * y
    spot = jnp.where((row >= 0) & (row < rows), ix * rows + row, -1)
    dets_n = flat.shape[1]
    at_z = (index_along((nz, dets_n), 0) == iz).astype(jnp.float32).astype(jnp.bfloat16)

    def body(i, carry):
        here = index_along((2 * rows, dets_n), 0) + i * (2 * rows)
        hot = (here == spot).astype(jnp.float32).astype(jnp.bfloat16)
        found = lax.dot_general(hot, at_z, (((1,), (1,)), ((), ())), preferred_element_type=jnp.float32)
        count[pl.ds(2 * i, 2)] = found.reshape(2, rows, nz)
        return carry

    lax.fori_loop(0, planes // 2, body, 0)


def photon_kernel(bg, labels, msg, labels_came, mine, fields, raw, sems):
    _, x, _, c = places(2)
    half = bg.shape[0] // 2
    cx = labels.shape[0]
    here, there = cx * x, cx * (1 - x)
    copies = [
        pltpu.make_async_copy(src, dst, sems.at[i])
        for i, (src, dst) in enumerate((
            (bg.at[half * x + c], mine.at[pl.ds(here, cx)]),
            (bg.at[half * x + 1 - c], fields.at[0, pl.ds(here, cx)]),
            (labels, raw),
        ))
    ]
    for copy in copies:
        copy.start()
    mine[pl.ds(there, cx)] = msg[pl.ds(cx * c, cx)]
    fields[0, pl.ds(there, cx)] = msg[pl.ds(cx * (1 - c), cx)]
    fields[1, pl.ds(there, cx)] = labels_came[...].astype(jnp.float32)
    for copy in copies:
        copy.wait()
    fields[1, pl.ds(here, cx)] = raw[...].astype(jnp.float32)


def unpacked(blocks, groups, s, store):
    n = len(blocks)
    cy, lanes = blocks[0][0].shape
    slab = lanes // n
    lane = index_along((cy, lanes), 1) // slab
    for f in range(2):
        for q in range(groups):
            values = [block[groups * f + q] for block in blocks]
            for j in range(n):
                plane = jnp.zeros((cy, lanes), jnp.float32)
                for k in range(n):
                    home = s ^ k
                    moved = pltpu.roll(values[k], ((home - j + n) % n) * slab, 1)
                    plane = jnp.where(lane == home, moved, plane)
                store(f, n * q + j, plane)


def join_kernel(*refs):
    joined, size = refs[-1], refs[0].shape[0]
    for i, ref in enumerate(refs[:-1]):
        joined[pl.ds(size * i, size)] = ref[...]


def own_half_kernel(vk, va, joined, half):
    s, _, _, _ = places(2)
    size = half.shape[1]
    groups = joined.shape[0] // 2 // (128 // vk.shape[2] - 1)
    n = size // groups
    own = [packed_planes(ref, q) for ref in (vk, va) for q in range(groups)]
    blocks = [own] + [[joined[2 * groups * k + i] for i in range(2 * groups)] for k in range(n - 1)]

    def store(f, i, plane):
        half[f, i] = plane

    unpacked(blocks, groups, s, store)


def vector_kernel(half, msg, joined, fields):
    s, x, _, _ = places(2)
    cx = half.shape[1]
    fields[:, pl.ds(cx * x, cx)] = half[...]
    n = lax.axis_size("src")
    groups = cx // n
    own = msg.shape[0] - 2 * groups
    blocks = [[msg[own + i] for i in range(2 * groups)]]
    blocks += [[joined[2 * groups * k + i] for i in range(2 * groups)] for k in range(n - 1)]
    there = cx * (1 - x)

    def store(f, i, plane):
        fields[f, there + i] = plane

    unpacked(blocks, groups, s, store)


def edge_shape(planes, lanes):
    return planes // GROUP, GROUP * REACH, lanes


def packed_edges(tiles):
    return jnp.concatenate([tile[:REACH] for tile in tiles], axis=0)


def edge_tile(packed, j, y):
    rows = packed[REACH * j : REACH * (j + 1)]
    tile = jnp.concatenate([rows, jnp.zeros((HALO - REACH, rows.shape[1]), jnp.float32)], axis=0)
    return jnp.where(y == 0, tile, shifted(tile, HALO - REACH, 0))


def near_rows(ref, i, first, y):
    tile = ref[i, pl.ds(first, HALO), :]
    return jnp.where(y == 0, shifted(tile, REACH - HALO, 0), tile)


def edges_of(own, got, edge, y, c):
    first = (own.shape[1] - HALO) * (1 - y)
    for g in range(edge.shape[0]):
        edge[g] = packed_edges([
            jnp.where(c != y, near_rows(own, GROUP * g + j, first, y), near_rows(got, GROUP * g + j, first, y))
            for j in range(GROUP)
        ])


def photon_edge_kernel(mine, fields, got, edge):
    _, _, y, c = places(2)
    edges_of(mine, got.at[0], edge.at[0], y, c)
    edges_of(fields.at[1], got.at[1], edge.at[1], y, c)


def vector_edge_kernel(fields, got, edge):
    _, _, y, c = places(2)
    for f in range(2):
        edges_of(fields.at[f], got.at[f], edge.at[f], y, c)


def solve(b, bufs, diag, fx, fy, fz, unroll, after_step=None):
    planes = b.shape[0]
    _, pairs = chebyshev_scalars()
    for step, (keep, push) in enumerate(pairs):
        src, dst = bufs[step % 2], bufs[(step + 1) % 2]

        def body(i, carry):
            u = src[i + 1]
            coef_y, coef_z = fy[i], fz[i]
            left = b[i] - diag[i] * u
            left = left + fx[i] * src[i] + fx[i + 1] * src[i + 2]
            left = left + coef_y * shifted(u, -1, 0) + shifted(coef_y * u, 1, 0)
            left = left + coef_z * shifted(u, -1, 1) + shifted(coef_z * u, 1, 1)
            change = u if step == 0 else u - dst[i + 1]
            dst[i + 1] = u + keep * change + push * left
            return carry

        lax.fori_loop(0, planes, body, 0, unroll=unroll)
        if after_step is not None:
            after_step(step + 1, dst)
    return bufs[len(pairs) % 2]


def folded(value):
    return jnp.sum(value.reshape(-1, 8, value.shape[1]), axis=0)


def framed_own(ref, shift, own, got, y, c):
    planes, cy, _ = own.shape
    there = pl.ds(shift, planes)
    base = HALO * y
    ref[there, pl.ds(base + cy * c, cy), :] = own[...]
    ref[there, pl.ds(base + cy * (1 - c), cy), :] = got[...]


def framed(ref, shift, own, got, edge, y, c):
    framed_own(ref, shift, own, got, y, c)
    cy = own.shape[1]
    for g in range(edge.shape[0]):
        packed = edge[g]
        for j in range(GROUP):
            ref[shift + GROUP * g + j, pl.ds(2 * cy * (1 - y), HALO), :] = edge_tile(packed, j, y)


def blank_ends(*refs):
    for ref in refs:
        blank = jnp.zeros(ref.shape[1:], jnp.float32)
        ref[0] = blank
        ref[ref.shape[0] - 1] = blank


def owned_rows(shape, base, count):
    at_row = index_along(shape, 0)
    return (at_row >= base) & (at_row < base + count)


def table_rows(kap_table, abs_table, shape):
    lane = index_along(shape, 1)
    kap_row = abs_row = jnp.zeros(shape, jnp.float32)
    for region in range(kap_table.shape[0]):
        kap_row = jnp.where(lane == region, kap_table[region], kap_row)
        abs_row = jnp.where(lane == region, abs_table[region], abs_row)
    return kap_row, abs_row


def stencil_kernel(
    kap_table, abs_table, mine, fields, got, count,
    kap, diag, fx, fy, fz, sums,
    labels,
):
    _, _, y, c = places(2)
    planes, cy, lanes = mine.shape
    rows = 2 * cy + HALO
    base = HALO * y
    framed_own(labels, 0, fields.at[1], got.at[1], y, c)
    labels[:, pl.ds(2 * cy * (1 - y), HALO), :] = jnp.zeros((planes, HALO, lanes), jnp.float32)
    blank_ends(kap)
    shape = (rows, lanes)
    lane = index_along(shape, 1)
    kap_row, abs_row = table_rows(kap_table, abs_table, shape)
    owned = owned_rows(shape, base, 2 * cy)

    def look_up(i, carry):
        at = labels[i].astype(jnp.int32)
        kap[i + 1] = jnp.where(owned, jnp.take_along_axis(kap_row, at, axis=1), 0.0)
        diag[i] = jnp.take_along_axis(abs_row, at, axis=1)
        return carry

    lax.fori_loop(0, planes, look_up, 0, unroll=4)
    fx[0] = 0.5 * kap[1]

    def set_up(i, carry):
        k = kap[i + 1]
        along_x = 0.5 * (k + kap[i + 2])
        along_y, along_z = 0.5 * (k + beyond(k, 1, 0)), 0.5 * (k + beyond(k, 1, 1))
        fx[i + 1] = along_x
        fy[i] = jnp.where(index_along(shape, 0) == rows - 1, 0.0, along_y)
        fz[i] = jnp.where(lane == lanes - 1, 0.0, along_z)
        back_y, back_z = 0.5 * (k + beyond(k, -1, 0)), 0.5 * (k + beyond(k, -1, 1))
        diag[i] = diag[i] + fx[i] + along_x + along_y + back_y + along_z + back_z
        total, square = carry
        for p, at in ((mine[i], c), (got[0, i], 1 - c)):
            part = count[i, pl.ds(base + cy * at, cy), :] * p
            total, square = total + folded(part), square + folded(part * p)
        return total, square

    zero = jnp.zeros((8, lanes), jnp.float32)
    sums[0], sums[1] = lax.fori_loop(0, planes, set_up, (zero, zero), unroll=4)


def halo_kernel(kap_table, abs_table, edge, kap, diag_in, fx_in, fy_in, fz_in, diag, fx, fy, fz):
    _, _, y, _ = places(2)
    planes, rows, lanes = diag.shape
    for ref, old in ((diag, diag_in), (fx, fx_in), (fy, fy_in), (fz, fz_in)):
        ref[...] = old[...]
    shape = (HALO, lanes)
    lane, row = index_along(shape, 1), index_along(shape, 0)
    kap_row, abs_row = table_rows(kap_table, abs_table, shape)
    low = y == 0
    here = pl.ds((rows - HALO) * (1 - y), HALO)
    beside_it = pl.ds((rows - 2 * HALO) * (1 - y) + HALO * y, HALO)
    labels = [edge_tile(edge[1, i // GROUP], i % GROUP, y).astype(jnp.int32) for i in range(planes)]
    tiles = [jnp.take_along_axis(kap_row, at, axis=1) for at in labels]
    none = jnp.zeros(shape, jnp.float32)
    before = 0.5 * tiles[0]
    fx[0, here, :] = before
    for i, k in enumerate(tiles):
        after = 0.5 * (k + (tiles[i + 1] if i + 1 < planes else none))
        own = kap[i + 1, beside_it, :]
        up, down = shifted(k, -1, 0), shifted(k, 1, 0)
        k_up = jnp.where(row == HALO - 1, jnp.where(low, 0.0, shifted(own, -1, 0)), up)
        k_down = jnp.where(row == 0, jnp.where(low, shifted(own, 1, 0), 0.0), down)
        along_y, back_y = 0.5 * (k + k_up), 0.5 * (k + k_down)
        along_z, back_z = 0.5 * (k + beyond(k, 1, 1)), 0.5 * (k + beyond(k, -1, 1))
        fx[i + 1, here, :] = after
        fy[i, here, :] = jnp.where(low & (row == HALO - 1), 0.0, along_y)
        fz[i, here, :] = jnp.where(lane == lanes - 1, 0.0, along_z)
        absorb = jnp.take_along_axis(abs_row, labels[i], axis=1)
        diag[i, here, :] = absorb + before + after + along_y + back_y + along_z + back_z
        before = after
        face_up = jnp.where(low & (row == HALO - 1), 0.5 * up, 0.0)
        face_down = jnp.where(low | (row > 0), 0.0, 0.5 * down)
        fy[i, beside_it, :] = fy_in[i, beside_it, :] + face_up
        diag[i, beside_it, :] = diag_in[i, beside_it, :] + face_up + face_down


def density_kernel(mine, got, edge, phi, phi_y, phi_z):
    _, _, y, c = places(2)
    framed(phi, 1, mine, got.at[0], edge.at[0], y, c)
    blank_ends(phi)

    def differ(i, carry):
        p = phi[i + 1]
        phi_y[i], phi_z[i] = p - beyond(p, 1, 0), p - beyond(p, 1, 1)
        return carry

    lax.fori_loop(0, phi_y.shape[0], differ, 0, unroll=4)


def rhs_into(b, buf, phi, vk, va, phi_y, phi_z):
    theta, _ = chebyshev_scalars()

    def set_up(i, carry):
        v, p = vk[i + 1], phi[i + 1]
        total = 0.5 * (v + vk[i]) * (p - phi[i]) + 0.5 * (v + vk[i + 2]) * (p - phi[i + 2])
        for axis, step in enumerate((phi_y, phi_z)):
            difference = p - beyond(p, 1, axis) if step is None else step[i]
            flow = 0.5 * (v + beyond(v, 1, axis)) * difference
            first = index_along(v.shape, axis) == 0
            total = total + flow + jnp.where(first, 0.5 * v * p, -shifted(flow, 1, axis))
        total = -(va[i] * p + total)
        b[i] = total
        buf[i + 1] = total * (1.0 / theta)
        return carry

    lax.fori_loop(0, b.shape[0], set_up, 0, unroll=4)


def tile_places(rows, y):
    size = HALO * 3
    return (rows - size) * (1 - y), (rows - 2 * HALO) * (1 - y) + HALO * y, (rows - size) * (1 - y) + 2 * HALO * y


def ahead_kernel(
    diag, fx, fy, fz, count, mine, got_photon, vector, got_vector,
    change, far, sums,
    phi, vk, va, b, buf_a, buf_b,
):
    _, _, y, c = places(2)
    planes, rows, lanes = change.shape
    cy = mine.shape[1]
    none = jnp.zeros((planes, HALO, lanes), jnp.float32)
    halo_rows = pl.ds(2 * cy * (1 - y), HALO)
    for ref, shift, own, got in (
        (phi, 1, mine, got_photon.at[0]), (vk, 1, vector.at[0], got_vector.at[0]), (va, 0, vector.at[1], got_vector.at[1])
    ):
        framed_own(ref, shift, own, got, y, c)
        ref[pl.ds(shift, planes), halo_rows, :] = none
    blank_ends(phi, vk, buf_a, buf_b)
    rhs_into(b, buf_a, phi, vk, va, None, None)
    _, near_row, far_row = tile_places(rows, y)

    def save(step, buf):
        if step < far.shape[0]:
            far[step] = buf[pl.ds(1, planes), pl.ds(far_row, HALO), :]

    save(0, buf_a)
    found = solve(b, (buf_a, buf_b), diag, fx, fy, fz, UNROLL, save)
    at_row = index_along((rows, lanes), 0)
    summed = owned_rows((rows, lanes), HALO * y, 2 * cy) & ((at_row < near_row) | (at_row >= near_row + HALO))

    def add_up(i, carry):
        u = found[i + 1]
        change[i] = u
        part = jnp.where(summed, count[i], 0.0) * u
        return carry[0] + folded(part), carry[1] + folded(part * phi[i + 1])

    zero = jnp.zeros((8, lanes), jnp.float32)
    sums[0], sums[1] = lax.fori_loop(0, planes, add_up, (zero, zero), unroll=4)


def beside_kernel(
    phi, diag, fx, fy, fz, count, sums, found_sums, far, vector, got_vector, edge,
    near, message,
    phi_in, vk, va, b, buf_a, buf_b,
):
    _, _, y, c = places(2)
    planes, rows, lanes = diag.shape
    cy = (rows - HALO) // 2
    all_row, near_row, far_row = tile_places(rows, y)
    window = pl.ds(pl.multiple_of(all_row, 8), 3 * HALO)
    inner = c != y
    source = pl.ds((cy - 2 * HALO) * (1 - y), 2 * HALO)
    for ref, shift, f in ((vk, 1, 0), (va, 0, 1)):
        for i in range(planes):
            own = jnp.where(inner, vector[f, i, source, :], got_vector[f, i, source, :])
            ref[shift + i, pl.ds(HALO * y, 2 * HALO), :] = own
            tile = edge_tile(edge[f, i // GROUP], i % GROUP, y)
            ref[shift + i, pl.ds(2 * HALO * (1 - y), HALO), :] = tile
    phi_in[...] = phi[:, window, :]
    blank_ends(vk, buf_a, buf_b)
    rhs_into(b, buf_a, phi_in, vk, va, None, None)
    given = pl.ds(2 * HALO * y, HALO)

    def give(step, buf):
        if step < far.shape[0]:
            buf[pl.ds(1, planes), given, :] = far[step]

    give(0, buf_a)
    views = (ref.at[:, window, :] for ref in (diag, fx, fy, fz))
    found = solve(b, (buf_a, buf_b), *views, UNROLL, give)
    seen, cross = found_sums[0], found_sums[1]
    near_rows_at = pl.ds(pl.multiple_of(near_row, 8), HALO)
    for i in range(planes):
        u = found[i + 1, pl.ds(HALO, HALO), :]
        near[i] = u
        part = count[i, near_rows_at, :] * u
        seen, cross = seen + part, cross + part * phi[i + 1, near_rows_at, :]
    size = GROUP * REACH
    for g in range(planes // GROUP):
        message[pl.ds(size * g, size), :] = packed_edges(
            [near_rows(near, GROUP * g + j, 0, y) for j in range(GROUP)]
        )
    rows_of_sums = [jnp.sum(part, axis=0, keepdims=True) for part in (sums[0], seen, cross, sums[1])]
    none = jnp.zeros((4, lanes), jnp.float32)
    message[pl.ds(REACH * planes, 8), :] = jnp.concatenate([*rows_of_sums, none], axis=0)


def second_kernel(
    phi, phi_y, phi_z, change, near, diag, fx, fy, fz, count, sent, came,
    own, message,
    b, buf_a, buf_b, grad_k, grad_a,
    *, dets,
):
    _, _, y, c = places(2)
    planes, rows, lanes = change.shape
    cy = (rows - HALO) // 2
    base = HALO * y
    edge = pl.ds(2 * cy * (1 - y), HALO)
    beside_edge = pl.ds(pl.multiple_of(tile_places(rows, y)[1], 8), HALO)
    tail = pl.ds(REACH * planes, 8)
    sums = jnp.sum(sent[tail, :] + came[tail, :], axis=1, keepdims=True)
    total, seen_sum, cross, square = (sums[g : g + 1] for g in range(4))
    mean = total / dets
    part = seen_sum / total
    level = (cross - part * square) / (total * mean)
    inverse = 1.0 / mean
    blank_ends(buf_a, buf_b)
    theta, _ = chebyshev_scalars()

    def weighted(n, u, p):
        return n * (((u - p * part) * inverse - level) * inverse)

    def set_up(i, carry):
        value = weighted(count[i], change[i], phi[i + 1])
        b[i] = value
        buf_a[i + 1] = value * (1.0 / theta)
        return carry

    lax.fori_loop(0, planes, set_up, 0, unroll=4)
    size = GROUP * REACH
    for i in range(planes):
        outer = edge_tile(came[pl.ds(size * (i // GROUP), size), :], i % GROUP, y)
        for rows_at, u in ((edge, outer), (beside_edge, near[i])):
            value = weighted(count[i, rows_at, :], u, phi[i + 1, rows_at, :])
            b[i, rows_at, :] = value
            buf_a[i + 1, rows_at, :] = value * (1.0 / theta)
    dual = solve(b, (buf_a, buf_b), diag, fx, fy, fz, UNROLL)

    def product(i, carry):
        p, u = phi[i + 1], dual[i + 1]
        grad = (p - phi[i]) * (u - dual[i]) + (p - phi[i + 2]) * (u - dual[i + 2])
        both = p * u
        for axis, step in enumerate((phi_y, phi_z)):
            flow = step[i] * (u - beyond(u, 1, axis))
            first = index_along(p.shape, axis) == 0
            grad = grad + flow + jnp.where(first, both, shifted(flow, 1, axis))
        grad_k[i] = -0.5 * grad
        grad_a[i] = -both
        for f, ref in enumerate((grad_k, grad_a)):
            own[f, i] = ref[i, pl.ds(base + cy * c, cy), :]
            message[f, i] = ref[i, pl.ds(base + cy * (1 - c), cy), :]
        return carry

    lax.fori_loop(0, planes, product, 0, unroll=4)


def packed_slabs(own, came, half, choices, outs):
    s, _, _, _ = places(2)
    _, planes, cy, lanes = own.shape
    n = planes // 2 // outs.shape[2]
    slab = lanes // n
    lane = index_along((cy, lanes), 1) // slab
    for f in range(2):
        for q in range(outs.shape[2]):
            at = planes // 2 * half + n * q
            parts = [own[f, at + j] + came[f, at + j] for j in range(n)]
            for i, k in enumerate(choices):
                to = s ^ k
                piece = jnp.zeros((cy, lanes), jnp.float32)
                for j in range(n):
                    moved = pltpu.roll(parts[j], ((j - to + n) % n) * slab, 1)
                    piece = jnp.where(lane == j, moved, piece)
                outs[i, f, q] = piece


def send_kernel(own, came, out, *, k):
    _, x, _, _ = places(2)
    packed_slabs(own, came, 1 - x, (k,), out)


def keep_kernel(own, came, kept):
    _, x, _, _ = places(2)
    packed_slabs(own, came, x, range(kept.shape[0]), kept)


def add_kernel(kept, came, out, *, k):
    out[...] = kept[k] + came[0]


def sum_kernel(*refs):
    total = refs[0][...]
    for ref in refs[1:-1]:
        total = total + ref[...]
    refs[-1][...] = total


def project_kernel(*refs, parts_n, n):
    beta_prev = refs[0]
    parts = refs[1 : 1 + parts_n]
    vk, va, qk, qa, w_k, w_a, tile = refs[1 + parts_n :]
    slab = 128 // n
    for f, (q_ref, w) in enumerate(((qk, w_k), (qa, w_a))):
        for q in range(vk.shape[0] // n):
            whole = sum(part[f, q] for part in parts[1:]) + parts[0][f, q]
            for j in range(n):
                i = n * q + j
                w[i] = whole[:, slab * j : slab * (j + 1)] - beta_prev[:, : vk.shape[2]] * q_ref[i]

    def total(value):
        return jnp.sum(jnp.sum(jnp.sum(value, axis=0), axis=0, keepdims=True), axis=1, keepdims=True)

    wk, wa, v_k, v_a = w_k[...], w_a[...], vk[...], va[...]
    wv = total(wk * v_k + wa * v_a)
    vv = total(v_k * v_k + v_a * v_a)
    a = jnp.where(vv > 0.0, wv / jnp.where(vv > 0.0, vv, 1.0), 0.0)
    u_k, u_a = wk - a * v_k, wa - a * v_a
    uv = total(u_k * v_k + u_a * v_a)
    uu = total(u_k * u_k + u_a * u_a)
    lane = index_along((1, 128), 1)
    values = jnp.zeros((1, 128), jnp.float32)
    for i, value in enumerate((wv, vv, a, uv, uu)):
        values = jnp.where(lane == i, value, values)
    tile[...] = values


def final_kernel(tiles, w_k, w_a, vk, va, next_k, next_a, coefs, *, cells):
    tile = jnp.concatenate([tiles[i] for i in range(tiles.shape[0])], axis=0)
    wv, vv, a, uv, uu = (tile[:, i : i + 1] for i in range(5))
    wv_sum = jnp.sum(wv, axis=0, keepdims=True)
    vv_sum = jnp.sum(vv, axis=0, keepdims=True)
    alpha = wv_sum / cells / (vv_sum / cells + eps_norm)
    off = alpha - a
    rr = jnp.sum(uu - 2.0 * off * uv + off * (off * vv), axis=0, keepdims=True)
    beta = jnp.sqrt(rr / cells + eps_norm)
    next_k[...] = (w_k[...] - alpha * vk[...]) / beta
    next_a[...] = (w_a[...] - alpha * va[...]) / beta
    coefs[0] = jnp.sum(alpha)
    coefs[1] = jnp.sum(beta)


def f32(*shape):
    return jax.ShapeDtypeStruct(shape, jnp.float32)


def run(kernel, outs, *args, after=(), scratch=(), copies=0, smem=(), hbm=(), mib=16, in_smem_out=(), cost=None):
    vmem = pl.BlockSpec(memory_space=pltpu.VMEM)
    scalar = pl.BlockSpec(memory_space=pltpu.SMEM)
    far = pl.BlockSpec(memory_space=pltpu.HBM)
    held = [pltpu.VMEM(shape, dtype) for shape, dtype in scratch]
    used, waits = len(args), len(after)

    def body(*refs):
        kernel(*refs[:used], *refs[used + waits :])

    args = (*args, *after)
    if copies:
        held.append(pltpu.SemaphoreType.DMA((copies,)))
    return pl.pallas_call(
        body if waits else kernel,
        out_shape=tuple(outs),
        in_specs=[scalar if i in smem else far if i in hbm else vmem for i in range(len(args))],
        out_specs=tuple(scalar if i in in_smem_out else vmem for i in range(len(outs))),
        scratch_shapes=held,
        compiler_params=pltpu.CompilerParams(vmem_limit_bytes=mib * 2**20),
        cost_estimate=cost,
    )(*args)


HALO = 8
UNROLL = 16
REACH = 6
GROUP = 4


def per_device_paired(
    labels, kappa_table, absorb_table, background, det_cells,
    v_kappa, v_absorb, q_kappa, q_absorb, beta_prev,
):
    sources, cx, cy, cz = background.shape
    n = lax.axis_size("src")
    planes, rows = 2 * cx, 2 * cy + HALO
    ny = cy * lax.axis_size("gy")
    dets = det_cells.shape[0]
    cells = planes * ny * cz
    groups = cx // n

    def swap_x(value):
        return lax.ppermute(value, "gx", [(0, 1), (1, 0)])

    def swap_core(value):
        return lax.ppermute(value, "gy", [(0, 1), (1, 0), (2, 3), (3, 2)])

    def along_z(value, k):
        return lax.ppermute(value, "src", [(i, i ^ k) for i in range(n)])

    block = (cx, cy, cz)
    float_block = lambda *shape: (shape, jnp.float32)
    raw_labels = (block, jnp.int32)
    packed, message = run(
        pack_kernel, (f32(2 * groups, cy, cz), f32(sources // 2 * cx + 2 * groups, cy, cz)),
        background, v_kappa, v_absorb, hbm=(0, 1, 2),
        scratch=(float_block(2, *v_kappa.shape),), copies=2 + sources // 2, mib=60,
    )
    long = pl.CostEstimate(flops=10**9, bytes_accessed=2**26, transcendentals=0)
    labels_came = swap_x(labels)
    came = swap_x(message)
    slabs = [along_z(packed, k) for k in range(1, n)]
    count, beta_row = run(
        functools.partial(count_kernel, ny=ny, nz=cz, half=2 * cy, halo=HALO),
        (f32(planes, rows, cz), f32(1, cz)), det_cells.reshape(1, dets), beta_prev, smem=(1,), after=(labels_came,),
        cost=pl.CostEstimate(flops=2 * planes * rows * cz * dets, bytes_accessed=planes * rows * cz * 4, transcendentals=0),
    )

    def across_y(value):
        return lax.ppermute(value, "gy", [(i, (i + 2) % 4) for i in range(4)])

    (joined,) = run(join_kernel, (f32(2 * groups * (n - 1), cy, cz),), *slabs, after=(count,))
    joined_came = swap_x(joined)
    (half_vector,) = run(own_half_kernel, (f32(2, *block),), v_kappa, v_absorb, joined)
    mine, fields = run(
        photon_kernel, (f32(planes, cy, cz), f32(2, planes, cy, cz)),
        background, labels, came, labels_came, after=(joined,), hbm=(0, 1), scratch=(raw_labels,), copies=3,
    )
    got = swap_core(fields)
    frame, wide = (planes, rows, cz), (planes + 2, rows, cz)
    float_frame, float_wide = float_block(*frame), float_block(*wide)
    coefs = (f32(*frame), f32(planes + 1, rows, cz), f32(*frame), f32(*frame))
    kap, *partial, sums = run(
        stencil_kernel, (f32(*wide), *coefs, f32(2, 8, cz)),
        kappa_table, absorb_table, mine, fields, got, count,
        smem=(0, 1), scratch=(float_frame,),
    )
    (vector,) = run(
        vector_kernel, (f32(2, planes, cy, cz),), half_vector, came, joined_came, after=(kap,)
    )
    edge = (f32(2, *edge_shape(planes, cz)),)
    (sent,) = run(photon_edge_kernel, edge, mine, fields, got, after=(vector,))
    photon_edge = across_y(sent)
    vector_got = swap_core(vector)
    (vector_sent,) = run(vector_edge_kernel, edge, vector, vector_got, after=(sent,))
    window = lambda count: float_block(count, 3 * HALO, cz)
    change, far, found_sums = run(
        ahead_kernel, (f32(*frame), f32(ITERS - 1, planes, HALO, cz), f32(2, 8, cz)),
        *partial, count, mine, got, vector, vector_got, after=(vector_sent,),
        scratch=(float_wide, float_wide, float_frame, float_frame, float_wide, float_wide),
    )
    diag, fx, fy, fz = run(
        halo_kernel, coefs, kappa_table, absorb_table, photon_edge, kap, *partial, after=(change,), smem=(0, 1)
    )
    densities = run(
        density_kernel, (f32(*wide), f32(*frame), f32(*frame)), mine, got, photon_edge, after=(fz,)
    )
    near, sent = run(
        beside_kernel, (f32(planes, HALO, cz), f32(REACH * planes + 8, cz)),
        densities[0], diag, fx, fy, fz, count, sums, found_sums, far, vector, vector_got, across_y(vector_sent),
        scratch=(window(planes + 2), window(planes + 2), window(planes), window(planes), window(planes + 2),
                 window(planes + 2)),
    )
    heard = across_y(sent)
    own, message = run(
        functools.partial(second_kernel, dets=dets),
        (f32(2, planes, cy, cz), f32(2, planes, cy, cz)),
        *densities, change, near, diag, fx, fy, fz, count, sent, heard,
        scratch=(float_frame, float_wide, float_wide, float_frame, float_frame),
    )
    piece = f32(2, groups, cy, cz)
    got = swap_core(message)
    crossed, last = {}, ()
    for k in reversed(range(n)):
        last = run(functools.partial(send_kernel, k=k), (f32(1, *piece.shape),), own, got, after=last)
        crossed[k] = swap_x(last[0])
    (kept,) = run(keep_kernel, (f32(n, *piece.shape),), own, got, after=last)
    totals = {
        k: run(functools.partial(add_kernel, k=k), (piece,), kept, value)[0] for k, value in crossed.items()
    }
    received = {k: along_z(totals[k], k) for k in reversed(range(1, n))}
    (distant,) = run(sum_kernel, (piece,), *(received[k] for k in range(n // 2, n)), cost=long)
    parts = [distant, totals[0]] + [received[k] for k in range(1, n // 2)]
    w_k, w_a, tile = run(
        functools.partial(project_kernel, parts_n=len(parts), n=n),
        (f32(*v_kappa.shape), f32(*v_kappa.shape), f32(1, 128)),
        beta_row, *parts, v_kappa, v_absorb, q_kappa, q_absorb,
    )
    everyone = ("src", "gx", "gy")
    tiles = lax.all_to_all(jnp.broadcast_to(tile, (8 * n, 1, 128)), everyone, 0, 0)
    return tuple(run(
        functools.partial(final_kernel, cells=cells),
        (f32(*v_kappa.shape), f32(*v_kappa.shape), f32(2)),
        tiles, w_k, w_a, v_kappa, v_absorb, in_smem_out=(2,),
    ))


def paired_fits(mesh):
    return mesh.shape["gx"] == 2 and mesh.shape["gy"] == 4


def body_for(mesh):
    if not paired_fits(mesh):
        return per_device

    def chosen(*args):
        sources, cx, cy, cz = args[3].shape
        n = lax.axis_size("src")
        fits = sources == 4 and cz == 128 and cx % n == 0 and cx % GROUP == 0 and cy % HALO == 0 and n > 1 and n & (n - 1) == 0
        devices = 8 * n
        return (per_device_paired if fits and devices <= 128 else per_device)(*args)

    return chosen


def solution(mesh):
    return jax.shard_map(
        body_for(mesh),
        mesh=mesh,
        in_specs=(
            P("gx", "gy", None),
            P(),
            P(),
            P("src", "gx", "gy", None),
            P(),
            P("gx", "gy", "src"),
            P("gx", "gy", "src"),
            P("gx", "gy", "src"),
            P("gx", "gy", "src"),
            P(),
        ),
        out_specs=(P("gx", "gy", "src"), P("gx", "gy", "src"), P()),
        check_vma=False,
    )
```

```python
import functools

import jax
import jax.numpy as jnp
from jax import lax
from jax.experimental import pallas as pl
from jax.experimental.pallas import tpu as pltpu
from jax.sharding import PartitionSpec as P

ITERS = 6


lam_low = 0.02
lam_high = 24.1
eps_norm = 1e-06


def padded_2(block, sides, width):
    for axis, dim in sides:
        count = lax.axis_size(axis)
        forward = [(i, i + 1) for i in range(count - 1)]
        backward = [(target, source) for source, target in forward]
        low = lax.ppermute(
            lax.slice_in_dim(block, block.shape[dim] - width, None, axis=dim), axis, forward
        )
        high = lax.ppermute(lax.slice_in_dim(block, 0, width, axis=dim), axis, backward)
        block = jnp.concatenate([low, block, high], axis=dim)
    return block


def regional(labels, table):
    field = jnp.zeros(labels.shape, jnp.float32)
    for region in range(table.shape[0]):
        field = field + jnp.where(labels == region, table[region], 0.0)
    return field


def beside(padded):
    widths = [(0, 0)] * (padded.ndim - 1) + [(1, 1)]
    full = jnp.pad(padded, widths)
    return [
        full[..., 2:, 1:-1, 1:-1],
        full[..., :-2, 1:-1, 1:-1],
        full[..., 1:-1, 2:, 1:-1],
        full[..., 1:-1, :-2, 1:-1],
        full[..., 1:-1, 1:-1, 2:],
        full[..., 1:-1, 1:-1, :-2],
    ]


def chebyshev(rhs, apply_op):
    theta = 0.5 * (lam_high + lam_low)
    delta = 0.5 * (lam_high - lam_low)
    sigma = theta / delta
    rho = 1.0 / sigma
    solution = jnp.zeros_like(rhs)
    remain = rhs
    step_dir = rhs / theta
    for step in range(ITERS):
        solution = solution + step_dir
        if step + 1 < ITERS:
            remain = remain - apply_op(step_dir)
            rho_next = 1.0 / (2.0 * sigma - rho)
            step_dir = rho_next * rho * step_dir + 2.0 * rho_next / delta * remain
            rho = rho_next
    return solution


def per_device(
    labels,
    kappa_table,
    absorb_table,
    background,
    det_cells,
    v_kappa,
    v_absorb,
    q_kappa,
    q_absorb,
    beta_prev,
):
    sources, cx, cy, cz = background.shape
    kappa = regional(labels, kappa_table)
    absorb = regional(labels, absorb_table)
    full_k, full_a = (
        lax.all_gather(v_kappa, "src", axis=2, tiled=True),
        lax.all_gather(v_absorb, "src", axis=2, tiled=True),
    )
    stacked = jnp.concatenate([background, kappa[None], full_k[None]], axis=0)
    rims = padded_2(stacked, (("gx", 1), ("gy", 2)), 1)
    near_all = beside(rims)
    kappa_faces = [0.5 * (kappa + near[sources]) for near in near_all]
    vk_faces = [0.5 * (full_k + near[sources + 1]) for near in near_all]
    phi_near = [near[:sources] for near in near_all]

    def apply_op(field):
        padded = padded_2(field, (("gx", 1), ("gy", 2)), 1)
        result = absorb * field
        for face, near in zip(kappa_faces, beside(padded)):
            result = result + face * (field - near)
        return result

    rhs = full_a * background
    for face, near in zip(vk_faces, phi_near):
        rhs = rhs + face * (background - near)
    rhs = -rhs
    change = chebyshev(rhs, apply_op)
    span_y = cy * lax.axis_size("gy")
    ix = det_cells // (span_y * cz)
    iy = det_cells // cz % span_y
    iz = det_cells % cz
    anchor_x = lax.axis_index("gx") * cx
    anchor_y = lax.axis_index("gy") * cy
    owned = (ix >= anchor_x) & (ix < anchor_x + cx) & (iy >= anchor_y) & (iy < anchor_y + cy)
    local = jnp.where(owned, ((ix - anchor_x) * cy + (iy - anchor_y)) * cz + iz, 0)
    seen_part = jnp.where(owned[None, :], change.reshape(sources, -1)[:, local], 0.0)
    base_part = jnp.where(owned[None, :], background.reshape(sources, -1)[:, local], 0.0)
    seen, base = lax.psum((seen_part, base_part), ("gx", "gy"))
    total = jnp.sum(base, axis=1, keepdims=True)
    mean_base = total / det_cells.shape[0]
    ratio = base / total
    jv_vals = (seen - ratio * jnp.sum(seen, axis=1, keepdims=True)) / mean_base
    weight = (jv_vals - jnp.sum(ratio * jv_vals, axis=1, keepdims=True)) / mean_base
    deposit = jnp.where(owned[None, :], weight, 0.0)
    source = (
        jnp.zeros((sources, cx * cy * cz), jnp.float32)
        .at[:, local]
        .add(deposit)
        .reshape(change.shape)
    )
    dual = chebyshev(source, apply_op)
    dual_rims = padded_2(dual, (("gx", 1), ("gy", 2)), 1)
    grad_a = -jnp.sum(background * dual, axis=0)
    grad_k = jnp.zeros_like(kappa)
    for near_phi, near_dual in zip(phi_near, beside(dual_rims)):
        grad_k = grad_k - 0.5 * jnp.sum((background - near_phi) * (dual - near_dual), axis=0)
    summed_k, summed_a = lax.psum((grad_k, grad_a), "src")
    slab = v_kappa.shape[2]
    offset = lax.axis_index("src") * slab
    hv_k = lax.dynamic_slice_in_dim(summed_k, offset, slab, 2)
    hv_a = lax.dynamic_slice_in_dim(summed_a, offset, slab, 2)
    cell_count = cx * lax.axis_size("gx") * cy * lax.axis_size("gy") * cz
    w_k = hv_k - beta_prev[0] * q_kappa
    w_a = hv_a - beta_prev[0] * q_absorb
    local_wv = jnp.sum(w_k * v_kappa) + jnp.sum(w_a * v_absorb)
    local_vv = jnp.sum(v_kappa * v_kappa) + jnp.sum(v_absorb * v_absorb)
    wv_sum, vv_sum = lax.psum((local_wv, local_vv), ("src", "gx", "gy"))
    alpha = wv_sum / cell_count / (vv_sum / cell_count + eps_norm)
    r_k = w_k - alpha * v_kappa
    r_a = w_a - alpha * v_absorb
    rr_sum = lax.psum(jnp.sum(r_k * r_k) + jnp.sum(r_a * r_a), ("src", "gx", "gy"))
    beta = jnp.sqrt(rr_sum / cell_count + eps_norm)
    return (r_k / beta, r_a / beta, jnp.stack([alpha, beta]))


def chebyshev_scalars():
    theta = 0.5 * (lam_high + lam_low)
    delta = 0.5 * (lam_high - lam_low)
    sigma = theta / delta
    rho = 1.0 / sigma
    pairs = []
    for _ in range(ITERS - 1):
        rho_next = 1.0 / (2.0 * sigma - rho)
        pairs.append((rho_next * rho, 2.0 * rho_next / delta))
        rho = rho_next
    return theta, pairs


def places(split):
    g = lax.axis_index("gy")
    return lax.axis_index("src"), lax.axis_index("gx"), g // split, g % split


def shifted(value, step, axis):
    return pltpu.roll(value, step % value.shape[axis], axis)


def index_along(shape, axis):
    return lax.broadcasted_iota(jnp.int32, shape, axis)


def beyond(value, step, axis):
    size = value.shape[axis]
    at = index_along(value.shape, axis)
    edge = size - 1 if step == 1 else 0
    return jnp.where(at == edge, 0.0, shifted(value, -step, axis))


def packed_planes(ref, q):
    per = 128 // ref.shape[2]
    return jnp.concatenate([ref[per * q + j] for j in range(per)], axis=1)


def pack_kernel(bg, vk, va, packed, message, v_in, sems):
    _, x, _, _ = places(2)
    half = bg.shape[0] // 2
    cx = bg.shape[1]
    copies = [
        pltpu.make_async_copy(src, dst, sems.at[i])
        for i, (src, dst) in enumerate((
            (vk, v_in.at[0]),
            (va, v_in.at[1]),
            *((bg.at[half * (1 - x) + i], message.at[pl.ds(cx * i, cx)]) for i in range(half)),
        ))
    ]
    for copy in copies:
        copy.start()
    groups = packed.shape[0] // 2
    for f in range(2):
        copies[f].wait()
        for q in range(groups):
            planes = packed_planes(v_in.at[f], q)
            packed[groups * f + q] = planes
            message[cx * half + groups * f + q] = planes
    for copy in copies[2:]:
        copy.wait()


def count_kernel(dets, beta_prev, count, beta_row, *, ny, nz, half, halo):
    beta_row[...] = jnp.full(beta_row.shape, beta_prev[0])
    _, _, y, _ = places(2)
    planes, rows, _ = count.shape
    flat = dets[...]
    iz = flat % nz
    line = flat // nz
    iy = line % ny
    ix = line // ny
    row = iy - (half - halo) * y
    spot = jnp.where((row >= 0) & (row < rows), ix * rows + row, -1)
    dets_n = flat.shape[1]
    at_z = (index_along((nz, dets_n), 0) == iz).astype(jnp.float32).astype(jnp.bfloat16)

    def body(i, carry):
        here = index_along((2 * rows, dets_n), 0) + i * (2 * rows)
        hot = (here == spot).astype(jnp.float32).astype(jnp.bfloat16)
        found = lax.dot_general(hot, at_z, (((1,), (1,)), ((), ())), preferred_element_type=jnp.float32)
        count[pl.ds(2 * i, 2)] = found.reshape(2, rows, nz)
        return carry

    lax.fori_loop(0, planes // 2, body, 0)


def photon_kernel(bg, labels, msg, labels_came, mine, fields, raw, sems):
    _, x, _, c = places(2)
    half = bg.shape[0] // 2
    cx = labels.shape[0]
    here, there = cx * x, cx * (1 - x)
    copies = [
        pltpu.make_async_copy(src, dst, sems.at[i])
        for i, (src, dst) in enumerate((
            (bg.at[half * x + c], mine.at[pl.ds(here, cx)]),
            (bg.at[half * x + 1 - c], fields.at[0, pl.ds(here, cx)]),
            (labels, raw),
        ))
    ]
    for copy in copies:
        copy.start()
    mine[pl.ds(there, cx)] = msg[pl.ds(cx * c, cx)]
    fields[0, pl.ds(there, cx)] = msg[pl.ds(cx * (1 - c), cx)]
    fields[1, pl.ds(there, cx)] = labels_came[...].astype(jnp.float32)
    for copy in copies:
        copy.wait()
    fields[1, pl.ds(here, cx)] = raw[...].astype(jnp.float32)


def unpacked(blocks, groups, s, store):
    n = len(blocks)
    cy, lanes = blocks[0][0].shape
    slab = lanes // n
    lane = index_along((cy, lanes), 1) // slab
    for f in range(2):
        for q in range(groups):
            values = [block[groups * f + q] for block in blocks]
            for j in range(n):
                plane = jnp.zeros((cy, lanes), jnp.float32)
                for k in range(n):
                    home = s ^ k
                    moved = pltpu.roll(values[k], ((home - j + n) % n) * slab, 1)
                    plane = jnp.where(lane == home, moved, plane)
                store(f, n * q + j, plane)


def join_kernel(*refs):
    joined, size = refs[-1], refs[0].shape[0]
    for i, ref in enumerate(refs[:-1]):
        joined[pl.ds(size * i, size)] = ref[...]


def own_half_kernel(vk, va, joined, half):
    s, _, _, _ = places(2)
    size = half.shape[1]
    groups = joined.shape[0] // 2 // (128 // vk.shape[2] - 1)
    n = size // groups
    own = [packed_planes(ref, q) for ref in (vk, va) for q in range(groups)]
    blocks = [own] + [[joined[2 * groups * k + i] for i in range(2 * groups)] for k in range(n - 1)]

    def store(f, i, plane):
        half[f, i] = plane

    unpacked(blocks, groups, s, store)


def vector_kernel(half, msg, joined, fields):
    s, x, _, _ = places(2)
    cx = half.shape[1]
    fields[:, pl.ds(cx * x, cx)] = half[...]
    n = lax.axis_size("src")
    groups = cx // n
    own = msg.shape[0] - 2 * groups
    blocks = [[msg[own + i] for i in range(2 * groups)]]
    blocks += [[joined[2 * groups * k + i] for i in range(2 * groups)] for k in range(n - 1)]
    there = cx * (1 - x)

    def store(f, i, plane):
        fields[f, there + i] = plane

    unpacked(blocks, groups, s, store)


def edge_shape(planes, lanes):
    return planes // GROUP, GROUP * REACH, lanes


def packed_edges(tiles):
    return jnp.concatenate([tile[:REACH] for tile in tiles], axis=0)


def edge_tile(packed, j, y):
    rows = packed[REACH * j : REACH * (j + 1)]
    tile = jnp.concatenate([rows, jnp.zeros((HALO - REACH, rows.shape[1]), jnp.float32)], axis=0)
    return jnp.where(y == 0, tile, shifted(tile, HALO - REACH, 0))


def near_rows(ref, i, first, y):
    tile = ref[i, pl.ds(first, HALO), :]
    return jnp.where(y == 0, shifted(tile, REACH - HALO, 0), tile)


def edges_of(own, got, edge, y, c):
    first = (own.shape[1] - HALO) * (1 - y)
    for g in range(edge.shape[0]):
        edge[g] = packed_edges([
            jnp.where(c != y, near_rows(own, GROUP * g + j, first, y), near_rows(got, GROUP * g + j, first, y))
            for j in range(GROUP)
        ])


def photon_edge_kernel(mine, fields, got, edge):
    _, _, y, c = places(2)
    edges_of(mine, got.at[0], edge.at[0], y, c)
    edges_of(fields.at[1], got.at[1], edge.at[1], y, c)


def vector_edge_kernel(fields, got, edge):
    _, _, y, c = places(2)
    for f in range(2):
        edges_of(fields.at[f], got.at[f], edge.at[f], y, c)


def solve(b, bufs, diag, fx, fy, fz, unroll):
    planes = b.shape[0]
    _, pairs = chebyshev_scalars()
    for step, (keep, push) in enumerate(pairs):
        src, dst = bufs[step % 2], bufs[(step + 1) % 2]

        def body(i, carry):
            u = src[i + 1]
            coef_y, coef_z = fy[i], fz[i]
            left = b[i] - diag[i] * u
            left = left + fx[i] * src[i] + fx[i + 1] * src[i + 2]
            left = left + coef_y * shifted(u, -1, 0) + shifted(coef_y * u, 1, 0)
            left = left + coef_z * shifted(u, -1, 1) + shifted(coef_z * u, 1, 1)
            change = u if step == 0 else u - dst[i + 1]
            dst[i + 1] = u + keep * change + push * left
            return carry

        lax.fori_loop(0, planes, body, 0, unroll=unroll)
    return bufs[len(pairs) % 2]


def folded(value):
    return jnp.sum(value.reshape(-1, 8, value.shape[1]), axis=0)


def framed_own(ref, shift, own, got, y, c):
    planes, cy, _ = own.shape
    there = pl.ds(shift, planes)
    base = HALO * y
    ref[there, pl.ds(base + cy * c, cy), :] = own[...]
    ref[there, pl.ds(base + cy * (1 - c), cy), :] = got[...]


def framed(ref, shift, own, got, edge, y, c):
    framed_own(ref, shift, own, got, y, c)
    cy = own.shape[1]
    for g in range(edge.shape[0]):
        packed = edge[g]
        for j in range(GROUP):
            ref[shift + GROUP * g + j, pl.ds(2 * cy * (1 - y), HALO), :] = edge_tile(packed, j, y)


def blank_ends(*refs):
    for ref in refs:
        blank = jnp.zeros(ref.shape[1:], jnp.float32)
        ref[0] = blank
        ref[ref.shape[0] - 1] = blank


def owned_rows(shape, base, count):
    at_row = index_along(shape, 0)
    return (at_row >= base) & (at_row < base + count)


def table_rows(kap_table, abs_table, shape):
    lane = index_along(shape, 1)
    kap_row = abs_row = jnp.zeros(shape, jnp.float32)
    for region in range(kap_table.shape[0]):
        kap_row = jnp.where(lane == region, kap_table[region], kap_row)
        abs_row = jnp.where(lane == region, abs_table[region], abs_row)
    return kap_row, abs_row


def stencil_kernel(
    kap_table, abs_table, mine, fields, got, count,
    kap, diag, fx, fy, fz, sums,
    labels,
):
    _, _, y, c = places(2)
    planes, cy, lanes = mine.shape
    rows = 2 * cy + HALO
    base = HALO * y
    framed_own(labels, 0, fields.at[1], got.at[1], y, c)
    labels[:, pl.ds(2 * cy * (1 - y), HALO), :] = jnp.zeros((planes, HALO, lanes), jnp.float32)
    blank_ends(kap)
    shape = (rows, lanes)
    lane = index_along(shape, 1)
    kap_row, abs_row = table_rows(kap_table, abs_table, shape)
    owned = owned_rows(shape, base, 2 * cy)

    def look_up(i, carry):
        at = labels[i].astype(jnp.int32)
        kap[i + 1] = jnp.where(owned, jnp.take_along_axis(kap_row, at, axis=1), 0.0)
        diag[i] = jnp.take_along_axis(abs_row, at, axis=1)
        return carry

    lax.fori_loop(0, planes, look_up, 0, unroll=4)
    fx[0] = 0.5 * kap[1]

    def set_up(i, carry):
        k = kap[i + 1]
        along_x = 0.5 * (k + kap[i + 2])
        along_y, along_z = 0.5 * (k + beyond(k, 1, 0)), 0.5 * (k + beyond(k, 1, 1))
        fx[i + 1] = along_x
        fy[i] = jnp.where(index_along(shape, 0) == rows - 1, 0.0, along_y)
        fz[i] = jnp.where(lane == lanes - 1, 0.0, along_z)
        back_y, back_z = 0.5 * (k + beyond(k, -1, 0)), 0.5 * (k + beyond(k, -1, 1))
        diag[i] = diag[i] + fx[i] + along_x + along_y + back_y + along_z + back_z
        total, square = carry
        for p, at in ((mine[i], c), (got[0, i], 1 - c)):
            part = count[i, pl.ds(base + cy * at, cy), :] * p
            total, square = total + folded(part), square + folded(part * p)
        return total, square

    zero = jnp.zeros((8, lanes), jnp.float32)
    sums[0], sums[1] = lax.fori_loop(0, planes, set_up, (zero, zero), unroll=4)


def halo_kernel(kap_table, abs_table, edge, kap, diag_in, fx_in, fy_in, fz_in, diag, fx, fy, fz):
    _, _, y, _ = places(2)
    planes, rows, lanes = diag.shape
    for ref, old in ((diag, diag_in), (fx, fx_in), (fy, fy_in), (fz, fz_in)):
        ref[...] = old[...]
    shape = (HALO, lanes)
    lane, row = index_along(shape, 1), index_along(shape, 0)
    kap_row, abs_row = table_rows(kap_table, abs_table, shape)
    low = y == 0
    here = pl.ds((rows - HALO) * (1 - y), HALO)
    beside_it = pl.ds((rows - 2 * HALO) * (1 - y) + HALO * y, HALO)
    labels = [edge_tile(edge[1, i // GROUP], i % GROUP, y).astype(jnp.int32) for i in range(planes)]
    tiles = [jnp.take_along_axis(kap_row, at, axis=1) for at in labels]
    none = jnp.zeros(shape, jnp.float32)
    before = 0.5 * tiles[0]
    fx[0, here, :] = before
    for i, k in enumerate(tiles):
        after = 0.5 * (k + (tiles[i + 1] if i + 1 < planes else none))
        own = kap[i + 1, beside_it, :]
        up, down = shifted(k, -1, 0), shifted(k, 1, 0)
        k_up = jnp.where(row == HALO - 1, jnp.where(low, 0.0, shifted(own, -1, 0)), up)
        k_down = jnp.where(row == 0, jnp.where(low, shifted(own, 1, 0), 0.0), down)
        along_y, back_y = 0.5 * (k + k_up), 0.5 * (k + k_down)
        along_z, back_z = 0.5 * (k + beyond(k, 1, 1)), 0.5 * (k + beyond(k, -1, 1))
        fx[i + 1, here, :] = after
        fy[i, here, :] = jnp.where(low & (row == HALO - 1), 0.0, along_y)
        fz[i, here, :] = jnp.where(lane == lanes - 1, 0.0, along_z)
        absorb = jnp.take_along_axis(abs_row, labels[i], axis=1)
        diag[i, here, :] = absorb + before + after + along_y + back_y + along_z + back_z
        before = after
        face_up = jnp.where(low & (row == HALO - 1), 0.5 * up, 0.0)
        face_down = jnp.where(low | (row > 0), 0.0, 0.5 * down)
        fy[i, beside_it, :] = fy_in[i, beside_it, :] + face_up
        diag[i, beside_it, :] = diag_in[i, beside_it, :] + face_up + face_down


def density_kernel(mine, got, edge, phi, phi_y, phi_z):
    _, _, y, c = places(2)
    framed(phi, 1, mine, got.at[0], edge.at[0], y, c)
    blank_ends(phi)

    def differ(i, carry):
        p = phi[i + 1]
        phi_y[i], phi_z[i] = p - beyond(p, 1, 0), p - beyond(p, 1, 1)
        return carry

    lax.fori_loop(0, phi_y.shape[0], differ, 0, unroll=4)


def first_kernel(
    phi, phi_y, phi_z, diag, fx, fy, fz, count, sums, vector, got_vector, edge,
    change, message,
    vk, va, b, buf_a, buf_b,
):
    _, _, y, c = places(2)
    planes, rows, lanes = change.shape
    cy = vector.shape[2]
    framed(vk, 1, vector.at[0], got_vector.at[0], edge.at[0], y, c)
    framed(va, 0, vector.at[1], got_vector.at[1], edge.at[1], y, c)
    blank_ends(vk, buf_a, buf_b)
    theta, _ = chebyshev_scalars()

    def set_up(i, carry):
        v, p = vk[i + 1], phi[i + 1]
        total = 0.5 * (v + vk[i]) * (p - phi[i]) + 0.5 * (v + vk[i + 2]) * (p - phi[i + 2])
        for axis, step in enumerate((phi_y, phi_z)):
            flow = 0.5 * (v + beyond(v, 1, axis)) * step[i]
            first = index_along(v.shape, axis) == 0
            total = total + flow + jnp.where(first, 0.5 * v * p, -shifted(flow, 1, axis))
        total = -(va[i] * p + total)
        b[i] = total
        buf_a[i + 1] = total * (1.0 / theta)
        return carry

    lax.fori_loop(0, planes, set_up, 0, unroll=8)
    found = solve(b, (buf_a, buf_b), diag, fx, fy, fz, UNROLL)
    owned = owned_rows((rows, lanes), HALO * y, 2 * cy)

    def add_up(i, carry):
        u = found[i + 1]
        change[i] = u
        part = jnp.where(owned, count[i], 0.0) * u
        return carry[0] + folded(part), carry[1] + folded(part * phi[i + 1])

    zero = jnp.zeros((8, lanes), jnp.float32)
    seen, cross = lax.fori_loop(0, planes, add_up, (zero, zero), unroll=8)
    first = (2 * cy - HALO) * (1 - y) + HALO * y
    size = GROUP * REACH
    for g in range(planes // GROUP):
        message[pl.ds(size * g, size), :] = packed_edges(
            [near_rows(found, 1 + GROUP * g + j, first, y) for j in range(GROUP)]
        )
    rows_of_sums = [jnp.sum(part, axis=0, keepdims=True) for part in (sums[0], seen, cross, sums[1])]
    message[pl.ds(REACH * planes, 8), :] = jnp.concatenate([*rows_of_sums, zero[:4]], axis=0)


def second_kernel(
    phi, phi_y, phi_z, change, diag, fx, fy, fz, count, sent, came,
    own, message,
    b, buf_a, buf_b, grad_k, grad_a,
    *, dets,
):
    _, _, y, c = places(2)
    planes, rows, lanes = change.shape
    cy = (rows - HALO) // 2
    base = HALO * y
    edge = pl.ds(2 * cy * (1 - y), HALO)
    tail = pl.ds(REACH * planes, 8)
    sums = jnp.sum(sent[tail, :] + came[tail, :], axis=1, keepdims=True)
    total, seen_sum, cross, square = (sums[g : g + 1] for g in range(4))
    mean = total / dets
    part = seen_sum / total
    level = (cross - part * square) / (total * mean)
    inverse = 1.0 / mean
    blank_ends(buf_a, buf_b)
    theta, _ = chebyshev_scalars()

    def weighted(n, u, p):
        return n * (((u - p * part) * inverse - level) * inverse)

    def set_up(i, carry):
        value = weighted(count[i], change[i], phi[i + 1])
        b[i] = value
        buf_a[i + 1] = value * (1.0 / theta)
        return carry

    lax.fori_loop(0, planes, set_up, 0, unroll=8)
    size = GROUP * REACH
    for i in range(planes):
        u = edge_tile(came[pl.ds(size * (i // GROUP), size), :], i % GROUP, y)
        value = weighted(count[i, edge, :], u, phi[i + 1, edge, :])
        b[i, edge, :] = value
        buf_a[i + 1, edge, :] = value * (1.0 / theta)
    dual = solve(b, (buf_a, buf_b), diag, fx, fy, fz, UNROLL)

    def product(i, carry):
        p, u = phi[i + 1], dual[i + 1]
        grad = (p - phi[i]) * (u - dual[i]) + (p - phi[i + 2]) * (u - dual[i + 2])
        both = p * u
        for axis, step in enumerate((phi_y, phi_z)):
            flow = step[i] * (u - beyond(u, 1, axis))
            first = index_along(p.shape, axis) == 0
            grad = grad + flow + jnp.where(first, both, shifted(flow, 1, axis))
        grad_k[i] = -0.5 * grad
        grad_a[i] = -both
        for f, ref in enumerate((grad_k, grad_a)):
            own[f, i] = ref[i, pl.ds(base + cy * c, cy), :]
            message[f, i] = ref[i, pl.ds(base + cy * (1 - c), cy), :]
        return carry

    lax.fori_loop(0, planes, product, 0, unroll=8)


def packed_slabs(own, came, half, choices, outs):
    s, _, _, _ = places(2)
    _, planes, cy, lanes = own.shape
    n = planes // 2 // outs.shape[2]
    slab = lanes // n
    lane = index_along((cy, lanes), 1) // slab
    for f in range(2):
        for q in range(outs.shape[2]):
            at = planes // 2 * half + n * q
            parts = [own[f, at + j] + came[f, at + j] for j in range(n)]
            for i, k in enumerate(choices):
                to = s ^ k
                piece = jnp.zeros((cy, lanes), jnp.float32)
                for j in range(n):
                    moved = pltpu.roll(parts[j], ((j - to + n) % n) * slab, 1)
                    piece = jnp.where(lane == j, moved, piece)
                outs[i, f, q] = piece


def send_kernel(own, came, out, *, k):
    _, x, _, _ = places(2)
    packed_slabs(own, came, 1 - x, (k,), out)


def keep_kernel(own, came, kept):
    _, x, _, _ = places(2)
    packed_slabs(own, came, x, range(kept.shape[0]), kept)


def add_kernel(kept, came, out, *, k):
    out[...] = kept[k] + came[0]


def sum_kernel(*refs):
    total = refs[0][...]
    for ref in refs[1:-1]:
        total = total + ref[...]
    refs[-1][...] = total


def project_kernel(*refs, parts_n, n):
    beta_prev = refs[0]
    parts = refs[1 : 1 + parts_n]
    vk, va, qk, qa, w_k, w_a, tile = refs[1 + parts_n :]
    slab = 128 // n
    for f, (q_ref, w) in enumerate(((qk, w_k), (qa, w_a))):
        for q in range(vk.shape[0] // n):
            whole = sum(part[f, q] for part in parts[1:]) + parts[0][f, q]
            for j in range(n):
                i = n * q + j
                w[i] = whole[:, slab * j : slab * (j + 1)] - beta_prev[:, : vk.shape[2]] * q_ref[i]

    def total(value):
        return jnp.sum(jnp.sum(jnp.sum(value, axis=0), axis=0, keepdims=True), axis=1, keepdims=True)

    wk, wa, v_k, v_a = w_k[...], w_a[...], vk[...], va[...]
    wv = total(wk * v_k + wa * v_a)
    vv = total(v_k * v_k + v_a * v_a)
    a = jnp.where(vv > 0.0, wv / jnp.where(vv > 0.0, vv, 1.0), 0.0)
    u_k, u_a = wk - a * v_k, wa - a * v_a
    uv = total(u_k * v_k + u_a * v_a)
    uu = total(u_k * u_k + u_a * u_a)
    lane = index_along((1, 128), 1)
    values = jnp.zeros((1, 128), jnp.float32)
    for i, value in enumerate((wv, vv, a, uv, uu)):
        values = jnp.where(lane == i, value, values)
    tile[...] = values


def final_kernel(tiles, w_k, w_a, vk, va, next_k, next_a, coefs, *, cells):
    tile = jnp.concatenate([tiles[i] for i in range(tiles.shape[0])], axis=0)
    wv, vv, a, uv, uu = (tile[:, i : i + 1] for i in range(5))
    wv_sum = jnp.sum(wv, axis=0, keepdims=True)
    vv_sum = jnp.sum(vv, axis=0, keepdims=True)
    alpha = wv_sum / cells / (vv_sum / cells + eps_norm)
    off = alpha - a
    rr = jnp.sum(uu - 2.0 * off * uv + off * (off * vv), axis=0, keepdims=True)
    beta = jnp.sqrt(rr / cells + eps_norm)
    next_k[...] = (w_k[...] - alpha * vk[...]) / beta
    next_a[...] = (w_a[...] - alpha * va[...]) / beta
    coefs[0] = jnp.sum(alpha)
    coefs[1] = jnp.sum(beta)


def f32(*shape):
    return jax.ShapeDtypeStruct(shape, jnp.float32)


def run(kernel, outs, *args, after=(), scratch=(), copies=0, smem=(), hbm=(), mib=16, in_smem_out=(), cost=None):
    vmem = pl.BlockSpec(memory_space=pltpu.VMEM)
    scalar = pl.BlockSpec(memory_space=pltpu.SMEM)
    far = pl.BlockSpec(memory_space=pltpu.HBM)
    held = [pltpu.VMEM(shape, dtype) for shape, dtype in scratch]
    used, waits = len(args), len(after)

    def body(*refs):
        kernel(*refs[:used], *refs[used + waits :])

    args = (*args, *after)
    if copies:
        held.append(pltpu.SemaphoreType.DMA((copies,)))
    return pl.pallas_call(
        body if waits else kernel,
        out_shape=tuple(outs),
        in_specs=[scalar if i in smem else far if i in hbm else vmem for i in range(len(args))],
        out_specs=tuple(scalar if i in in_smem_out else vmem for i in range(len(outs))),
        scratch_shapes=held,
        compiler_params=pltpu.CompilerParams(vmem_limit_bytes=mib * 2**20),
        cost_estimate=cost,
    )(*args)


HALO = 8
UNROLL = 16
REACH = 6
GROUP = 4


def per_device_paired(
    labels, kappa_table, absorb_table, background, det_cells,
    v_kappa, v_absorb, q_kappa, q_absorb, beta_prev,
):
    sources, cx, cy, cz = background.shape
    n = lax.axis_size("src")
    planes, rows = 2 * cx, 2 * cy + HALO
    ny = cy * lax.axis_size("gy")
    dets = det_cells.shape[0]
    cells = planes * ny * cz
    groups = cx // n

    def swap_x(value):
        return lax.ppermute(value, "gx", [(0, 1), (1, 0)])

    def swap_core(value):
        return lax.ppermute(value, "gy", [(0, 1), (1, 0), (2, 3), (3, 2)])

    def along_z(value, k):
        return lax.ppermute(value, "src", [(i, i ^ k) for i in range(n)])

    block = (cx, cy, cz)
    float_block = lambda *shape: (shape, jnp.float32)
    raw_labels = (block, jnp.int32)
    packed, message = run(
        pack_kernel, (f32(2 * groups, cy, cz), f32(sources // 2 * cx + 2 * groups, cy, cz)),
        background, v_kappa, v_absorb, hbm=(0, 1, 2),
        scratch=(float_block(2, *v_kappa.shape),), copies=2 + sources // 2, mib=60,
    )
    long = pl.CostEstimate(flops=10**9, bytes_accessed=2**26, transcendentals=0)
    labels_came = swap_x(labels)
    came = swap_x(message)
    slabs = [along_z(packed, k) for k in range(1, n)]
    count, beta_row = run(
        functools.partial(count_kernel, ny=ny, nz=cz, half=2 * cy, halo=HALO),
        (f32(planes, rows, cz), f32(1, cz)), det_cells.reshape(1, dets), beta_prev, smem=(1,), after=(labels_came,),
        cost=pl.CostEstimate(flops=2 * planes * rows * cz * dets, bytes_accessed=planes * rows * cz * 4, transcendentals=0),
    )

    def across_y(value):
        return lax.ppermute(value, "gy", [(i, (i + 2) % 4) for i in range(4)])

    (joined,) = run(join_kernel, (f32(2 * groups * (n - 1), cy, cz),), *slabs, after=(count,))
    joined_came = swap_x(joined)
    (half_vector,) = run(own_half_kernel, (f32(2, *block),), v_kappa, v_absorb, joined)
    mine, fields = run(
        photon_kernel, (f32(planes, cy, cz), f32(2, planes, cy, cz)),
        background, labels, came, labels_came, after=(joined,), hbm=(0, 1), scratch=(raw_labels,), copies=3,
    )
    got = swap_core(fields)
    (vector,) = run(
        vector_kernel, (f32(2, planes, cy, cz),), half_vector, came, joined_came, after=(mine,)
    )
    edge = (f32(2, *edge_shape(planes, cz)),)
    (sent,) = run(photon_edge_kernel, edge, mine, fields, got, after=(vector,))
    photon_edge = across_y(sent)
    vector_got = swap_core(vector)
    (vector_sent,) = run(vector_edge_kernel, edge, vector, vector_got, after=(sent,))
    frame, wide = (planes, rows, cz), (planes + 2, rows, cz)
    float_frame, float_wide = float_block(*frame), float_block(*wide)
    coefs = (f32(*frame), f32(planes + 1, rows, cz), f32(*frame), f32(*frame))
    kap, *partial, sums = run(
        stencil_kernel, (f32(*wide), *coefs, f32(2, 8, cz)),
        kappa_table, absorb_table, mine, fields, got, count, after=(vector_sent,), cost=long,
        smem=(0, 1), scratch=(float_frame,),
    )
    diag, fx, fy, fz = run(
        halo_kernel, coefs, kappa_table, absorb_table, photon_edge, kap, *partial, smem=(0, 1)
    )
    densities = run(
        density_kernel, (f32(*wide), f32(*frame), f32(*frame)), mine, got, photon_edge, after=(fz,)
    )
    change, sent = run(
        first_kernel, (f32(*frame), f32(REACH * planes + 8, cz)),
        *densities, diag, fx, fy, fz, count, sums, vector, vector_got, across_y(vector_sent),
        scratch=(float_wide, float_frame, float_frame, float_wide, float_wide),
    )
    heard = across_y(sent)
    own, message = run(
        functools.partial(second_kernel, dets=dets),
        (f32(2, planes, cy, cz), f32(2, planes, cy, cz)),
        *densities, change, diag, fx, fy, fz, count, sent, heard,
        scratch=(float_frame, float_wide, float_wide, float_frame, float_frame),
    )
    piece = f32(2, groups, cy, cz)
    got = swap_core(message)
    crossed, last = {}, ()
    for k in reversed(range(n)):
        last = run(functools.partial(send_kernel, k=k), (f32(1, *piece.shape),), own, got, after=last)
        crossed[k] = swap_x(last[0])
    (kept,) = run(keep_kernel, (f32(n, *piece.shape),), own, got, after=last)
    totals = {
        k: run(functools.partial(add_kernel, k=k), (piece,), kept, value)[0] for k, value in crossed.items()
    }
    received = {k: along_z(totals[k], k) for k in reversed(range(1, n))}
    (distant,) = run(sum_kernel, (piece,), *(received[k] for k in range(n // 2, n)), cost=long)
    parts = [distant, totals[0]] + [received[k] for k in range(1, n // 2)]
    w_k, w_a, tile = run(
        functools.partial(project_kernel, parts_n=len(parts), n=n),
        (f32(*v_kappa.shape), f32(*v_kappa.shape), f32(1, 128)),
        beta_row, *parts, v_kappa, v_absorb, q_kappa, q_absorb,
    )
    everyone = ("src", "gx", "gy")
    tiles = lax.all_to_all(jnp.broadcast_to(tile, (8 * n, 1, 128)), everyone, 0, 0)
    return tuple(run(
        functools.partial(final_kernel, cells=cells),
        (f32(*v_kappa.shape), f32(*v_kappa.shape), f32(2)),
        tiles, w_k, w_a, v_kappa, v_absorb, in_smem_out=(2,),
    ))


def paired_fits(mesh):
    return mesh.shape["gx"] == 2 and mesh.shape["gy"] == 4


def body_for(mesh):
    if not paired_fits(mesh):
        return per_device

    def chosen(*args):
        sources, cx, cy, cz = args[3].shape
        n = lax.axis_size("src")
        fits = sources == 4 and cz == 128 and cx % n == 0 and cx % GROUP == 0 and cy % HALO == 0 and n > 1 and n & (n - 1) == 0
        devices = 8 * n
        return (per_device_paired if fits and devices <= 128 else per_device)(*args)

    return chosen


def solution(mesh):
    return jax.shard_map(
        body_for(mesh),
        mesh=mesh,
        in_specs=(
            P("gx", "gy", None),
            P(),
            P(),
            P("src", "gx", "gy", None),
            P(),
            P("gx", "gy", "src"),
            P("gx", "gy", "src"),
            P("gx", "gy", "src"),
            P("gx", "gy", "src"),
            P(),
        ),
        out_specs=(P("gx", "gy", "src"), P("gx", "gy", "src"), P()),
        check_vma=False,
    )
```

```python
import functools

import jax
import jax.numpy as jnp
from jax import lax
from jax.experimental import pallas as pl
from jax.experimental.pallas import tpu as pltpu
from jax.sharding import PartitionSpec as P

ITERS = 6


lam_low = 0.02
lam_high = 24.1
eps_norm = 1e-06


def padded_2(block, sides, width):
    for axis, dim in sides:
        count = lax.axis_size(axis)
        forward = [(i, i + 1) for i in range(count - 1)]
        backward = [(target, source) for source, target in forward]
        low = lax.ppermute(
            lax.slice_in_dim(block, block.shape[dim] - width, None, axis=dim), axis, forward
        )
        high = lax.ppermute(lax.slice_in_dim(block, 0, width, axis=dim), axis, backward)
        block = jnp.concatenate([low, block, high], axis=dim)
    return block


def regional(labels, table):
    field = jnp.zeros(labels.shape, jnp.float32)
    for region in range(table.shape[0]):
        field = field + jnp.where(labels == region, table[region], 0.0)
    return field


def beside(padded):
    widths = [(0, 0)] * (padded.ndim - 1) + [(1, 1)]
    full = jnp.pad(padded, widths)
    return [
        full[..., 2:, 1:-1, 1:-1],
        full[..., :-2, 1:-1, 1:-1],
        full[..., 1:-1, 2:, 1:-1],
        full[..., 1:-1, :-2, 1:-1],
        full[..., 1:-1, 1:-1, 2:],
        full[..., 1:-1, 1:-1, :-2],
    ]


def chebyshev(rhs, apply_op):
    theta = 0.5 * (lam_high + lam_low)
    delta = 0.5 * (lam_high - lam_low)
    sigma = theta / delta
    rho = 1.0 / sigma
    solution = jnp.zeros_like(rhs)
    remain = rhs
    step_dir = rhs / theta
    for step in range(ITERS):
        solution = solution + step_dir
        if step + 1 < ITERS:
            remain = remain - apply_op(step_dir)
            rho_next = 1.0 / (2.0 * sigma - rho)
            step_dir = rho_next * rho * step_dir + 2.0 * rho_next / delta * remain
            rho = rho_next
    return solution


def per_device(
    labels,
    kappa_table,
    absorb_table,
    background,
    det_cells,
    v_kappa,
    v_absorb,
    q_kappa,
    q_absorb,
    beta_prev,
):
    sources, cx, cy, cz = background.shape
    kappa = regional(labels, kappa_table)
    absorb = regional(labels, absorb_table)
    full_k, full_a = (
        lax.all_gather(v_kappa, "src", axis=2, tiled=True),
        lax.all_gather(v_absorb, "src", axis=2, tiled=True),
    )
    stacked = jnp.concatenate([background, kappa[None], full_k[None]], axis=0)
    rims = padded_2(stacked, (("gx", 1), ("gy", 2)), 1)
    near_all = beside(rims)
    kappa_faces = [0.5 * (kappa + near[sources]) for near in near_all]
    vk_faces = [0.5 * (full_k + near[sources + 1]) for near in near_all]
    phi_near = [near[:sources] for near in near_all]

    def apply_op(field):
        padded = padded_2(field, (("gx", 1), ("gy", 2)), 1)
        result = absorb * field
        for face, near in zip(kappa_faces, beside(padded)):
            result = result + face * (field - near)
        return result

    rhs = full_a * background
    for face, near in zip(vk_faces, phi_near):
        rhs = rhs + face * (background - near)
    rhs = -rhs
    change = chebyshev(rhs, apply_op)
    span_y = cy * lax.axis_size("gy")
    ix = det_cells // (span_y * cz)
    iy = det_cells // cz % span_y
    iz = det_cells % cz
    anchor_x = lax.axis_index("gx") * cx
    anchor_y = lax.axis_index("gy") * cy
    owned = (ix >= anchor_x) & (ix < anchor_x + cx) & (iy >= anchor_y) & (iy < anchor_y + cy)
    local = jnp.where(owned, ((ix - anchor_x) * cy + (iy - anchor_y)) * cz + iz, 0)
    seen_part = jnp.where(owned[None, :], change.reshape(sources, -1)[:, local], 0.0)
    base_part = jnp.where(owned[None, :], background.reshape(sources, -1)[:, local], 0.0)
    seen, base = lax.psum((seen_part, base_part), ("gx", "gy"))
    total = jnp.sum(base, axis=1, keepdims=True)
    mean_base = total / det_cells.shape[0]
    ratio = base / total
    jv_vals = (seen - ratio * jnp.sum(seen, axis=1, keepdims=True)) / mean_base
    weight = (jv_vals - jnp.sum(ratio * jv_vals, axis=1, keepdims=True)) / mean_base
    deposit = jnp.where(owned[None, :], weight, 0.0)
    source = (
        jnp.zeros((sources, cx * cy * cz), jnp.float32)
        .at[:, local]
        .add(deposit)
        .reshape(change.shape)
    )
    dual = chebyshev(source, apply_op)
    dual_rims = padded_2(dual, (("gx", 1), ("gy", 2)), 1)
    grad_a = -jnp.sum(background * dual, axis=0)
    grad_k = jnp.zeros_like(kappa)
    for near_phi, near_dual in zip(phi_near, beside(dual_rims)):
        grad_k = grad_k - 0.5 * jnp.sum((background - near_phi) * (dual - near_dual), axis=0)
    summed_k, summed_a = lax.psum((grad_k, grad_a), "src")
    slab = v_kappa.shape[2]
    offset = lax.axis_index("src") * slab
    hv_k = lax.dynamic_slice_in_dim(summed_k, offset, slab, 2)
    hv_a = lax.dynamic_slice_in_dim(summed_a, offset, slab, 2)
    cell_count = cx * lax.axis_size("gx") * cy * lax.axis_size("gy") * cz
    w_k = hv_k - beta_prev[0] * q_kappa
    w_a = hv_a - beta_prev[0] * q_absorb
    local_wv = jnp.sum(w_k * v_kappa) + jnp.sum(w_a * v_absorb)
    local_vv = jnp.sum(v_kappa * v_kappa) + jnp.sum(v_absorb * v_absorb)
    wv_sum, vv_sum = lax.psum((local_wv, local_vv), ("src", "gx", "gy"))
    alpha = wv_sum / cell_count / (vv_sum / cell_count + eps_norm)
    r_k = w_k - alpha * v_kappa
    r_a = w_a - alpha * v_absorb
    rr_sum = lax.psum(jnp.sum(r_k * r_k) + jnp.sum(r_a * r_a), ("src", "gx", "gy"))
    beta = jnp.sqrt(rr_sum / cell_count + eps_norm)
    return (r_k / beta, r_a / beta, jnp.stack([alpha, beta]))


def chebyshev_scalars():
    theta = 0.5 * (lam_high + lam_low)
    delta = 0.5 * (lam_high - lam_low)
    sigma = theta / delta
    rho = 1.0 / sigma
    pairs = []
    for _ in range(ITERS - 1):
        rho_next = 1.0 / (2.0 * sigma - rho)
        pairs.append((rho_next * rho, 2.0 * rho_next / delta))
        rho = rho_next
    return theta, pairs


def places(split):
    g = lax.axis_index("gy")
    return lax.axis_index("src"), lax.axis_index("gx"), g // split, g % split


def shifted(value, step, axis):
    return pltpu.roll(value, step % value.shape[axis], axis)


def index_along(shape, axis):
    return lax.broadcasted_iota(jnp.int32, shape, axis)


def beyond(value, step, axis):
    size = value.shape[axis]
    at = index_along(value.shape, axis)
    edge = size - 1 if step == 1 else 0
    return jnp.where(at == edge, 0.0, shifted(value, -step, axis))


def packed_planes(ref, q):
    per = 128 // ref.shape[2]
    return jnp.concatenate([ref[per * q + j] for j in range(per)], axis=1)


def pack_kernel(bg, vk, va, packed, message, v_in, sems):
    _, x, _, _ = places(2)
    half = bg.shape[0] // 2
    cx = bg.shape[1]
    copies = [
        pltpu.make_async_copy(src, dst, sems.at[i])
        for i, (src, dst) in enumerate((
            (vk, v_in.at[0]),
            (va, v_in.at[1]),
            *((bg.at[half * (1 - x) + i], message.at[pl.ds(cx * i, cx)]) for i in range(half)),
        ))
    ]
    for copy in copies:
        copy.start()
    groups = packed.shape[0] // 2
    for f in range(2):
        copies[f].wait()
        for q in range(groups):
            planes = packed_planes(v_in.at[f], q)
            packed[groups * f + q] = planes
            message[cx * half + groups * f + q] = planes
    for copy in copies[2:]:
        copy.wait()


def count_kernel(dets, beta_prev, count, beta_row, *, ny, nz, half, halo):
    beta_row[...] = jnp.full(beta_row.shape, beta_prev[0])
    _, _, y, _ = places(2)
    planes, rows, _ = count.shape
    flat = dets[...]
    iz = flat % nz
    line = flat // nz
    iy = line % ny
    ix = line // ny
    row = iy - (half - halo) * y
    spot = jnp.where((row >= 0) & (row < rows), ix * rows + row, -1)
    dets_n = flat.shape[1]
    at_z = (index_along((nz, dets_n), 0) == iz).astype(jnp.float32).astype(jnp.bfloat16)

    def body(i, carry):
        here = index_along((2 * rows, dets_n), 0) + i * (2 * rows)
        hot = (here == spot).astype(jnp.float32).astype(jnp.bfloat16)
        found = lax.dot_general(hot, at_z, (((1,), (1,)), ((), ())), preferred_element_type=jnp.float32)
        count[pl.ds(2 * i, 2)] = found.reshape(2, rows, nz)
        return carry

    lax.fori_loop(0, planes // 2, body, 0)


def photon_kernel(bg, labels, msg, labels_came, mine, fields, raw, sems):
    _, x, _, c = places(2)
    half = bg.shape[0] // 2
    cx = labels.shape[0]
    here, there = cx * x, cx * (1 - x)
    copies = [
        pltpu.make_async_copy(src, dst, sems.at[i])
        for i, (src, dst) in enumerate((
            (bg.at[half * x + c], mine.at[pl.ds(here, cx)]),
            (bg.at[half * x + 1 - c], fields.at[0, pl.ds(here, cx)]),
            (labels, raw),
        ))
    ]
    for copy in copies:
        copy.start()
    mine[pl.ds(there, cx)] = msg[pl.ds(cx * c, cx)]
    fields[0, pl.ds(there, cx)] = msg[pl.ds(cx * (1 - c), cx)]
    fields[1, pl.ds(there, cx)] = labels_came[...].astype(jnp.float32)
    for copy in copies:
        copy.wait()
    fields[1, pl.ds(here, cx)] = raw[...].astype(jnp.float32)


def unpacked(blocks, groups, s, store):
    n = len(blocks)
    cy, lanes = blocks[0][0].shape
    slab = lanes // n
    lane = index_along((cy, lanes), 1) // slab
    for f in range(2):
        for q in range(groups):
            values = [block[groups * f + q] for block in blocks]
            for j in range(n):
                plane = jnp.zeros((cy, lanes), jnp.float32)
                for k in range(n):
                    home = s ^ k
                    moved = pltpu.roll(values[k], ((home - j + n) % n) * slab, 1)
                    plane = jnp.where(lane == home, moved, plane)
                store(f, n * q + j, plane)


def join_kernel(*refs):
    joined, size = refs[-1], refs[0].shape[0]
    for i, ref in enumerate(refs[:-1]):
        joined[pl.ds(size * i, size)] = ref[...]


def own_half_kernel(vk, va, joined, half):
    s, _, _, _ = places(2)
    size = half.shape[1]
    groups = joined.shape[0] // 2 // (128 // vk.shape[2] - 1)
    n = size // groups
    own = [packed_planes(ref, q) for ref in (vk, va) for q in range(groups)]
    blocks = [own] + [[joined[2 * groups * k + i] for i in range(2 * groups)] for k in range(n - 1)]

    def store(f, i, plane):
        half[f, i] = plane

    unpacked(blocks, groups, s, store)


def vector_kernel(half, msg, joined, fields):
    s, x, _, _ = places(2)
    cx = half.shape[1]
    fields[:, pl.ds(cx * x, cx)] = half[...]
    n = lax.axis_size("src")
    groups = cx // n
    own = msg.shape[0] - 2 * groups
    blocks = [[msg[own + i] for i in range(2 * groups)]]
    blocks += [[joined[2 * groups * k + i] for i in range(2 * groups)] for k in range(n - 1)]
    there = cx * (1 - x)

    def store(f, i, plane):
        fields[f, there + i] = plane

    unpacked(blocks, groups, s, store)


def edge_shape(planes, lanes):
    return planes // GROUP, GROUP * REACH, lanes


def packed_edges(tiles):
    return jnp.concatenate([tile[:REACH] for tile in tiles], axis=0)


def edge_tile(packed, j, y):
    rows = packed[REACH * j : REACH * (j + 1)]
    tile = jnp.concatenate([rows, jnp.zeros((HALO - REACH, rows.shape[1]), jnp.float32)], axis=0)
    return jnp.where(y == 0, tile, shifted(tile, HALO - REACH, 0))


def near_rows(ref, i, first, y):
    tile = ref[i, pl.ds(first, HALO), :]
    return jnp.where(y == 0, shifted(tile, REACH - HALO, 0), tile)


def edges_of(own, got, edge, y, c):
    first = (own.shape[1] - HALO) * (1 - y)
    for g in range(edge.shape[0]):
        edge[g] = packed_edges([
            jnp.where(c != y, near_rows(own, GROUP * g + j, first, y), near_rows(got, GROUP * g + j, first, y))
            for j in range(GROUP)
        ])


def photon_edge_kernel(mine, fields, got, edge):
    _, _, y, c = places(2)
    edges_of(mine, got.at[0], edge.at[0], y, c)
    edges_of(fields.at[1], got.at[1], edge.at[1], y, c)


def vector_edge_kernel(fields, got, edge):
    _, _, y, c = places(2)
    for f in range(2):
        edges_of(fields.at[f], got.at[f], edge.at[f], y, c)


def solve(b, bufs, diag, fx, fy, fz, unroll):
    planes = b.shape[0]
    _, pairs = chebyshev_scalars()
    for step, (keep, push) in enumerate(pairs):
        src, dst = bufs[step % 2], bufs[(step + 1) % 2]

        def body(i, carry):
            u = src[i + 1]
            coef_y, coef_z = fy[i], fz[i]
            left = b[i] - diag[i] * u
            left = left + fx[i] * src[i] + fx[i + 1] * src[i + 2]
            left = left + coef_y * shifted(u, -1, 0) + shifted(coef_y * u, 1, 0)
            left = left + coef_z * shifted(u, -1, 1) + shifted(coef_z * u, 1, 1)
            change = u if step == 0 else u - dst[i + 1]
            dst[i + 1] = u + keep * change + push * left
            return carry

        lax.fori_loop(0, planes, body, 0, unroll=unroll)
    return bufs[len(pairs) % 2]


def folded(value):
    return jnp.sum(value.reshape(-1, 8, value.shape[1]), axis=0)


def framed_own(ref, shift, own, got, y, c):
    planes, cy, _ = own.shape
    there = pl.ds(shift, planes)
    base = HALO * y
    ref[there, pl.ds(base + cy * c, cy), :] = own[...]
    ref[there, pl.ds(base + cy * (1 - c), cy), :] = got[...]


def framed(ref, shift, own, got, edge, y, c):
    framed_own(ref, shift, own, got, y, c)
    cy = own.shape[1]
    for g in range(edge.shape[0]):
        packed = edge[g]
        for j in range(GROUP):
            ref[shift + GROUP * g + j, pl.ds(2 * cy * (1 - y), HALO), :] = edge_tile(packed, j, y)


def blank_ends(*refs):
    for ref in refs:
        blank = jnp.zeros(ref.shape[1:], jnp.float32)
        ref[0] = blank
        ref[ref.shape[0] - 1] = blank


def owned_rows(shape, base, count):
    at_row = index_along(shape, 0)
    return (at_row >= base) & (at_row < base + count)


def table_rows(kap_table, abs_table, shape):
    lane = index_along(shape, 1)
    kap_row = abs_row = jnp.zeros(shape, jnp.float32)
    for region in range(kap_table.shape[0]):
        kap_row = jnp.where(lane == region, kap_table[region], kap_row)
        abs_row = jnp.where(lane == region, abs_table[region], abs_row)
    return kap_row, abs_row


def stencil_kernel(
    kap_table, abs_table, mine, fields, got, count,
    kap, diag, fx, fy, fz, sums,
    labels,
):
    _, _, y, c = places(2)
    planes, cy, lanes = mine.shape
    rows = 2 * cy + HALO
    base = HALO * y
    framed_own(labels, 0, fields.at[1], got.at[1], y, c)
    labels[:, pl.ds(2 * cy * (1 - y), HALO), :] = jnp.zeros((planes, HALO, lanes), jnp.float32)
    blank_ends(kap)
    shape = (rows, lanes)
    lane = index_along(shape, 1)
    kap_row, abs_row = table_rows(kap_table, abs_table, shape)
    owned = owned_rows(shape, base, 2 * cy)

    def look_up(i, carry):
        at = labels[i].astype(jnp.int32)
        kap[i + 1] = jnp.where(owned, jnp.take_along_axis(kap_row, at, axis=1), 0.0)
        diag[i] = jnp.take_along_axis(abs_row, at, axis=1)
        return carry

    lax.fori_loop(0, planes, look_up, 0, unroll=4)
    fx[0] = 0.5 * kap[1]

    def set_up(i, carry):
        k = kap[i + 1]
        along_x = 0.5 * (k + kap[i + 2])
        along_y, along_z = 0.5 * (k + beyond(k, 1, 0)), 0.5 * (k + beyond(k, 1, 1))
        fx[i + 1] = along_x
        fy[i] = jnp.where(index_along(shape, 0) == rows - 1, 0.0, along_y)
        fz[i] = jnp.where(lane == lanes - 1, 0.0, along_z)
        back_y, back_z = 0.5 * (k + beyond(k, -1, 0)), 0.5 * (k + beyond(k, -1, 1))
        diag[i] = diag[i] + fx[i] + along_x + along_y + back_y + along_z + back_z
        total, square = carry
        for p, at in ((mine[i], c), (got[0, i], 1 - c)):
            part = count[i, pl.ds(base + cy * at, cy), :] * p
            total, square = total + folded(part), square + folded(part * p)
        return total, square

    zero = jnp.zeros((8, lanes), jnp.float32)
    sums[0], sums[1] = lax.fori_loop(0, planes, set_up, (zero, zero), unroll=4)


def halo_kernel(kap_table, abs_table, edge, kap, diag_in, fx_in, fy_in, fz_in, diag, fx, fy, fz):
    _, _, y, _ = places(2)
    planes, rows, lanes = diag.shape
    for ref, old in ((diag, diag_in), (fx, fx_in), (fy, fy_in), (fz, fz_in)):
        ref[...] = old[...]
    shape = (HALO, lanes)
    lane, row = index_along(shape, 1), index_along(shape, 0)
    kap_row, abs_row = table_rows(kap_table, abs_table, shape)
    low = y == 0
    here = pl.ds((rows - HALO) * (1 - y), HALO)
    beside_it = pl.ds((rows - 2 * HALO) * (1 - y) + HALO * y, HALO)
    labels = [edge_tile(edge[1, i // GROUP], i % GROUP, y).astype(jnp.int32) for i in range(planes)]
    tiles = [jnp.take_along_axis(kap_row, at, axis=1) for at in labels]
    none = jnp.zeros(shape, jnp.float32)
    before = 0.5 * tiles[0]
    fx[0, here, :] = before
    for i, k in enumerate(tiles):
        after = 0.5 * (k + (tiles[i + 1] if i + 1 < planes else none))
        own = kap[i + 1, beside_it, :]
        up, down = shifted(k, -1, 0), shifted(k, 1, 0)
        k_up = jnp.where(row == HALO - 1, jnp.where(low, 0.0, shifted(own, -1, 0)), up)
        k_down = jnp.where(row == 0, jnp.where(low, shifted(own, 1, 0), 0.0), down)
        along_y, back_y = 0.5 * (k + k_up), 0.5 * (k + k_down)
        along_z, back_z = 0.5 * (k + beyond(k, 1, 1)), 0.5 * (k + beyond(k, -1, 1))
        fx[i + 1, here, :] = after
        fy[i, here, :] = jnp.where(low & (row == HALO - 1), 0.0, along_y)
        fz[i, here, :] = jnp.where(lane == lanes - 1, 0.0, along_z)
        absorb = jnp.take_along_axis(abs_row, labels[i], axis=1)
        diag[i, here, :] = absorb + before + after + along_y + back_y + along_z + back_z
        before = after
        face_up = jnp.where(low & (row == HALO - 1), 0.5 * up, 0.0)
        face_down = jnp.where(low | (row > 0), 0.0, 0.5 * down)
        fy[i, beside_it, :] = fy_in[i, beside_it, :] + face_up
        diag[i, beside_it, :] = diag_in[i, beside_it, :] + face_up + face_down


def density_kernel(mine, got, edge, phi, phi_y, phi_z):
    _, _, y, c = places(2)
    framed(phi, 1, mine, got.at[0], edge.at[0], y, c)
    blank_ends(phi)

    def differ(i, carry):
        p = phi[i + 1]
        phi_y[i], phi_z[i] = p - beyond(p, 1, 0), p - beyond(p, 1, 1)
        return carry

    lax.fori_loop(0, phi_y.shape[0], differ, 0, unroll=4)


def first_kernel(
    phi, phi_y, phi_z, diag, fx, fy, fz, count, sums, vector, got_vector, edge,
    change, message,
    vk, va, b, buf_a, buf_b,
):
    _, _, y, c = places(2)
    planes, rows, lanes = change.shape
    cy = vector.shape[2]
    framed(vk, 1, vector.at[0], got_vector.at[0], edge.at[0], y, c)
    framed(va, 0, vector.at[1], got_vector.at[1], edge.at[1], y, c)
    blank_ends(vk, buf_a, buf_b)
    theta, _ = chebyshev_scalars()

    def set_up(i, carry):
        v, p = vk[i + 1], phi[i + 1]
        total = 0.5 * (v + vk[i]) * (p - phi[i]) + 0.5 * (v + vk[i + 2]) * (p - phi[i + 2])
        for axis, step in enumerate((phi_y, phi_z)):
            flow = 0.5 * (v + beyond(v, 1, axis)) * step[i]
            first = index_along(v.shape, axis) == 0
            total = total + flow + jnp.where(first, 0.5 * v * p, -shifted(flow, 1, axis))
        total = -(va[i] * p + total)
        b[i] = total
        buf_a[i + 1] = total * (1.0 / theta)
        return carry

    lax.fori_loop(0, planes, set_up, 0, unroll=8)
    found = solve(b, (buf_a, buf_b), diag, fx, fy, fz, UNROLL)
    owned = owned_rows((rows, lanes), HALO * y, 2 * cy)

    def add_up(i, carry):
        u = found[i + 1]
        change[i] = u
        part = jnp.where(owned, count[i], 0.0) * u
        return carry[0] + folded(part), carry[1] + folded(part * phi[i + 1])

    zero = jnp.zeros((8, lanes), jnp.float32)
    seen, cross = lax.fori_loop(0, planes, add_up, (zero, zero), unroll=8)
    first = (2 * cy - HALO) * (1 - y) + HALO * y
    size = GROUP * REACH
    for g in range(planes // GROUP):
        message[pl.ds(size * g, size), :] = packed_edges(
            [near_rows(found, 1 + GROUP * g + j, first, y) for j in range(GROUP)]
        )
    rows_of_sums = [jnp.sum(part, axis=0, keepdims=True) for part in (sums[0], seen, cross, sums[1])]
    message[pl.ds(REACH * planes, 8), :] = jnp.concatenate([*rows_of_sums, zero[:4]], axis=0)


def second_kernel(
    phi, phi_y, phi_z, change, diag, fx, fy, fz, count, sent, came,
    own, message,
    b, buf_a, buf_b, grad_k, grad_a,
    *, dets,
):
    _, _, y, c = places(2)
    planes, rows, lanes = change.shape
    cy = (rows - HALO) // 2
    base = HALO * y
    edge = pl.ds(2 * cy * (1 - y), HALO)
    tail = pl.ds(REACH * planes, 8)
    sums = jnp.sum(sent[tail, :] + came[tail, :], axis=1, keepdims=True)
    total, seen_sum, cross, square = (sums[g : g + 1] for g in range(4))
    mean = total / dets
    part = seen_sum / total
    level = (cross - part * square) / (total * mean)
    inverse = 1.0 / mean
    blank_ends(buf_a, buf_b)
    theta, _ = chebyshev_scalars()

    def weighted(n, u, p):
        return n * (((u - p * part) * inverse - level) * inverse)

    def set_up(i, carry):
        value = weighted(count[i], change[i], phi[i + 1])
        b[i] = value
        buf_a[i + 1] = value * (1.0 / theta)
        return carry

    lax.fori_loop(0, planes, set_up, 0, unroll=8)
    size = GROUP * REACH
    for i in range(planes):
        u = edge_tile(came[pl.ds(size * (i // GROUP), size), :], i % GROUP, y)
        value = weighted(count[i, edge, :], u, phi[i + 1, edge, :])
        b[i, edge, :] = value
        buf_a[i + 1, edge, :] = value * (1.0 / theta)
    dual = solve(b, (buf_a, buf_b), diag, fx, fy, fz, UNROLL)

    def product(i, carry):
        p, u = phi[i + 1], dual[i + 1]
        grad = (p - phi[i]) * (u - dual[i]) + (p - phi[i + 2]) * (u - dual[i + 2])
        both = p * u
        for axis, step in enumerate((phi_y, phi_z)):
            flow = step[i] * (u - beyond(u, 1, axis))
            first = index_along(p.shape, axis) == 0
            grad = grad + flow + jnp.where(first, both, shifted(flow, 1, axis))
        grad_k[i] = -0.5 * grad
        grad_a[i] = -both
        for f, ref in enumerate((grad_k, grad_a)):
            own[f, i] = ref[i, pl.ds(base + cy * c, cy), :]
            message[f, i] = ref[i, pl.ds(base + cy * (1 - c), cy), :]
        return carry

    lax.fori_loop(0, planes, product, 0, unroll=8)


def packed_slabs(own, came, half, choices, outs):
    s, _, _, _ = places(2)
    _, planes, cy, lanes = own.shape
    n = planes // 2 // outs.shape[2]
    slab = lanes // n
    lane = index_along((cy, lanes), 1) // slab
    for f in range(2):
        for q in range(outs.shape[2]):
            at = planes // 2 * half + n * q
            parts = [own[f, at + j] + came[f, at + j] for j in range(n)]
            for i, k in enumerate(choices):
                to = s ^ k
                piece = jnp.zeros((cy, lanes), jnp.float32)
                for j in range(n):
                    moved = pltpu.roll(parts[j], ((j - to + n) % n) * slab, 1)
                    piece = jnp.where(lane == j, moved, piece)
                outs[i, f, q] = piece


def send_kernel(own, came, out, *, k):
    _, x, _, _ = places(2)
    packed_slabs(own, came, 1 - x, (k,), out)


def keep_kernel(own, came, kept):
    _, x, _, _ = places(2)
    packed_slabs(own, came, x, range(kept.shape[0]), kept)


def add_kernel(kept, came, out, *, k):
    out[...] = kept[k] + came[0]


def sum_kernel(*refs):
    total = refs[0][...]
    for ref in refs[1:-1]:
        total = total + ref[...]
    refs[-1][...] = total


def project_kernel(*refs, parts_n, n):
    beta_prev = refs[0]
    parts = refs[1 : 1 + parts_n]
    vk, va, qk, qa, w_k, w_a, tile = refs[1 + parts_n :]
    slab = 128 // n
    for f, (q_ref, w) in enumerate(((qk, w_k), (qa, w_a))):
        for q in range(vk.shape[0] // n):
            whole = sum(part[f, q] for part in parts[1:]) + parts[0][f, q]
            for j in range(n):
                i = n * q + j
                w[i] = whole[:, slab * j : slab * (j + 1)] - beta_prev[:, : vk.shape[2]] * q_ref[i]

    def total(value):
        return jnp.sum(jnp.sum(jnp.sum(value, axis=0), axis=0, keepdims=True), axis=1, keepdims=True)

    wk, wa, v_k, v_a = w_k[...], w_a[...], vk[...], va[...]
    wv = total(wk * v_k + wa * v_a)
    vv = total(v_k * v_k + v_a * v_a)
    a = jnp.where(vv > 0.0, wv / jnp.where(vv > 0.0, vv, 1.0), 0.0)
    u_k, u_a = wk - a * v_k, wa - a * v_a
    uv = total(u_k * v_k + u_a * v_a)
    uu = total(u_k * u_k + u_a * u_a)
    lane = index_along((1, 128), 1)
    values = jnp.zeros((1, 128), jnp.float32)
    for i, value in enumerate((wv, vv, a, uv, uu)):
        values = jnp.where(lane == i, value, values)
    tile[...] = values


def final_kernel(tiles, w_k, w_a, vk, va, next_k, next_a, coefs, *, cells):
    tile = jnp.concatenate([tiles[i] for i in range(tiles.shape[0])], axis=0)
    wv, vv, a, uv, uu = (tile[:, i : i + 1] for i in range(5))
    wv_sum = jnp.sum(wv, axis=0, keepdims=True)
    vv_sum = jnp.sum(vv, axis=0, keepdims=True)
    alpha = wv_sum / cells / (vv_sum / cells + eps_norm)
    off = alpha - a
    rr = jnp.sum(uu - 2.0 * off * uv + off * (off * vv), axis=0, keepdims=True)
    beta = jnp.sqrt(rr / cells + eps_norm)
    next_k[...] = (w_k[...] - alpha * vk[...]) / beta
    next_a[...] = (w_a[...] - alpha * va[...]) / beta
    coefs[0] = jnp.sum(alpha)
    coefs[1] = jnp.sum(beta)


def f32(*shape):
    return jax.ShapeDtypeStruct(shape, jnp.float32)


def run(kernel, outs, *args, after=(), scratch=(), copies=0, smem=(), hbm=(), mib=16, in_smem_out=(), cost=None):
    vmem = pl.BlockSpec(memory_space=pltpu.VMEM)
    scalar = pl.BlockSpec(memory_space=pltpu.SMEM)
    far = pl.BlockSpec(memory_space=pltpu.HBM)
    held = [pltpu.VMEM(shape, dtype) for shape, dtype in scratch]
    used, waits = len(args), len(after)

    def body(*refs):
        kernel(*refs[:used], *refs[used + waits :])

    args = (*args, *after)
    if copies:
        held.append(pltpu.SemaphoreType.DMA((copies,)))
    return pl.pallas_call(
        body if waits else kernel,
        out_shape=tuple(outs),
        in_specs=[scalar if i in smem else far if i in hbm else vmem for i in range(len(args))],
        out_specs=tuple(scalar if i in in_smem_out else vmem for i in range(len(outs))),
        scratch_shapes=held,
        compiler_params=pltpu.CompilerParams(vmem_limit_bytes=mib * 2**20),
        cost_estimate=cost,
    )(*args)


HALO = 8
UNROLL = 16
REACH = 6
GROUP = 4


def per_device_paired(
    labels, kappa_table, absorb_table, background, det_cells,
    v_kappa, v_absorb, q_kappa, q_absorb, beta_prev,
):
    sources, cx, cy, cz = background.shape
    n = lax.axis_size("src")
    planes, rows = 2 * cx, 2 * cy + HALO
    ny = cy * lax.axis_size("gy")
    dets = det_cells.shape[0]
    cells = planes * ny * cz
    groups = cx // n

    def swap_x(value):
        return lax.ppermute(value, "gx", [(0, 1), (1, 0)])

    def swap_core(value):
        return lax.ppermute(value, "gy", [(0, 1), (1, 0), (2, 3), (3, 2)])

    def along_z(value, k):
        return lax.ppermute(value, "src", [(i, i ^ k) for i in range(n)])

    block = (cx, cy, cz)
    float_block = lambda *shape: (shape, jnp.float32)
    raw_labels = (block, jnp.int32)
    packed, message = run(
        pack_kernel, (f32(2 * groups, cy, cz), f32(sources // 2 * cx + 2 * groups, cy, cz)),
        background, v_kappa, v_absorb, hbm=(0, 1, 2),
        scratch=(float_block(2, *v_kappa.shape),), copies=2 + sources // 2, mib=60,
    )
    long = pl.CostEstimate(flops=10**9, bytes_accessed=2**26, transcendentals=0)
    labels_came = swap_x(labels)
    came = swap_x(message)
    slabs = [along_z(packed, k) for k in range(1, n)]
    count, beta_row = run(
        functools.partial(count_kernel, ny=ny, nz=cz, half=2 * cy, halo=HALO),
        (f32(planes, rows, cz), f32(1, cz)), det_cells.reshape(1, dets), beta_prev, smem=(1,), after=(labels_came,),
        cost=pl.CostEstimate(flops=2 * planes * rows * cz * dets, bytes_accessed=planes * rows * cz * 4, transcendentals=0),
    )

    def across_y(value):
        return lax.ppermute(value, "gy", [(i, (i + 2) % 4) for i in range(4)])

    (joined,) = run(join_kernel, (f32(2 * groups * (n - 1), cy, cz),), *slabs, after=(count,))
    joined_came = swap_x(joined)
    (half_vector,) = run(own_half_kernel, (f32(2, *block),), v_kappa, v_absorb, joined)
    mine, fields = run(
        photon_kernel, (f32(planes, cy, cz), f32(2, planes, cy, cz)),
        background, labels, came, labels_came, after=(joined,), hbm=(0, 1), scratch=(raw_labels,), copies=3,
    )
    got = swap_core(fields)
    (vector,) = run(
        vector_kernel, (f32(2, planes, cy, cz),), half_vector, came, joined_came, after=(mine,)
    )
    edge = (f32(2, *edge_shape(planes, cz)),)
    (sent,) = run(photon_edge_kernel, edge, mine, fields, got, after=(vector,))
    photon_edge = across_y(sent)
    vector_got = swap_core(vector)
    (vector_sent,) = run(vector_edge_kernel, edge, vector, vector_got, after=(sent,))
    frame, wide = (planes, rows, cz), (planes + 2, rows, cz)
    float_frame, float_wide = float_block(*frame), float_block(*wide)
    coefs = (f32(*frame), f32(planes + 1, rows, cz), f32(*frame), f32(*frame))
    kap, *partial, sums = run(
        stencil_kernel, (f32(*wide), *coefs, f32(2, 8, cz)),
        kappa_table, absorb_table, mine, fields, got, count, after=(vector_sent,), cost=long,
        smem=(0, 1), scratch=(float_frame,),
    )
    diag, fx, fy, fz = run(
        halo_kernel, coefs, kappa_table, absorb_table, photon_edge, kap, *partial, smem=(0, 1)
    )
    densities = run(
        density_kernel, (f32(*wide), f32(*frame), f32(*frame)), mine, got, photon_edge, after=(fz,)
    )
    change, sent = run(
        first_kernel, (f32(*frame), f32(REACH * planes + 8, cz)),
        *densities, diag, fx, fy, fz, count, sums, vector, vector_got, across_y(vector_sent),
        scratch=(float_wide, float_frame, float_frame, float_wide, float_wide),
    )
    heard = across_y(sent)
    own, message = run(
        functools.partial(second_kernel, dets=dets),
        (f32(2, planes, cy, cz), f32(2, planes, cy, cz)),
        *densities, change, diag, fx, fy, fz, count, sent, heard,
        scratch=(float_frame, float_wide, float_wide, float_frame, float_frame),
    )
    piece = f32(2, groups, cy, cz)
    got = swap_core(message)
    crossed, last = {}, ()
    for k in reversed(range(n)):
        last = run(functools.partial(send_kernel, k=k), (f32(1, *piece.shape),), own, got, after=last)
        crossed[k] = swap_x(last[0])
    (kept,) = run(keep_kernel, (f32(n, *piece.shape),), own, got, after=last)
    totals = {
        k: run(functools.partial(add_kernel, k=k), (piece,), kept, value)[0] for k, value in crossed.items()
    }
    received = {k: along_z(totals[k], k) for k in reversed(range(1, n))}
    (distant,) = run(sum_kernel, (piece,), *(received[k] for k in range(n // 2, n)), cost=long)
    parts = [distant, totals[0]] + [received[k] for k in range(1, n // 2)]
    w_k, w_a, tile = run(
        functools.partial(project_kernel, parts_n=len(parts), n=n),
        (f32(*v_kappa.shape), f32(*v_kappa.shape), f32(1, 128)),
        beta_row, *parts, v_kappa, v_absorb, q_kappa, q_absorb,
    )
    everyone = ("gy", "gx", "src")
    tiles = lax.all_to_all(jnp.broadcast_to(tile, (8 * n, 1, 128)), everyone, 0, 0)
    return tuple(run(
        functools.partial(final_kernel, cells=cells),
        (f32(*v_kappa.shape), f32(*v_kappa.shape), f32(2)),
        tiles, w_k, w_a, v_kappa, v_absorb, in_smem_out=(2,),
    ))


def paired_fits(mesh):
    return mesh.shape["gx"] == 2 and mesh.shape["gy"] == 4


def body_for(mesh):
    if not paired_fits(mesh):
        return per_device

    def chosen(*args):
        sources, cx, cy, cz = args[3].shape
        n = lax.axis_size("src")
        fits = sources == 4 and cz == 128 and cx % n == 0 and cx % GROUP == 0 and cy % HALO == 0 and n > 1 and n & (n - 1) == 0
        devices = 8 * n
        return (per_device_paired if fits and devices <= 128 else per_device)(*args)

    return chosen


def solution(mesh):
    return jax.shard_map(
        body_for(mesh),
        mesh=mesh,
        in_specs=(
            P("gx", "gy", None),
            P(),
            P(),
            P("src", "gx", "gy", None),
            P(),
            P("gx", "gy", "src"),
            P("gx", "gy", "src"),
            P("gx", "gy", "src"),
            P("gx", "gy", "src"),
            P(),
        ),
        out_specs=(P("gx", "gy", "src"), P("gx", "gy", "src"), P()),
        check_vma=False,
    )
```

```python
import functools

import jax
import jax.numpy as jnp
from jax import lax
from jax.experimental import pallas as pl
from jax.experimental.pallas import tpu as pltpu
from jax.sharding import PartitionSpec as P

ITERS = 6


lam_low = 0.02
lam_high = 24.1
eps_norm = 1e-06


def padded_2(block, sides, width):
    for axis, dim in sides:
        count = lax.axis_size(axis)
        forward = [(i, i + 1) for i in range(count - 1)]
        backward = [(target, source) for source, target in forward]
        low = lax.ppermute(
            lax.slice_in_dim(block, block.shape[dim] - width, None, axis=dim), axis, forward
        )
        high = lax.ppermute(lax.slice_in_dim(block, 0, width, axis=dim), axis, backward)
        block = jnp.concatenate([low, block, high], axis=dim)
    return block


def regional(labels, table):
    field = jnp.zeros(labels.shape, jnp.float32)
    for region in range(table.shape[0]):
        field = field + jnp.where(labels == region, table[region], 0.0)
    return field


def beside(padded):
    widths = [(0, 0)] * (padded.ndim - 1) + [(1, 1)]
    full = jnp.pad(padded, widths)
    return [
        full[..., 2:, 1:-1, 1:-1],
        full[..., :-2, 1:-1, 1:-1],
        full[..., 1:-1, 2:, 1:-1],
        full[..., 1:-1, :-2, 1:-1],
        full[..., 1:-1, 1:-1, 2:],
        full[..., 1:-1, 1:-1, :-2],
    ]


def chebyshev(rhs, apply_op):
    theta = 0.5 * (lam_high + lam_low)
    delta = 0.5 * (lam_high - lam_low)
    sigma = theta / delta
    rho = 1.0 / sigma
    solution = jnp.zeros_like(rhs)
    remain = rhs
    step_dir = rhs / theta
    for step in range(ITERS):
        solution = solution + step_dir
        if step + 1 < ITERS:
            remain = remain - apply_op(step_dir)
            rho_next = 1.0 / (2.0 * sigma - rho)
            step_dir = rho_next * rho * step_dir + 2.0 * rho_next / delta * remain
            rho = rho_next
    return solution


def per_device(
    labels,
    kappa_table,
    absorb_table,
    background,
    det_cells,
    v_kappa,
    v_absorb,
    q_kappa,
    q_absorb,
    beta_prev,
):
    sources, cx, cy, cz = background.shape
    kappa = regional(labels, kappa_table)
    absorb = regional(labels, absorb_table)
    full_k, full_a = (
        lax.all_gather(v_kappa, "src", axis=2, tiled=True),
        lax.all_gather(v_absorb, "src", axis=2, tiled=True),
    )
    stacked = jnp.concatenate([background, kappa[None], full_k[None]], axis=0)
    rims = padded_2(stacked, (("gx", 1), ("gy", 2)), 1)
    near_all = beside(rims)
    kappa_faces = [0.5 * (kappa + near[sources]) for near in near_all]
    vk_faces = [0.5 * (full_k + near[sources + 1]) for near in near_all]
    phi_near = [near[:sources] for near in near_all]

    def apply_op(field):
        padded = padded_2(field, (("gx", 1), ("gy", 2)), 1)
        result = absorb * field
        for face, near in zip(kappa_faces, beside(padded)):
            result = result + face * (field - near)
        return result

    rhs = full_a * background
    for face, near in zip(vk_faces, phi_near):
        rhs = rhs + face * (background - near)
    rhs = -rhs
    change = chebyshev(rhs, apply_op)
    span_y = cy * lax.axis_size("gy")
    ix = det_cells // (span_y * cz)
    iy = det_cells // cz % span_y
    iz = det_cells % cz
    anchor_x = lax.axis_index("gx") * cx
    anchor_y = lax.axis_index("gy") * cy
    owned = (ix >= anchor_x) & (ix < anchor_x + cx) & (iy >= anchor_y) & (iy < anchor_y + cy)
    local = jnp.where(owned, ((ix - anchor_x) * cy + (iy - anchor_y)) * cz + iz, 0)
    seen_part = jnp.where(owned[None, :], change.reshape(sources, -1)[:, local], 0.0)
    base_part = jnp.where(owned[None, :], background.reshape(sources, -1)[:, local], 0.0)
    seen, base = lax.psum((seen_part, base_part), ("gx", "gy"))
    total = jnp.sum(base, axis=1, keepdims=True)
    mean_base = total / det_cells.shape[0]
    ratio = base / total
    jv_vals = (seen - ratio * jnp.sum(seen, axis=1, keepdims=True)) / mean_base
    weight = (jv_vals - jnp.sum(ratio * jv_vals, axis=1, keepdims=True)) / mean_base
    deposit = jnp.where(owned[None, :], weight, 0.0)
    source = (
        jnp.zeros((sources, cx * cy * cz), jnp.float32)
        .at[:, local]
        .add(deposit)
        .reshape(change.shape)
    )
    dual = chebyshev(source, apply_op)
    dual_rims = padded_2(dual, (("gx", 1), ("gy", 2)), 1)
    grad_a = -jnp.sum(background * dual, axis=0)
    grad_k = jnp.zeros_like(kappa)
    for near_phi, near_dual in zip(phi_near, beside(dual_rims)):
        grad_k = grad_k - 0.5 * jnp.sum((background - near_phi) * (dual - near_dual), axis=0)
    summed_k, summed_a = lax.psum((grad_k, grad_a), "src")
    slab = v_kappa.shape[2]
    offset = lax.axis_index("src") * slab
    hv_k = lax.dynamic_slice_in_dim(summed_k, offset, slab, 2)
    hv_a = lax.dynamic_slice_in_dim(summed_a, offset, slab, 2)
    cell_count = cx * lax.axis_size("gx") * cy * lax.axis_size("gy") * cz
    w_k = hv_k - beta_prev[0] * q_kappa
    w_a = hv_a - beta_prev[0] * q_absorb
    local_wv = jnp.sum(w_k * v_kappa) + jnp.sum(w_a * v_absorb)
    local_vv = jnp.sum(v_kappa * v_kappa) + jnp.sum(v_absorb * v_absorb)
    wv_sum, vv_sum = lax.psum((local_wv, local_vv), ("src", "gx", "gy"))
    alpha = wv_sum / cell_count / (vv_sum / cell_count + eps_norm)
    r_k = w_k - alpha * v_kappa
    r_a = w_a - alpha * v_absorb
    rr_sum = lax.psum(jnp.sum(r_k * r_k) + jnp.sum(r_a * r_a), ("src", "gx", "gy"))
    beta = jnp.sqrt(rr_sum / cell_count + eps_norm)
    return (r_k / beta, r_a / beta, jnp.stack([alpha, beta]))


def chebyshev_scalars():
    theta = 0.5 * (lam_high + lam_low)
    delta = 0.5 * (lam_high - lam_low)
    sigma = theta / delta
    rho = 1.0 / sigma
    pairs = []
    for _ in range(ITERS - 1):
        rho_next = 1.0 / (2.0 * sigma - rho)
        pairs.append((rho_next * rho, 2.0 * rho_next / delta))
        rho = rho_next
    return theta, pairs


def places(split):
    g = lax.axis_index("gy")
    return lax.axis_index("src"), lax.axis_index("gx"), g // split, g % split


def shifted(value, step, axis):
    return pltpu.roll(value, step % value.shape[axis], axis)


def index_along(shape, axis):
    return lax.broadcasted_iota(jnp.int32, shape, axis)


def beyond(value, step, axis):
    size = value.shape[axis]
    at = index_along(value.shape, axis)
    edge = size - 1 if step == 1 else 0
    return jnp.where(at == edge, 0.0, shifted(value, -step, axis))


def packed_planes(ref, q):
    per = 128 // ref.shape[2]
    return jnp.concatenate([ref[per * q + j] for j in range(per)], axis=1)


def pack_kernel(bg, vk, va, packed, message, v_in, sems):
    _, x, _, _ = places(2)
    half = bg.shape[0] // 2
    cx = bg.shape[1]
    copies = [
        pltpu.make_async_copy(src, dst, sems.at[i])
        for i, (src, dst) in enumerate((
            (vk, v_in.at[0]),
            (va, v_in.at[1]),
            *((bg.at[half * (1 - x) + i], message.at[pl.ds(cx * i, cx)]) for i in range(half)),
        ))
    ]
    for copy in copies:
        copy.start()
    groups = packed.shape[0] // 2
    for f in range(2):
        copies[f].wait()
        for q in range(groups):
            planes = packed_planes(v_in.at[f], q)
            packed[groups * f + q] = planes
            message[cx * half + groups * f + q] = planes
    for copy in copies[2:]:
        copy.wait()


def count_kernel(dets, beta_prev, count, beta_row, *, ny, nz, half, halo):
    beta_row[...] = jnp.full(beta_row.shape, beta_prev[0])
    _, _, y, _ = places(2)
    planes, rows, _ = count.shape
    flat = dets[...]
    iz = flat % nz
    line = flat // nz
    iy = line % ny
    ix = line // ny
    row = iy - (half - halo) * y
    spot = jnp.where((row >= 0) & (row < rows), ix * rows + row, -1)
    dets_n = flat.shape[1]
    at_z = (index_along((nz, dets_n), 0) == iz).astype(jnp.float32).astype(jnp.bfloat16)

    def body(i, carry):
        here = index_along((2 * rows, dets_n), 0) + i * (2 * rows)
        hot = (here == spot).astype(jnp.float32).astype(jnp.bfloat16)
        found = lax.dot_general(hot, at_z, (((1,), (1,)), ((), ())), preferred_element_type=jnp.float32)
        count[pl.ds(2 * i, 2)] = found.reshape(2, rows, nz)
        return carry

    lax.fori_loop(0, planes // 2, body, 0)


def photon_kernel(bg, labels, msg, labels_came, mine, fields, raw, sems):
    _, x, _, c = places(2)
    half = bg.shape[0] // 2
    cx = labels.shape[0]
    here, there = cx * x, cx * (1 - x)
    copies = [
        pltpu.make_async_copy(src, dst, sems.at[i])
        for i, (src, dst) in enumerate((
            (bg.at[half * x + c], mine.at[pl.ds(here, cx)]),
            (bg.at[half * x + 1 - c], fields.at[0, pl.ds(here, cx)]),
            (labels, raw),
        ))
    ]
    for copy in copies:
        copy.start()
    mine[pl.ds(there, cx)] = msg[pl.ds(cx * c, cx)]
    fields[0, pl.ds(there, cx)] = msg[pl.ds(cx * (1 - c), cx)]
    fields[1, pl.ds(there, cx)] = labels_came[...].astype(jnp.float32)
    for copy in copies:
        copy.wait()
    fields[1, pl.ds(here, cx)] = raw[...].astype(jnp.float32)


def unpacked(blocks, groups, s, store):
    n = len(blocks)
    cy, lanes = blocks[0][0].shape
    slab = lanes // n
    lane = index_along((cy, lanes), 1) // slab
    for f in range(2):
        for q in range(groups):
            values = [block[groups * f + q] for block in blocks]
            for j in range(n):
                plane = jnp.zeros((cy, lanes), jnp.float32)
                for k in range(n):
                    home = s ^ k
                    moved = pltpu.roll(values[k], ((home - j + n) % n) * slab, 1)
                    plane = jnp.where(lane == home, moved, plane)
                store(f, n * q + j, plane)


def join_kernel(*refs):
    joined, size = refs[-1], refs[0].shape[0]
    for i, ref in enumerate(refs[:-1]):
        joined[pl.ds(size * i, size)] = ref[...]


def own_half_kernel(vk, va, joined, half):
    s, _, _, _ = places(2)
    size = half.shape[1]
    groups = joined.shape[0] // 2 // (128 // vk.shape[2] - 1)
    n = size // groups
    own = [packed_planes(ref, q) for ref in (vk, va) for q in range(groups)]
    blocks = [own] + [[joined[2 * groups * k + i] for i in range(2 * groups)] for k in range(n - 1)]

    def store(f, i, plane):
        half[f, i] = plane

    unpacked(blocks, groups, s, store)


def vector_kernel(half, msg, joined, fields):
    s, x, _, _ = places(2)
    cx = half.shape[1]
    fields[:, pl.ds(cx * x, cx)] = half[...]
    n = lax.axis_size("src")
    groups = cx // n
    own = msg.shape[0] - 2 * groups
    blocks = [[msg[own + i] for i in range(2 * groups)]]
    blocks += [[joined[2 * groups * k + i] for i in range(2 * groups)] for k in range(n - 1)]
    there = cx * (1 - x)

    def store(f, i, plane):
        fields[f, there + i] = plane

    unpacked(blocks, groups, s, store)


def edge_shape(planes, lanes):
    return planes // GROUP, GROUP * REACH, lanes


def packed_edges(tiles):
    return jnp.concatenate([tile[:REACH] for tile in tiles], axis=0)


def edge_tile(packed, j, y):
    rows = packed[REACH * j : REACH * (j + 1)]
    tile = jnp.concatenate([rows, jnp.zeros((HALO - REACH, rows.shape[1]), jnp.float32)], axis=0)
    return jnp.where(y == 0, tile, shifted(tile, HALO - REACH, 0))


def near_rows(ref, i, first, y):
    tile = ref[i, pl.ds(first, HALO), :]
    return jnp.where(y == 0, shifted(tile, REACH - HALO, 0), tile)


def edges_of(own, got, edge, y, c):
    first = (own.shape[1] - HALO) * (1 - y)
    for g in range(edge.shape[0]):
        edge[g] = packed_edges([
            jnp.where(c != y, near_rows(own, GROUP * g + j, first, y), near_rows(got, GROUP * g + j, first, y))
            for j in range(GROUP)
        ])


def photon_edge_kernel(mine, fields, got, edge):
    _, _, y, c = places(2)
    edges_of(mine, got.at[0], edge.at[0], y, c)
    edges_of(fields.at[1], got.at[1], edge.at[1], y, c)


def vector_edge_kernel(fields, got, edge):
    _, _, y, c = places(2)
    for f in range(2):
        edges_of(fields.at[f], got.at[f], edge.at[f], y, c)


def solve(b, bufs, diag, fx, fy, fz, unroll):
    planes = b.shape[0]
    _, pairs = chebyshev_scalars()
    for step, (keep, push) in enumerate(pairs):
        src, dst = bufs[step % 2], bufs[(step + 1) % 2]

        def body(i, carry):
            u = src[i + 1]
            coef_y, coef_z = fy[i], fz[i]
            left = b[i] - diag[i] * u
            left = left + fx[i] * src[i] + fx[i + 1] * src[i + 2]
            left = left + coef_y * shifted(u, -1, 0) + shifted(coef_y * u, 1, 0)
            left = left + coef_z * shifted(u, -1, 1) + shifted(coef_z * u, 1, 1)
            change = u if step == 0 else u - dst[i + 1]
            dst[i + 1] = u + keep * change + push * left
            return carry

        lax.fori_loop(0, planes, body, 0, unroll=unroll)
    return bufs[len(pairs) % 2]


def folded(value):
    return jnp.sum(value.reshape(-1, 8, value.shape[1]), axis=0)


def framed_own(ref, shift, own, got, y, c):
    planes, cy, _ = own.shape
    there = pl.ds(shift, planes)
    base = HALO * y
    ref[there, pl.ds(base + cy * c, cy), :] = own[...]
    ref[there, pl.ds(base + cy * (1 - c), cy), :] = got[...]


def framed(ref, shift, own, got, edge, y, c):
    framed_own(ref, shift, own, got, y, c)
    cy = own.shape[1]
    for g in range(edge.shape[0]):
        packed = edge[g]
        for j in range(GROUP):
            ref[shift + GROUP * g + j, pl.ds(2 * cy * (1 - y), HALO), :] = edge_tile(packed, j, y)


def blank_ends(*refs):
    for ref in refs:
        blank = jnp.zeros(ref.shape[1:], jnp.float32)
        ref[0] = blank
        ref[ref.shape[0] - 1] = blank


def owned_rows(shape, base, count):
    at_row = index_along(shape, 0)
    return (at_row >= base) & (at_row < base + count)


def table_rows(kap_table, abs_table, shape):
    lane = index_along(shape, 1)
    kap_row = abs_row = jnp.zeros(shape, jnp.float32)
    for region in range(kap_table.shape[0]):
        kap_row = jnp.where(lane == region, kap_table[region], kap_row)
        abs_row = jnp.where(lane == region, abs_table[region], abs_row)
    return kap_row, abs_row


def stencil_kernel(
    kap_table, abs_table, mine, fields, got, count,
    kap, diag, fx, fy, fz, sums,
    labels,
):
    _, _, y, c = places(2)
    planes, cy, lanes = mine.shape
    rows = 2 * cy + HALO
    base = HALO * y
    framed_own(labels, 0, fields.at[1], got.at[1], y, c)
    labels[:, pl.ds(2 * cy * (1 - y), HALO), :] = jnp.zeros((planes, HALO, lanes), jnp.float32)
    blank_ends(kap)
    shape = (rows, lanes)
    lane = index_along(shape, 1)
    kap_row, abs_row = table_rows(kap_table, abs_table, shape)
    owned = owned_rows(shape, base, 2 * cy)

    def look_up(i, carry):
        at = labels[i].astype(jnp.int32)
        kap[i + 1] = jnp.where(owned, jnp.take_along_axis(kap_row, at, axis=1), 0.0)
        diag[i] = jnp.take_along_axis(abs_row, at, axis=1)
        return carry

    lax.fori_loop(0, planes, look_up, 0, unroll=4)
    fx[0] = 0.5 * kap[1]

    def set_up(i, carry):
        k = kap[i + 1]
        along_x = 0.5 * (k + kap[i + 2])
        along_y, along_z = 0.5 * (k + beyond(k, 1, 0)), 0.5 * (k + beyond(k, 1, 1))
        fx[i + 1] = along_x
        fy[i] = jnp.where(index_along(shape, 0) == rows - 1, 0.0, along_y)
        fz[i] = jnp.where(lane == lanes - 1, 0.0, along_z)
        back_y, back_z = 0.5 * (k + beyond(k, -1, 0)), 0.5 * (k + beyond(k, -1, 1))
        diag[i] = diag[i] + fx[i] + along_x + along_y + back_y + along_z + back_z
        total, square = carry
        for p, at in ((mine[i], c), (got[0, i], 1 - c)):
            part = count[i, pl.ds(base + cy * at, cy), :] * p
            total, square = total + folded(part), square + folded(part * p)
        return total, square

    zero = jnp.zeros((8, lanes), jnp.float32)
    sums[0], sums[1] = lax.fori_loop(0, planes, set_up, (zero, zero), unroll=4)


def halo_kernel(kap_table, abs_table, edge, kap, diag_in, fx_in, fy_in, fz_in, diag, fx, fy, fz):
    _, _, y, _ = places(2)
    planes, rows, lanes = diag.shape
    for ref, old in ((diag, diag_in), (fx, fx_in), (fy, fy_in), (fz, fz_in)):
        ref[...] = old[...]
    shape = (HALO, lanes)
    lane, row = index_along(shape, 1), index_along(shape, 0)
    kap_row, abs_row = table_rows(kap_table, abs_table, shape)
    low = y == 0
    here = pl.ds((rows - HALO) * (1 - y), HALO)
    beside_it = pl.ds((rows - 2 * HALO) * (1 - y) + HALO * y, HALO)
    labels = [edge_tile(edge[1, i // GROUP], i % GROUP, y).astype(jnp.int32) for i in range(planes)]
    tiles = [jnp.take_along_axis(kap_row, at, axis=1) for at in labels]
    none = jnp.zeros(shape, jnp.float32)
    before = 0.5 * tiles[0]
    fx[0, here, :] = before
    for i, k in enumerate(tiles):
        after = 0.5 * (k + (tiles[i + 1] if i + 1 < planes else none))
        own = kap[i + 1, beside_it, :]
        up, down = shifted(k, -1, 0), shifted(k, 1, 0)
        k_up = jnp.where(row == HALO - 1, jnp.where(low, 0.0, shifted(own, -1, 0)), up)
        k_down = jnp.where(row == 0, jnp.where(low, shifted(own, 1, 0), 0.0), down)
        along_y, back_y = 0.5 * (k + k_up), 0.5 * (k + k_down)
        along_z, back_z = 0.5 * (k + beyond(k, 1, 1)), 0.5 * (k + beyond(k, -1, 1))
        fx[i + 1, here, :] = after
        fy[i, here, :] = jnp.where(low & (row == HALO - 1), 0.0, along_y)
        fz[i, here, :] = jnp.where(lane == lanes - 1, 0.0, along_z)
        absorb = jnp.take_along_axis(abs_row, labels[i], axis=1)
        diag[i, here, :] = absorb + before + after + along_y + back_y + along_z + back_z
        before = after
        face_up = jnp.where(low & (row == HALO - 1), 0.5 * up, 0.0)
        face_down = jnp.where(low | (row > 0), 0.0, 0.5 * down)
        fy[i, beside_it, :] = fy_in[i, beside_it, :] + face_up
        diag[i, beside_it, :] = diag_in[i, beside_it, :] + face_up + face_down


def density_kernel(mine, got, edge, phi, phi_y, phi_z):
    _, _, y, c = places(2)
    framed(phi, 1, mine, got.at[0], edge.at[0], y, c)
    blank_ends(phi)

    def differ(i, carry):
        p = phi[i + 1]
        phi_y[i], phi_z[i] = p - beyond(p, 1, 0), p - beyond(p, 1, 1)
        return carry

    lax.fori_loop(0, phi_y.shape[0], differ, 0, unroll=4)


def first_kernel(
    phi, phi_y, phi_z, diag, fx, fy, fz, count, sums, vector, got_vector, edge,
    change, message,
    vk, va, b, buf_a, buf_b,
):
    _, _, y, c = places(2)
    planes, rows, lanes = change.shape
    cy = vector.shape[2]
    framed(vk, 1, vector.at[0], got_vector.at[0], edge.at[0], y, c)
    framed(va, 0, vector.at[1], got_vector.at[1], edge.at[1], y, c)
    blank_ends(vk, buf_a, buf_b)
    theta, _ = chebyshev_scalars()

    def set_up(i, carry):
        v, p = vk[i + 1], phi[i + 1]
        total = 0.5 * (v + vk[i]) * (p - phi[i]) + 0.5 * (v + vk[i + 2]) * (p - phi[i + 2])
        for axis, step in enumerate((phi_y, phi_z)):
            flow = 0.5 * (v + beyond(v, 1, axis)) * step[i]
            first = index_along(v.shape, axis) == 0
            total = total + flow + jnp.where(first, 0.5 * v * p, -shifted(flow, 1, axis))
        total = -(va[i] * p + total)
        b[i] = total
        buf_a[i + 1] = total * (1.0 / theta)
        return carry

    lax.fori_loop(0, planes, set_up, 0, unroll=8)
    found = solve(b, (buf_a, buf_b), diag, fx, fy, fz, UNROLL)
    owned = owned_rows((rows, lanes), HALO * y, 2 * cy)

    def add_up(i, carry):
        u = found[i + 1]
        change[i] = u
        part = jnp.where(owned, count[i], 0.0) * u
        return carry[0] + folded(part), carry[1] + folded(part * phi[i + 1])

    zero = jnp.zeros((8, lanes), jnp.float32)
    seen, cross = lax.fori_loop(0, planes, add_up, (zero, zero), unroll=8)
    first = (2 * cy - HALO) * (1 - y) + HALO * y
    size = GROUP * REACH
    for g in range(planes // GROUP):
        message[pl.ds(size * g, size), :] = packed_edges(
            [near_rows(found, 1 + GROUP * g + j, first, y) for j in range(GROUP)]
        )
    rows_of_sums = [jnp.sum(part, axis=0, keepdims=True) for part in (sums[0], seen, cross, sums[1])]
    message[pl.ds(REACH * planes, 8), :] = jnp.concatenate([*rows_of_sums, zero[:4]], axis=0)


def second_kernel(
    phi, phi_y, phi_z, change, diag, fx, fy, fz, count, sent, came,
    own, message,
    b, buf_a, buf_b, grad_k, grad_a,
    *, dets,
):
    _, _, y, c = places(2)
    planes, rows, lanes = change.shape
    cy = (rows - HALO) // 2
    base = HALO * y
    edge = pl.ds(2 * cy * (1 - y), HALO)
    tail = pl.ds(REACH * planes, 8)
    sums = jnp.sum(sent[tail, :] + came[tail, :], axis=1, keepdims=True)
    total, seen_sum, cross, square = (sums[g : g + 1] for g in range(4))
    mean = total / dets
    part = seen_sum / total
    level = (cross - part * square) / (total * mean)
    inverse = 1.0 / mean
    blank_ends(buf_a, buf_b)
    theta, _ = chebyshev_scalars()

    def weighted(n, u, p):
        return n * (((u - p * part) * inverse - level) * inverse)

    def set_up(i, carry):
        value = weighted(count[i], change[i], phi[i + 1])
        b[i] = value
        buf_a[i + 1] = value * (1.0 / theta)
        return carry

    lax.fori_loop(0, planes, set_up, 0, unroll=8)
    size = GROUP * REACH
    for i in range(planes):
        u = edge_tile(came[pl.ds(size * (i // GROUP), size), :], i % GROUP, y)
        value = weighted(count[i, edge, :], u, phi[i + 1, edge, :])
        b[i, edge, :] = value
        buf_a[i + 1, edge, :] = value * (1.0 / theta)
    dual = solve(b, (buf_a, buf_b), diag, fx, fy, fz, UNROLL)

    def product(i, carry):
        p, u = phi[i + 1], dual[i + 1]
        grad = (p - phi[i]) * (u - dual[i]) + (p - phi[i + 2]) * (u - dual[i + 2])
        both = p * u
        for axis, step in enumerate((phi_y, phi_z)):
            flow = step[i] * (u - beyond(u, 1, axis))
            first = index_along(p.shape, axis) == 0
            grad = grad + flow + jnp.where(first, both, shifted(flow, 1, axis))
        grad_k[i] = -0.5 * grad
        grad_a[i] = -both
        for f, ref in enumerate((grad_k, grad_a)):
            own[f, i] = ref[i, pl.ds(base + cy * c, cy), :]
            message[f, i] = ref[i, pl.ds(base + cy * (1 - c), cy), :]
        return carry

    lax.fori_loop(0, planes, product, 0, unroll=8)


def packed_slabs(own, came, half, choices, outs):
    s, _, _, _ = places(2)
    _, planes, cy, lanes = own.shape
    n = planes // 2 // outs.shape[2]
    slab = lanes // n
    lane = index_along((cy, lanes), 1) // slab
    for f in range(2):
        for q in range(outs.shape[2]):
            at = planes // 2 * half + n * q
            parts = [own[f, at + j] + came[f, at + j] for j in range(n)]
            for i, k in enumerate(choices):
                to = s ^ k
                piece = jnp.zeros((cy, lanes), jnp.float32)
                for j in range(n):
                    moved = pltpu.roll(parts[j], ((j - to + n) % n) * slab, 1)
                    piece = jnp.where(lane == j, moved, piece)
                outs[i, f, q] = piece


def send_kernel(own, came, out, *, choices):
    _, x, _, _ = places(2)
    packed_slabs(own, came, 1 - x, choices, out)


def keep_kernel(own, came, kept):
    _, x, _, _ = places(2)
    packed_slabs(own, came, x, range(kept.shape[0]), kept)


def add_kernel(kept, came, out, *, k, at):
    out[...] = kept[k] + came[at]


def sum_kernel(*refs):
    total = refs[0][...]
    for ref in refs[1:-1]:
        total = total + ref[...]
    refs[-1][...] = total


def project_kernel(*refs, parts_n, n):
    beta_prev = refs[0]
    parts = refs[1 : 1 + parts_n]
    vk, va, qk, qa, w_k, w_a, tile = refs[1 + parts_n :]
    slab = 128 // n
    for f, (q_ref, w) in enumerate(((qk, w_k), (qa, w_a))):
        for q in range(vk.shape[0] // n):
            whole = sum(part[f, q] for part in parts[1:]) + parts[0][f, q]
            for j in range(n):
                i = n * q + j
                w[i] = whole[:, slab * j : slab * (j + 1)] - beta_prev[:, : vk.shape[2]] * q_ref[i]

    def total(value):
        return jnp.sum(jnp.sum(jnp.sum(value, axis=0), axis=0, keepdims=True), axis=1, keepdims=True)

    wk, wa, v_k, v_a = w_k[...], w_a[...], vk[...], va[...]
    wv = total(wk * v_k + wa * v_a)
    vv = total(v_k * v_k + v_a * v_a)
    a = jnp.where(vv > 0.0, wv / jnp.where(vv > 0.0, vv, 1.0), 0.0)
    u_k, u_a = wk - a * v_k, wa - a * v_a
    uv = total(u_k * v_k + u_a * v_a)
    uu = total(u_k * u_k + u_a * u_a)
    lane = index_along((1, 128), 1)
    values = jnp.zeros((1, 128), jnp.float32)
    for i, value in enumerate((wv, vv, a, uv, uu)):
        values = jnp.where(lane == i, value, values)
    tile[...] = values


def final_kernel(tiles, w_k, w_a, vk, va, next_k, next_a, coefs, *, cells):
    tile = jnp.concatenate([tiles[i] for i in range(tiles.shape[0])], axis=0)
    wv, vv, a, uv, uu = (tile[:, i : i + 1] for i in range(5))
    wv_sum = jnp.sum(wv, axis=0, keepdims=True)
    vv_sum = jnp.sum(vv, axis=0, keepdims=True)
    alpha = wv_sum / cells / (vv_sum / cells + eps_norm)
    off = alpha - a
    rr = jnp.sum(uu - 2.0 * off * uv + off * (off * vv), axis=0, keepdims=True)
    beta = jnp.sqrt(rr / cells + eps_norm)
    next_k[...] = (w_k[...] - alpha * vk[...]) / beta
    next_a[...] = (w_a[...] - alpha * va[...]) / beta
    coefs[0] = jnp.sum(alpha)
    coefs[1] = jnp.sum(beta)


def f32(*shape):
    return jax.ShapeDtypeStruct(shape, jnp.float32)


def run(kernel, outs, *args, after=(), scratch=(), copies=0, smem=(), hbm=(), mib=16, in_smem_out=(), cost=None):
    vmem = pl.BlockSpec(memory_space=pltpu.VMEM)
    scalar = pl.BlockSpec(memory_space=pltpu.SMEM)
    far = pl.BlockSpec(memory_space=pltpu.HBM)
    held = [pltpu.VMEM(shape, dtype) for shape, dtype in scratch]
    used, waits = len(args), len(after)

    def body(*refs):
        kernel(*refs[:used], *refs[used + waits :])

    args = (*args, *after)
    if copies:
        held.append(pltpu.SemaphoreType.DMA((copies,)))
    return pl.pallas_call(
        body if waits else kernel,
        out_shape=tuple(outs),
        in_specs=[scalar if i in smem else far if i in hbm else vmem for i in range(len(args))],
        out_specs=tuple(scalar if i in in_smem_out else vmem for i in range(len(outs))),
        scratch_shapes=held,
        compiler_params=pltpu.CompilerParams(vmem_limit_bytes=mib * 2**20),
        cost_estimate=cost,
    )(*args)


HALO = 8
UNROLL = 16
REACH = 6
GROUP = 4


def per_device_paired(
    labels, kappa_table, absorb_table, background, det_cells,
    v_kappa, v_absorb, q_kappa, q_absorb, beta_prev,
):
    sources, cx, cy, cz = background.shape
    n = lax.axis_size("src")
    planes, rows = 2 * cx, 2 * cy + HALO
    ny = cy * lax.axis_size("gy")
    dets = det_cells.shape[0]
    cells = planes * ny * cz
    groups = cx // n

    def swap_x(value):
        return lax.ppermute(value, "gx", [(0, 1), (1, 0)])

    def swap_core(value):
        return lax.ppermute(value, "gy", [(0, 1), (1, 0), (2, 3), (3, 2)])

    def along_z(value, k):
        return lax.ppermute(value, "src", [(i, i ^ k) for i in range(n)])

    block = (cx, cy, cz)
    float_block = lambda *shape: (shape, jnp.float32)
    raw_labels = (block, jnp.int32)
    packed, message = run(
        pack_kernel, (f32(2 * groups, cy, cz), f32(sources // 2 * cx + 2 * groups, cy, cz)),
        background, v_kappa, v_absorb, hbm=(0, 1, 2),
        scratch=(float_block(2, *v_kappa.shape),), copies=2 + sources // 2, mib=60,
    )
    long = pl.CostEstimate(flops=10**9, bytes_accessed=2**26, transcendentals=0)
    labels_came = swap_x(labels)
    came = swap_x(message)
    slabs = [along_z(packed, k) for k in range(1, n)]
    count, beta_row = run(
        functools.partial(count_kernel, ny=ny, nz=cz, half=2 * cy, halo=HALO),
        (f32(planes, rows, cz), f32(1, cz)), det_cells.reshape(1, dets), beta_prev, smem=(1,), after=(labels_came,),
        cost=pl.CostEstimate(flops=2 * planes * rows * cz * dets, bytes_accessed=planes * rows * cz * 4, transcendentals=0),
    )

    def across_y(value):
        return lax.ppermute(value, "gy", [(i, (i + 2) % 4) for i in range(4)])

    (joined,) = run(join_kernel, (f32(2 * groups * (n - 1), cy, cz),), *slabs, after=(count,))
    joined_came = swap_x(joined)
    (half_vector,) = run(own_half_kernel, (f32(2, *block),), v_kappa, v_absorb, joined)
    mine, fields = run(
        photon_kernel, (f32(planes, cy, cz), f32(2, planes, cy, cz)),
        background, labels, came, labels_came, after=(joined,), hbm=(0, 1), scratch=(raw_labels,), copies=3,
    )
    got = swap_core(fields)
    (vector,) = run(
        vector_kernel, (f32(2, planes, cy, cz),), half_vector, came, joined_came, after=(mine,)
    )
    edge = (f32(2, *edge_shape(planes, cz)),)
    (sent,) = run(photon_edge_kernel, edge, mine, fields, got, after=(vector,))
    photon_edge = across_y(sent)
    vector_got = swap_core(vector)
    (vector_sent,) = run(vector_edge_kernel, edge, vector, vector_got, after=(sent,))
    frame, wide = (planes, rows, cz), (planes + 2, rows, cz)
    float_frame, float_wide = float_block(*frame), float_block(*wide)
    coefs = (f32(*frame), f32(planes + 1, rows, cz), f32(*frame), f32(*frame))
    kap, *partial, sums = run(
        stencil_kernel, (f32(*wide), *coefs, f32(2, 8, cz)),
        kappa_table, absorb_table, mine, fields, got, count, after=(vector_sent,), cost=long,
        smem=(0, 1), scratch=(float_frame,),
    )
    diag, fx, fy, fz = run(
        halo_kernel, coefs, kappa_table, absorb_table, photon_edge, kap, *partial, smem=(0, 1)
    )
    densities = run(
        density_kernel, (f32(*wide), f32(*frame), f32(*frame)), mine, got, photon_edge, after=(fz,)
    )
    change, sent = run(
        first_kernel, (f32(*frame), f32(REACH * planes + 8, cz)),
        *densities, diag, fx, fy, fz, count, sums, vector, vector_got, across_y(vector_sent),
        scratch=(float_wide, float_frame, float_frame, float_wide, float_wide),
    )
    heard = across_y(sent)
    own, message = run(
        functools.partial(second_kernel, dets=dets),
        (f32(2, planes, cy, cz), f32(2, planes, cy, cz)),
        *densities, change, diag, fx, fy, fz, count, sent, heard,
        scratch=(float_frame, float_wide, float_wide, float_frame, float_frame),
    )
    piece = f32(2, groups, cy, cz)
    got = swap_core(message)
    crossed, last = {}, ()
    half = n // 2
    for choices in (*((k,) for k in reversed(range(half, n))), tuple(range(half))):
        last = run(
            functools.partial(send_kernel, choices=choices), (f32(len(choices), *piece.shape),), own, got, after=last
        )
        value = swap_x(last[0])
        crossed.update({k: (value, at) for at, k in enumerate(choices)})
    (kept,) = run(keep_kernel, (f32(n, *piece.shape),), own, got, after=last)
    totals = {
        k: run(functools.partial(add_kernel, k=k, at=at), (piece,), kept, value)[0]
        for k, (value, at) in crossed.items()
    }
    received = {k: along_z(totals[k], k) for k in reversed(range(1, n))}
    (distant,) = run(sum_kernel, (piece,), *(received[k] for k in range(n // 2, n)), cost=long)
    parts = [distant, totals[0]] + [received[k] for k in range(1, n // 2)]
    w_k, w_a, tile = run(
        functools.partial(project_kernel, parts_n=len(parts), n=n),
        (f32(*v_kappa.shape), f32(*v_kappa.shape), f32(1, 128)),
        beta_row, *parts, v_kappa, v_absorb, q_kappa, q_absorb,
    )
    everyone = ("src", "gx", "gy")
    tiles = lax.all_to_all(jnp.broadcast_to(tile, (8 * n, 1, 128)), everyone, 0, 0)
    return tuple(run(
        functools.partial(final_kernel, cells=cells),
        (f32(*v_kappa.shape), f32(*v_kappa.shape), f32(2)),
        tiles, w_k, w_a, v_kappa, v_absorb, in_smem_out=(2,),
    ))


def paired_fits(mesh):
    return mesh.shape["gx"] == 2 and mesh.shape["gy"] == 4


def body_for(mesh):
    if not paired_fits(mesh):
        return per_device

    def chosen(*args):
        sources, cx, cy, cz = args[3].shape
        n = lax.axis_size("src")
        fits = sources == 4 and cz == 128 and cx % n == 0 and cx % GROUP == 0 and cy % HALO == 0 and n > 1 and n & (n - 1) == 0
        devices = 8 * n
        return (per_device_paired if fits and devices <= 128 else per_device)(*args)

    return chosen


def solution(mesh):
    return jax.shard_map(
        body_for(mesh),
        mesh=mesh,
        in_specs=(
            P("gx", "gy", None),
            P(),
            P(),
            P("src", "gx", "gy", None),
            P(),
            P("gx", "gy", "src"),
            P("gx", "gy", "src"),
            P("gx", "gy", "src"),
            P("gx", "gy", "src"),
            P(),
        ),
        out_specs=(P("gx", "gy", "src"), P("gx", "gy", "src"), P()),
        check_vma=False,
    )
```

```python
import functools

import jax
import jax.numpy as jnp
from jax import lax
from jax.experimental import pallas as pl
from jax.experimental.pallas import tpu as pltpu
from jax.sharding import PartitionSpec as P

ITERS = 6


lam_low = 0.02
lam_high = 24.1
eps_norm = 1e-06


def padded_2(block, sides, width):
    for axis, dim in sides:
        count = lax.axis_size(axis)
        forward = [(i, i + 1) for i in range(count - 1)]
        backward = [(target, source) for source, target in forward]
        low = lax.ppermute(
            lax.slice_in_dim(block, block.shape[dim] - width, None, axis=dim), axis, forward
        )
        high = lax.ppermute(lax.slice_in_dim(block, 0, width, axis=dim), axis, backward)
        block = jnp.concatenate([low, block, high], axis=dim)
    return block


def regional(labels, table):
    field = jnp.zeros(labels.shape, jnp.float32)
    for region in range(table.shape[0]):
        field = field + jnp.where(labels == region, table[region], 0.0)
    return field


def beside(padded):
    widths = [(0, 0)] * (padded.ndim - 1) + [(1, 1)]
    full = jnp.pad(padded, widths)
    return [
        full[..., 2:, 1:-1, 1:-1],
        full[..., :-2, 1:-1, 1:-1],
        full[..., 1:-1, 2:, 1:-1],
        full[..., 1:-1, :-2, 1:-1],
        full[..., 1:-1, 1:-1, 2:],
        full[..., 1:-1, 1:-1, :-2],
    ]


def chebyshev(rhs, apply_op):
    theta = 0.5 * (lam_high + lam_low)
    delta = 0.5 * (lam_high - lam_low)
    sigma = theta / delta
    rho = 1.0 / sigma
    solution = jnp.zeros_like(rhs)
    remain = rhs
    step_dir = rhs / theta
    for step in range(ITERS):
        solution = solution + step_dir
        if step + 1 < ITERS:
            remain = remain - apply_op(step_dir)
            rho_next = 1.0 / (2.0 * sigma - rho)
            step_dir = rho_next * rho * step_dir + 2.0 * rho_next / delta * remain
            rho = rho_next
    return solution


def per_device(
    labels,
    kappa_table,
    absorb_table,
    background,
    det_cells,
    v_kappa,
    v_absorb,
    q_kappa,
    q_absorb,
    beta_prev,
):
    sources, cx, cy, cz = background.shape
    kappa = regional(labels, kappa_table)
    absorb = regional(labels, absorb_table)
    full_k, full_a = (
        lax.all_gather(v_kappa, "src", axis=2, tiled=True),
        lax.all_gather(v_absorb, "src", axis=2, tiled=True),
    )
    stacked = jnp.concatenate([background, kappa[None], full_k[None]], axis=0)
    rims = padded_2(stacked, (("gx", 1), ("gy", 2)), 1)
    near_all = beside(rims)
    kappa_faces = [0.5 * (kappa + near[sources]) for near in near_all]
    vk_faces = [0.5 * (full_k + near[sources + 1]) for near in near_all]
    phi_near = [near[:sources] for near in near_all]

    def apply_op(field):
        padded = padded_2(field, (("gx", 1), ("gy", 2)), 1)
        result = absorb * field
        for face, near in zip(kappa_faces, beside(padded)):
            result = result + face * (field - near)
        return result

    rhs = full_a * background
    for face, near in zip(vk_faces, phi_near):
        rhs = rhs + face * (background - near)
    rhs = -rhs
    change = chebyshev(rhs, apply_op)
    span_y = cy * lax.axis_size("gy")
    ix = det_cells // (span_y * cz)
    iy = det_cells // cz % span_y
    iz = det_cells % cz
    anchor_x = lax.axis_index("gx") * cx
    anchor_y = lax.axis_index("gy") * cy
    owned = (ix >= anchor_x) & (ix < anchor_x + cx) & (iy >= anchor_y) & (iy < anchor_y + cy)
    local = jnp.where(owned, ((ix - anchor_x) * cy + (iy - anchor_y)) * cz + iz, 0)
    seen_part = jnp.where(owned[None, :], change.reshape(sources, -1)[:, local], 0.0)
    base_part = jnp.where(owned[None, :], background.reshape(sources, -1)[:, local], 0.0)
    seen, base = lax.psum((seen_part, base_part), ("gx", "gy"))
    total = jnp.sum(base, axis=1, keepdims=True)
    mean_base = total / det_cells.shape[0]
    ratio = base / total
    jv_vals = (seen - ratio * jnp.sum(seen, axis=1, keepdims=True)) / mean_base
    weight = (jv_vals - jnp.sum(ratio * jv_vals, axis=1, keepdims=True)) / mean_base
    deposit = jnp.where(owned[None, :], weight, 0.0)
    source = (
        jnp.zeros((sources, cx * cy * cz), jnp.float32)
        .at[:, local]
        .add(deposit)
        .reshape(change.shape)
    )
    dual = chebyshev(source, apply_op)
    dual_rims = padded_2(dual, (("gx", 1), ("gy", 2)), 1)
    grad_a = -jnp.sum(background * dual, axis=0)
    grad_k = jnp.zeros_like(kappa)
    for near_phi, near_dual in zip(phi_near, beside(dual_rims)):
        grad_k = grad_k - 0.5 * jnp.sum((background - near_phi) * (dual - near_dual), axis=0)
    summed_k, summed_a = lax.psum((grad_k, grad_a), "src")
    slab = v_kappa.shape[2]
    offset = lax.axis_index("src") * slab
    hv_k = lax.dynamic_slice_in_dim(summed_k, offset, slab, 2)
    hv_a = lax.dynamic_slice_in_dim(summed_a, offset, slab, 2)
    cell_count = cx * lax.axis_size("gx") * cy * lax.axis_size("gy") * cz
    w_k = hv_k - beta_prev[0] * q_kappa
    w_a = hv_a - beta_prev[0] * q_absorb
    local_wv = jnp.sum(w_k * v_kappa) + jnp.sum(w_a * v_absorb)
    local_vv = jnp.sum(v_kappa * v_kappa) + jnp.sum(v_absorb * v_absorb)
    wv_sum, vv_sum = lax.psum((local_wv, local_vv), ("src", "gx", "gy"))
    alpha = wv_sum / cell_count / (vv_sum / cell_count + eps_norm)
    r_k = w_k - alpha * v_kappa
    r_a = w_a - alpha * v_absorb
    rr_sum = lax.psum(jnp.sum(r_k * r_k) + jnp.sum(r_a * r_a), ("src", "gx", "gy"))
    beta = jnp.sqrt(rr_sum / cell_count + eps_norm)
    return (r_k / beta, r_a / beta, jnp.stack([alpha, beta]))


def chebyshev_scalars():
    theta = 0.5 * (lam_high + lam_low)
    delta = 0.5 * (lam_high - lam_low)
    sigma = theta / delta
    rho = 1.0 / sigma
    pairs = []
    for _ in range(ITERS - 1):
        rho_next = 1.0 / (2.0 * sigma - rho)
        pairs.append((rho_next * rho, 2.0 * rho_next / delta))
        rho = rho_next
    return theta, pairs


def places(split):
    g = lax.axis_index("gy")
    return lax.axis_index("src"), lax.axis_index("gx"), g // split, g % split


def shifted(value, step, axis):
    return pltpu.roll(value, step % value.shape[axis], axis)


def index_along(shape, axis):
    return lax.broadcasted_iota(jnp.int32, shape, axis)


def beyond(value, step, axis):
    size = value.shape[axis]
    at = index_along(value.shape, axis)
    edge = size - 1 if step == 1 else 0
    return jnp.where(at == edge, 0.0, shifted(value, -step, axis))


def packed_planes(ref, q):
    per = 128 // ref.shape[2]
    return jnp.concatenate([ref[per * q + j] for j in range(per)], axis=1)


def pack_kernel(bg, vk, va, packed, message, v_in, sems):
    _, x, _, _ = places(2)
    half = bg.shape[0] // 2
    cx = bg.shape[1]
    copies = [
        pltpu.make_async_copy(src, dst, sems.at[i])
        for i, (src, dst) in enumerate((
            (vk, v_in.at[0]),
            (va, v_in.at[1]),
            *((bg.at[half * (1 - x) + i], message.at[pl.ds(cx * i, cx)]) for i in range(half)),
        ))
    ]
    for copy in copies:
        copy.start()
    groups = packed.shape[0] // 2
    for f in range(2):
        copies[f].wait()
        for q in range(groups):
            planes = packed_planes(v_in.at[f], q)
            packed[groups * f + q] = planes
            message[cx * half + groups * f + q] = planes
    for copy in copies[2:]:
        copy.wait()


def count_kernel(dets, beta_prev, count, beta_row, *, ny, nz, half, halo):
    beta_row[...] = jnp.full(beta_row.shape, beta_prev[0])
    _, _, y, _ = places(2)
    planes, rows, _ = count.shape
    flat = dets[...]
    iz = flat % nz
    line = flat // nz
    iy = line % ny
    ix = line // ny
    row = iy - (half - halo) * y
    spot = jnp.where((row >= 0) & (row < rows), ix * rows + row, -1)
    dets_n = flat.shape[1]
    at_z = (index_along((nz, dets_n), 0) == iz).astype(jnp.float32).astype(jnp.bfloat16)

    def body(i, carry):
        here = index_along((2 * rows, dets_n), 0) + i * (2 * rows)
        hot = (here == spot).astype(jnp.float32).astype(jnp.bfloat16)
        found = lax.dot_general(hot, at_z, (((1,), (1,)), ((), ())), preferred_element_type=jnp.float32)
        count[pl.ds(2 * i, 2)] = found.reshape(2, rows, nz)
        return carry

    lax.fori_loop(0, planes // 2, body, 0)


def photon_kernel(bg, labels, msg, labels_came, mine, fields, raw, sems):
    _, x, _, c = places(2)
    half = bg.shape[0] // 2
    cx = labels.shape[0]
    here, there = cx * x, cx * (1 - x)
    copies = [
        pltpu.make_async_copy(src, dst, sems.at[i])
        for i, (src, dst) in enumerate((
            (bg.at[half * x + c], mine.at[pl.ds(here, cx)]),
            (bg.at[half * x + 1 - c], fields.at[0, pl.ds(here, cx)]),
            (labels, raw),
        ))
    ]
    for copy in copies:
        copy.start()
    mine[pl.ds(there, cx)] = msg[pl.ds(cx * c, cx)]
    fields[0, pl.ds(there, cx)] = msg[pl.ds(cx * (1 - c), cx)]
    fields[1, pl.ds(there, cx)] = labels_came[...].astype(jnp.float32)
    for copy in copies:
        copy.wait()
    fields[1, pl.ds(here, cx)] = raw[...].astype(jnp.float32)


def unpacked(blocks, groups, s, store):
    n = len(blocks)
    cy, lanes = blocks[0][0].shape
    slab = lanes // n
    lane = index_along((cy, lanes), 1) // slab
    for f in range(2):
        for q in range(groups):
            values = [block[groups * f + q] for block in blocks]
            for j in range(n):
                plane = jnp.zeros((cy, lanes), jnp.float32)
                for k in range(n):
                    home = s ^ k
                    moved = pltpu.roll(values[k], ((home - j + n) % n) * slab, 1)
                    plane = jnp.where(lane == home, moved, plane)
                store(f, n * q + j, plane)


def join_kernel(*refs):
    joined, size = refs[-1], refs[0].shape[0]
    for i, ref in enumerate(refs[:-1]):
        joined[pl.ds(size * i, size)] = ref[...]


def own_half_kernel(vk, va, joined, half):
    s, _, _, _ = places(2)
    size = half.shape[1]
    groups = joined.shape[0] // 2 // (128 // vk.shape[2] - 1)
    n = size // groups
    own = [packed_planes(ref, q) for ref in (vk, va) for q in range(groups)]
    blocks = [own] + [[joined[2 * groups * k + i] for i in range(2 * groups)] for k in range(n - 1)]

    def store(f, i, plane):
        half[f, i] = plane

    unpacked(blocks, groups, s, store)


def vector_kernel(half, msg, joined, fields):
    s, x, _, _ = places(2)
    cx = half.shape[1]
    fields[:, pl.ds(cx * x, cx)] = half[...]
    n = lax.axis_size("src")
    groups = cx // n
    own = msg.shape[0] - 2 * groups
    blocks = [[msg[own + i] for i in range(2 * groups)]]
    blocks += [[joined[2 * groups * k + i] for i in range(2 * groups)] for k in range(n - 1)]
    there = cx * (1 - x)

    def store(f, i, plane):
        fields[f, there + i] = plane

    unpacked(blocks, groups, s, store)


def edge_shape(planes, lanes):
    return planes // GROUP, GROUP * REACH, lanes


def packed_edges(tiles):
    return jnp.concatenate([tile[:REACH] for tile in tiles], axis=0)


def edge_tile(packed, j, y):
    rows = packed[REACH * j : REACH * (j + 1)]
    tile = jnp.concatenate([rows, jnp.zeros((HALO - REACH, rows.shape[1]), jnp.float32)], axis=0)
    return jnp.where(y == 0, tile, shifted(tile, HALO - REACH, 0))


def near_rows(ref, i, first, y):
    tile = ref[i, pl.ds(first, HALO), :]
    return jnp.where(y == 0, shifted(tile, REACH - HALO, 0), tile)


def edges_of(own, got, edge, y, c):
    first = (own.shape[1] - HALO) * (1 - y)
    for g in range(edge.shape[0]):
        edge[g] = packed_edges([
            jnp.where(c != y, near_rows(own, GROUP * g + j, first, y), near_rows(got, GROUP * g + j, first, y))
            for j in range(GROUP)
        ])


def photon_edge_kernel(mine, fields, got, edge):
    _, _, y, c = places(2)
    edges_of(mine, got.at[0], edge.at[0], y, c)
    edges_of(fields.at[1], got.at[1], edge.at[1], y, c)


def vector_edge_kernel(fields, got, edge):
    _, _, y, c = places(2)
    for f in range(2):
        edges_of(fields.at[f], got.at[f], edge.at[f], y, c)


def solve(b, bufs, diag, fx, fy, fz, unroll):
    planes = b.shape[0]
    _, pairs = chebyshev_scalars()
    for step, (keep, push) in enumerate(pairs):
        src, dst = bufs[step % 2], bufs[(step + 1) % 2]

        def body(i, carry):
            u = src[i + 1]
            coef_y, coef_z = fy[i], fz[i]
            left = b[i] - diag[i] * u
            left = left + fx[i] * src[i] + fx[i + 1] * src[i + 2]
            left = left + coef_y * shifted(u, -1, 0) + shifted(coef_y * u, 1, 0)
            left = left + coef_z * shifted(u, -1, 1) + shifted(coef_z * u, 1, 1)
            change = u if step == 0 else u - dst[i + 1]
            dst[i + 1] = u + keep * change + push * left
            return carry

        lax.fori_loop(0, planes, body, 0, unroll=unroll)
    return bufs[len(pairs) % 2]


def folded(value):
    return jnp.sum(value.reshape(-1, 8, value.shape[1]), axis=0)


def framed_own(ref, shift, own, got, y, c):
    planes, cy, _ = own.shape
    there = pl.ds(shift, planes)
    base = HALO * y
    ref[there, pl.ds(base + cy * c, cy), :] = own[...]
    ref[there, pl.ds(base + cy * (1 - c), cy), :] = got[...]


def framed(ref, shift, own, got, edge, y, c):
    framed_own(ref, shift, own, got, y, c)
    cy = own.shape[1]
    for g in range(edge.shape[0]):
        packed = edge[g]
        for j in range(GROUP):
            ref[shift + GROUP * g + j, pl.ds(2 * cy * (1 - y), HALO), :] = edge_tile(packed, j, y)


def blank_ends(*refs):
    for ref in refs:
        blank = jnp.zeros(ref.shape[1:], jnp.float32)
        ref[0] = blank
        ref[ref.shape[0] - 1] = blank


def owned_rows(shape, base, count):
    at_row = index_along(shape, 0)
    return (at_row >= base) & (at_row < base + count)


def table_rows(kap_table, abs_table, shape):
    lane = index_along(shape, 1)
    kap_row = abs_row = jnp.zeros(shape, jnp.float32)
    for region in range(kap_table.shape[0]):
        kap_row = jnp.where(lane == region, kap_table[region], kap_row)
        abs_row = jnp.where(lane == region, abs_table[region], abs_row)
    return kap_row, abs_row


def stencil_kernel(
    kap_table, abs_table, mine, fields, got, count,
    kap, diag, fx, fy, fz, sums,
    labels,
):
    _, _, y, c = places(2)
    planes, cy, lanes = mine.shape
    rows = 2 * cy + HALO
    base = HALO * y
    framed_own(labels, 0, fields.at[1], got.at[1], y, c)
    labels[:, pl.ds(2 * cy * (1 - y), HALO), :] = jnp.zeros((planes, HALO, lanes), jnp.float32)
    blank_ends(kap)
    shape = (rows, lanes)
    lane = index_along(shape, 1)
    kap_row, abs_row = table_rows(kap_table, abs_table, shape)
    owned = owned_rows(shape, base, 2 * cy)

    def look_up(i, carry):
        at = labels[i].astype(jnp.int32)
        kap[i + 1] = jnp.where(owned, jnp.take_along_axis(kap_row, at, axis=1), 0.0)
        diag[i] = jnp.take_along_axis(abs_row, at, axis=1)
        return carry

    lax.fori_loop(0, planes, look_up, 0, unroll=4)
    fx[0] = 0.5 * kap[1]

    def set_up(i, carry):
        k = kap[i + 1]
        along_x = 0.5 * (k + kap[i + 2])
        along_y, along_z = 0.5 * (k + beyond(k, 1, 0)), 0.5 * (k + beyond(k, 1, 1))
        fx[i + 1] = along_x
        fy[i] = jnp.where(index_along(shape, 0) == rows - 1, 0.0, along_y)
        fz[i] = jnp.where(lane == lanes - 1, 0.0, along_z)
        back_y, back_z = 0.5 * (k + beyond(k, -1, 0)), 0.5 * (k + beyond(k, -1, 1))
        diag[i] = diag[i] + fx[i] + along_x + along_y + back_y + along_z + back_z
        total, square = carry
        for p, at in ((mine[i], c), (got[0, i], 1 - c)):
            part = count[i, pl.ds(base + cy * at, cy), :] * p
            total, square = total + folded(part), square + folded(part * p)
        return total, square

    zero = jnp.zeros((8, lanes), jnp.float32)
    sums[0], sums[1] = lax.fori_loop(0, planes, set_up, (zero, zero), unroll=4)


def halo_kernel(kap_table, abs_table, edge, kap, diag_in, fx_in, fy_in, fz_in, diag, fx, fy, fz):
    _, _, y, _ = places(2)
    planes, rows, lanes = diag.shape
    for ref, old in ((diag, diag_in), (fx, fx_in), (fy, fy_in), (fz, fz_in)):
        ref[...] = old[...]
    shape = (HALO, lanes)
    lane, row = index_along(shape, 1), index_along(shape, 0)
    kap_row, abs_row = table_rows(kap_table, abs_table, shape)
    low = y == 0
    here = pl.ds((rows - HALO) * (1 - y), HALO)
    beside_it = pl.ds((rows - 2 * HALO) * (1 - y) + HALO * y, HALO)
    labels = [edge_tile(edge[1, i // GROUP], i % GROUP, y).astype(jnp.int32) for i in range(planes)]
    tiles = [jnp.take_along_axis(kap_row, at, axis=1) for at in labels]
    none = jnp.zeros(shape, jnp.float32)
    before = 0.5 * tiles[0]
    fx[0, here, :] = before
    for i, k in enumerate(tiles):
        after = 0.5 * (k + (tiles[i + 1] if i + 1 < planes else none))
        own = kap[i + 1, beside_it, :]
        up, down = shifted(k, -1, 0), shifted(k, 1, 0)
        k_up = jnp.where(row == HALO - 1, jnp.where(low, 0.0, shifted(own, -1, 0)), up)
        k_down = jnp.where(row == 0, jnp.where(low, shifted(own, 1, 0), 0.0), down)
        along_y, back_y = 0.5 * (k + k_up), 0.5 * (k + k_down)
        along_z, back_z = 0.5 * (k + beyond(k, 1, 1)), 0.5 * (k + beyond(k, -1, 1))
        fx[i + 1, here, :] = after
        fy[i, here, :] = jnp.where(low & (row == HALO - 1), 0.0, along_y)
        fz[i, here, :] = jnp.where(lane == lanes - 1, 0.0, along_z)
        absorb = jnp.take_along_axis(abs_row, labels[i], axis=1)
        diag[i, here, :] = absorb + before + after + along_y + back_y + along_z + back_z
        before = after
        face_up = jnp.where(low & (row == HALO - 1), 0.5 * up, 0.0)
        face_down = jnp.where(low | (row > 0), 0.0, 0.5 * down)
        fy[i, beside_it, :] = fy_in[i, beside_it, :] + face_up
        diag[i, beside_it, :] = diag_in[i, beside_it, :] + face_up + face_down


def density_kernel(mine, got, edge, phi, phi_y, phi_z):
    _, _, y, c = places(2)
    framed(phi, 1, mine, got.at[0], edge.at[0], y, c)
    blank_ends(phi)

    def differ(i, carry):
        p = phi[i + 1]
        phi_y[i], phi_z[i] = p - beyond(p, 1, 0), p - beyond(p, 1, 1)
        return carry

    lax.fori_loop(0, phi_y.shape[0], differ, 0, unroll=4)


def first_kernel(
    phi, phi_y, phi_z, diag, fx, fy, fz, count, sums, vector, got_vector, edge,
    change, message,
    vk, va, b, buf_a, buf_b,
):
    _, _, y, c = places(2)
    planes, rows, lanes = change.shape
    cy = vector.shape[2]
    framed(vk, 1, vector.at[0], got_vector.at[0], edge.at[0], y, c)
    framed(va, 0, vector.at[1], got_vector.at[1], edge.at[1], y, c)
    blank_ends(vk, buf_a, buf_b)
    theta, _ = chebyshev_scalars()

    def set_up(i, carry):
        v, p = vk[i + 1], phi[i + 1]
        total = 0.5 * (v + vk[i]) * (p - phi[i]) + 0.5 * (v + vk[i + 2]) * (p - phi[i + 2])
        for axis, step in enumerate((phi_y, phi_z)):
            flow = 0.5 * (v + beyond(v, 1, axis)) * step[i]
            first = index_along(v.shape, axis) == 0
            total = total + flow + jnp.where(first, 0.5 * v * p, -shifted(flow, 1, axis))
        total = -(va[i] * p + total)
        b[i] = total
        buf_a[i + 1] = total * (1.0 / theta)
        return carry

    lax.fori_loop(0, planes, set_up, 0, unroll=8)
    found = solve(b, (buf_a, buf_b), diag, fx, fy, fz, UNROLL)
    owned = owned_rows((rows, lanes), HALO * y, 2 * cy)

    def add_up(i, carry):
        u = found[i + 1]
        change[i] = u
        part = jnp.where(owned, count[i], 0.0) * u
        return carry[0] + folded(part), carry[1] + folded(part * phi[i + 1])

    zero = jnp.zeros((8, lanes), jnp.float32)
    seen, cross = lax.fori_loop(0, planes, add_up, (zero, zero), unroll=8)
    first = (2 * cy - HALO) * (1 - y) + HALO * y
    size = GROUP * REACH
    for g in range(planes // GROUP):
        message[pl.ds(size * g, size), :] = packed_edges(
            [near_rows(found, 1 + GROUP * g + j, first, y) for j in range(GROUP)]
        )
    rows_of_sums = [jnp.sum(part, axis=0, keepdims=True) for part in (sums[0], seen, cross, sums[1])]
    message[pl.ds(REACH * planes, 8), :] = jnp.concatenate([*rows_of_sums, zero[:4]], axis=0)


def second_kernel(
    phi, phi_y, phi_z, change, diag, fx, fy, fz, count, sent, came,
    own, message,
    b, buf_a, buf_b, grad_k, grad_a,
    *, dets,
):
    _, _, y, c = places(2)
    planes, rows, lanes = change.shape
    cy = (rows - HALO) // 2
    base = HALO * y
    edge = pl.ds(2 * cy * (1 - y), HALO)
    tail = pl.ds(REACH * planes, 8)
    sums = jnp.sum(sent[tail, :] + came[tail, :], axis=1, keepdims=True)
    total, seen_sum, cross, square = (sums[g : g + 1] for g in range(4))
    mean = total / dets
    part = seen_sum / total
    level = (cross - part * square) / (total * mean)
    inverse = 1.0 / mean
    blank_ends(buf_a, buf_b)
    theta, _ = chebyshev_scalars()

    def weighted(n, u, p):
        return n * (((u - p * part) * inverse - level) * inverse)

    def set_up(i, carry):
        value = weighted(count[i], change[i], phi[i + 1])
        b[i] = value
        buf_a[i + 1] = value * (1.0 / theta)
        return carry

    lax.fori_loop(0, planes, set_up, 0, unroll=8)
    size = GROUP * REACH
    for i in range(planes):
        u = edge_tile(came[pl.ds(size * (i // GROUP), size), :], i % GROUP, y)
        value = weighted(count[i, edge, :], u, phi[i + 1, edge, :])
        b[i, edge, :] = value
        buf_a[i + 1, edge, :] = value * (1.0 / theta)
    dual = solve(b, (buf_a, buf_b), diag, fx, fy, fz, UNROLL)

    def product(i, carry):
        p, u = phi[i + 1], dual[i + 1]
        grad = (p - phi[i]) * (u - dual[i]) + (p - phi[i + 2]) * (u - dual[i + 2])
        both = p * u
        for axis, step in enumerate((phi_y, phi_z)):
            flow = step[i] * (u - beyond(u, 1, axis))
            first = index_along(p.shape, axis) == 0
            grad = grad + flow + jnp.where(first, both, shifted(flow, 1, axis))
        grad_k[i] = -0.5 * grad
        grad_a[i] = -both
        for f, ref in enumerate((grad_k, grad_a)):
            own[f, i] = ref[i, pl.ds(base + cy * c, cy), :]
            message[f, i] = ref[i, pl.ds(base + cy * (1 - c), cy), :]
        return carry

    lax.fori_loop(0, planes, product, 0, unroll=8)


def packed_slabs(own, came, half, out):
    s, _, _, _ = places(2)
    _, planes, cy, lanes = own.shape
    n, _, groups = out.shape[:3]
    slab = lanes // n
    block = index_along((cy, lanes), 1) // slab
    for f in range(2):
        for q in range(groups):
            at = planes // 2 * half + n * q
            parts = [own[f, at + j] + came[f, at + j] for j in range(n)]
            size = n // 2
            while size:
                low = block & size == 0
                for j in range(n):
                    if not j & size:
                        a, b = parts[j], parts[j | size]
                        parts[j] = jnp.where(low, a, shifted(b, size * slab, 1))
                        parts[j | size] = jnp.where(low, shifted(a, -size * slab, 1), b)
                size //= 2
            for t in range(n):
                out[s ^ t, f, q] = parts[t]


def send_kernel(own, came, *refs):
    _, x, _, _ = places(2)
    outs, packed = refs[:-1], refs[-1]
    packed_slabs(own, came, 1 - x, packed)
    for k, out in enumerate(outs):
        out[0] = packed[k]


def keep_kernel(own, came, kept):
    _, x, _, _ = places(2)
    packed_slabs(own, came, x, kept)


def add_kernel(kept, came, out, *, k):
    out[...] = kept[k] + came[0]


def sum_kernel(*refs):
    total = refs[0][...]
    for ref in refs[1:-1]:
        total = total + ref[...]
    refs[-1][...] = total


def project_kernel(*refs, parts_n, n):
    beta_prev = refs[0]
    parts = refs[1 : 1 + parts_n]
    vk, va, qk, qa, w_k, w_a, tile = refs[1 + parts_n :]
    slab = 128 // n
    for f, (q_ref, w) in enumerate(((qk, w_k), (qa, w_a))):
        for q in range(vk.shape[0] // n):
            whole = sum(part[f, q] for part in parts[1:]) + parts[0][f, q]
            for j in range(n):
                i = n * q + j
                w[i] = whole[:, slab * j : slab * (j + 1)] - beta_prev[:, : vk.shape[2]] * q_ref[i]

    def total(value):
        return jnp.sum(jnp.sum(jnp.sum(value, axis=0), axis=0, keepdims=True), axis=1, keepdims=True)

    wk, wa, v_k, v_a = w_k[...], w_a[...], vk[...], va[...]
    wv = total(wk * v_k + wa * v_a)
    vv = total(v_k * v_k + v_a * v_a)
    a = jnp.where(vv > 0.0, wv / jnp.where(vv > 0.0, vv, 1.0), 0.0)
    u_k, u_a = wk - a * v_k, wa - a * v_a
    uv = total(u_k * v_k + u_a * v_a)
    uu = total(u_k * u_k + u_a * u_a)
    lane = index_along((1, 128), 1)
    values = jnp.zeros((1, 128), jnp.float32)
    for i, value in enumerate((wv, vv, a, uv, uu)):
        values = jnp.where(lane == i, value, values)
    tile[...] = values


def final_kernel(tiles, w_k, w_a, vk, va, next_k, next_a, coefs, *, cells):
    tile = jnp.concatenate([tiles[i] for i in range(tiles.shape[0])], axis=0)
    wv, vv, a, uv, uu = (tile[:, i : i + 1] for i in range(5))
    wv_sum = jnp.sum(wv, axis=0, keepdims=True)
    vv_sum = jnp.sum(vv, axis=0, keepdims=True)
    alpha = wv_sum / cells / (vv_sum / cells + eps_norm)
    off = alpha - a
    rr = jnp.sum(uu - 2.0 * off * uv + off * (off * vv), axis=0, keepdims=True)
    beta = jnp.sqrt(rr / cells + eps_norm)
    next_k[...] = (w_k[...] - alpha * vk[...]) / beta
    next_a[...] = (w_a[...] - alpha * va[...]) / beta
    coefs[0] = jnp.sum(alpha)
    coefs[1] = jnp.sum(beta)


def f32(*shape):
    return jax.ShapeDtypeStruct(shape, jnp.float32)


def run(kernel, outs, *args, after=(), scratch=(), copies=0, smem=(), hbm=(), mib=16, in_smem_out=(), cost=None):
    vmem = pl.BlockSpec(memory_space=pltpu.VMEM)
    scalar = pl.BlockSpec(memory_space=pltpu.SMEM)
    far = pl.BlockSpec(memory_space=pltpu.HBM)
    held = [pltpu.VMEM(shape, dtype) for shape, dtype in scratch]
    used, waits = len(args), len(after)

    def body(*refs):
        kernel(*refs[:used], *refs[used + waits :])

    args = (*args, *after)
    if copies:
        held.append(pltpu.SemaphoreType.DMA((copies,)))
    return pl.pallas_call(
        body if waits else kernel,
        out_shape=tuple(outs),
        in_specs=[scalar if i in smem else far if i in hbm else vmem for i in range(len(args))],
        out_specs=tuple(scalar if i in in_smem_out else vmem for i in range(len(outs))),
        scratch_shapes=held,
        compiler_params=pltpu.CompilerParams(vmem_limit_bytes=mib * 2**20),
        cost_estimate=cost,
    )(*args)


HALO = 8
UNROLL = 16
REACH = 6
GROUP = 4


def per_device_paired(
    labels, kappa_table, absorb_table, background, det_cells,
    v_kappa, v_absorb, q_kappa, q_absorb, beta_prev,
):
    sources, cx, cy, cz = background.shape
    n = lax.axis_size("src")
    planes, rows = 2 * cx, 2 * cy + HALO
    ny = cy * lax.axis_size("gy")
    dets = det_cells.shape[0]
    cells = planes * ny * cz
    groups = cx // n

    def swap_x(value):
        return lax.ppermute(value, "gx", [(0, 1), (1, 0)])

    def swap_core(value):
        return lax.ppermute(value, "gy", [(0, 1), (1, 0), (2, 3), (3, 2)])

    def along_z(value, k):
        return lax.ppermute(value, "src", [(i, i ^ k) for i in range(n)])

    block = (cx, cy, cz)
    float_block = lambda *shape: (shape, jnp.float32)
    raw_labels = (block, jnp.int32)
    packed, message = run(
        pack_kernel, (f32(2 * groups, cy, cz), f32(sources // 2 * cx + 2 * groups, cy, cz)),
        background, v_kappa, v_absorb, hbm=(0, 1, 2),
        scratch=(float_block(2, *v_kappa.shape),), copies=2 + sources // 2, mib=60,
    )
    long = pl.CostEstimate(flops=10**9, bytes_accessed=2**26, transcendentals=0)
    labels_came = swap_x(labels)
    came = swap_x(message)
    slabs = [along_z(packed, k) for k in range(1, n)]
    count, beta_row = run(
        functools.partial(count_kernel, ny=ny, nz=cz, half=2 * cy, halo=HALO),
        (f32(planes, rows, cz), f32(1, cz)), det_cells.reshape(1, dets), beta_prev, smem=(1,), after=(labels_came,),
        cost=pl.CostEstimate(flops=2 * planes * rows * cz * dets, bytes_accessed=planes * rows * cz * 4, transcendentals=0),
    )

    def across_y(value):
        return lax.ppermute(value, "gy", [(i, (i + 2) % 4) for i in range(4)])

    (joined,) = run(join_kernel, (f32(2 * groups * (n - 1), cy, cz),), *slabs, after=(count,))
    joined_came = swap_x(joined)
    (half_vector,) = run(own_half_kernel, (f32(2, *block),), v_kappa, v_absorb, joined)
    mine, fields = run(
        photon_kernel, (f32(planes, cy, cz), f32(2, planes, cy, cz)),
        background, labels, came, labels_came, after=(joined,), hbm=(0, 1), scratch=(raw_labels,), copies=3,
    )
    got = swap_core(fields)
    (vector,) = run(
        vector_kernel, (f32(2, planes, cy, cz),), half_vector, came, joined_came, after=(mine,)
    )
    edge = (f32(2, *edge_shape(planes, cz)),)
    (sent,) = run(photon_edge_kernel, edge, mine, fields, got, after=(vector,))
    photon_edge = across_y(sent)
    vector_got = swap_core(vector)
    (vector_sent,) = run(vector_edge_kernel, edge, vector, vector_got, after=(sent,))
    frame, wide = (planes, rows, cz), (planes + 2, rows, cz)
    float_frame, float_wide = float_block(*frame), float_block(*wide)
    coefs = (f32(*frame), f32(planes + 1, rows, cz), f32(*frame), f32(*frame))
    kap, *partial, sums = run(
        stencil_kernel, (f32(*wide), *coefs, f32(2, 8, cz)),
        kappa_table, absorb_table, mine, fields, got, count, after=(vector_sent,), cost=long,
        smem=(0, 1), scratch=(float_frame,),
    )
    diag, fx, fy, fz = run(
        halo_kernel, coefs, kappa_table, absorb_table, photon_edge, kap, *partial, smem=(0, 1)
    )
    densities = run(
        density_kernel, (f32(*wide), f32(*frame), f32(*frame)), mine, got, photon_edge, after=(fz,)
    )
    change, sent = run(
        first_kernel, (f32(*frame), f32(REACH * planes + 8, cz)),
        *densities, diag, fx, fy, fz, count, sums, vector, vector_got, across_y(vector_sent),
        scratch=(float_wide, float_frame, float_frame, float_wide, float_wide),
    )
    heard = across_y(sent)
    own, message = run(
        functools.partial(second_kernel, dets=dets),
        (f32(2, planes, cy, cz), f32(2, planes, cy, cz)),
        *densities, change, diag, fx, fy, fz, count, sent, heard,
        scratch=(float_frame, float_wide, float_wide, float_frame, float_frame),
    )
    piece = f32(2, groups, cy, cz)
    got = swap_core(message)
    last = run(
        send_kernel, [f32(1, *piece.shape)] * n, own, got, scratch=(float_block(n, *piece.shape),)
    )
    crossed = {k: swap_x(last[k]) for k in reversed(range(n))}
    (kept,) = run(keep_kernel, (f32(n, *piece.shape),), own, got, after=(last[0],))
    totals = {
        k: run(functools.partial(add_kernel, k=k), (piece,), kept, value)[0] for k, value in crossed.items()
    }
    received = {k: along_z(totals[k], k) for k in reversed(range(1, n))}
    (distant,) = run(sum_kernel, (piece,), *(received[k] for k in range(n // 2, n)), cost=long)
    parts = [distant, totals[0]] + [received[k] for k in range(1, n // 2)]
    w_k, w_a, tile = run(
        functools.partial(project_kernel, parts_n=len(parts), n=n),
        (f32(*v_kappa.shape), f32(*v_kappa.shape), f32(1, 128)),
        beta_row, *parts, v_kappa, v_absorb, q_kappa, q_absorb,
    )
    everyone = ("src", "gx", "gy")
    tiles = lax.all_to_all(jnp.broadcast_to(tile, (8 * n, 1, 128)), everyone, 0, 0)
    return tuple(run(
        functools.partial(final_kernel, cells=cells),
        (f32(*v_kappa.shape), f32(*v_kappa.shape), f32(2)),
        tiles, w_k, w_a, v_kappa, v_absorb, in_smem_out=(2,),
    ))


def paired_fits(mesh):
    return mesh.shape["gx"] == 2 and mesh.shape["gy"] == 4


def body_for(mesh):
    if not paired_fits(mesh):
        return per_device

    def chosen(*args):
        sources, cx, cy, cz = args[3].shape
        n = lax.axis_size("src")
        fits = sources == 4 and cz == 128 and cx % n == 0 and cx % GROUP == 0 and cy % HALO == 0 and n > 1 and n & (n - 1) == 0
        devices = 8 * n
        return (per_device_paired if fits and devices <= 128 else per_device)(*args)

    return chosen


def solution(mesh):
    return jax.shard_map(
        body_for(mesh),
        mesh=mesh,
        in_specs=(
            P("gx", "gy", None),
            P(),
            P(),
            P("src", "gx", "gy", None),
            P(),
            P("gx", "gy", "src"),
            P("gx", "gy", "src"),
            P("gx", "gy", "src"),
            P("gx", "gy", "src"),
            P(),
        ),
        out_specs=(P("gx", "gy", "src"), P("gx", "gy", "src"), P()),
        check_vma=False,
    )
```

```python
import functools

import jax
import jax.numpy as jnp
from jax import lax
from jax.experimental import pallas as pl
from jax.experimental.pallas import tpu as pltpu
from jax.sharding import PartitionSpec as P

ITERS = 6


lam_low = 0.02
lam_high = 24.1
eps_norm = 1e-06


def padded_2(block, sides, width):
    for axis, dim in sides:
        count = lax.axis_size(axis)
        forward = [(i, i + 1) for i in range(count - 1)]
        backward = [(target, source) for source, target in forward]
        low = lax.ppermute(
            lax.slice_in_dim(block, block.shape[dim] - width, None, axis=dim), axis, forward
        )
        high = lax.ppermute(lax.slice_in_dim(block, 0, width, axis=dim), axis, backward)
        block = jnp.concatenate([low, block, high], axis=dim)
    return block


def regional(labels, table):
    field = jnp.zeros(labels.shape, jnp.float32)
    for region in range(table.shape[0]):
        field = field + jnp.where(labels == region, table[region], 0.0)
    return field


def beside(padded):
    widths = [(0, 0)] * (padded.ndim - 1) + [(1, 1)]
    full = jnp.pad(padded, widths)
    return [
        full[..., 2:, 1:-1, 1:-1],
        full[..., :-2, 1:-1, 1:-1],
        full[..., 1:-1, 2:, 1:-1],
        full[..., 1:-1, :-2, 1:-1],
        full[..., 1:-1, 1:-1, 2:],
        full[..., 1:-1, 1:-1, :-2],
    ]


def chebyshev(rhs, apply_op):
    theta = 0.5 * (lam_high + lam_low)
    delta = 0.5 * (lam_high - lam_low)
    sigma = theta / delta
    rho = 1.0 / sigma
    solution = jnp.zeros_like(rhs)
    remain = rhs
    step_dir = rhs / theta
    for step in range(ITERS):
        solution = solution + step_dir
        if step + 1 < ITERS:
            remain = remain - apply_op(step_dir)
            rho_next = 1.0 / (2.0 * sigma - rho)
            step_dir = rho_next * rho * step_dir + 2.0 * rho_next / delta * remain
            rho = rho_next
    return solution


def per_device(
    labels,
    kappa_table,
    absorb_table,
    background,
    det_cells,
    v_kappa,
    v_absorb,
    q_kappa,
    q_absorb,
    beta_prev,
):
    sources, cx, cy, cz = background.shape
    kappa = regional(labels, kappa_table)
    absorb = regional(labels, absorb_table)
    full_k, full_a = (
        lax.all_gather(v_kappa, "src", axis=2, tiled=True),
        lax.all_gather(v_absorb, "src", axis=2, tiled=True),
    )
    stacked = jnp.concatenate([background, kappa[None], full_k[None]], axis=0)
    rims = padded_2(stacked, (("gx", 1), ("gy", 2)), 1)
    near_all = beside(rims)
    kappa_faces = [0.5 * (kappa + near[sources]) for near in near_all]
    vk_faces = [0.5 * (full_k + near[sources + 1]) for near in near_all]
    phi_near = [near[:sources] for near in near_all]

    def apply_op(field):
        padded = padded_2(field, (("gx", 1), ("gy", 2)), 1)
        result = absorb * field
        for face, near in zip(kappa_faces, beside(padded)):
            result = result + face * (field - near)
        return result

    rhs = full_a * background
    for face, near in zip(vk_faces, phi_near):
        rhs = rhs + face * (background - near)
    rhs = -rhs
    change = chebyshev(rhs, apply_op)
    span_y = cy * lax.axis_size("gy")
    ix = det_cells // (span_y * cz)
    iy = det_cells // cz % span_y
    iz = det_cells % cz
    anchor_x = lax.axis_index("gx") * cx
    anchor_y = lax.axis_index("gy") * cy
    owned = (ix >= anchor_x) & (ix < anchor_x + cx) & (iy >= anchor_y) & (iy < anchor_y + cy)
    local = jnp.where(owned, ((ix - anchor_x) * cy + (iy - anchor_y)) * cz + iz, 0)
    seen_part = jnp.where(owned[None, :], change.reshape(sources, -1)[:, local], 0.0)
    base_part = jnp.where(owned[None, :], background.reshape(sources, -1)[:, local], 0.0)
    seen, base = lax.psum((seen_part, base_part), ("gx", "gy"))
    total = jnp.sum(base, axis=1, keepdims=True)
    mean_base = total / det_cells.shape[0]
    ratio = base / total
    jv_vals = (seen - ratio * jnp.sum(seen, axis=1, keepdims=True)) / mean_base
    weight = (jv_vals - jnp.sum(ratio * jv_vals, axis=1, keepdims=True)) / mean_base
    deposit = jnp.where(owned[None, :], weight, 0.0)
    source = (
        jnp.zeros((sources, cx * cy * cz), jnp.float32)
        .at[:, local]
        .add(deposit)
        .reshape(change.shape)
    )
    dual = chebyshev(source, apply_op)
    dual_rims = padded_2(dual, (("gx", 1), ("gy", 2)), 1)
    grad_a = -jnp.sum(background * dual, axis=0)
    grad_k = jnp.zeros_like(kappa)
    for near_phi, near_dual in zip(phi_near, beside(dual_rims)):
        grad_k = grad_k - 0.5 * jnp.sum((background - near_phi) * (dual - near_dual), axis=0)
    summed_k, summed_a = lax.psum((grad_k, grad_a), "src")
    slab = v_kappa.shape[2]
    offset = lax.axis_index("src") * slab
    hv_k = lax.dynamic_slice_in_dim(summed_k, offset, slab, 2)
    hv_a = lax.dynamic_slice_in_dim(summed_a, offset, slab, 2)
    cell_count = cx * lax.axis_size("gx") * cy * lax.axis_size("gy") * cz
    w_k = hv_k - beta_prev[0] * q_kappa
    w_a = hv_a - beta_prev[0] * q_absorb
    local_wv = jnp.sum(w_k * v_kappa) + jnp.sum(w_a * v_absorb)
    local_vv = jnp.sum(v_kappa * v_kappa) + jnp.sum(v_absorb * v_absorb)
    wv_sum, vv_sum = lax.psum((local_wv, local_vv), ("src", "gx", "gy"))
    alpha = wv_sum / cell_count / (vv_sum / cell_count + eps_norm)
    r_k = w_k - alpha * v_kappa
    r_a = w_a - alpha * v_absorb
    rr_sum = lax.psum(jnp.sum(r_k * r_k) + jnp.sum(r_a * r_a), ("src", "gx", "gy"))
    beta = jnp.sqrt(rr_sum / cell_count + eps_norm)
    return (r_k / beta, r_a / beta, jnp.stack([alpha, beta]))


def chebyshev_scalars():
    theta = 0.5 * (lam_high + lam_low)
    delta = 0.5 * (lam_high - lam_low)
    sigma = theta / delta
    rho = 1.0 / sigma
    pairs = []
    for _ in range(ITERS - 1):
        rho_next = 1.0 / (2.0 * sigma - rho)
        pairs.append((rho_next * rho, 2.0 * rho_next / delta))
        rho = rho_next
    return theta, pairs


def places(split):
    g = lax.axis_index("gy")
    return lax.axis_index("src"), lax.axis_index("gx"), g // split, g % split


def shifted(value, step, axis):
    return pltpu.roll(value, step % value.shape[axis], axis)


def index_along(shape, axis):
    return lax.broadcasted_iota(jnp.int32, shape, axis)


def beyond(value, step, axis):
    size = value.shape[axis]
    at = index_along(value.shape, axis)
    edge = size - 1 if step == 1 else 0
    return jnp.where(at == edge, 0.0, shifted(value, -step, axis))


def packed_planes(ref, q):
    per = 128 // ref.shape[2]
    return jnp.concatenate([ref[per * q + j] for j in range(per)], axis=1)


def pack_kernel(bg, vk, va, packed, message, v_in, sems):
    _, x, _, _ = places(2)
    half = bg.shape[0] // 2
    cx = bg.shape[1]
    copies = [
        pltpu.make_async_copy(src, dst, sems.at[i])
        for i, (src, dst) in enumerate((
            (vk, v_in.at[0]),
            (va, v_in.at[1]),
            *((bg.at[half * (1 - x) + i], message.at[pl.ds(cx * i, cx)]) for i in range(half)),
        ))
    ]
    for copy in copies:
        copy.start()
    groups = packed.shape[0] // 2
    for f in range(2):
        copies[f].wait()
        for q in range(groups):
            planes = packed_planes(v_in.at[f], q)
            packed[groups * f + q] = planes
            message[cx * half + groups * f + q] = planes
    for copy in copies[2:]:
        copy.wait()


def count_kernel(dets, beta_prev, count, beta_row, *, ny, nz, half, halo):
    beta_row[...] = jnp.full(beta_row.shape, beta_prev[0])
    _, _, y, _ = places(2)
    planes, rows, _ = count.shape
    flat = dets[...]
    iz = flat % nz
    line = flat // nz
    iy = line % ny
    ix = line // ny
    row = iy - (half - halo) * y
    spot = jnp.where((row >= 0) & (row < rows), ix * rows + row, -1)
    dets_n = flat.shape[1]
    at_z = (index_along((nz, dets_n), 0) == iz).astype(jnp.float32).astype(jnp.bfloat16)

    def body(i, carry):
        here = index_along((2 * rows, dets_n), 0) + i * (2 * rows)
        hot = (here == spot).astype(jnp.float32).astype(jnp.bfloat16)
        found = lax.dot_general(hot, at_z, (((1,), (1,)), ((), ())), preferred_element_type=jnp.float32)
        count[pl.ds(2 * i, 2)] = found.reshape(2, rows, nz)
        return carry

    lax.fori_loop(0, planes // 2, body, 0)


def photon_kernel(bg, labels, msg, labels_came, mine, fields, raw, sems):
    _, x, _, c = places(2)
    half = bg.shape[0] // 2
    cx = labels.shape[0]
    here, there = cx * x, cx * (1 - x)
    copies = [
        pltpu.make_async_copy(src, dst, sems.at[i])
        for i, (src, dst) in enumerate((
            (bg.at[half * x + c], mine.at[pl.ds(here, cx)]),
            (bg.at[half * x + 1 - c], fields.at[0, pl.ds(here, cx)]),
            (labels, raw),
        ))
    ]
    for copy in copies:
        copy.start()
    mine[pl.ds(there, cx)] = msg[pl.ds(cx * c, cx)]
    fields[0, pl.ds(there, cx)] = msg[pl.ds(cx * (1 - c), cx)]
    fields[1, pl.ds(there, cx)] = labels_came[...].astype(jnp.float32)
    for copy in copies:
        copy.wait()
    fields[1, pl.ds(here, cx)] = raw[...].astype(jnp.float32)


def unpacked(blocks, groups, s, store):
    n = len(blocks)
    cy, lanes = blocks[0][0].shape
    slab = lanes // n
    lane = index_along((cy, lanes), 1) // slab
    for f in range(2):
        for q in range(groups):
            values = [block[groups * f + q] for block in blocks]
            for j in range(n):
                plane = jnp.zeros((cy, lanes), jnp.float32)
                for k in range(n):
                    home = s ^ k
                    moved = pltpu.roll(values[k], ((home - j + n) % n) * slab, 1)
                    plane = jnp.where(lane == home, moved, plane)
                store(f, n * q + j, plane)


def join_kernel(*refs):
    joined, size = refs[-1], refs[0].shape[0]
    for i, ref in enumerate(refs[:-1]):
        joined[pl.ds(size * i, size)] = ref[...]


def own_half_kernel(vk, va, joined, half):
    s, _, _, _ = places(2)
    size = half.shape[1]
    groups = joined.shape[0] // 2 // (128 // vk.shape[2] - 1)
    n = size // groups
    own = [packed_planes(ref, q) for ref in (vk, va) for q in range(groups)]
    blocks = [own] + [[joined[2 * groups * k + i] for i in range(2 * groups)] for k in range(n - 1)]

    def store(f, i, plane):
        half[f, i] = plane

    unpacked(blocks, groups, s, store)


def vector_kernel(half, msg, joined, fields):
    s, x, _, _ = places(2)
    cx = half.shape[1]
    fields[:, pl.ds(cx * x, cx)] = half[...]
    n = lax.axis_size("src")
    groups = cx // n
    own = msg.shape[0] - 2 * groups
    blocks = [[msg[own + i] for i in range(2 * groups)]]
    blocks += [[joined[2 * groups * k + i] for i in range(2 * groups)] for k in range(n - 1)]
    there = cx * (1 - x)

    def store(f, i, plane):
        fields[f, there + i] = plane

    unpacked(blocks, groups, s, store)


def edge_shape(planes, lanes):
    return planes // GROUP, GROUP * REACH, lanes


def packed_edges(tiles):
    return jnp.concatenate([tile[:REACH] for tile in tiles], axis=0)


def edge_tile(packed, j, y):
    rows = packed[REACH * j : REACH * (j + 1)]
    tile = jnp.concatenate([rows, jnp.zeros((HALO - REACH, rows.shape[1]), jnp.float32)], axis=0)
    return jnp.where(y == 0, tile, shifted(tile, HALO - REACH, 0))


def near_rows(ref, i, first, y):
    tile = ref[i, pl.ds(first, HALO), :]
    return jnp.where(y == 0, shifted(tile, REACH - HALO, 0), tile)


def edges_of(own, got, edge, y, c):
    first = (own.shape[1] - HALO) * (1 - y)
    for g in range(edge.shape[0]):
        edge[g] = packed_edges([
            jnp.where(c != y, near_rows(own, GROUP * g + j, first, y), near_rows(got, GROUP * g + j, first, y))
            for j in range(GROUP)
        ])


def photon_edge_kernel(mine, fields, got, edge):
    _, _, y, c = places(2)
    edges_of(mine, got.at[0], edge.at[0], y, c)
    edges_of(fields.at[1], got.at[1], edge.at[1], y, c)


def vector_edge_kernel(fields, got, edge):
    _, _, y, c = places(2)
    for f in range(2):
        edges_of(fields.at[f], got.at[f], edge.at[f], y, c)


def solve(b, bufs, diag, fx, fy, fz, unroll):
    planes = b.shape[0]
    _, pairs = chebyshev_scalars()
    for step, (keep, push) in enumerate(pairs):
        src, dst = bufs[step % 2], bufs[(step + 1) % 2]

        def body(i, carry):
            u = src[i + 1]
            coef_y, coef_z = fy[i], fz[i]
            left = b[i] - diag[i] * u
            left = left + fx[i] * src[i] + fx[i + 1] * src[i + 2]
            left = left + coef_y * shifted(u, -1, 0) + shifted(coef_y * u, 1, 0)
            left = left + coef_z * shifted(u, -1, 1) + shifted(coef_z * u, 1, 1)
            change = u if step == 0 else u - dst[i + 1]
            dst[i + 1] = u + keep * change + push * left
            return carry

        lax.fori_loop(0, planes, body, 0, unroll=unroll)
    return bufs[len(pairs) % 2]


def folded(value):
    return jnp.sum(value.reshape(-1, 8, value.shape[1]), axis=0)


def framed_own(ref, shift, own, got, y, c):
    planes, cy, _ = own.shape
    there = pl.ds(shift, planes)
    base = HALO * y
    ref[there, pl.ds(base + cy * c, cy), :] = own[...]
    ref[there, pl.ds(base + cy * (1 - c), cy), :] = got[...]


def framed(ref, shift, own, got, edge, y, c):
    framed_own(ref, shift, own, got, y, c)
    cy = own.shape[1]
    for g in range(edge.shape[0]):
        packed = edge[g]
        for j in range(GROUP):
            ref[shift + GROUP * g + j, pl.ds(2 * cy * (1 - y), HALO), :] = edge_tile(packed, j, y)


def blank_ends(*refs):
    for ref in refs:
        blank = jnp.zeros(ref.shape[1:], jnp.float32)
        ref[0] = blank
        ref[ref.shape[0] - 1] = blank


def owned_rows(shape, base, count):
    at_row = index_along(shape, 0)
    return (at_row >= base) & (at_row < base + count)


def table_rows(kap_table, abs_table, shape):
    lane = index_along(shape, 1)
    kap_row = abs_row = jnp.zeros(shape, jnp.float32)
    for region in range(kap_table.shape[0]):
        kap_row = jnp.where(lane == region, kap_table[region], kap_row)
        abs_row = jnp.where(lane == region, abs_table[region], abs_row)
    return kap_row, abs_row


def stencil_kernel(
    kap_table, abs_table, mine, fields, got, count,
    kap, diag, fx, fy, fz, sums,
    labels,
):
    _, _, y, c = places(2)
    planes, cy, lanes = mine.shape
    rows = 2 * cy + HALO
    base = HALO * y
    framed_own(labels, 0, fields.at[1], got.at[1], y, c)
    labels[:, pl.ds(2 * cy * (1 - y), HALO), :] = jnp.zeros((planes, HALO, lanes), jnp.float32)
    blank_ends(kap)
    shape = (rows, lanes)
    lane = index_along(shape, 1)
    kap_row, abs_row = table_rows(kap_table, abs_table, shape)
    owned = owned_rows(shape, base, 2 * cy)

    def look_up(i, carry):
        at = labels[i].astype(jnp.int32)
        kap[i + 1] = jnp.where(owned, jnp.take_along_axis(kap_row, at, axis=1), 0.0)
        diag[i] = jnp.take_along_axis(abs_row, at, axis=1)
        return carry

    lax.fori_loop(0, planes, look_up, 0, unroll=4)
    fx[0] = 0.5 * kap[1]

    def set_up(i, carry):
        k = kap[i + 1]
        along_x = 0.5 * (k + kap[i + 2])
        along_y, along_z = 0.5 * (k + beyond(k, 1, 0)), 0.5 * (k + beyond(k, 1, 1))
        fx[i + 1] = along_x
        fy[i] = jnp.where(index_along(shape, 0) == rows - 1, 0.0, along_y)
        fz[i] = jnp.where(lane == lanes - 1, 0.0, along_z)
        back_y, back_z = 0.5 * (k + beyond(k, -1, 0)), 0.5 * (k + beyond(k, -1, 1))
        diag[i] = diag[i] + fx[i] + along_x + along_y + back_y + along_z + back_z
        total, square = carry
        for p, at in ((mine[i], c), (got[0, i], 1 - c)):
            part = count[i, pl.ds(base + cy * at, cy), :] * p
            total, square = total + folded(part), square + folded(part * p)
        return total, square

    zero = jnp.zeros((8, lanes), jnp.float32)
    sums[0], sums[1] = lax.fori_loop(0, planes, set_up, (zero, zero), unroll=4)


def halo_kernel(kap_table, abs_table, edge, kap, diag_in, fx_in, fy_in, fz_in, diag, fx, fy, fz):
    _, _, y, _ = places(2)
    planes, rows, lanes = diag.shape
    for ref, old in ((diag, diag_in), (fx, fx_in), (fy, fy_in), (fz, fz_in)):
        ref[...] = old[...]
    shape = (HALO, lanes)
    lane, row = index_along(shape, 1), index_along(shape, 0)
    kap_row, abs_row = table_rows(kap_table, abs_table, shape)
    low = y == 0
    here = pl.ds((rows - HALO) * (1 - y), HALO)
    beside_it = pl.ds((rows - 2 * HALO) * (1 - y) + HALO * y, HALO)
    labels = [edge_tile(edge[1, i // GROUP], i % GROUP, y).astype(jnp.int32) for i in range(planes)]
    tiles = [jnp.take_along_axis(kap_row, at, axis=1) for at in labels]
    none = jnp.zeros(shape, jnp.float32)
    before = 0.5 * tiles[0]
    fx[0, here, :] = before
    for i, k in enumerate(tiles):
        after = 0.5 * (k + (tiles[i + 1] if i + 1 < planes else none))
        own = kap[i + 1, beside_it, :]
        up, down = shifted(k, -1, 0), shifted(k, 1, 0)
        k_up = jnp.where(row == HALO - 1, jnp.where(low, 0.0, shifted(own, -1, 0)), up)
        k_down = jnp.where(row == 0, jnp.where(low, shifted(own, 1, 0), 0.0), down)
        along_y, back_y = 0.5 * (k + k_up), 0.5 * (k + k_down)
        along_z, back_z = 0.5 * (k + beyond(k, 1, 1)), 0.5 * (k + beyond(k, -1, 1))
        fx[i + 1, here, :] = after
        fy[i, here, :] = jnp.where(low & (row == HALO - 1), 0.0, along_y)
        fz[i, here, :] = jnp.where(lane == lanes - 1, 0.0, along_z)
        absorb = jnp.take_along_axis(abs_row, labels[i], axis=1)
        diag[i, here, :] = absorb + before + after + along_y + back_y + along_z + back_z
        before = after
        face_up = jnp.where(low & (row == HALO - 1), 0.5 * up, 0.0)
        face_down = jnp.where(low | (row > 0), 0.0, 0.5 * down)
        fy[i, beside_it, :] = fy_in[i, beside_it, :] + face_up
        diag[i, beside_it, :] = diag_in[i, beside_it, :] + face_up + face_down


def density_kernel(mine, got, edge, phi, phi_y, phi_z):
    _, _, y, c = places(2)
    framed(phi, 1, mine, got.at[0], edge.at[0], y, c)
    blank_ends(phi)

    def differ(i, carry):
        p = phi[i + 1]
        phi_y[i], phi_z[i] = p - beyond(p, 1, 0), p - beyond(p, 1, 1)
        return carry

    lax.fori_loop(0, phi_y.shape[0], differ, 0, unroll=4)


def first_kernel(
    phi, phi_y, phi_z, diag, fx, fy, fz, count, sums, vector, got_vector, edge,
    change, message,
    vk, va, b, buf_a, buf_b,
):
    _, _, y, c = places(2)
    planes, rows, lanes = change.shape
    cy = vector.shape[2]
    framed(vk, 1, vector.at[0], got_vector.at[0], edge.at[0], y, c)
    framed(va, 0, vector.at[1], got_vector.at[1], edge.at[1], y, c)
    blank_ends(vk, buf_a, buf_b)
    theta, _ = chebyshev_scalars()

    def set_up(i, carry):
        v, p = vk[i + 1], phi[i + 1]
        total = 0.5 * (v + vk[i]) * (p - phi[i]) + 0.5 * (v + vk[i + 2]) * (p - phi[i + 2])
        for axis, step in enumerate((phi_y, phi_z)):
            flow = 0.5 * (v + beyond(v, 1, axis)) * step[i]
            first = index_along(v.shape, axis) == 0
            total = total + flow + jnp.where(first, 0.5 * v * p, -shifted(flow, 1, axis))
        total = -(va[i] * p + total)
        b[i] = total
        buf_a[i + 1] = total * (1.0 / theta)
        return carry

    lax.fori_loop(0, planes, set_up, 0, unroll=8)
    found = solve(b, (buf_a, buf_b), diag, fx, fy, fz, UNROLL)
    owned = owned_rows((rows, lanes), HALO * y, 2 * cy)

    def add_up(i, carry):
        u = found[i + 1]
        change[i] = u
        part = jnp.where(owned, count[i], 0.0) * u
        return carry[0] + folded(part), carry[1] + folded(part * phi[i + 1])

    zero = jnp.zeros((8, lanes), jnp.float32)
    seen, cross = lax.fori_loop(0, planes, add_up, (zero, zero), unroll=UNROLL)
    first = (2 * cy - HALO) * (1 - y) + HALO * y
    size = GROUP * REACH
    for g in range(planes // GROUP):
        message[pl.ds(size * g, size), :] = packed_edges(
            [near_rows(found, 1 + GROUP * g + j, first, y) for j in range(GROUP)]
        )
    rows_of_sums = [jnp.sum(part, axis=0, keepdims=True) for part in (sums[0], seen, cross, sums[1])]
    message[pl.ds(REACH * planes, 8), :] = jnp.concatenate([*rows_of_sums, zero[:4]], axis=0)


def second_kernel(
    phi, phi_y, phi_z, change, diag, fx, fy, fz, count, sent, came,
    own, message,
    b, buf_a, buf_b, grad_k, grad_a,
    *, dets,
):
    _, _, y, c = places(2)
    planes, rows, lanes = change.shape
    cy = (rows - HALO) // 2
    base = HALO * y
    edge = pl.ds(2 * cy * (1 - y), HALO)
    tail = pl.ds(REACH * planes, 8)
    sums = jnp.sum(sent[tail, :] + came[tail, :], axis=1, keepdims=True)
    total, seen_sum, cross, square = (sums[g : g + 1] for g in range(4))
    mean = total / dets
    part = seen_sum / total
    level = (cross - part * square) / (total * mean)
    inverse = 1.0 / mean
    blank_ends(buf_a, buf_b)
    theta, _ = chebyshev_scalars()

    def weighted(n, u, p):
        return n * (((u - p * part) * inverse - level) * inverse)

    def set_up(i, carry):
        value = weighted(count[i], change[i], phi[i + 1])
        b[i] = value
        buf_a[i + 1] = value * (1.0 / theta)
        return carry

    lax.fori_loop(0, planes, set_up, 0, unroll=8)
    size = GROUP * REACH
    for i in range(planes):
        u = edge_tile(came[pl.ds(size * (i // GROUP), size), :], i % GROUP, y)
        value = weighted(count[i, edge, :], u, phi[i + 1, edge, :])
        b[i, edge, :] = value
        buf_a[i + 1, edge, :] = value * (1.0 / theta)
    dual = solve(b, (buf_a, buf_b), diag, fx, fy, fz, UNROLL)

    def product(i, carry):
        p, u = phi[i + 1], dual[i + 1]
        grad = (p - phi[i]) * (u - dual[i]) + (p - phi[i + 2]) * (u - dual[i + 2])
        both = p * u
        for axis, step in enumerate((phi_y, phi_z)):
            flow = step[i] * (u - beyond(u, 1, axis))
            first = index_along(p.shape, axis) == 0
            grad = grad + flow + jnp.where(first, both, shifted(flow, 1, axis))
        grad_k[i] = -0.5 * grad
        grad_a[i] = -both
        for f, ref in enumerate((grad_k, grad_a)):
            own[f, i] = ref[i, pl.ds(base + cy * c, cy), :]
            message[f, i] = ref[i, pl.ds(base + cy * (1 - c), cy), :]
        return carry

    lax.fori_loop(0, planes, product, 0, unroll=UNROLL)


def packed_slabs(own, came, half, choices, outs):
    s, _, _, _ = places(2)
    _, planes, cy, lanes = own.shape
    n = planes // 2 // outs.shape[2]
    slab = lanes // n
    lane = index_along((cy, lanes), 1) // slab
    for f in range(2):
        for q in range(outs.shape[2]):
            at = planes // 2 * half + n * q
            parts = [own[f, at + j] + came[f, at + j] for j in range(n)]
            for i, k in enumerate(choices):
                to = s ^ k
                piece = jnp.zeros((cy, lanes), jnp.float32)
                for j in range(n):
                    moved = pltpu.roll(parts[j], ((j - to + n) % n) * slab, 1)
                    piece = jnp.where(lane == j, moved, piece)
                outs[i, f, q] = piece


def send_kernel(own, came, out, *, k):
    _, x, _, _ = places(2)
    packed_slabs(own, came, 1 - x, (k,), out)


def keep_kernel(own, came, kept):
    _, x, _, _ = places(2)
    packed_slabs(own, came, x, range(kept.shape[0]), kept)


def add_kernel(kept, came, out, *, k):
    out[...] = kept[k] + came[0]


def sum_kernel(*refs):
    total = refs[0][...]
    for ref in refs[1:-1]:
        total = total + ref[...]
    refs[-1][...] = total


def project_kernel(*refs, parts_n, n):
    beta_prev = refs[0]
    parts = refs[1 : 1 + parts_n]
    vk, va, qk, qa, w_k, w_a, tile = refs[1 + parts_n :]
    slab = 128 // n
    for f, (q_ref, w) in enumerate(((qk, w_k), (qa, w_a))):
        for q in range(vk.shape[0] // n):
            whole = sum(part[f, q] for part in parts[1:]) + parts[0][f, q]
            for j in range(n):
                i = n * q + j
                w[i] = whole[:, slab * j : slab * (j + 1)] - beta_prev[:, : vk.shape[2]] * q_ref[i]

    def total(value):
        return jnp.sum(jnp.sum(jnp.sum(value, axis=0), axis=0, keepdims=True), axis=1, keepdims=True)

    wk, wa, v_k, v_a = w_k[...], w_a[...], vk[...], va[...]
    wv = total(wk * v_k + wa * v_a)
    vv = total(v_k * v_k + v_a * v_a)
    a = jnp.where(vv > 0.0, wv / jnp.where(vv > 0.0, vv, 1.0), 0.0)
    u_k, u_a = wk - a * v_k, wa - a * v_a
    uv = total(u_k * v_k + u_a * v_a)
    uu = total(u_k * u_k + u_a * u_a)
    lane = index_along((1, 128), 1)
    values = jnp.zeros((1, 128), jnp.float32)
    for i, value in enumerate((wv, vv, a, uv, uu)):
        values = jnp.where(lane == i, value, values)
    tile[...] = values


def final_kernel(tiles, w_k, w_a, vk, va, next_k, next_a, coefs, *, cells):
    tile = jnp.concatenate([tiles[i] for i in range(tiles.shape[0])], axis=0)
    wv, vv, a, uv, uu = (tile[:, i : i + 1] for i in range(5))
    wv_sum = jnp.sum(wv, axis=0, keepdims=True)
    vv_sum = jnp.sum(vv, axis=0, keepdims=True)
    alpha = wv_sum / cells / (vv_sum / cells + eps_norm)
    off = alpha - a
    rr = jnp.sum(uu - 2.0 * off * uv + off * (off * vv), axis=0, keepdims=True)
    beta = jnp.sqrt(rr / cells + eps_norm)
    next_k[...] = (w_k[...] - alpha * vk[...]) / beta
    next_a[...] = (w_a[...] - alpha * va[...]) / beta
    coefs[0] = jnp.sum(alpha)
    coefs[1] = jnp.sum(beta)


def f32(*shape):
    return jax.ShapeDtypeStruct(shape, jnp.float32)


def run(kernel, outs, *args, after=(), scratch=(), copies=0, smem=(), hbm=(), mib=16, in_smem_out=(), cost=None):
    vmem = pl.BlockSpec(memory_space=pltpu.VMEM)
    scalar = pl.BlockSpec(memory_space=pltpu.SMEM)
    far = pl.BlockSpec(memory_space=pltpu.HBM)
    held = [pltpu.VMEM(shape, dtype) for shape, dtype in scratch]
    used, waits = len(args), len(after)

    def body(*refs):
        kernel(*refs[:used], *refs[used + waits :])

    args = (*args, *after)
    if copies:
        held.append(pltpu.SemaphoreType.DMA((copies,)))
    return pl.pallas_call(
        body if waits else kernel,
        out_shape=tuple(outs),
        in_specs=[scalar if i in smem else far if i in hbm else vmem for i in range(len(args))],
        out_specs=tuple(scalar if i in in_smem_out else vmem for i in range(len(outs))),
        scratch_shapes=held,
        compiler_params=pltpu.CompilerParams(vmem_limit_bytes=mib * 2**20),
        cost_estimate=cost,
    )(*args)


HALO = 8
UNROLL = 16
REACH = 6
GROUP = 4


def per_device_paired(
    labels, kappa_table, absorb_table, background, det_cells,
    v_kappa, v_absorb, q_kappa, q_absorb, beta_prev,
):
    sources, cx, cy, cz = background.shape
    n = lax.axis_size("src")
    planes, rows = 2 * cx, 2 * cy + HALO
    ny = cy * lax.axis_size("gy")
    dets = det_cells.shape[0]
    cells = planes * ny * cz
    groups = cx // n

    def swap_x(value):
        return lax.ppermute(value, "gx", [(0, 1), (1, 0)])

    def swap_core(value):
        return lax.ppermute(value, "gy", [(0, 1), (1, 0), (2, 3), (3, 2)])

    def along_z(value, k):
        return lax.ppermute(value, "src", [(i, i ^ k) for i in range(n)])

    block = (cx, cy, cz)
    float_block = lambda *shape: (shape, jnp.float32)
    raw_labels = (block, jnp.int32)
    packed, message = run(
        pack_kernel, (f32(2 * groups, cy, cz), f32(sources // 2 * cx + 2 * groups, cy, cz)),
        background, v_kappa, v_absorb, hbm=(0, 1, 2),
        scratch=(float_block(2, *v_kappa.shape),), copies=2 + sources // 2, mib=60,
    )
    long = pl.CostEstimate(flops=10**9, bytes_accessed=2**26, transcendentals=0)
    labels_came = swap_x(labels)
    came = swap_x(message)
    slabs = [along_z(packed, k) for k in range(1, n)]
    count, beta_row = run(
        functools.partial(count_kernel, ny=ny, nz=cz, half=2 * cy, halo=HALO),
        (f32(planes, rows, cz), f32(1, cz)), det_cells.reshape(1, dets), beta_prev, smem=(1,), after=(labels_came,),
        cost=pl.CostEstimate(flops=2 * planes * rows * cz * dets, bytes_accessed=planes * rows * cz * 4, transcendentals=0),
    )

    def across_y(value):
        return lax.ppermute(value, "gy", [(i, (i + 2) % 4) for i in range(4)])

    (joined,) = run(join_kernel, (f32(2 * groups * (n - 1), cy, cz),), *slabs, after=(count,))
    joined_came = swap_x(joined)
    (half_vector,) = run(own_half_kernel, (f32(2, *block),), v_kappa, v_absorb, joined)
    mine, fields = run(
        photon_kernel, (f32(planes, cy, cz), f32(2, planes, cy, cz)),
        background, labels, came, labels_came, after=(joined,), hbm=(0, 1), scratch=(raw_labels,), copies=3,
    )
    got = swap_core(fields)
    (vector,) = run(
        vector_kernel, (f32(2, planes, cy, cz),), half_vector, came, joined_came, after=(mine,)
    )
    edge = (f32(2, *edge_shape(planes, cz)),)
    (sent,) = run(photon_edge_kernel, edge, mine, fields, got, after=(vector,))
    photon_edge = across_y(sent)
    vector_got = swap_core(vector)
    (vector_sent,) = run(vector_edge_kernel, edge, vector, vector_got, after=(sent,))
    frame, wide = (planes, rows, cz), (planes + 2, rows, cz)
    float_frame, float_wide = float_block(*frame), float_block(*wide)
    coefs = (f32(*frame), f32(planes + 1, rows, cz), f32(*frame), f32(*frame))
    kap, *partial, sums = run(
        stencil_kernel, (f32(*wide), *coefs, f32(2, 8, cz)),
        kappa_table, absorb_table, mine, fields, got, count, after=(vector_sent,), cost=long,
        smem=(0, 1), scratch=(float_frame,),
    )
    diag, fx, fy, fz = run(
        halo_kernel, coefs, kappa_table, absorb_table, photon_edge, kap, *partial, smem=(0, 1)
    )
    densities = run(
        density_kernel, (f32(*wide), f32(*frame), f32(*frame)), mine, got, photon_edge, after=(fz,)
    )
    change, sent = run(
        first_kernel, (f32(*frame), f32(REACH * planes + 8, cz)),
        *densities, diag, fx, fy, fz, count, sums, vector, vector_got, across_y(vector_sent),
        scratch=(float_wide, float_frame, float_frame, float_wide, float_wide),
    )
    heard = across_y(sent)
    own, message = run(
        functools.partial(second_kernel, dets=dets),
        (f32(2, planes, cy, cz), f32(2, planes, cy, cz)),
        *densities, change, diag, fx, fy, fz, count, sent, heard,
        scratch=(float_frame, float_wide, float_wide, float_frame, float_frame),
    )
    piece = f32(2, groups, cy, cz)
    got = swap_core(message)
    crossed, last = {}, ()
    for k in reversed(range(n)):
        last = run(functools.partial(send_kernel, k=k), (f32(1, *piece.shape),), own, got, after=last)
        crossed[k] = swap_x(last[0])
    (kept,) = run(keep_kernel, (f32(n, *piece.shape),), own, got, after=last)
    totals = {
        k: run(functools.partial(add_kernel, k=k), (piece,), kept, value)[0] for k, value in crossed.items()
    }
    received = {k: along_z(totals[k], k) for k in reversed(range(1, n))}
    (distant,) = run(sum_kernel, (piece,), *(received[k] for k in range(n // 2, n)), cost=long)
    parts = [distant, totals[0]] + [received[k] for k in range(1, n // 2)]
    w_k, w_a, tile = run(
        functools.partial(project_kernel, parts_n=len(parts), n=n),
        (f32(*v_kappa.shape), f32(*v_kappa.shape), f32(1, 128)),
        beta_row, *parts, v_kappa, v_absorb, q_kappa, q_absorb,
    )
    everyone = ("src", "gx", "gy")
    tiles = lax.all_to_all(jnp.broadcast_to(tile, (8 * n, 1, 128)), everyone, 0, 0)
    return tuple(run(
        functools.partial(final_kernel, cells=cells),
        (f32(*v_kappa.shape), f32(*v_kappa.shape), f32(2)),
        tiles, w_k, w_a, v_kappa, v_absorb, in_smem_out=(2,),
    ))


def paired_fits(mesh):
    return mesh.shape["gx"] == 2 and mesh.shape["gy"] == 4


def body_for(mesh):
    if not paired_fits(mesh):
        return per_device

    def chosen(*args):
        sources, cx, cy, cz = args[3].shape
        n = lax.axis_size("src")
        fits = sources == 4 and cz == 128 and cx % n == 0 and cx % GROUP == 0 and cy % HALO == 0 and n > 1 and n & (n - 1) == 0
        devices = 8 * n
        return (per_device_paired if fits and devices <= 128 else per_device)(*args)

    return chosen


def solution(mesh):
    return jax.shard_map(
        body_for(mesh),
        mesh=mesh,
        in_specs=(
            P("gx", "gy", None),
            P(),
            P(),
            P("src", "gx", "gy", None),
            P(),
            P("gx", "gy", "src"),
            P("gx", "gy", "src"),
            P("gx", "gy", "src"),
            P("gx", "gy", "src"),
            P(),
        ),
        out_specs=(P("gx", "gy", "src"), P("gx", "gy", "src"), P()),
        check_vma=False,
    )
```

```python
import functools

import jax
import jax.numpy as jnp
from jax import lax
from jax.experimental import pallas as pl
from jax.experimental.pallas import tpu as pltpu
from jax.sharding import PartitionSpec as P

ITERS = 6


lam_low = 0.02
lam_high = 24.1
eps_norm = 1e-06


def padded_2(block, sides, width):
    for axis, dim in sides:
        count = lax.axis_size(axis)
        forward = [(i, i + 1) for i in range(count - 1)]
        backward = [(target, source) for source, target in forward]
        low = lax.ppermute(
            lax.slice_in_dim(block, block.shape[dim] - width, None, axis=dim), axis, forward
        )
        high = lax.ppermute(lax.slice_in_dim(block, 0, width, axis=dim), axis, backward)
        block = jnp.concatenate([low, block, high], axis=dim)
    return block


def regional(labels, table):
    field = jnp.zeros(labels.shape, jnp.float32)
    for region in range(table.shape[0]):
        field = field + jnp.where(labels == region, table[region], 0.0)
    return field


def beside(padded):
    widths = [(0, 0)] * (padded.ndim - 1) + [(1, 1)]
    full = jnp.pad(padded, widths)
    return [
        full[..., 2:, 1:-1, 1:-1],
        full[..., :-2, 1:-1, 1:-1],
        full[..., 1:-1, 2:, 1:-1],
        full[..., 1:-1, :-2, 1:-1],
        full[..., 1:-1, 1:-1, 2:],
        full[..., 1:-1, 1:-1, :-2],
    ]


def chebyshev(rhs, apply_op):
    theta = 0.5 * (lam_high + lam_low)
    delta = 0.5 * (lam_high - lam_low)
    sigma = theta / delta
    rho = 1.0 / sigma
    solution = jnp.zeros_like(rhs)
    remain = rhs
    step_dir = rhs / theta
    for step in range(ITERS):
        solution = solution + step_dir
        if step + 1 < ITERS:
            remain = remain - apply_op(step_dir)
            rho_next = 1.0 / (2.0 * sigma - rho)
            step_dir = rho_next * rho * step_dir + 2.0 * rho_next / delta * remain
            rho = rho_next
    return solution


def per_device(
    labels,
    kappa_table,
    absorb_table,
    background,
    det_cells,
    v_kappa,
    v_absorb,
    q_kappa,
    q_absorb,
    beta_prev,
):
    sources, cx, cy, cz = background.shape
    kappa = regional(labels, kappa_table)
    absorb = regional(labels, absorb_table)
    full_k, full_a = (
        lax.all_gather(v_kappa, "src", axis=2, tiled=True),
        lax.all_gather(v_absorb, "src", axis=2, tiled=True),
    )
    stacked = jnp.concatenate([background, kappa[None], full_k[None]], axis=0)
    rims = padded_2(stacked, (("gx", 1), ("gy", 2)), 1)
    near_all = beside(rims)
    kappa_faces = [0.5 * (kappa + near[sources]) for near in near_all]
    vk_faces = [0.5 * (full_k + near[sources + 1]) for near in near_all]
    phi_near = [near[:sources] for near in near_all]

    def apply_op(field):
        padded = padded_2(field, (("gx", 1), ("gy", 2)), 1)
        result = absorb * field
        for face, near in zip(kappa_faces, beside(padded)):
            result = result + face * (field - near)
        return result

    rhs = full_a * background
    for face, near in zip(vk_faces, phi_near):
        rhs = rhs + face * (background - near)
    rhs = -rhs
    change = chebyshev(rhs, apply_op)
    span_y = cy * lax.axis_size("gy")
    ix = det_cells // (span_y * cz)
    iy = det_cells // cz % span_y
    iz = det_cells % cz
    anchor_x = lax.axis_index("gx") * cx
    anchor_y = lax.axis_index("gy") * cy
    owned = (ix >= anchor_x) & (ix < anchor_x + cx) & (iy >= anchor_y) & (iy < anchor_y + cy)
    local = jnp.where(owned, ((ix - anchor_x) * cy + (iy - anchor_y)) * cz + iz, 0)
    seen_part = jnp.where(owned[None, :], change.reshape(sources, -1)[:, local], 0.0)
    base_part = jnp.where(owned[None, :], background.reshape(sources, -1)[:, local], 0.0)
    seen, base = lax.psum((seen_part, base_part), ("gx", "gy"))
    total = jnp.sum(base, axis=1, keepdims=True)
    mean_base = total / det_cells.shape[0]
    ratio = base / total
    jv_vals = (seen - ratio * jnp.sum(seen, axis=1, keepdims=True)) / mean_base
    weight = (jv_vals - jnp.sum(ratio * jv_vals, axis=1, keepdims=True)) / mean_base
    deposit = jnp.where(owned[None, :], weight, 0.0)
    source = (
        jnp.zeros((sources, cx * cy * cz), jnp.float32)
        .at[:, local]
        .add(deposit)
        .reshape(change.shape)
    )
    dual = chebyshev(source, apply_op)
    dual_rims = padded_2(dual, (("gx", 1), ("gy", 2)), 1)
    grad_a = -jnp.sum(background * dual, axis=0)
    grad_k = jnp.zeros_like(kappa)
    for near_phi, near_dual in zip(phi_near, beside(dual_rims)):
        grad_k = grad_k - 0.5 * jnp.sum((background - near_phi) * (dual - near_dual), axis=0)
    summed_k, summed_a = lax.psum((grad_k, grad_a), "src")
    slab = v_kappa.shape[2]
    offset = lax.axis_index("src") * slab
    hv_k = lax.dynamic_slice_in_dim(summed_k, offset, slab, 2)
    hv_a = lax.dynamic_slice_in_dim(summed_a, offset, slab, 2)
    cell_count = cx * lax.axis_size("gx") * cy * lax.axis_size("gy") * cz
    w_k = hv_k - beta_prev[0] * q_kappa
    w_a = hv_a - beta_prev[0] * q_absorb
    local_wv = jnp.sum(w_k * v_kappa) + jnp.sum(w_a * v_absorb)
    local_vv = jnp.sum(v_kappa * v_kappa) + jnp.sum(v_absorb * v_absorb)
    wv_sum, vv_sum = lax.psum((local_wv, local_vv), ("src", "gx", "gy"))
    alpha = wv_sum / cell_count / (vv_sum / cell_count + eps_norm)
    r_k = w_k - alpha * v_kappa
    r_a = w_a - alpha * v_absorb
    rr_sum = lax.psum(jnp.sum(r_k * r_k) + jnp.sum(r_a * r_a), ("src", "gx", "gy"))
    beta = jnp.sqrt(rr_sum / cell_count + eps_norm)
    return (r_k / beta, r_a / beta, jnp.stack([alpha, beta]))


def chebyshev_scalars():
    theta = 0.5 * (lam_high + lam_low)
    delta = 0.5 * (lam_high - lam_low)
    sigma = theta / delta
    rho = 1.0 / sigma
    pairs = []
    for _ in range(ITERS - 1):
        rho_next = 1.0 / (2.0 * sigma - rho)
        pairs.append((rho_next * rho, 2.0 * rho_next / delta))
        rho = rho_next
    return theta, pairs


def places(split):
    g = lax.axis_index("gy")
    return lax.axis_index("src"), lax.axis_index("gx"), g // split, g % split


def shifted(value, step, axis):
    return pltpu.roll(value, step % value.shape[axis], axis)


def index_along(shape, axis):
    return lax.broadcasted_iota(jnp.int32, shape, axis)


def beyond(value, step, axis):
    size = value.shape[axis]
    at = index_along(value.shape, axis)
    edge = size - 1 if step == 1 else 0
    return jnp.where(at == edge, 0.0, shifted(value, -step, axis))


def packed_planes(ref, q):
    per = 128 // ref.shape[2]
    return jnp.concatenate([ref[per * q + j] for j in range(per)], axis=1)


def pack_kernel(bg, vk, va, packed, message, v_in, sems):
    _, x, _, _ = places(2)
    half = bg.shape[0] // 2
    cx = bg.shape[1]
    copies = [
        pltpu.make_async_copy(src, dst, sems.at[i])
        for i, (src, dst) in enumerate((
            (vk, v_in.at[0]),
            (va, v_in.at[1]),
            *((bg.at[half * (1 - x) + i], message.at[pl.ds(cx * i, cx)]) for i in range(half)),
        ))
    ]
    for copy in copies:
        copy.start()
    groups = packed.shape[0] // 2
    for f in range(2):
        copies[f].wait()
        for q in range(groups):
            planes = packed_planes(v_in.at[f], q)
            packed[groups * f + q] = planes
            message[cx * half + groups * f + q] = planes
    for copy in copies[2:]:
        copy.wait()


def count_kernel(dets, beta_prev, count, beta_row, *, ny, nz, half, halo):
    beta_row[...] = jnp.full(beta_row.shape, beta_prev[0])
    _, _, y, _ = places(2)
    planes, rows, _ = count.shape
    flat = dets[...]
    iz = flat % nz
    line = flat // nz
    iy = line % ny
    ix = line // ny
    row = iy - (half - halo) * y
    spot = jnp.where((row >= 0) & (row < rows), ix * rows + row, -1)
    dets_n = flat.shape[1]
    at_z = (index_along((nz, dets_n), 0) == iz).astype(jnp.float32).astype(jnp.bfloat16)

    def body(i, carry):
        here = index_along((2 * rows, dets_n), 0) + i * (2 * rows)
        hot = (here == spot).astype(jnp.float32).astype(jnp.bfloat16)
        found = lax.dot_general(hot, at_z, (((1,), (1,)), ((), ())), preferred_element_type=jnp.float32)
        count[pl.ds(2 * i, 2)] = found.reshape(2, rows, nz)
        return carry

    lax.fori_loop(0, planes // 2, body, 0)


def photon_kernel(bg, labels, msg, labels_came, mine, fields, raw, sems):
    _, x, _, c = places(2)
    half = bg.shape[0] // 2
    cx = labels.shape[0]
    here, there = cx * x, cx * (1 - x)
    copies = [
        pltpu.make_async_copy(src, dst, sems.at[i])
        for i, (src, dst) in enumerate((
            (bg.at[half * x + c], mine.at[pl.ds(here, cx)]),
            (bg.at[half * x + 1 - c], fields.at[0, pl.ds(here, cx)]),
            (labels, raw),
        ))
    ]
    for copy in copies:
        copy.start()
    mine[pl.ds(there, cx)] = msg[pl.ds(cx * c, cx)]
    fields[0, pl.ds(there, cx)] = msg[pl.ds(cx * (1 - c), cx)]
    fields[1, pl.ds(there, cx)] = labels_came[...].astype(jnp.float32)
    for copy in copies:
        copy.wait()
    fields[1, pl.ds(here, cx)] = raw[...].astype(jnp.float32)


def unpacked(blocks, groups, s, store):
    n = len(blocks)
    cy, lanes = blocks[0][0].shape
    slab = lanes // n
    lane = index_along((cy, lanes), 1) // slab
    for f in range(2):
        for q in range(groups):
            values = [block[groups * f + q] for block in blocks]
            for j in range(n):
                plane = jnp.zeros((cy, lanes), jnp.float32)
                for k in range(n):
                    home = s ^ k
                    moved = pltpu.roll(values[k], ((home - j + n) % n) * slab, 1)
                    plane = jnp.where(lane == home, moved, plane)
                store(f, n * q + j, plane)


def join_kernel(*refs):
    joined, size = refs[-1], refs[0].shape[0]
    for i, ref in enumerate(refs[:-1]):
        joined[pl.ds(size * i, size)] = ref[...]


def own_half_kernel(vk, va, joined, half):
    s, _, _, _ = places(2)
    size = half.shape[1]
    groups = joined.shape[0] // 2 // (128 // vk.shape[2] - 1)
    n = size // groups
    own = [packed_planes(ref, q) for ref in (vk, va) for q in range(groups)]
    blocks = [own] + [[joined[2 * groups * k + i] for i in range(2 * groups)] for k in range(n - 1)]

    def store(f, i, plane):
        half[f, i] = plane

    unpacked(blocks, groups, s, store)


def vector_kernel(half, msg, joined, fields):
    s, x, _, _ = places(2)
    cx = half.shape[1]
    fields[:, pl.ds(cx * x, cx)] = half[...]
    n = lax.axis_size("src")
    groups = cx // n
    own = msg.shape[0] - 2 * groups
    blocks = [[msg[own + i] for i in range(2 * groups)]]
    blocks += [[joined[2 * groups * k + i] for i in range(2 * groups)] for k in range(n - 1)]
    there = cx * (1 - x)

    def store(f, i, plane):
        fields[f, there + i] = plane

    unpacked(blocks, groups, s, store)


def edge_shape(planes, lanes):
    return planes // GROUP, GROUP * REACH, lanes


def packed_edges(tiles):
    return jnp.concatenate([tile[:REACH] for tile in tiles], axis=0)


def edge_tile(packed, j, y):
    rows = packed[REACH * j : REACH * (j + 1)]
    tile = jnp.concatenate([rows, jnp.zeros((HALO - REACH, rows.shape[1]), jnp.float32)], axis=0)
    return jnp.where(y == 0, tile, shifted(tile, HALO - REACH, 0))


def near_rows(ref, i, first, y):
    tile = ref[i, pl.ds(first, HALO), :]
    return jnp.where(y == 0, shifted(tile, REACH - HALO, 0), tile)


def edges_of(own, got, edge, y, c):
    first = (own.shape[1] - HALO) * (1 - y)
    for g in range(edge.shape[0]):
        edge[g] = packed_edges([
            jnp.where(c != y, near_rows(own, GROUP * g + j, first, y), near_rows(got, GROUP * g + j, first, y))
            for j in range(GROUP)
        ])


def photon_edge_kernel(mine, fields, got, edge):
    _, _, y, c = places(2)
    edges_of(mine, got.at[0], edge.at[0], y, c)
    edges_of(fields.at[1], got.at[1], edge.at[1], y, c)


def vector_edge_kernel(fields, got, edge):
    _, _, y, c = places(2)
    for f in range(2):
        edges_of(fields.at[f], got.at[f], edge.at[f], y, c)


def solve(b, bufs, diag, fx, fy, fz, unroll):
    planes = b.shape[0]
    _, pairs = chebyshev_scalars()
    for step, (keep, push) in enumerate(pairs):
        src, dst = bufs[step % 2], bufs[(step + 1) % 2]

        def body(i, carry):
            u = src[i + 1]
            coef_y, coef_z = fy[i], fz[i]
            left = b[i] - diag[i] * u
            left = left + fx[i] * src[i] + fx[i + 1] * src[i + 2]
            left = left + coef_y * shifted(u, -1, 0) + shifted(coef_y * u, 1, 0)
            left = left + coef_z * shifted(u, -1, 1) + shifted(coef_z * u, 1, 1)
            change = u if step == 0 else u - dst[i + 1]
            dst[i + 1] = u + keep * change + push * left
            return carry

        lax.fori_loop(0, planes, body, 0, unroll=unroll)
    return bufs[len(pairs) % 2]


def folded(value):
    return jnp.sum(value.reshape(-1, 8, value.shape[1]), axis=0)


def framed_own(ref, shift, own, got, y, c):
    planes, cy, _ = own.shape
    there = pl.ds(shift, planes)
    base = HALO * y
    ref[there, pl.ds(base + cy * c, cy), :] = own[...]
    ref[there, pl.ds(base + cy * (1 - c), cy), :] = got[...]


def framed(ref, shift, own, got, edge, y, c):
    framed_own(ref, shift, own, got, y, c)
    cy = own.shape[1]
    for g in range(edge.shape[0]):
        packed = edge[g]
        for j in range(GROUP):
            ref[shift + GROUP * g + j, pl.ds(2 * cy * (1 - y), HALO), :] = edge_tile(packed, j, y)


def blank_ends(*refs):
    for ref in refs:
        blank = jnp.zeros(ref.shape[1:], jnp.float32)
        ref[0] = blank
        ref[ref.shape[0] - 1] = blank


def owned_rows(shape, base, count):
    at_row = index_along(shape, 0)
    return (at_row >= base) & (at_row < base + count)


def table_rows(kap_table, abs_table, shape):
    lane = index_along(shape, 1)
    kap_row = abs_row = jnp.zeros(shape, jnp.float32)
    for region in range(kap_table.shape[0]):
        kap_row = jnp.where(lane == region, kap_table[region], kap_row)
        abs_row = jnp.where(lane == region, abs_table[region], abs_row)
    return kap_row, abs_row


def stencil_kernel(
    kap_table, abs_table, mine, fields, got, count,
    kap, diag, fx, fy, fz, sums,
    labels,
):
    _, _, y, c = places(2)
    planes, cy, lanes = mine.shape
    rows = 2 * cy + HALO
    base = HALO * y
    framed_own(labels, 0, fields.at[1], got.at[1], y, c)
    labels[:, pl.ds(2 * cy * (1 - y), HALO), :] = jnp.zeros((planes, HALO, lanes), jnp.float32)
    blank_ends(kap)
    shape = (rows, lanes)
    lane = index_along(shape, 1)
    kap_row, abs_row = table_rows(kap_table, abs_table, shape)
    owned = owned_rows(shape, base, 2 * cy)

    def look_up(i, carry):
        at = labels[i].astype(jnp.int32)
        kap[i + 1] = jnp.where(owned, jnp.take_along_axis(kap_row, at, axis=1), 0.0)
        diag[i] = jnp.take_along_axis(abs_row, at, axis=1)
        return carry

    lax.fori_loop(0, planes, look_up, 0, unroll=4)
    fx[0] = 0.5 * kap[1]

    def set_up(i, carry):
        k = kap[i + 1]
        along_x = 0.5 * (k + kap[i + 2])
        along_y, along_z = 0.5 * (k + beyond(k, 1, 0)), 0.5 * (k + beyond(k, 1, 1))
        fx[i + 1] = along_x
        fy[i] = jnp.where(index_along(shape, 0) == rows - 1, 0.0, along_y)
        fz[i] = jnp.where(lane == lanes - 1, 0.0, along_z)
        back_y, back_z = 0.5 * (k + beyond(k, -1, 0)), 0.5 * (k + beyond(k, -1, 1))
        diag[i] = diag[i] + fx[i] + along_x + along_y + back_y + along_z + back_z
        total, square = carry
        for p, at in ((mine[i], c), (got[0, i], 1 - c)):
            part = count[i, pl.ds(base + cy * at, cy), :] * p
            total, square = total + folded(part), square + folded(part * p)
        return total, square

    zero = jnp.zeros((8, lanes), jnp.float32)
    sums[0], sums[1] = lax.fori_loop(0, planes, set_up, (zero, zero), unroll=4)


def halo_kernel(kap_table, abs_table, edge, kap, diag_in, fx_in, fy_in, fz_in, diag, fx, fy, fz):
    _, _, y, _ = places(2)
    planes, rows, lanes = diag.shape
    for ref, old in ((diag, diag_in), (fx, fx_in), (fy, fy_in), (fz, fz_in)):
        ref[...] = old[...]
    shape = (HALO, lanes)
    lane, row = index_along(shape, 1), index_along(shape, 0)
    kap_row, abs_row = table_rows(kap_table, abs_table, shape)
    low = y == 0
    here = pl.ds((rows - HALO) * (1 - y), HALO)
    beside_it = pl.ds((rows - 2 * HALO) * (1 - y) + HALO * y, HALO)
    labels = [edge_tile(edge[1, i // GROUP], i % GROUP, y).astype(jnp.int32) for i in range(planes)]
    tiles = [jnp.take_along_axis(kap_row, at, axis=1) for at in labels]
    none = jnp.zeros(shape, jnp.float32)
    before = 0.5 * tiles[0]
    fx[0, here, :] = before
    for i, k in enumerate(tiles):
        after = 0.5 * (k + (tiles[i + 1] if i + 1 < planes else none))
        own = kap[i + 1, beside_it, :]
        up, down = shifted(k, -1, 0), shifted(k, 1, 0)
        k_up = jnp.where(row == HALO - 1, jnp.where(low, 0.0, shifted(own, -1, 0)), up)
        k_down = jnp.where(row == 0, jnp.where(low, shifted(own, 1, 0), 0.0), down)
        along_y, back_y = 0.5 * (k + k_up), 0.5 * (k + k_down)
        along_z, back_z = 0.5 * (k + beyond(k, 1, 1)), 0.5 * (k + beyond(k, -1, 1))
        fx[i + 1, here, :] = after
        fy[i, here, :] = jnp.where(low & (row == HALO - 1), 0.0, along_y)
        fz[i, here, :] = jnp.where(lane == lanes - 1, 0.0, along_z)
        absorb = jnp.take_along_axis(abs_row, labels[i], axis=1)
        diag[i, here, :] = absorb + before + after + along_y + back_y + along_z + back_z
        before = after
        face_up = jnp.where(low & (row == HALO - 1), 0.5 * up, 0.0)
        face_down = jnp.where(low | (row > 0), 0.0, 0.5 * down)
        fy[i, beside_it, :] = fy_in[i, beside_it, :] + face_up
        diag[i, beside_it, :] = diag_in[i, beside_it, :] + face_up + face_down


def density_kernel(mine, got, edge, phi, phi_y, phi_z):
    _, _, y, c = places(2)
    framed(phi, 1, mine, got.at[0], edge.at[0], y, c)
    blank_ends(phi)

    def differ(i, carry):
        p = phi[i + 1]
        phi_y[i], phi_z[i] = p - beyond(p, 1, 0), p - beyond(p, 1, 1)
        return carry

    lax.fori_loop(0, phi_y.shape[0], differ, 0, unroll=4)


def first_kernel(
    phi, phi_y, phi_z, diag, fx, fy, fz, count, sums, vector, got_vector, edge,
    change, message,
    vk, va, b, buf_a, buf_b,
):
    _, _, y, c = places(2)
    planes, rows, lanes = change.shape
    cy = vector.shape[2]
    framed(vk, 1, vector.at[0], got_vector.at[0], edge.at[0], y, c)
    framed(va, 0, vector.at[1], got_vector.at[1], edge.at[1], y, c)
    blank_ends(vk, buf_a, buf_b)
    theta, _ = chebyshev_scalars()

    def set_up(i, carry):
        v, p = vk[i + 1], phi[i + 1]
        total = 0.5 * (v + vk[i]) * (p - phi[i]) + 0.5 * (v + vk[i + 2]) * (p - phi[i + 2])
        for axis, step in enumerate((phi_y, phi_z)):
            flow = 0.5 * (v + beyond(v, 1, axis)) * step[i]
            first = index_along(v.shape, axis) == 0
            total = total + flow + jnp.where(first, 0.5 * v * p, -shifted(flow, 1, axis))
        total = -(va[i] * p + total)
        b[i] = total
        buf_a[i + 1] = total * (1.0 / theta)
        return carry

    lax.fori_loop(0, planes, set_up, 0, unroll=8)
    found = solve(b, (buf_a, buf_b), diag, fx, fy, fz, UNROLL)
    owned = owned_rows((rows, lanes), HALO * y, 2 * cy)

    def add_up(i, carry):
        u = found[i + 1]
        change[i] = u
        part = jnp.where(owned, count[i], 0.0) * u
        return carry[0] + folded(part), carry[1] + folded(part * phi[i + 1])

    zero = jnp.zeros((8, lanes), jnp.float32)
    seen, cross = lax.fori_loop(0, planes, add_up, (zero, zero), unroll=UNROLL)
    first = (2 * cy - HALO) * (1 - y) + HALO * y
    size = GROUP * REACH
    for g in range(planes // GROUP):
        message[pl.ds(size * g, size), :] = packed_edges(
            [near_rows(found, 1 + GROUP * g + j, first, y) for j in range(GROUP)]
        )
    rows_of_sums = [jnp.sum(part, axis=0, keepdims=True) for part in (sums[0], seen, cross, sums[1])]
    message[pl.ds(REACH * planes, 8), :] = jnp.concatenate([*rows_of_sums, zero[:4]], axis=0)


def second_kernel(
    phi, phi_y, phi_z, change, diag, fx, fy, fz, count, sent, came,
    own, message,
    b, buf_a, buf_b, grad_k, grad_a,
    *, dets,
):
    _, _, y, c = places(2)
    planes, rows, lanes = change.shape
    cy = (rows - HALO) // 2
    base = HALO * y
    edge = pl.ds(2 * cy * (1 - y), HALO)
    tail = pl.ds(REACH * planes, 8)
    sums = jnp.sum(sent[tail, :] + came[tail, :], axis=1, keepdims=True)
    total, seen_sum, cross, square = (sums[g : g + 1] for g in range(4))
    mean = total / dets
    part = seen_sum / total
    level = (cross - part * square) / (total * mean)
    inverse = 1.0 / mean
    blank_ends(buf_a, buf_b)
    theta, _ = chebyshev_scalars()

    def weighted(n, u, p):
        return n * (((u - p * part) * inverse - level) * inverse)

    def set_up(i, carry):
        value = weighted(count[i], change[i], phi[i + 1])
        b[i] = value
        buf_a[i + 1] = value * (1.0 / theta)
        return carry

    lax.fori_loop(0, planes, set_up, 0, unroll=8)
    size = GROUP * REACH
    for i in range(planes):
        u = edge_tile(came[pl.ds(size * (i // GROUP), size), :], i % GROUP, y)
        value = weighted(count[i, edge, :], u, phi[i + 1, edge, :])
        b[i, edge, :] = value
        buf_a[i + 1, edge, :] = value * (1.0 / theta)
    dual = solve(b, (buf_a, buf_b), diag, fx, fy, fz, UNROLL)

    def product(i, carry):
        p, u = phi[i + 1], dual[i + 1]
        grad = (p - phi[i]) * (u - dual[i]) + (p - phi[i + 2]) * (u - dual[i + 2])
        both = p * u
        for axis, step in enumerate((phi_y, phi_z)):
            flow = step[i] * (u - beyond(u, 1, axis))
            first = index_along(p.shape, axis) == 0
            grad = grad + flow + jnp.where(first, both, shifted(flow, 1, axis))
        grad_k[i] = -0.5 * grad
        grad_a[i] = -both
        for f, ref in enumerate((grad_k, grad_a)):
            own[f, i] = ref[i, pl.ds(base + cy * c, cy), :]
            message[f, i] = ref[i, pl.ds(base + cy * (1 - c), cy), :]
        return carry

    lax.fori_loop(0, planes, product, 0, unroll=8)


def packed_slabs(own, came, half, out):
    s, _, _, _ = places(2)
    _, planes, cy, lanes = own.shape
    n, _, groups = out.shape[:3]
    slab = lanes // n
    block = index_along((cy, lanes), 1) // slab
    for f in range(2):
        for q in range(groups):
            at = planes // 2 * half + n * q
            parts = [own[f, at + j] + came[f, at + j] for j in range(n)]
            size = n // 2
            while size:
                low = block & size == 0
                for j in range(n):
                    if not j & size:
                        a, b = parts[j], parts[j | size]
                        parts[j] = jnp.where(low, a, shifted(b, size * slab, 1))
                        parts[j | size] = jnp.where(low, shifted(a, -size * slab, 1), b)
                size //= 2
            for t in range(n):
                out[s ^ t, f, q] = parts[t]


def send_kernel(own, came, *refs):
    _, x, _, _ = places(2)
    outs, packed = refs[:-1], refs[-1]
    packed_slabs(own, came, 1 - x, packed)
    for k, out in enumerate(outs):
        out[0] = packed[k]


def keep_kernel(own, came, kept):
    _, x, _, _ = places(2)
    packed_slabs(own, came, x, kept)


def add_kernel(kept, came, out, *, k):
    out[...] = kept[k] + came[0]


def sum_kernel(*refs):
    total = refs[0][...]
    for ref in refs[1:-1]:
        total = total + ref[...]
    refs[-1][...] = total


def project_kernel(*refs, parts_n, n):
    beta_prev = refs[0]
    parts = refs[1 : 1 + parts_n]
    vk, va, qk, qa, w_k, w_a, tile = refs[1 + parts_n :]
    slab = 128 // n
    for f, (q_ref, w) in enumerate(((qk, w_k), (qa, w_a))):
        for q in range(vk.shape[0] // n):
            whole = sum(part[f, q] for part in parts[1:]) + parts[0][f, q]
            for j in range(n):
                i = n * q + j
                w[i] = whole[:, slab * j : slab * (j + 1)] - beta_prev[:, : vk.shape[2]] * q_ref[i]

    def total(value):
        return jnp.sum(jnp.sum(jnp.sum(value, axis=0), axis=0, keepdims=True), axis=1, keepdims=True)

    wk, wa, v_k, v_a = w_k[...], w_a[...], vk[...], va[...]
    wv = total(wk * v_k + wa * v_a)
    vv = total(v_k * v_k + v_a * v_a)
    a = jnp.where(vv > 0.0, wv / jnp.where(vv > 0.0, vv, 1.0), 0.0)
    u_k, u_a = wk - a * v_k, wa - a * v_a
    uv = total(u_k * v_k + u_a * v_a)
    uu = total(u_k * u_k + u_a * u_a)
    lane = index_along((1, 128), 1)
    values = jnp.zeros((1, 128), jnp.float32)
    for i, value in enumerate((wv, vv, a, uv, uu)):
        values = jnp.where(lane == i, value, values)
    tile[...] = values


def final_kernel(tiles, w_k, w_a, vk, va, next_k, next_a, coefs, *, cells):
    tile = jnp.concatenate([tiles[i] for i in range(tiles.shape[0])], axis=0)
    wv, vv, a, uv, uu = (tile[:, i : i + 1] for i in range(5))
    wv_sum = jnp.sum(wv, axis=0, keepdims=True)
    vv_sum = jnp.sum(vv, axis=0, keepdims=True)
    alpha = wv_sum / cells / (vv_sum / cells + eps_norm)
    off = alpha - a
    rr = jnp.sum(uu - 2.0 * off * uv + off * (off * vv), axis=0, keepdims=True)
    beta = jnp.sqrt(rr / cells + eps_norm)
    next_k[...] = (w_k[...] - alpha * vk[...]) / beta
    next_a[...] = (w_a[...] - alpha * va[...]) / beta
    coefs[0] = jnp.sum(alpha)
    coefs[1] = jnp.sum(beta)


def f32(*shape):
    return jax.ShapeDtypeStruct(shape, jnp.float32)


def run(kernel, outs, *args, after=(), scratch=(), copies=0, smem=(), hbm=(), mib=16, in_smem_out=(), cost=None):
    vmem = pl.BlockSpec(memory_space=pltpu.VMEM)
    scalar = pl.BlockSpec(memory_space=pltpu.SMEM)
    far = pl.BlockSpec(memory_space=pltpu.HBM)
    held = [pltpu.VMEM(shape, dtype) for shape, dtype in scratch]
    used, waits = len(args), len(after)

    def body(*refs):
        kernel(*refs[:used], *refs[used + waits :])

    args = (*args, *after)
    if copies:
        held.append(pltpu.SemaphoreType.DMA((copies,)))
    return pl.pallas_call(
        body if waits else kernel,
        out_shape=tuple(outs),
        in_specs=[scalar if i in smem else far if i in hbm else vmem for i in range(len(args))],
        out_specs=tuple(scalar if i in in_smem_out else vmem for i in range(len(outs))),
        scratch_shapes=held,
        compiler_params=pltpu.CompilerParams(vmem_limit_bytes=mib * 2**20),
        cost_estimate=cost,
    )(*args)


HALO = 8
UNROLL = 16
REACH = 6
GROUP = 4


def per_device_paired(
    labels, kappa_table, absorb_table, background, det_cells,
    v_kappa, v_absorb, q_kappa, q_absorb, beta_prev,
):
    sources, cx, cy, cz = background.shape
    n = lax.axis_size("src")
    planes, rows = 2 * cx, 2 * cy + HALO
    ny = cy * lax.axis_size("gy")
    dets = det_cells.shape[0]
    cells = planes * ny * cz
    groups = cx // n

    def swap_x(value):
        return lax.ppermute(value, "gx", [(0, 1), (1, 0)])

    def swap_core(value):
        return lax.ppermute(value, "gy", [(0, 1), (1, 0), (2, 3), (3, 2)])

    def along_z(value, k):
        return lax.ppermute(value, "src", [(i, i ^ k) for i in range(n)])

    block = (cx, cy, cz)
    float_block = lambda *shape: (shape, jnp.float32)
    raw_labels = (block, jnp.int32)
    packed, message = run(
        pack_kernel, (f32(2 * groups, cy, cz), f32(sources // 2 * cx + 2 * groups, cy, cz)),
        background, v_kappa, v_absorb, hbm=(0, 1, 2),
        scratch=(float_block(2, *v_kappa.shape),), copies=2 + sources // 2, mib=60,
    )
    long = pl.CostEstimate(flops=10**9, bytes_accessed=2**26, transcendentals=0)
    labels_came = swap_x(labels)
    came = swap_x(message)
    slabs = [along_z(packed, k) for k in range(1, n)]
    count, beta_row = run(
        functools.partial(count_kernel, ny=ny, nz=cz, half=2 * cy, halo=HALO),
        (f32(planes, rows, cz), f32(1, cz)), det_cells.reshape(1, dets), beta_prev, smem=(1,), after=(labels_came,),
        cost=pl.CostEstimate(flops=2 * planes * rows * cz * dets, bytes_accessed=planes * rows * cz * 4, transcendentals=0),
    )

    def across_y(value):
        return lax.ppermute(value, "gy", [(i, (i + 2) % 4) for i in range(4)])

    (joined,) = run(join_kernel, (f32(2 * groups * (n - 1), cy, cz),), *slabs, after=(count,))
    joined_came = swap_x(joined)
    (half_vector,) = run(own_half_kernel, (f32(2, *block),), v_kappa, v_absorb, joined)
    mine, fields = run(
        photon_kernel, (f32(planes, cy, cz), f32(2, planes, cy, cz)),
        background, labels, came, labels_came, after=(joined,), hbm=(0, 1), scratch=(raw_labels,), copies=3,
    )
    got = swap_core(fields)
    (vector,) = run(
        vector_kernel, (f32(2, planes, cy, cz),), half_vector, came, joined_came, after=(mine,)
    )
    edge = (f32(2, *edge_shape(planes, cz)),)
    (sent,) = run(photon_edge_kernel, edge, mine, fields, got, after=(vector,))
    photon_edge = across_y(sent)
    vector_got = swap_core(vector)
    (vector_sent,) = run(vector_edge_kernel, edge, vector, vector_got, after=(sent,))
    frame, wide = (planes, rows, cz), (planes + 2, rows, cz)
    float_frame, float_wide = float_block(*frame), float_block(*wide)
    coefs = (f32(*frame), f32(planes + 1, rows, cz), f32(*frame), f32(*frame))
    kap, *partial, sums = run(
        stencil_kernel, (f32(*wide), *coefs, f32(2, 8, cz)),
        kappa_table, absorb_table, mine, fields, got, count, after=(vector_sent,), cost=long,
        smem=(0, 1), scratch=(float_frame,),
    )
    diag, fx, fy, fz = run(
        halo_kernel, coefs, kappa_table, absorb_table, photon_edge, kap, *partial, smem=(0, 1)
    )
    densities = run(
        density_kernel, (f32(*wide), f32(*frame), f32(*frame)), mine, got, photon_edge, after=(fz,)
    )
    change, sent = run(
        first_kernel, (f32(*frame), f32(REACH * planes + 8, cz)),
        *densities, diag, fx, fy, fz, count, sums, vector, vector_got, across_y(vector_sent),
        scratch=(float_wide, float_frame, float_frame, float_wide, float_wide),
    )
    heard = across_y(sent)
    own, message = run(
        functools.partial(second_kernel, dets=dets),
        (f32(2, planes, cy, cz), f32(2, planes, cy, cz)),
        *densities, change, diag, fx, fy, fz, count, sent, heard,
        scratch=(float_frame, float_wide, float_wide, float_frame, float_frame),
    )
    piece = f32(2, groups, cy, cz)
    got = swap_core(message)
    last = run(
        send_kernel, [f32(1, *piece.shape)] * n, own, got, scratch=(float_block(n, *piece.shape),)
    )
    crossed = {k: swap_x(last[k]) for k in reversed(range(n))}
    (kept,) = run(keep_kernel, (f32(n, *piece.shape),), own, got, after=(last[0],))
    totals = {
        k: run(functools.partial(add_kernel, k=k), (piece,), kept, value)[0] for k, value in crossed.items()
    }
    received = {k: along_z(totals[k], k) for k in reversed(range(1, n))}
    (distant,) = run(sum_kernel, (piece,), *(received[k] for k in range(n // 2, n)), cost=long)
    parts = [distant, totals[0]] + [received[k] for k in range(1, n // 2)]
    w_k, w_a, tile = run(
        functools.partial(project_kernel, parts_n=len(parts), n=n),
        (f32(*v_kappa.shape), f32(*v_kappa.shape), f32(1, 128)),
        beta_row, *parts, v_kappa, v_absorb, q_kappa, q_absorb,
    )
    everyone = ("src", "gx", "gy")
    tiles = lax.all_to_all(jnp.broadcast_to(tile, (8 * n, 1, 128)), everyone, 0, 0)
    return tuple(run(
        functools.partial(final_kernel, cells=cells),
        (f32(*v_kappa.shape), f32(*v_kappa.shape), f32(2)),
        tiles, w_k, w_a, v_kappa, v_absorb, in_smem_out=(2,),
    ))


def paired_fits(mesh):
    return mesh.shape["gx"] == 2 and mesh.shape["gy"] == 4


def body_for(mesh):
    if not paired_fits(mesh):
        return per_device

    def chosen(*args):
        sources, cx, cy, cz = args[3].shape
        n = lax.axis_size("src")
        fits = sources == 4 and cz == 128 and cx % n == 0 and cx % GROUP == 0 and cy % HALO == 0 and n > 1 and n & (n - 1) == 0
        devices = 8 * n
        return (per_device_paired if fits and devices <= 128 else per_device)(*args)

    return chosen


def solution(mesh):
    return jax.shard_map(
        body_for(mesh),
        mesh=mesh,
        in_specs=(
            P("gx", "gy", None),
            P(),
            P(),
            P("src", "gx", "gy", None),
            P(),
            P("gx", "gy", "src"),
            P("gx", "gy", "src"),
            P("gx", "gy", "src"),
            P("gx", "gy", "src"),
            P(),
        ),
        out_specs=(P("gx", "gy", "src"), P("gx", "gy", "src"), P()),
        check_vma=False,
    )
```
